32 devices in a mesh: ctx: 8 (over z, y), fsdp: 4 (over x, core).
Axes of the slice: x: 2, y: 2, z: 4, core: 2. Of those that a mesh axis runs over, the one named last changes fastest.
Arguments:
- tokens: bfloat16 [12, 512, 2048], P('fsdp', 'ctx'), may hold values from -6 to 6
- lengths: int32 [12], P('fsdp'), may hold values from 128 to 512, as said below
- norm_gains: float32 [2, 2048], replicated, may hold values from 0.24 to 1.8
- attention_weight: float32 [2048, 6144], P(('ctx', 'fsdp'))
- feed_weight: float32 [2048, 24576], P(('ctx', 'fsdp'))
- cotangent: bfloat16 [12, 512, 2048], P('fsdp', 'ctx'), may hold values from -7.5 to 7.5
- attention_mean: float32 [2048, 6144], P(('ctx', 'fsdp'))
- attention_square: float32 [2048, 6144], P(('ctx', 'fsdp')), as said below
- feed_mean: float32 [2048, 24576], P(('ctx', 'fsdp'))
- feed_square: float32 [2048, 24576], P(('ctx', 'fsdp')), as said below
- gain_mean: float32 [2, 2048], replicated
- gain_square: float32 [2, 2048], replicated, as said below
Outputs:
- layer_output: bfloat16 [12, 512, 2048], P('fsdp', 'ctx')
- input_gradient: float32 [12, 512, 2048], P('fsdp', 'ctx')
- gradient_norm: float32 [], replicated
- attention_master: float32 [2048, 6144], P(('ctx', 'fsdp'))
- attention_means: float32 [2048, 6144], P(('ctx', 'fsdp'))
- attention_squares: float32 [2048, 6144], P(('ctx', 'fsdp'))
- attention_copy: bfloat16 [2048, 6144], P(('ctx', 'fsdp'))
- feed_master: float32 [2048, 24576], P(('ctx', 'fsdp'))
- feed_means: float32 [2048, 24576], P(('ctx', 'fsdp'))
- feed_squares: float32 [2048, 24576], P(('ctx', 'fsdp'))
- feed_copy: bfloat16 [2048, 24576], P(('ctx', 'fsdp'))
- gains_updated: float32 [2, 2048], replicated
- gains_means: float32 [2, 2048], replicated
- gains_squares: float32 [2, 2048], replicated
The draws below stay inside these ranges and needn't reach their ends.
Inputs may be any that keep to these rules, and one draw needn't show every extreme that they name: `lengths`: of the 3 consecutive sequences on one index of fsdp, one has length 512. `attention_square`: positive. `feed_square`: positive. `gain_square`: positive.
All inputs are finite; a program needn't handle non-finite values.
Results may differ from the reference program's by a relative error of at most 0.013.
Values may be sent and summed in bfloat16 or wider, within the bound.
A program may use at most 896 MiB of HBM per device.

```python
import jax
import jax.numpy as jnp
from jax import lax

D = 2048
QUERY_HEADS = 8
KEY_VALUE_HEADS = 4
HEAD_SIZE = 256
FF = 8192
SEQS_DEV = 3
STEP = 10
QW = 2048
KW = 1024
BATCH = 12
PADDED_LENGTH = 512


def square_scale():
    return 1.0 / (D * (2 * QW + 2 * KW + 3 * FF) + 2 * D)


def moment_mean(key, shape, squared):
    return jax.random.truncated_normal(key, -4.0, 4.0, shape, jnp.float32) * (0.111 * squared ** 0.5)


def moment_square(key, shape, squared):
    lower = jnp.log(0.0526 * squared)
    upper = jnp.log(0.21 * squared)
    return jnp.exp(jax.random.uniform(key, shape, jnp.float32, lower, upper))


def draw_lengths(key, part):
    key = jax.random.fold_in(key, 11)
    key_ragged, key_chosen = jax.random.split(key)
    ragged = jax.random.randint(key_ragged, (BATCH,), PADDED_LENGTH // 4, PADDED_LENGTH + 1)
    chosen = jax.random.randint(key_chosen, (BATCH // SEQS_DEV,), 0, SEQS_DEV)
    filled = jnp.arange(BATCH) % SEQS_DEV == jnp.repeat(chosen, SEQS_DEV)
    return jnp.where(filled, PADDED_LENGTH, ragged).astype(jnp.int32)


def draw_norm_gains(key, part):
    key = jax.random.fold_in(key, 12)
    ramp = jnp.arange(D).astype(jnp.float32) / (D - 1)
    base = 0.5 + ramp
    noise = jax.random.uniform(key, (2, D), jnp.float32, 0.8, 1.2)
    return base[None, :] * noise


def draw_cotangent(key, part):
    key = jax.random.fold_in(key, 13)
    ramp = jnp.arange(D).astype(jnp.float32) / (D - 1)
    noise = jax.random.truncated_normal(key, -5.0, 5.0, (BATCH, PADDED_LENGTH, D), jnp.float32)
    base = 0.5 + ramp
    return (noise * base).astype(jnp.bfloat16)


def draw_attention_weight(key, part):
    key = jax.random.fold_in(key, 14)
    columns = 2 * QW + 2 * KW
    noise = jax.random.truncated_normal(key, -3.0, 3.0, (D, columns), jnp.float32)
    index = jnp.arange(columns)
    scale = jnp.where(index < QW + 2 * KW, D ** (-0.5), (PADDED_LENGTH / 16.0) ** 0.5 * QW ** (-0.5))
    return noise * scale[None, :]


def draw_feed_weight(key, part):
    key = jax.random.fold_in(key, 15)
    noise = jax.random.truncated_normal(key, -3.0, 3.0, (D, 3 * FF), jnp.float32)
    index = jnp.arange(3 * FF)
    scale = jnp.where(index < 2 * FF, D ** (-0.5), 1.5 * FF ** (-0.5))
    return noise * scale[None, :]


def draw_attention_mean(key, part):
    key = jax.random.fold_in(key, 16)
    return moment_mean(key, (D, 2 * QW + 2 * KW), square_scale())


def draw_attention_square(key, part):
    key = jax.random.fold_in(key, 17)
    return moment_square(key, (D, 2 * QW + 2 * KW), square_scale())


def draw_feed_mean(key, part):
    key = jax.random.fold_in(key, 18)
    return moment_mean(key, (D, 3 * FF), square_scale())


def draw_feed_square(key, part):
    key = jax.random.fold_in(key, 19)
    return moment_square(key, (D, 3 * FF), square_scale())


def draw_gain_mean(key, part):
    key = jax.random.fold_in(key, 20)
    return moment_mean(key, (2, D), 9.0 * square_scale())


def draw_gain_square(key, part):
    key = jax.random.fold_in(key, 21)
    return moment_square(key, (2, D), 9.0 * square_scale())


def levels(own_key, shape, cuts, low, high):
    def one(dim, blocks):
        heights = jax.random.uniform(jax.random.fold_in(jax.random.fold_in(own_key, 6), dim), (blocks,), jnp.float32, low / len(cuts), high / len(cuts))
        return jnp.repeat(jnp.exp(heights), shape[dim] // blocks).reshape((-1,) + (1,) * (len(shape) - dim - 1))

    factor_of = one(*cuts[0])
    for cut in cuts[1:]:
        factor_of = factor_of * one(*cut)
    return factor_of


def bell_draw(key, dims, width, reach, cuts=(), held_as=jnp.bfloat16):
    values = jax.random.normal(key, dims, jnp.float32) * width
    if len(cuts) > 0:
        values = levels(key, dims, cuts, -0.22, 0.18) * values
    return jnp.clip(values, min=-reach, max=reach).astype(held_as)


def setup_inputs(seed: int = 0) -> dict:
    streams_of = jax.random.split(jax.random.key(seed), 13)
    return {
        "tokens": bell_draw(streams_of[0], (BATCH, PADDED_LENGTH, D), 1.0, 6.0, ((0, 4), (1, 8))),
        "lengths": draw_lengths(jax.random.fold_in(streams_of[12], 71), 0),
        "norm_gains": draw_norm_gains(jax.random.fold_in(streams_of[12], 71), 0),
        "attention_weight": draw_attention_weight(jax.random.fold_in(streams_of[12], 71), 0),
        "feed_weight": draw_feed_weight(jax.random.fold_in(streams_of[12], 71), 0),
        "cotangent": draw_cotangent(jax.random.fold_in(streams_of[12], 71), 0),
        "attention_mean": draw_attention_mean(jax.random.fold_in(streams_of[12], 71), 0),
        "attention_square": draw_attention_square(jax.random.fold_in(streams_of[12], 71), 0),
        "feed_mean": draw_feed_mean(jax.random.fold_in(streams_of[12], 71), 0),
        "feed_square": draw_feed_square(jax.random.fold_in(streams_of[12], 71), 0),
        "gain_mean": draw_gain_mean(jax.random.fold_in(streams_of[12], 71), 0),
        "gain_square": draw_gain_square(jax.random.fold_in(streams_of[12], 71), 0),
    }


@jax.custom_vjp
def reduced_precision(v):
    return lax.optimization_barrier(v.astype(jnp.bfloat16)).astype(jnp.float32)

@jax.custom_vjp
def reduced_backward(v):
    return v

def low_keep(v):
    return (reduced_precision(v), None)

def low_pass(kept, grad):
    return (grad,)

def back_keep(v):
    return (v, None)

def back_low(kept, grad):
    return (reduced_precision(grad),)
reduced_precision.defvjp(low_keep, low_pass)
reduced_backward.defvjp(back_keep, back_low)
norm_eps = 1e-06
rope_base = 1000042.0
masked_value = -1e+30
clip_norm = 1.0
beta_one = 0.9
beta_two = 0.95
adam_eps = 1e-08
matrix_rate = 0.03
gain_rate = 0.4
weight_decay = 0.1

def product_result(pattern, left_side, right_side):
    return jnp.einsum(pattern, left_side, right_side, precision=lax.Precision.HIGHEST)

def angle_tables(positions):
    half_dim = HEAD_SIZE // 2
    frequency = rope_base ** (-(jnp.arange(half_dim).astype(jnp.float32) * 2.0) / HEAD_SIZE)
    phases = positions.astype(jnp.float32)[:, None] * frequency[None, :]
    return (jnp.cos(phases), jnp.sin(phases))

def apply_rotation(value_tensor, cos_table, sin_table):
    half_dim = value_tensor.shape[-1] // 2
    lower_half = value_tensor[..., :half_dim]
    upper_half = value_tensor[..., half_dim:]
    return jnp.concatenate([lower_half * cos_table - upper_half * sin_table, upper_half * cos_table + lower_half * sin_table], axis=-1)

def rms_norm(value_tensor, gain_row):
    return value_tensor * lax.rsqrt(lax.optimization_barrier(jnp.mean(value_tensor * value_tensor, axis=-1, keepdims=True)) + norm_eps) * gain_row

def layer_sequence(gains, attention_low, feed_low, row_values, length):
    positions = jnp.arange(PADDED_LENGTH)
    cos_table, sin_table = angle_tables(positions)
    cosine_per_head = cos_table[:, None, :]
    sine_per_head = sin_table[:, None, :]
    query_weight = attention_low[:, :QW]
    key_matrix = attention_low[:, QW:QW + KW]
    value_matrix = attention_low[:, QW + KW:QW + 2 * KW]
    out_weight = attention_low[:, QW + 2 * KW:]
    first_hidden = reduced_precision(rms_norm(row_values, gains[0]))
    query_tensor = reduced_precision(apply_rotation(reduced_backward(product_result('nq,qc->nc', first_hidden, query_weight)).reshape(PADDED_LENGTH, QUERY_HEADS, HEAD_SIZE), cosine_per_head, sine_per_head))
    key_tensor = reduced_precision(apply_rotation(reduced_backward(product_result('nq,qc->nc', first_hidden, key_matrix)).reshape(PADDED_LENGTH, KEY_VALUE_HEADS, HEAD_SIZE), cosine_per_head, sine_per_head))
    value_tensor = reduced_precision(reduced_backward(product_result('nq,qc->nc', first_hidden, value_matrix))).reshape(PADDED_LENGTH, KEY_VALUE_HEADS, HEAD_SIZE)
    grouped_rows = query_tensor.reshape(PADDED_LENGTH, KEY_VALUE_HEADS, QUERY_HEADS // KEY_VALUE_HEADS, HEAD_SIZE)
    scores = reduced_backward(product_result('pkjd,tkd->kjpt', grouped_rows, key_tensor)) * HEAD_SIZE ** (-0.5)
    allowed = (positions[None, :] <= positions[:, None]) & (positions[None, :] < length)
    scores = jnp.where(allowed, scores, masked_value)
    row_max = lax.optimization_barrier(jnp.max(scores, axis=-1, keepdims=True))
    exponent = jnp.exp(scores - row_max)
    soft = reduced_precision(exponent / lax.optimization_barrier(jnp.sum(exponent, axis=-1, keepdims=True)))
    mixed = reduced_precision(reduced_backward(product_result('kjpt,tkd->pkjd', soft, value_tensor).reshape(PADDED_LENGTH, QW)))
    residual_mid = row_values + reduced_backward(product_result('pe,de->pd', mixed, out_weight))
    hidden_two = reduced_precision(rms_norm(residual_mid, gains[1]))
    gate = reduced_backward(product_result('pd,df->pf', hidden_two, feed_low[:, :FF]))
    upward = reduced_backward(product_result('pd,df->pf', hidden_two, feed_low[:, FF:2 * FF]))
    inner = reduced_precision(jax.nn.silu(gate) * upward)
    return residual_mid + reduced_backward(product_result('pf,df->pd', inner, feed_low[:, 2 * FF:]))

def forward(rows, gains, attention_weight, feed_weight, lengths):
    attention_low = reduced_precision(attention_weight)
    feed_low = reduced_precision(feed_weight)

    def one_sequence(operands):
        return layer_sequence(gains, attention_low, feed_low, operands[0], operands[1])
    return lax.map(jax.checkpoint(one_sequence), (rows, lengths))

def adamw(weight, gradient, moment_one, moment_two, step_rate, decay_rate):
    mean_new = beta_one * moment_one + (1.0 - beta_one) * gradient
    square_new = beta_two * moment_two + (1.0 - beta_two) * gradient * gradient
    direction = mean_new / (1.0 - beta_one ** STEP) / (jnp.sqrt(square_new / (1.0 - beta_two ** STEP)) + adam_eps)
    return (weight - step_rate * (direction + decay_rate * weight), mean_new, square_new)

def reference(tokens, lengths, norm_gains, attention_weight, feed_weight, cotangent, attention_mean, attention_square, feed_mean, feed_square, gain_mean, gain_square):
    rows = tokens.astype(jnp.float32)

    def closed(row_values, gains, attention_in, feed_in):
        return forward(row_values, gains, attention_in, feed_in, lengths)
    result, pullback = jax.vjp(closed, rows, norm_gains, attention_weight, feed_weight)
    valid = (jnp.arange(PADDED_LENGTH)[None, :] < lengths[:, None]).astype(jnp.float32)
    outer_grad = cotangent.astype(jnp.float32) * valid[:, :, None]
    input_gradient, gain_grad, attention_grad, feed_grad = pullback(outer_grad)
    total = jnp.sum(attention_grad * attention_grad) + jnp.sum(feed_grad * feed_grad) + jnp.sum(gain_grad * gain_grad)
    gradient_norm = jnp.sqrt(total)
    factor = clip_norm / gradient_norm
    attention_master, attention_means, attention_squares = adamw(attention_weight, attention_grad * factor, attention_mean, attention_square, matrix_rate, weight_decay)
    feed_master, feed_means, feed_squares = adamw(feed_weight, feed_grad * factor, feed_mean, feed_square, matrix_rate, weight_decay)
    gains_updated, gains_means, gains_squares = adamw(norm_gains, gain_grad * factor, gain_mean, gain_square, gain_rate, 0.0)
    return (result.astype(jnp.bfloat16), input_gradient, gradient_norm, attention_master, attention_means, attention_squares, attention_master.astype(jnp.bfloat16), feed_master, feed_means, feed_squares, feed_master.astype(jnp.bfloat16), gains_updated, gains_means, gains_squares)
```

```python
import jax
import jax.numpy as jnp
from jax import lax
from jax.sharding import Mesh, PartitionSpec as P

QUERY_HEADS = 8
KEY_VALUE_HEADS = 4
HEAD_SIZE = 256
FF = 8192
STEP = 10

norm_eps = 1e-06
rope_base = 1000042.0
masked_value = -1e30
clip_norm = 1.0
beta_one = 0.9
beta_two = 0.95
adam_eps = 1e-08
matrix_rate = 0.03
gain_rate = 0.4
weight_decay = 0.1

TEAM = ("y", "x", "c")
ALL = ("z", "y", "x", "c")


def dot(left, right, contract):
    return lax.dot_general(left, right, (contract, ((), ())), preferred_element_type=jnp.float32)


def mm(left, right):
    return dot(left, right, ((1,), (0,)))


def mm_nt(left, right):
    return dot(left, right, ((1,), (1,)))


def mm_tn(left, right):
    return dot(left, right, ((0,), (0,)))


def bmm(pattern, left, right):
    return jnp.einsum(pattern, left, right, preferred_element_type=jnp.float32)


def angle_tables(positions):
    half_dim = HEAD_SIZE // 2
    frequency = rope_base ** (-(jnp.arange(half_dim).astype(jnp.float32) * 2.0) / HEAD_SIZE)
    phases = positions.astype(jnp.float32)[:, None] * frequency[None, :]
    return (jnp.cos(phases), jnp.sin(phases))


def rotate(value, cos_table, sin_table):
    half = value.shape[-1] // 2
    a, b = value[..., :half], value[..., half:]
    return jnp.concatenate([a * cos_table - b * sin_table, b * cos_table + a * sin_table], axis=-1)


def rms_forward(value, gain_row):
    inverse = lax.rsqrt(jnp.mean(value * value, axis=-1, keepdims=True) + norm_eps)
    return (value * inverse * gain_row, inverse)


def rms_back(grad_out, value, inverse, gain_row):
    scaled = grad_out * gain_row
    grad_in = inverse * (
        scaled - value * inverse * inverse * jnp.mean(scaled * value, axis=-1, keepdims=True)
    )
    return (grad_in, jnp.sum(grad_out * value * inverse, axis=0))


def adamw(weight, gradient, moment_one, moment_two, step_rate, decay_rate):
    mean_new = beta_one * moment_one + (1.0 - beta_one) * gradient
    square_new = beta_two * moment_two + (1.0 - beta_two) * gradient * gradient
    direction = (
        mean_new
        / (1.0 - beta_one**STEP)
        / (jnp.sqrt(square_new / (1.0 - beta_two**STEP)) + adam_eps)
    )
    return (weight - step_rate * (direction + decay_rate * weight), mean_new, square_new)


def gather_columns(blocks):
    turned = lax.all_to_all(blocks, TEAM, split_axis=0, concat_axis=0, tiled=True)
    return lax.all_gather(turned.reshape(-1, blocks.shape[-1]), "z", axis=0, tiled=True)


def scatter_columns(gradient, team):
    rows = lax.psum_scatter(gradient.astype(jnp.bfloat16), "z", scatter_dimension=0, tiled=True)
    blocks = rows.reshape(team, -1, rows.shape[-1])
    return lax.all_to_all(blocks, TEAM, split_axis=0, concat_axis=0, tiled=True)


def team_gather(local):
    return lax.all_gather(local, TEAM, axis=0, tiled=True)


def team_sum(partial):
    return lax.psum_scatter(partial.astype(jnp.bfloat16), TEAM, scatter_dimension=0, tiled=True).astype(jnp.float32)


def local(
    tokens,
    lengths,
    norm_gains,
    attention_weight,
    feed_weight,
    cotangent,
    attention_mean,
    attention_square,
    feed_mean,
    feed_square,
    gain_mean,
    gain_square,
):
    low = jnp.bfloat16
    sequences, span, width = tokens.shape
    ny, nx, nz = lax.axis_size("y"), lax.axis_size("x"), lax.axis_size("z")
    team = ny * nx * 2
    core = lax.axis_index("c")
    rows = attention_weight.shape[0]
    q_width, kv_width = QUERY_HEADS * HEAD_SIZE, KEY_VALUE_HEADS * HEAD_SIZE
    count = sequences * span
    all_sequences = nx * 2 * sequences
    reach = ny * span
    padded = nz * reach
    ff_part = FF // team

    attention_low = attention_weight.astype(low)
    feed_low = feed_weight.astype(low)
    q_cols = attention_low[:, :q_width].reshape(rows, team, HEAD_SIZE)
    kv_cols = (
        attention_low[:, q_width : q_width + 2 * kv_width]
        .reshape(rows, 2, KEY_VALUE_HEADS, HEAD_SIZE)
        .transpose(0, 2, 1, 3)
        .reshape(rows, team, HEAD_SIZE)
    )
    o_cols = attention_low[:, q_width + 2 * kv_width :].reshape(rows, team, HEAD_SIZE)
    attention_blocks = jnp.concatenate([q_cols, kv_cols, o_cols], axis=-1).transpose(1, 0, 2)
    attention_mine = gather_columns(attention_blocks)
    query_weight = attention_mine[:, :HEAD_SIZE]
    kv_weight = attention_mine[:, HEAD_SIZE : 2 * HEAD_SIZE]
    out_weight = attention_mine[:, 2 * HEAD_SIZE :]

    def feed_block(index):
        part = feed_low[:, index * FF : (index + 1) * FF].reshape(rows, team, ff_part)
        return gather_columns(part.transpose(1, 0, 2))

    gate_weight, up_weight, down_weight = feed_block(0), feed_block(1), feed_block(2)

    team_pos = lax.axis_index("z") * reach + jnp.arange(reach, dtype=jnp.int32)
    own_pos = lax.axis_index("z") * reach + lax.axis_index("y") * span + jnp.arange(span, dtype=jnp.int32)
    key_pos = jnp.arange(padded, dtype=jnp.int32)
    lengths_all = lax.all_gather(lengths, ("x", "c"), axis=0, tiled=True)
    cos_table, sin_table = angle_tables(team_pos)
    valid = (own_pos[None, :] < lengths[:, None]).astype(jnp.float32).reshape(count, 1)
    allowed = (key_pos[None, None, :] <= team_pos[None, :, None]) & (
        key_pos[None, None, :] < lengths_all[:, None, None]
    )

    def by_sequence(value):
        return (
            value.reshape(ny, all_sequences, span, -1)
            .transpose(1, 0, 2, 3)
            .reshape(all_sequences, reach, -1)
        )

    def by_device(value):
        return (
            value.reshape(all_sequences, ny, span, -1)
            .transpose(1, 0, 2, 3)
            .reshape(all_sequences * reach, -1)
        )

    x_in = tokens.reshape(count, width).astype(jnp.float32)
    normed_one, inverse_one = rms_forward(x_in, norm_gains[0])
    h1 = team_gather(normed_one.astype(low))
    outer_grad = cotangent.reshape(count, width).astype(jnp.float32) * valid
    dyb = team_gather(outer_grad.astype(low))

    q = rotate(by_sequence(mm(h1, query_weight)), cos_table, sin_table).astype(low)
    kv_raw = by_sequence(mm(h1, kv_weight))
    kv = jnp.where(core == 0, rotate(kv_raw, cos_table, sin_table), kv_raw).astype(low)
    kv = lax.all_gather(kv, "z", axis=1, tiled=True)
    kv = lax.all_gather(kv, "c", axis=0, tiled=False)
    k, v = kv[0], kv[1]
    scale = HEAD_SIZE ** (-0.5)

    def scores_of():
        return jnp.where(allowed, bmm("spd,std->spt", q, k) * scale, masked_value)

    scores = scores_of()
    row_max = jnp.max(scores, axis=-1, keepdims=True)
    exponent = jnp.exp(scores - row_max)
    soft = exponent / jnp.sum(exponent, axis=-1, keepdims=True)
    soft_low = soft.astype(low)
    o = by_device(bmm("spt,std->spd", soft_low, v).astype(low))
    r = x_in + team_sum(mm_nt(o, out_weight))

    normed_two, inverse_two = rms_forward(r, norm_gains[1])
    h2 = team_gather(normed_two.astype(low))
    gate = mm(h2, gate_weight)
    upward = mm(h2, up_weight)
    sig = jax.nn.sigmoid(gate)
    m = (gate * sig * upward).astype(low)
    layer_output = (r + team_sum(mm_nt(m, down_weight))).astype(low)
    down_grad = scatter_columns(mm_tn(dyb, m), team)

    dm = mm(dyb, down_weight)
    d_gate = (dm * upward * sig * (1.0 + gate * (1.0 - sig))).astype(low)
    d_up = (dm * gate * sig).astype(low)
    dh2 = team_sum(mm_nt(d_gate, gate_weight) + mm_nt(d_up, up_weight))
    gate_grad = scatter_columns(mm_tn(h2, d_gate), team)
    up_grad = scatter_columns(mm_tn(h2, d_up), team)
    mid_grad, gain_two = rms_back(dh2, r, inverse_two, norm_gains[1])
    dr = outer_grad + mid_grad
    drb = team_gather(dr.astype(low))

    do = by_sequence(mm(drb, out_weight).astype(low))
    dp = bmm("spd,std->spt", do, v)
    delta = jnp.sum(soft * dp, axis=-1, keepdims=True)
    ds = (soft * (dp - delta) * scale).astype(low)
    dq = by_device(rotate(bmm("spt,std->spd", ds, k), cos_table, -sin_table).astype(low))
    dk_term = bmm("spt,spd->std", ds, q)
    dv_term = bmm("spt,spd->std", soft_low, do)
    mine = jnp.where(core == 0, dk_term, dv_term)
    theirs = jnp.where(core == 0, dv_term, dk_term).astype(low)
    dkv = mine + lax.ppermute(theirs, "c", [(0, 1), (1, 0)]).astype(jnp.float32)
    dkv = lax.psum_scatter(dkv.astype(low), "z", scatter_dimension=1, tiled=True).astype(jnp.float32)
    dkv = by_device(jnp.where(core == 0, rotate(dkv, cos_table, -sin_table), dkv).astype(low))
    dh1 = team_sum(mm_nt(dq, query_weight) + mm_nt(dkv, kv_weight))
    in_grad, gain_one = rms_back(dh1, x_in, inverse_one, norm_gains[0])
    input_gradient = dr + in_grad
    attention_grad = scatter_columns(
        jnp.concatenate([mm_tn(h1, dq), mm_tn(h1, dkv), mm_tn(drb, o)], axis=1), team
    )

    def columns_of(blocks):
        return blocks.transpose(1, 0, 2).reshape(rows, -1)

    grad32 = attention_grad.astype(jnp.float32)
    kv_grad = grad32[:, :, HEAD_SIZE : 2 * HEAD_SIZE].reshape(KEY_VALUE_HEADS, 2, rows, HEAD_SIZE)
    attention_grad = jnp.concatenate(
        [
            columns_of(grad32[:, :, :HEAD_SIZE]),
            kv_grad.transpose(2, 1, 0, 3).reshape(rows, 2 * kv_width),
            columns_of(grad32[:, :, 2 * HEAD_SIZE :]),
        ],
        axis=1,
    )
    feed_grad = jnp.concatenate(
        [columns_of(g.astype(jnp.float32)) for g in (gate_grad, up_grad, down_grad)], axis=1
    )
    local_squares = jnp.sum(attention_grad * attention_grad) + jnp.sum(feed_grad * feed_grad)
    gain_grad, squares = lax.psum((jnp.stack([gain_one, gain_two]), local_squares), ALL)
    gradient_norm = jnp.sqrt(squares + jnp.sum(gain_grad * gain_grad))
    factor = clip_norm / gradient_norm
    attention_new = adamw(
        attention_weight, attention_grad * factor, attention_mean, attention_square, matrix_rate, weight_decay
    )
    feed_new = adamw(feed_weight, feed_grad * factor, feed_mean, feed_square, matrix_rate, weight_decay)
    gains_new = adamw(norm_gains, gain_grad * factor, gain_mean, gain_square, gain_rate, 0.0)
    return (
        layer_output.reshape(sequences, span, width),
        input_gradient.reshape(sequences, span, width),
        gradient_norm,
        *attention_new,
        attention_new[0].astype(low),
        *feed_new,
        feed_new[0].astype(low),
        *gains_new,
    )


def solution(mesh):
    ctx, fsdp = mesh.shape["ctx"], mesh.shape["fsdp"]
    inner = QUERY_HEADS // fsdp
    fine = Mesh(mesh.devices.reshape(ctx // inner, inner, fsdp // 2, 2), ALL)
    act = P(("x", "c"), ("z", "y"), None)
    matrix = P(ALL, None)
    return jax.shard_map(
        local,
        mesh=fine,
        in_specs=(act, P(("x", "c")), P(), matrix, matrix, act, matrix, matrix, matrix, matrix, P(), P()),
        out_specs=(act, act, P(), matrix, matrix, matrix, matrix, matrix, matrix, matrix, matrix, P(), P(), P()),
        check_vma=False,
    )
```

```python
import functools

import jax
import jax.numpy as jnp
from jax import lax
from jax.experimental import pallas as pl
from jax.experimental.pallas import tpu as pltpu
from jax.sharding import Mesh, PartitionSpec as P

QUERY_HEADS = 8
KEY_VALUE_HEADS = 4
HEAD_SIZE = 256
FF = 8192
STEP = 10

norm_eps = 1e-06
rope_base = 1000042.0
masked_value = -1e30
clip_norm = 1.0
beta_one = 0.9
beta_two = 0.95
adam_eps = 1e-08
matrix_rate = 0.03
gain_rate = 0.4
weight_decay = 0.1

TEAM = ("y", "x", "c")
ALL = ("z", "y", "x", "c")


MESH = pl.DeviceIdType.MESH
VMEM = pl.BlockSpec(memory_space=pltpu.VMEM)
HBM = pl.BlockSpec(memory_space=pl.ANY)


def place():
    y, x, c = lax.axis_index("y"), lax.axis_index("x"), lax.axis_index("c")
    return y, x, c, lambda yy, xx, cc: (yy * 2 + xx) * 2 + cc


def greet(others):
    barrier = pltpu.get_barrier_semaphore()
    for other in others:
        pl.semaphore_signal(barrier, inc=1, device_id=other, device_id_type=MESH)
    pl.semaphore_wait(barrier, len(others))


def gather_kernel(src, *refs):
    out, send, recv, own = refs[-4:]
    y, x, c, index = place()
    to_x, to_y, to_s = {"x": 1 - x}, {"y": 1 - y}, {"c": 1 - c}
    me, at_x, at_y, at_d = index(y, x, c), index(y, 1 - x, c), index(1 - y, x, c), index(1 - y, 1 - x, c)
    half = src.shape[0] // 2
    rows = (pl.ds(0, half), pl.ds(half, half))
    local = pltpu.make_async_copy(src, out.at[me], own)
    local.start()
    greet((to_x, to_y, to_s))

    def hop(slot, block, part, where, first=False):
        piece = out.at[block, rows[part]]
        return pltpu.make_async_remote_copy(
            src_ref=src.at[rows[part]] if first else piece,
            dst_ref=piece,
            send_sem=send.at[slot],
            recv_sem=recv.at[slot],
            device_id=where,
            device_id_type=MESH,
        )

    x0, x1 = hop(0, me, 0, to_x, True), hop(1, me, 1, to_x, True)
    y1, y0 = hop(2, me, 1, to_y, True), hop(3, me, 0, to_y, True)
    s0, s1 = hop(4, me, 0, to_s, True), hop(5, me, 1, to_s, True)
    for copy in (x0, y1, x1, y0, s0, s1):
        copy.start()
    x0.wait_recv()
    d0 = hop(6, at_x, 0, to_y)
    d0.start()
    y1.wait_recv()
    d1 = hop(7, at_y, 1, to_x)
    d1.start()
    sx0, sy1 = hop(8, at_x, 0, to_s), hop(9, at_y, 1, to_s)
    sx0.start()
    sy1.start()
    x1.wait_recv()
    sx1 = hop(10, at_x, 1, to_s)
    sx1.start()
    y0.wait_recv()
    sy0 = hop(11, at_y, 0, to_s)
    sy0.start()
    d0.wait_recv()
    sd0 = hop(12, at_d, 0, to_s)
    sd0.start()
    d1.wait_recv()
    sd1 = hop(13, at_d, 1, to_s)
    sd1.start()
    for copy in (s0, s1, sx0, sy1, sx1, sy0, sd0, sd1):
        copy.wait_recv()
    for copy in (x0, x1, y0, y1, s0, s1, d0, d1, sx0, sy1, sx1, sy0, sd0, sd1):
        copy.wait_send()
    local.wait()


def plane_gather(value, number, after=()):
    return pl.pallas_call(
        gather_kernel,
        out_shape=jax.ShapeDtypeStruct((8, *value.shape), value.dtype),
        in_specs=[HBM] * (1 + len(after)),
        out_specs=HBM,
        scratch_shapes=[
            pltpu.SemaphoreType.DMA((14,)),
            pltpu.SemaphoreType.DMA((14,)),
            pltpu.SemaphoreType.DMA,
        ],
        compiler_params=pltpu.CompilerParams(collective_id=number, has_side_effects=True),
        cost_estimate=pl.CostEstimate(flops=1, bytes_accessed=1, transcendentals=0),
        name="plane_gather",
    )(value, *after)


def sum_kernel(pairs, tile, *refs):
    a_refs, w_refs = refs[:pairs], refs[pairs : 2 * pairs]
    out, s_send, s_recv, d_send, d_recv, x_send, x_recv, y_send, y_recv, x_acc, y_acc, send, recv = refs[-13:]
    y, x, c, index = place()
    to_x, to_y, to_s = {"x": 1 - x}, {"y": 1 - y}, {"c": 1 - c}
    rows, width = out.shape
    half = rows // 2
    parts = (pl.ds(0, half), pl.ds(half, half))
    f32, low = jnp.float32, jnp.bfloat16

    def product(block, put):
        lines = pl.ds(pl.multiple_of(block * rows, rows), rows)

        @pl.loop(0, width // tile)
        def _(step):
            cols = pl.ds(pl.multiple_of(step * tile, tile), tile)
            total = None
            for a_ref, w_ref in zip(a_refs, w_refs):
                term = lax.dot_general(
                    a_ref[lines, :], w_ref[cols, :], (((1,), (1,)), ((), ())), preferred_element_type=f32
                )
                total = term if total is None else total + term
            put(cols, total)

    def hop(slot, src, dst, where):
        copy = pltpu.make_async_remote_copy(
            src_ref=src, dst_ref=dst, send_sem=send.at[slot], recv_sem=recv.at[slot],
            device_id=where, device_id_type=MESH,
        )
        return copy

    def to_sibling(slot, yy, xx):
        def put(cols, total):
            s_send[slot, :, cols] = total.astype(low)

        product(index(yy, xx, 1 - c), put)
        copy = hop(slot, s_send.at[slot], s_recv.at[slot], to_s)
        copy.start()
        return copy

    def with_sibling(slot, yy, xx, keep):
        def put(cols, total):
            keep[:, cols] = (total + s_recv[slot, :, cols].astype(f32)).astype(keep.dtype)

        product(index(yy, xx, c), put)

    greet((to_x, to_y, to_s))
    s0 = to_sibling(0, 1 - y, 1 - x)
    s1 = to_sibling(1, y, 1 - x)
    s2 = to_sibling(2, 1 - y, x)
    s0.wait_recv()
    with_sibling(0, 1 - y, 1 - x, d_send)
    d0 = hop(4, d_send.at[parts[0]], d_recv.at[parts[0]], to_x)
    d1 = hop(5, d_send.at[parts[1]], d_recv.at[parts[1]], to_y)
    d0.start()
    d1.start()
    s1.wait_recv()
    with_sibling(1, y, 1 - x, x_acc)
    x_send[parts[0]] = x_acc[parts[0]].astype(low)
    x0 = hop(6, x_send.at[parts[0]], x_recv.at[parts[0]], to_x)
    x0.start()
    s2.wait_recv()
    with_sibling(2, 1 - y, x, y_acc)
    y_send[parts[1]] = y_acc[parts[1]].astype(low)
    y1 = hop(7, y_send.at[parts[1]], y_recv.at[parts[1]], to_y)
    y1.start()
    s3 = to_sibling(3, y, x)
    d1.wait_recv()
    x_send[parts[1]] = (x_acc[parts[1]] + d_recv[parts[1]].astype(f32)).astype(low)
    x1 = hop(8, x_send.at[parts[1]], x_recv.at[parts[1]], to_x)
    x1.start()
    d0.wait_recv()
    y_send[parts[0]] = (y_acc[parts[0]] + d_recv[parts[0]].astype(f32)).astype(low)
    y0 = hop(9, y_send.at[parts[0]], y_recv.at[parts[0]], to_y)
    y0.start()
    s3.wait_recv()
    with_sibling(3, y, x, out)
    x0.wait_recv()
    y1.wait_recv()
    x1.wait_recv()
    y0.wait_recv()
    out[...] += x_recv[...].astype(f32) + y_recv[...].astype(f32)
    for copy in (s0, s1, s2, s3, d0, d1, x0, x1, y0, y1):
        copy.wait_send()


def plane_sum(lefts, rights, number, after=(), tile=512):
    pairs = len(lefts)
    rows, width = lefts[0].shape[0] // 8, rights[0].shape[0]
    block = (rows, width)
    low, f32 = jnp.bfloat16, jnp.float32
    depth = sum(a.shape[1] for a in lefts)
    return pl.pallas_call(
        functools.partial(sum_kernel, pairs, min(tile, width)),
        out_shape=jax.ShapeDtypeStruct(block, f32),
        in_specs=[VMEM] * (2 * pairs) + [HBM] * len(after),
        out_specs=VMEM,
        scratch_shapes=[
            pltpu.VMEM((4, *block), low),
            pltpu.VMEM((4, *block), low),
            *[pltpu.VMEM(block, low)] * 6,
            pltpu.VMEM(block, f32),
            pltpu.VMEM(block, f32),
            pltpu.SemaphoreType.DMA((10,)),
            pltpu.SemaphoreType.DMA((10,)),
        ],
        compiler_params=pltpu.CompilerParams(
            collective_id=number, has_side_effects=True, vmem_limit_bytes=48 * 2**20
        ),
        cost_estimate=pl.CostEstimate(flops=1, bytes_accessed=1, transcendentals=0),
        name="plane_sum",
    )(*lefts, *rights, *after)


def swap_kernel(pieces, takes, *refs):
    count = len(pieces)
    sources, (send, recv, own) = refs[: -2 * count - 3], refs[-3:]
    outs, holds = refs[-2 * count - 3 : -count - 3], refs[-count - 3 : -3]
    y, x, c, index = place()
    me = index(y, x, c)
    flips = [(fy, fx, fc) for fy, fx in ((1, 1), (0, 1), (1, 0), (0, 0)) for fc in (0, 1)]
    flips = [flip for flip in flips if flip != (0, 0, 0)]

    def there(flip):
        return tuple(1 - at if f else at for at, f in zip((y, x, c), flip))

    greet([dict(zip(("y", "x", "c"), there(flip))) for flip in flips])
    copies = []
    for piece in range(count):
        for number, flip in enumerate(flips):
            yy, xx, cc = there(flip)
            member = index(yy, xx, cc)
            holds[piece][number] = takes[piece](sources, member, cc)
            copy = pltpu.make_async_remote_copy(
                src_ref=holds[piece].at[number],
                dst_ref=outs[piece].at[me],
                send_sem=send.at[piece * 7 + number],
                recv_sem=recv.at[piece * 7 + number],
                device_id={"y": yy, "x": xx, "c": cc},
                device_id_type=MESH,
            )
            copy.start()
            copies.append(copy)
        holds[piece][7] = takes[piece](sources, me, c)
        keep = pltpu.make_async_copy(holds[piece].at[7], outs[piece].at[me], own.at[piece])
        keep.start()
        copies.append(keep)
    for copy in copies:
        copy.wait()


def plane_swap(sources, shapes, takes, number, after=()):
    low = jnp.bfloat16
    count = len(shapes)
    return pl.pallas_call(
        functools.partial(swap_kernel, shapes, takes),
        out_shape=[jax.ShapeDtypeStruct((8, *shape), low) for shape in shapes],
        in_specs=[VMEM] * len(sources) + [HBM] * len(after),
        out_specs=[HBM] * count,
        scratch_shapes=[
            *[pltpu.VMEM((8, *shape), low) for shape in shapes],
            pltpu.SemaphoreType.DMA((7 * count,)),
            pltpu.SemaphoreType.DMA((7 * count,)),
            pltpu.SemaphoreType.DMA((count,)),
        ],
        compiler_params=pltpu.CompilerParams(
            collective_id=number, has_side_effects=True, vmem_limit_bytes=48 * 2**20
        ),
        cost_estimate=pl.CostEstimate(flops=1, bytes_accessed=1, transcendentals=0),
        name="plane_swap",
    )(*sources, *after)


def total_kernel(planes, src, out, near, far, send, recv):
    y, x, c, index = place()
    z = lax.axis_index("z")
    me = index(y, x, c)
    flips = [(fy, fx, fc) for fy in (0, 1) for fx in (0, 1) for fc in (0, 1)][1:]
    team = [
        dict(zip(("y", "x", "c"), (1 - at if f else at for at, f in zip((y, x, c), flip)))) for flip in flips
    ]
    column = [{"z": lax.rem(z + step, planes)} for step in range(1, planes)]
    near[me] = src[...]
    greet(team + column)

    def spread(buffer, at, others, base):
        copies = [
            pltpu.make_async_remote_copy(
                src_ref=buffer.at[at],
                dst_ref=buffer.at[at],
                send_sem=send.at[base + number],
                recv_sem=recv.at[base + number],
                device_id=other,
                device_id_type=MESH,
            )
            for number, other in enumerate(others)
        ]
        for copy in copies:
            copy.start()
        for copy in copies:
            copy.wait()

    spread(near, me, team, 0)
    far[z] = jnp.sum(near[...], axis=0)
    spread(far, z, column, 7)
    out[...] = jnp.sum(far[...], axis=0)


def total_sum(value, planes, number):
    return pl.pallas_call(
        functools.partial(total_kernel, planes),
        out_shape=jax.ShapeDtypeStruct(value.shape, value.dtype),
        in_specs=[VMEM],
        out_specs=VMEM,
        scratch_shapes=[
            pltpu.VMEM((8, *value.shape), value.dtype),
            pltpu.VMEM((planes, *value.shape), value.dtype),
            pltpu.SemaphoreType.DMA((6 + planes,)),
            pltpu.SemaphoreType.DMA((6 + planes,)),
        ],
        compiler_params=pltpu.CompilerParams(collective_id=number, has_side_effects=True),
        cost_estimate=pl.CostEstimate(flops=1, bytes_accessed=1, transcendentals=0),
        name="total_sum",
    )(value)


def dot(left, right, contract):
    return lax.dot_general(left, right, (contract, ((), ())), preferred_element_type=jnp.float32)


def mm(left, right):
    return dot(left, right, ((1,), (0,)))


def mm_nt(left, right):
    return dot(left, right, ((1,), (1,)))


def mm_tn(left, right):
    return dot(left, right, ((0,), (0,)))


def bmm(pattern, left, right):
    return jnp.einsum(pattern, left, right, preferred_element_type=jnp.float32)


def angle_tables(positions):
    half_dim = HEAD_SIZE // 2
    frequency = rope_base ** (-(jnp.arange(half_dim).astype(jnp.float32) * 2.0) / HEAD_SIZE)
    phases = positions.astype(jnp.float32)[:, None] * frequency[None, :]
    return (jnp.cos(phases), jnp.sin(phases))


def rotate(value, cos_table, sin_table):
    half = value.shape[-1] // 2
    a, b = value[..., :half], value[..., half:]
    return jnp.concatenate([a * cos_table - b * sin_table, b * cos_table + a * sin_table], axis=-1)


def rms_forward(value, gain_row):
    inverse = lax.rsqrt(jnp.mean(value * value, axis=-1, keepdims=True) + norm_eps)
    return (value * inverse * gain_row, inverse)


def rms_back(grad_out, value, inverse, gain_row):
    scaled = grad_out * gain_row
    grad_in = inverse * (
        scaled - value * inverse * inverse * jnp.mean(scaled * value, axis=-1, keepdims=True)
    )
    return (grad_in, jnp.sum(grad_out * value * inverse, axis=0))


def adamw(weight, gradient, moment_one, moment_two, step_rate, decay_rate):
    mean_new = beta_one * moment_one + (1.0 - beta_one) * gradient
    square_new = beta_two * moment_two + (1.0 - beta_two) * gradient * gradient
    direction = (
        mean_new
        / (1.0 - beta_one**STEP)
        / (jnp.sqrt(square_new / (1.0 - beta_two**STEP)) + adam_eps)
    )
    return (weight - step_rate * (direction + decay_rate * weight), mean_new, square_new)


def is_square():
    return lax.axis_size("y") == 2 and lax.axis_size("x") == 2


def swap(blocks):
    return lax.all_to_all(blocks, TEAM, split_axis=0, concat_axis=0, tiled=True)


def over_planes(blocks):
    return lax.all_gather(blocks.reshape(-1, blocks.shape[-1]), "z", axis=0, tiled=True)


def scatter_planes(term):
    return lax.psum_scatter(term, "z", scatter_dimension=0, tiled=True)


def scatter_team(rows, number, after=()):
    if not is_square():
        return swap(rows.reshape(8, -1, rows.shape[-1]))
    count = rows.shape[0] // 8

    def take(sources, member, core):
        return sources[0][pl.ds(pl.multiple_of(member * count, count), count), :]

    return plane_swap([rows], [(count, rows.shape[1])], [take], number, after)[0]


def team_gather(local, number, after=()):
    if not is_square():
        return lax.all_gather(local, TEAM, axis=0, tiled=True)
    return plane_gather(local, number, after).reshape(-1, local.shape[1])


def team_sum(lefts, rights, number, after=()):
    if is_square():
        return plane_sum(lefts, rights, number, after)
    partial = sum(mm_nt(a, w) for a, w in zip(lefts, rights))
    return lax.psum_scatter(partial.astype(jnp.bfloat16), TEAM, scatter_dimension=0, tiled=True).astype(jnp.float32)


def local(
    tokens,
    lengths,
    norm_gains,
    attention_weight,
    feed_weight,
    cotangent,
    attention_mean,
    attention_square,
    feed_mean,
    feed_square,
    gain_mean,
    gain_square,
):
    low = jnp.bfloat16
    sequences, span, width = tokens.shape
    ny, nx, nz = lax.axis_size("y"), lax.axis_size("x"), lax.axis_size("z")
    team = ny * nx * 2
    core = lax.axis_index("c")
    rows = attention_weight.shape[0]
    q_width, kv_width = QUERY_HEADS * HEAD_SIZE, KEY_VALUE_HEADS * HEAD_SIZE
    count = sequences * span
    all_sequences = nx * 2 * sequences
    reach = ny * span
    near = nz <= 4
    ff_part = FF // team

    def columns(start, size):
        return pl.ds(pl.multiple_of(start, size), size)

    def take_attention(sources, member, c):
        source = sources[0]
        starts = (
            member * HEAD_SIZE,
            q_width + c * kv_width + (member - c) // 2 * HEAD_SIZE,
            q_width + 2 * kv_width + member * HEAD_SIZE,
        )
        return jnp.concatenate([source[:, columns(s, HEAD_SIZE)].astype(low) for s in starts], axis=1)

    def take_gate_up(sources, member, c):
        source = sources[0]
        starts = (member * ff_part, FF + member * ff_part)
        return jnp.concatenate([source[:, columns(s, ff_part)].astype(low) for s in starts], axis=1)

    def take_down(sources, member, c):
        return sources[0][:, columns(2 * FF + member * ff_part, ff_part)].astype(low)

    def spread(source, shapes, takes, number, after=()):
        if is_square():
            return plane_swap([source], shapes, takes, number, after)
        return [
            swap(jnp.stack([take([source], member, member % 2) for member in range(8)])) for take in takes
        ]

    (attention_blocks,) = spread(attention_weight, [(rows, 3 * HEAD_SIZE)], [take_attention], 1)
    attention_mine = over_planes(attention_blocks)
    query_weight = attention_mine[:, :HEAD_SIZE]
    kv_weight = attention_mine[:, HEAD_SIZE : 2 * HEAD_SIZE]
    out_weight = attention_mine[:, 2 * HEAD_SIZE :]
    (gate_up_blocks,) = spread(feed_weight, [(rows, 2 * ff_part)], [take_gate_up], 2, [attention_blocks])
    gate_up_weight = over_planes(gate_up_blocks)

    team_base = lax.axis_index("z") * reach
    team_pos = team_base + jnp.arange(reach, dtype=jnp.int32)
    own_pos = team_base + lax.axis_index("y") * span + jnp.arange(span, dtype=jnp.int32)
    if near:
        key_pos = jnp.concatenate([team_base - back * reach + jnp.arange(reach, dtype=jnp.int32) for back in range(nz)])
    else:
        key_pos = jnp.arange(nz * reach, dtype=jnp.int32)
    lengths_all = lax.all_gather(lengths, ("x", "c"), axis=0, tiled=True)
    cos_table, sin_table = angle_tables(team_pos)
    valid = (own_pos[None, :] < lengths[:, None]).astype(jnp.float32).reshape(count, 1)
    allowed = (
        (key_pos[None, None, :] <= team_pos[None, :, None])
        & (key_pos[None, None, :] < lengths_all[:, None, None])
        & (key_pos >= 0)[None, None, :]
    )

    def by_sequence(value):
        return (
            value.reshape(ny, all_sequences, span, -1)
            .transpose(1, 0, 2, 3)
            .reshape(all_sequences, reach, -1)
        )

    def by_device(value):
        return (
            value.reshape(all_sequences, ny, span, -1)
            .transpose(1, 0, 2, 3)
            .reshape(all_sequences * reach, -1)
        )

    x_in = tokens.reshape(count, width).astype(jnp.float32)
    normed_one, inverse_one = rms_forward(x_in, norm_gains[0])
    h1 = team_gather(normed_one.astype(low), 3)
    outer_grad = cotangent.reshape(count, width).astype(jnp.float32) * valid
    dyb = team_gather(outer_grad.astype(low), 15)

    (down_blocks,) = spread(feed_weight, [(rows, ff_part)], [take_down], 12, [h1])
    down_weight = over_planes(down_blocks)
    q = rotate(by_sequence(mm(h1, query_weight)), cos_table, sin_table).astype(low)
    kv_raw = by_sequence(mm(h1, kv_weight))
    kv = jnp.where(core == 0, rotate(kv_raw, cos_table, sin_table), kv_raw).astype(low)
    if near:
        earlier = [
            lax.ppermute(kv, "z", [(at, at + back) for at in range(nz - back)]) for back in range(1, nz)
        ]
        kv = jnp.concatenate([kv, *earlier], axis=1)
    else:
        kv = lax.all_gather(kv, "z", axis=1, tiled=True)
    other = lax.ppermute(kv, "c", [(0, 1), (1, 0)])
    k, v = jnp.where(core == 0, kv, other), jnp.where(core == 0, other, kv)
    scale = HEAD_SIZE ** (-0.5)

    def scores_of():
        return jnp.where(allowed, bmm("spd,std->spt", q, k) * scale, masked_value)

    scores = scores_of()
    row_max = jnp.max(scores, axis=-1, keepdims=True)
    exponent = jnp.exp(scores - row_max)
    soft = exponent / jnp.sum(exponent, axis=-1, keepdims=True)
    soft_low = soft.astype(low)
    o = by_device(bmm("spt,std->spd", soft_low, v).astype(low))
    r = x_in + team_sum([o], [out_weight], 4)

    normed_two, inverse_two = rms_forward(r, norm_gains[1])
    h2 = team_gather(normed_two.astype(low), 16)
    both = mm(h2, gate_up_weight)
    gate, upward = both[:, :ff_part], both[:, ff_part:]
    sig = jax.nn.sigmoid(gate)
    m = (gate * sig * upward).astype(low)
    down_term = mm_tn(dyb, m).astype(low)
    down_rows = scatter_planes(down_term)
    down_weight, down_term = lax.optimization_barrier((down_weight, down_term))

    dm = mm(dyb, down_weight)
    d_gate = (dm * upward * sig * (1.0 + gate * (1.0 - sig))).astype(low)
    d_up = (dm * gate * sig).astype(low)
    d_both = jnp.concatenate([d_gate, d_up], axis=1)
    dh2 = team_sum([d_both], [gate_up_weight], 7, [down_term])
    gate_term, up_term = mm_tn(h2, d_gate).astype(low), mm_tn(h2, d_up).astype(low)
    gate_rows, up_rows = scatter_planes(gate_term), scatter_planes(up_term)
    mid_grad, gain_two = rms_back(dh2, r, inverse_two, norm_gains[1])
    dr = outer_grad + mid_grad
    drb = team_gather(dr.astype(low), 13, [gate_term, up_term, down_rows])

    do = by_sequence(mm(drb, out_weight).astype(low))
    dp = bmm("spd,std->spt", do, v)
    delta = jnp.sum(soft * dp, axis=-1, keepdims=True)
    ds = (soft * (dp - delta) * scale).astype(low)
    dq = by_device(rotate(bmm("spt,std->spd", ds, k), cos_table, -sin_table).astype(low))
    dk_term = bmm("spt,spd->std", ds, q)
    dv_term = bmm("spt,spd->std", soft_low, do)
    feed_sum = team_sum([m], [down_weight], 5, [drb])
    down_grad = scatter_team(down_rows, 6, [drb])
    dk_term, dv_term, gate_rows, feed_sum, down_grad = lax.optimization_barrier(
        (dk_term, dv_term, gate_rows, feed_sum, down_grad)
    )
    layer_output = (r + feed_sum).astype(low)
    mine = jnp.where(core == 0, dk_term, dv_term)
    theirs = jnp.where(core == 0, dv_term, dk_term).astype(low)
    dkv = mine + lax.ppermute(theirs, "c", [(0, 1), (1, 0)]).astype(jnp.float32)
    if near:
        terms = [dkv[:, back * reach : (back + 1) * reach] for back in range(nz)]
        dkv = terms[0]
        for back in range(1, nz):
            pairs = [(at + back, at) for at in range(nz - back)]
            dkv = dkv + lax.ppermute(terms[back].astype(low), "z", pairs).astype(jnp.float32)
    else:
        dkv = lax.psum_scatter(dkv.astype(low), "z", scatter_dimension=1, tiled=True).astype(jnp.float32)
    dkv = by_device(jnp.where(core == 0, rotate(dkv, cos_table, -sin_table), dkv).astype(low))
    kv_term = mm_tn(h1, dkv).astype(low)
    d_qkv = jnp.concatenate([dq, dkv], axis=1)
    dh1 = team_sum([d_qkv], [attention_mine[:, : 2 * HEAD_SIZE]], 9, [kv_term])
    in_grad, gain_one = rms_back(dh1, x_in, inverse_one, norm_gains[0])
    input_gradient = dr + in_grad
    qo_rows = scatter_planes(jnp.concatenate([mm_tn(h1, dq), mm_tn(drb, o)], axis=1).astype(low))
    kv_rows = scatter_planes(kv_term)
    gate_grad, up_grad = scatter_team(gate_rows, 8, [kv_term]), scatter_team(up_rows, 17, [kv_term])
    qo_grad = scatter_team(qo_rows, 10, [kv_term]).astype(jnp.float32)
    kv_grad = scatter_team(kv_rows, 14).astype(jnp.float32)

    def columns_of(blocks):
        return blocks.transpose(1, 0, 2).reshape(rows, -1)

    attention_grad = jnp.concatenate(
        [
            columns_of(qo_grad[:, :, :HEAD_SIZE]),
            kv_grad.reshape(KEY_VALUE_HEADS, 2, rows, HEAD_SIZE).transpose(2, 1, 0, 3).reshape(rows, 2 * kv_width),
            columns_of(qo_grad[:, :, HEAD_SIZE:]),
        ],
        axis=1,
    )
    feed_grad = jnp.concatenate(
        [columns_of(g.astype(jnp.float32)) for g in (gate_grad, up_grad, down_grad)], axis=1
    )
    local_squares = jnp.sum(attention_grad * attention_grad) + jnp.sum(feed_grad * feed_grad)
    gain_local = jnp.stack([gain_one, gain_two])
    if is_square():
        lines = jnp.concatenate([gain_local.reshape(-1, 128), jnp.full((8, 128), local_squares)], axis=0)
        lines = total_sum(lines, nz, 11)
        gain_grad, squares = lines[:-8].reshape(2, width), lines[-1, 0]
    else:
        gain_grad, squares = lax.psum((gain_local, local_squares), ALL)
    gradient_norm = jnp.sqrt(squares + jnp.sum(gain_grad * gain_grad))
    factor = clip_norm / gradient_norm
    attention_new = adamw(
        attention_weight, attention_grad * factor, attention_mean, attention_square, matrix_rate, weight_decay
    )
    feed_new = adamw(feed_weight, feed_grad * factor, feed_mean, feed_square, matrix_rate, weight_decay)
    gains_new = adamw(norm_gains, gain_grad * factor, gain_mean, gain_square, gain_rate, 0.0)
    return (
        layer_output.reshape(sequences, span, width),
        input_gradient.reshape(sequences, span, width),
        gradient_norm,
        *attention_new,
        attention_new[0].astype(low),
        *feed_new,
        feed_new[0].astype(low),
        *gains_new,
    )


def solution(mesh):
    ctx, fsdp = mesh.shape["ctx"], mesh.shape["fsdp"]
    inner = QUERY_HEADS // fsdp
    fine = Mesh(mesh.devices.reshape(ctx // inner, inner, fsdp // 2, 2), ALL)
    act = P(("x", "c"), ("z", "y"), None)
    matrix = P(ALL, None)
    return jax.shard_map(
        local,
        mesh=fine,
        in_specs=(act, P(("x", "c")), P(), matrix, matrix, act, matrix, matrix, matrix, matrix, P(), P()),
        out_specs=(act, act, P(), matrix, matrix, matrix, matrix, matrix, matrix, matrix, matrix, P(), P(), P()),
        check_vma=False,
    )
```

```python
import functools

import jax
import jax.numpy as jnp
from jax import lax
from jax.experimental import pallas as pl
from jax.experimental.pallas import tpu as pltpu
from jax.sharding import Mesh, PartitionSpec as P

QUERY_HEADS = 8
KEY_VALUE_HEADS = 4
HEAD_SIZE = 256
FF = 8192
STEP = 10

norm_eps = 1e-06
rope_base = 1000042.0
masked_value = -1e30
clip_norm = 1.0
beta_one = 0.9
beta_two = 0.95
adam_eps = 1e-08
matrix_rate = 0.03
gain_rate = 0.4
weight_decay = 0.1

TEAM = ("y", "x", "c")
ALL = ("z", "y", "x", "c")


MESH = pl.DeviceIdType.MESH
VMEM = pl.BlockSpec(memory_space=pltpu.VMEM)
HBM = pl.BlockSpec(memory_space=pl.ANY)


def place():
    y, x, c = lax.axis_index("y"), lax.axis_index("x"), lax.axis_index("c")
    return y, x, c, lambda yy, xx, cc: (yy * 2 + xx) * 2 + cc


def greet(others):
    barrier = pltpu.get_barrier_semaphore()
    for other in others:
        pl.semaphore_signal(barrier, inc=1, device_id=other, device_id_type=MESH)
    pl.semaphore_wait(barrier, len(others))


def gather_kernel(src, *refs):
    out, send, recv, own = refs[-4:]
    y, x, c, index = place()
    to_x, to_y, to_s = {"x": 1 - x}, {"y": 1 - y}, {"c": 1 - c}
    me, at_x, at_y, at_d = index(y, x, c), index(y, 1 - x, c), index(1 - y, x, c), index(1 - y, 1 - x, c)
    half = src.shape[0] // 2
    rows = (pl.ds(0, half), pl.ds(half, half))
    local = pltpu.make_async_copy(src, out.at[me], own)
    local.start()
    greet((to_x, to_y, to_s))

    def hop(slot, block, part, where, first=False):
        piece = out.at[block, rows[part]]
        return pltpu.make_async_remote_copy(
            src_ref=src.at[rows[part]] if first else piece,
            dst_ref=piece,
            send_sem=send.at[slot],
            recv_sem=recv.at[slot],
            device_id=where,
            device_id_type=MESH,
        )

    x0, x1 = hop(0, me, 0, to_x, True), hop(1, me, 1, to_x, True)
    y1, y0 = hop(2, me, 1, to_y, True), hop(3, me, 0, to_y, True)
    s0, s1 = hop(4, me, 0, to_s, True), hop(5, me, 1, to_s, True)
    for copy in (x0, y1, x1, y0, s0, s1):
        copy.start()
    x0.wait_recv()
    d0 = hop(6, at_x, 0, to_y)
    d0.start()
    y1.wait_recv()
    d1 = hop(7, at_y, 1, to_x)
    d1.start()
    sx0, sy1 = hop(8, at_x, 0, to_s), hop(9, at_y, 1, to_s)
    sx0.start()
    sy1.start()
    x1.wait_recv()
    sx1 = hop(10, at_x, 1, to_s)
    sx1.start()
    y0.wait_recv()
    sy0 = hop(11, at_y, 0, to_s)
    sy0.start()
    d0.wait_recv()
    sd0 = hop(12, at_d, 0, to_s)
    sd0.start()
    d1.wait_recv()
    sd1 = hop(13, at_d, 1, to_s)
    sd1.start()
    for copy in (s0, s1, sx0, sy1, sx1, sy0, sd0, sd1):
        copy.wait_recv()
    for copy in (x0, x1, y0, y1, s0, s1, d0, d1, sx0, sy1, sx1, sy0, sd0, sd1):
        copy.wait_send()
    local.wait()


def plane_gather(value, number, after=()):
    return pl.pallas_call(
        gather_kernel,
        out_shape=jax.ShapeDtypeStruct((8, *value.shape), value.dtype),
        in_specs=[HBM] * (1 + len(after)),
        out_specs=HBM,
        scratch_shapes=[
            pltpu.SemaphoreType.DMA((14,)),
            pltpu.SemaphoreType.DMA((14,)),
            pltpu.SemaphoreType.DMA,
        ],
        compiler_params=pltpu.CompilerParams(collective_id=number, has_side_effects=True),
        cost_estimate=pl.CostEstimate(flops=1, bytes_accessed=1, transcendentals=0),
        name="plane_gather",
    )(value, *after)


def sum_kernel(lefts, terms, tile, *refs):
    a_refs, w_refs = refs[:lefts], refs[lefts : lefts + len(terms)]
    out, s_send, s_recv, d_send, d_recv, x_send, x_recv, y_send, y_recv, x_acc, y_acc, send, recv = refs[-13:]
    y, x, c, index = place()
    to_x, to_y, to_s = {"x": 1 - x}, {"y": 1 - y}, {"c": 1 - c}
    rows, width = out.shape
    half = rows // 2
    parts = (pl.ds(0, half), pl.ds(half, half))
    f32, low = jnp.float32, jnp.bfloat16

    def product(block, put):
        lines = pl.ds(pl.multiple_of(block * rows, rows), rows)

        @pl.loop(0, width // tile)
        def _(step):
            cols = pl.ds(pl.multiple_of(step * tile, tile), tile)
            total = None
            for (left, start), w_ref in zip(terms, w_refs):
                term = mm_nt(a_refs[left][lines, start : start + w_ref.shape[1]], w_ref[cols, :])
                total = term if total is None else total + term
            put(cols, total)

    def hop(slot, src, dst, where):
        copy = pltpu.make_async_remote_copy(
            src_ref=src, dst_ref=dst, send_sem=send.at[slot], recv_sem=recv.at[slot],
            device_id=where, device_id_type=MESH,
        )
        return copy

    def to_sibling(slot, yy, xx):
        def put(cols, total):
            s_send[slot, :, cols] = total.astype(low)

        product(index(yy, xx, 1 - c), put)
        copy = hop(slot, s_send.at[slot], s_recv.at[slot], to_s)
        copy.start()
        return copy

    def with_sibling(slot, yy, xx, keep):
        def put(cols, total):
            keep[:, cols] = (total + s_recv[slot, :, cols].astype(f32)).astype(keep.dtype)

        product(index(yy, xx, c), put)

    greet((to_x, to_y, to_s))
    s0 = to_sibling(0, 1 - y, 1 - x)
    s1 = to_sibling(1, y, 1 - x)
    s2 = to_sibling(2, 1 - y, x)
    s0.wait_recv()
    with_sibling(0, 1 - y, 1 - x, d_send)
    d0 = hop(4, d_send.at[parts[0]], d_recv.at[parts[0]], to_x)
    d1 = hop(5, d_send.at[parts[1]], d_recv.at[parts[1]], to_y)
    d0.start()
    d1.start()
    s1.wait_recv()
    with_sibling(1, y, 1 - x, x_acc)
    x_send[parts[0]] = x_acc[parts[0]].astype(low)
    x0 = hop(6, x_send.at[parts[0]], x_recv.at[parts[0]], to_x)
    x0.start()
    s2.wait_recv()
    with_sibling(2, 1 - y, x, y_acc)
    y_send[parts[1]] = y_acc[parts[1]].astype(low)
    y1 = hop(7, y_send.at[parts[1]], y_recv.at[parts[1]], to_y)
    y1.start()
    s3 = to_sibling(3, y, x)
    d1.wait_recv()
    x_send[parts[1]] = (x_acc[parts[1]] + d_recv[parts[1]].astype(f32)).astype(low)
    x1 = hop(8, x_send.at[parts[1]], x_recv.at[parts[1]], to_x)
    x1.start()
    d0.wait_recv()
    y_send[parts[0]] = (y_acc[parts[0]] + d_recv[parts[0]].astype(f32)).astype(low)
    y0 = hop(9, y_send.at[parts[0]], y_recv.at[parts[0]], to_y)
    y0.start()
    s3.wait_recv()
    with_sibling(3, y, x, out)
    x0.wait_recv()
    y1.wait_recv()
    x1.wait_recv()
    y0.wait_recv()
    out[...] += x_recv[...].astype(f32) + y_recv[...].astype(f32)
    for copy in (s0, s1, s2, s3, d0, d1, x0, x1, y0, y1):
        copy.wait_send()


def plane_sum(lefts, rights, number, after=(), tile=512):
    ends = [(left, start) for left, a in enumerate(lefts) for start in range(0, a.shape[1], rights[0].shape[1])]
    terms = tuple(ends[: len(rights)])
    rows, width = lefts[0].shape[0] // 8, rights[0].shape[0]
    block = (rows, width)
    low, f32 = jnp.bfloat16, jnp.float32
    return pl.pallas_call(
        functools.partial(sum_kernel, len(lefts), terms, min(tile, width)),
        out_shape=jax.ShapeDtypeStruct(block, f32),
        in_specs=[VMEM] * (len(lefts) + len(rights)) + [HBM] * len(after),
        out_specs=VMEM,
        scratch_shapes=[
            pltpu.VMEM((4, *block), low),
            pltpu.VMEM((4, *block), low),
            *[pltpu.VMEM(block, low)] * 6,
            pltpu.VMEM(block, f32),
            pltpu.VMEM(block, f32),
            pltpu.SemaphoreType.DMA((10,)),
            pltpu.SemaphoreType.DMA((10,)),
        ],
        compiler_params=pltpu.CompilerParams(
            collective_id=number, has_side_effects=True, vmem_limit_bytes=48 * 2**20
        ),
        cost_estimate=pl.CostEstimate(flops=1, bytes_accessed=1, transcendentals=0),
        name="plane_sum",
    )(*lefts, *rights, *after)


def swap_kernel(pieces, takes, *refs):
    count = len(pieces)
    sources, (send, recv, own) = refs[: -2 * count - 3], refs[-3:]
    outs, holds = refs[-2 * count - 3 : -count - 3], refs[-count - 3 : -3]
    y, x, c, index = place()
    me = index(y, x, c)
    flips = [(fy, fx, fc) for fy, fx in ((1, 1), (0, 1), (1, 0), (0, 0)) for fc in (0, 1)]
    flips = [flip for flip in flips if flip != (0, 0, 0)]

    def there(flip):
        return tuple(1 - at if f else at for at, f in zip((y, x, c), flip))

    greet([dict(zip(("y", "x", "c"), there(flip))) for flip in flips])
    copies = []
    for piece in range(count):
        for number, flip in enumerate(flips):
            yy, xx, cc = there(flip)
            member = index(yy, xx, cc)
            holds[piece][number] = takes[piece](sources, member, cc)
            copy = pltpu.make_async_remote_copy(
                src_ref=holds[piece].at[number],
                dst_ref=outs[piece].at[me],
                send_sem=send.at[piece * 7 + number],
                recv_sem=recv.at[piece * 7 + number],
                device_id={"y": yy, "x": xx, "c": cc},
                device_id_type=MESH,
            )
            copy.start()
            copies.append(copy)
        holds[piece][7] = takes[piece](sources, me, c)
        keep = pltpu.make_async_copy(holds[piece].at[7], outs[piece].at[me], own.at[piece])
        keep.start()
        copies.append(keep)
    for copy in copies:
        copy.wait()


def plane_swap(sources, shapes, takes, number, after=()):
    low = jnp.bfloat16
    count = len(shapes)
    return pl.pallas_call(
        functools.partial(swap_kernel, shapes, takes),
        out_shape=[jax.ShapeDtypeStruct((8, *shape), low) for shape in shapes],
        in_specs=[VMEM] * len(sources) + [HBM] * len(after),
        out_specs=[HBM] * count,
        scratch_shapes=[
            *[pltpu.VMEM((8, *shape), low) for shape in shapes],
            pltpu.SemaphoreType.DMA((7 * count,)),
            pltpu.SemaphoreType.DMA((7 * count,)),
            pltpu.SemaphoreType.DMA((count,)),
        ],
        compiler_params=pltpu.CompilerParams(
            collective_id=number, has_side_effects=True, vmem_limit_bytes=48 * 2**20
        ),
        cost_estimate=pl.CostEstimate(flops=1, bytes_accessed=1, transcendentals=0),
        name="plane_swap",
    )(*sources, *after)


def total_kernel(planes, src, out, near, far, send, recv):
    y, x, c, index = place()
    z = lax.axis_index("z")
    me = index(y, x, c)
    flips = [(fy, fx, fc) for fy in (0, 1) for fx in (0, 1) for fc in (0, 1)][1:]
    team = [
        dict(zip(("y", "x", "c"), (1 - at if f else at for at, f in zip((y, x, c), flip)))) for flip in flips
    ]
    column = [{"z": lax.rem(z + step, planes)} for step in range(1, planes)]
    near[me] = src[...]
    greet(team + column)

    def spread(buffer, at, others, base):
        copies = [
            pltpu.make_async_remote_copy(
                src_ref=buffer.at[at],
                dst_ref=buffer.at[at],
                send_sem=send.at[base + number],
                recv_sem=recv.at[base + number],
                device_id=other,
                device_id_type=MESH,
            )
            for number, other in enumerate(others)
        ]
        for copy in copies:
            copy.start()
        for copy in copies:
            copy.wait()

    spread(near, me, team, 0)
    far[z] = jnp.sum(near[...], axis=0)
    spread(far, z, column, 7)
    out[...] = jnp.sum(far[...], axis=0)


def total_sum(value, planes, number):
    return pl.pallas_call(
        functools.partial(total_kernel, planes),
        out_shape=jax.ShapeDtypeStruct(value.shape, value.dtype),
        in_specs=[VMEM],
        out_specs=VMEM,
        scratch_shapes=[
            pltpu.VMEM((8, *value.shape), value.dtype),
            pltpu.VMEM((planes, *value.shape), value.dtype),
            pltpu.SemaphoreType.DMA((6 + planes,)),
            pltpu.SemaphoreType.DMA((6 + planes,)),
        ],
        compiler_params=pltpu.CompilerParams(collective_id=number, has_side_effects=True),
        cost_estimate=pl.CostEstimate(flops=1, bytes_accessed=1, transcendentals=0),
        name="total_sum",
    )(value)


def dot(left, right, contract):
    return lax.dot_general(left, right, (contract, ((), ())), preferred_element_type=jnp.float32)


def mm(left, right):
    return dot(left, right, ((1,), (0,)))


def mm_nt(left, right):
    return dot(left, right, ((1,), (1,)))


def mm_tn(left, right):
    return dot(left, right, ((0,), (0,)))


def bmm(pattern, left, right):
    return jnp.einsum(pattern, left, right, preferred_element_type=jnp.float32)


def angle_tables(positions):
    half_dim = HEAD_SIZE // 2
    frequency = rope_base ** (-(jnp.arange(half_dim).astype(jnp.float32) * 2.0) / HEAD_SIZE)
    phases = positions.astype(jnp.float32)[:, None] * frequency[None, :]
    return (jnp.cos(phases), jnp.sin(phases))


def rotate(value, cos_table, sin_table):
    half = value.shape[-1] // 2
    a, b = value[..., :half], value[..., half:]
    return jnp.concatenate([a * cos_table - b * sin_table, b * cos_table + a * sin_table], axis=-1)


def rms_forward(value, gain_row):
    inverse = lax.rsqrt(jnp.mean(value * value, axis=-1, keepdims=True) + norm_eps)
    return (value * inverse * gain_row, inverse)


def rms_back(grad_out, value, inverse, gain_row):
    scaled = grad_out * gain_row
    grad_in = inverse * (
        scaled - value * inverse * inverse * jnp.mean(scaled * value, axis=-1, keepdims=True)
    )
    return (grad_in, jnp.sum(grad_out * value * inverse, axis=0))


def adamw(weight, gradient, moment_one, moment_two, step_rate, decay_rate):
    mean_new = beta_one * moment_one + (1.0 - beta_one) * gradient
    square_new = beta_two * moment_two + (1.0 - beta_two) * gradient * gradient
    direction = (
        mean_new
        / (1.0 - beta_one**STEP)
        / (jnp.sqrt(square_new / (1.0 - beta_two**STEP)) + adam_eps)
    )
    return (weight - step_rate * (direction + decay_rate * weight), mean_new, square_new)


def attention_parts(core, length, q_ref, mine_ref, other_ref, query_ref, key_ref):
    mine, other = mine_ref[...].reshape(-1, HEAD_SIZE), other_ref[...].reshape(-1, HEAD_SIZE)
    first = core == 0
    k, v = jnp.where(first, mine, other), jnp.where(first, other, mine)
    q = q_ref[...].reshape(-1, HEAD_SIZE)
    at, key_at = query_ref[...], key_ref[...]
    allowed = (key_at <= at) & (key_at < length) & (key_at >= 0)
    scores = jnp.where(allowed, mm_nt(q, k) * HEAD_SIZE ** (-0.5), masked_value)
    exponent = jnp.exp(scores - jnp.max(scores, axis=-1, keepdims=True))
    return q, k, v, exponent / jnp.sum(exponent, axis=-1, keepdims=True)


def attention_kernel(core_ref, length_ref, q_ref, mine_ref, other_ref, query_ref, key_ref, out_ref):
    length = length_ref[pl.program_id(0)]
    _, _, v, soft = attention_parts(core_ref[0], length, q_ref, mine_ref, other_ref, query_ref, key_ref)
    out_ref[...] = mm(soft.astype(jnp.bfloat16), v).astype(jnp.bfloat16).reshape(out_ref.shape)


def attention_back_kernel(
    core_ref, length_ref, q_ref, mine_ref, other_ref, query_ref, key_ref, do_ref, cos_ref, sin_ref,
    dq_ref, keep_ref, send_ref,
):
    low = jnp.bfloat16
    core = core_ref[0]
    length = length_ref[pl.program_id(0)]
    q, k, v, soft = attention_parts(core, length, q_ref, mine_ref, other_ref, query_ref, key_ref)
    do = do_ref[...].reshape(-1, HEAD_SIZE)
    dp = mm_nt(do, v)
    delta = jnp.sum(soft * dp, axis=-1, keepdims=True)
    ds = (soft * (dp - delta) * HEAD_SIZE ** (-0.5)).astype(low)
    dq = mm(ds, k)
    cos_table, sin_table = cos_ref[...], sin_ref[...]
    half = HEAD_SIZE // 2
    a, b = dq[:, :half], dq[:, half:]
    turned = jnp.concatenate([a * cos_table + b * sin_table, b * cos_table - a * sin_table], axis=-1)
    dq_ref[...] = turned.astype(low).reshape(dq_ref.shape)
    dk, dv = mm_tn(ds, q), mm_tn(soft.astype(low), do)
    first = core == 0
    keep_ref[...] = jnp.where(first, dk, dv).reshape(keep_ref.shape)
    send_ref[...] = jnp.where(first, dv, dk).astype(low).reshape(send_ref.shape)


def attention_call(kernel, core, lengths, q, mine, other, query_pos, key_pos, extra, outs, name):
    ny, count, span, size = q.shape
    nz = mine.shape[0]
    rows = pl.BlockSpec((ny, 1, span, size), lambda i, *_: (0, i, 0, 0))
    keys = pl.BlockSpec((nz, ny, 1, span, size), lambda i, *_: (0, 0, i, 0, 0))

    def whole(value):
        return pl.BlockSpec(value.shape, lambda i, *_: (0,) * value.ndim)

    kinds = {"rows": (rows, q.shape), "keys": (keys, mine.shape)}
    return pl.pallas_call(
        kernel,
        grid_spec=pltpu.PrefetchScalarGridSpec(
            num_scalar_prefetch=2,
            grid=(count,),
            in_specs=[rows, keys, keys, whole(query_pos), whole(key_pos)]
            + [rows if value.shape == q.shape else whole(value) for value in extra],
            out_specs=[kinds[kind][0] for kind, _ in outs],
        ),
        out_shape=[jax.ShapeDtypeStruct(kinds[kind][1], dtype) for kind, dtype in outs],
        compiler_params=pltpu.CompilerParams(vmem_limit_bytes=48 * 2**20),
        cost_estimate=pl.CostEstimate(
            flops=10 * q.size * nz * ny * span, bytes_accessed=8 * mine.size, transcendentals=0
        ),
        name=name,
    )(core, lengths, q, mine, other, query_pos, key_pos, *extra)


def feed_back_kernel(dyb_ref, weight_ref, gate_ref, up_ref, out_ref):
    dm = mm(dyb_ref[...], weight_ref[...])
    gate, upward = gate_ref[...], up_ref[...]
    sig = jax.nn.sigmoid(gate)
    part = gate.shape[1]
    out_ref[:, :part] = (dm * upward * sig * (1.0 + gate * (1.0 - sig))).astype(out_ref.dtype)
    out_ref[:, part:] = (dm * gate * sig).astype(out_ref.dtype)


def feed_back(dyb, weight, gate, upward, lines=256):
    count, part = gate.shape

    def rows(width):
        return pl.BlockSpec((lines, width), lambda i: (i, 0))

    return pl.pallas_call(
        feed_back_kernel,
        grid=(count // lines,),
        in_specs=[rows(dyb.shape[1]), pl.BlockSpec(weight.shape, lambda i: (0, 0)), rows(part), rows(part)],
        out_specs=rows(2 * part),
        out_shape=jax.ShapeDtypeStruct((count, 2 * part), jnp.bfloat16),
        compiler_params=pltpu.CompilerParams(vmem_limit_bytes=48 * 2**20),
        cost_estimate=pl.CostEstimate(
            flops=2 * count * weight.size, bytes_accessed=12 * count * part, transcendentals=0
        ),
        name="feed_back",
    )(dyb, weight, gate, upward)


def is_square():
    return lax.axis_size("y") == 2 and lax.axis_size("x") == 2


def swap(blocks):
    return lax.all_to_all(blocks, TEAM, split_axis=0, concat_axis=0, tiled=True)


def over_planes(blocks):
    return lax.all_gather(blocks.reshape(-1, blocks.shape[-1]), "z", axis=0, tiled=True)


def scatter_planes(term):
    return lax.psum_scatter(term, "z", scatter_dimension=0, tiled=True)


def scatter_team(rows, number, after=()):
    if not is_square():
        return swap(rows.reshape(8, -1, rows.shape[-1]))
    count = rows.shape[0] // 8

    def take(sources, member, core):
        return sources[0][pl.ds(pl.multiple_of(member * count, count), count), :]

    return plane_swap([rows], [(count, rows.shape[1])], [take], number, after)[0]


def team_gather(local, number, after=()):
    if not is_square():
        return lax.all_gather(local, TEAM, axis=0, tiled=True)
    return plane_gather(local, number, after).reshape(-1, local.shape[1])


def team_sum(lefts, rights, number, after=()):
    if is_square():
        return plane_sum(lefts, rights, number, after)
    partial = mm_nt(jnp.concatenate(lefts, axis=1), jnp.concatenate(rights, axis=1))
    return lax.psum_scatter(partial.astype(jnp.bfloat16), TEAM, scatter_dimension=0, tiled=True).astype(jnp.float32)


def local(
    tokens,
    lengths,
    norm_gains,
    attention_weight,
    feed_weight,
    cotangent,
    attention_mean,
    attention_square,
    feed_mean,
    feed_square,
    gain_mean,
    gain_square,
):
    low = jnp.bfloat16
    sequences, span, width = tokens.shape
    ny, nx, nz = lax.axis_size("y"), lax.axis_size("x"), lax.axis_size("z")
    team = ny * nx * 2
    core = lax.axis_index("c")
    rows = attention_weight.shape[0]
    q_width, kv_width = QUERY_HEADS * HEAD_SIZE, KEY_VALUE_HEADS * HEAD_SIZE
    count = sequences * span
    all_sequences = nx * 2 * sequences
    reach = ny * span
    near = nz <= 4
    ff_part = FF // team

    def columns(start, size):
        return pl.ds(pl.multiple_of(start, size), size)

    def take_attention(sources, member, c):
        source = sources[0]
        starts = (
            member * HEAD_SIZE,
            q_width + c * kv_width + (member - c) // 2 * HEAD_SIZE,
            q_width + 2 * kv_width + member * HEAD_SIZE,
        )
        return jnp.concatenate([source[:, columns(s, HEAD_SIZE)].astype(low) for s in starts], axis=1)

    def take_feed(part):
        return lambda sources, member, c: sources[0][
            :, columns(part * FF + member * ff_part, ff_part)
        ].astype(low)

    def spread(source, take, size, number, after=()):
        if is_square():
            blocks = plane_swap([source], [(rows, size)], [take], number, after)[0]
        else:
            blocks = swap(jnp.stack([take([source], member, member % 2) for member in range(8)]))
        return blocks, over_planes(blocks)

    attention_blocks, attention_mine = spread(attention_weight, take_attention, 3 * HEAD_SIZE, 1)
    gate_blocks, gate_weight = spread(feed_weight, take_feed(0), ff_part, 2, [attention_blocks])

    team_base = lax.axis_index("z") * reach
    team_pos = team_base + jnp.arange(reach, dtype=jnp.int32)
    own_pos = team_base + lax.axis_index("y") * span + jnp.arange(span, dtype=jnp.int32)
    if near:
        key_pos = jnp.concatenate([team_pos - back * reach for back in range(nz)])
    else:
        key_pos = jnp.arange(nz * reach, dtype=jnp.int32)
    query_at, key_at = team_pos[:, None], key_pos[None, :]
    cos_table, sin_table = angle_tables(team_pos)
    cos_rows, sin_rows = (t.reshape(ny, 1, span, -1) for t in (cos_table, sin_table))
    valid = (own_pos[None, :] < lengths[:, None]).astype(jnp.float32).reshape(count, 1)
    lengths_all = lax.all_gather(lengths, ("x", "c"), axis=0, tiled=True)
    core_at = jnp.reshape(core, (1,)).astype(jnp.int32)

    def heads(value):
        return value.reshape(ny, all_sequences, span, HEAD_SIZE)

    x_in = tokens.reshape(count, width).astype(jnp.float32)
    normed_one, inverse_one = rms_forward(x_in, norm_gains[0])
    outer_grad = cotangent.reshape(count, width).astype(jnp.float32) * valid
    h1 = team_gather(normed_one.astype(low), 3, [gate_blocks])
    up_blocks, up_weight = spread(feed_weight, take_feed(1), ff_part, 18, [h1])
    attention_mine, up_blocks, lengths_all = lax.optimization_barrier((attention_mine, up_blocks, lengths_all))
    query_weight = attention_mine[:, :HEAD_SIZE]
    kv_weight = attention_mine[:, HEAD_SIZE : 2 * HEAD_SIZE]
    out_weight = attention_mine[:, 2 * HEAD_SIZE :]
    kv_raw = heads(mm(h1, kv_weight))
    kv = jnp.where(core == 0, rotate(kv_raw, cos_rows, sin_rows), kv_raw).astype(low)
    q = rotate(heads(mm(h1, query_weight)), cos_rows, sin_rows).astype(low)
    dyb = team_gather(outer_grad.astype(low), 15, [kv])
    down_blocks, down_weight = spread(feed_weight, take_feed(2), ff_part, 12, [dyb])
    if near:
        earlier = [
            lax.ppermute(kv, "z", [(at, at + back) for at in range(nz - back)]) for back in range(1, nz)
        ]
        *earlier, dyb, down_blocks, q = lax.optimization_barrier((*earlier, dyb, down_blocks, q))
        kv = jnp.stack([kv, *earlier])
    else:
        kv = lax.all_gather(kv, "z", axis=0, tiled=False)
    other = lax.ppermute(kv, "c", [(0, 1), (1, 0)])
    attend = (core_at, lengths_all, q, kv, other, query_at, key_at)
    (o,) = attention_call(attention_kernel, *attend, (), [("rows", low)], "attention")
    o = o.reshape(-1, HEAD_SIZE)
    r = x_in + team_sum([o], [out_weight], 4)

    normed_two, inverse_two = rms_forward(r, norm_gains[1])
    h2 = team_gather(normed_two.astype(low), 16)
    gate, upward = mm(h2, gate_weight), mm(h2, up_weight)
    sig = jax.nn.sigmoid(gate)
    m = (gate * sig * upward).astype(low)
    down_term = mm_tn(dyb, m).astype(low)
    down_rows = scatter_planes(down_term)
    down_weight, down_term = lax.optimization_barrier((down_weight, down_term))
    d_both = feed_back(dyb, down_weight, gate, upward)
    dh2 = team_sum([d_both], [gate_weight, up_weight], 7, [down_term])
    gate_up_term = mm_tn(h2, d_both).astype(low)
    gate_up_rows = scatter_planes(gate_up_term)
    mid_grad, gain_two = rms_back(dh2, r, inverse_two, norm_gains[1])
    dr = outer_grad + mid_grad
    drb = team_gather(dr.astype(low), 13, [gate_up_term, down_rows])

    do = heads(mm(drb, out_weight).astype(low))
    dq, keep, theirs = attention_call(
        attention_back_kernel,
        *attend,
        (do, cos_table, sin_table),
        [("rows", low), ("keys", jnp.float32), ("keys", low)],
        "attention_back",
    )
    dq = dq.reshape(-1, HEAD_SIZE)
    dkv = keep + lax.ppermute(theirs, "c", [(0, 1), (1, 0)]).astype(jnp.float32)
    low_terms = dkv.astype(low)
    feed_sum = team_sum([m], [down_weight], 5, [theirs])
    layer_output = (r + feed_sum).astype(low)
    down_grad = scatter_team(down_rows, 6, [theirs])
    low_terms, gate_up_rows, feed_sum, down_grad = lax.optimization_barrier(
        (low_terms, gate_up_rows, feed_sum, down_grad)
    )
    gate_up_grad = scatter_team(gate_up_rows, 8, [low_terms])
    if near:
        later = [
            lax.ppermute(low_terms[back], "z", [(at + back, at) for at in range(nz - back)])
            for back in range(1, nz)
        ]
        *later, gate_up_grad = lax.optimization_barrier((*later, gate_up_grad))
        dkv = dkv[0] + sum(term.astype(jnp.float32) for term in later)
    else:
        dkv = lax.psum_scatter(low_terms, "z", scatter_dimension=0, tiled=True)[0].astype(jnp.float32)
    dkv = jnp.where(core == 0, rotate(dkv, cos_rows, -sin_rows), dkv).astype(low).reshape(-1, HEAD_SIZE)
    qo_rows = scatter_planes(jnp.concatenate([mm_tn(h1, dq), mm_tn(drb, o)], axis=1).astype(low))
    kv_term = mm_tn(h1, dkv).astype(low)
    kv_rows = scatter_planes(kv_term)
    dh1 = team_sum([dq, dkv], [query_weight, kv_weight], 9, [kv_term])
    in_grad, gain_one = rms_back(dh1, x_in, inverse_one, norm_gains[0])
    input_gradient = dr + in_grad
    qo_grad = scatter_team(qo_rows, 10, [kv_term]).astype(jnp.float32)
    kv_grad = scatter_team(kv_rows, 14).astype(jnp.float32)

    def columns_of(blocks):
        return blocks.transpose(1, 0, 2).reshape(rows, -1)

    attention_grad = jnp.concatenate(
        [
            columns_of(qo_grad[:, :, :HEAD_SIZE]),
            kv_grad.reshape(KEY_VALUE_HEADS, 2, rows, HEAD_SIZE).transpose(2, 1, 0, 3).reshape(rows, 2 * kv_width),
            columns_of(qo_grad[:, :, HEAD_SIZE:]),
        ],
        axis=1,
    )
    feed_grad = jnp.concatenate(
        [
            columns_of(g.astype(jnp.float32))
            for g in (gate_up_grad[:, :, :ff_part], gate_up_grad[:, :, ff_part:], down_grad)
        ], axis=1
    )
    local_squares = jnp.sum(attention_grad * attention_grad) + jnp.sum(feed_grad * feed_grad)
    gain_local = jnp.stack([gain_one, gain_two])
    if is_square():
        lines = jnp.concatenate([gain_local.reshape(-1, 128), jnp.full((8, 128), local_squares)], axis=0)
        lines = total_sum(lines, nz, 11)
        gain_grad, squares = lines[:-8].reshape(2, width), lines[-1, 0]
    else:
        gain_grad, squares = lax.psum((gain_local, local_squares), ALL)
    gradient_norm = jnp.sqrt(squares + jnp.sum(gain_grad * gain_grad))
    factor = clip_norm / gradient_norm
    attention_new = adamw(
        attention_weight, attention_grad * factor, attention_mean, attention_square, matrix_rate, weight_decay
    )
    feed_new = adamw(feed_weight, feed_grad * factor, feed_mean, feed_square, matrix_rate, weight_decay)
    gains_new = adamw(norm_gains, gain_grad * factor, gain_mean, gain_square, gain_rate, 0.0)
    return (
        layer_output.reshape(sequences, span, width),
        input_gradient.reshape(sequences, span, width),
        gradient_norm,
        *attention_new,
        attention_new[0].astype(low),
        *feed_new,
        feed_new[0].astype(low),
        *gains_new,
    )


def solution(mesh):
    ctx, fsdp = mesh.shape["ctx"], mesh.shape["fsdp"]
    inner = QUERY_HEADS // fsdp
    fine = Mesh(mesh.devices.reshape(ctx // inner, inner, fsdp // 2, 2), ALL)
    act = P(("x", "c"), ("z", "y"), None)
    matrix = P(ALL, None)
    return jax.shard_map(
        local,
        mesh=fine,
        in_specs=(act, P(("x", "c")), P(), matrix, matrix, act, matrix, matrix, matrix, matrix, P(), P()),
        out_specs=(act, act, P(), matrix, matrix, matrix, matrix, matrix, matrix, matrix, matrix, P(), P(), P()),
        check_vma=False,
    )
```

```python
import functools

import jax
import jax.numpy as jnp
from jax import lax
from jax.experimental import pallas as pl
from jax.experimental.pallas import tpu as pltpu
from jax.sharding import Mesh, PartitionSpec as P

QUERY_HEADS = 8
KEY_VALUE_HEADS = 4
HEAD_SIZE = 256
FF = 8192
STEP = 10

norm_eps = 1e-06
rope_base = 1000042.0
masked_value = -1e30
clip_norm = 1.0
beta_one = 0.9
beta_two = 0.95
adam_eps = 1e-08
matrix_rate = 0.03
gain_rate = 0.4
weight_decay = 0.1

TEAM = ("y", "x", "c")
ALL = ("z", "y", "x", "c")


MESH = pl.DeviceIdType.MESH
VMEM = pl.BlockSpec(memory_space=pltpu.VMEM)
HBM = pl.BlockSpec(memory_space=pl.ANY)


def place():
    y, x, c = lax.axis_index("y"), lax.axis_index("x"), lax.axis_index("c")
    return y, x, c, lambda yy, xx, cc: (yy * 2 + xx) * 2 + cc


def greet(others):
    barrier = pltpu.get_barrier_semaphore()
    for other in others:
        pl.semaphore_signal(barrier, inc=1, device_id=other, device_id_type=MESH)
    pl.semaphore_wait(barrier, len(others))


def gather_kernel(src, *refs):
    out, send, recv, own = refs[-4:]
    y, x, c, index = place()
    to_x, to_y, to_s = {"x": 1 - x}, {"y": 1 - y}, {"c": 1 - c}
    me, at_x, at_y, at_d = index(y, x, c), index(y, 1 - x, c), index(1 - y, x, c), index(1 - y, 1 - x, c)
    half = src.shape[0] // 2
    rows = (pl.ds(0, half), pl.ds(half, half))
    local = pltpu.make_async_copy(src, out.at[me], own)
    local.start()
    greet((to_x, to_y, to_s))

    def hop(slot, block, part, where, first=False):
        piece = out.at[block, rows[part]]
        return pltpu.make_async_remote_copy(
            src_ref=src.at[rows[part]] if first else piece,
            dst_ref=piece,
            send_sem=send.at[slot],
            recv_sem=recv.at[slot],
            device_id=where,
            device_id_type=MESH,
        )

    x0, x1 = hop(0, me, 0, to_x, True), hop(1, me, 1, to_x, True)
    y1, y0 = hop(2, me, 1, to_y, True), hop(3, me, 0, to_y, True)
    s0, s1 = hop(4, me, 0, to_s, True), hop(5, me, 1, to_s, True)
    for copy in (x0, y1, x1, y0, s0, s1):
        copy.start()
    x0.wait_recv()
    d0 = hop(6, at_x, 0, to_y)
    d0.start()
    y1.wait_recv()
    d1 = hop(7, at_y, 1, to_x)
    d1.start()
    sx0, sy1 = hop(8, at_x, 0, to_s), hop(9, at_y, 1, to_s)
    sx0.start()
    sy1.start()
    x1.wait_recv()
    sx1 = hop(10, at_x, 1, to_s)
    sx1.start()
    y0.wait_recv()
    sy0 = hop(11, at_y, 0, to_s)
    sy0.start()
    d0.wait_recv()
    sd0 = hop(12, at_d, 0, to_s)
    sd0.start()
    d1.wait_recv()
    sd1 = hop(13, at_d, 1, to_s)
    sd1.start()
    for copy in (s0, s1, sx0, sy1, sx1, sy0, sd0, sd1):
        copy.wait_recv()
    for copy in (x0, x1, y0, y1, s0, s1, d0, d1, sx0, sy1, sx1, sy0, sd0, sd1):
        copy.wait_send()
    local.wait()


def plane_gather(value, number, after=()):
    return pl.pallas_call(
        gather_kernel,
        out_shape=jax.ShapeDtypeStruct((8, *value.shape), value.dtype),
        in_specs=[HBM] * (1 + len(after)),
        out_specs=HBM,
        scratch_shapes=[
            pltpu.SemaphoreType.DMA((14,)),
            pltpu.SemaphoreType.DMA((14,)),
            pltpu.SemaphoreType.DMA,
        ],
        compiler_params=pltpu.CompilerParams(collective_id=number, has_side_effects=True),
        cost_estimate=pl.CostEstimate(flops=1, bytes_accessed=1, transcendentals=0),
        name="plane_gather",
    )(value, *after)


def sum_kernel(lefts, terms, tile, *refs):
    a_refs, w_refs = refs[:lefts], refs[lefts : lefts + len(terms)]
    out, s_send, s_recv, d_send, d_recv, x_send, x_recv, y_send, y_recv, x_acc, y_acc, send, recv = refs[-13:]
    y, x, c, index = place()
    to_x, to_y, to_s = {"x": 1 - x}, {"y": 1 - y}, {"c": 1 - c}
    rows, width = out.shape
    half = rows // 2
    parts = (pl.ds(0, half), pl.ds(half, half))
    f32, low = jnp.float32, jnp.bfloat16

    def product(block, put):
        lines = pl.ds(pl.multiple_of(block * rows, rows), rows)

        @pl.loop(0, width // tile)
        def _(step):
            cols = pl.ds(pl.multiple_of(step * tile, tile), tile)
            total = None
            for (left, start), w_ref in zip(terms, w_refs):
                term = mm_nt(a_refs[left][lines, start : start + w_ref.shape[1]], w_ref[cols, :])
                total = term if total is None else total + term
            put(cols, total)

    def hop(slot, src, dst, where):
        copy = pltpu.make_async_remote_copy(
            src_ref=src, dst_ref=dst, send_sem=send.at[slot], recv_sem=recv.at[slot],
            device_id=where, device_id_type=MESH,
        )
        return copy

    def to_sibling(slot, yy, xx):
        def put(cols, total):
            s_send[slot, :, cols] = total.astype(low)

        product(index(yy, xx, 1 - c), put)
        copy = hop(slot, s_send.at[slot], s_recv.at[slot], to_s)
        copy.start()
        return copy

    def with_sibling(slot, yy, xx, keep):
        def put(cols, total):
            keep[:, cols] = (total + s_recv[slot, :, cols].astype(f32)).astype(keep.dtype)

        product(index(yy, xx, c), put)

    greet((to_x, to_y, to_s))
    s0 = to_sibling(0, 1 - y, 1 - x)
    s1 = to_sibling(1, y, 1 - x)
    s0.wait_recv()
    with_sibling(0, 1 - y, 1 - x, d_send)
    d0 = hop(4, d_send.at[parts[0]], d_recv.at[parts[0]], to_x)
    d1 = hop(5, d_send.at[parts[1]], d_recv.at[parts[1]], to_y)
    d0.start()
    d1.start()
    s1.wait_recv()
    with_sibling(1, y, 1 - x, x_acc)
    x_send[parts[0]] = x_acc[parts[0]].astype(low)
    x0 = hop(6, x_send.at[parts[0]], x_recv.at[parts[0]], to_x)
    x0.start()
    s2 = to_sibling(2, 1 - y, x)
    s2.wait_recv()
    with_sibling(2, 1 - y, x, y_acc)
    y_send[parts[1]] = y_acc[parts[1]].astype(low)
    y1 = hop(7, y_send.at[parts[1]], y_recv.at[parts[1]], to_y)
    y1.start()
    s3 = to_sibling(3, y, x)
    d1.wait_recv()
    x_send[parts[1]] = (x_acc[parts[1]] + d_recv[parts[1]].astype(f32)).astype(low)
    x1 = hop(8, x_send.at[parts[1]], x_recv.at[parts[1]], to_x)
    x1.start()
    d0.wait_recv()
    y_send[parts[0]] = (y_acc[parts[0]] + d_recv[parts[0]].astype(f32)).astype(low)
    y0 = hop(9, y_send.at[parts[0]], y_recv.at[parts[0]], to_y)
    y0.start()
    s3.wait_recv()
    with_sibling(3, y, x, out)
    x0.wait_recv()
    y1.wait_recv()
    x1.wait_recv()
    y0.wait_recv()
    out[...] += x_recv[...].astype(f32) + y_recv[...].astype(f32)
    for copy in (s0, s1, s2, s3, d0, d1, x0, x1, y0, y1):
        copy.wait_send()


def plane_sum(lefts, rights, number, after=(), tile=512):
    ends = [(left, start) for left, a in enumerate(lefts) for start in range(0, a.shape[1], rights[0].shape[1])]
    terms = tuple(ends[: len(rights)])
    rows, width = lefts[0].shape[0] // 8, rights[0].shape[0]
    block = (rows, width)
    low, f32 = jnp.bfloat16, jnp.float32
    return pl.pallas_call(
        functools.partial(sum_kernel, len(lefts), terms, min(tile, width)),
        out_shape=jax.ShapeDtypeStruct(block, f32),
        in_specs=[VMEM] * (len(lefts) + len(rights)) + [HBM] * len(after),
        out_specs=VMEM,
        scratch_shapes=[
            pltpu.VMEM((4, *block), low),
            pltpu.VMEM((4, *block), low),
            *[pltpu.VMEM(block, low)] * 6,
            pltpu.VMEM(block, f32),
            pltpu.VMEM(block, f32),
            pltpu.SemaphoreType.DMA((10,)),
            pltpu.SemaphoreType.DMA((10,)),
        ],
        compiler_params=pltpu.CompilerParams(
            collective_id=number, has_side_effects=True, vmem_limit_bytes=48 * 2**20
        ),
        cost_estimate=pl.CostEstimate(flops=1, bytes_accessed=1, transcendentals=0),
        name="plane_sum",
    )(*lefts, *rights, *after)


def swap_kernel(pieces, takes, *refs):
    count = len(pieces)
    sources, (send, recv, own) = refs[: -2 * count - 3], refs[-3:]
    outs, holds = refs[-2 * count - 3 : -count - 3], refs[-count - 3 : -3]
    y, x, c, index = place()
    me = index(y, x, c)
    flips = [(fy, fx, fc) for fy, fx in ((1, 1), (0, 1), (1, 0), (0, 0)) for fc in (0, 1)]
    flips = [flip for flip in flips if flip != (0, 0, 0)]

    def there(flip):
        return tuple(1 - at if f else at for at, f in zip((y, x, c), flip))

    greet([dict(zip(("y", "x", "c"), there(flip))) for flip in flips])
    copies = []
    for piece in range(count):
        for number, flip in enumerate(flips):
            yy, xx, cc = there(flip)
            member = index(yy, xx, cc)
            holds[piece][number] = takes[piece](sources, member, cc)
            copy = pltpu.make_async_remote_copy(
                src_ref=holds[piece].at[number],
                dst_ref=outs[piece].at[me],
                send_sem=send.at[piece * 7 + number],
                recv_sem=recv.at[piece * 7 + number],
                device_id={"y": yy, "x": xx, "c": cc},
                device_id_type=MESH,
            )
            copy.start()
            copies.append(copy)
        holds[piece][7] = takes[piece](sources, me, c)
        keep = pltpu.make_async_copy(holds[piece].at[7], outs[piece].at[me], own.at[piece])
        keep.start()
        copies.append(keep)
    for copy in copies:
        copy.wait()


def plane_swap(sources, shapes, takes, number, after=()):
    low = jnp.bfloat16
    count = len(shapes)
    return pl.pallas_call(
        functools.partial(swap_kernel, shapes, takes),
        out_shape=[jax.ShapeDtypeStruct((8, *shape), low) for shape in shapes],
        in_specs=[VMEM] * len(sources) + [HBM] * len(after),
        out_specs=[HBM] * count,
        scratch_shapes=[
            *[pltpu.VMEM((8, *shape), low) for shape in shapes],
            pltpu.SemaphoreType.DMA((7 * count,)),
            pltpu.SemaphoreType.DMA((7 * count,)),
            pltpu.SemaphoreType.DMA((count,)),
        ],
        compiler_params=pltpu.CompilerParams(
            collective_id=number, has_side_effects=True, vmem_limit_bytes=48 * 2**20
        ),
        cost_estimate=pl.CostEstimate(flops=1, bytes_accessed=1, transcendentals=0),
        name="plane_swap",
    )(*sources, *after)


def total_kernel(planes, src, out, near, far, send, recv):
    y, x, c, index = place()
    z = lax.axis_index("z")
    me = index(y, x, c)
    flips = [(fy, fx, fc) for fy in (0, 1) for fx in (0, 1) for fc in (0, 1)][1:]
    team = [
        dict(zip(("y", "x", "c"), (1 - at if f else at for at, f in zip((y, x, c), flip)))) for flip in flips
    ]
    column = [{"z": lax.rem(z + step, planes)} for step in range(1, planes)]
    near[me] = src[...]
    greet(team + column)

    def spread(buffer, at, others, base):
        copies = [
            pltpu.make_async_remote_copy(
                src_ref=buffer.at[at],
                dst_ref=buffer.at[at],
                send_sem=send.at[base + number],
                recv_sem=recv.at[base + number],
                device_id=other,
                device_id_type=MESH,
            )
            for number, other in enumerate(others)
        ]
        for copy in copies:
            copy.start()
        for copy in copies:
            copy.wait()

    spread(near, me, team, 0)
    far[z] = jnp.sum(near[...], axis=0)
    spread(far, z, column, 7)
    out[...] = jnp.sum(far[...], axis=0)


def total_sum(value, planes, number):
    return pl.pallas_call(
        functools.partial(total_kernel, planes),
        out_shape=jax.ShapeDtypeStruct(value.shape, value.dtype),
        in_specs=[VMEM],
        out_specs=VMEM,
        scratch_shapes=[
            pltpu.VMEM((8, *value.shape), value.dtype),
            pltpu.VMEM((planes, *value.shape), value.dtype),
            pltpu.SemaphoreType.DMA((6 + planes,)),
            pltpu.SemaphoreType.DMA((6 + planes,)),
        ],
        compiler_params=pltpu.CompilerParams(collective_id=number, has_side_effects=True),
        cost_estimate=pl.CostEstimate(flops=1, bytes_accessed=1, transcendentals=0),
        name="total_sum",
    )(value)


def dot(left, right, contract):
    return lax.dot_general(left, right, (contract, ((), ())), preferred_element_type=jnp.float32)


def mm(left, right):
    return dot(left, right, ((1,), (0,)))


def mm_nt(left, right):
    return dot(left, right, ((1,), (1,)))


def mm_tn(left, right):
    return dot(left, right, ((0,), (0,)))


def bmm(pattern, left, right):
    return jnp.einsum(pattern, left, right, preferred_element_type=jnp.float32)


def angle_tables(positions):
    half_dim = HEAD_SIZE // 2
    frequency = rope_base ** (-(jnp.arange(half_dim).astype(jnp.float32) * 2.0) / HEAD_SIZE)
    phases = positions.astype(jnp.float32)[:, None] * frequency[None, :]
    return (jnp.cos(phases), jnp.sin(phases))


def rotate(value, cos_table, sin_table):
    half = value.shape[-1] // 2
    a, b = value[..., :half], value[..., half:]
    return jnp.concatenate([a * cos_table - b * sin_table, b * cos_table + a * sin_table], axis=-1)


def rms_forward(value, gain_row):
    inverse = lax.rsqrt(jnp.mean(value * value, axis=-1, keepdims=True) + norm_eps)
    return (value * inverse * gain_row, inverse)


def rms_back(grad_out, value, inverse, gain_row):
    scaled = grad_out * gain_row
    grad_in = inverse * (
        scaled - value * inverse * inverse * jnp.mean(scaled * value, axis=-1, keepdims=True)
    )
    return (grad_in, jnp.sum(grad_out * value * inverse, axis=0))


def adamw(weight, gradient, moment_one, moment_two, step_rate, decay_rate):
    mean_new = beta_one * moment_one + (1.0 - beta_one) * gradient
    square_new = beta_two * moment_two + (1.0 - beta_two) * gradient * gradient
    direction = (
        mean_new
        / (1.0 - beta_one**STEP)
        / (jnp.sqrt(square_new / (1.0 - beta_two**STEP)) + adam_eps)
    )
    return (weight - step_rate * (direction + decay_rate * weight), mean_new, square_new)


def attention_parts(core, length, q_ref, mine_ref, other_ref, query_ref, key_ref):
    mine, other = mine_ref[...].reshape(-1, HEAD_SIZE), other_ref[...].reshape(-1, HEAD_SIZE)
    first = core == 0
    k, v = jnp.where(first, mine, other), jnp.where(first, other, mine)
    q = q_ref[...].reshape(-1, HEAD_SIZE)
    at, key_at = query_ref[...], key_ref[...]
    allowed = (key_at <= at) & (key_at < length) & (key_at >= 0)
    scores = jnp.where(allowed, mm_nt(q, k) * HEAD_SIZE ** (-0.5), masked_value)
    exponent = jnp.exp(scores - jnp.max(scores, axis=-1, keepdims=True))
    return q, k, v, exponent / jnp.sum(exponent, axis=-1, keepdims=True)


def attention_kernel(core_ref, length_ref, q_ref, mine_ref, other_ref, query_ref, key_ref, out_ref):
    length = length_ref[pl.program_id(0)]
    _, _, v, soft = attention_parts(core_ref[0], length, q_ref, mine_ref, other_ref, query_ref, key_ref)
    out_ref[...] = mm(soft.astype(jnp.bfloat16), v).astype(jnp.bfloat16).reshape(out_ref.shape)


def attention_back_kernel(
    core_ref, length_ref, q_ref, mine_ref, other_ref, query_ref, key_ref, do_ref, cos_ref, sin_ref,
    dq_ref, keep_ref, send_ref,
):
    low = jnp.bfloat16
    core = core_ref[0]
    length = length_ref[pl.program_id(0)]
    q, k, v, soft = attention_parts(core, length, q_ref, mine_ref, other_ref, query_ref, key_ref)
    do = do_ref[...].reshape(-1, HEAD_SIZE)
    dp = mm_nt(do, v)
    delta = jnp.sum(soft * dp, axis=-1, keepdims=True)
    ds = (soft * (dp - delta) * HEAD_SIZE ** (-0.5)).astype(low)
    dq = mm(ds, k)
    cos_table, sin_table = cos_ref[...], sin_ref[...]
    half = HEAD_SIZE // 2
    a, b = dq[:, :half], dq[:, half:]
    turned = jnp.concatenate([a * cos_table + b * sin_table, b * cos_table - a * sin_table], axis=-1)
    dq_ref[...] = turned.astype(low).reshape(dq_ref.shape)
    dk, dv = mm_tn(ds, q), mm_tn(soft.astype(low), do)
    first = core == 0
    keep_ref[...] = jnp.where(first, dk, dv).reshape(keep_ref.shape)
    send_ref[...] = jnp.where(first, dv, dk).astype(low).reshape(send_ref.shape)


def attention_call(kernel, core, lengths, q, mine, other, query_pos, key_pos, extra, outs, name):
    ny, count, span, size = q.shape
    nz = mine.shape[0]
    rows = pl.BlockSpec((ny, 1, span, size), lambda i, *_: (0, i, 0, 0))
    keys = pl.BlockSpec((nz, ny, 1, span, size), lambda i, *_: (0, 0, i, 0, 0))

    def whole(value):
        return pl.BlockSpec(value.shape, lambda i, *_: (0,) * value.ndim)

    kinds = {"rows": (rows, q.shape), "keys": (keys, mine.shape)}
    return pl.pallas_call(
        kernel,
        grid_spec=pltpu.PrefetchScalarGridSpec(
            num_scalar_prefetch=2,
            grid=(count,),
            in_specs=[rows, keys, keys, whole(query_pos), whole(key_pos)]
            + [rows if value.shape == q.shape else whole(value) for value in extra],
            out_specs=[kinds[kind][0] for kind, _ in outs],
        ),
        out_shape=[jax.ShapeDtypeStruct(kinds[kind][1], dtype) for kind, dtype in outs],
        compiler_params=pltpu.CompilerParams(vmem_limit_bytes=48 * 2**20),
        cost_estimate=pl.CostEstimate(flops=1, bytes_accessed=1, transcendentals=0),
        name=name,
    )(core, lengths, q, mine, other, query_pos, key_pos, *extra)


def feed_back_kernel(dyb_ref, weight_ref, gate_ref, up_ref, out_ref):
    dm = mm(dyb_ref[...], weight_ref[...])
    gate, upward = gate_ref[...], up_ref[...]
    sig = jax.nn.sigmoid(gate)
    part = gate.shape[1]
    out_ref[:, :part] = (dm * upward * sig * (1.0 + gate * (1.0 - sig))).astype(out_ref.dtype)
    out_ref[:, part:] = (dm * gate * sig).astype(out_ref.dtype)


def feed_back(dyb, weight, gate, upward, lines=256):
    count, part = gate.shape

    def rows(width):
        return pl.BlockSpec((lines, width), lambda i: (i, 0))

    return pl.pallas_call(
        feed_back_kernel,
        grid=(count // lines,),
        in_specs=[rows(dyb.shape[1]), pl.BlockSpec(weight.shape, lambda i: (0, 0)), rows(part), rows(part)],
        out_specs=rows(2 * part),
        out_shape=jax.ShapeDtypeStruct((count, 2 * part), jnp.bfloat16),
        compiler_params=pltpu.CompilerParams(vmem_limit_bytes=48 * 2**20),
        cost_estimate=pl.CostEstimate(flops=1, bytes_accessed=1, transcendentals=0),
        name="feed_back",
    )(dyb, weight, gate, upward)


def is_square():
    return lax.axis_size("y") == 2 and lax.axis_size("x") == 2


def swap(blocks):
    return lax.all_to_all(blocks, TEAM, split_axis=0, concat_axis=0, tiled=True)


def over_planes(blocks):
    return lax.all_gather(blocks.reshape(-1, blocks.shape[-1]), "z", axis=0, tiled=True)


def over_planes_direct(blocks):
    planes = lax.axis_size("z")
    own = blocks.reshape(-1, blocks.shape[-1])
    return [own] + [
        lax.ppermute(own, "z", [(at, (at + step) % planes) for at in range(planes)]) for step in range(1, planes)
    ]


def put_planes(pieces):
    planes, count = lax.axis_size("z"), pieces[0].shape[0]
    whole = jnp.zeros((planes * count, pieces[0].shape[1]), pieces[0].dtype)
    for step, piece in enumerate(pieces):
        at = (lax.axis_index("z") - step) % planes * count
        whole = lax.dynamic_update_slice(whole, piece, (at, 0))
    return whole


def scatter_planes(term):
    return lax.psum_scatter(term, "z", scatter_dimension=0, tiled=True)


def scatter_team(rows, number, after=()):
    if not is_square():
        return swap(rows.reshape(8, -1, rows.shape[-1]))
    count = rows.shape[0] // 8

    def take(sources, member, core):
        return sources[0][pl.ds(pl.multiple_of(member * count, count), count), :]

    return plane_swap([rows], [(count, rows.shape[1])], [take], number, after)[0]


def team_gather(local, number, after=()):
    if not is_square():
        return lax.all_gather(local, TEAM, axis=0, tiled=True)
    return plane_gather(local, number, after).reshape(-1, local.shape[1])


def team_sum(lefts, rights, number, after=()):
    if is_square():
        return plane_sum(lefts, rights, number, after)
    partial = mm_nt(jnp.concatenate(lefts, axis=1), jnp.concatenate(rights, axis=1))
    return lax.psum_scatter(partial.astype(jnp.bfloat16), TEAM, scatter_dimension=0, tiled=True).astype(jnp.float32)


def local(
    tokens,
    lengths,
    norm_gains,
    attention_weight,
    feed_weight,
    cotangent,
    attention_mean,
    attention_square,
    feed_mean,
    feed_square,
    gain_mean,
    gain_square,
):
    low = jnp.bfloat16
    sequences, span, width = tokens.shape
    ny, nx, nz = lax.axis_size("y"), lax.axis_size("x"), lax.axis_size("z")
    team = ny * nx * 2
    core = lax.axis_index("c")
    rows = attention_weight.shape[0]
    q_width, kv_width = QUERY_HEADS * HEAD_SIZE, KEY_VALUE_HEADS * HEAD_SIZE
    count = sequences * span
    all_sequences = nx * 2 * sequences
    reach = ny * span
    near = nz <= 4
    ff_part = FF // team

    def columns(start, size):
        return pl.ds(pl.multiple_of(start, size), size)

    def take_attention(sources, member, c):
        source = sources[0]
        starts = (
            member * HEAD_SIZE,
            q_width + c * kv_width + (member - c) // 2 * HEAD_SIZE,
            q_width + 2 * kv_width + member * HEAD_SIZE,
        )
        return jnp.concatenate([source[:, columns(s, HEAD_SIZE)].astype(low) for s in starts], axis=1)

    def take_feed(part):
        return lambda sources, member, c: sources[0][
            :, columns(part * FF + member * ff_part, ff_part)
        ].astype(low)

    def spread(source, take, size, number, after=(), gather=over_planes):
        if is_square():
            blocks = plane_swap([source], [(rows, size)], [take], number, after)[0]
        else:
            blocks = swap(jnp.stack([take([source], member, member % 2) for member in range(8)]))
        return blocks, gather(blocks)

    attention_blocks, attention_mine = spread(attention_weight, take_attention, 3 * HEAD_SIZE, 1)
    gate_blocks, gate_weight = spread(feed_weight, take_feed(0), ff_part, 2, [attention_blocks])

    team_base = lax.axis_index("z") * reach
    team_pos = team_base + jnp.arange(reach, dtype=jnp.int32)
    own_pos = team_base + lax.axis_index("y") * span + jnp.arange(span, dtype=jnp.int32)
    if near:
        key_pos = jnp.concatenate([team_pos - back * reach for back in range(nz)])
    else:
        key_pos = jnp.arange(nz * reach, dtype=jnp.int32)
    query_at, key_at = team_pos[:, None], key_pos[None, :]
    cos_table, sin_table = angle_tables(team_pos)
    cos_rows, sin_rows = (t.reshape(ny, 1, span, -1) for t in (cos_table, sin_table))
    valid = (own_pos[None, :] < lengths[:, None]).astype(jnp.float32).reshape(count, 1)
    lengths_all = lax.all_gather(lengths, ("x", "c"), axis=0, tiled=True)
    core_at = jnp.reshape(core, (1,)).astype(jnp.int32)

    def heads(value):
        return value.reshape(ny, all_sequences, span, HEAD_SIZE)

    x_in = tokens.reshape(count, width).astype(jnp.float32)
    normed_one, inverse_one = rms_forward(x_in, norm_gains[0])
    outer_grad = cotangent.reshape(count, width).astype(jnp.float32) * valid
    h1 = team_gather(normed_one.astype(low), 3, [gate_blocks])
    up_blocks, up_pieces = spread(feed_weight, take_feed(1), ff_part, 18, [h1], over_planes_direct if near else over_planes)
    attention_mine, up_blocks, lengths_all = lax.optimization_barrier((attention_mine, up_blocks, lengths_all))
    query_weight = attention_mine[:, :HEAD_SIZE]
    kv_weight = attention_mine[:, HEAD_SIZE : 2 * HEAD_SIZE]
    out_weight = attention_mine[:, 2 * HEAD_SIZE :]
    kv_raw = heads(mm(h1, kv_weight))
    kv = jnp.where(core == 0, rotate(kv_raw, cos_rows, sin_rows), kv_raw).astype(low)
    q = rotate(heads(mm(h1, query_weight)), cos_rows, sin_rows).astype(low)
    dyb = team_gather(outer_grad.astype(low), 15, [kv])
    down_blocks, down_weight = spread(feed_weight, take_feed(2), ff_part, 12, [dyb])
    if near:
        earlier = [
            lax.ppermute(kv, "z", [(at, at + back) for at in range(nz - back)]) for back in range(1, nz)
        ]
        *earlier, dyb, down_blocks, q = lax.optimization_barrier((*earlier, dyb, down_blocks, q))
        kv = jnp.stack([kv, *earlier])
    else:
        kv = lax.all_gather(kv, "z", axis=0, tiled=False)
    other = lax.ppermute(kv, "c", [(0, 1), (1, 0)])
    attend = (core_at, lengths_all, q, kv, other, query_at, key_at)
    (o,) = attention_call(attention_kernel, *attend, (), [("rows", low)], "attention")
    o = o.reshape(-1, HEAD_SIZE)
    r = x_in + team_sum([o], [out_weight], 4)

    normed_two, inverse_two = rms_forward(r, norm_gains[1])
    h2 = team_gather(normed_two.astype(low), 16)
    gate = mm(h2, gate_weight)
    if near:
        gate, *up_pieces = lax.optimization_barrier((gate, *up_pieces))
        up_weight = put_planes(up_pieces)
    else:
        up_weight = up_pieces
    upward = mm(h2, up_weight)
    sig = jax.nn.sigmoid(gate)
    m = (gate * sig * upward).astype(low)
    down_term = mm_tn(dyb, m).astype(low)
    down_rows = scatter_planes(down_term)
    down_weight, down_term = lax.optimization_barrier((down_weight, down_term))
    d_both = feed_back(dyb, down_weight, gate, upward)
    dh2 = team_sum([d_both], [gate_weight, up_weight], 7, [down_term])
    gate_up_term = mm_tn(h2, d_both).astype(low)
    gate_up_rows = scatter_planes(gate_up_term)
    mid_grad, gain_two = rms_back(dh2, r, inverse_two, norm_gains[1])
    dr = outer_grad + mid_grad
    drb = team_gather(dr.astype(low), 13, [gate_up_term, down_rows])

    do = heads(mm(drb, out_weight).astype(low))
    dq, keep, theirs = attention_call(
        attention_back_kernel,
        *attend,
        (do, cos_table, sin_table),
        [("rows", low), ("keys", jnp.float32), ("keys", low)],
        "attention_back",
    )
    dq = dq.reshape(-1, HEAD_SIZE)
    dkv = keep + lax.ppermute(theirs, "c", [(0, 1), (1, 0)]).astype(jnp.float32)
    low_terms = dkv.astype(low)
    feed_sum = team_sum([m], [down_weight], 5, [low_terms])
    down_grad = scatter_team(down_rows, 6, [low_terms])
    if near:
        later = [
            lax.ppermute(low_terms[back], "z", [(at + back, at) for at in range(nz - back)])
            for back in range(1, nz)
        ]
        *later, feed_sum, down_grad, gate_up_rows = lax.optimization_barrier(
            (*later, feed_sum, down_grad, gate_up_rows)
        )
        dkv = dkv[0] + sum(term.astype(jnp.float32) for term in later)
    else:
        dkv = lax.psum_scatter(low_terms, "z", scatter_dimension=0, tiled=True)[0].astype(jnp.float32)
    dkv = jnp.where(core == 0, rotate(dkv, cos_rows, -sin_rows), dkv).astype(low).reshape(-1, HEAD_SIZE)
    layer_output = (r + feed_sum).astype(low)
    attention_term = jnp.concatenate([mm_tn(h1, dq), mm_tn(h1, dkv), mm_tn(drb, o)], axis=1).astype(low)
    attention_rows = scatter_planes(attention_term)
    dh1 = team_sum([dq, dkv], [query_weight, kv_weight], 9, [attention_term])
    in_grad, gain_one = rms_back(dh1, x_in, inverse_one, norm_gains[0])
    input_gradient = dr + in_grad
    gate_up_grad = scatter_team(gate_up_rows, 8, [attention_term])
    blocks_grad = scatter_team(attention_rows, 10).astype(jnp.float32)
    kv_grad = blocks_grad[:, :, HEAD_SIZE : 2 * HEAD_SIZE]

    def columns_of(blocks):
        return blocks.transpose(1, 0, 2).reshape(rows, -1)

    attention_grad = jnp.concatenate(
        [
            columns_of(blocks_grad[:, :, :HEAD_SIZE]),
            kv_grad.reshape(KEY_VALUE_HEADS, 2, rows, HEAD_SIZE).transpose(2, 1, 0, 3).reshape(rows, 2 * kv_width),
            columns_of(blocks_grad[:, :, 2 * HEAD_SIZE :]),
        ],
        axis=1,
    )
    feed_grad = jnp.concatenate(
        [
            columns_of(g.astype(jnp.float32))
            for g in (gate_up_grad[:, :, :ff_part], gate_up_grad[:, :, ff_part:], down_grad)
        ], axis=1
    )
    local_squares = jnp.sum(attention_grad * attention_grad) + jnp.sum(feed_grad * feed_grad)
    gain_local = jnp.stack([gain_one, gain_two])
    if is_square():
        lines = jnp.concatenate([gain_local.reshape(-1, 128), jnp.full((8, 128), local_squares)], axis=0)
        lines = total_sum(lines, nz, 11)
        gain_grad, squares = lines[:-8].reshape(2, width), lines[-1, 0]
    else:
        gain_grad, squares = lax.psum((gain_local, local_squares), ALL)
    gradient_norm = jnp.sqrt(squares + jnp.sum(gain_grad * gain_grad))
    factor = clip_norm / gradient_norm
    attention_new = adamw(
        attention_weight, attention_grad * factor, attention_mean, attention_square, matrix_rate, weight_decay
    )
    feed_new = adamw(feed_weight, feed_grad * factor, feed_mean, feed_square, matrix_rate, weight_decay)
    gains_new = adamw(norm_gains, gain_grad * factor, gain_mean, gain_square, gain_rate, 0.0)
    return (
        layer_output.reshape(sequences, span, width),
        input_gradient.reshape(sequences, span, width),
        gradient_norm,
        *attention_new,
        attention_new[0].astype(low),
        *feed_new,
        feed_new[0].astype(low),
        *gains_new,
    )


def solution(mesh):
    ctx, fsdp = mesh.shape["ctx"], mesh.shape["fsdp"]
    inner = QUERY_HEADS // fsdp
    fine = Mesh(mesh.devices.reshape(ctx // inner, inner, fsdp // 2, 2), ALL)
    act = P(("x", "c"), ("z", "y"), None)
    matrix = P(ALL, None)
    return jax.shard_map(
        local,
        mesh=fine,
        in_specs=(act, P(("x", "c")), P(), matrix, matrix, act, matrix, matrix, matrix, matrix, P(), P()),
        out_specs=(act, act, P(), matrix, matrix, matrix, matrix, matrix, matrix, matrix, matrix, P(), P(), P()),
        check_vma=False,
    )
```

```python
import functools

import jax
import jax.numpy as jnp
from jax import lax
from jax.experimental import pallas as pl
from jax.experimental.pallas import tpu as pltpu
from jax.sharding import Mesh, PartitionSpec as P

QUERY_HEADS = 8
KEY_VALUE_HEADS = 4
HEAD_SIZE = 256
FF = 8192
STEP = 10

norm_eps = 1e-06
rope_base = 1000042.0
masked_value = -1e30
clip_norm = 1.0
beta_one = 0.9
beta_two = 0.95
adam_eps = 1e-08
matrix_rate = 0.03
gain_rate = 0.4
weight_decay = 0.1

TEAM = ("u", "v", "c")
ALL = ("h", "u", "v", "x", "c")


MESH = pl.DeviceIdType.MESH
VMEM = pl.BlockSpec(memory_space=pltpu.VMEM)
HBM = pl.BlockSpec(memory_space=pl.ANY)


def place():
    u, v, c = lax.axis_index("u"), lax.axis_index("v"), lax.axis_index("c")
    return u, v, c, lambda uu, vv, cc: (uu * 2 + vv) * 2 + cc


def greet(others):
    barrier = pltpu.get_barrier_semaphore()
    for other in others:
        pl.semaphore_signal(barrier, inc=1, device_id=other, device_id_type=MESH)
    pl.semaphore_wait(barrier, len(others))


def gather_kernel(src, *refs):
    out, send, recv, own = refs[-4:]
    u, v, c, index = place()
    to_v, to_u, to_s = {"v": 1 - v}, {"u": 1 - u}, {"c": 1 - c}
    me, at_v, at_u, at_d = index(u, v, c), index(u, 1 - v, c), index(1 - u, v, c), index(1 - u, 1 - v, c)
    half = src.shape[0] // 2
    rows = (pl.ds(0, half), pl.ds(half, half))
    local = pltpu.make_async_copy(src, out.at[me], own)
    local.start()
    greet((to_v, to_u, to_s))

    def hop(slot, block, part, where, first=False):
        piece = out.at[block, rows[part]]
        return pltpu.make_async_remote_copy(
            src_ref=src.at[rows[part]] if first else piece,
            dst_ref=piece,
            send_sem=send.at[slot],
            recv_sem=recv.at[slot],
            device_id=where,
            device_id_type=MESH,
        )

    v0, v1 = hop(0, me, 0, to_v, True), hop(1, me, 1, to_v, True)
    u1, u0 = hop(2, me, 1, to_u, True), hop(3, me, 0, to_u, True)
    s0, s1 = hop(4, me, 0, to_s, True), hop(5, me, 1, to_s, True)
    for copy in (v0, u1, v1, u0, s0, s1):
        copy.start()
    v0.wait_recv()
    d0 = hop(6, at_v, 0, to_u)
    d0.start()
    u1.wait_recv()
    d1 = hop(7, at_u, 1, to_v)
    d1.start()
    sv0, su1 = hop(8, at_v, 0, to_s), hop(9, at_u, 1, to_s)
    sv0.start()
    su1.start()
    v1.wait_recv()
    sv1 = hop(10, at_v, 1, to_s)
    sv1.start()
    u0.wait_recv()
    su0 = hop(11, at_u, 0, to_s)
    su0.start()
    d0.wait_recv()
    sd0 = hop(12, at_d, 0, to_s)
    sd0.start()
    d1.wait_recv()
    sd1 = hop(13, at_d, 1, to_s)
    sd1.start()
    for copy in (s0, s1, sv0, su1, sv1, su0, sd0, sd1):
        copy.wait_recv()
    for copy in (v0, v1, u0, u1, s0, s1, d0, d1, sv0, su1, sv1, su0, sd0, sd1):
        copy.wait_send()
    local.wait()


def plane_gather(value, number, after=()):
    return pl.pallas_call(
        gather_kernel,
        out_shape=jax.ShapeDtypeStruct((8, *value.shape), value.dtype),
        in_specs=[HBM] * (1 + len(after)),
        out_specs=HBM,
        scratch_shapes=[
            pltpu.SemaphoreType.DMA((14,)),
            pltpu.SemaphoreType.DMA((14,)),
            pltpu.SemaphoreType.DMA,
        ],
        compiler_params=pltpu.CompilerParams(collective_id=number, has_side_effects=True),
        cost_estimate=pl.CostEstimate(flops=1, bytes_accessed=1, transcendentals=0),
        name="plane_gather",
    )(value, *after)


def sum_kernel(lefts, terms, tile, *refs):
    a_refs, w_refs = refs[:lefts], refs[lefts : lefts + len(terms)]
    out, s_send, s_recv, d_send, d_recv, v_send, v_recv, u_send, u_recv, v_acc, u_acc, send, recv = refs[-13:]
    u, v, c, index = place()
    to_v, to_u, to_s = {"v": 1 - v}, {"u": 1 - u}, {"c": 1 - c}
    rows, width = out.shape
    half = rows // 2
    parts = (pl.ds(0, half), pl.ds(half, half))
    f32, low = jnp.float32, jnp.bfloat16

    def product(block, put):
        lines = pl.ds(pl.multiple_of(block * rows, rows), rows)

        @pl.loop(0, width // tile)
        def _(step):
            cols = pl.ds(pl.multiple_of(step * tile, tile), tile)
            total = None
            for (left, start), w_ref in zip(terms, w_refs):
                term = mm_nt(a_refs[left][lines, start : start + w_ref.shape[1]], w_ref[cols, :])
                total = term if total is None else total + term
            put(cols, total)

    def hop(slot, src, dst, where):
        copy = pltpu.make_async_remote_copy(
            src_ref=src, dst_ref=dst, send_sem=send.at[slot], recv_sem=recv.at[slot],
            device_id=where, device_id_type=MESH,
        )
        return copy

    def to_sibling(slot, uu, vv):
        def put(cols, total):
            s_send[slot, :, cols] = total.astype(low)

        product(index(uu, vv, 1 - c), put)
        copy = hop(slot, s_send.at[slot], s_recv.at[slot], to_s)
        copy.start()
        return copy

    def with_sibling(slot, uu, vv, keep):
        def put(cols, total):
            keep[:, cols] = (total + s_recv[slot, :, cols].astype(f32)).astype(keep.dtype)

        product(index(uu, vv, c), put)

    greet((to_v, to_u, to_s))
    s0 = to_sibling(0, 1 - u, 1 - v)
    s1 = to_sibling(1, u, 1 - v)
    s0.wait_recv()
    with_sibling(0, 1 - u, 1 - v, d_send)
    d0 = hop(4, d_send.at[parts[0]], d_recv.at[parts[0]], to_v)
    d1 = hop(5, d_send.at[parts[1]], d_recv.at[parts[1]], to_u)
    d0.start()
    d1.start()
    s1.wait_recv()
    with_sibling(1, u, 1 - v, v_acc)
    v_send[parts[0]] = v_acc[parts[0]].astype(low)
    v0 = hop(6, v_send.at[parts[0]], v_recv.at[parts[0]], to_v)
    v0.start()
    s2 = to_sibling(2, 1 - u, v)
    s2.wait_recv()
    with_sibling(2, 1 - u, v, u_acc)
    u_send[parts[1]] = u_acc[parts[1]].astype(low)
    u1 = hop(7, u_send.at[parts[1]], u_recv.at[parts[1]], to_u)
    u1.start()
    s3 = to_sibling(3, u, v)
    d1.wait_recv()
    v_send[parts[1]] = (v_acc[parts[1]] + d_recv[parts[1]].astype(f32)).astype(low)
    v1 = hop(8, v_send.at[parts[1]], v_recv.at[parts[1]], to_v)
    v1.start()
    d0.wait_recv()
    u_send[parts[0]] = (u_acc[parts[0]] + d_recv[parts[0]].astype(f32)).astype(low)
    u0 = hop(9, u_send.at[parts[0]], u_recv.at[parts[0]], to_u)
    u0.start()
    s3.wait_recv()
    with_sibling(3, u, v, out)
    v0.wait_recv()
    u1.wait_recv()
    v1.wait_recv()
    u0.wait_recv()
    out[...] += v_recv[...].astype(f32) + u_recv[...].astype(f32)
    for copy in (s0, s1, s2, s3, d0, d1, v0, v1, u0, u1):
        copy.wait_send()


def plane_sum(lefts, rights, number, after=(), tile=512):
    ends = [(left, start) for left, a in enumerate(lefts) for start in range(0, a.shape[1], rights[0].shape[1])]
    terms = tuple(ends[: len(rights)])
    rows, width = lefts[0].shape[0] // 8, rights[0].shape[0]
    block = (rows, width)
    low, f32 = jnp.bfloat16, jnp.float32
    return pl.pallas_call(
        functools.partial(sum_kernel, len(lefts), terms, min(tile, width)),
        out_shape=jax.ShapeDtypeStruct(block, f32),
        in_specs=[VMEM] * (len(lefts) + len(rights)) + [HBM] * len(after),
        out_specs=VMEM,
        scratch_shapes=[
            pltpu.VMEM((4, *block), low),
            pltpu.VMEM((4, *block), low),
            *[pltpu.VMEM(block, low)] * 6,
            pltpu.VMEM(block, f32),
            pltpu.VMEM(block, f32),
            pltpu.SemaphoreType.DMA((10,)),
            pltpu.SemaphoreType.DMA((10,)),
        ],
        compiler_params=pltpu.CompilerParams(
            collective_id=number, has_side_effects=True, vmem_limit_bytes=48 * 2**20
        ),
        cost_estimate=pl.CostEstimate(flops=1, bytes_accessed=1, transcendentals=0),
        name="plane_sum",
    )(*lefts, *rights, *after)


def swap_kernel(pieces, takes, *refs):
    count = len(pieces)
    sources, (send, recv, own) = refs[: -2 * count - 3], refs[-3:]
    outs, holds = refs[-2 * count - 3 : -count - 3], refs[-count - 3 : -3]
    u, v, c, index = place()
    me = index(u, v, c)
    flips = [(fu, fv, fc) for fu, fv in ((1, 1), (0, 1), (1, 0), (0, 0)) for fc in (0, 1)]
    flips = [flip for flip in flips if flip != (0, 0, 0)]

    def there(flip):
        return tuple(1 - at if f else at for at, f in zip((u, v, c), flip))

    greet([dict(zip(("u", "v", "c"), there(flip))) for flip in flips])
    copies = []
    for piece in range(count):
        for number, flip in enumerate(flips):
            uu, vv, cc = there(flip)
            member = index(uu, vv, cc)
            holds[piece][number] = takes[piece](sources, member, cc)
            copy = pltpu.make_async_remote_copy(
                src_ref=holds[piece].at[number],
                dst_ref=outs[piece].at[me],
                send_sem=send.at[piece * 7 + number],
                recv_sem=recv.at[piece * 7 + number],
                device_id={"u": uu, "v": vv, "c": cc},
                device_id_type=MESH,
            )
            copy.start()
            copies.append(copy)
        holds[piece][7] = takes[piece](sources, me, c)
        keep = pltpu.make_async_copy(holds[piece].at[7], outs[piece].at[me], own.at[piece])
        keep.start()
        copies.append(keep)
    for copy in copies:
        copy.wait()


def plane_swap(sources, shapes, takes, number, after=()):
    low = jnp.bfloat16
    count = len(shapes)
    return pl.pallas_call(
        functools.partial(swap_kernel, shapes, takes),
        out_shape=[jax.ShapeDtypeStruct((8, *shape), low) for shape in shapes],
        in_specs=[VMEM] * len(sources) + [HBM] * len(after),
        out_specs=[HBM] * count,
        scratch_shapes=[
            *[pltpu.VMEM((8, *shape), low) for shape in shapes],
            pltpu.SemaphoreType.DMA((7 * count,)),
            pltpu.SemaphoreType.DMA((7 * count,)),
            pltpu.SemaphoreType.DMA((count,)),
        ],
        compiler_params=pltpu.CompilerParams(
            collective_id=number, has_side_effects=True, vmem_limit_bytes=48 * 2**20
        ),
        cost_estimate=pl.CostEstimate(flops=1, bytes_accessed=1, transcendentals=0),
        name="plane_swap",
    )(*sources, *after)


def total_kernel(pools, src, out, near, far, send, recv):
    u, v, c, index = place()
    across, high = pools
    xx, hh = lax.axis_index("x"), lax.axis_index("h")
    at = xx * high + hh
    me = index(u, v, c)
    flips = [(fu, fv, fc) for fu in (0, 1) for fv in (0, 1) for fc in (0, 1)][1:]
    team = [
        dict(zip(("u", "v", "c"), (1 - at if f else at for at, f in zip((u, v, c), flip)))) for flip in flips
    ]
    column = [
        {"x": lax.rem(xx + fx, across), "h": lax.rem(hh + fh, high)} for fx in range(across) for fh in range(high)
    ][1:]
    near[me] = src[...]
    greet(team + column)

    def spread(buffer, at, others, base):
        copies = [
            pltpu.make_async_remote_copy(
                src_ref=buffer.at[at],
                dst_ref=buffer.at[at],
                send_sem=send.at[base + number],
                recv_sem=recv.at[base + number],
                device_id=other,
                device_id_type=MESH,
            )
            for number, other in enumerate(others)
        ]
        for copy in copies:
            copy.start()
        for copy in copies:
            copy.wait()

    spread(near, me, team, 0)
    far[at] = jnp.sum(near[...], axis=0)
    spread(far, at, column, 7)
    out[...] = jnp.sum(far[...], axis=0)


def total_sum(value, pools, number):
    return pl.pallas_call(
        functools.partial(total_kernel, pools),
        out_shape=jax.ShapeDtypeStruct(value.shape, value.dtype),
        in_specs=[VMEM],
        out_specs=VMEM,
        scratch_shapes=[
            pltpu.VMEM((8, *value.shape), value.dtype),
            pltpu.VMEM((pools[0] * pools[1], *value.shape), value.dtype),
            pltpu.SemaphoreType.DMA((6 + pools[0] * pools[1],)),
            pltpu.SemaphoreType.DMA((6 + pools[0] * pools[1],)),
        ],
        compiler_params=pltpu.CompilerParams(collective_id=number, has_side_effects=True),
        cost_estimate=pl.CostEstimate(flops=1, bytes_accessed=1, transcendentals=0),
        name="total_sum",
    )(value)


def dot(left, right, contract):
    return lax.dot_general(left, right, (contract, ((), ())), preferred_element_type=jnp.float32)


def mm(left, right):
    return dot(left, right, ((1,), (0,)))


def mm_nt(left, right):
    return dot(left, right, ((1,), (1,)))


def mm_tn(left, right):
    return dot(left, right, ((0,), (0,)))


def bmm(pattern, left, right):
    return jnp.einsum(pattern, left, right, preferred_element_type=jnp.float32)


def angle_tables(positions):
    half_dim = HEAD_SIZE // 2
    frequency = rope_base ** (-(jnp.arange(half_dim).astype(jnp.float32) * 2.0) / HEAD_SIZE)
    phases = positions.astype(jnp.float32)[:, None] * frequency[None, :]
    return (jnp.cos(phases), jnp.sin(phases))


def rotate(value, cos_table, sin_table):
    half = value.shape[-1] // 2
    a, b = value[..., :half], value[..., half:]
    return jnp.concatenate([a * cos_table - b * sin_table, b * cos_table + a * sin_table], axis=-1)


def rms_forward(value, gain_row):
    inverse = lax.rsqrt(jnp.mean(value * value, axis=-1, keepdims=True) + norm_eps)
    return (value * inverse * gain_row, inverse)


def rms_back(grad_out, value, inverse, gain_row):
    scaled = grad_out * gain_row
    grad_in = inverse * (
        scaled - value * inverse * inverse * jnp.mean(scaled * value, axis=-1, keepdims=True)
    )
    return (grad_in, jnp.sum(grad_out * value * inverse, axis=0))


def adamw(weight, gradient, moment_one, moment_two, step_rate, decay_rate):
    mean_new = beta_one * moment_one + (1.0 - beta_one) * gradient
    square_new = beta_two * moment_two + (1.0 - beta_two) * gradient * gradient
    direction = (
        mean_new
        / (1.0 - beta_one**STEP)
        / (jnp.sqrt(square_new / (1.0 - beta_two**STEP)) + adam_eps)
    )
    return (weight - step_rate * (direction + decay_rate * weight), mean_new, square_new)


def attention_parts(core, length, q_ref, mine_ref, other_ref, query_ref, key_ref):
    mine, other = mine_ref[...].reshape(-1, HEAD_SIZE), other_ref[...].reshape(-1, HEAD_SIZE)
    first = core == 0
    k, v = jnp.where(first, mine, other), jnp.where(first, other, mine)
    q = q_ref[...].reshape(-1, HEAD_SIZE)
    at, key_at = query_ref[...], key_ref[...]
    allowed = (key_at <= at) & (key_at < length) & (key_at >= 0)
    scores = jnp.where(allowed, mm_nt(q, k) * HEAD_SIZE ** (-0.5), masked_value)
    exponent = jnp.exp(scores - jnp.max(scores, axis=-1, keepdims=True))
    return q, k, v, exponent / jnp.sum(exponent, axis=-1, keepdims=True)


def attention_kernel(core_ref, length_ref, q_ref, mine_ref, other_ref, query_ref, key_ref, out_ref):
    length = length_ref[pl.program_id(0)]
    _, _, v, soft = attention_parts(core_ref[0], length, q_ref, mine_ref, other_ref, query_ref, key_ref)
    out_ref[...] = mm(soft.astype(jnp.bfloat16), v).astype(jnp.bfloat16).reshape(out_ref.shape)


def attention_back_kernel(
    core_ref, length_ref, q_ref, mine_ref, other_ref, query_ref, key_ref, do_ref, cos_ref, sin_ref,
    dq_ref, keep_ref, send_ref,
):
    low = jnp.bfloat16
    core = core_ref[0]
    length = length_ref[pl.program_id(0)]
    q, k, v, soft = attention_parts(core, length, q_ref, mine_ref, other_ref, query_ref, key_ref)
    do = do_ref[...].reshape(-1, HEAD_SIZE)
    dp = mm_nt(do, v)
    delta = jnp.sum(soft * dp, axis=-1, keepdims=True)
    ds = (soft * (dp - delta) * HEAD_SIZE ** (-0.5)).astype(low)
    dq = mm(ds, k)
    cos_table, sin_table = cos_ref[...], sin_ref[...]
    half = HEAD_SIZE // 2
    a, b = dq[:, :half], dq[:, half:]
    turned = jnp.concatenate([a * cos_table + b * sin_table, b * cos_table - a * sin_table], axis=-1)
    dq_ref[...] = turned.astype(low).reshape(dq_ref.shape)
    dk, dv = mm_tn(ds, q), mm_tn(soft.astype(low), do)
    first = core == 0
    keep_ref[...] = jnp.where(first, dk, dv).reshape(keep_ref.shape)
    send_ref[...] = jnp.where(first, dv, dk).astype(low).reshape(send_ref.shape)


def attention_call(kernel, core, lengths, q, mine, other, query_pos, key_pos, extra, outs, name):
    ny, count, span, size = q.shape
    nz = mine.shape[0]
    rows = pl.BlockSpec((ny, 1, span, size), lambda i, *_: (0, i, 0, 0))
    keys = pl.BlockSpec((nz, ny, 1, span, size), lambda i, *_: (0, 0, i, 0, 0))

    def whole(value):
        return pl.BlockSpec(value.shape, lambda i, *_: (0,) * value.ndim)

    kinds = {"rows": (rows, q.shape), "keys": (keys, mine.shape)}
    return pl.pallas_call(
        kernel,
        grid_spec=pltpu.PrefetchScalarGridSpec(
            num_scalar_prefetch=2,
            grid=(count,),
            in_specs=[rows, keys, keys, whole(query_pos), whole(key_pos)]
            + [rows if value.shape == q.shape else whole(value) for value in extra],
            out_specs=[kinds[kind][0] for kind, _ in outs],
        ),
        out_shape=[jax.ShapeDtypeStruct(kinds[kind][1], dtype) for kind, dtype in outs],
        compiler_params=pltpu.CompilerParams(vmem_limit_bytes=48 * 2**20),
        cost_estimate=pl.CostEstimate(flops=1, bytes_accessed=1, transcendentals=0),
        name=name,
    )(core, lengths, q, mine, other, query_pos, key_pos, *extra)


def feed_back_kernel(dyb_ref, weight_ref, gate_ref, up_ref, out_ref):
    dm = mm(dyb_ref[...], weight_ref[...])
    gate, upward = gate_ref[...], up_ref[...]
    sig = jax.nn.sigmoid(gate)
    part = gate.shape[1]
    out_ref[:, :part] = (dm * upward * sig * (1.0 + gate * (1.0 - sig))).astype(out_ref.dtype)
    out_ref[:, part:] = (dm * gate * sig).astype(out_ref.dtype)


def feed_back(dyb, weight, gate, upward, lines=256):
    count, part = gate.shape

    def rows(width):
        return pl.BlockSpec((lines, width), lambda i: (i, 0))

    return pl.pallas_call(
        feed_back_kernel,
        grid=(count // lines,),
        in_specs=[rows(dyb.shape[1]), pl.BlockSpec(weight.shape, lambda i: (0, 0)), rows(part), rows(part)],
        out_specs=rows(2 * part),
        out_shape=jax.ShapeDtypeStruct((count, 2 * part), jnp.bfloat16),
        compiler_params=pltpu.CompilerParams(vmem_limit_bytes=48 * 2**20),
        cost_estimate=pl.CostEstimate(flops=1, bytes_accessed=1, transcendentals=0),
        name="feed_back",
    )(dyb, weight, gate, upward)


def exchange_x(value):
    return lax.ppermute(value, "x", [(0, 1), (1, 0)])


def gather_teams(blocks):
    return lax.all_gather(blocks.reshape(-1, blocks.shape[-1]), "h", axis=0, tiled=True)


def gather_across(own):
    if lax.axis_size("x") == 2:
        return [own, exchange_x(own)]
    return [lax.all_gather(own, "x", axis=0, tiled=True)]


def halves(left):
    if lax.axis_size("x") == 2:
        half = left.shape[1] // 2
        return left[:, :half], left[:, half:]
    return left, None


def arrive(go):
    return None if go is None else exchange_x(go)


def add_across(stay, came):
    low = jnp.bfloat16
    if came is None:
        return lax.psum_scatter(stay.astype(low), "x", scatter_dimension=0, tiled=True)
    return (stay + came.astype(jnp.float32)).astype(low)


def scatter_teams(term):
    return lax.psum_scatter(term, "h", scatter_dimension=0, tiled=True)


def together(*values):
    return lax.optimization_barrier(values)


def scatter_team(rows, number, after=()):
    count = rows.shape[0] // 8

    def take(sources, member, core):
        return sources[0][pl.ds(pl.multiple_of(member * count, count), count), :]

    return plane_swap([rows], [(count, rows.shape[1])], [take], number, after)[0]


def team_gather(local, number, after=()):
    return plane_gather(local, number, after).reshape(-1, local.shape[1])


def features_in(value):
    high, across = lax.axis_size("h"), lax.axis_size("x")
    shape = value.shape
    value = jnp.swapaxes(value.reshape(*shape[:-1], high * 4, across, -1), -3, -2)
    if across == 2:
        value = jnp.where(lax.axis_index("x") == 0, value, jnp.flip(value, -3))
    return value.reshape(shape)


def features_out(value):
    high, across = lax.axis_size("h"), lax.axis_size("x")
    shape = value.shape
    value = value.reshape(*shape[:-1], across, high * 4, -1)
    if across == 2:
        value = jnp.where(lax.axis_index("x") == 0, value, jnp.flip(value, -3))
    return jnp.swapaxes(value, -3, -2).reshape(shape)


def local(
    tokens,
    lengths,
    norm_gains,
    attention_weight,
    feed_weight,
    cotangent,
    attention_mean,
    attention_square,
    feed_mean,
    feed_square,
    gain_mean,
    gain_square,
):
    low = jnp.bfloat16
    sequences, span, width = tokens.shape
    high, across = lax.axis_size("h"), lax.axis_size("x")
    core, first = lax.axis_index("c"), lax.axis_index("c") == 0
    rows = attention_weight.shape[0]
    q_width, kv_width = QUERY_HEADS * HEAD_SIZE, KEY_VALUE_HEADS * HEAD_SIZE
    count = sequences * span
    reach = 4 * span
    near = high <= 4
    ff_part = FF // 8

    def columns(start, size):
        return pl.ds(pl.multiple_of(start, size), size)

    def take_attention(sources, member, c):
        source = sources[0]
        starts = (
            member * HEAD_SIZE,
            q_width + c * kv_width + (member - c) // 2 * HEAD_SIZE,
            q_width + 2 * kv_width + member * HEAD_SIZE,
        )
        return jnp.concatenate([source[:, columns(s, HEAD_SIZE)].astype(low) for s in starts], axis=1)

    def take_feed(part):
        return lambda sources, member, c: sources[0][
            :, columns(part * FF + member * ff_part, ff_part)
        ].astype(low)

    def spread(source, take, size, number, after=()):
        blocks = plane_swap([source], [(rows, size)], [take], number, after)[0]
        return blocks, gather_teams(blocks)

    def product(left, right):
        stay, go = halves(left)
        return mm_tn(stay, right), None if go is None else mm_tn(go, right).astype(low)

    attention_blocks, attention_mine = spread(attention_weight, take_attention, 3 * HEAD_SIZE, 1)
    gate_blocks, gate_weight = spread(feed_weight, take_feed(0), ff_part, 2, [attention_blocks])

    team_base = lax.axis_index("h") * reach
    team_pos = team_base + jnp.arange(reach, dtype=jnp.int32)
    own_pos = team_base + (lax.axis_index("u") * 2 + lax.axis_index("v")) * span + jnp.arange(span, dtype=jnp.int32)
    if near:
        key_pos = jnp.concatenate([team_pos - back * reach for back in range(high)])
    else:
        key_pos = jnp.arange(high * reach, dtype=jnp.int32)
    query_at, key_at = team_pos[:, None], key_pos[None, :]
    cos_table, sin_table = angle_tables(team_pos)
    cos_rows, sin_rows = (t.reshape(4, 1, span, -1) for t in (cos_table, sin_table))
    valid = (own_pos[None, :] < lengths[:, None]).astype(jnp.float32).reshape(count, 1)
    lengths_all = lax.all_gather(lengths, "c", axis=0, tiled=True)
    core_at = jnp.reshape(core, (1,)).astype(jnp.int32)

    def heads(value):
        return value.reshape(4, 2 * sequences, span, HEAD_SIZE)

    gains = features_in(norm_gains)
    x_in = features_in(tokens.reshape(count, width).astype(jnp.float32))
    normed_one, inverse_one = rms_forward(x_in, gains[0])
    outer_grad = features_in(cotangent.reshape(count, width)).astype(jnp.float32) * valid
    h1 = team_gather(normed_one.astype(low), 3, [gate_blocks])
    up_blocks, up_weight = spread(feed_weight, take_feed(1), ff_part, 18, [h1])
    attention_mine = gather_across(attention_mine)
    attention_mine, up_blocks, lengths_all = together(attention_mine, up_blocks, lengths_all)
    attention_mine = jnp.concatenate(attention_mine)
    query_weight = attention_mine[:, :HEAD_SIZE]
    kv_weight = attention_mine[:, HEAD_SIZE : 2 * HEAD_SIZE]
    out_weight = attention_mine[:, 2 * HEAD_SIZE :]
    kv_raw = heads(mm(h1, kv_weight))
    kv = jnp.where(first, rotate(kv_raw, cos_rows, sin_rows), kv_raw).astype(low)
    q = rotate(heads(mm(h1, query_weight)), cos_rows, sin_rows).astype(low)
    gate_weight, kv = together(gate_weight, kv)
    gate_weight = gather_across(gate_weight)
    dyb = team_gather(outer_grad.astype(low), 15, [kv])
    down_blocks, down_weight = spread(feed_weight, take_feed(2), ff_part, 12, [dyb])
    if near:
        earlier = [
            lax.ppermute(kv, "h", [(at, at + back) for at in range(high - back)]) for back in range(1, high)
        ]
        *earlier, dyb, down_blocks, q = together(*earlier, dyb, down_blocks, q)
        kv = jnp.stack([kv, *earlier])
    else:
        kv = lax.all_gather(kv, "h", axis=0, tiled=False)
    other = lax.ppermute(kv, "c", [(0, 1), (1, 0)])
    attend = (core_at, lengths_all, q, kv, other, query_at, key_at)
    (o,) = attention_call(attention_kernel, *attend, (), [("rows", low)], "attention")
    o = o.reshape(-1, HEAD_SIZE)
    up_weight, o = together(up_weight, o)
    up_weight = gather_across(up_weight)
    r = x_in + plane_sum([o], [out_weight], 4)

    normed_two, inverse_two = rms_forward(r, gains[1])
    h2 = team_gather(normed_two.astype(low), 16)
    h2, down_weight = together(h2, down_weight)
    down_weight = gather_across(down_weight)
    gate_weight, up_weight = jnp.concatenate(gate_weight), jnp.concatenate(up_weight)
    gate, upward = mm(h2, gate_weight), mm(h2, up_weight)
    m = (gate * jax.nn.sigmoid(gate) * upward).astype(low)
    down_stay, down_go = product(dyb, m)
    down_came = arrive(down_go)
    down_weight, down_stay = together(down_weight, down_stay)
    down_weight = jnp.concatenate(down_weight)
    d_both = feed_back(dyb, down_weight, gate, upward)
    gate_up_stay, gate_up_go = product(h2, d_both)
    gate_up_came = arrive(gate_up_go)
    d_both, gate_up_go, down_came = together(d_both, gate_up_go, down_came)
    down_rows = scatter_teams(add_across(down_stay, down_came))
    dh2 = plane_sum([d_both], [gate_weight, up_weight], 7)
    mid_grad, gain_two = rms_back(dh2, r, inverse_two, gains[1])
    dr = outer_grad + mid_grad
    drb = team_gather(dr.astype(low), 13, [gate_up_stay, down_rows])

    do = heads(mm(drb, out_weight).astype(low))
    do, gate_up_came = together(do, gate_up_came)
    gate_up_rows = scatter_teams(add_across(gate_up_stay, gate_up_came))
    dq, keep, theirs = attention_call(
        attention_back_kernel,
        *attend,
        (do, cos_table, sin_table),
        [("rows", low), ("keys", jnp.float32), ("keys", low)],
        "attention_back",
    )
    dq = dq.reshape(-1, HEAD_SIZE)
    terms = [product(h1, dq), product(drb, o)]
    qo_stay = jnp.concatenate([stay for stay, _ in terms], axis=1)
    qo_go = None if terms[0][1] is None else jnp.concatenate([go for _, go in terms], axis=1)
    qo_rows = scatter_teams(add_across(qo_stay, arrive(qo_go)))
    dkv = keep + lax.ppermute(theirs, "c", [(0, 1), (1, 0)]).astype(jnp.float32)
    low_terms = dkv.astype(low)
    feed_sum = plane_sum([m], [down_weight], 5, [low_terms])
    down_grad = scatter_team(down_rows, 6, [low_terms])
    if near:
        later = [
            lax.ppermute(low_terms[back], "h", [(at + back, at) for at in range(high - back)])
            for back in range(1, high)
        ]
        *later, feed_sum, down_grad, gate_up_rows = together(*later, feed_sum, down_grad, gate_up_rows)
        dkv = dkv[0] + sum(term.astype(jnp.float32) for term in later)
    else:
        dkv = lax.psum_scatter(low_terms, "h", scatter_dimension=0, tiled=True)[0].astype(jnp.float32)
    dkv = jnp.where(first, rotate(dkv, cos_rows, -sin_rows), dkv).astype(low).reshape(-1, HEAD_SIZE)
    layer_output = features_out(r + feed_sum).astype(low)
    kv_stay, kv_go = product(h1, dkv)
    kv_term = add_across(kv_stay, arrive(kv_go))
    kv_rows = scatter_teams(kv_term)
    dh1 = plane_sum([dq, dkv], [query_weight, kv_weight], 9, [kv_stay] if kv_go is None else [kv_stay, kv_go])
    in_grad, gain_one = rms_back(dh1, x_in, inverse_one, gains[0])
    input_gradient = features_out(dr + in_grad)
    gate_up_grad = scatter_team(gate_up_rows, 8, [dh1, kv_term])
    qo_grad = scatter_team(qo_rows, 10, [dh1, kv_term]).astype(jnp.float32)
    kv_grad = scatter_team(kv_rows, 14).astype(jnp.float32)

    def columns_of(blocks):
        return blocks.transpose(1, 0, 2).reshape(rows, -1)

    attention_grad = jnp.concatenate(
        [
            columns_of(qo_grad[:, :, :HEAD_SIZE]),
            kv_grad.reshape(KEY_VALUE_HEADS, 2, rows, HEAD_SIZE).transpose(2, 1, 0, 3).reshape(rows, 2 * kv_width),
            columns_of(qo_grad[:, :, HEAD_SIZE:]),
        ],
        axis=1,
    )
    feed_grad = jnp.concatenate(
        [
            columns_of(g.astype(jnp.float32))
            for g in (gate_up_grad[:, :, :ff_part], gate_up_grad[:, :, ff_part:], down_grad)
        ], axis=1
    )
    local_squares = jnp.sum(attention_grad * attention_grad) + jnp.sum(feed_grad * feed_grad)
    gain_local = features_out(jnp.stack([gain_one, gain_two]))
    lines = jnp.concatenate([gain_local.reshape(-1, 128), jnp.full((8, 128), local_squares)], axis=0)
    lines = total_sum(lines, (across, high), 11)
    gain_grad, squares = lines[:-8].reshape(2, width), lines[-1, 0]
    gradient_norm = jnp.sqrt(squares + jnp.sum(gain_grad * gain_grad))
    factor = clip_norm / gradient_norm
    attention_new = adamw(
        attention_weight, attention_grad * factor, attention_mean, attention_square, matrix_rate, weight_decay
    )
    feed_new = adamw(feed_weight, feed_grad * factor, feed_mean, feed_square, matrix_rate, weight_decay)
    gains_new = adamw(norm_gains, gain_grad * factor, gain_mean, gain_square, gain_rate, 0.0)
    return (
        layer_output.reshape(sequences, span, width),
        input_gradient.reshape(sequences, span, width),
        gradient_norm,
        *attention_new,
        attention_new[0].astype(low),
        *feed_new,
        feed_new[0].astype(low),
        *gains_new,
    )


def solution(mesh):
    ctx, fsdp = mesh.shape["ctx"], mesh.shape["fsdp"]
    fine = Mesh(mesh.devices.reshape(ctx // 4, 2, 2, fsdp // 2, 2), ALL)
    act = P(("x", "c"), ("h", "u", "v"), None)
    matrix = P(ALL, None)
    return jax.shard_map(
        local,
        mesh=fine,
        in_specs=(act, P(("x", "c")), P(), matrix, matrix, act, matrix, matrix, matrix, matrix, P(), P()),
        out_specs=(act, act, P(), matrix, matrix, matrix, matrix, matrix, matrix, matrix, matrix, P(), P(), P()),
        check_vma=False,
    )
```

```python
import functools

import jax
import jax.numpy as jnp
from jax import lax
from jax.experimental import pallas as pl
from jax.experimental.pallas import tpu as pltpu
from jax.sharding import Mesh, PartitionSpec as P

QUERY_HEADS = 8
KEY_VALUE_HEADS = 4
HEAD_SIZE = 256
FF = 8192
STEP = 10

norm_eps = 1e-06
rope_base = 1000042.0
masked_value = -1e30
clip_norm = 1.0
beta_one = 0.9
beta_two = 0.95
adam_eps = 1e-08
matrix_rate = 0.03
gain_rate = 0.4
weight_decay = 0.1

TEAM = ("u", "v", "c")
ALL = ("h", "u", "v", "x", "c")


MESH = pl.DeviceIdType.MESH
VMEM = pl.BlockSpec(memory_space=pltpu.VMEM)
HBM = pl.BlockSpec(memory_space=pl.ANY)


def place():
    u, v, c = lax.axis_index("u"), lax.axis_index("v"), lax.axis_index("c")
    return u, v, c, lambda uu, vv, cc: (uu * 2 + vv) * 2 + cc


def greet(others):
    barrier = pltpu.get_barrier_semaphore()
    for other in others:
        pl.semaphore_signal(barrier, inc=1, device_id=other, device_id_type=MESH)
    pl.semaphore_wait(barrier, len(others))


def gather_kernel(src, *refs):
    out, send, recv, own = refs[-4:]
    u, v, c, index = place()
    to_v, to_u, to_s = {"v": 1 - v}, {"u": 1 - u}, {"c": 1 - c}
    me, at_v, at_u, at_d = index(u, v, c), index(u, 1 - v, c), index(1 - u, v, c), index(1 - u, 1 - v, c)
    third = src.shape[0] // 3
    rows = (pl.ds(0, third), pl.ds(third, 2 * third))
    local = pltpu.make_async_copy(src, out.at[me], own)
    local.start()
    greet((to_v, to_u, to_s))

    def hop(slot, block, part, where, first=False):
        piece = out.at[block, rows[part]]
        return pltpu.make_async_remote_copy(
            src_ref=src.at[rows[part]] if first else piece,
            dst_ref=piece,
            send_sem=send.at[slot],
            recv_sem=recv.at[slot],
            device_id=where,
            device_id_type=MESH,
        )

    v0, v1 = hop(0, me, 0, to_v, True), hop(1, me, 1, to_v, True)
    u1, u0 = hop(2, me, 1, to_u, True), hop(3, me, 0, to_u, True)
    s0, s1 = hop(4, me, 0, to_s, True), hop(5, me, 1, to_s, True)
    for copy in (v0, u1, v1, u0, s0, s1):
        copy.start()
    v0.wait_recv()
    d0 = hop(6, at_v, 0, to_u)
    d0.start()
    u1.wait_recv()
    d1 = hop(7, at_u, 1, to_v)
    d1.start()
    sv0, su1 = hop(8, at_v, 0, to_s), hop(9, at_u, 1, to_s)
    sv0.start()
    su1.start()
    v1.wait_recv()
    sv1 = hop(10, at_v, 1, to_s)
    sv1.start()
    u0.wait_recv()
    su0 = hop(11, at_u, 0, to_s)
    su0.start()
    d0.wait_recv()
    sd0 = hop(12, at_d, 0, to_s)
    sd0.start()
    d1.wait_recv()
    sd1 = hop(13, at_d, 1, to_s)
    sd1.start()
    for copy in (s0, s1, sv0, su1, sv1, su0, sd0, sd1):
        copy.wait_recv()
    for copy in (v0, v1, u0, u1, s0, s1, d0, d1, sv0, su1, sv1, su0, sd0, sd1):
        copy.wait_send()
    local.wait()


def plane_gather(value, number, after=()):
    return pl.pallas_call(
        gather_kernel,
        out_shape=jax.ShapeDtypeStruct((8, *value.shape), value.dtype),
        in_specs=[HBM] * (1 + len(after)),
        out_specs=HBM,
        scratch_shapes=[
            pltpu.SemaphoreType.DMA((14,)),
            pltpu.SemaphoreType.DMA((14,)),
            pltpu.SemaphoreType.DMA,
        ],
        compiler_params=pltpu.CompilerParams(collective_id=number, has_side_effects=True),
        cost_estimate=pl.CostEstimate(flops=1, bytes_accessed=1, transcendentals=0),
        name="plane_gather",
    )(value, *after)


def sum_kernel(lefts, terms, tile, *refs):
    a_refs, w_refs = refs[:lefts], refs[lefts : lefts + len(terms)]
    out, s_send, s_recv, d_send, d_recv, v_send, v_recv, u_send, u_recv, v_acc, u_acc, send, recv = refs[-13:]
    u, v, c, index = place()
    to_v, to_u, to_s = {"v": 1 - v}, {"u": 1 - u}, {"c": 1 - c}
    rows, width = out.shape
    third = rows // 3
    parts = (pl.ds(0, 2 * third), pl.ds(2 * third, third))
    f32, low = jnp.float32, jnp.bfloat16

    def product(block, put):
        lines = pl.ds(pl.multiple_of(block * rows, rows), rows)

        @pl.loop(0, width // tile)
        def _(step):
            cols = pl.ds(pl.multiple_of(step * tile, tile), tile)
            total = None
            for (left, start), w_ref in zip(terms, w_refs):
                term = mm_nt(a_refs[left][lines, start : start + w_ref.shape[1]], w_ref[cols, :])
                total = term if total is None else total + term
            put(cols, total)

    def hop(slot, src, dst, where):
        copy = pltpu.make_async_remote_copy(
            src_ref=src, dst_ref=dst, send_sem=send.at[slot], recv_sem=recv.at[slot],
            device_id=where, device_id_type=MESH,
        )
        return copy

    def to_sibling(slot, uu, vv):
        def put(cols, total):
            s_send[slot, :, cols] = total.astype(low)

        product(index(uu, vv, 1 - c), put)
        copy = hop(slot, s_send.at[slot], s_recv.at[slot], to_s)
        copy.start()
        return copy

    def with_sibling(slot, uu, vv, keep):
        def put(cols, total):
            keep[:, cols] = (total + s_recv[slot, :, cols].astype(f32)).astype(keep.dtype)

        product(index(uu, vv, c), put)

    greet((to_v, to_u, to_s))
    s0 = to_sibling(0, 1 - u, 1 - v)
    s1 = to_sibling(1, u, 1 - v)
    s0.wait_recv()
    with_sibling(0, 1 - u, 1 - v, d_send)
    d0 = hop(4, d_send.at[parts[0]], d_recv.at[parts[0]], to_v)
    d1 = hop(5, d_send.at[parts[1]], d_recv.at[parts[1]], to_u)
    d0.start()
    d1.start()
    s1.wait_recv()
    with_sibling(1, u, 1 - v, v_acc)
    v_send[parts[0]] = v_acc[parts[0]].astype(low)
    v0 = hop(6, v_send.at[parts[0]], v_recv.at[parts[0]], to_v)
    v0.start()
    s2 = to_sibling(2, 1 - u, v)
    s2.wait_recv()
    with_sibling(2, 1 - u, v, u_acc)
    u_send[parts[1]] = u_acc[parts[1]].astype(low)
    u1 = hop(7, u_send.at[parts[1]], u_recv.at[parts[1]], to_u)
    u1.start()
    s3 = to_sibling(3, u, v)
    d1.wait_recv()
    v_send[parts[1]] = (v_acc[parts[1]] + d_recv[parts[1]].astype(f32)).astype(low)
    v1 = hop(8, v_send.at[parts[1]], v_recv.at[parts[1]], to_v)
    v1.start()
    d0.wait_recv()
    u_send[parts[0]] = (u_acc[parts[0]] + d_recv[parts[0]].astype(f32)).astype(low)
    u0 = hop(9, u_send.at[parts[0]], u_recv.at[parts[0]], to_u)
    u0.start()
    s3.wait_recv()
    with_sibling(3, u, v, out)
    v0.wait_recv()
    u1.wait_recv()
    v1.wait_recv()
    u0.wait_recv()
    out[...] += v_recv[...].astype(f32) + u_recv[...].astype(f32)
    for copy in (s0, s1, s2, s3, d0, d1, v0, v1, u0, u1):
        copy.wait_send()


def plane_sum(lefts, rights, number, after=(), tile=512):
    ends = [(left, start) for left, a in enumerate(lefts) for start in range(0, a.shape[1], rights[0].shape[1])]
    terms = tuple(ends[: len(rights)])
    rows, width = lefts[0].shape[0] // 8, rights[0].shape[0]
    block = (rows, width)
    low, f32 = jnp.bfloat16, jnp.float32
    return pl.pallas_call(
        functools.partial(sum_kernel, len(lefts), terms, min(tile, width)),
        out_shape=jax.ShapeDtypeStruct(block, f32),
        in_specs=[VMEM] * (len(lefts) + len(rights)) + [HBM] * len(after),
        out_specs=VMEM,
        scratch_shapes=[
            pltpu.VMEM((4, *block), low),
            pltpu.VMEM((4, *block), low),
            *[pltpu.VMEM(block, low)] * 6,
            pltpu.VMEM(block, f32),
            pltpu.VMEM(block, f32),
            pltpu.SemaphoreType.DMA((10,)),
            pltpu.SemaphoreType.DMA((10,)),
        ],
        compiler_params=pltpu.CompilerParams(
            collective_id=number, has_side_effects=True, vmem_limit_bytes=48 * 2**20
        ),
        cost_estimate=pl.CostEstimate(flops=1, bytes_accessed=1, transcendentals=0),
        name="plane_sum",
    )(*lefts, *rights, *after)


def swap_kernel(pieces, takes, *refs):
    count = len(pieces)
    sources, (send, recv, own) = refs[: -2 * count - 3], refs[-3:]
    outs, holds = refs[-2 * count - 3 : -count - 3], refs[-count - 3 : -3]
    u, v, c, index = place()
    me = index(u, v, c)
    flips = [(fu, fv, fc) for fu, fv in ((1, 1), (0, 1), (1, 0), (0, 0)) for fc in (0, 1)]
    flips = [flip for flip in flips if flip != (0, 0, 0)]

    def there(flip):
        return tuple(1 - at if f else at for at, f in zip((u, v, c), flip))

    greet([dict(zip(("u", "v", "c"), there(flip))) for flip in flips])
    copies = []
    for piece in range(count):
        for number, flip in enumerate(flips):
            uu, vv, cc = there(flip)
            member = index(uu, vv, cc)
            holds[piece][number] = takes[piece](sources, member, cc)
            copy = pltpu.make_async_remote_copy(
                src_ref=holds[piece].at[number],
                dst_ref=outs[piece].at[me],
                send_sem=send.at[piece * 7 + number],
                recv_sem=recv.at[piece * 7 + number],
                device_id={"u": uu, "v": vv, "c": cc},
                device_id_type=MESH,
            )
            copy.start()
            copies.append(copy)
        holds[piece][7] = takes[piece](sources, me, c)
        keep = pltpu.make_async_copy(holds[piece].at[7], outs[piece].at[me], own.at[piece])
        keep.start()
        copies.append(keep)
    for copy in copies:
        copy.wait()


def plane_swap(sources, shapes, takes, number, after=()):
    low = jnp.bfloat16
    count = len(shapes)
    return pl.pallas_call(
        functools.partial(swap_kernel, shapes, takes),
        out_shape=[jax.ShapeDtypeStruct((8, *shape), low) for shape in shapes],
        in_specs=[VMEM] * len(sources) + [HBM] * len(after),
        out_specs=[HBM] * count,
        scratch_shapes=[
            *[pltpu.VMEM((8, *shape), low) for shape in shapes],
            pltpu.SemaphoreType.DMA((7 * count,)),
            pltpu.SemaphoreType.DMA((7 * count,)),
            pltpu.SemaphoreType.DMA((count,)),
        ],
        compiler_params=pltpu.CompilerParams(
            collective_id=number, has_side_effects=True, vmem_limit_bytes=48 * 2**20
        ),
        cost_estimate=pl.CostEstimate(flops=1, bytes_accessed=1, transcendentals=0),
        name="plane_swap",
    )(*sources, *after)


def total_kernel(pools, src, out, near, far, send, recv):
    u, v, c, index = place()
    across, high = pools
    xx, hh = lax.axis_index("x"), lax.axis_index("h")
    at = xx * high + hh
    me = index(u, v, c)
    flips = [(fu, fv, fc) for fu in (0, 1) for fv in (0, 1) for fc in (0, 1)][1:]
    team = [
        dict(zip(("u", "v", "c"), (1 - at if f else at for at, f in zip((u, v, c), flip)))) for flip in flips
    ]
    column = [
        {"x": lax.rem(xx + fx, across), "h": lax.rem(hh + fh, high)} for fx in range(across) for fh in range(high)
    ][1:]
    near[me] = src[...]
    greet(team + column)

    def spread(buffer, at, others, base):
        copies = [
            pltpu.make_async_remote_copy(
                src_ref=buffer.at[at],
                dst_ref=buffer.at[at],
                send_sem=send.at[base + number],
                recv_sem=recv.at[base + number],
                device_id=other,
                device_id_type=MESH,
            )
            for number, other in enumerate(others)
        ]
        for copy in copies:
            copy.start()
        for copy in copies:
            copy.wait()

    spread(near, me, team, 0)
    far[at] = jnp.sum(near[...], axis=0)
    spread(far, at, column, 7)
    out[...] = jnp.sum(far[...], axis=0)


def total_sum(value, pools, number):
    return pl.pallas_call(
        functools.partial(total_kernel, pools),
        out_shape=jax.ShapeDtypeStruct(value.shape, value.dtype),
        in_specs=[VMEM],
        out_specs=VMEM,
        scratch_shapes=[
            pltpu.VMEM((8, *value.shape), value.dtype),
            pltpu.VMEM((pools[0] * pools[1], *value.shape), value.dtype),
            pltpu.SemaphoreType.DMA((6 + pools[0] * pools[1],)),
            pltpu.SemaphoreType.DMA((6 + pools[0] * pools[1],)),
        ],
        compiler_params=pltpu.CompilerParams(collective_id=number, has_side_effects=True),
        cost_estimate=pl.CostEstimate(flops=1, bytes_accessed=1, transcendentals=0),
        name="total_sum",
    )(value)


def dot(left, right, contract):
    return lax.dot_general(left, right, (contract, ((), ())), preferred_element_type=jnp.float32)


def mm(left, right):
    return dot(left, right, ((1,), (0,)))


def mm_nt(left, right):
    return dot(left, right, ((1,), (1,)))


def mm_tn(left, right):
    return dot(left, right, ((0,), (0,)))


def bmm(pattern, left, right):
    return jnp.einsum(pattern, left, right, preferred_element_type=jnp.float32)


def angle_tables(positions):
    half_dim = HEAD_SIZE // 2
    frequency = rope_base ** (-(jnp.arange(half_dim).astype(jnp.float32) * 2.0) / HEAD_SIZE)
    phases = positions.astype(jnp.float32)[:, None] * frequency[None, :]
    return (jnp.cos(phases), jnp.sin(phases))


def rotate(value, cos_table, sin_table):
    half = value.shape[-1] // 2
    a, b = value[..., :half], value[..., half:]
    return jnp.concatenate([a * cos_table - b * sin_table, b * cos_table + a * sin_table], axis=-1)


def rms_forward(value, gain_row):
    inverse = lax.rsqrt(jnp.mean(value * value, axis=-1, keepdims=True) + norm_eps)
    return (value * inverse * gain_row, inverse)


def rms_back(grad_out, value, inverse, gain_row):
    scaled = grad_out * gain_row
    grad_in = inverse * (
        scaled - value * inverse * inverse * jnp.mean(scaled * value, axis=-1, keepdims=True)
    )
    return (grad_in, jnp.sum(grad_out * value * inverse, axis=0))


def adamw(weight, gradient, moment_one, moment_two, step_rate, decay_rate):
    mean_new = beta_one * moment_one + (1.0 - beta_one) * gradient
    square_new = beta_two * moment_two + (1.0 - beta_two) * gradient * gradient
    direction = (
        mean_new
        / (1.0 - beta_one**STEP)
        / (jnp.sqrt(square_new / (1.0 - beta_two**STEP)) + adam_eps)
    )
    return (weight - step_rate * (direction + decay_rate * weight), mean_new, square_new)


def attention_parts(core, length, q_ref, mine_ref, other_ref, query_ref, key_ref):
    mine, other = mine_ref[...].reshape(-1, HEAD_SIZE), other_ref[...].reshape(-1, HEAD_SIZE)
    first = core == 0
    k, v = jnp.where(first, mine, other), jnp.where(first, other, mine)
    q = q_ref[...].reshape(-1, HEAD_SIZE)
    at, key_at = query_ref[...], key_ref[...]
    allowed = (key_at <= at) & (key_at < length) & (key_at >= 0)
    scores = jnp.where(allowed, mm_nt(q, k) * HEAD_SIZE ** (-0.5), masked_value)
    exponent = jnp.exp(scores - jnp.max(scores, axis=-1, keepdims=True))
    return q, k, v, exponent / jnp.sum(exponent, axis=-1, keepdims=True)


def attention_kernel(core_ref, length_ref, q_ref, mine_ref, other_ref, query_ref, key_ref, out_ref):
    length = length_ref[pl.program_id(0)]
    _, _, v, soft = attention_parts(core_ref[0], length, q_ref, mine_ref, other_ref, query_ref, key_ref)
    out_ref[...] = mm(soft.astype(jnp.bfloat16), v).astype(jnp.bfloat16).reshape(out_ref.shape)


def attention_back_kernel(
    core_ref, length_ref, q_ref, mine_ref, other_ref, query_ref, key_ref, do_ref, cos_ref, sin_ref,
    dq_ref, keep_ref, send_ref,
):
    low = jnp.bfloat16
    core = core_ref[0]
    length = length_ref[pl.program_id(0)]
    q, k, v, soft = attention_parts(core, length, q_ref, mine_ref, other_ref, query_ref, key_ref)
    do = do_ref[...].reshape(-1, HEAD_SIZE)
    dp = mm_nt(do, v)
    delta = jnp.sum(soft * dp, axis=-1, keepdims=True)
    ds = (soft * (dp - delta) * HEAD_SIZE ** (-0.5)).astype(low)
    dq = mm(ds, k)
    cos_table, sin_table = cos_ref[...], sin_ref[...]
    half = HEAD_SIZE // 2
    a, b = dq[:, :half], dq[:, half:]
    turned = jnp.concatenate([a * cos_table + b * sin_table, b * cos_table - a * sin_table], axis=-1)
    dq_ref[...] = turned.astype(low).reshape(dq_ref.shape)
    dk, dv = mm_tn(ds, q), mm_tn(soft.astype(low), do)
    first = core == 0
    keep_ref[...] = jnp.where(first, dk, dv).reshape(keep_ref.shape)
    send_ref[...] = jnp.where(first, dv, dk).astype(low).reshape(send_ref.shape)


def attention_call(kernel, core, lengths, q, mine, other, query_pos, key_pos, extra, outs, name):
    ny, count, span, size = q.shape
    nz = mine.shape[0]
    rows = pl.BlockSpec((ny, 1, span, size), lambda i, *_: (0, i, 0, 0))
    keys = pl.BlockSpec((nz, ny, 1, span, size), lambda i, *_: (0, 0, i, 0, 0))

    def whole(value):
        return pl.BlockSpec(value.shape, lambda i, *_: (0,) * value.ndim)

    kinds = {"rows": (rows, q.shape), "keys": (keys, mine.shape)}
    return pl.pallas_call(
        kernel,
        grid_spec=pltpu.PrefetchScalarGridSpec(
            num_scalar_prefetch=2,
            grid=(count,),
            in_specs=[rows, keys, keys, whole(query_pos), whole(key_pos)]
            + [rows if value.shape == q.shape else whole(value) for value in extra],
            out_specs=[kinds[kind][0] for kind, _ in outs],
        ),
        out_shape=[jax.ShapeDtypeStruct(kinds[kind][1], dtype) for kind, dtype in outs],
        compiler_params=pltpu.CompilerParams(vmem_limit_bytes=48 * 2**20),
        cost_estimate=pl.CostEstimate(flops=1, bytes_accessed=1, transcendentals=0),
        name=name,
    )(core, lengths, q, mine, other, query_pos, key_pos, *extra)


def feed_back_kernel(dyb_ref, weight_ref, gate_ref, up_ref, out_ref):
    dm = mm(dyb_ref[...], weight_ref[...])
    gate, upward = gate_ref[...], up_ref[...]
    sig = jax.nn.sigmoid(gate)
    part = gate.shape[1]
    out_ref[:, :part] = (dm * upward * sig * (1.0 + gate * (1.0 - sig))).astype(out_ref.dtype)
    out_ref[:, part:] = (dm * gate * sig).astype(out_ref.dtype)


def feed_back(dyb, weight, gate, upward, lines=256):
    count, part = gate.shape

    def rows(width):
        return pl.BlockSpec((lines, width), lambda i: (i, 0))

    return pl.pallas_call(
        feed_back_kernel,
        grid=(count // lines,),
        in_specs=[rows(dyb.shape[1]), pl.BlockSpec(weight.shape, lambda i: (0, 0)), rows(part), rows(part)],
        out_specs=rows(2 * part),
        out_shape=jax.ShapeDtypeStruct((count, 2 * part), jnp.bfloat16),
        compiler_params=pltpu.CompilerParams(vmem_limit_bytes=48 * 2**20),
        cost_estimate=pl.CostEstimate(flops=1, bytes_accessed=1, transcendentals=0),
        name="feed_back",
    )(dyb, weight, gate, upward)


def exchange_x(value):
    return lax.ppermute(value, "x", [(0, 1), (1, 0)])


def gather_teams(blocks):
    return lax.all_gather(blocks.reshape(-1, blocks.shape[-1]), "h", axis=0, tiled=True)


def gather_across(own):
    if lax.axis_size("x") == 2:
        return [own, exchange_x(own)]
    return [lax.all_gather(own, "x", axis=0, tiled=True)]


def halves(left):
    if lax.axis_size("x") == 2:
        half = left.shape[1] // 2
        return left[:, :half], left[:, half:]
    return left, None


def arrive(go):
    return None if go is None else exchange_x(go)


def add_across(stay, came):
    low = jnp.bfloat16
    if came is None:
        return lax.psum_scatter(stay.astype(low), "x", scatter_dimension=0, tiled=True)
    return (stay + came.astype(jnp.float32)).astype(low)


def scatter_teams(term):
    return lax.psum_scatter(term, "h", scatter_dimension=0, tiled=True)


def together(*values):
    return lax.optimization_barrier(values)


def scatter_team(rows, number, after=()):
    count = rows.shape[0] // 8

    def take(sources, member, core):
        return sources[0][pl.ds(pl.multiple_of(member * count, count), count), :]

    return plane_swap([rows], [(count, rows.shape[1])], [take], number, after)[0]


def team_gather(local, number, after=()):
    return plane_gather(local, number, after).reshape(-1, local.shape[1])


def features_in(value):
    high, across = lax.axis_size("h"), lax.axis_size("x")
    shape = value.shape
    value = jnp.swapaxes(value.reshape(*shape[:-1], high * 4, across, -1), -3, -2)
    if across == 2:
        value = jnp.where(lax.axis_index("x") == 0, value, jnp.flip(value, -3))
    return value.reshape(shape)


def features_out(value):
    high, across = lax.axis_size("h"), lax.axis_size("x")
    shape = value.shape
    value = value.reshape(*shape[:-1], across, high * 4, -1)
    if across == 2:
        value = jnp.where(lax.axis_index("x") == 0, value, jnp.flip(value, -3))
    return jnp.swapaxes(value, -3, -2).reshape(shape)


def local(
    tokens,
    lengths,
    norm_gains,
    attention_weight,
    feed_weight,
    cotangent,
    attention_mean,
    attention_square,
    feed_mean,
    feed_square,
    gain_mean,
    gain_square,
):
    low = jnp.bfloat16
    sequences, span, width = tokens.shape
    high, across = lax.axis_size("h"), lax.axis_size("x")
    core, first = lax.axis_index("c"), lax.axis_index("c") == 0
    rows = attention_weight.shape[0]
    q_width, kv_width = QUERY_HEADS * HEAD_SIZE, KEY_VALUE_HEADS * HEAD_SIZE
    count = sequences * span
    reach = 4 * span
    near = high <= 4
    ff_part = FF // 8

    def columns(start, size):
        return pl.ds(pl.multiple_of(start, size), size)

    def take_attention(sources, member, c):
        source = sources[0]
        starts = (
            member * HEAD_SIZE,
            q_width + c * kv_width + (member - c) // 2 * HEAD_SIZE,
            q_width + 2 * kv_width + member * HEAD_SIZE,
        )
        return jnp.concatenate([source[:, columns(s, HEAD_SIZE)].astype(low) for s in starts], axis=1)

    def take_feed(part):
        return lambda sources, member, c: sources[0][
            :, columns(part * FF + member * ff_part, ff_part)
        ].astype(low)

    def spread(source, take, size, number, after=()):
        blocks = plane_swap([source], [(rows, size)], [take], number, after)[0]
        return blocks, gather_teams(blocks)

    def product(left, right):
        stay, go = halves(left)
        return mm_tn(stay, right), None if go is None else mm_tn(go, right).astype(low)

    attention_blocks, attention_mine = spread(attention_weight, take_attention, 3 * HEAD_SIZE, 1)

    team_base = lax.axis_index("h") * reach
    team_pos = team_base + jnp.arange(reach, dtype=jnp.int32)
    own_pos = team_base + (lax.axis_index("u") * 2 + lax.axis_index("v")) * span + jnp.arange(span, dtype=jnp.int32)
    if near:
        key_pos = jnp.concatenate([team_pos - back * reach for back in range(high)])
    else:
        key_pos = jnp.arange(high * reach, dtype=jnp.int32)
    query_at, key_at = team_pos[:, None], key_pos[None, :]
    cos_table, sin_table = angle_tables(team_pos)
    cos_rows, sin_rows = (t.reshape(4, 1, span, -1) for t in (cos_table, sin_table))
    valid = (own_pos[None, :] < lengths[:, None]).astype(jnp.float32).reshape(count, 1)
    lengths_all = lax.all_gather(lengths, "c", axis=0, tiled=True)
    core_at = jnp.reshape(core, (1,)).astype(jnp.int32)

    def heads(value):
        return value.reshape(4, 2 * sequences, span, HEAD_SIZE)

    gains = features_in(norm_gains)
    x_in = features_in(tokens.reshape(count, width).astype(jnp.float32))
    normed_one, inverse_one = rms_forward(x_in, gains[0])
    outer_grad = features_in(cotangent.reshape(count, width)).astype(jnp.float32) * valid
    h1 = team_gather(normed_one.astype(low), 3, [attention_blocks])
    gate_blocks, gate_weight = spread(feed_weight, take_feed(0), ff_part, 2, [h1])
    up_blocks, up_weight = spread(feed_weight, take_feed(1), ff_part, 18, [gate_blocks, attention_mine])
    down_blocks, down_weight = spread(feed_weight, take_feed(2), ff_part, 12, [up_blocks])
    attention_mine = gather_across(attention_mine)
    attention_mine, down_blocks, lengths_all = together(attention_mine, down_blocks, lengths_all)
    attention_mine = jnp.concatenate(attention_mine)
    query_weight = attention_mine[:, :HEAD_SIZE]
    kv_weight = attention_mine[:, HEAD_SIZE : 2 * HEAD_SIZE]
    out_weight = attention_mine[:, 2 * HEAD_SIZE :]
    kv_raw = heads(mm(h1, kv_weight))
    kv = jnp.where(first, rotate(kv_raw, cos_rows, sin_rows), kv_raw).astype(low)
    q = rotate(heads(mm(h1, query_weight)), cos_rows, sin_rows).astype(low)
    gate_weight, kv = together(gate_weight, kv)
    gate_weight = gather_across(gate_weight)
    dyb = team_gather(outer_grad.astype(low), 15, [kv])
    if near:
        earlier = [
            lax.ppermute(kv, "h", [(at, at + back) for at in range(high - back)]) for back in range(1, high)
        ]
        *earlier, dyb, q = together(*earlier, dyb, q)
        kv = jnp.stack([kv, *earlier])
    else:
        kv = lax.all_gather(kv, "h", axis=0, tiled=False)
    other = lax.ppermute(kv, "c", [(0, 1), (1, 0)])
    attend = (core_at, lengths_all, q, kv, other, query_at, key_at)
    (o,) = attention_call(attention_kernel, *attend, (), [("rows", low)], "attention")
    o = o.reshape(-1, HEAD_SIZE)
    r = x_in + plane_sum([o], [out_weight], 4)
    up_weight, r = together(up_weight, r)
    up_weight = gather_across(up_weight)

    normed_two, inverse_two = rms_forward(r, gains[1])
    h2 = team_gather(normed_two.astype(low), 16)
    h2, down_weight = together(h2, down_weight)
    down_weight = gather_across(down_weight)
    gate_weight, up_weight = jnp.concatenate(gate_weight), jnp.concatenate(up_weight)
    gate, upward = mm(h2, gate_weight), mm(h2, up_weight)
    m = (gate * jax.nn.sigmoid(gate) * upward).astype(low)
    down_stay, down_go = product(dyb, m)
    down_came = arrive(down_go)
    down_weight, down_stay = together(down_weight, down_stay)
    down_weight = jnp.concatenate(down_weight)
    d_both = feed_back(dyb, down_weight, gate, upward)
    gate_up_stay, gate_up_go = product(h2, d_both)
    gate_up_came = arrive(gate_up_go)
    d_both, gate_up_go, gate_up_stay, down_came = together(d_both, gate_up_go, gate_up_stay, down_came)
    down_rows = scatter_teams(add_across(down_stay, down_came))
    dh2 = plane_sum([d_both], [gate_weight, up_weight], 7)
    mid_grad, gain_two = rms_back(dh2, r, inverse_two, gains[1])
    dr = outer_grad + mid_grad
    drb = team_gather(dr.astype(low), 13, [gate_up_stay, down_rows])

    do = heads(mm(drb, out_weight).astype(low))
    do, gate_up_came = together(do, gate_up_came)
    gate_up_rows = scatter_teams(add_across(gate_up_stay, gate_up_came))
    dq, keep, theirs = attention_call(
        attention_back_kernel,
        *attend,
        (do, cos_table, sin_table),
        [("rows", low), ("keys", jnp.float32), ("keys", low)],
        "attention_back",
    )
    dq = dq.reshape(-1, HEAD_SIZE)
    terms = [product(h1, dq), product(drb, o)]
    qo_stay = jnp.concatenate([stay for stay, _ in terms], axis=1)
    qo_go = None if terms[0][1] is None else jnp.concatenate([go for _, go in terms], axis=1)
    qo_came = arrive(qo_go)
    dkv = keep + lax.ppermute(theirs, "c", [(0, 1), (1, 0)]).astype(jnp.float32)
    low_terms = dkv.astype(low)
    feed_sum = plane_sum([m], [down_weight], 5, [low_terms])
    down_grad = scatter_team(down_rows, 6, [low_terms])
    qo_came, feed_sum = together(qo_came, feed_sum)
    qo_rows = scatter_teams(add_across(qo_stay, qo_came))
    if near:
        later = [
            lax.ppermute(low_terms[back], "h", [(at + back, at) for at in range(high - back)])
            for back in range(1, high)
        ]
        *later, feed_sum, down_grad, gate_up_rows = together(*later, feed_sum, down_grad, gate_up_rows)
        dkv = dkv[0] + sum(term.astype(jnp.float32) for term in later)
    else:
        dkv = lax.psum_scatter(low_terms, "h", scatter_dimension=0, tiled=True)[0].astype(jnp.float32)
    dkv = jnp.where(first, rotate(dkv, cos_rows, -sin_rows), dkv).astype(low).reshape(-1, HEAD_SIZE)
    layer_output = features_out(r + feed_sum).astype(low)
    kv_stay, kv_go = product(h1, dkv)
    kv_term = add_across(kv_stay, arrive(kv_go))
    kv_rows = scatter_teams(kv_term)
    dh1 = plane_sum([dq, dkv], [query_weight, kv_weight], 9, [kv_stay] if kv_go is None else [kv_stay, kv_go])
    in_grad, gain_one = rms_back(dh1, x_in, inverse_one, gains[0])
    input_gradient = features_out(dr + in_grad)
    gate_up_grad = scatter_team(gate_up_rows, 8, [dh1, kv_term])
    qo_grad = scatter_team(qo_rows, 10, [dh1, kv_term]).astype(jnp.float32)
    kv_grad = scatter_team(kv_rows, 14).astype(jnp.float32)

    def columns_of(blocks):
        return blocks.transpose(1, 0, 2).reshape(rows, -1)

    attention_grad = jnp.concatenate(
        [
            columns_of(qo_grad[:, :, :HEAD_SIZE]),
            kv_grad.reshape(KEY_VALUE_HEADS, 2, rows, HEAD_SIZE).transpose(2, 1, 0, 3).reshape(rows, 2 * kv_width),
            columns_of(qo_grad[:, :, HEAD_SIZE:]),
        ],
        axis=1,
    )
    feed_grad = jnp.concatenate(
        [
            columns_of(g.astype(jnp.float32))
            for g in (gate_up_grad[:, :, :ff_part], gate_up_grad[:, :, ff_part:], down_grad)
        ], axis=1
    )
    local_squares = jnp.sum(attention_grad * attention_grad) + jnp.sum(feed_grad * feed_grad)
    gain_local = features_out(jnp.stack([gain_one, gain_two]))
    lines = jnp.concatenate([gain_local.reshape(-1, 128), jnp.full((8, 128), local_squares)], axis=0)
    lines = total_sum(lines, (across, high), 11)
    gain_grad, squares = lines[:-8].reshape(2, width), lines[-1, 0]
    gradient_norm = jnp.sqrt(squares + jnp.sum(gain_grad * gain_grad))
    factor = clip_norm / gradient_norm
    attention_new = adamw(
        attention_weight, attention_grad * factor, attention_mean, attention_square, matrix_rate, weight_decay
    )
    feed_new = adamw(feed_weight, feed_grad * factor, feed_mean, feed_square, matrix_rate, weight_decay)
    gains_new = adamw(norm_gains, gain_grad * factor, gain_mean, gain_square, gain_rate, 0.0)
    return (
        layer_output.reshape(sequences, span, width),
        input_gradient.reshape(sequences, span, width),
        gradient_norm,
        *attention_new,
        attention_new[0].astype(low),
        *feed_new,
        feed_new[0].astype(low),
        *gains_new,
    )


def solution(mesh):
    ctx, fsdp = mesh.shape["ctx"], mesh.shape["fsdp"]
    fine = Mesh(mesh.devices.reshape(ctx // 4, 2, 2, fsdp // 2, 2), ALL)
    act = P(("x", "c"), ("h", "u", "v"), None)
    matrix = P(ALL, None)
    return jax.shard_map(
        local,
        mesh=fine,
        in_specs=(act, P(("x", "c")), P(), matrix, matrix, act, matrix, matrix, matrix, matrix, P(), P()),
        out_specs=(act, act, P(), matrix, matrix, matrix, matrix, matrix, matrix, matrix, matrix, P(), P(), P()),
        check_vma=False,
    )
```

```python
import functools

import jax
import jax.numpy as jnp
from jax import lax
from jax.experimental import pallas as pl
from jax.experimental.pallas import tpu as pltpu
from jax.sharding import Mesh, PartitionSpec as P

QUERY_HEADS = 8
KEY_VALUE_HEADS = 4
HEAD_SIZE = 256
FF = 8192
STEP = 10

norm_eps = 1e-06
rope_base = 1000042.0
masked_value = -1e30
clip_norm = 1.0
beta_one = 0.9
beta_two = 0.95
adam_eps = 1e-08
matrix_rate = 0.03
gain_rate = 0.4
weight_decay = 0.1

TEAM = ("y", "x", "c")
ALL = ("z", "y", "x", "c")


MESH = pl.DeviceIdType.MESH
VMEM = pl.BlockSpec(memory_space=pltpu.VMEM)
HBM = pl.BlockSpec(memory_space=pl.ANY)


def place():
    y, x, c = lax.axis_index("y"), lax.axis_index("x"), lax.axis_index("c")
    return y, x, c, lambda yy, xx, cc: (yy * 2 + xx) * 2 + cc


def greet(others):
    barrier = pltpu.get_barrier_semaphore()
    for other in others:
        pl.semaphore_signal(barrier, inc=1, device_id=other, device_id_type=MESH)
    pl.semaphore_wait(barrier, len(others))


def gather_kernel(src, *refs):
    out, send, recv, own = refs[-4:]
    y, x, c, index = place()
    to_x, to_y, to_s = {"x": 1 - x}, {"y": 1 - y}, {"c": 1 - c}
    me, at_x, at_y, at_d = index(y, x, c), index(y, 1 - x, c), index(1 - y, x, c), index(1 - y, 1 - x, c)
    half = src.shape[0] // 2
    rows = (pl.ds(0, half), pl.ds(half, half))
    local = pltpu.make_async_copy(src, out.at[me], own)
    local.start()
    greet((to_x, to_y, to_s))

    def hop(slot, block, part, where, first=False):
        piece = out.at[block, rows[part]]
        return pltpu.make_async_remote_copy(
            src_ref=src.at[rows[part]] if first else piece,
            dst_ref=piece,
            send_sem=send.at[slot],
            recv_sem=recv.at[slot],
            device_id=where,
            device_id_type=MESH,
        )

    x0, x1 = hop(0, me, 0, to_x, True), hop(1, me, 1, to_x, True)
    y1, y0 = hop(2, me, 1, to_y, True), hop(3, me, 0, to_y, True)
    s0, s1 = hop(4, me, 0, to_s, True), hop(5, me, 1, to_s, True)
    for copy in (x0, y1, x1, y0, s0, s1):
        copy.start()
    x0.wait_recv()
    d0 = hop(6, at_x, 0, to_y)
    d0.start()
    y1.wait_recv()
    d1 = hop(7, at_y, 1, to_x)
    d1.start()
    sx0, sy1 = hop(8, at_x, 0, to_s), hop(9, at_y, 1, to_s)
    sx0.start()
    sy1.start()
    x1.wait_recv()
    sx1 = hop(10, at_x, 1, to_s)
    sx1.start()
    y0.wait_recv()
    sy0 = hop(11, at_y, 0, to_s)
    sy0.start()
    d0.wait_recv()
    sd0 = hop(12, at_d, 0, to_s)
    sd0.start()
    d1.wait_recv()
    sd1 = hop(13, at_d, 1, to_s)
    sd1.start()
    for copy in (s0, s1, sx0, sy1, sx1, sy0, sd0, sd1):
        copy.wait_recv()
    for copy in (x0, x1, y0, y1, s0, s1, d0, d1, sx0, sy1, sx1, sy0, sd0, sd1):
        copy.wait_send()
    local.wait()


def plane_gather(value, number, after=()):
    return pl.pallas_call(
        gather_kernel,
        out_shape=jax.ShapeDtypeStruct((8, *value.shape), value.dtype),
        in_specs=[HBM] * (1 + len(after)),
        out_specs=HBM,
        scratch_shapes=[
            pltpu.SemaphoreType.DMA((14,)),
            pltpu.SemaphoreType.DMA((14,)),
            pltpu.SemaphoreType.DMA,
        ],
        compiler_params=pltpu.CompilerParams(collective_id=number, has_side_effects=True),
        cost_estimate=pl.CostEstimate(flops=1, bytes_accessed=1, transcendentals=0),
        name="plane_gather",
    )(value, *after)


def sum_kernel(lefts, terms, tile, *refs):
    a_refs, w_refs = refs[:lefts], refs[lefts : lefts + len(terms)]
    out, s_send, s_recv, d_send, d_recv, x_send, x_recv, y_send, y_recv, x_acc, y_acc, send, recv = refs[-13:]
    y, x, c, index = place()
    to_x, to_y, to_s = {"x": 1 - x}, {"y": 1 - y}, {"c": 1 - c}
    rows, width = out.shape
    half = rows // 2
    parts = (pl.ds(0, half), pl.ds(half, half))
    f32, low = jnp.float32, jnp.bfloat16

    def product(block, put):
        lines = pl.ds(pl.multiple_of(block * rows, rows), rows)

        @pl.loop(0, width // tile)
        def _(step):
            cols = pl.ds(pl.multiple_of(step * tile, tile), tile)
            total = None
            for (left, start), w_ref in zip(terms, w_refs):
                term = mm_nt(a_refs[left][lines, start : start + w_ref.shape[1]], w_ref[cols, :])
                total = term if total is None else total + term
            put(cols, total)

    def hop(slot, src, dst, where):
        copy = pltpu.make_async_remote_copy(
            src_ref=src, dst_ref=dst, send_sem=send.at[slot], recv_sem=recv.at[slot],
            device_id=where, device_id_type=MESH,
        )
        return copy

    def to_sibling(slot, yy, xx):
        def put(cols, total):
            s_send[slot, :, cols] = total.astype(low)

        product(index(yy, xx, 1 - c), put)
        copy = hop(slot, s_send.at[slot], s_recv.at[slot], to_s)
        copy.start()
        return copy

    def with_sibling(slot, yy, xx, keep):
        def put(cols, total):
            keep[:, cols] = (total + s_recv[slot, :, cols].astype(f32)).astype(keep.dtype)

        product(index(yy, xx, c), put)

    greet((to_x, to_y, to_s))
    s0 = to_sibling(0, 1 - y, 1 - x)
    s1 = to_sibling(1, y, 1 - x)
    s0.wait_recv()
    with_sibling(0, 1 - y, 1 - x, d_send)
    d0 = hop(4, d_send.at[parts[0]], d_recv.at[parts[0]], to_x)
    d1 = hop(5, d_send.at[parts[1]], d_recv.at[parts[1]], to_y)
    d0.start()
    d1.start()
    s1.wait_recv()
    with_sibling(1, y, 1 - x, x_acc)
    x_send[parts[0]] = x_acc[parts[0]].astype(low)
    x0 = hop(6, x_send.at[parts[0]], x_recv.at[parts[0]], to_x)
    x0.start()
    s2 = to_sibling(2, 1 - y, x)
    s2.wait_recv()
    with_sibling(2, 1 - y, x, y_acc)
    y_send[parts[1]] = y_acc[parts[1]].astype(low)
    y1 = hop(7, y_send.at[parts[1]], y_recv.at[parts[1]], to_y)
    y1.start()
    s3 = to_sibling(3, y, x)
    d1.wait_recv()
    x_send[parts[1]] = (x_acc[parts[1]] + d_recv[parts[1]].astype(f32)).astype(low)
    x1 = hop(8, x_send.at[parts[1]], x_recv.at[parts[1]], to_x)
    x1.start()
    d0.wait_recv()
    y_send[parts[0]] = (y_acc[parts[0]] + d_recv[parts[0]].astype(f32)).astype(low)
    y0 = hop(9, y_send.at[parts[0]], y_recv.at[parts[0]], to_y)
    y0.start()
    s3.wait_recv()
    with_sibling(3, y, x, out)
    x0.wait_recv()
    y1.wait_recv()
    x1.wait_recv()
    y0.wait_recv()
    out[...] += x_recv[...].astype(f32) + y_recv[...].astype(f32)
    for copy in (s0, s1, s2, s3, d0, d1, x0, x1, y0, y1):
        copy.wait_send()


def plane_sum(lefts, rights, number, after=(), tile=512):
    ends = [(left, start) for left, a in enumerate(lefts) for start in range(0, a.shape[1], rights[0].shape[1])]
    terms = tuple(ends[: len(rights)])
    rows, width = lefts[0].shape[0] // 8, rights[0].shape[0]
    block = (rows, width)
    low, f32 = jnp.bfloat16, jnp.float32
    return pl.pallas_call(
        functools.partial(sum_kernel, len(lefts), terms, min(tile, width)),
        out_shape=jax.ShapeDtypeStruct(block, f32),
        in_specs=[VMEM] * (len(lefts) + len(rights)) + [HBM] * len(after),
        out_specs=VMEM,
        scratch_shapes=[
            pltpu.VMEM((4, *block), low),
            pltpu.VMEM((4, *block), low),
            *[pltpu.VMEM(block, low)] * 6,
            pltpu.VMEM(block, f32),
            pltpu.VMEM(block, f32),
            pltpu.SemaphoreType.DMA((10,)),
            pltpu.SemaphoreType.DMA((10,)),
        ],
        compiler_params=pltpu.CompilerParams(
            collective_id=number, has_side_effects=True, vmem_limit_bytes=48 * 2**20
        ),
        cost_estimate=pl.CostEstimate(flops=1, bytes_accessed=1, transcendentals=0),
        name="plane_sum",
    )(*lefts, *rights, *after)


def swap_kernel(pieces, takes, *refs):
    count = len(pieces)
    sources, (send, recv, own) = refs[: -2 * count - 3], refs[-3:]
    outs, holds = refs[-2 * count - 3 : -count - 3], refs[-count - 3 : -3]
    y, x, c, index = place()
    me = index(y, x, c)
    flips = [(fy, fx, fc) for fy, fx in ((1, 1), (0, 1), (1, 0), (0, 0)) for fc in (0, 1)]
    flips = [flip for flip in flips if flip != (0, 0, 0)]

    def there(flip):
        return tuple(1 - at if f else at for at, f in zip((y, x, c), flip))

    greet([dict(zip(("y", "x", "c"), there(flip))) for flip in flips])
    copies = []
    for piece in range(count):
        for number, flip in enumerate(flips):
            yy, xx, cc = there(flip)
            member = index(yy, xx, cc)
            holds[piece][number] = takes[piece](sources, member, cc)
            copy = pltpu.make_async_remote_copy(
                src_ref=holds[piece].at[number],
                dst_ref=outs[piece].at[me],
                send_sem=send.at[piece * 7 + number],
                recv_sem=recv.at[piece * 7 + number],
                device_id={"y": yy, "x": xx, "c": cc},
                device_id_type=MESH,
            )
            copy.start()
            copies.append(copy)
        holds[piece][7] = takes[piece](sources, me, c)
        keep = pltpu.make_async_copy(holds[piece].at[7], outs[piece].at[me], own.at[piece])
        keep.start()
        copies.append(keep)
    for copy in copies:
        copy.wait()


def plane_swap(sources, shapes, takes, number, after=()):
    low = jnp.bfloat16
    count = len(shapes)
    return pl.pallas_call(
        functools.partial(swap_kernel, shapes, takes),
        out_shape=[jax.ShapeDtypeStruct((8, *shape), low) for shape in shapes],
        in_specs=[VMEM] * len(sources) + [HBM] * len(after),
        out_specs=[HBM] * count,
        scratch_shapes=[
            *[pltpu.VMEM((8, *shape), low) for shape in shapes],
            pltpu.SemaphoreType.DMA((7 * count,)),
            pltpu.SemaphoreType.DMA((7 * count,)),
            pltpu.SemaphoreType.DMA((count,)),
        ],
        compiler_params=pltpu.CompilerParams(
            collective_id=number, has_side_effects=True, vmem_limit_bytes=48 * 2**20
        ),
        cost_estimate=pl.CostEstimate(flops=1, bytes_accessed=1, transcendentals=0),
        name="plane_swap",
    )(*sources, *after)


def total_kernel(planes, src, out, near, far, send, recv):
    y, x, c, index = place()
    z = lax.axis_index("z")
    me = index(y, x, c)
    flips = [(fy, fx, fc) for fy in (0, 1) for fx in (0, 1) for fc in (0, 1)][1:]
    team = [
        dict(zip(("y", "x", "c"), (1 - at if f else at for at, f in zip((y, x, c), flip)))) for flip in flips
    ]
    column = [{"z": lax.rem(z + step, planes)} for step in range(1, planes)]
    near[me] = src[...]
    greet(team + column)

    def spread(buffer, at, others, base):
        copies = [
            pltpu.make_async_remote_copy(
                src_ref=buffer.at[at],
                dst_ref=buffer.at[at],
                send_sem=send.at[base + number],
                recv_sem=recv.at[base + number],
                device_id=other,
                device_id_type=MESH,
            )
            for number, other in enumerate(others)
        ]
        for copy in copies:
            copy.start()
        for copy in copies:
            copy.wait()

    spread(near, me, team, 0)
    far[z] = jnp.sum(near[...], axis=0)
    spread(far, z, column, 7)
    out[...] = jnp.sum(far[...], axis=0)


def total_sum(value, planes, number):
    return pl.pallas_call(
        functools.partial(total_kernel, planes),
        out_shape=jax.ShapeDtypeStruct(value.shape, value.dtype),
        in_specs=[VMEM],
        out_specs=VMEM,
        scratch_shapes=[
            pltpu.VMEM((8, *value.shape), value.dtype),
            pltpu.VMEM((planes, *value.shape), value.dtype),
            pltpu.SemaphoreType.DMA((6 + planes,)),
            pltpu.SemaphoreType.DMA((6 + planes,)),
        ],
        compiler_params=pltpu.CompilerParams(collective_id=number, has_side_effects=True),
        cost_estimate=pl.CostEstimate(flops=1, bytes_accessed=1, transcendentals=0),
        name="total_sum",
    )(value)


def dot(left, right, contract):
    return lax.dot_general(left, right, (contract, ((), ())), preferred_element_type=jnp.float32)


def mm(left, right):
    return dot(left, right, ((1,), (0,)))


def mm_nt(left, right):
    return dot(left, right, ((1,), (1,)))


def mm_tn(left, right):
    return dot(left, right, ((0,), (0,)))


def bmm(pattern, left, right):
    return jnp.einsum(pattern, left, right, preferred_element_type=jnp.float32)


def angle_tables(positions):
    half_dim = HEAD_SIZE // 2
    frequency = rope_base ** (-(jnp.arange(half_dim).astype(jnp.float32) * 2.0) / HEAD_SIZE)
    phases = positions.astype(jnp.float32)[:, None] * frequency[None, :]
    return (jnp.cos(phases), jnp.sin(phases))


def rotate(value, cos_table, sin_table):
    half = value.shape[-1] // 2
    a, b = value[..., :half], value[..., half:]
    return jnp.concatenate([a * cos_table - b * sin_table, b * cos_table + a * sin_table], axis=-1)


def rms_forward(value, gain_row):
    inverse = lax.rsqrt(jnp.mean(value * value, axis=-1, keepdims=True) + norm_eps)
    return (value * inverse * gain_row, inverse)


def rms_back(grad_out, value, inverse, gain_row):
    scaled = grad_out * gain_row
    grad_in = inverse * (
        scaled - value * inverse * inverse * jnp.mean(scaled * value, axis=-1, keepdims=True)
    )
    return (grad_in, jnp.sum(grad_out * value * inverse, axis=0))


def adamw(weight, gradient, moment_one, moment_two, step_rate, decay_rate):
    mean_new = beta_one * moment_one + (1.0 - beta_one) * gradient
    square_new = beta_two * moment_two + (1.0 - beta_two) * gradient * gradient
    direction = (
        mean_new
        / (1.0 - beta_one**STEP)
        / (jnp.sqrt(square_new / (1.0 - beta_two**STEP)) + adam_eps)
    )
    return (weight - step_rate * (direction + decay_rate * weight), mean_new, square_new)


def attention_parts(core, length, q_ref, mine_ref, other_ref, query_ref, key_ref):
    mine, other = mine_ref[...].reshape(-1, HEAD_SIZE), other_ref[...].reshape(-1, HEAD_SIZE)
    first = core == 0
    k, v = jnp.where(first, mine, other), jnp.where(first, other, mine)
    q = q_ref[...].reshape(-1, HEAD_SIZE)
    at, key_at = query_ref[...], key_ref[...]
    allowed = (key_at <= at) & (key_at < length) & (key_at >= 0)
    scores = jnp.where(allowed, mm_nt(q, k) * HEAD_SIZE ** (-0.5), masked_value)
    exponent = jnp.exp(scores - jnp.max(scores, axis=-1, keepdims=True))
    return q, k, v, exponent / jnp.sum(exponent, axis=-1, keepdims=True)


def attention_kernel(core_ref, length_ref, q_ref, mine_ref, other_ref, query_ref, key_ref, out_ref):
    length = length_ref[pl.program_id(0)]
    _, _, v, soft = attention_parts(core_ref[0], length, q_ref, mine_ref, other_ref, query_ref, key_ref)
    out_ref[...] = mm(soft.astype(jnp.bfloat16), v).astype(jnp.bfloat16).reshape(out_ref.shape)


def attention_back_kernel(
    core_ref, length_ref, q_ref, mine_ref, other_ref, query_ref, key_ref, do_ref, cos_ref, sin_ref,
    dq_ref, keep_ref, send_ref,
):
    low = jnp.bfloat16
    core = core_ref[0]
    length = length_ref[pl.program_id(0)]
    q, k, v, soft = attention_parts(core, length, q_ref, mine_ref, other_ref, query_ref, key_ref)
    do = do_ref[...].reshape(-1, HEAD_SIZE)
    dp = mm_nt(do, v)
    delta = jnp.sum(soft * dp, axis=-1, keepdims=True)
    ds = (soft * (dp - delta) * HEAD_SIZE ** (-0.5)).astype(low)
    dq = mm(ds, k)
    cos_table, sin_table = cos_ref[...], sin_ref[...]
    half = HEAD_SIZE // 2
    a, b = dq[:, :half], dq[:, half:]
    turned = jnp.concatenate([a * cos_table + b * sin_table, b * cos_table - a * sin_table], axis=-1)
    dq_ref[...] = turned.astype(low).reshape(dq_ref.shape)
    dk, dv = mm_tn(ds, q), mm_tn(soft.astype(low), do)
    first = core == 0
    keep_ref[...] = jnp.where(first, dk, dv).reshape(keep_ref.shape)
    send_ref[...] = jnp.where(first, dv, dk).astype(low).reshape(send_ref.shape)


def attention_call(kernel, core, lengths, q, mine, other, query_pos, key_pos, extra, outs, name):
    ny, count, span, size = q.shape
    nz = mine.shape[0]
    rows = pl.BlockSpec((ny, 1, span, size), lambda i, *_: (0, i, 0, 0))
    keys = pl.BlockSpec((nz, ny, 1, span, size), lambda i, *_: (0, 0, i, 0, 0))

    def whole(value):
        return pl.BlockSpec(value.shape, lambda i, *_: (0,) * value.ndim)

    kinds = {"rows": (rows, q.shape), "keys": (keys, mine.shape)}
    return pl.pallas_call(
        kernel,
        grid_spec=pltpu.PrefetchScalarGridSpec(
            num_scalar_prefetch=2,
            grid=(count,),
            in_specs=[rows, keys, keys, whole(query_pos), whole(key_pos)]
            + [rows if value.shape == q.shape else whole(value) for value in extra],
            out_specs=[kinds[kind][0] for kind, _ in outs],
        ),
        out_shape=[jax.ShapeDtypeStruct(kinds[kind][1], dtype) for kind, dtype in outs],
        compiler_params=pltpu.CompilerParams(vmem_limit_bytes=48 * 2**20),
        cost_estimate=pl.CostEstimate(flops=1, bytes_accessed=1, transcendentals=0),
        name=name,
    )(core, lengths, q, mine, other, query_pos, key_pos, *extra)


def feed_back_kernel(dyb_ref, weight_ref, gate_ref, up_ref, out_ref):
    dm = mm(dyb_ref[...], weight_ref[...])
    gate, upward = gate_ref[...], up_ref[...]
    sig = jax.nn.sigmoid(gate)
    part = gate.shape[1]
    out_ref[:, :part] = (dm * upward * sig * (1.0 + gate * (1.0 - sig))).astype(out_ref.dtype)
    out_ref[:, part:] = (dm * gate * sig).astype(out_ref.dtype)


def feed_back(dyb, weight, gate, upward, lines=256):
    count, part = gate.shape

    def rows(width):
        return pl.BlockSpec((lines, width), lambda i: (i, 0))

    return pl.pallas_call(
        feed_back_kernel,
        grid=(count // lines,),
        in_specs=[rows(dyb.shape[1]), pl.BlockSpec(weight.shape, lambda i: (0, 0)), rows(part), rows(part)],
        out_specs=rows(2 * part),
        out_shape=jax.ShapeDtypeStruct((count, 2 * part), jnp.bfloat16),
        compiler_params=pltpu.CompilerParams(vmem_limit_bytes=48 * 2**20),
        cost_estimate=pl.CostEstimate(flops=1, bytes_accessed=1, transcendentals=0),
        name="feed_back",
    )(dyb, weight, gate, upward)


def is_square():
    return lax.axis_size("y") == 2 and lax.axis_size("x") == 2


def swap(blocks):
    return lax.all_to_all(blocks, TEAM, split_axis=0, concat_axis=0, tiled=True)


def over_planes(blocks):
    return lax.all_gather(blocks.reshape(-1, blocks.shape[-1]), "z", axis=0, tiled=True)


def scatter_planes(term):
    return lax.psum_scatter(term, "z", scatter_dimension=0, tiled=True)


def scatter_team(rows, number, after=()):
    if not is_square():
        return swap(rows.reshape(8, -1, rows.shape[-1]))
    count = rows.shape[0] // 8

    def take(sources, member, core):
        return sources[0][pl.ds(pl.multiple_of(member * count, count), count), :]

    return plane_swap([rows], [(count, rows.shape[1])], [take], number, after)[0]


def team_gather(local, number, after=()):
    if not is_square():
        return lax.all_gather(local, TEAM, axis=0, tiled=True)
    return plane_gather(local, number, after).reshape(-1, local.shape[1])


def team_sum(lefts, rights, number, after=()):
    if is_square():
        return plane_sum(lefts, rights, number, after)
    partial = mm_nt(jnp.concatenate(lefts, axis=1), jnp.concatenate(rights, axis=1))
    return lax.psum_scatter(partial.astype(jnp.bfloat16), TEAM, scatter_dimension=0, tiled=True).astype(jnp.float32)


def local(
    tokens,
    lengths,
    norm_gains,
    attention_weight,
    feed_weight,
    cotangent,
    attention_mean,
    attention_square,
    feed_mean,
    feed_square,
    gain_mean,
    gain_square,
):
    low = jnp.bfloat16
    sequences, span, width = tokens.shape
    ny, nx, nz = lax.axis_size("y"), lax.axis_size("x"), lax.axis_size("z")
    team = ny * nx * 2
    core = lax.axis_index("c")
    rows = attention_weight.shape[0]
    q_width, kv_width = QUERY_HEADS * HEAD_SIZE, KEY_VALUE_HEADS * HEAD_SIZE
    count = sequences * span
    all_sequences = nx * 2 * sequences
    reach = ny * span
    near = nz <= 4
    ff_part = FF // team

    def columns(start, size):
        return pl.ds(pl.multiple_of(start, size), size)

    def take_attention(sources, member, c):
        source = sources[0]
        starts = (
            member * HEAD_SIZE,
            q_width + c * kv_width + (member - c) // 2 * HEAD_SIZE,
            q_width + 2 * kv_width + member * HEAD_SIZE,
        )
        return jnp.concatenate([source[:, columns(s, HEAD_SIZE)].astype(low) for s in starts], axis=1)

    def take_feed(part):
        return lambda sources, member, c: sources[0][
            :, columns(part * FF + member * ff_part, ff_part)
        ].astype(low)

    def spread(source, take, size, number, after=()):
        if is_square():
            blocks = plane_swap([source], [(rows, size)], [take], number, after)[0]
        else:
            blocks = swap(jnp.stack([take([source], member, member % 2) for member in range(8)]))
        return blocks, over_planes(blocks)

    attention_blocks, attention_mine = spread(attention_weight, take_attention, 3 * HEAD_SIZE, 1)
    gate_blocks, gate_weight = spread(feed_weight, take_feed(0), ff_part, 2, [attention_blocks])

    team_base = lax.axis_index("z") * reach
    team_pos = team_base + jnp.arange(reach, dtype=jnp.int32)
    own_pos = team_base + lax.axis_index("y") * span + jnp.arange(span, dtype=jnp.int32)
    if near:
        key_pos = jnp.concatenate([team_pos - back * reach for back in range(nz)])
    else:
        key_pos = jnp.arange(nz * reach, dtype=jnp.int32)
    query_at, key_at = team_pos[:, None], key_pos[None, :]
    cos_table, sin_table = angle_tables(team_pos)
    cos_rows, sin_rows = (t.reshape(ny, 1, span, -1) for t in (cos_table, sin_table))
    valid = (own_pos[None, :] < lengths[:, None]).astype(jnp.float32).reshape(count, 1)
    lengths_all = lax.all_gather(lengths, ("x", "c"), axis=0, tiled=True)
    core_at = jnp.reshape(core, (1,)).astype(jnp.int32)

    def heads(value):
        return value.reshape(ny, all_sequences, span, HEAD_SIZE)

    x_in = tokens.reshape(count, width).astype(jnp.float32)
    normed_one, inverse_one = rms_forward(x_in, norm_gains[0])
    outer_grad = cotangent.reshape(count, width).astype(jnp.float32) * valid
    h1 = team_gather(normed_one.astype(low), 3, [gate_blocks])
    up_blocks, up_weight = spread(feed_weight, take_feed(1), ff_part, 18, [h1])
    attention_mine, up_blocks, lengths_all = lax.optimization_barrier((attention_mine, up_blocks, lengths_all))
    query_weight = attention_mine[:, :HEAD_SIZE]
    kv_weight = attention_mine[:, HEAD_SIZE : 2 * HEAD_SIZE]
    out_weight = attention_mine[:, 2 * HEAD_SIZE :]
    kv_raw = heads(mm(h1, kv_weight))
    kv = jnp.where(core == 0, rotate(kv_raw, cos_rows, sin_rows), kv_raw).astype(low)
    q = rotate(heads(mm(h1, query_weight)), cos_rows, sin_rows).astype(low)
    dyb = team_gather(outer_grad.astype(low), 15, [kv])
    down_blocks, down_weight = spread(feed_weight, take_feed(2), ff_part, 12, [dyb])
    if near:
        earlier = [
            lax.ppermute(kv, "z", [(at, at + back) for at in range(nz - back)]) for back in range(1, nz)
        ]
        *earlier, dyb, down_blocks, q = lax.optimization_barrier((*earlier, dyb, down_blocks, q))
        kv = jnp.stack([kv, *earlier])
    else:
        kv = lax.all_gather(kv, "z", axis=0, tiled=False)
    other = lax.ppermute(kv, "c", [(0, 1), (1, 0)])
    attend = (core_at, lengths_all, q, kv, other, query_at, key_at)
    (o,) = attention_call(attention_kernel, *attend, (), [("rows", low)], "attention")
    o = o.reshape(-1, HEAD_SIZE)
    r = x_in + team_sum([o], [out_weight], 4)

    normed_two, inverse_two = rms_forward(r, norm_gains[1])
    h2 = team_gather(normed_two.astype(low), 16)
    gate, upward = mm(h2, gate_weight), mm(h2, up_weight)
    sig = jax.nn.sigmoid(gate)
    m = (gate * sig * upward).astype(low)
    down_term = mm_tn(dyb, m).astype(low)
    down_rows = scatter_planes(down_term)
    down_weight, down_term = lax.optimization_barrier((down_weight, down_term))
    d_both = feed_back(dyb, down_weight, gate, upward)
    dh2 = team_sum([d_both], [gate_weight, up_weight], 7, [down_term])
    gate_up_term = mm_tn(h2, d_both).astype(low)
    gate_up_rows = scatter_planes(gate_up_term)
    mid_grad, gain_two = rms_back(dh2, r, inverse_two, norm_gains[1])
    dr = outer_grad + mid_grad
    drb = team_gather(dr.astype(low), 13, [gate_up_term, down_rows])

    do = heads(mm(drb, out_weight).astype(low))
    dq, keep, theirs = attention_call(
        attention_back_kernel,
        *attend,
        (do, cos_table, sin_table),
        [("rows", low), ("keys", jnp.float32), ("keys", low)],
        "attention_back",
    )
    dq = dq.reshape(-1, HEAD_SIZE)
    dkv = keep + lax.ppermute(theirs, "c", [(0, 1), (1, 0)]).astype(jnp.float32)
    low_terms = dkv.astype(low)
    qo_term = jnp.concatenate([mm_tn(h1, dq), mm_tn(drb, o)], axis=1).astype(low)
    feed_sum = team_sum([m], [down_weight], 5, [low_terms])
    down_grad = scatter_team(down_rows, 6, [low_terms])
    if near:
        later = [
            lax.ppermute(low_terms[back], "z", [(at + back, at) for at in range(nz - back)])
            for back in range(1, nz)
        ]
        *later, feed_sum, down_grad, gate_up_rows = lax.optimization_barrier(
            (*later, feed_sum, down_grad, gate_up_rows)
        )
        dkv = dkv[0] + sum(term.astype(jnp.float32) for term in later)
    else:
        dkv = lax.psum_scatter(low_terms, "z", scatter_dimension=0, tiled=True)[0].astype(jnp.float32)
    dkv = jnp.where(core == 0, rotate(dkv, cos_rows, -sin_rows), dkv).astype(low).reshape(-1, HEAD_SIZE)
    layer_output = (r + feed_sum).astype(low)
    qo_rows = scatter_planes(qo_term)
    kv_term = mm_tn(h1, dkv).astype(low)
    kv_rows = scatter_planes(kv_term)
    dh1 = team_sum([dq, dkv], [query_weight, kv_weight], 9, [kv_term])
    in_grad, gain_one = rms_back(dh1, x_in, inverse_one, norm_gains[0])
    input_gradient = dr + in_grad
    gate_up_grad = scatter_team(gate_up_rows, 8, [dh1])
    qo_grad = scatter_team(qo_rows, 10, [dh1]).astype(jnp.float32)
    kv_grad = scatter_team(kv_rows, 14).astype(jnp.float32)

    def columns_of(blocks):
        return blocks.transpose(1, 0, 2).reshape(rows, -1)

    attention_grad = jnp.concatenate(
        [
            columns_of(qo_grad[:, :, :HEAD_SIZE]),
            kv_grad.reshape(KEY_VALUE_HEADS, 2, rows, HEAD_SIZE).transpose(2, 1, 0, 3).reshape(rows, 2 * kv_width),
            columns_of(qo_grad[:, :, HEAD_SIZE:]),
        ],
        axis=1,
    )
    feed_grad = jnp.concatenate(
        [
            columns_of(g.astype(jnp.float32))
            for g in (gate_up_grad[:, :, :ff_part], gate_up_grad[:, :, ff_part:], down_grad)
        ], axis=1
    )
    local_squares = jnp.sum(attention_grad * attention_grad) + jnp.sum(feed_grad * feed_grad)
    gain_local = jnp.stack([gain_one, gain_two])
    if is_square():
        lines = jnp.concatenate([gain_local.reshape(-1, 128), jnp.full((8, 128), local_squares)], axis=0)
        lines = total_sum(lines, nz, 11)
        gain_grad, squares = lines[:-8].reshape(2, width), lines[-1, 0]
    else:
        gain_grad, squares = lax.psum((gain_local, local_squares), ALL)
    gradient_norm = jnp.sqrt(squares + jnp.sum(gain_grad * gain_grad))
    factor = clip_norm / gradient_norm
    attention_new = adamw(
        attention_weight, attention_grad * factor, attention_mean, attention_square, matrix_rate, weight_decay
    )
    feed_new = adamw(feed_weight, feed_grad * factor, feed_mean, feed_square, matrix_rate, weight_decay)
    gains_new = adamw(norm_gains, gain_grad * factor, gain_mean, gain_square, gain_rate, 0.0)
    return (
        layer_output.reshape(sequences, span, width),
        input_gradient.reshape(sequences, span, width),
        gradient_norm,
        *attention_new,
        attention_new[0].astype(low),
        *feed_new,
        feed_new[0].astype(low),
        *gains_new,
    )


def solution(mesh):
    ctx, fsdp = mesh.shape["ctx"], mesh.shape["fsdp"]
    inner = QUERY_HEADS // fsdp
    fine = Mesh(mesh.devices.reshape(ctx // inner, inner, fsdp // 2, 2), ALL)
    act = P(("x", "c"), ("z", "y"), None)
    matrix = P(ALL, None)
    return jax.shard_map(
        local,
        mesh=fine,
        in_specs=(act, P(("x", "c")), P(), matrix, matrix, act, matrix, matrix, matrix, matrix, P(), P()),
        out_specs=(act, act, P(), matrix, matrix, matrix, matrix, matrix, matrix, matrix, matrix, P(), P(), P()),
        check_vma=False,
    )
```

```python
import functools

import jax
import jax.numpy as jnp
from jax import lax
from jax.experimental import pallas as pl
from jax.experimental.pallas import tpu as pltpu
from jax.sharding import Mesh, PartitionSpec as P

QUERY_HEADS = 8
KEY_VALUE_HEADS = 4
HEAD_SIZE = 256
FF = 8192
STEP = 10

norm_eps = 1e-06
rope_base = 1000042.0
masked_value = -1e30
clip_norm = 1.0
beta_one = 0.9
beta_two = 0.95
adam_eps = 1e-08
matrix_rate = 0.03
gain_rate = 0.4
weight_decay = 0.1

TEAM = ("y", "x", "c")
ALL = ("z", "y", "x", "c")


MESH = pl.DeviceIdType.MESH
VMEM = pl.BlockSpec(memory_space=pltpu.VMEM)
HBM = pl.BlockSpec(memory_space=pl.ANY)


def place():
    y, x, c = lax.axis_index("y"), lax.axis_index("x"), lax.axis_index("c")
    return y, x, c, lambda yy, xx, cc: (yy * 2 + xx) * 2 + cc


def greet(others):
    barrier = pltpu.get_barrier_semaphore()
    for other in others:
        pl.semaphore_signal(barrier, inc=1, device_id=other, device_id_type=MESH)
    pl.semaphore_wait(barrier, len(others))


def gather_kernel(src, *refs):
    out, send, recv, own = refs[-4:]
    y, x, c, index = place()
    to_x, to_y, to_s = {"x": 1 - x}, {"y": 1 - y}, {"c": 1 - c}
    me, at_x, at_y, at_d = index(y, x, c), index(y, 1 - x, c), index(1 - y, x, c), index(1 - y, 1 - x, c)
    half = src.shape[0] // 2
    rows = (pl.ds(0, half), pl.ds(half, half))
    local = pltpu.make_async_copy(src, out.at[me], own)
    local.start()
    greet((to_x, to_y, to_s))

    def hop(slot, block, part, where, first=False):
        piece = out.at[block, rows[part]]
        return pltpu.make_async_remote_copy(
            src_ref=src.at[rows[part]] if first else piece,
            dst_ref=piece,
            send_sem=send.at[slot],
            recv_sem=recv.at[slot],
            device_id=where,
            device_id_type=MESH,
        )

    x0, x1 = hop(0, me, 0, to_x, True), hop(1, me, 1, to_x, True)
    y1, y0 = hop(2, me, 1, to_y, True), hop(3, me, 0, to_y, True)
    s0, s1 = hop(4, me, 0, to_s, True), hop(5, me, 1, to_s, True)
    for copy in (x0, y1, x1, y0, s0, s1):
        copy.start()
    x0.wait_recv()
    d0 = hop(6, at_x, 0, to_y)
    d0.start()
    y1.wait_recv()
    d1 = hop(7, at_y, 1, to_x)
    d1.start()
    sx0, sy1 = hop(8, at_x, 0, to_s), hop(9, at_y, 1, to_s)
    sx0.start()
    sy1.start()
    x1.wait_recv()
    sx1 = hop(10, at_x, 1, to_s)
    sx1.start()
    y0.wait_recv()
    sy0 = hop(11, at_y, 0, to_s)
    sy0.start()
    d0.wait_recv()
    sd0 = hop(12, at_d, 0, to_s)
    sd0.start()
    d1.wait_recv()
    sd1 = hop(13, at_d, 1, to_s)
    sd1.start()
    for copy in (s0, s1, sx0, sy1, sx1, sy0, sd0, sd1):
        copy.wait_recv()
    for copy in (x0, x1, y0, y1, s0, s1, d0, d1, sx0, sy1, sx1, sy0, sd0, sd1):
        copy.wait_send()
    local.wait()


def plane_gather(value, number, after=()):
    return pl.pallas_call(
        gather_kernel,
        out_shape=jax.ShapeDtypeStruct((8, *value.shape), value.dtype),
        in_specs=[HBM] * (1 + len(after)),
        out_specs=HBM,
        scratch_shapes=[
            pltpu.SemaphoreType.DMA((14,)),
            pltpu.SemaphoreType.DMA((14,)),
            pltpu.SemaphoreType.DMA,
        ],
        compiler_params=pltpu.CompilerParams(collective_id=number, has_side_effects=True),
        cost_estimate=pl.CostEstimate(flops=1, bytes_accessed=1, transcendentals=0),
        name="plane_gather",
    )(value, *after)


def sum_kernel(lefts, terms, tile, *refs):
    a_refs, w_refs = refs[:lefts], refs[lefts : lefts + len(terms)]
    out, s_send, s_recv, d_send, d_recv, x_send, x_recv, y_send, y_recv, x_acc, y_acc, send, recv = refs[-13:]
    y, x, c, index = place()
    to_x, to_y, to_s = {"x": 1 - x}, {"y": 1 - y}, {"c": 1 - c}
    rows, width = out.shape
    half = rows // 2
    parts = (pl.ds(0, half), pl.ds(half, half))
    f32, low = jnp.float32, jnp.bfloat16

    def product(block, put):
        lines = pl.ds(pl.multiple_of(block * rows, rows), rows)

        @pl.loop(0, width // tile)
        def _(step):
            cols = pl.ds(pl.multiple_of(step * tile, tile), tile)
            total = None
            for (left, start), w_ref in zip(terms, w_refs):
                term = mm_nt(a_refs[left][lines, start : start + w_ref.shape[1]], w_ref[cols, :])
                total = term if total is None else total + term
            put(cols, total)

    def hop(slot, src, dst, where):
        copy = pltpu.make_async_remote_copy(
            src_ref=src, dst_ref=dst, send_sem=send.at[slot], recv_sem=recv.at[slot],
            device_id=where, device_id_type=MESH,
        )
        return copy

    def to_sibling(slot, yy, xx):
        def put(cols, total):
            s_send[slot, :, cols] = total.astype(low)

        product(index(yy, xx, 1 - c), put)
        copy = hop(slot, s_send.at[slot], s_recv.at[slot], to_s)
        copy.start()
        return copy

    def with_sibling(slot, yy, xx, keep):
        def put(cols, total):
            keep[:, cols] = (total + s_recv[slot, :, cols].astype(f32)).astype(keep.dtype)

        product(index(yy, xx, c), put)

    greet((to_x, to_y, to_s))
    s0 = to_sibling(0, 1 - y, 1 - x)
    s1 = to_sibling(1, y, 1 - x)
    s0.wait_recv()
    with_sibling(0, 1 - y, 1 - x, d_send)
    d0 = hop(4, d_send.at[parts[0]], d_recv.at[parts[0]], to_x)
    d1 = hop(5, d_send.at[parts[1]], d_recv.at[parts[1]], to_y)
    d0.start()
    d1.start()
    s1.wait_recv()
    with_sibling(1, y, 1 - x, x_acc)
    x_send[parts[0]] = x_acc[parts[0]].astype(low)
    x0 = hop(6, x_send.at[parts[0]], x_recv.at[parts[0]], to_x)
    x0.start()
    s2 = to_sibling(2, 1 - y, x)
    s2.wait_recv()
    with_sibling(2, 1 - y, x, y_acc)
    y_send[parts[1]] = y_acc[parts[1]].astype(low)
    y1 = hop(7, y_send.at[parts[1]], y_recv.at[parts[1]], to_y)
    y1.start()
    s3 = to_sibling(3, y, x)
    d1.wait_recv()
    x_send[parts[1]] = (x_acc[parts[1]] + d_recv[parts[1]].astype(f32)).astype(low)
    x1 = hop(8, x_send.at[parts[1]], x_recv.at[parts[1]], to_x)
    x1.start()
    d0.wait_recv()
    y_send[parts[0]] = (y_acc[parts[0]] + d_recv[parts[0]].astype(f32)).astype(low)
    y0 = hop(9, y_send.at[parts[0]], y_recv.at[parts[0]], to_y)
    y0.start()
    s3.wait_recv()
    with_sibling(3, y, x, out)
    x0.wait_recv()
    y1.wait_recv()
    x1.wait_recv()
    y0.wait_recv()
    out[...] += x_recv[...].astype(f32) + y_recv[...].astype(f32)
    for copy in (s0, s1, s2, s3, d0, d1, x0, x1, y0, y1):
        copy.wait_send()


def plane_sum(lefts, rights, number, after=(), tile=512):
    ends = [(left, start) for left, a in enumerate(lefts) for start in range(0, a.shape[1], rights[0].shape[1])]
    terms = tuple(ends[: len(rights)])
    rows, width = lefts[0].shape[0] // 8, rights[0].shape[0]
    block = (rows, width)
    low, f32 = jnp.bfloat16, jnp.float32
    return pl.pallas_call(
        functools.partial(sum_kernel, len(lefts), terms, min(tile, width)),
        out_shape=jax.ShapeDtypeStruct(block, f32),
        in_specs=[VMEM] * (len(lefts) + len(rights)) + [HBM] * len(after),
        out_specs=VMEM,
        scratch_shapes=[
            pltpu.VMEM((4, *block), low),
            pltpu.VMEM((4, *block), low),
            *[pltpu.VMEM(block, low)] * 6,
            pltpu.VMEM(block, f32),
            pltpu.VMEM(block, f32),
            pltpu.SemaphoreType.DMA((10,)),
            pltpu.SemaphoreType.DMA((10,)),
        ],
        compiler_params=pltpu.CompilerParams(
            collective_id=number, has_side_effects=True, vmem_limit_bytes=48 * 2**20
        ),
        cost_estimate=pl.CostEstimate(flops=1, bytes_accessed=1, transcendentals=0),
        name="plane_sum",
    )(*lefts, *rights, *after)


def swap_kernel(pieces, takes, *refs):
    count = len(pieces)
    sources, (send, recv, own) = refs[: -2 * count - 3], refs[-3:]
    outs, holds = refs[-2 * count - 3 : -count - 3], refs[-count - 3 : -3]
    y, x, c, index = place()
    me = index(y, x, c)
    flips = [(fy, fx, fc) for fy, fx in ((1, 1), (0, 1), (1, 0), (0, 0)) for fc in (0, 1)]
    flips = [flip for flip in flips if flip != (0, 0, 0)]

    def there(flip):
        return tuple(1 - at if f else at for at, f in zip((y, x, c), flip))

    greet([dict(zip(("y", "x", "c"), there(flip))) for flip in flips])
    copies = []
    for piece in range(count):
        for number, flip in enumerate(flips):
            yy, xx, cc = there(flip)
            member = index(yy, xx, cc)
            holds[piece][number] = takes[piece](sources, member, cc)
            copy = pltpu.make_async_remote_copy(
                src_ref=holds[piece].at[number],
                dst_ref=outs[piece].at[me],
                send_sem=send.at[piece * 7 + number],
                recv_sem=recv.at[piece * 7 + number],
                device_id={"y": yy, "x": xx, "c": cc},
                device_id_type=MESH,
            )
            copy.start()
            copies.append(copy)
        holds[piece][7] = takes[piece](sources, me, c)
        keep = pltpu.make_async_copy(holds[piece].at[7], outs[piece].at[me], own.at[piece])
        keep.start()
        copies.append(keep)
    for copy in copies:
        copy.wait()


def plane_swap(sources, shapes, takes, number, after=()):
    low = jnp.bfloat16
    count = len(shapes)
    return pl.pallas_call(
        functools.partial(swap_kernel, shapes, takes),
        out_shape=[jax.ShapeDtypeStruct((8, *shape), low) for shape in shapes],
        in_specs=[VMEM] * len(sources) + [HBM] * len(after),
        out_specs=[HBM] * count,
        scratch_shapes=[
            *[pltpu.VMEM((8, *shape), low) for shape in shapes],
            pltpu.SemaphoreType.DMA((7 * count,)),
            pltpu.SemaphoreType.DMA((7 * count,)),
            pltpu.SemaphoreType.DMA((count,)),
        ],
        compiler_params=pltpu.CompilerParams(
            collective_id=number, has_side_effects=True, vmem_limit_bytes=48 * 2**20
        ),
        cost_estimate=pl.CostEstimate(flops=1, bytes_accessed=1, transcendentals=0),
        name="plane_swap",
    )(*sources, *after)


def total_kernel(planes, src, out, near, far, send, recv):
    y, x, c, index = place()
    z = lax.axis_index("z")
    me = index(y, x, c)
    flips = [(fy, fx, fc) for fy in (0, 1) for fx in (0, 1) for fc in (0, 1)][1:]
    team = [
        dict(zip(("y", "x", "c"), (1 - at if f else at for at, f in zip((y, x, c), flip)))) for flip in flips
    ]
    column = [{"z": lax.rem(z + step, planes)} for step in range(1, planes)]
    near[me] = src[...]
    greet(team + column)

    def spread(buffer, at, others, base):
        copies = [
            pltpu.make_async_remote_copy(
                src_ref=buffer.at[at],
                dst_ref=buffer.at[at],
                send_sem=send.at[base + number],
                recv_sem=recv.at[base + number],
                device_id=other,
                device_id_type=MESH,
            )
            for number, other in enumerate(others)
        ]
        for copy in copies:
            copy.start()
        for copy in copies:
            copy.wait()

    spread(near, me, team, 0)
    far[z] = jnp.sum(near[...], axis=0)
    spread(far, z, column, 7)
    out[...] = jnp.sum(far[...], axis=0)


def total_sum(value, planes, number):
    return pl.pallas_call(
        functools.partial(total_kernel, planes),
        out_shape=jax.ShapeDtypeStruct(value.shape, value.dtype),
        in_specs=[VMEM],
        out_specs=VMEM,
        scratch_shapes=[
            pltpu.VMEM((8, *value.shape), value.dtype),
            pltpu.VMEM((planes, *value.shape), value.dtype),
            pltpu.SemaphoreType.DMA((6 + planes,)),
            pltpu.SemaphoreType.DMA((6 + planes,)),
        ],
        compiler_params=pltpu.CompilerParams(collective_id=number, has_side_effects=True),
        cost_estimate=pl.CostEstimate(flops=1, bytes_accessed=1, transcendentals=0),
        name="total_sum",
    )(value)


def dot(left, right, contract):
    return lax.dot_general(left, right, (contract, ((), ())), preferred_element_type=jnp.float32)


def mm(left, right):
    return dot(left, right, ((1,), (0,)))


def mm_nt(left, right):
    return dot(left, right, ((1,), (1,)))


def mm_tn(left, right):
    return dot(left, right, ((0,), (0,)))


def bmm(pattern, left, right):
    return jnp.einsum(pattern, left, right, preferred_element_type=jnp.float32)


def angle_tables(positions):
    half_dim = HEAD_SIZE // 2
    frequency = rope_base ** (-(jnp.arange(half_dim).astype(jnp.float32) * 2.0) / HEAD_SIZE)
    phases = positions.astype(jnp.float32)[:, None] * frequency[None, :]
    return (jnp.cos(phases), jnp.sin(phases))


def rotate(value, cos_table, sin_table):
    half = value.shape[-1] // 2
    a, b = value[..., :half], value[..., half:]
    return jnp.concatenate([a * cos_table - b * sin_table, b * cos_table + a * sin_table], axis=-1)


def rms_forward(value, gain_row):
    inverse = lax.rsqrt(jnp.mean(value * value, axis=-1, keepdims=True) + norm_eps)
    return (value * inverse * gain_row, inverse)


def rms_back(grad_out, value, inverse, gain_row):
    scaled = grad_out * gain_row
    grad_in = inverse * (
        scaled - value * inverse * inverse * jnp.mean(scaled * value, axis=-1, keepdims=True)
    )
    return (grad_in, jnp.sum(grad_out * value * inverse, axis=0))


def adamw(weight, gradient, moment_one, moment_two, step_rate, decay_rate):
    mean_new = beta_one * moment_one + (1.0 - beta_one) * gradient
    square_new = beta_two * moment_two + (1.0 - beta_two) * gradient * gradient
    direction = (
        mean_new
        / (1.0 - beta_one**STEP)
        / (jnp.sqrt(square_new / (1.0 - beta_two**STEP)) + adam_eps)
    )
    return (weight - step_rate * (direction + decay_rate * weight), mean_new, square_new)


def attention_parts(core, length, q_ref, mine_ref, other_ref, query_ref, key_ref):
    mine, other = mine_ref[...].reshape(-1, HEAD_SIZE), other_ref[...].reshape(-1, HEAD_SIZE)
    first = core == 0
    k, v = jnp.where(first, mine, other), jnp.where(first, other, mine)
    q = q_ref[...].reshape(-1, HEAD_SIZE)
    at, key_at = query_ref[...], key_ref[...]
    allowed = (key_at <= at) & (key_at < length) & (key_at >= 0)
    scores = jnp.where(allowed, mm_nt(q, k) * HEAD_SIZE ** (-0.5), masked_value)
    exponent = jnp.exp(scores - jnp.max(scores, axis=-1, keepdims=True))
    return q, k, v, exponent / jnp.sum(exponent, axis=-1, keepdims=True)


def attention_kernel(core_ref, length_ref, q_ref, mine_ref, other_ref, query_ref, key_ref, out_ref):
    length = length_ref[pl.program_id(0)]
    _, _, v, soft = attention_parts(core_ref[0], length, q_ref, mine_ref, other_ref, query_ref, key_ref)
    out_ref[...] = mm(soft.astype(jnp.bfloat16), v).astype(jnp.bfloat16).reshape(out_ref.shape)


def attention_back_kernel(
    core_ref, length_ref, q_ref, mine_ref, other_ref, query_ref, key_ref, do_ref, cos_ref, sin_ref,
    dq_ref, keep_ref, send_ref,
):
    low = jnp.bfloat16
    core = core_ref[0]
    length = length_ref[pl.program_id(0)]
    q, k, v, soft = attention_parts(core, length, q_ref, mine_ref, other_ref, query_ref, key_ref)
    do = do_ref[...].reshape(-1, HEAD_SIZE)
    dp = mm_nt(do, v)
    delta = jnp.sum(soft * dp, axis=-1, keepdims=True)
    ds = (soft * (dp - delta) * HEAD_SIZE ** (-0.5)).astype(low)
    dq = mm(ds, k)
    cos_table, sin_table = cos_ref[...], sin_ref[...]
    half = HEAD_SIZE // 2
    a, b = dq[:, :half], dq[:, half:]
    turned = jnp.concatenate([a * cos_table + b * sin_table, b * cos_table - a * sin_table], axis=-1)
    dq_ref[...] = turned.astype(low).reshape(dq_ref.shape)
    dk, dv = mm_tn(ds, q), mm_tn(soft.astype(low), do)
    first = core == 0
    keep, send = (t.reshape(keep_ref.shape) for t in (jnp.where(first, dk, dv), jnp.where(first, dv, dk)))
    for block in range(keep_ref.shape[0]):
        at = core_ref[1 + block]
        keep_ref[at] = keep[block]
        send_ref[at] = send[block].astype(low)


def attention_call(kernel, core, lengths, q, mine, other, query_pos, key_pos, extra, outs, name):
    ny, count, span, size = q.shape
    nz = mine.shape[0]
    rows = pl.BlockSpec((ny, 1, span, size), lambda i, *_: (0, i, 0, 0))
    keys = pl.BlockSpec((nz, ny, 1, span, size), lambda i, *_: (0, 0, i, 0, 0))

    def whole(value):
        return pl.BlockSpec(value.shape, lambda i, *_: (0,) * value.ndim)

    kinds = {"rows": (rows, q.shape), "keys": (keys, mine.shape)}
    return pl.pallas_call(
        kernel,
        grid_spec=pltpu.PrefetchScalarGridSpec(
            num_scalar_prefetch=2,
            grid=(count,),
            in_specs=[rows, keys, keys, whole(query_pos), whole(key_pos)]
            + [rows if value.shape == q.shape else whole(value) for value in extra],
            out_specs=[kinds[kind][0] for kind, _ in outs],
        ),
        out_shape=[jax.ShapeDtypeStruct(kinds[kind][1], dtype) for kind, dtype in outs],
        compiler_params=pltpu.CompilerParams(vmem_limit_bytes=48 * 2**20),
        cost_estimate=pl.CostEstimate(flops=1, bytes_accessed=1, transcendentals=0),
        name=name,
    )(core, lengths, q, mine, other, query_pos, key_pos, *extra)


def feed_back_kernel(dyb_ref, weight_ref, gate_ref, up_ref, out_ref):
    dm = mm(dyb_ref[...], weight_ref[...])
    gate, upward = gate_ref[...], up_ref[...]
    sig = jax.nn.sigmoid(gate)
    part = gate.shape[1]
    out_ref[:, :part] = (dm * upward * sig * (1.0 + gate * (1.0 - sig))).astype(out_ref.dtype)
    out_ref[:, part:] = (dm * gate * sig).astype(out_ref.dtype)


def feed_back(dyb, weight, gate, upward, lines=256):
    count, part = gate.shape

    def rows(width):
        return pl.BlockSpec((lines, width), lambda i: (i, 0))

    return pl.pallas_call(
        feed_back_kernel,
        grid=(count // lines,),
        in_specs=[rows(dyb.shape[1]), pl.BlockSpec(weight.shape, lambda i: (0, 0)), rows(part), rows(part)],
        out_specs=rows(2 * part),
        out_shape=jax.ShapeDtypeStruct((count, 2 * part), jnp.bfloat16),
        compiler_params=pltpu.CompilerParams(vmem_limit_bytes=48 * 2**20),
        cost_estimate=pl.CostEstimate(flops=1, bytes_accessed=1, transcendentals=0),
        name="feed_back",
    )(dyb, weight, gate, upward)


def attention_part(step, grad_ref):
    column = jnp.where(step < 2, 0, jnp.where(step < 4, 1, 2))
    parts = []
    for head in range(4):
        member = jnp.where((step == 2) | (step == 3), 2 * head + step - 2, 4 * (step % 2) + head)
        parts.append(grad_ref[member, :, pl.ds(pl.multiple_of(column * HEAD_SIZE, HEAD_SIZE), HEAD_SIZE)])
    return jnp.concatenate(parts, axis=1)


def feed_part(step, gate_up_ref, down_ref):
    size = down_ref.shape[2]
    both = gate_up_ref[step % 8, :, pl.ds(pl.multiple_of(jnp.minimum(step // 8, 1) * size, size), size)]
    return jnp.where(step < 16, both, down_ref[step % 8])


def update_kernel(part, factor_ref, weight_ref, mean_ref, square_ref, *refs):
    grads, (new_ref, new_mean_ref, new_square_ref, copy_ref) = refs[:-4], refs[-4:]
    gradient = part(pl.program_id(0), *grads).astype(jnp.float32) * factor_ref[0]
    new, mean, square = adamw(
        weight_ref[...], gradient, mean_ref[...], square_ref[...], matrix_rate, weight_decay
    )
    new_ref[...] = new
    new_mean_ref[...] = mean
    new_square_ref[...] = square
    copy_ref[...] = new.astype(copy_ref.dtype)


def update(part, factor, weight, mean, square, grads, size=1024):
    rows, width = weight.shape
    block = pl.BlockSpec((rows, size), lambda i: (0, i))
    f32 = jnp.float32
    return pl.pallas_call(
        functools.partial(update_kernel, part),
        grid=(width // size,),
        in_specs=[pl.BlockSpec(memory_space=pltpu.SMEM), block, block, block]
        + [pl.BlockSpec(grad.shape, lambda i: (0, 0, 0)) for grad in grads],
        out_specs=[block] * 4,
        out_shape=[jax.ShapeDtypeStruct(weight.shape, dtype) for dtype in (f32, f32, f32, jnp.bfloat16)],
        compiler_params=pltpu.CompilerParams(vmem_limit_bytes=48 * 2**20),
        name="update",
    )(jnp.reshape(factor, (1,)), weight, mean, square, *grads)


def is_square():
    return lax.axis_size("y") == 2 and lax.axis_size("x") == 2


def swap(blocks):
    return lax.all_to_all(blocks, TEAM, split_axis=0, concat_axis=0, tiled=True)


def over_planes(blocks):
    return lax.all_gather(blocks.reshape(-1, blocks.shape[-1]), "z", axis=0, tiled=True)


def scatter_planes(term):
    return lax.psum_scatter(term, "z", scatter_dimension=0, tiled=True)


def chain_round(blocks, step, came):
    planes, z = lax.axis_size("z"), lax.axis_index("z")
    sums = [
        lax.dynamic_index_in_dim(blocks, jnp.clip(at, 0, planes - 1), keepdims=False)
        for at in (planes - step + z, step - planes + z)
    ]
    if came:
        sums = [(a.astype(jnp.float32) + b.astype(jnp.float32)).astype(a.dtype) for a, b in zip(sums, came)]
    return (
        lax.ppermute(sums[0], "z", [(at, at + 1) for at in range(step)]),
        lax.ppermute(sums[1], "z", [(planes - 1 - at, planes - 2 - at) for at in range(step)]),
    )


def chain_end(blocks, came):
    own = lax.dynamic_index_in_dim(blocks, lax.axis_index("z"), keepdims=False).astype(jnp.float32)
    return (own + came[0].astype(jnp.float32) + came[1].astype(jnp.float32)).astype(blocks.dtype)


def together(*values):
    return lax.optimization_barrier(values)


def scatter_team(rows, number, after=()):
    if not is_square():
        return swap(rows.reshape(8, -1, rows.shape[-1]))
    count = rows.shape[0] // 8

    def take(sources, member, core):
        return sources[0][pl.ds(pl.multiple_of(member * count, count), count), :]

    return plane_swap([rows], [(count, rows.shape[1])], [take], number, after)[0]


def team_gather(local, number, after=()):
    if not is_square():
        return lax.all_gather(local, TEAM, axis=0, tiled=True)
    return plane_gather(local, number, after).reshape(-1, local.shape[1])


def team_sum(lefts, rights, number, after=()):
    if is_square():
        return plane_sum(lefts, rights, number, after)
    partial = mm_nt(jnp.concatenate(lefts, axis=1), jnp.concatenate(rights, axis=1))
    return lax.psum_scatter(partial.astype(jnp.bfloat16), TEAM, scatter_dimension=0, tiled=True).astype(jnp.float32)


def local(
    tokens,
    lengths,
    norm_gains,
    attention_weight,
    feed_weight,
    cotangent,
    attention_mean,
    attention_square,
    feed_mean,
    feed_square,
    gain_mean,
    gain_square,
):
    low = jnp.bfloat16
    sequences, span, width = tokens.shape
    ny, nx, nz = lax.axis_size("y"), lax.axis_size("x"), lax.axis_size("z")
    team = ny * nx * 2
    core = lax.axis_index("c")
    rows = attention_weight.shape[0]
    q_width, kv_width = QUERY_HEADS * HEAD_SIZE, KEY_VALUE_HEADS * HEAD_SIZE
    count = sequences * span
    all_sequences = nx * 2 * sequences
    reach = ny * span
    near = nz <= 4
    ff_part = FF // team

    def columns(start, size):
        return pl.ds(pl.multiple_of(start, size), size)

    def take_attention(sources, member, c):
        source = sources[0]
        starts = (
            member * HEAD_SIZE,
            q_width + c * kv_width + (member - c) // 2 * HEAD_SIZE,
            q_width + 2 * kv_width + member * HEAD_SIZE,
        )
        return jnp.concatenate([source[:, columns(s, HEAD_SIZE)].astype(low) for s in starts], axis=1)

    def take_feed(part):
        return lambda sources, member, c: sources[0][
            :, columns(part * FF + member * ff_part, ff_part)
        ].astype(low)

    def spread(source, take, size, number, after=()):
        if is_square():
            blocks = plane_swap([source], [(rows, size)], [take], number, after)[0]
        else:
            blocks = swap(jnp.stack([take([source], member, member % 2) for member in range(8)]))
        return blocks, over_planes(blocks)

    attention_blocks, attention_mine = spread(attention_weight, take_attention, 3 * HEAD_SIZE, 1)
    gate_blocks, gate_weight = spread(feed_weight, take_feed(0), ff_part, 2, [attention_blocks])

    team_base = lax.axis_index("z") * reach
    team_pos = team_base + jnp.arange(reach, dtype=jnp.int32)
    own_pos = team_base + lax.axis_index("y") * span + jnp.arange(span, dtype=jnp.int32)
    if near:
        key_pos = jnp.concatenate([team_pos - back * reach for back in range(nz)])
    else:
        key_pos = jnp.arange(nz * reach, dtype=jnp.int32)
    query_at, key_at = team_pos[:, None], key_pos[None, :]
    cos_table, sin_table = angle_tables(team_pos)
    cos_rows, sin_rows = (t.reshape(ny, 1, span, -1) for t in (cos_table, sin_table))
    valid = (own_pos[None, :] < lengths[:, None]).astype(jnp.float32).reshape(count, 1)
    lengths_all = lax.all_gather(lengths, ("x", "c"), axis=0, tiled=True)
    planes = jnp.arange(nz, dtype=jnp.int32)
    if near:
        planes = (lax.axis_index("z") - planes) % nz
    core_at = jnp.concatenate([jnp.reshape(core, (1,)), planes]).astype(jnp.int32)

    def heads(value):
        return value.reshape(ny, all_sequences, span, HEAD_SIZE)

    x_in = tokens.reshape(count, width).astype(jnp.float32)
    normed_one, inverse_one = rms_forward(x_in, norm_gains[0])
    outer_grad = cotangent.reshape(count, width).astype(jnp.float32) * valid
    h1 = team_gather(normed_one.astype(low), 3, [gate_blocks])
    up_blocks, up_weight = spread(feed_weight, take_feed(1), ff_part, 18, [h1])
    attention_mine, up_blocks, lengths_all = lax.optimization_barrier((attention_mine, up_blocks, lengths_all))
    query_weight = attention_mine[:, :HEAD_SIZE]
    kv_weight = attention_mine[:, HEAD_SIZE : 2 * HEAD_SIZE]
    out_weight = attention_mine[:, 2 * HEAD_SIZE :]
    kv_raw = heads(mm(h1, kv_weight))
    kv = jnp.where(core == 0, rotate(kv_raw, cos_rows, sin_rows), kv_raw).astype(low)
    q = rotate(heads(mm(h1, query_weight)), cos_rows, sin_rows).astype(low)
    dyb = team_gather(outer_grad.astype(low), 15, [kv])
    down_blocks, down_weight = spread(feed_weight, take_feed(2), ff_part, 12, [dyb])
    if near:
        earlier = [
            lax.ppermute(kv, "z", [(at, at + back) for at in range(nz - back)]) for back in range(1, nz)
        ]
        *earlier, dyb, down_blocks, q = lax.optimization_barrier((*earlier, dyb, down_blocks, q))
        kv = jnp.stack([kv, *earlier])
    else:
        kv = lax.all_gather(kv, "z", axis=0, tiled=False)
    other = lax.ppermute(kv, "c", [(0, 1), (1, 0)])
    attend = (core_at, lengths_all, q, kv, other, query_at, key_at)
    (o,) = attention_call(attention_kernel, *attend, (), [("rows", low)], "attention")
    o = o.reshape(-1, HEAD_SIZE)
    r = x_in + team_sum([o], [out_weight], 4)

    normed_two, inverse_two = rms_forward(r, norm_gains[1])
    h2 = team_gather(normed_two.astype(low), 16)
    gate, upward = mm(h2, gate_weight), mm(h2, up_weight)
    sig = jax.nn.sigmoid(gate)
    m = (gate * sig * upward).astype(low)
    down_term = mm_tn(dyb, m).astype(low)
    if near:
        down_blocks, came = down_term.reshape(nz, -1, ff_part), ()
        for step in range(1, nz - 1):
            came = chain_round(down_blocks, step, came)
        down_weight, *came = together(down_weight, *came)
        came = chain_round(down_blocks, nz - 1, came)
    else:
        down_rows = scatter_planes(down_term)
        down_weight, down_term = together(down_weight, down_term)
    d_both = feed_back(dyb, down_weight, gate, upward)
    gate_up_term = mm_tn(h2, d_both).astype(low)
    if near:
        d_both, gate_up_term, *came = together(d_both, gate_up_term, *came)
        down_rows = chain_end(down_blocks, came)
    gate_up_rows = scatter_planes(gate_up_term)
    dh2 = team_sum([d_both], [gate_weight, up_weight], 7, [gate_up_term])
    mid_grad, gain_two = rms_back(dh2, r, inverse_two, norm_gains[1])
    dr = outer_grad + mid_grad
    drb = team_gather(dr.astype(low), 13, [down_rows])

    do = heads(mm(drb, out_weight).astype(low))
    dq, keep, theirs = attention_call(
        attention_back_kernel,
        *attend,
        (do, cos_table, sin_table),
        [("rows", low), ("keys", jnp.float32), ("keys", low)],
        "attention_back",
    )
    dq = dq.reshape(-1, HEAD_SIZE)
    dkv = keep + lax.ppermute(theirs, "c", [(0, 1), (1, 0)]).astype(jnp.float32)
    low_terms = dkv.astype(low)
    feed_sum = team_sum([m], [down_weight], 5, [low_terms])
    down_grad = scatter_team(down_rows, 6, [low_terms])
    low_terms, feed_sum, down_grad, gate_up_rows = together(low_terms, feed_sum, down_grad, gate_up_rows)
    dkv = lax.psum_scatter(low_terms, "z", scatter_dimension=0, tiled=True)[0].astype(jnp.float32)
    dkv = jnp.where(core == 0, rotate(dkv, cos_rows, -sin_rows), dkv).astype(low).reshape(-1, HEAD_SIZE)
    layer_output = (r + feed_sum).astype(low)
    attention_term = jnp.concatenate([mm_tn(h1, dq), mm_tn(h1, dkv), mm_tn(drb, o)], axis=1).astype(low)
    attention_rows = scatter_planes(attention_term)
    dh1 = team_sum([dq, dkv], [query_weight, kv_weight], 9, [attention_term])
    in_grad, gain_one = rms_back(dh1, x_in, inverse_one, norm_gains[0])
    input_gradient = dr + in_grad
    gate_up_grad = scatter_team(gate_up_rows, 8, [dh1])
    attention_grad = scatter_team(attention_rows, 10)
    grads = (gate_up_grad, down_grad, attention_grad)
    local_squares = sum(jnp.sum(jnp.square(grad.astype(jnp.float32))) for grad in grads)
    gain_local = jnp.stack([gain_one, gain_two])
    if is_square():
        lines = jnp.concatenate([gain_local.reshape(-1, 128), jnp.full((8, 128), local_squares)], axis=0)
        lines = total_sum(lines, nz, 11)
        gain_grad, squares = lines[:-8].reshape(2, width), lines[-1, 0]
    else:
        gain_grad, squares = lax.psum((gain_local, local_squares), ALL)
    gradient_norm = jnp.sqrt(squares + jnp.sum(gain_grad * gain_grad))
    factor = clip_norm / gradient_norm
    attention_new = update(attention_part, factor, attention_weight, attention_mean, attention_square, [attention_grad])
    feed_new = update(feed_part, factor, feed_weight, feed_mean, feed_square, [gate_up_grad, down_grad])
    gains_new = adamw(norm_gains, gain_grad * factor, gain_mean, gain_square, gain_rate, 0.0)
    return (
        layer_output.reshape(sequences, span, width),
        input_gradient.reshape(sequences, span, width),
        gradient_norm,
        *attention_new,
        *feed_new,
        *gains_new,
    )


def solution(mesh):
    ctx, fsdp = mesh.shape["ctx"], mesh.shape["fsdp"]
    inner = QUERY_HEADS // fsdp
    fine = Mesh(mesh.devices.reshape(ctx // inner, inner, fsdp // 2, 2), ALL)
    act = P(("x", "c"), ("z", "y"), None)
    matrix = P(ALL, None)
    return jax.shard_map(
        local,
        mesh=fine,
        in_specs=(act, P(("x", "c")), P(), matrix, matrix, act, matrix, matrix, matrix, matrix, P(), P()),
        out_specs=(act, act, P(), matrix, matrix, matrix, matrix, matrix, matrix, matrix, matrix, P(), P(), P()),
        check_vma=False,
    )
```

```python
import functools

import jax
import jax.numpy as jnp
from jax import lax
from jax.experimental import pallas as pl
from jax.experimental.pallas import tpu as pltpu
from jax.sharding import Mesh, PartitionSpec as P

QUERY_HEADS = 8
KEY_VALUE_HEADS = 4
HEAD_SIZE = 256
FF = 8192
STEP = 10

norm_eps = 1e-06
rope_base = 1000042.0
masked_value = -1e30
clip_norm = 1.0
beta_one = 0.9
beta_two = 0.95
adam_eps = 1e-08
matrix_rate = 0.03
gain_rate = 0.4
weight_decay = 0.1

TEAM = ("y", "x", "c")
ALL = ("z", "y", "x", "c")


MESH = pl.DeviceIdType.MESH
VMEM = pl.BlockSpec(memory_space=pltpu.VMEM)
HBM = pl.BlockSpec(memory_space=pl.ANY)


def place():
    y, x, c = lax.axis_index("y"), lax.axis_index("x"), lax.axis_index("c")
    return y, x, c, lambda yy, xx, cc: (yy * 2 + xx) * 2 + cc


def greet(others):
    barrier = pltpu.get_barrier_semaphore()
    for other in others:
        pl.semaphore_signal(barrier, inc=1, device_id=other, device_id_type=MESH)
    pl.semaphore_wait(barrier, len(others))


def gather_kernel(src, *refs):
    out, send, recv, own = refs[-4:]
    y, x, c, index = place()
    to_x, to_y, to_s = {"x": 1 - x}, {"y": 1 - y}, {"c": 1 - c}
    me, at_x, at_y, at_d = index(y, x, c), index(y, 1 - x, c), index(1 - y, x, c), index(1 - y, 1 - x, c)
    half = src.shape[0] // 2
    rows = (pl.ds(0, half), pl.ds(half, half))
    local = pltpu.make_async_copy(src, out.at[me], own)
    local.start()
    greet((to_x, to_y, to_s))

    def hop(slot, block, part, where, first=False):
        piece = out.at[block, rows[part]]
        return pltpu.make_async_remote_copy(
            src_ref=src.at[rows[part]] if first else piece,
            dst_ref=piece,
            send_sem=send.at[slot],
            recv_sem=recv.at[slot],
            device_id=where,
            device_id_type=MESH,
        )

    x0, x1 = hop(0, me, 0, to_x, True), hop(1, me, 1, to_x, True)
    y1, y0 = hop(2, me, 1, to_y, True), hop(3, me, 0, to_y, True)
    s0, s1 = hop(4, me, 0, to_s, True), hop(5, me, 1, to_s, True)
    for copy in (x0, y1, x1, y0, s0, s1):
        copy.start()
    x0.wait_recv()
    d0 = hop(6, at_x, 0, to_y)
    d0.start()
    y1.wait_recv()
    d1 = hop(7, at_y, 1, to_x)
    d1.start()
    sx0, sy1 = hop(8, at_x, 0, to_s), hop(9, at_y, 1, to_s)
    sx0.start()
    sy1.start()
    x1.wait_recv()
    sx1 = hop(10, at_x, 1, to_s)
    sx1.start()
    y0.wait_recv()
    sy0 = hop(11, at_y, 0, to_s)
    sy0.start()
    d0.wait_recv()
    sd0 = hop(12, at_d, 0, to_s)
    sd0.start()
    d1.wait_recv()
    sd1 = hop(13, at_d, 1, to_s)
    sd1.start()
    for copy in (s0, s1, sx0, sy1, sx1, sy0, sd0, sd1):
        copy.wait_recv()
    for copy in (x0, x1, y0, y1, s0, s1, d0, d1, sx0, sy1, sx1, sy0, sd0, sd1):
        copy.wait_send()
    local.wait()


def plane_gather(value, number, after=()):
    return pl.pallas_call(
        gather_kernel,
        out_shape=jax.ShapeDtypeStruct((8, *value.shape), value.dtype),
        in_specs=[HBM] * (1 + len(after)),
        out_specs=HBM,
        scratch_shapes=[
            pltpu.SemaphoreType.DMA((14,)),
            pltpu.SemaphoreType.DMA((14,)),
            pltpu.SemaphoreType.DMA,
        ],
        compiler_params=pltpu.CompilerParams(collective_id=number, has_side_effects=True),
        cost_estimate=pl.CostEstimate(flops=1, bytes_accessed=1, transcendentals=0),
        name="plane_gather",
    )(value, *after)


def sum_kernel(lefts, terms, tile, *refs):
    a_refs, w_refs = refs[:lefts], refs[lefts : lefts + len(terms)]
    out, s_send, s_recv, d_send, d_recv, x_send, x_recv, y_send, y_recv, x_acc, y_acc, send, recv = refs[-13:]
    y, x, c, index = place()
    to_x, to_y, to_s = {"x": 1 - x}, {"y": 1 - y}, {"c": 1 - c}
    rows, width = out.shape
    half = rows // 2
    parts = (pl.ds(0, half), pl.ds(half, half))
    f32, low = jnp.float32, jnp.bfloat16

    def product(block, put):
        lines = pl.ds(pl.multiple_of(block * rows, rows), rows)

        @pl.loop(0, width // tile)
        def _(step):
            cols = pl.ds(pl.multiple_of(step * tile, tile), tile)
            total = None
            for (left, start), w_ref in zip(terms, w_refs):
                term = mm_nt(a_refs[left][lines, start : start + w_ref.shape[1]], w_ref[cols, :])
                total = term if total is None else total + term
            put(cols, total)

    def hop(slot, src, dst, where):
        copy = pltpu.make_async_remote_copy(
            src_ref=src, dst_ref=dst, send_sem=send.at[slot], recv_sem=recv.at[slot],
            device_id=where, device_id_type=MESH,
        )
        return copy

    def to_sibling(slot, yy, xx):
        def put(cols, total):
            s_send[slot, :, cols] = total.astype(low)

        product(index(yy, xx, 1 - c), put)
        copy = hop(slot, s_send.at[slot], s_recv.at[slot], to_s)
        copy.start()
        return copy

    def with_sibling(slot, yy, xx, keep):
        def put(cols, total):
            keep[:, cols] = (total + s_recv[slot, :, cols].astype(f32)).astype(keep.dtype)

        product(index(yy, xx, c), put)

    greet((to_x, to_y, to_s))
    s0 = to_sibling(0, 1 - y, 1 - x)
    s1 = to_sibling(1, y, 1 - x)
    s0.wait_recv()
    with_sibling(0, 1 - y, 1 - x, d_send)
    d0 = hop(4, d_send.at[parts[0]], d_recv.at[parts[0]], to_x)
    d1 = hop(5, d_send.at[parts[1]], d_recv.at[parts[1]], to_y)
    d0.start()
    d1.start()
    s1.wait_recv()
    with_sibling(1, y, 1 - x, x_acc)
    x_send[parts[0]] = x_acc[parts[0]].astype(low)
    x0 = hop(6, x_send.at[parts[0]], x_recv.at[parts[0]], to_x)
    x0.start()
    s2 = to_sibling(2, 1 - y, x)
    s2.wait_recv()
    with_sibling(2, 1 - y, x, y_acc)
    y_send[parts[1]] = y_acc[parts[1]].astype(low)
    y1 = hop(7, y_send.at[parts[1]], y_recv.at[parts[1]], to_y)
    y1.start()
    s3 = to_sibling(3, y, x)
    d1.wait_recv()
    x_send[parts[1]] = (x_acc[parts[1]] + d_recv[parts[1]].astype(f32)).astype(low)
    x1 = hop(8, x_send.at[parts[1]], x_recv.at[parts[1]], to_x)
    x1.start()
    d0.wait_recv()
    y_send[parts[0]] = (y_acc[parts[0]] + d_recv[parts[0]].astype(f32)).astype(low)
    y0 = hop(9, y_send.at[parts[0]], y_recv.at[parts[0]], to_y)
    y0.start()
    s3.wait_recv()
    with_sibling(3, y, x, out)
    x0.wait_recv()
    y1.wait_recv()
    x1.wait_recv()
    y0.wait_recv()
    out[...] += x_recv[...].astype(f32) + y_recv[...].astype(f32)
    for copy in (s0, s1, s2, s3, d0, d1, x0, x1, y0, y1):
        copy.wait_send()


def plane_sum(lefts, rights, number, after=(), tile=512):
    ends = [(left, start) for left, a in enumerate(lefts) for start in range(0, a.shape[1], rights[0].shape[1])]
    terms = tuple(ends[: len(rights)])
    rows, width = lefts[0].shape[0] // 8, rights[0].shape[0]
    block = (rows, width)
    low, f32 = jnp.bfloat16, jnp.float32
    return pl.pallas_call(
        functools.partial(sum_kernel, len(lefts), terms, min(tile, width)),
        out_shape=jax.ShapeDtypeStruct(block, f32),
        in_specs=[VMEM] * (len(lefts) + len(rights)) + [HBM] * len(after),
        out_specs=VMEM,
        scratch_shapes=[
            pltpu.VMEM((4, *block), low),
            pltpu.VMEM((4, *block), low),
            *[pltpu.VMEM(block, low)] * 6,
            pltpu.VMEM(block, f32),
            pltpu.VMEM(block, f32),
            pltpu.SemaphoreType.DMA((10,)),
            pltpu.SemaphoreType.DMA((10,)),
        ],
        compiler_params=pltpu.CompilerParams(
            collective_id=number, has_side_effects=True, vmem_limit_bytes=48 * 2**20
        ),
        cost_estimate=pl.CostEstimate(flops=1, bytes_accessed=1, transcendentals=0),
        name="plane_sum",
    )(*lefts, *rights, *after)


def swap_kernel(pieces, takes, *refs):
    count = len(pieces)
    sources, (send, recv, own) = refs[: -2 * count - 3], refs[-3:]
    outs, holds = refs[-2 * count - 3 : -count - 3], refs[-count - 3 : -3]
    y, x, c, index = place()
    me = index(y, x, c)
    flips = [(fy, fx, fc) for fy, fx in ((1, 1), (0, 1), (1, 0), (0, 0)) for fc in (0, 1)]
    flips = [flip for flip in flips if flip != (0, 0, 0)]

    def there(flip):
        return tuple(1 - at if f else at for at, f in zip((y, x, c), flip))

    greet([dict(zip(("y", "x", "c"), there(flip))) for flip in flips])
    copies = []
    for piece in range(count):
        for number, flip in enumerate(flips):
            yy, xx, cc = there(flip)
            member = index(yy, xx, cc)
            holds[piece][number] = takes[piece](sources, member, cc)
            copy = pltpu.make_async_remote_copy(
                src_ref=holds[piece].at[number],
                dst_ref=outs[piece].at[me],
                send_sem=send.at[piece * 7 + number],
                recv_sem=recv.at[piece * 7 + number],
                device_id={"y": yy, "x": xx, "c": cc},
                device_id_type=MESH,
            )
            copy.start()
            copies.append(copy)
        holds[piece][7] = takes[piece](sources, me, c)
        keep = pltpu.make_async_copy(holds[piece].at[7], outs[piece].at[me], own.at[piece])
        keep.start()
        copies.append(keep)
    for copy in copies:
        copy.wait()


def plane_swap(sources, shapes, takes, number, after=()):
    low = jnp.bfloat16
    count = len(shapes)
    return pl.pallas_call(
        functools.partial(swap_kernel, shapes, takes),
        out_shape=[jax.ShapeDtypeStruct((8, *shape), low) for shape in shapes],
        in_specs=[VMEM] * len(sources) + [HBM] * len(after),
        out_specs=[HBM] * count,
        scratch_shapes=[
            *[pltpu.VMEM((8, *shape), low) for shape in shapes],
            pltpu.SemaphoreType.DMA((7 * count,)),
            pltpu.SemaphoreType.DMA((7 * count,)),
            pltpu.SemaphoreType.DMA((count,)),
        ],
        compiler_params=pltpu.CompilerParams(
            collective_id=number, has_side_effects=True, vmem_limit_bytes=48 * 2**20
        ),
        cost_estimate=pl.CostEstimate(flops=1, bytes_accessed=1, transcendentals=0),
        name="plane_swap",
    )(*sources, *after)


def total_kernel(planes, src, out, near, far, send, recv):
    y, x, c, index = place()
    z = lax.axis_index("z")
    me = index(y, x, c)
    flips = [(fy, fx, fc) for fy in (0, 1) for fx in (0, 1) for fc in (0, 1)][1:]
    team = [
        dict(zip(("y", "x", "c"), (1 - at if f else at for at, f in zip((y, x, c), flip)))) for flip in flips
    ]
    column = [{"z": lax.rem(z + step, planes)} for step in range(1, planes)]
    near[me] = src[...]
    greet(team + column)

    def spread(buffer, at, others, base):
        copies = [
            pltpu.make_async_remote_copy(
                src_ref=buffer.at[at],
                dst_ref=buffer.at[at],
                send_sem=send.at[base + number],
                recv_sem=recv.at[base + number],
                device_id=other,
                device_id_type=MESH,
            )
            for number, other in enumerate(others)
        ]
        for copy in copies:
            copy.start()
        for copy in copies:
            copy.wait()

    spread(near, me, team, 0)
    far[z] = jnp.sum(near[...], axis=0)
    spread(far, z, column, 7)
    out[...] = jnp.sum(far[...], axis=0)


def total_sum(value, planes, number):
    return pl.pallas_call(
        functools.partial(total_kernel, planes),
        out_shape=jax.ShapeDtypeStruct(value.shape, value.dtype),
        in_specs=[VMEM],
        out_specs=VMEM,
        scratch_shapes=[
            pltpu.VMEM((8, *value.shape), value.dtype),
            pltpu.VMEM((planes, *value.shape), value.dtype),
            pltpu.SemaphoreType.DMA((6 + planes,)),
            pltpu.SemaphoreType.DMA((6 + planes,)),
        ],
        compiler_params=pltpu.CompilerParams(collective_id=number, has_side_effects=True),
        cost_estimate=pl.CostEstimate(flops=1, bytes_accessed=1, transcendentals=0),
        name="total_sum",
    )(value)


def dot(left, right, contract):
    return lax.dot_general(left, right, (contract, ((), ())), preferred_element_type=jnp.float32)


def mm(left, right):
    return dot(left, right, ((1,), (0,)))


def mm_nt(left, right):
    return dot(left, right, ((1,), (1,)))


def mm_tn(left, right):
    return dot(left, right, ((0,), (0,)))


def bmm(pattern, left, right):
    return jnp.einsum(pattern, left, right, preferred_element_type=jnp.float32)


def angle_tables(positions):
    half_dim = HEAD_SIZE // 2
    frequency = rope_base ** (-(jnp.arange(half_dim).astype(jnp.float32) * 2.0) / HEAD_SIZE)
    phases = positions.astype(jnp.float32)[:, None] * frequency[None, :]
    return (jnp.cos(phases), jnp.sin(phases))


def rotate(value, cos_table, sin_table):
    half = value.shape[-1] // 2
    a, b = value[..., :half], value[..., half:]
    return jnp.concatenate([a * cos_table - b * sin_table, b * cos_table + a * sin_table], axis=-1)


def rms_forward(value, gain_row):
    inverse = lax.rsqrt(jnp.mean(value * value, axis=-1, keepdims=True) + norm_eps)
    return (value * inverse * gain_row, inverse)


def rms_back(grad_out, value, inverse, gain_row):
    scaled = grad_out * gain_row
    grad_in = inverse * (
        scaled - value * inverse * inverse * jnp.mean(scaled * value, axis=-1, keepdims=True)
    )
    return (grad_in, jnp.sum(grad_out * value * inverse, axis=0))


def adamw(weight, gradient, moment_one, moment_two, step_rate, decay_rate):
    mean_new = beta_one * moment_one + (1.0 - beta_one) * gradient
    square_new = beta_two * moment_two + (1.0 - beta_two) * gradient * gradient
    direction = (mean_new * (1.0 / (1.0 - beta_one**STEP))) / (
        jnp.sqrt(square_new * (1.0 / (1.0 - beta_two**STEP))) + adam_eps
    )
    return (weight - step_rate * (direction + decay_rate * weight), mean_new, square_new)


def attention_parts(core, length, q_ref, mine_ref, other_ref, query_ref, key_ref):
    mine, other = mine_ref[...].reshape(-1, HEAD_SIZE), other_ref[...].reshape(-1, HEAD_SIZE)
    first = core == 0
    k, v = jnp.where(first, mine, other), jnp.where(first, other, mine)
    q = q_ref[...].reshape(-1, HEAD_SIZE)
    at, key_at = query_ref[...], key_ref[...]
    allowed = (key_at <= at) & (key_at < length) & (key_at >= 0)
    scores = jnp.where(allowed, mm_nt(q, k) * HEAD_SIZE ** (-0.5), masked_value)
    exponent = jnp.exp(scores - jnp.max(scores, axis=-1, keepdims=True))
    return q, k, v, exponent / jnp.sum(exponent, axis=-1, keepdims=True)


def attention_kernel(core_ref, length_ref, q_ref, mine_ref, other_ref, query_ref, key_ref, out_ref):
    length = length_ref[pl.program_id(0)]
    _, _, v, soft = attention_parts(core_ref[0], length, q_ref, mine_ref, other_ref, query_ref, key_ref)
    out_ref[...] = mm(soft.astype(jnp.bfloat16), v).astype(jnp.bfloat16).reshape(out_ref.shape)


def attention_back_kernel(
    core_ref, length_ref, q_ref, mine_ref, other_ref, query_ref, key_ref, do_ref, cos_ref, sin_ref,
    dq_ref, keep_ref, send_ref,
):
    low = jnp.bfloat16
    core = core_ref[0]
    length = length_ref[pl.program_id(0)]
    q, k, v, soft = attention_parts(core, length, q_ref, mine_ref, other_ref, query_ref, key_ref)
    do = do_ref[...].reshape(-1, HEAD_SIZE)
    dp = mm_nt(do, v)
    delta = jnp.sum(soft * dp, axis=-1, keepdims=True)
    ds = (soft * (dp - delta) * HEAD_SIZE ** (-0.5)).astype(low)
    dq = mm(ds, k)
    cos_table, sin_table = cos_ref[...], sin_ref[...]
    half = HEAD_SIZE // 2
    a, b = dq[:, :half], dq[:, half:]
    turned = jnp.concatenate([a * cos_table + b * sin_table, b * cos_table - a * sin_table], axis=-1)
    dq_ref[...] = turned.astype(low).reshape(dq_ref.shape)
    dk, dv = mm_tn(ds, q), mm_tn(soft.astype(low), do)
    first = core == 0
    keep, send = (t.reshape(keep_ref.shape) for t in (jnp.where(first, dk, dv), jnp.where(first, dv, dk)))
    for block in range(keep_ref.shape[0]):
        at = core_ref[1 + block]
        keep_ref[at] = keep[block]
        send_ref[at] = send[block].astype(low)


def attention_call(kernel, core, lengths, q, mine, other, query_pos, key_pos, extra, outs, name):
    ny, count, span, size = q.shape
    nz = mine.shape[0]
    rows = pl.BlockSpec((ny, 1, span, size), lambda i, *_: (0, i, 0, 0))
    keys = pl.BlockSpec((nz, ny, 1, span, size), lambda i, *_: (0, 0, i, 0, 0))

    def whole(value):
        return pl.BlockSpec(value.shape, lambda i, *_: (0,) * value.ndim)

    kinds = {"rows": (rows, q.shape), "keys": (keys, mine.shape)}
    return pl.pallas_call(
        kernel,
        grid_spec=pltpu.PrefetchScalarGridSpec(
            num_scalar_prefetch=2,
            grid=(count,),
            in_specs=[rows, keys, keys, whole(query_pos), whole(key_pos)]
            + [rows if value.shape == q.shape else whole(value) for value in extra],
            out_specs=[kinds[kind][0] for kind, _ in outs],
        ),
        out_shape=[jax.ShapeDtypeStruct(kinds[kind][1], dtype) for kind, dtype in outs],
        compiler_params=pltpu.CompilerParams(vmem_limit_bytes=48 * 2**20),
        cost_estimate=pl.CostEstimate(flops=1, bytes_accessed=1, transcendentals=0),
        name=name,
    )(core, lengths, q, mine, other, query_pos, key_pos, *extra)


def feed_back_kernel(dyb_ref, weight_ref, gate_ref, up_ref, out_ref):
    dm = mm(dyb_ref[...], weight_ref[...])
    gate, upward = gate_ref[...], up_ref[...]
    sig = jax.nn.sigmoid(gate)
    part = gate.shape[1]
    out_ref[:, :part] = (dm * upward * sig * (1.0 + gate * (1.0 - sig))).astype(out_ref.dtype)
    out_ref[:, part:] = (dm * gate * sig).astype(out_ref.dtype)


def feed_back(dyb, weight, both, lines=256):
    count, part = both.shape[0], both.shape[1] // 2

    def rows(width, column=0):
        return pl.BlockSpec((lines, width), lambda i: (i, column))

    return pl.pallas_call(
        feed_back_kernel,
        grid=(count // lines,),
        in_specs=[rows(dyb.shape[1]), pl.BlockSpec(weight.shape, lambda i: (0, 0)), rows(part), rows(part, 1)],
        out_specs=rows(2 * part),
        out_shape=jax.ShapeDtypeStruct((count, 2 * part), jnp.bfloat16),
        compiler_params=pltpu.CompilerParams(vmem_limit_bytes=48 * 2**20),
        cost_estimate=pl.CostEstimate(flops=1, bytes_accessed=1, transcendentals=0),
        name="feed_back",
    )(dyb, weight, both, both)


def attention_part(step, grad_ref):
    column = jnp.where(step < 2, 0, jnp.where(step < 4, 1, 2))
    parts = []
    for head in range(4):
        member = jnp.where((step == 2) | (step == 3), 2 * head + step - 2, 4 * (step % 2) + head)
        parts.append(grad_ref[member, :, pl.ds(pl.multiple_of(column * HEAD_SIZE, HEAD_SIZE), HEAD_SIZE)])
    return jnp.concatenate(parts, axis=1)


def feed_part(step, gate_up_ref, down_ref):
    size = down_ref.shape[2]
    both = gate_up_ref[step % 8, :, pl.ds(pl.multiple_of(jnp.minimum(step // 8, 1) * size, size), size)]
    return jnp.where(step < 16, both, down_ref[step % 8])


def update_kernel(part, factor_ref, weight_ref, mean_ref, square_ref, *refs):
    grads, (new_ref, new_mean_ref, new_square_ref, copy_ref) = refs[:-4], refs[-4:]
    gradient = part(pl.program_id(0), *grads).astype(jnp.float32) * factor_ref[0]
    new, mean, square = adamw(
        weight_ref[...], gradient, mean_ref[...], square_ref[...], matrix_rate, weight_decay
    )
    new_ref[...] = new
    new_mean_ref[...] = mean
    new_square_ref[...] = square
    copy_ref[...] = new.astype(copy_ref.dtype)


def update(part, factor, weight, mean, square, grads, size=1024):
    rows, width = weight.shape
    block = pl.BlockSpec((rows, size), lambda i: (0, i))
    f32 = jnp.float32
    return pl.pallas_call(
        functools.partial(update_kernel, part),
        grid=(width // size,),
        in_specs=[pl.BlockSpec(memory_space=pltpu.SMEM), block, block, block]
        + [pl.BlockSpec(grad.shape, lambda i: (0, 0, 0)) for grad in grads],
        out_specs=[block] * 4,
        out_shape=[jax.ShapeDtypeStruct(weight.shape, dtype) for dtype in (f32, f32, f32, jnp.bfloat16)],
        compiler_params=pltpu.CompilerParams(vmem_limit_bytes=48 * 2**20),
        name="update",
    )(jnp.reshape(factor, (1,)), weight, mean, square, *grads)


def is_square():
    return lax.axis_size("y") == 2 and lax.axis_size("x") == 2


def swap(blocks):
    return lax.all_to_all(blocks, TEAM, split_axis=0, concat_axis=0, tiled=True)


def over_planes(blocks):
    return lax.all_gather(blocks.reshape(-1, blocks.shape[-1]), "z", axis=0, tiled=True)


def scatter_planes(term):
    return lax.psum_scatter(term, "z", scatter_dimension=0, tiled=True)


def together(*values):
    return lax.optimization_barrier(values)


def scatter_team(rows, number, after=()):
    if not is_square():
        return swap(rows.reshape(8, -1, rows.shape[-1]))
    count = rows.shape[0] // 8

    def take(sources, member, core):
        return sources[0][pl.ds(pl.multiple_of(member * count, count), count), :]

    return plane_swap([rows], [(count, rows.shape[1])], [take], number, after)[0]


def team_gather(local, number, after=()):
    if not is_square():
        return lax.all_gather(local, TEAM, axis=0, tiled=True)
    return plane_gather(local, number, after).reshape(-1, local.shape[1])


def team_sum(lefts, rights, number, after=()):
    if is_square():
        return plane_sum(lefts, rights, number, after)
    partial = mm_nt(jnp.concatenate(lefts, axis=1), jnp.concatenate(rights, axis=1))
    return lax.psum_scatter(partial.astype(jnp.bfloat16), TEAM, scatter_dimension=0, tiled=True).astype(jnp.float32)


def local(
    tokens,
    lengths,
    norm_gains,
    attention_weight,
    feed_weight,
    cotangent,
    attention_mean,
    attention_square,
    feed_mean,
    feed_square,
    gain_mean,
    gain_square,
):
    low = jnp.bfloat16
    sequences, span, width = tokens.shape
    ny, nx, nz = lax.axis_size("y"), lax.axis_size("x"), lax.axis_size("z")
    team = ny * nx * 2
    core = lax.axis_index("c")
    rows = attention_weight.shape[0]
    q_width, kv_width = QUERY_HEADS * HEAD_SIZE, KEY_VALUE_HEADS * HEAD_SIZE
    count = sequences * span
    all_sequences = nx * 2 * sequences
    reach = ny * span
    near = nz <= 4
    ff_part = FF // team

    def columns(start, size):
        return pl.ds(pl.multiple_of(start, size), size)

    def take_attention(sources, member, c):
        source = sources[0]
        starts = (
            member * HEAD_SIZE,
            q_width + c * kv_width + (member - c) // 2 * HEAD_SIZE,
            q_width + 2 * kv_width + member * HEAD_SIZE,
        )
        return jnp.concatenate([source[:, columns(s, HEAD_SIZE)].astype(low) for s in starts], axis=1)

    def take_feed(*parts):
        return lambda sources, member, c: jnp.concatenate(
            [sources[0][:, columns(part * FF + member * ff_part, ff_part)].astype(low) for part in parts], axis=1
        )

    def spread(source, take, size, number, after=()):
        if is_square():
            blocks = plane_swap([source], [(rows, size)], [take], number, after)[0]
        else:
            blocks = swap(jnp.stack([take([source], member, member % 2) for member in range(8)]))
        return blocks, over_planes(blocks)

    attention_blocks, attention_mine = spread(attention_weight, take_attention, 3 * HEAD_SIZE, 1)
    gate_up_blocks, gate_up_weight = spread(feed_weight, take_feed(0, 1), 2 * ff_part, 2, [attention_blocks])

    team_base = lax.axis_index("z") * reach
    team_pos = team_base + jnp.arange(reach, dtype=jnp.int32)
    own_pos = team_base + lax.axis_index("y") * span + jnp.arange(span, dtype=jnp.int32)
    if near:
        key_pos = jnp.concatenate([team_pos - back * reach for back in range(nz)])
    else:
        key_pos = jnp.arange(nz * reach, dtype=jnp.int32)
    query_at, key_at = team_pos[:, None], key_pos[None, :]
    cos_table, sin_table = angle_tables(team_pos)
    cos_rows, sin_rows = (t.reshape(ny, 1, span, -1) for t in (cos_table, sin_table))
    valid = (own_pos[None, :] < lengths[:, None]).astype(jnp.float32).reshape(count, 1)
    lengths_all = lax.all_gather(lengths, ("x", "c"), axis=0, tiled=True)
    planes = jnp.arange(nz, dtype=jnp.int32)
    if near:
        planes = (lax.axis_index("z") - planes) % nz
    core_at = jnp.concatenate([jnp.reshape(core, (1,)), planes]).astype(jnp.int32)

    def heads(value):
        return value.reshape(ny, all_sequences, span, HEAD_SIZE)

    x_in = tokens.reshape(count, width).astype(jnp.float32)
    normed_one, inverse_one = rms_forward(x_in, norm_gains[0])
    outer_grad = cotangent.reshape(count, width).astype(jnp.float32) * valid
    h1 = team_gather(normed_one.astype(low), 3, [gate_up_blocks])
    attention_mine, lengths_all = together(attention_mine, lengths_all)
    query_weight = attention_mine[:, :HEAD_SIZE]
    kv_weight = attention_mine[:, HEAD_SIZE : 2 * HEAD_SIZE]
    out_weight = attention_mine[:, 2 * HEAD_SIZE :]
    kv_raw = heads(mm(h1, kv_weight))
    kv = jnp.where(core == 0, rotate(kv_raw, cos_rows, sin_rows), kv_raw).astype(low)
    q = rotate(heads(mm(h1, query_weight)), cos_rows, sin_rows).astype(low)
    dyb = team_gather(outer_grad.astype(low), 15, [kv])
    down_blocks, down_weight = spread(feed_weight, take_feed(2), ff_part, 12, [dyb])
    if near:
        earlier = [
            lax.ppermute(kv, "z", [(at, at + back) for at in range(nz - back)]) for back in range(1, nz)
        ]
        *earlier, dyb, down_blocks, q = lax.optimization_barrier((*earlier, dyb, down_blocks, q))
        kv = jnp.stack([kv, *earlier])
    else:
        kv = lax.all_gather(kv, "z", axis=0, tiled=False)
    other = lax.ppermute(kv, "c", [(0, 1), (1, 0)])
    attend = (core_at, lengths_all, q, kv, other, query_at, key_at)
    (o,) = attention_call(attention_kernel, *attend, (), [("rows", low)], "attention")
    o = o.reshape(-1, HEAD_SIZE)
    r = x_in + team_sum([o], [out_weight], 4)

    normed_two, inverse_two = rms_forward(r, norm_gains[1])
    h2 = team_gather(normed_two.astype(low), 16)
    both = mm(h2, gate_up_weight)
    gate, upward = both[:, :ff_part], both[:, ff_part:]
    sig = jax.nn.sigmoid(gate)
    m = (gate * sig * upward).astype(low)
    down_term = mm_tn(dyb, m).astype(low)
    down_rows = scatter_planes(down_term)
    down_weight, down_term = together(down_weight, down_term)
    d_both = feed_back(dyb, down_weight, both)
    gate_up_term = mm_tn(h2, d_both).astype(low)
    gate_up_rows = scatter_planes(gate_up_term)
    dh2 = team_sum([d_both], [gate_up_weight], 7, [gate_up_term, down_term])
    mid_grad, gain_two = rms_back(dh2, r, inverse_two, norm_gains[1])
    dr = outer_grad + mid_grad
    drb = team_gather(dr.astype(low), 13, [down_rows])

    do = heads(mm(drb, out_weight).astype(low))
    dq, keep, theirs = attention_call(
        attention_back_kernel,
        *attend,
        (do, cos_table, sin_table),
        [("rows", low), ("keys", jnp.float32), ("keys", low)],
        "attention_back",
    )
    dq = dq.reshape(-1, HEAD_SIZE)
    dkv = keep + lax.ppermute(theirs, "c", [(0, 1), (1, 0)]).astype(jnp.float32)
    low_terms = dkv.astype(low)
    feed_sum = team_sum([m], [down_weight], 5, [low_terms])
    down_grad = scatter_team(down_rows, 6, [low_terms])
    dkv = lax.psum_scatter(low_terms, "z", scatter_dimension=0, tiled=True)[0]
    dkv, feed_sum, down_grad, gate_up_rows = together(dkv, feed_sum, down_grad, gate_up_rows)
    dkv = dkv.astype(jnp.float32)
    dkv = jnp.where(core == 0, rotate(dkv, cos_rows, -sin_rows), dkv).astype(low).reshape(-1, HEAD_SIZE)
    layer_output = (r + feed_sum).astype(low)
    attention_term = jnp.concatenate([mm_tn(h1, dq), mm_tn(h1, dkv), mm_tn(drb, o)], axis=1).astype(low)
    attention_rows = scatter_planes(attention_term)
    dh1 = team_sum([dq, dkv], [query_weight, kv_weight], 9, [attention_term])
    in_grad, gain_one = rms_back(dh1, x_in, inverse_one, norm_gains[0])
    input_gradient = dr + in_grad
    gate_up_grad = scatter_team(gate_up_rows, 8, [dh1])
    attention_grad = scatter_team(attention_rows, 10)
    grads = (gate_up_grad, down_grad, attention_grad)
    local_squares = sum(jnp.sum(jnp.square(grad.astype(jnp.float32))) for grad in grads)
    gain_local = jnp.stack([gain_one, gain_two])
    if is_square():
        lines = jnp.concatenate([gain_local.reshape(-1, 128), jnp.full((8, 128), local_squares)], axis=0)
        lines = total_sum(lines, nz, 11)
        gain_grad, squares = lines[:-8].reshape(2, width), lines[-1, 0]
    else:
        gain_grad, squares = lax.psum((gain_local, local_squares), ALL)
    gradient_norm = jnp.sqrt(squares + jnp.sum(gain_grad * gain_grad))
    factor = clip_norm / gradient_norm
    attention_new = update(attention_part, factor, attention_weight, attention_mean, attention_square, [attention_grad])
    feed_new = update(feed_part, factor, feed_weight, feed_mean, feed_square, [gate_up_grad, down_grad])
    gains_new = adamw(norm_gains, gain_grad * factor, gain_mean, gain_square, gain_rate, 0.0)
    return (
        layer_output.reshape(sequences, span, width),
        input_gradient.reshape(sequences, span, width),
        gradient_norm,
        *attention_new,
        *feed_new,
        *gains_new,
    )


def solution(mesh):
    ctx, fsdp = mesh.shape["ctx"], mesh.shape["fsdp"]
    inner = QUERY_HEADS // fsdp
    fine = Mesh(mesh.devices.reshape(ctx // inner, inner, fsdp // 2, 2), ALL)
    act = P(("x", "c"), ("z", "y"), None)
    matrix = P(ALL, None)
    return jax.shard_map(
        local,
        mesh=fine,
        in_specs=(act, P(("x", "c")), P(), matrix, matrix, act, matrix, matrix, matrix, matrix, P(), P()),
        out_specs=(act, act, P(), matrix, matrix, matrix, matrix, matrix, matrix, matrix, matrix, P(), P(), P()),
        check_vma=False,
    )
```

```python
import functools

import jax
import jax.numpy as jnp
from jax import lax
from jax.experimental import pallas as pl
from jax.experimental.pallas import tpu as pltpu
from jax.sharding import Mesh, PartitionSpec as P

QUERY_HEADS = 8
KEY_VALUE_HEADS = 4
HEAD_SIZE = 256
FF = 8192
STEP = 10

norm_eps = 1e-06
rope_base = 1000042.0
masked_value = -1e30
clip_norm = 1.0
beta_one = 0.9
beta_two = 0.95
adam_eps = 1e-08
matrix_rate = 0.03
gain_rate = 0.4
weight_decay = 0.1

TEAM = ("y", "x", "c")
ALL = ("z", "y", "x", "c")


MESH = pl.DeviceIdType.MESH
VMEM = pl.BlockSpec(memory_space=pltpu.VMEM)
HBM = pl.BlockSpec(memory_space=pl.ANY)


def place():
    y, x, c = lax.axis_index("y"), lax.axis_index("x"), lax.axis_index("c")
    return y, x, c, lambda yy, xx, cc: (yy * 2 + xx) * 2 + cc


def greet(others):
    barrier = pltpu.get_barrier_semaphore()
    for other in others:
        pl.semaphore_signal(barrier, inc=1, device_id=other, device_id_type=MESH)
    pl.semaphore_wait(barrier, len(others))


def gather_kernel(src, *refs):
    out, send, recv, own = refs[-4:]
    y, x, c, index = place()
    to_x, to_y, to_s = {"x": 1 - x}, {"y": 1 - y}, {"c": 1 - c}
    me, at_x, at_y, at_d = index(y, x, c), index(y, 1 - x, c), index(1 - y, x, c), index(1 - y, 1 - x, c)
    half = src.shape[0] // 2
    rows = (pl.ds(0, half), pl.ds(half, half))
    local = pltpu.make_async_copy(src, out.at[me], own)
    local.start()
    greet((to_x, to_y, to_s))

    def hop(slot, block, part, where, first=False):
        piece = out.at[block, rows[part]]
        return pltpu.make_async_remote_copy(
            src_ref=src.at[rows[part]] if first else piece,
            dst_ref=piece,
            send_sem=send.at[slot],
            recv_sem=recv.at[slot],
            device_id=where,
            device_id_type=MESH,
        )

    x0, x1 = hop(0, me, 0, to_x, True), hop(1, me, 1, to_x, True)
    y1, y0 = hop(2, me, 1, to_y, True), hop(3, me, 0, to_y, True)
    s0, s1 = hop(4, me, 0, to_s, True), hop(5, me, 1, to_s, True)
    for copy in (x0, y1, x1, y0, s0, s1):
        copy.start()
    x0.wait_recv()
    d0 = hop(6, at_x, 0, to_y)
    d0.start()
    y1.wait_recv()
    d1 = hop(7, at_y, 1, to_x)
    d1.start()
    sx0, sy1 = hop(8, at_x, 0, to_s), hop(9, at_y, 1, to_s)
    sx0.start()
    sy1.start()
    x1.wait_recv()
    sx1 = hop(10, at_x, 1, to_s)
    sx1.start()
    y0.wait_recv()
    sy0 = hop(11, at_y, 0, to_s)
    sy0.start()
    d0.wait_recv()
    sd0 = hop(12, at_d, 0, to_s)
    sd0.start()
    d1.wait_recv()
    sd1 = hop(13, at_d, 1, to_s)
    sd1.start()
    for copy in (s0, s1, sx0, sy1, sx1, sy0, sd0, sd1):
        copy.wait_recv()
    for copy in (x0, x1, y0, y1, s0, s1, d0, d1, sx0, sy1, sx1, sy0, sd0, sd1):
        copy.wait_send()
    local.wait()


def plane_gather(value, number, after=()):
    return pl.pallas_call(
        gather_kernel,
        out_shape=jax.ShapeDtypeStruct((8, *value.shape), value.dtype),
        in_specs=[HBM] * (1 + len(after)),
        out_specs=HBM,
        scratch_shapes=[
            pltpu.SemaphoreType.DMA((14,)),
            pltpu.SemaphoreType.DMA((14,)),
            pltpu.SemaphoreType.DMA,
        ],
        compiler_params=pltpu.CompilerParams(collective_id=number, has_side_effects=True),
        cost_estimate=pl.CostEstimate(flops=1, bytes_accessed=1, transcendentals=0),
        name="plane_gather",
    )(value, *after)


def sum_kernel(lefts, terms, tile, *refs):
    a_refs, w_refs = refs[:lefts], refs[lefts : lefts + len(terms)]
    out, s_send, s_recv, d_send, d_recv, x_send, x_recv, y_send, y_recv, x_acc, y_acc, send, recv = refs[-13:]
    y, x, c, index = place()
    to_x, to_y, to_s = {"x": 1 - x}, {"y": 1 - y}, {"c": 1 - c}
    rows, width = out.shape
    half = rows // 2
    parts = (pl.ds(0, half), pl.ds(half, half))
    f32, low = jnp.float32, jnp.bfloat16

    def product(block, put):
        lines = pl.ds(pl.multiple_of(block * rows, rows), rows)

        @pl.loop(0, width // tile)
        def _(step):
            cols = pl.ds(pl.multiple_of(step * tile, tile), tile)
            total = None
            for (left, start), w_ref in zip(terms, w_refs):
                term = mm_nt(a_refs[left][lines, start : start + w_ref.shape[1]], w_ref[cols, :])
                total = term if total is None else total + term
            put(cols, total)

    def hop(slot, src, dst, where):
        copy = pltpu.make_async_remote_copy(
            src_ref=src, dst_ref=dst, send_sem=send.at[slot], recv_sem=recv.at[slot],
            device_id=where, device_id_type=MESH,
        )
        return copy

    def to_sibling(slot, yy, xx):
        def put(cols, total):
            s_send[slot, :, cols] = total.astype(low)

        product(index(yy, xx, 1 - c), put)
        copy = hop(slot, s_send.at[slot], s_recv.at[slot], to_s)
        copy.start()
        return copy

    def with_sibling(slot, yy, xx, keep):
        def put(cols, total):
            keep[:, cols] = (total + s_recv[slot, :, cols].astype(f32)).astype(keep.dtype)

        product(index(yy, xx, c), put)

    greet((to_x, to_y, to_s))
    s0 = to_sibling(0, 1 - y, 1 - x)
    s1 = to_sibling(1, y, 1 - x)
    s0.wait_recv()
    with_sibling(0, 1 - y, 1 - x, d_send)
    d0 = hop(4, d_send.at[parts[0]], d_recv.at[parts[0]], to_x)
    d1 = hop(5, d_send.at[parts[1]], d_recv.at[parts[1]], to_y)
    d0.start()
    d1.start()
    s1.wait_recv()
    with_sibling(1, y, 1 - x, x_acc)
    x_send[parts[0]] = x_acc[parts[0]].astype(low)
    x0 = hop(6, x_send.at[parts[0]], x_recv.at[parts[0]], to_x)
    x0.start()
    s2 = to_sibling(2, 1 - y, x)
    s2.wait_recv()
    with_sibling(2, 1 - y, x, y_acc)
    y_send[parts[1]] = y_acc[parts[1]].astype(low)
    y1 = hop(7, y_send.at[parts[1]], y_recv.at[parts[1]], to_y)
    y1.start()
    s3 = to_sibling(3, y, x)
    d1.wait_recv()
    x_send[parts[1]] = (x_acc[parts[1]] + d_recv[parts[1]].astype(f32)).astype(low)
    x1 = hop(8, x_send.at[parts[1]], x_recv.at[parts[1]], to_x)
    x1.start()
    d0.wait_recv()
    y_send[parts[0]] = (y_acc[parts[0]] + d_recv[parts[0]].astype(f32)).astype(low)
    y0 = hop(9, y_send.at[parts[0]], y_recv.at[parts[0]], to_y)
    y0.start()
    s3.wait_recv()
    with_sibling(3, y, x, out)
    x0.wait_recv()
    y1.wait_recv()
    x1.wait_recv()
    y0.wait_recv()
    out[...] += x_recv[...].astype(f32) + y_recv[...].astype(f32)
    for copy in (s0, s1, s2, s3, d0, d1, x0, x1, y0, y1):
        copy.wait_send()


def plane_sum(lefts, rights, number, after=(), tile=512):
    ends = [(left, start) for left, a in enumerate(lefts) for start in range(0, a.shape[1], rights[0].shape[1])]
    terms = tuple(ends[: len(rights)])
    rows, width = lefts[0].shape[0] // 8, rights[0].shape[0]
    block = (rows, width)
    low, f32 = jnp.bfloat16, jnp.float32
    return pl.pallas_call(
        functools.partial(sum_kernel, len(lefts), terms, min(tile, width)),
        out_shape=jax.ShapeDtypeStruct(block, f32),
        in_specs=[VMEM] * (len(lefts) + len(rights)) + [HBM] * len(after),
        out_specs=VMEM,
        scratch_shapes=[
            pltpu.VMEM((4, *block), low),
            pltpu.VMEM((4, *block), low),
            *[pltpu.VMEM(block, low)] * 6,
            pltpu.VMEM(block, f32),
            pltpu.VMEM(block, f32),
            pltpu.SemaphoreType.DMA((10,)),
            pltpu.SemaphoreType.DMA((10,)),
        ],
        compiler_params=pltpu.CompilerParams(
            collective_id=number, has_side_effects=True, vmem_limit_bytes=48 * 2**20
        ),
        cost_estimate=pl.CostEstimate(flops=1, bytes_accessed=1, transcendentals=0),
        name="plane_sum",
    )(*lefts, *rights, *after)


def swap_kernel(pieces, takes, *refs):
    count = len(pieces)
    sources, (send, recv, own) = refs[: -2 * count - 3], refs[-3:]
    outs, holds = refs[-2 * count - 3 : -count - 3], refs[-count - 3 : -3]
    y, x, c, index = place()
    me = index(y, x, c)
    flips = [(fy, fx, fc) for fy, fx in ((1, 1), (0, 1), (1, 0), (0, 0)) for fc in (0, 1)]
    flips = [flip for flip in flips if flip != (0, 0, 0)]

    def there(flip):
        return tuple(1 - at if f else at for at, f in zip((y, x, c), flip))

    greet([dict(zip(("y", "x", "c"), there(flip))) for flip in flips])
    copies = []
    for piece in range(count):
        for number, flip in enumerate(flips):
            yy, xx, cc = there(flip)
            member = index(yy, xx, cc)
            holds[piece][number] = takes[piece](sources, member, cc)
            copy = pltpu.make_async_remote_copy(
                src_ref=holds[piece].at[number],
                dst_ref=outs[piece].at[me],
                send_sem=send.at[piece * 7 + number],
                recv_sem=recv.at[piece * 7 + number],
                device_id={"y": yy, "x": xx, "c": cc},
                device_id_type=MESH,
            )
            copy.start()
            copies.append(copy)
        holds[piece][7] = takes[piece](sources, me, c)
        keep = pltpu.make_async_copy(holds[piece].at[7], outs[piece].at[me], own.at[piece])
        keep.start()
        copies.append(keep)
    for copy in copies:
        copy.wait()


def plane_swap(sources, shapes, takes, number, after=()):
    low = jnp.bfloat16
    count = len(shapes)
    return pl.pallas_call(
        functools.partial(swap_kernel, shapes, takes),
        out_shape=[jax.ShapeDtypeStruct((8, *shape), low) for shape in shapes],
        in_specs=[VMEM] * len(sources) + [HBM] * len(after),
        out_specs=[HBM] * count,
        scratch_shapes=[
            *[pltpu.VMEM((8, *shape), low) for shape in shapes],
            pltpu.SemaphoreType.DMA((7 * count,)),
            pltpu.SemaphoreType.DMA((7 * count,)),
            pltpu.SemaphoreType.DMA((count,)),
        ],
        compiler_params=pltpu.CompilerParams(
            collective_id=number, has_side_effects=True, vmem_limit_bytes=48 * 2**20
        ),
        cost_estimate=pl.CostEstimate(flops=1, bytes_accessed=1, transcendentals=0),
        name="plane_swap",
    )(*sources, *after)


def team_of(y, x, c):
    flips = [(fy, fx, fc) for fy, fx in ((1, 1), (0, 1), (1, 0), (0, 0)) for fc in (0, 1)]
    return [
        tuple(1 - at if f else at for at, f in zip((y, x, c), flip)) for flip in flips if flip != (0, 0, 0)
    ]


def turn_kernel(planes, src, *refs):
    y, x, c, index = place()
    me = index(y, x, c)
    others = team_of(y, x, c)
    ids = [dict(zip(("y", "x", "c"), other)) for other in others]
    if planes:
        lines, out, total, near, far, send, recv, own, send_lines, recv_lines = refs[:1] + refs[-9:]
        z = lax.axis_index("z")
        column = [{"z": lax.rem(z + step, planes)} for step in range(1, planes)]
        near[me] = lines[...]
    else:
        out, send, recv, own = refs[-4:]
        column = []
    greet(ids + column)
    count = src.shape[0] // 8

    def rows(member):
        return src.at[pl.ds(pl.multiple_of(member * count, count), count)]

    def spread(buffer, at, where, base):
        copies = [
            pltpu.make_async_remote_copy(
                src_ref=buffer.at[at],
                dst_ref=buffer.at[at],
                send_sem=send_lines.at[base + number],
                recv_sem=recv_lines.at[base + number],
                device_id=other,
                device_id_type=MESH,
            )
            for number, other in enumerate(where)
        ]
        for copy in copies:
            copy.start()
        return copies

    small = spread(near, me, ids, 0) if planes else []
    copies = [
        pltpu.make_async_remote_copy(
            src_ref=rows(index(*other)),
            dst_ref=out.at[me],
            send_sem=send.at[number],
            recv_sem=recv.at[number],
            device_id=where,
            device_id_type=MESH,
        )
        for number, (other, where) in enumerate(zip(others, ids))
    ]
    copies.append(pltpu.make_async_copy(rows(me), out.at[me], own))
    for copy in copies:
        copy.start()
    if planes:
        for copy in small:
            copy.wait()
        far[z] = jnp.sum(near[...], axis=0)
        for copy in spread(far, z, column, 7):
            copy.wait()
        total[...] = jnp.sum(far[...], axis=0)
    for copy in copies:
        copy.wait()


def turn(rows, number, after=(), lines=None, planes=0):
    block = (rows.shape[0] // 8, rows.shape[1])
    dma = pltpu.SemaphoreType.DMA
    out_shape, out_specs = [jax.ShapeDtypeStruct((8, *block), rows.dtype)], [HBM]
    in_specs, scratch = [HBM], [dma((7,)), dma((7,)), dma]
    operands = [rows]
    if planes:
        operands.append(lines)
        in_specs.append(VMEM)
        out_shape.append(jax.ShapeDtypeStruct(lines.shape, lines.dtype))
        out_specs.append(VMEM)
        buffers = [pltpu.VMEM((size, *lines.shape), lines.dtype) for size in (8, planes)]
        scratch = buffers + scratch + [dma((6 + planes,)), dma((6 + planes,))]
    return pl.pallas_call(
        functools.partial(turn_kernel, planes),
        out_shape=out_shape,
        in_specs=in_specs + [HBM] * len(after),
        out_specs=out_specs,
        scratch_shapes=scratch,
        compiler_params=pltpu.CompilerParams(collective_id=number, has_side_effects=True),
        cost_estimate=pl.CostEstimate(flops=1, bytes_accessed=1, transcendentals=0),
        name="turn",
    )(*operands, *after)


def dot(left, right, contract):
    return lax.dot_general(left, right, (contract, ((), ())), preferred_element_type=jnp.float32)


def mm(left, right):
    return dot(left, right, ((1,), (0,)))


def mm_nt(left, right):
    return dot(left, right, ((1,), (1,)))


def mm_tn(left, right):
    return dot(left, right, ((0,), (0,)))


def bmm(pattern, left, right):
    return jnp.einsum(pattern, left, right, preferred_element_type=jnp.float32)


def angle_tables(positions):
    half_dim = HEAD_SIZE // 2
    frequency = rope_base ** (-(jnp.arange(half_dim).astype(jnp.float32) * 2.0) / HEAD_SIZE)
    phases = positions.astype(jnp.float32)[:, None] * frequency[None, :]
    return (jnp.cos(phases), jnp.sin(phases))


def rotate(value, cos_table, sin_table):
    half = value.shape[-1] // 2
    a, b = value[..., :half], value[..., half:]
    return jnp.concatenate([a * cos_table - b * sin_table, b * cos_table + a * sin_table], axis=-1)


def rms_forward(value, gain_row):
    inverse = lax.rsqrt(jnp.mean(value * value, axis=-1, keepdims=True) + norm_eps)
    return (value * inverse * gain_row, inverse)


def rms_back(grad_out, value, inverse, gain_row):
    scaled = grad_out * gain_row
    grad_in = inverse * (
        scaled - value * inverse * inverse * jnp.mean(scaled * value, axis=-1, keepdims=True)
    )
    return (grad_in, jnp.sum(grad_out * value * inverse, axis=0))


def adamw(weight, gradient, moment_one, moment_two, step_rate, decay_rate, invert=jnp.reciprocal):
    mean_new = beta_one * moment_one + (1.0 - beta_one) * gradient
    square_new = beta_two * moment_two + (1.0 - beta_two) * gradient * gradient
    below = jnp.sqrt(square_new * (1.0 / (1.0 - beta_two**STEP))) + adam_eps
    direction = mean_new * (1.0 / (1.0 - beta_one**STEP)) * invert(below)
    return (weight - step_rate * (direction + decay_rate * weight), mean_new, square_new)


def attention_parts(core, length, q_ref, mine_ref, other_ref, query_ref, key_ref):
    mine, other = mine_ref[...].reshape(-1, HEAD_SIZE), other_ref[...].reshape(-1, HEAD_SIZE)
    first = core == 0
    k, v = jnp.where(first, mine, other), jnp.where(first, other, mine)
    q = q_ref[...].reshape(-1, HEAD_SIZE)
    at, key_at = query_ref[...], key_ref[...]
    allowed = (key_at <= at) & (key_at < length) & (key_at >= 0)
    scores = jnp.where(allowed, mm_nt(q, k) * HEAD_SIZE ** (-0.5), masked_value)
    exponent = jnp.exp(scores - jnp.max(scores, axis=-1, keepdims=True))
    return q, k, v, exponent / jnp.sum(exponent, axis=-1, keepdims=True)


def attention_kernel(core_ref, length_ref, q_ref, mine_ref, other_ref, query_ref, key_ref, out_ref):
    length = length_ref[pl.program_id(0)]
    _, _, v, soft = attention_parts(core_ref[0], length, q_ref, mine_ref, other_ref, query_ref, key_ref)
    out_ref[...] = mm(soft.astype(jnp.bfloat16), v).astype(jnp.bfloat16).reshape(out_ref.shape)


def attention_back_kernel(
    core_ref, length_ref, q_ref, mine_ref, other_ref, query_ref, key_ref, do_ref, cos_ref, sin_ref,
    dq_ref, keep_ref, send_ref,
):
    low = jnp.bfloat16
    core = core_ref[0]
    length = length_ref[pl.program_id(0)]
    q, k, v, soft = attention_parts(core, length, q_ref, mine_ref, other_ref, query_ref, key_ref)
    do = do_ref[...].reshape(-1, HEAD_SIZE)
    dp = mm_nt(do, v)
    delta = jnp.sum(soft * dp, axis=-1, keepdims=True)
    ds = (soft * (dp - delta) * HEAD_SIZE ** (-0.5)).astype(low)
    dq = mm(ds, k)
    cos_table, sin_table = cos_ref[...], sin_ref[...]
    half = HEAD_SIZE // 2
    a, b = dq[:, :half], dq[:, half:]
    turned = jnp.concatenate([a * cos_table + b * sin_table, b * cos_table - a * sin_table], axis=-1)
    dq_ref[...] = turned.astype(low).reshape(dq_ref.shape)
    dk, dv = mm_tn(ds, q), mm_tn(soft.astype(low), do)
    first = core == 0
    keep, send = (t.reshape(keep_ref.shape) for t in (jnp.where(first, dk, dv), jnp.where(first, dv, dk)))
    for block in range(keep_ref.shape[0]):
        at = core_ref[1 + block]
        keep_ref[at] = keep[block]
        send_ref[at] = send[block].astype(low)


def attention_call(kernel, core, lengths, q, mine, other, query_pos, key_pos, extra, outs, name):
    ny, count, span, size = q.shape
    nz = mine.shape[0]
    rows = pl.BlockSpec((ny, 1, span, size), lambda i, *_: (0, i, 0, 0))
    keys = pl.BlockSpec((nz, ny, 1, span, size), lambda i, *_: (0, 0, i, 0, 0))

    def whole(value):
        return pl.BlockSpec(value.shape, lambda i, *_: (0,) * value.ndim)

    kinds = {"rows": (rows, q.shape), "keys": (keys, mine.shape)}
    return pl.pallas_call(
        kernel,
        grid_spec=pltpu.PrefetchScalarGridSpec(
            num_scalar_prefetch=2,
            grid=(count,),
            in_specs=[rows, keys, keys, whole(query_pos), whole(key_pos)]
            + [rows if value.shape == q.shape else whole(value) for value in extra],
            out_specs=[kinds[kind][0] for kind, _ in outs],
        ),
        out_shape=[jax.ShapeDtypeStruct(kinds[kind][1], dtype) for kind, dtype in outs],
        compiler_params=pltpu.CompilerParams(vmem_limit_bytes=48 * 2**20),
        cost_estimate=pl.CostEstimate(flops=1, bytes_accessed=1, transcendentals=0),
        name=name,
    )(core, lengths, q, mine, other, query_pos, key_pos, *extra)


def feed_back_kernel(dyb_ref, weight_ref, gate_ref, up_ref, out_ref):
    dm = mm(dyb_ref[...], weight_ref[...])
    gate, upward = gate_ref[...], up_ref[...]
    sig = jax.nn.sigmoid(gate)
    part = gate.shape[1]
    out_ref[:, :part] = (dm * upward * sig * (1.0 + gate * (1.0 - sig))).astype(out_ref.dtype)
    out_ref[:, part:] = (dm * gate * sig).astype(out_ref.dtype)


def feed_back(dyb, weight, both, lines=256):
    count, part = both.shape[0], both.shape[1] // 2

    def rows(width, column=0):
        return pl.BlockSpec((lines, width), lambda i: (i, column))

    return pl.pallas_call(
        feed_back_kernel,
        grid=(count // lines,),
        in_specs=[rows(dyb.shape[1]), pl.BlockSpec(weight.shape, lambda i: (0, 0)), rows(part), rows(part, 1)],
        out_specs=rows(2 * part),
        out_shape=jax.ShapeDtypeStruct((count, 2 * part), jnp.bfloat16),
        compiler_params=pltpu.CompilerParams(vmem_limit_bytes=48 * 2**20),
        cost_estimate=pl.CostEstimate(flops=1, bytes_accessed=1, transcendentals=0),
        name="feed_back",
    )(dyb, weight, both, both)


def attention_part(step, grad_ref):
    column = jnp.where(step < 2, 0, jnp.where(step < 4, 1, 2))
    parts = []
    for head in range(4):
        member = jnp.where((step == 2) | (step == 3), 2 * head + step - 2, 4 * (step % 2) + head)
        parts.append(grad_ref[member, :, pl.ds(pl.multiple_of(column * HEAD_SIZE, HEAD_SIZE), HEAD_SIZE)])
    return jnp.concatenate(parts, axis=1)


def feed_part(step, gate_up_ref, down_ref):
    size = down_ref.shape[2]
    both = gate_up_ref[step % 8, :, pl.ds(pl.multiple_of(jnp.minimum(step // 8, 1) * size, size), size)]
    return jnp.where(step < 16, both, down_ref[step % 8])


def close_reciprocal(value):
    guess = pltpu.reciprocal(value, approx=True)
    return guess * (2.0 - value * guess)


def update_kernel(part, lines_ref, weight_ref, mean_ref, square_ref, *refs):
    grads, (new_ref, new_mean_ref, new_square_ref, copy_ref, factor_ref) = refs[:-5], refs[-5:]

    @pl.when(pl.program_id(0) == 0)
    def _():
        gains, squares = lines_ref[:-8], lines_ref[-8:]
        total = jnp.sum(gains * gains, keepdims=True) + jnp.max(squares, keepdims=True)
        factor_ref[...] = clip_norm / jnp.sqrt(total)

    gradient = part(pl.program_id(0), *grads).astype(jnp.float32) * factor_ref[...]
    new, mean, square = adamw(
        weight_ref[...], gradient, mean_ref[...], square_ref[...], matrix_rate, weight_decay, close_reciprocal
    )
    new_ref[...] = new
    new_mean_ref[...] = mean
    new_square_ref[...] = square
    copy_ref[...] = new.astype(copy_ref.dtype)


def update(part, lines, weight, mean, square, grads, size=1024):
    rows, width = weight.shape
    block = pl.BlockSpec((rows, size), lambda i: (0, i))
    f32 = jnp.float32
    return pl.pallas_call(
        functools.partial(update_kernel, part),
        grid=(width // size,),
        in_specs=[pl.BlockSpec(lines.shape, lambda i: (0, 0)), block, block, block]
        + [pl.BlockSpec(grad.shape, lambda i: (0, 0, 0)) for grad in grads],
        out_specs=[block] * 4,
        out_shape=[jax.ShapeDtypeStruct(weight.shape, dtype) for dtype in (f32, f32, f32, jnp.bfloat16)],
        scratch_shapes=[pltpu.VMEM((1, 1), f32)],
        compiler_params=pltpu.CompilerParams(vmem_limit_bytes=48 * 2**20),
        name="update",
    )(lines, weight, mean, square, *grads)


def is_square():
    return lax.axis_size("y") == 2 and lax.axis_size("x") == 2


def swap(blocks):
    return lax.all_to_all(blocks, TEAM, split_axis=0, concat_axis=0, tiled=True)


def over_planes(blocks):
    return lax.all_gather(blocks.reshape(-1, blocks.shape[-1]), "z", axis=0, tiled=True)


def scatter_planes(term):
    return lax.psum_scatter(term, "z", scatter_dimension=0, tiled=True)


def together(*values):
    return lax.optimization_barrier(values)


def scatter_team(rows, number, after=()):
    if not is_square():
        return swap(rows.reshape(8, -1, rows.shape[-1]))
    return turn(rows, number, after)[0]


def team_gather(local, number, after=()):
    if not is_square():
        return lax.all_gather(local, TEAM, axis=0, tiled=True)
    return plane_gather(local, number, after).reshape(-1, local.shape[1])


def team_sum(lefts, rights, number, after=()):
    if is_square():
        return plane_sum(lefts, rights, number, after)
    partial = mm_nt(jnp.concatenate(lefts, axis=1), jnp.concatenate(rights, axis=1))
    return lax.psum_scatter(partial.astype(jnp.bfloat16), TEAM, scatter_dimension=0, tiled=True).astype(jnp.float32)


def local(
    tokens,
    lengths,
    norm_gains,
    attention_weight,
    feed_weight,
    cotangent,
    attention_mean,
    attention_square,
    feed_mean,
    feed_square,
    gain_mean,
    gain_square,
):
    low = jnp.bfloat16
    sequences, span, width = tokens.shape
    ny, nx, nz = lax.axis_size("y"), lax.axis_size("x"), lax.axis_size("z")
    team = ny * nx * 2
    core = lax.axis_index("c")
    rows = attention_weight.shape[0]
    q_width, kv_width = QUERY_HEADS * HEAD_SIZE, KEY_VALUE_HEADS * HEAD_SIZE
    count = sequences * span
    all_sequences = nx * 2 * sequences
    reach = ny * span
    near = nz <= 4
    ff_part = FF // team

    def columns(start, size):
        return pl.ds(pl.multiple_of(start, size), size)

    def take_attention(sources, member, c):
        source = sources[0]
        starts = (
            member * HEAD_SIZE,
            q_width + c * kv_width + (member - c) // 2 * HEAD_SIZE,
            q_width + 2 * kv_width + member * HEAD_SIZE,
        )
        return jnp.concatenate([source[:, columns(s, HEAD_SIZE)].astype(low) for s in starts], axis=1)

    def take_feed(*parts):
        return lambda sources, member, c: jnp.concatenate(
            [sources[0][:, columns(part * FF + member * ff_part, ff_part)].astype(low) for part in parts], axis=1
        )

    def spread(source, take, size, number, after=()):
        if is_square():
            blocks = plane_swap([source], [(rows, size)], [take], number, after)[0]
        else:
            blocks = swap(jnp.stack([take([source], member, member % 2) for member in range(8)]))
        return blocks, over_planes(blocks)

    attention_blocks, attention_mine = spread(attention_weight, take_attention, 3 * HEAD_SIZE, 1)
    gate_up_blocks, gate_up_weight = spread(feed_weight, take_feed(0, 1), 2 * ff_part, 2, [attention_blocks])

    team_base = lax.axis_index("z") * reach
    team_pos = team_base + jnp.arange(reach, dtype=jnp.int32)
    own_pos = team_base + lax.axis_index("y") * span + jnp.arange(span, dtype=jnp.int32)
    if near:
        key_pos = jnp.concatenate([team_pos - back * reach for back in range(nz)])
    else:
        key_pos = jnp.arange(nz * reach, dtype=jnp.int32)
    query_at, key_at = team_pos[:, None], key_pos[None, :]
    cos_table, sin_table = angle_tables(team_pos)
    cos_rows, sin_rows = (t.reshape(ny, 1, span, -1) for t in (cos_table, sin_table))
    valid = (own_pos[None, :] < lengths[:, None]).astype(jnp.float32).reshape(count, 1)
    lengths_all = lax.all_gather(lengths, ("x", "c"), axis=0, tiled=True)
    planes = jnp.arange(nz, dtype=jnp.int32)
    if near:
        planes = (lax.axis_index("z") - planes) % nz
    core_at = jnp.concatenate([jnp.reshape(core, (1,)), planes]).astype(jnp.int32)

    def heads(value):
        return value.reshape(ny, all_sequences, span, HEAD_SIZE)

    x_in = tokens.reshape(count, width).astype(jnp.float32)
    normed_one, inverse_one = rms_forward(x_in, norm_gains[0])
    outer_grad = cotangent.reshape(count, width).astype(jnp.float32) * valid
    h1 = team_gather(normed_one.astype(low), 3, [gate_up_blocks])
    attention_mine, lengths_all = together(attention_mine, lengths_all)
    query_weight = attention_mine[:, :HEAD_SIZE]
    kv_weight = attention_mine[:, HEAD_SIZE : 2 * HEAD_SIZE]
    out_weight = attention_mine[:, 2 * HEAD_SIZE :]
    kv_raw = heads(mm(h1, kv_weight))
    kv = jnp.where(core == 0, rotate(kv_raw, cos_rows, sin_rows), kv_raw).astype(low)
    q = rotate(heads(mm(h1, query_weight)), cos_rows, sin_rows).astype(low)
    dyb = team_gather(outer_grad.astype(low), 15, [kv])
    down_blocks, down_weight = spread(feed_weight, take_feed(2), ff_part, 12, [dyb])
    if near:
        earlier = [
            lax.ppermute(kv, "z", [(at, at + back) for at in range(nz - back)]) for back in range(1, nz)
        ]
        *earlier, dyb, down_blocks, q = lax.optimization_barrier((*earlier, dyb, down_blocks, q))
        kv = jnp.stack([kv, *earlier])
    else:
        kv = lax.all_gather(kv, "z", axis=0, tiled=False)
    other = lax.ppermute(kv, "c", [(0, 1), (1, 0)])
    attend = (core_at, lengths_all, q, kv, other, query_at, key_at)
    (o,) = attention_call(attention_kernel, *attend, (), [("rows", low)], "attention")
    o = o.reshape(-1, HEAD_SIZE)
    r = x_in + team_sum([o], [out_weight], 4)

    normed_two, inverse_two = rms_forward(r, norm_gains[1])
    h2 = team_gather(normed_two.astype(low), 16)
    both = mm(h2, gate_up_weight)
    gate, upward = both[:, :ff_part], both[:, ff_part:]
    sig = jax.nn.sigmoid(gate)
    m = (gate * sig * upward).astype(low)
    down_term = mm_tn(dyb, m).astype(low)
    down_rows = scatter_planes(down_term)
    down_weight, down_term = together(down_weight, down_term)
    d_both = feed_back(dyb, down_weight, both)
    gate_up_term = mm_tn(h2, d_both).astype(low)
    gate_up_rows = scatter_planes(gate_up_term)
    dh2 = team_sum([d_both], [gate_up_weight], 7, [gate_up_term, down_term])
    mid_grad, gain_two = rms_back(dh2, r, inverse_two, norm_gains[1])
    dr = outer_grad + mid_grad
    drb = team_gather(dr.astype(low), 13, [down_rows])

    do = heads(mm(drb, out_weight).astype(low))
    dq, keep, theirs = attention_call(
        attention_back_kernel,
        *attend,
        (do, cos_table, sin_table),
        [("rows", low), ("keys", jnp.float32), ("keys", low)],
        "attention_back",
    )
    dq = dq.reshape(-1, HEAD_SIZE)
    dkv = keep + lax.ppermute(theirs, "c", [(0, 1), (1, 0)]).astype(jnp.float32)
    low_terms = dkv.astype(low)
    feed_sum = team_sum([m], [down_weight], 5, [low_terms])
    down_grad = scatter_team(down_rows, 6, [low_terms])
    dkv = lax.psum_scatter(low_terms, "z", scatter_dimension=0, tiled=True)[0]
    gate_up_grad = scatter_team(gate_up_rows, 8, [feed_sum, down_grad])
    dkv, gate_up_grad = together(dkv, gate_up_grad)
    dkv = dkv.astype(jnp.float32)
    dkv = jnp.where(core == 0, rotate(dkv, cos_rows, -sin_rows), dkv).astype(low).reshape(-1, HEAD_SIZE)
    layer_output = (r + feed_sum).astype(low)
    attention_term = jnp.concatenate([mm_tn(h1, dq), mm_tn(h1, dkv), mm_tn(drb, o)], axis=1).astype(low)
    attention_rows = scatter_planes(attention_term)
    dh1 = team_sum([dq, dkv], [query_weight, kv_weight], 9, [attention_term])
    in_grad, gain_one = rms_back(dh1, x_in, inverse_one, norm_gains[0])
    input_gradient = dr + in_grad
    part_rows = (gate_up_rows, down_rows, attention_rows)
    local_squares = sum(jnp.sum(jnp.square(part.astype(jnp.float32))) for part in part_rows)
    gain_local = jnp.stack([gain_one, gain_two])
    lines = jnp.concatenate([gain_local.reshape(-1, 128), jnp.full((8, 128), local_squares)], axis=0)
    if is_square():
        attention_grad, lines = turn(attention_rows, 10, (), lines, nz)
    else:
        attention_grad, lines = scatter_team(attention_rows, 10), lax.psum(lines, ALL)
    gain_grad, squares = lines[:-8].reshape(2, width), lines[-1, 0]
    gradient_norm = jnp.sqrt(squares + jnp.sum(gain_grad * gain_grad))
    factor = clip_norm / gradient_norm
    attention_new = update(attention_part, lines, attention_weight, attention_mean, attention_square, [attention_grad])
    feed_new = update(feed_part, lines, feed_weight, feed_mean, feed_square, [gate_up_grad, down_grad])
    gains_new = adamw(norm_gains, gain_grad * factor, gain_mean, gain_square, gain_rate, 0.0)
    return (
        layer_output.reshape(sequences, span, width),
        input_gradient.reshape(sequences, span, width),
        gradient_norm,
        *attention_new,
        *feed_new,
        *gains_new,
    )


def solution(mesh):
    ctx, fsdp = mesh.shape["ctx"], mesh.shape["fsdp"]
    inner = QUERY_HEADS // fsdp
    fine = Mesh(mesh.devices.reshape(ctx // inner, inner, fsdp // 2, 2), ALL)
    act = P(("x", "c"), ("z", "y"), None)
    matrix = P(ALL, None)
    return jax.shard_map(
        local,
        mesh=fine,
        in_specs=(act, P(("x", "c")), P(), matrix, matrix, act, matrix, matrix, matrix, matrix, P(), P()),
        out_specs=(act, act, P(), matrix, matrix, matrix, matrix, matrix, matrix, matrix, matrix, P(), P(), P()),
        check_vma=False,
    )
```

```python
import functools

import jax
import jax.numpy as jnp
from jax import lax
from jax.experimental import pallas as pl
from jax.experimental.pallas import tpu as pltpu
from jax.sharding import Mesh, PartitionSpec as P

QUERY_HEADS = 8
KEY_VALUE_HEADS = 4
HEAD_SIZE = 256
FF = 8192
STEP = 10

norm_eps = 1e-06
rope_base = 1000042.0
masked_value = -1e30
clip_norm = 1.0
beta_one = 0.9
beta_two = 0.95
adam_eps = 1e-08
matrix_rate = 0.03
gain_rate = 0.4
weight_decay = 0.1

TEAM = ("y", "x", "c")
ALL = ("z", "y", "x", "c")


MESH = pl.DeviceIdType.MESH
VMEM = pl.BlockSpec(memory_space=pltpu.VMEM)
HBM = pl.BlockSpec(memory_space=pl.ANY)


def place():
    y, x, c = lax.axis_index("y"), lax.axis_index("x"), lax.axis_index("c")
    return y, x, c, lambda yy, xx, cc: (yy * 2 + xx) * 2 + cc


def greet(others):
    barrier = pltpu.get_barrier_semaphore()
    for other in others:
        pl.semaphore_signal(barrier, inc=1, device_id=other, device_id_type=MESH)
    pl.semaphore_wait(barrier, len(others))


def gather_kernel(src, *refs):
    out, send, recv, own = refs[-4:]
    y, x, c, index = place()
    to_x, to_y, to_s = {"x": 1 - x}, {"y": 1 - y}, {"c": 1 - c}
    me, at_x, at_y, at_d = index(y, x, c), index(y, 1 - x, c), index(1 - y, x, c), index(1 - y, 1 - x, c)
    half = src.shape[0] // 2
    rows = (pl.ds(0, half), pl.ds(half, half))
    local = pltpu.make_async_copy(src, out.at[me], own)
    local.start()
    greet((to_x, to_y, to_s))

    def hop(slot, block, part, where, first=False):
        piece = out.at[block, rows[part]]
        return pltpu.make_async_remote_copy(
            src_ref=src.at[rows[part]] if first else piece,
            dst_ref=piece,
            send_sem=send.at[slot],
            recv_sem=recv.at[slot],
            device_id=where,
            device_id_type=MESH,
        )

    x0, x1 = hop(0, me, 0, to_x, True), hop(1, me, 1, to_x, True)
    y1, y0 = hop(2, me, 1, to_y, True), hop(3, me, 0, to_y, True)
    s0, s1 = hop(4, me, 0, to_s, True), hop(5, me, 1, to_s, True)
    for copy in (x0, y1, x1, y0, s0, s1):
        copy.start()
    x0.wait_recv()
    d0 = hop(6, at_x, 0, to_y)
    d0.start()
    y1.wait_recv()
    d1 = hop(7, at_y, 1, to_x)
    d1.start()
    sx0, sy1 = hop(8, at_x, 0, to_s), hop(9, at_y, 1, to_s)
    sx0.start()
    sy1.start()
    x1.wait_recv()
    sx1 = hop(10, at_x, 1, to_s)
    sx1.start()
    y0.wait_recv()
    sy0 = hop(11, at_y, 0, to_s)
    sy0.start()
    d0.wait_recv()
    sd0 = hop(12, at_d, 0, to_s)
    sd0.start()
    d1.wait_recv()
    sd1 = hop(13, at_d, 1, to_s)
    sd1.start()
    for copy in (s0, s1, sx0, sy1, sx1, sy0, sd0, sd1):
        copy.wait_recv()
    for copy in (x0, x1, y0, y1, s0, s1, d0, d1, sx0, sy1, sx1, sy0, sd0, sd1):
        copy.wait_send()
    local.wait()


def plane_gather(value, number, after=()):
    return pl.pallas_call(
        gather_kernel,
        out_shape=jax.ShapeDtypeStruct((8, *value.shape), value.dtype),
        in_specs=[HBM] * (1 + len(after)),
        out_specs=HBM,
        scratch_shapes=[
            pltpu.SemaphoreType.DMA((14,)),
            pltpu.SemaphoreType.DMA((14,)),
            pltpu.SemaphoreType.DMA,
        ],
        compiler_params=pltpu.CompilerParams(collective_id=number, has_side_effects=True),
        cost_estimate=pl.CostEstimate(flops=1, bytes_accessed=1, transcendentals=0),
        name="plane_gather",
    )(value, *after)


def sum_kernel(lefts, terms, tile, *refs):
    a_refs, w_refs = refs[:lefts], refs[lefts : lefts + len(terms)]
    out, s_send, s_recv, d_send, d_recv, x_send, x_recv, y_send, y_recv, x_acc, y_acc, send, recv = refs[-13:]
    y, x, c, index = place()
    to_x, to_y, to_s = {"x": 1 - x}, {"y": 1 - y}, {"c": 1 - c}
    rows, width = out.shape
    half = rows // 2
    parts = (pl.ds(0, half), pl.ds(half, half))
    f32, low = jnp.float32, jnp.bfloat16

    def product(block, put):
        lines = pl.ds(pl.multiple_of(block * rows, rows), rows)

        @pl.loop(0, width // tile)
        def _(step):
            cols = pl.ds(pl.multiple_of(step * tile, tile), tile)
            total = None
            for (left, start), w_ref in zip(terms, w_refs):
                term = mm_nt(a_refs[left][lines, start : start + w_ref.shape[1]], w_ref[cols, :])
                total = term if total is None else total + term
            put(cols, total)

    def hop(slot, src, dst, where):
        copy = pltpu.make_async_remote_copy(
            src_ref=src, dst_ref=dst, send_sem=send.at[slot], recv_sem=recv.at[slot],
            device_id=where, device_id_type=MESH,
        )
        return copy

    def to_sibling(slot, yy, xx):
        def put(cols, total):
            s_send[slot, :, cols] = total.astype(low)

        product(index(yy, xx, 1 - c), put)
        copy = hop(slot, s_send.at[slot], s_recv.at[slot], to_s)
        copy.start()
        return copy

    def with_sibling(slot, yy, xx, keep):
        def put(cols, total):
            keep[:, cols] = (total + s_recv[slot, :, cols].astype(f32)).astype(keep.dtype)

        product(index(yy, xx, c), put)

    greet((to_x, to_y, to_s))
    s0 = to_sibling(0, 1 - y, 1 - x)
    s1 = to_sibling(1, y, 1 - x)
    s0.wait_recv()
    with_sibling(0, 1 - y, 1 - x, d_send)
    d0 = hop(4, d_send.at[parts[0]], d_recv.at[parts[0]], to_x)
    d1 = hop(5, d_send.at[parts[1]], d_recv.at[parts[1]], to_y)
    d0.start()
    d1.start()
    s1.wait_recv()
    with_sibling(1, y, 1 - x, x_acc)
    x_send[parts[0]] = x_acc[parts[0]].astype(low)
    x0 = hop(6, x_send.at[parts[0]], x_recv.at[parts[0]], to_x)
    x0.start()
    s2 = to_sibling(2, 1 - y, x)
    s2.wait_recv()
    with_sibling(2, 1 - y, x, y_acc)
    y_send[parts[1]] = y_acc[parts[1]].astype(low)
    y1 = hop(7, y_send.at[parts[1]], y_recv.at[parts[1]], to_y)
    y1.start()
    s3 = to_sibling(3, y, x)
    d1.wait_recv()
    x_send[parts[1]] = (x_acc[parts[1]] + d_recv[parts[1]].astype(f32)).astype(low)
    x1 = hop(8, x_send.at[parts[1]], x_recv.at[parts[1]], to_x)
    x1.start()
    d0.wait_recv()
    y_send[parts[0]] = (y_acc[parts[0]] + d_recv[parts[0]].astype(f32)).astype(low)
    y0 = hop(9, y_send.at[parts[0]], y_recv.at[parts[0]], to_y)
    y0.start()
    s3.wait_recv()
    with_sibling(3, y, x, out)
    x0.wait_recv()
    y1.wait_recv()
    x1.wait_recv()
    y0.wait_recv()
    out[...] += x_recv[...].astype(f32) + y_recv[...].astype(f32)
    for copy in (s0, s1, s2, s3, d0, d1, x0, x1, y0, y1):
        copy.wait_send()


def plane_sum(lefts, rights, number, after=(), tile=512):
    ends = [(left, start) for left, a in enumerate(lefts) for start in range(0, a.shape[1], rights[0].shape[1])]
    terms = tuple(ends[: len(rights)])
    rows, width = lefts[0].shape[0] // 8, rights[0].shape[0]
    block = (rows, width)
    low, f32 = jnp.bfloat16, jnp.float32
    return pl.pallas_call(
        functools.partial(sum_kernel, len(lefts), terms, min(tile, width)),
        out_shape=jax.ShapeDtypeStruct(block, f32),
        in_specs=[VMEM] * (len(lefts) + len(rights)) + [HBM] * len(after),
        out_specs=VMEM,
        scratch_shapes=[
            pltpu.VMEM((4, *block), low),
            pltpu.VMEM((4, *block), low),
            *[pltpu.VMEM(block, low)] * 6,
            pltpu.VMEM(block, f32),
            pltpu.VMEM(block, f32),
            pltpu.SemaphoreType.DMA((10,)),
            pltpu.SemaphoreType.DMA((10,)),
        ],
        compiler_params=pltpu.CompilerParams(
            collective_id=number, has_side_effects=True, vmem_limit_bytes=48 * 2**20
        ),
        cost_estimate=pl.CostEstimate(flops=1, bytes_accessed=1, transcendentals=0),
        name="plane_sum",
    )(*lefts, *rights, *after)


def swap_kernel(pieces, takes, *refs):
    count = len(pieces)
    sources, (send, recv, own) = refs[: -2 * count - 3], refs[-3:]
    outs, holds = refs[-2 * count - 3 : -count - 3], refs[-count - 3 : -3]
    y, x, c, index = place()
    me = index(y, x, c)
    flips = [(fy, fx, fc) for fy, fx in ((1, 1), (0, 1), (1, 0), (0, 0)) for fc in (0, 1)]
    flips = [flip for flip in flips if flip != (0, 0, 0)]

    def there(flip):
        return tuple(1 - at if f else at for at, f in zip((y, x, c), flip))

    greet([dict(zip(("y", "x", "c"), there(flip))) for flip in flips])
    copies = []
    for piece in range(count):
        for number, flip in enumerate(flips):
            yy, xx, cc = there(flip)
            member = index(yy, xx, cc)
            holds[piece][number] = takes[piece](sources, member, cc)
            copy = pltpu.make_async_remote_copy(
                src_ref=holds[piece].at[number],
                dst_ref=outs[piece].at[me],
                send_sem=send.at[piece * 7 + number],
                recv_sem=recv.at[piece * 7 + number],
                device_id={"y": yy, "x": xx, "c": cc},
                device_id_type=MESH,
            )
            copy.start()
            copies.append(copy)
        holds[piece][7] = takes[piece](sources, me, c)
        keep = pltpu.make_async_copy(holds[piece].at[7], outs[piece].at[me], own.at[piece])
        keep.start()
        copies.append(keep)
    for copy in copies:
        copy.wait()


def plane_swap(sources, shapes, takes, number, after=()):
    low = jnp.bfloat16
    count = len(shapes)
    return pl.pallas_call(
        functools.partial(swap_kernel, shapes, takes),
        out_shape=[jax.ShapeDtypeStruct((8, *shape), low) for shape in shapes],
        in_specs=[VMEM] * len(sources) + [HBM] * len(after),
        out_specs=[HBM] * count,
        scratch_shapes=[
            *[pltpu.VMEM((8, *shape), low) for shape in shapes],
            pltpu.SemaphoreType.DMA((7 * count,)),
            pltpu.SemaphoreType.DMA((7 * count,)),
            pltpu.SemaphoreType.DMA((count,)),
        ],
        compiler_params=pltpu.CompilerParams(
            collective_id=number, has_side_effects=True, vmem_limit_bytes=48 * 2**20
        ),
        cost_estimate=pl.CostEstimate(flops=1, bytes_accessed=1, transcendentals=0),
        name="plane_swap",
    )(*sources, *after)


def team_of(y, x, c):
    flips = [(fy, fx, fc) for fy, fx in ((1, 1), (0, 1), (1, 0), (0, 0)) for fc in (0, 1)]
    return [
        tuple(1 - at if f else at for at, f in zip((y, x, c), flip)) for flip in flips if flip != (0, 0, 0)
    ]


def turn_kernel(planes, src, *refs):
    y, x, c, index = place()
    me = index(y, x, c)
    others = team_of(y, x, c)
    ids = [dict(zip(("y", "x", "c"), other)) for other in others]
    if planes:
        lines, out, total, near, far, held, send, recv, own, send_lines, recv_lines = refs[:1] + refs[-10:]
        z = lax.axis_index("z")
        column = [{"z": lax.rem(z + step, planes)} for step in range(1, planes)]
        fetch = pltpu.make_async_copy(src, held, own)
        fetch.start()
        fetch.wait()
        near[me] = lines[...]
        squares = jnp.zeros((8, held.shape[1]), jnp.float32)
        for start in range(0, held.shape[0], 64):
            part = held[start : start + 64].astype(jnp.float32)
            squares += jnp.sum(jnp.square(part).reshape(8, 8, -1), axis=0)
        near[me, 2:3] += jnp.sum(squares, keepdims=True)
    else:
        out, send, recv, own = refs[-4:]
        column = []
    greet(ids + column)
    count = src.shape[0] // 8

    def rows(member):
        return src.at[pl.ds(pl.multiple_of(member * count, count), count)]

    def spread(buffer, at, where, base):
        copies = [
            pltpu.make_async_remote_copy(
                src_ref=buffer.at[at],
                dst_ref=buffer.at[at],
                send_sem=send_lines.at[base + number],
                recv_sem=recv_lines.at[base + number],
                device_id=other,
                device_id_type=MESH,
            )
            for number, other in enumerate(where)
        ]
        for copy in copies:
            copy.start()
        return copies

    small = spread(near, me, ids, 0) if planes else []
    copies = [
        pltpu.make_async_remote_copy(
            src_ref=rows(index(*other)),
            dst_ref=out.at[me],
            send_sem=send.at[number],
            recv_sem=recv.at[number],
            device_id=where,
            device_id_type=MESH,
        )
        for number, (other, where) in enumerate(zip(others, ids))
    ]
    copies.append(pltpu.make_async_copy(rows(me), out.at[me], own))
    for copy in copies:
        copy.start()
    if planes:
        for copy in small:
            copy.wait()
        far[z] = jnp.sum(near[...], axis=0)
        for copy in spread(far, z, column, 7):
            copy.wait()
        total[...] = jnp.sum(far[...], axis=0)
    for copy in copies:
        copy.wait()


def turn(rows, number, after=(), lines=None, planes=0):
    block = (rows.shape[0] // 8, rows.shape[1])
    dma = pltpu.SemaphoreType.DMA
    out_shape, out_specs = [jax.ShapeDtypeStruct((8, *block), rows.dtype)], [HBM]
    in_specs, scratch = [HBM], [dma((7,)), dma((7,)), dma]
    operands = [rows]
    if planes:
        operands.append(lines)
        in_specs.append(VMEM)
        out_shape.append(jax.ShapeDtypeStruct(lines.shape, lines.dtype))
        out_specs.append(VMEM)
        buffers = [pltpu.VMEM((size, *lines.shape), lines.dtype) for size in (8, planes)]
        scratch = buffers + [pltpu.VMEM(rows.shape, rows.dtype)] + scratch + [dma((6 + planes,)), dma((6 + planes,))]
    return pl.pallas_call(
        functools.partial(turn_kernel, planes),
        out_shape=out_shape,
        in_specs=in_specs + [HBM] * len(after),
        out_specs=out_specs,
        scratch_shapes=scratch,
        compiler_params=pltpu.CompilerParams(
            collective_id=number, has_side_effects=True, vmem_limit_bytes=16 * 2**20
        ),
        cost_estimate=pl.CostEstimate(flops=1, bytes_accessed=1, transcendentals=0),
        name="turn",
    )(*operands, *after)


def dot(left, right, contract):
    return lax.dot_general(left, right, (contract, ((), ())), preferred_element_type=jnp.float32)


def mm(left, right):
    return dot(left, right, ((1,), (0,)))


def mm_nt(left, right):
    return dot(left, right, ((1,), (1,)))


def mm_tn(left, right):
    return dot(left, right, ((0,), (0,)))


def bmm(pattern, left, right):
    return jnp.einsum(pattern, left, right, preferred_element_type=jnp.float32)


def angle_tables(positions):
    half_dim = HEAD_SIZE // 2
    frequency = rope_base ** (-(jnp.arange(half_dim).astype(jnp.float32) * 2.0) / HEAD_SIZE)
    phases = positions.astype(jnp.float32)[:, None] * frequency[None, :]
    return (jnp.cos(phases), jnp.sin(phases))


def rotate(value, cos_table, sin_table):
    half = value.shape[-1] // 2
    a, b = value[..., :half], value[..., half:]
    return jnp.concatenate([a * cos_table - b * sin_table, b * cos_table + a * sin_table], axis=-1)


def rms_forward(value, gain_row):
    inverse = lax.rsqrt(jnp.mean(value * value, axis=-1, keepdims=True) + norm_eps)
    return (value * inverse * gain_row, inverse)


def rms_back(grad_out, value, inverse, gain_row):
    scaled = grad_out * gain_row
    grad_in = inverse * (
        scaled - value * inverse * inverse * jnp.mean(scaled * value, axis=-1, keepdims=True)
    )
    return (grad_in, jnp.sum(grad_out * value * inverse, axis=0))


def adamw(weight, gradient, moment_one, moment_two, step_rate, decay_rate, invert=jnp.reciprocal):
    mean_new = beta_one * moment_one + (1.0 - beta_one) * gradient
    square_new = beta_two * moment_two + (1.0 - beta_two) * gradient * gradient
    below = jnp.sqrt(square_new * (1.0 / (1.0 - beta_two**STEP))) + adam_eps
    direction = mean_new * (1.0 / (1.0 - beta_one**STEP)) * invert(below)
    return (weight - step_rate * (direction + decay_rate * weight), mean_new, square_new)


def attention_parts(core, length, q_ref, mine_ref, other_ref, query_ref, key_ref):
    mine, other = mine_ref[...].reshape(-1, HEAD_SIZE), other_ref[...].reshape(-1, HEAD_SIZE)
    first = core == 0
    k, v = jnp.where(first, mine, other), jnp.where(first, other, mine)
    q = q_ref[...].reshape(-1, HEAD_SIZE)
    at, key_at = query_ref[...], key_ref[...]
    allowed = (key_at <= at) & (key_at < length) & (key_at >= 0)
    scores = jnp.where(allowed, mm_nt(q, k) * HEAD_SIZE ** (-0.5), masked_value)
    exponent = jnp.exp(scores - jnp.max(scores, axis=-1, keepdims=True))
    return q, k, v, exponent / jnp.sum(exponent, axis=-1, keepdims=True)


def attention_kernel(core_ref, length_ref, q_ref, mine_ref, other_ref, query_ref, key_ref, out_ref):
    length = length_ref[pl.program_id(0)]
    _, _, v, soft = attention_parts(core_ref[0], length, q_ref, mine_ref, other_ref, query_ref, key_ref)
    out_ref[...] = mm(soft.astype(jnp.bfloat16), v).astype(jnp.bfloat16).reshape(out_ref.shape)


def attention_back_kernel(
    core_ref, length_ref, q_ref, mine_ref, other_ref, query_ref, key_ref, do_ref, cos_ref, sin_ref,
    dq_ref, keep_ref, send_ref,
):
    low = jnp.bfloat16
    core = core_ref[0]
    length = length_ref[pl.program_id(0)]
    q, k, v, soft = attention_parts(core, length, q_ref, mine_ref, other_ref, query_ref, key_ref)
    do = do_ref[...].reshape(-1, HEAD_SIZE)
    dp = mm_nt(do, v)
    delta = jnp.sum(soft * dp, axis=-1, keepdims=True)
    ds = (soft * (dp - delta) * HEAD_SIZE ** (-0.5)).astype(low)
    dq = mm(ds, k)
    cos_table, sin_table = cos_ref[...], sin_ref[...]
    half = HEAD_SIZE // 2
    a, b = dq[:, :half], dq[:, half:]
    turned = jnp.concatenate([a * cos_table + b * sin_table, b * cos_table - a * sin_table], axis=-1)
    dq_ref[...] = turned.astype(low).reshape(dq_ref.shape)
    dk, dv = mm_tn(ds, q), mm_tn(soft.astype(low), do)
    first = core == 0
    keep, send = (t.reshape(keep_ref.shape) for t in (jnp.where(first, dk, dv), jnp.where(first, dv, dk)))
    for block in range(keep_ref.shape[0]):
        at = core_ref[1 + block]
        keep_ref[at] = keep[block]
        send_ref[at] = send[block].astype(low)


def attention_call(kernel, core, lengths, q, mine, other, query_pos, key_pos, extra, outs, name):
    ny, count, span, size = q.shape
    nz = mine.shape[0]
    rows = pl.BlockSpec((ny, 1, span, size), lambda i, *_: (0, i, 0, 0))
    keys = pl.BlockSpec((nz, ny, 1, span, size), lambda i, *_: (0, 0, i, 0, 0))

    def whole(value):
        return pl.BlockSpec(value.shape, lambda i, *_: (0,) * value.ndim)

    kinds = {"rows": (rows, q.shape), "keys": (keys, mine.shape)}
    return pl.pallas_call(
        kernel,
        grid_spec=pltpu.PrefetchScalarGridSpec(
            num_scalar_prefetch=2,
            grid=(count,),
            in_specs=[rows, keys, keys, whole(query_pos), whole(key_pos)]
            + [rows if value.shape == q.shape else whole(value) for value in extra],
            out_specs=[kinds[kind][0] for kind, _ in outs],
        ),
        out_shape=[jax.ShapeDtypeStruct(kinds[kind][1], dtype) for kind, dtype in outs],
        compiler_params=pltpu.CompilerParams(vmem_limit_bytes=48 * 2**20),
        cost_estimate=pl.CostEstimate(flops=1, bytes_accessed=1, transcendentals=0),
        name=name,
    )(core, lengths, q, mine, other, query_pos, key_pos, *extra)


def feed_back_kernel(dyb_ref, weight_ref, gate_ref, up_ref, out_ref):
    dm = mm(dyb_ref[...], weight_ref[...])
    gate, upward = gate_ref[...], up_ref[...]
    sig = jax.nn.sigmoid(gate)
    part = gate.shape[1]
    out_ref[:, :part] = (dm * upward * sig * (1.0 + gate * (1.0 - sig))).astype(out_ref.dtype)
    out_ref[:, part:] = (dm * gate * sig).astype(out_ref.dtype)


def feed_back(dyb, weight, both, lines=256):
    count, part = both.shape[0], both.shape[1] // 2

    def rows(width, column=0):
        return pl.BlockSpec((lines, width), lambda i: (i, column))

    return pl.pallas_call(
        feed_back_kernel,
        grid=(count // lines,),
        in_specs=[rows(dyb.shape[1]), pl.BlockSpec(weight.shape, lambda i: (0, 0)), rows(part), rows(part, 1)],
        out_specs=rows(2 * part),
        out_shape=jax.ShapeDtypeStruct((count, 2 * part), jnp.bfloat16),
        compiler_params=pltpu.CompilerParams(vmem_limit_bytes=48 * 2**20),
        cost_estimate=pl.CostEstimate(flops=1, bytes_accessed=1, transcendentals=0),
        name="feed_back",
    )(dyb, weight, both, both)


def attention_part(step, grad_ref):
    parts = []
    for head in range(8):
        member = jnp.where(step == 1, 2 * (head % 4) + head // 4, head)
        parts.append(grad_ref[member, :, pl.ds(pl.multiple_of(step * HEAD_SIZE, HEAD_SIZE), HEAD_SIZE)])
    return jnp.concatenate(parts, axis=1)


def feed_part(step, gate_up_ref, down_ref):
    size = down_ref.shape[2]
    at = pl.ds(pl.multiple_of(jnp.minimum(step // 2, 1) * size, size), size)
    parts = []
    for number in range(4):
        member = 4 * (step % 2) + number
        parts.append(jnp.where(step < 4, gate_up_ref[member, :, at], down_ref[member]))
    return jnp.concatenate(parts, axis=1)


def close_reciprocal(value):
    guess = pltpu.reciprocal(value, approx=True)
    return guess * (2.0 - value * guess)


def norm_of(lines_ref):
    gains = lines_ref[0:2]
    return jnp.sqrt(jnp.sum(gains * gains, keepdims=True) + lines_ref[2:3, 0:1])


def update_gains_kernel(lines_ref, weight_ref, mean_ref, square_ref, new_ref, new_mean_ref, new_square_ref, norm_ref):
    norm = norm_of(lines_ref)
    norm_ref[...] = norm
    new_ref[...], new_mean_ref[...], new_square_ref[...] = adamw(
        weight_ref[...], lines_ref[0:2] * (clip_norm / norm), mean_ref[...], square_ref[...], gain_rate, 0.0
    )


def update_gains(lines, weight, mean, square):
    f32 = jnp.float32
    return pl.pallas_call(
        update_gains_kernel,
        in_specs=[VMEM] * 4,
        out_specs=[VMEM] * 4,
        out_shape=[jax.ShapeDtypeStruct(weight.shape, f32)] * 3 + [jax.ShapeDtypeStruct((1, 1), f32)],
        name="update_gains",
    )(lines, weight, mean, square)


def update_kernel(part, lines_ref, weight_ref, mean_ref, square_ref, *refs):
    grads, (new_ref, new_mean_ref, new_square_ref, copy_ref, factor_ref) = refs[:-5], refs[-5:]

    @pl.when(pl.program_id(0) == 0)
    def _():
        factor_ref[...] = clip_norm / norm_of(lines_ref)

    gradient = part(pl.program_id(0), *grads).astype(jnp.float32) * factor_ref[...]
    new, mean, square = adamw(
        weight_ref[...], gradient, mean_ref[...], square_ref[...], matrix_rate, weight_decay, close_reciprocal
    )
    new_ref[...] = new
    new_mean_ref[...] = mean
    new_square_ref[...] = square
    copy_ref[...] = new.astype(copy_ref.dtype)


def update(part, lines, weight, mean, square, grads):
    size = 2048 if part is attention_part else 4096
    rows, width = weight.shape
    block = pl.BlockSpec((rows, size), lambda i: (0, i))
    f32 = jnp.float32
    return pl.pallas_call(
        functools.partial(update_kernel, part),
        grid=(width // size,),
        in_specs=[pl.BlockSpec(lines.shape, lambda i: (0, 0)), block, block, block]
        + [pl.BlockSpec(grad.shape, lambda i: (0, 0, 0)) for grad in grads],
        out_specs=[block] * 4,
        out_shape=[jax.ShapeDtypeStruct(weight.shape, dtype) for dtype in (f32, f32, f32, jnp.bfloat16)],
        scratch_shapes=[pltpu.VMEM((1, 1), f32)],
        compiler_params=pltpu.CompilerParams(vmem_limit_bytes=48 * 2**20),
        name="update",
    )(lines, weight, mean, square, *grads)


def is_square():
    return lax.axis_size("y") == 2 and lax.axis_size("x") == 2


def swap(blocks):
    return lax.all_to_all(blocks, TEAM, split_axis=0, concat_axis=0, tiled=True)


def over_planes(blocks):
    return lax.all_gather(blocks.reshape(-1, blocks.shape[-1]), "z", axis=0, tiled=True)


def scatter_planes(term):
    return lax.psum_scatter(term, "z", scatter_dimension=0, tiled=True)


def together(*values):
    return lax.optimization_barrier(values)


def scatter_team(rows, number, after=()):
    if not is_square():
        return swap(rows.reshape(8, -1, rows.shape[-1]))
    return turn(rows, number, after)[0]


def team_gather(local, number, after=()):
    if not is_square():
        return lax.all_gather(local, TEAM, axis=0, tiled=True)
    return plane_gather(local, number, after).reshape(-1, local.shape[1])


def team_sum(lefts, rights, number, after=()):
    if is_square():
        return plane_sum(lefts, rights, number, after)
    partial = mm_nt(jnp.concatenate(lefts, axis=1), jnp.concatenate(rights, axis=1))
    return lax.psum_scatter(partial.astype(jnp.bfloat16), TEAM, scatter_dimension=0, tiled=True).astype(jnp.float32)


def local(
    tokens,
    lengths,
    norm_gains,
    attention_weight,
    feed_weight,
    cotangent,
    attention_mean,
    attention_square,
    feed_mean,
    feed_square,
    gain_mean,
    gain_square,
):
    low = jnp.bfloat16
    sequences, span, width = tokens.shape
    ny, nx, nz = lax.axis_size("y"), lax.axis_size("x"), lax.axis_size("z")
    team = ny * nx * 2
    core = lax.axis_index("c")
    rows = attention_weight.shape[0]
    q_width, kv_width = QUERY_HEADS * HEAD_SIZE, KEY_VALUE_HEADS * HEAD_SIZE
    count = sequences * span
    all_sequences = nx * 2 * sequences
    reach = ny * span
    near = nz <= 4
    ff_part = FF // team

    def columns(start, size):
        return pl.ds(pl.multiple_of(start, size), size)

    def take_attention(sources, member, c):
        source = sources[0]
        starts = (
            member * HEAD_SIZE,
            q_width + c * kv_width + (member - c) // 2 * HEAD_SIZE,
            q_width + 2 * kv_width + member * HEAD_SIZE,
        )
        return jnp.concatenate([source[:, columns(s, HEAD_SIZE)].astype(low) for s in starts], axis=1)

    def take_feed(*parts):
        return lambda sources, member, c: jnp.concatenate(
            [sources[0][:, columns(part * FF + member * ff_part, ff_part)].astype(low) for part in parts], axis=1
        )

    def spread(source, take, size, number, after=()):
        if is_square():
            blocks = plane_swap([source], [(rows, size)], [take], number, after)[0]
        else:
            blocks = swap(jnp.stack([take([source], member, member % 2) for member in range(8)]))
        return blocks, over_planes(blocks)

    attention_blocks, attention_mine = spread(attention_weight, take_attention, 3 * HEAD_SIZE, 1)
    gate_up_blocks, gate_up_weight = spread(feed_weight, take_feed(0, 1), 2 * ff_part, 2, [attention_blocks])

    team_base = lax.axis_index("z") * reach
    team_pos = team_base + jnp.arange(reach, dtype=jnp.int32)
    own_pos = team_base + lax.axis_index("y") * span + jnp.arange(span, dtype=jnp.int32)
    if near:
        key_pos = jnp.concatenate([team_pos - back * reach for back in range(nz)])
    else:
        key_pos = jnp.arange(nz * reach, dtype=jnp.int32)
    query_at, key_at = team_pos[:, None], key_pos[None, :]
    cos_table, sin_table = angle_tables(team_pos)
    cos_rows, sin_rows = (t.reshape(ny, 1, span, -1) for t in (cos_table, sin_table))
    valid = (own_pos[None, :] < lengths[:, None]).astype(jnp.float32).reshape(count, 1)
    lengths_all = lax.all_gather(lengths, ("x", "c"), axis=0, tiled=True)
    planes = jnp.arange(nz, dtype=jnp.int32)
    if near:
        planes = (lax.axis_index("z") - planes) % nz
    core_at = jnp.concatenate([jnp.reshape(core, (1,)), planes]).astype(jnp.int32)

    def heads(value):
        return value.reshape(ny, all_sequences, span, HEAD_SIZE)

    x_in = tokens.reshape(count, width).astype(jnp.float32)
    normed_one, inverse_one = rms_forward(x_in, norm_gains[0])
    outer_grad = cotangent.reshape(count, width).astype(jnp.float32) * valid
    h1 = team_gather(normed_one.astype(low), 3, [gate_up_blocks])
    attention_mine, lengths_all = together(attention_mine, lengths_all)
    query_weight = attention_mine[:, :HEAD_SIZE]
    kv_weight = attention_mine[:, HEAD_SIZE : 2 * HEAD_SIZE]
    out_weight = attention_mine[:, 2 * HEAD_SIZE :]
    kv_raw = heads(mm(h1, kv_weight))
    kv = jnp.where(core == 0, rotate(kv_raw, cos_rows, sin_rows), kv_raw).astype(low)
    q = rotate(heads(mm(h1, query_weight)), cos_rows, sin_rows).astype(low)
    dyb = team_gather(outer_grad.astype(low), 15, [kv])
    down_blocks, down_weight = spread(feed_weight, take_feed(2), ff_part, 12, [dyb])
    if near:
        earlier = [
            lax.ppermute(kv, "z", [(at, at + back) for at in range(nz - back)]) for back in range(1, nz)
        ]
        *earlier, dyb, down_blocks, q = lax.optimization_barrier((*earlier, dyb, down_blocks, q))
        kv = jnp.stack([kv, *earlier])
    else:
        kv = lax.all_gather(kv, "z", axis=0, tiled=False)
    other = lax.ppermute(kv, "c", [(0, 1), (1, 0)])
    attend = (core_at, lengths_all, q, kv, other, query_at, key_at)
    (o,) = attention_call(attention_kernel, *attend, (), [("rows", low)], "attention")
    o = o.reshape(-1, HEAD_SIZE)
    r = x_in + team_sum([o], [out_weight], 4)

    normed_two, inverse_two = rms_forward(r, norm_gains[1])
    h2 = team_gather(normed_two.astype(low), 16)
    both = mm(h2, gate_up_weight)
    gate, upward = both[:, :ff_part], both[:, ff_part:]
    sig = jax.nn.sigmoid(gate)
    m = (gate * sig * upward).astype(low)
    down_term = mm_tn(dyb, m).astype(low)
    down_rows = scatter_planes(down_term)
    down_weight, down_term = together(down_weight, down_term)
    d_both = feed_back(dyb, down_weight, both)
    gate_up_term = mm_tn(h2, d_both).astype(low)
    gate_up_rows = scatter_planes(gate_up_term)
    dh2 = team_sum([d_both], [gate_up_weight], 7, [gate_up_term, down_term])
    mid_grad, gain_two = rms_back(dh2, r, inverse_two, norm_gains[1])
    dr = outer_grad + mid_grad
    drb = team_gather(dr.astype(low), 13, [down_rows])

    do = heads(mm(drb, out_weight).astype(low))
    dq, keep, theirs = attention_call(
        attention_back_kernel,
        *attend,
        (do, cos_table, sin_table),
        [("rows", low), ("keys", jnp.float32), ("keys", low)],
        "attention_back",
    )
    dq = dq.reshape(-1, HEAD_SIZE)
    dkv = keep + lax.ppermute(theirs, "c", [(0, 1), (1, 0)]).astype(jnp.float32)
    low_terms = dkv.astype(low)
    feed_sum = team_sum([m], [down_weight], 5, [low_terms])
    down_grad = scatter_team(down_rows, 6, [low_terms])
    dkv = lax.psum_scatter(low_terms, "z", scatter_dimension=0, tiled=True)[0]
    gate_up_grad = scatter_team(gate_up_rows, 8, [feed_sum, down_grad])
    dkv, gate_up_grad = together(dkv, gate_up_grad)
    dkv = dkv.astype(jnp.float32)
    dkv = jnp.where(core == 0, rotate(dkv, cos_rows, -sin_rows), dkv).astype(low).reshape(-1, HEAD_SIZE)
    layer_output = (r + feed_sum).astype(low)
    attention_term = jnp.concatenate([mm_tn(h1, dq), mm_tn(h1, dkv), mm_tn(drb, o)], axis=1).astype(low)
    attention_rows = scatter_planes(attention_term)
    dh1 = team_sum([dq, dkv], [query_weight, kv_weight], 9, [attention_term])
    in_grad, gain_one = rms_back(dh1, x_in, inverse_one, norm_gains[0])
    input_gradient = dr + in_grad
    local_squares = sum(jnp.sum(jnp.square(part.astype(jnp.float32))) for part in (gate_up_rows, down_rows))
    squares_line = jnp.full((6, width), local_squares)
    lines = jnp.concatenate([jnp.stack([gain_one, gain_two]), squares_line], axis=0)
    if is_square():
        attention_grad, lines = turn(attention_rows, 10, (), lines, nz)
    else:
        attention_grad = scatter_team(attention_rows, 10)
        lines = lines.at[2:].add(jnp.sum(jnp.square(attention_rows.astype(jnp.float32))))
        lines = lax.psum(lines, ALL)
    feed_new = update(feed_part, lines, feed_weight, feed_mean, feed_square, [gate_up_grad, down_grad])
    attention_new = update(attention_part, lines, attention_weight, attention_mean, attention_square, [attention_grad])
    *gains_new, gradient_norm = update_gains(lines, norm_gains, gain_mean, gain_square)
    return (
        layer_output.reshape(sequences, span, width),
        input_gradient.reshape(sequences, span, width),
        gradient_norm.reshape(()),
        *attention_new,
        *feed_new,
        *gains_new,
    )


def solution(mesh):
    ctx, fsdp = mesh.shape["ctx"], mesh.shape["fsdp"]
    inner = QUERY_HEADS // fsdp
    fine = Mesh(mesh.devices.reshape(ctx // inner, inner, fsdp // 2, 2), ALL)
    act = P(("x", "c"), ("z", "y"), None)
    matrix = P(ALL, None)
    return jax.shard_map(
        local,
        mesh=fine,
        in_specs=(act, P(("x", "c")), P(), matrix, matrix, act, matrix, matrix, matrix, matrix, P(), P()),
        out_specs=(act, act, P(), matrix, matrix, matrix, matrix, matrix, matrix, matrix, matrix, P(), P(), P()),
        check_vma=False,
    )
```

```python
import functools

import jax
import jax.numpy as jnp
from jax import lax
from jax.experimental import pallas as pl
from jax.experimental.pallas import tpu as pltpu
from jax.sharding import Mesh, PartitionSpec as P

QUERY_HEADS = 8
KEY_VALUE_HEADS = 4
HEAD_SIZE = 256
FF = 8192
STEP = 10

norm_eps = 1e-06
rope_base = 1000042.0
masked_value = -1e30
clip_norm = 1.0
beta_one = 0.9
beta_two = 0.95
adam_eps = 1e-08
matrix_rate = 0.03
gain_rate = 0.4
weight_decay = 0.1

TEAM = ("y", "x", "c")
ALL = ("z", "y", "x", "c")


MESH = pl.DeviceIdType.MESH
VMEM = pl.BlockSpec(memory_space=pltpu.VMEM)
HBM = pl.BlockSpec(memory_space=pl.ANY)


def place():
    y, x, c = lax.axis_index("y"), lax.axis_index("x"), lax.axis_index("c")
    return y, x, c, lambda yy, xx, cc: (yy * 2 + xx) * 2 + cc


def greet(others):
    barrier = pltpu.get_barrier_semaphore()
    for other in others:
        pl.semaphore_signal(barrier, inc=1, device_id=other, device_id_type=MESH)
    pl.semaphore_wait(barrier, len(others))


def gather_kernel(src, *refs):
    out, send, recv, own = refs[-4:]
    y, x, c, index = place()
    to_x, to_y, to_s = {"x": 1 - x}, {"y": 1 - y}, {"c": 1 - c}
    me, at_x, at_y, at_d = index(y, x, c), index(y, 1 - x, c), index(1 - y, x, c), index(1 - y, 1 - x, c)
    half = src.shape[0] // 2
    rows = (pl.ds(0, half), pl.ds(half, half))
    local = pltpu.make_async_copy(src, out.at[me], own)
    local.start()
    greet((to_x, to_y, to_s))

    def hop(slot, block, part, where, first=False):
        piece = out.at[block, rows[part]]
        return pltpu.make_async_remote_copy(
            src_ref=src.at[rows[part]] if first else piece,
            dst_ref=piece,
            send_sem=send.at[slot],
            recv_sem=recv.at[slot],
            device_id=where,
            device_id_type=MESH,
        )

    x0, x1 = hop(0, me, 0, to_x, True), hop(1, me, 1, to_x, True)
    y1, y0 = hop(2, me, 1, to_y, True), hop(3, me, 0, to_y, True)
    s0, s1 = hop(4, me, 0, to_s, True), hop(5, me, 1, to_s, True)
    for copy in (x0, y1, x1, y0, s0, s1):
        copy.start()
    x0.wait_recv()
    d0 = hop(6, at_x, 0, to_y)
    d0.start()
    y1.wait_recv()
    d1 = hop(7, at_y, 1, to_x)
    d1.start()
    sx0, sy1 = hop(8, at_x, 0, to_s), hop(9, at_y, 1, to_s)
    sx0.start()
    sy1.start()
    x1.wait_recv()
    sx1 = hop(10, at_x, 1, to_s)
    sx1.start()
    y0.wait_recv()
    sy0 = hop(11, at_y, 0, to_s)
    sy0.start()
    d0.wait_recv()
    sd0 = hop(12, at_d, 0, to_s)
    sd0.start()
    d1.wait_recv()
    sd1 = hop(13, at_d, 1, to_s)
    sd1.start()
    for copy in (s0, s1, sx0, sy1, sx1, sy0, sd0, sd1):
        copy.wait_recv()
    for copy in (x0, x1, y0, y1, s0, s1, d0, d1, sx0, sy1, sx1, sy0, sd0, sd1):
        copy.wait_send()
    local.wait()


def plane_gather(value, number, after=()):
    return pl.pallas_call(
        gather_kernel,
        out_shape=jax.ShapeDtypeStruct((8, *value.shape), value.dtype),
        in_specs=[HBM] * (1 + len(after)),
        out_specs=HBM,
        scratch_shapes=[
            pltpu.SemaphoreType.DMA((14,)),
            pltpu.SemaphoreType.DMA((14,)),
            pltpu.SemaphoreType.DMA,
        ],
        compiler_params=pltpu.CompilerParams(collective_id=number, has_side_effects=True),
        cost_estimate=pl.CostEstimate(flops=1, bytes_accessed=1, transcendentals=0),
        name="plane_gather",
    )(value, *after)


def sum_kernel(lefts, terms, tile, *refs):
    a_refs, w_refs = refs[:lefts], refs[lefts : lefts + len(terms)]
    out, s_send, s_recv, d_send, d_recv, x_send, x_recv, y_send, y_recv, x_acc, y_acc, send, recv = refs[-13:]
    y, x, c, index = place()
    to_x, to_y, to_s = {"x": 1 - x}, {"y": 1 - y}, {"c": 1 - c}
    rows, width = out.shape
    half = rows // 2
    parts = (pl.ds(0, half), pl.ds(half, half))
    f32, low = jnp.float32, jnp.bfloat16

    def product(block, put):
        lines = pl.ds(pl.multiple_of(block * rows, rows), rows)

        @pl.loop(0, width // tile)
        def _(step):
            cols = pl.ds(pl.multiple_of(step * tile, tile), tile)
            total = None
            for (left, start), w_ref in zip(terms, w_refs):
                term = mm_nt(a_refs[left][lines, start : start + w_ref.shape[1]], w_ref[cols, :])
                total = term if total is None else total + term
            put(cols, total)

    def hop(slot, src, dst, where):
        copy = pltpu.make_async_remote_copy(
            src_ref=src, dst_ref=dst, send_sem=send.at[slot], recv_sem=recv.at[slot],
            device_id=where, device_id_type=MESH,
        )
        return copy

    def to_sibling(slot, yy, xx):
        def put(cols, total):
            s_send[slot, :, cols] = total.astype(low)

        product(index(yy, xx, 1 - c), put)
        copy = hop(slot, s_send.at[slot], s_recv.at[slot], to_s)
        copy.start()
        return copy

    def with_sibling(slot, yy, xx, keep):
        def put(cols, total):
            keep[:, cols] = (total + s_recv[slot, :, cols].astype(f32)).astype(keep.dtype)

        product(index(yy, xx, c), put)

    greet((to_x, to_y, to_s))
    s0 = to_sibling(0, 1 - y, 1 - x)
    s1 = to_sibling(1, y, 1 - x)
    s0.wait_recv()
    with_sibling(0, 1 - y, 1 - x, d_send)
    d0 = hop(4, d_send.at[parts[0]], d_recv.at[parts[0]], to_x)
    d1 = hop(5, d_send.at[parts[1]], d_recv.at[parts[1]], to_y)
    d0.start()
    d1.start()
    s1.wait_recv()
    with_sibling(1, y, 1 - x, x_acc)
    x_send[parts[0]] = x_acc[parts[0]].astype(low)
    x0 = hop(6, x_send.at[parts[0]], x_recv.at[parts[0]], to_x)
    x0.start()
    s2 = to_sibling(2, 1 - y, x)
    s2.wait_recv()
    with_sibling(2, 1 - y, x, y_acc)
    y_send[parts[1]] = y_acc[parts[1]].astype(low)
    y1 = hop(7, y_send.at[parts[1]], y_recv.at[parts[1]], to_y)
    y1.start()
    s3 = to_sibling(3, y, x)
    d1.wait_recv()
    x_send[parts[1]] = (x_acc[parts[1]] + d_recv[parts[1]].astype(f32)).astype(low)
    x1 = hop(8, x_send.at[parts[1]], x_recv.at[parts[1]], to_x)
    x1.start()
    d0.wait_recv()
    y_send[parts[0]] = (y_acc[parts[0]] + d_recv[parts[0]].astype(f32)).astype(low)
    y0 = hop(9, y_send.at[parts[0]], y_recv.at[parts[0]], to_y)
    y0.start()
    s3.wait_recv()
    with_sibling(3, y, x, out)
    x0.wait_recv()
    y1.wait_recv()
    x1.wait_recv()
    y0.wait_recv()
    out[...] += x_recv[...].astype(f32) + y_recv[...].astype(f32)
    for copy in (s0, s1, s2, s3, d0, d1, x0, x1, y0, y1):
        copy.wait_send()


def plane_sum(lefts, rights, number, after=(), tile=512):
    ends = [(left, start) for left, a in enumerate(lefts) for start in range(0, a.shape[1], rights[0].shape[1])]
    terms = tuple(ends[: len(rights)])
    rows, width = lefts[0].shape[0] // 8, rights[0].shape[0]
    block = (rows, width)
    low, f32 = jnp.bfloat16, jnp.float32
    return pl.pallas_call(
        functools.partial(sum_kernel, len(lefts), terms, min(tile, width)),
        out_shape=jax.ShapeDtypeStruct(block, f32),
        in_specs=[VMEM] * (len(lefts) + len(rights)) + [HBM] * len(after),
        out_specs=VMEM,
        scratch_shapes=[
            pltpu.VMEM((4, *block), low),
            pltpu.VMEM((4, *block), low),
            *[pltpu.VMEM(block, low)] * 6,
            pltpu.VMEM(block, f32),
            pltpu.VMEM(block, f32),
            pltpu.SemaphoreType.DMA((10,)),
            pltpu.SemaphoreType.DMA((10,)),
        ],
        compiler_params=pltpu.CompilerParams(
            collective_id=number, has_side_effects=True, vmem_limit_bytes=48 * 2**20
        ),
        cost_estimate=pl.CostEstimate(flops=1, bytes_accessed=1, transcendentals=0),
        name="plane_sum",
    )(*lefts, *rights, *after)


def swap_kernel(pieces, takes, *refs):
    count = len(pieces)
    sources, (send, recv, own) = refs[: -2 * count - 3], refs[-3:]
    outs, holds = refs[-2 * count - 3 : -count - 3], refs[-count - 3 : -3]
    y, x, c, index = place()
    me = index(y, x, c)
    flips = [(fy, fx, fc) for fy, fx in ((1, 1), (0, 1), (1, 0), (0, 0)) for fc in (0, 1)]
    flips = [flip for flip in flips if flip != (0, 0, 0)]

    def there(flip):
        return tuple(1 - at if f else at for at, f in zip((y, x, c), flip))

    greet([dict(zip(("y", "x", "c"), there(flip))) for flip in flips])
    copies = []
    for piece in range(count):
        for number, flip in enumerate(flips):
            yy, xx, cc = there(flip)
            member = index(yy, xx, cc)
            holds[piece][number] = takes[piece](sources, member, cc)
            copy = pltpu.make_async_remote_copy(
                src_ref=holds[piece].at[number],
                dst_ref=outs[piece].at[me],
                send_sem=send.at[piece * 7 + number],
                recv_sem=recv.at[piece * 7 + number],
                device_id={"y": yy, "x": xx, "c": cc},
                device_id_type=MESH,
            )
            copy.start()
            copies.append(copy)
        holds[piece][7] = takes[piece](sources, me, c)
        keep = pltpu.make_async_copy(holds[piece].at[7], outs[piece].at[me], own.at[piece])
        keep.start()
        copies.append(keep)
    for copy in copies:
        copy.wait()


def plane_swap(sources, shapes, takes, number, after=()):
    low = jnp.bfloat16
    count = len(shapes)
    return pl.pallas_call(
        functools.partial(swap_kernel, shapes, takes),
        out_shape=[jax.ShapeDtypeStruct((8, *shape), low) for shape in shapes],
        in_specs=[VMEM] * len(sources) + [HBM] * len(after),
        out_specs=[HBM] * count,
        scratch_shapes=[
            *[pltpu.VMEM((8, *shape), low) for shape in shapes],
            pltpu.SemaphoreType.DMA((7 * count,)),
            pltpu.SemaphoreType.DMA((7 * count,)),
            pltpu.SemaphoreType.DMA((count,)),
        ],
        compiler_params=pltpu.CompilerParams(
            collective_id=number, has_side_effects=True, vmem_limit_bytes=48 * 2**20
        ),
        cost_estimate=pl.CostEstimate(flops=1, bytes_accessed=1, transcendentals=0),
        name="plane_swap",
    )(*sources, *after)


def team_of(y, x, c):
    flips = [(fy, fx, fc) for fy, fx in ((1, 1), (0, 1), (1, 0), (0, 0)) for fc in (0, 1)]
    return [
        tuple(1 - at if f else at for at, f in zip((y, x, c), flip)) for flip in flips if flip != (0, 0, 0)
    ]


def turn_kernel(planes, src, *refs):
    y, x, c, index = place()
    me = index(y, x, c)
    others = team_of(y, x, c)
    ids = [dict(zip(("y", "x", "c"), other)) for other in others]
    if planes:
        lines, out, total, near, far, held, send, recv, own, send_lines, recv_lines = refs[:1] + refs[-10:]
        z = lax.axis_index("z")
        column = [{"z": lax.rem(z + step, planes)} for step in range(1, planes)]
        fetch = pltpu.make_async_copy(src, held, own)
        fetch.start()
        fetch.wait()
        near[me] = lines[...]
        squares = jnp.zeros((8, held.shape[1]), jnp.float32)
        for start in range(0, held.shape[0], 64):
            part = held[start : start + 64].astype(jnp.float32)
            squares += jnp.sum(jnp.square(part).reshape(8, 8, -1), axis=0)
        near[me, 2:3] += jnp.sum(squares, keepdims=True)
    else:
        out, send, recv, own = refs[-4:]
        column = []
    greet(ids + column)
    count = src.shape[0] // 8

    def rows(member):
        return src.at[pl.ds(pl.multiple_of(member * count, count), count)]

    def spread(buffer, at, where, base):
        copies = [
            pltpu.make_async_remote_copy(
                src_ref=buffer.at[at],
                dst_ref=buffer.at[at],
                send_sem=send_lines.at[base + number],
                recv_sem=recv_lines.at[base + number],
                device_id=other,
                device_id_type=MESH,
            )
            for number, other in enumerate(where)
        ]
        for copy in copies:
            copy.start()
        return copies

    small = spread(near, me, ids, 0) if planes else []
    copies = [
        pltpu.make_async_remote_copy(
            src_ref=rows(index(*other)),
            dst_ref=out.at[me],
            send_sem=send.at[number],
            recv_sem=recv.at[number],
            device_id=where,
            device_id_type=MESH,
        )
        for number, (other, where) in enumerate(zip(others, ids))
    ]
    copies.append(pltpu.make_async_copy(rows(me), out.at[me], own))
    for copy in copies:
        copy.start()
    if planes:
        for copy in small:
            copy.wait()
        far[z] = jnp.sum(near[...], axis=0)
        for copy in spread(far, z, column, 7):
            copy.wait()
        total[...] = jnp.sum(far[...], axis=0)
    for copy in copies:
        copy.wait()


def turn(rows, number, after=(), lines=None, planes=0):
    block = (rows.shape[0] // 8, rows.shape[1])
    dma = pltpu.SemaphoreType.DMA
    out_shape, out_specs = [jax.ShapeDtypeStruct((8, *block), rows.dtype)], [HBM]
    in_specs, scratch = [HBM], [dma((7,)), dma((7,)), dma]
    operands = [rows]
    if planes:
        operands.append(lines)
        in_specs.append(VMEM)
        out_shape.append(jax.ShapeDtypeStruct(lines.shape, lines.dtype))
        out_specs.append(VMEM)
        buffers = [pltpu.VMEM((size, *lines.shape), lines.dtype) for size in (8, planes)]
        scratch = buffers + [pltpu.VMEM(rows.shape, rows.dtype)] + scratch + [dma((6 + planes,)), dma((6 + planes,))]
    return pl.pallas_call(
        functools.partial(turn_kernel, planes),
        out_shape=out_shape,
        in_specs=in_specs + [HBM] * len(after),
        out_specs=out_specs,
        scratch_shapes=scratch,
        compiler_params=pltpu.CompilerParams(
            collective_id=number, has_side_effects=True, vmem_limit_bytes=16 * 2**20
        ),
        cost_estimate=pl.CostEstimate(flops=1, bytes_accessed=1, transcendentals=0),
        name="turn",
    )(*operands, *after)


def hops(planes, send, recv, block, up):
    z = lax.axis_index("z")

    def step(number):
        gone, came = (z - number + 1, z - number) if up else (z + number - 1, z + number)
        goes = ((gone >= 0) & (z + 1 < planes)) if up else ((gone < planes) & (z >= 1))
        comes = (came >= 0) if up else (came < planes)

        def copy(b):
            return pltpu.make_async_remote_copy(
                src_ref=block(b),
                dst_ref=block(b),
                send_sem=send.at[number - 1],
                recv_sem=recv.at[number - 1],
                device_id={"z": z + 1 if up else z - 1},
                device_id_type=MESH,
            )

        return (
            lambda: pl.when(goes)(lambda: copy(gone).start()),
            lambda: pl.when(comes)(lambda: copy(came).wait_recv()),
            lambda: pl.when(goes)(lambda: copy(gone).wait_send()),
        )

    return [step(number) for number in range(1, planes)]


def ring(planes):
    z = lax.axis_index("z")
    return [{"z": lax.rem(z + 1, planes)}, {"z": lax.rem(z + planes - 1, planes)}]


def begin_kernel(
    planes, take_attention, take_gate_up, attention, feed, rows, all_attention, gate_up, all_rows,
    attention_hold, gate_up_hold, a_send, a_recv, g_send, g_recv, r_send, r_recv, u_send, u_recv, d_send, d_recv, own,
):
    y, x, c, index = place()
    z = lax.axis_index("z")
    me, at_x, at_y, at_d = index(y, x, c), index(y, 1 - x, c), index(1 - y, x, c), index(1 - y, 1 - x, c)
    others = team_of(y, x, c)
    ids = [dict(zip(("y", "x", "c"), other)) for other in others]
    to_x, to_y, to_s = {"x": 1 - x}, {"y": 1 - y}, {"c": 1 - c}
    count = attention.shape[0]

    def spread(source, take, hold, place_of, send, recv, local):
        copies = []
        for number, (other, where) in enumerate(zip(others, ids)):
            hold[number] = take([source], index(*other), other[2])
            copy = pltpu.make_async_remote_copy(
                src_ref=hold.at[number], dst_ref=place_of(me), send_sem=send.at[number], recv_sem=recv.at[number],
                device_id=where, device_id_type=MESH,
            )
            copy.start()
            copies.append(copy)
        hold[7] = take([source], me, c)
        keep = pltpu.make_async_copy(hold.at[7], place_of(me), local)
        keep.start()
        return copies, keep

    half = rows.shape[0] // 2
    parts = (pl.ds(0, half), pl.ds(half, half))

    def hop(slot, block, part, where, first=False):
        piece = all_rows.at[block, parts[part]]
        copy = pltpu.make_async_remote_copy(
            src_ref=rows.at[parts[part]] if first else piece, dst_ref=piece,
            send_sem=r_send.at[slot], recv_sem=r_recv.at[slot], device_id=where, device_id_type=MESH,
        )
        copy.start()
        return copy

    def attention_rows(start, size):
        return all_attention.at[pl.ds(pl.multiple_of(start, count), size)]

    greet(ids + ring(planes))
    mine = pltpu.make_async_copy(rows, all_rows.at[me], own.at[0])
    mine.start()
    a_copies, a_keep = spread(
        attention, take_attention, attention_hold, lambda m: attention_rows((z * 8 + m) * count, count), a_send, a_recv, own.at[1]
    )
    x0, y1 = hop(0, me, 0, to_x, True), hop(2, me, 1, to_y, True)
    x1, y0 = hop(1, me, 1, to_x, True), hop(3, me, 0, to_y, True)
    s0, s1 = hop(4, me, 0, to_s, True), hop(5, me, 1, to_s, True)
    for copy in a_copies:
        copy.wait_recv()
    a_keep.wait()

    def plane_block(b):
        return attention_rows(b * 8 * count, 8 * count)

    up = hops(planes, u_send, u_recv, plane_block, True)
    down = hops(planes, d_send, d_recv, plane_block, False)

    def pass_on(number):
        if number > 0:
            up[number - 1][1]()
            down[number - 1][1]()
        if number < planes - 1:
            up[number][0]()
            down[number][0]()

    pass_on(0)
    x0.wait_recv()
    d0 = hop(6, at_x, 0, to_y)
    y1.wait_recv()
    d1 = hop(7, at_y, 1, to_x)
    sx0, sy1 = hop(8, at_x, 0, to_s), hop(9, at_y, 1, to_s)
    g_copies, g_keep = spread(feed, take_gate_up, gate_up_hold, lambda m: gate_up.at[m], g_send, g_recv, own.at[2])
    x1.wait_recv()
    sx1 = hop(10, at_x, 1, to_s)
    y0.wait_recv()
    sy0 = hop(11, at_y, 0, to_s)
    pass_on(1)
    d0.wait_recv()
    sd0 = hop(12, at_d, 0, to_s)
    d1.wait_recv()
    sd1 = hop(13, at_d, 1, to_s)
    for number in range(2, planes):
        pass_on(number)
    for copy in (s0, s1, sx0, sy1, sx1, sy0, sd0, sd1, *g_copies):
        copy.wait_recv()
    for copy in (x0, x1, y0, y1, s0, s1, d0, d1, sx0, sy1, sx1, sy0, sd0, sd1, *a_copies, *g_copies):
        copy.wait_send()
    for step in up + down:
        step[2]()
    g_keep.wait()
    mine.wait()


def begin(attention, feed, rows, takes, widths, planes, number):
    low, dma = jnp.bfloat16, pltpu.SemaphoreType.DMA
    count = attention.shape[0]
    return pl.pallas_call(
        functools.partial(begin_kernel, planes, *takes),
        out_shape=[
            jax.ShapeDtypeStruct((planes * 8 * count, widths[0]), low),
            jax.ShapeDtypeStruct((8, count, widths[1]), low),
            jax.ShapeDtypeStruct((8, *rows.shape), low),
        ],
        in_specs=[VMEM, VMEM, HBM],
        out_specs=[HBM] * 3,
        scratch_shapes=[pltpu.VMEM((8, count, width), low) for width in widths]
        + [dma((size,)) for size in (7, 7, 7, 7, 14, 14, *[planes - 1] * 4, 3)],
        compiler_params=pltpu.CompilerParams(
            collective_id=number, has_side_effects=True, vmem_limit_bytes=32 * 2**20
        ),
        cost_estimate=pl.CostEstimate(flops=1, bytes_accessed=1, transcendentals=0),
        name="begin",
    )(attention, feed, rows)


def climb_kernel(planes, block, mine, other, u_send, u_recv, s_send, s_recv, own, fill):
    z, c = lax.axis_index("z"), lax.axis_index("c")
    to_s = {"c": 1 - c}
    greet([to_s] + ring(planes))

    def across(n):
        return pltpu.make_async_remote_copy(
            src_ref=block if n == 0 else mine.at[n], dst_ref=other.at[n], send_sem=s_send.at[n], recv_sem=s_recv.at[n],
            device_id=to_s, device_id_type=MESH,
        )

    def along(n):
        return pltpu.make_async_remote_copy(
            src_ref=block if n == 1 else mine.at[n - 1], dst_ref=mine.at[n], send_sem=u_send.at[n - 1], recv_sem=u_recv.at[n - 1],
            device_id={"z": z + 1}, device_id_type=MESH,
        )

    keep = pltpu.make_async_copy(block, mine.at[0], own)
    keep.start()
    more = z + 1 < planes
    pl.when(more)(lambda: along(1).start())
    across(0).start()
    for n in range(1, planes):

        @pl.when(z < n)
        def _():
            for number, buffer in enumerate((mine, other)):
                pltpu.make_async_copy(block, buffer.at[n], fill.at[2 * (n - 1) + number]).start()

    for n in range(1, planes):

        @pl.when(z >= n)
        def _():
            along(n).wait_recv()
            if n + 1 < planes:
                pl.when(more)(lambda: along(n + 1).start())
            across(n).start()

    across(0).wait()
    keep.wait()
    for n in range(1, planes):

        @pl.when(z >= n)
        def _():
            across(n).wait()

        @pl.when(z < n)
        def _():
            for number, buffer in enumerate((mine, other)):
                pltpu.make_async_copy(block, buffer.at[n], fill.at[2 * (n - 1) + number]).wait()

        pl.when((z >= n - 1) & more)(lambda: along(n).wait_send())


def climb(block, planes, number):
    dma = pltpu.SemaphoreType.DMA
    return pl.pallas_call(
        functools.partial(climb_kernel, planes),
        out_shape=[jax.ShapeDtypeStruct((planes, *block.shape), block.dtype)] * 2,
        in_specs=[HBM],
        out_specs=[HBM] * 2,
        scratch_shapes=[dma((planes - 1,))] * 2 + [dma((planes,))] * 2 + [dma, dma((2 * (planes - 1),))],
        compiler_params=pltpu.CompilerParams(collective_id=number, has_side_effects=True),
        cost_estimate=pl.CostEstimate(flops=1, bytes_accessed=1, transcendentals=0),
        name="climb",
    )(block)


def dot(left, right, contract):
    return lax.dot_general(left, right, (contract, ((), ())), preferred_element_type=jnp.float32)


def mm(left, right):
    return dot(left, right, ((1,), (0,)))


def mm_nt(left, right):
    return dot(left, right, ((1,), (1,)))


def mm_tn(left, right):
    return dot(left, right, ((0,), (0,)))


def bmm(pattern, left, right):
    return jnp.einsum(pattern, left, right, preferred_element_type=jnp.float32)


def angle_tables(positions):
    half_dim = HEAD_SIZE // 2
    frequency = rope_base ** (-(jnp.arange(half_dim).astype(jnp.float32) * 2.0) / HEAD_SIZE)
    phases = positions.astype(jnp.float32)[:, None] * frequency[None, :]
    return (jnp.cos(phases), jnp.sin(phases))


def rotate(value, cos_table, sin_table):
    half = value.shape[-1] // 2
    a, b = value[..., :half], value[..., half:]
    return jnp.concatenate([a * cos_table - b * sin_table, b * cos_table + a * sin_table], axis=-1)


def rms_forward(value, gain_row):
    inverse = lax.rsqrt(jnp.mean(value * value, axis=-1, keepdims=True) + norm_eps)
    return (value * inverse * gain_row, inverse)


def rms_back(grad_out, value, inverse, gain_row):
    scaled = grad_out * gain_row
    grad_in = inverse * (
        scaled - value * inverse * inverse * jnp.mean(scaled * value, axis=-1, keepdims=True)
    )
    return (grad_in, jnp.sum(grad_out * value * inverse, axis=0))


def adamw(weight, gradient, moment_one, moment_two, step_rate, decay_rate, invert=jnp.reciprocal):
    mean_new = beta_one * moment_one + (1.0 - beta_one) * gradient
    square_new = beta_two * moment_two + (1.0 - beta_two) * gradient * gradient
    below = jnp.sqrt(square_new * (1.0 / (1.0 - beta_two**STEP))) + adam_eps
    direction = mean_new * (1.0 / (1.0 - beta_one**STEP)) * invert(below)
    return (weight - step_rate * (direction + decay_rate * weight), mean_new, square_new)


def attention_parts(core, length, q_ref, mine_ref, other_ref, query_ref, key_ref):
    mine, other = mine_ref[...].reshape(-1, HEAD_SIZE), other_ref[...].reshape(-1, HEAD_SIZE)
    first = core == 0
    k, v = jnp.where(first, mine, other), jnp.where(first, other, mine)
    q = q_ref[...].reshape(-1, HEAD_SIZE)
    at, key_at = query_ref[...], key_ref[...]
    allowed = (key_at <= at) & (key_at < length) & (key_at >= 0)
    scores = jnp.where(allowed, mm_nt(q, k) * HEAD_SIZE ** (-0.5), masked_value)
    exponent = jnp.exp(scores - jnp.max(scores, axis=-1, keepdims=True))
    return q, k, v, exponent / jnp.sum(exponent, axis=-1, keepdims=True)


def attention_kernel(core_ref, length_ref, q_ref, mine_ref, other_ref, query_ref, key_ref, out_ref):
    length = length_ref[pl.program_id(0)]
    _, _, v, soft = attention_parts(core_ref[0], length, q_ref, mine_ref, other_ref, query_ref, key_ref)
    out_ref[...] = mm(soft.astype(jnp.bfloat16), v).astype(jnp.bfloat16).reshape(out_ref.shape)


def attention_back_kernel(
    core_ref, length_ref, q_ref, mine_ref, other_ref, query_ref, key_ref, do_ref, cos_ref, sin_ref,
    dq_ref, keep_ref, send_ref,
):
    low = jnp.bfloat16
    core = core_ref[0]
    length = length_ref[pl.program_id(0)]
    q, k, v, soft = attention_parts(core, length, q_ref, mine_ref, other_ref, query_ref, key_ref)
    do = do_ref[...].reshape(-1, HEAD_SIZE)
    dp = mm_nt(do, v)
    delta = jnp.sum(soft * dp, axis=-1, keepdims=True)
    ds = (soft * (dp - delta) * HEAD_SIZE ** (-0.5)).astype(low)
    dq = mm(ds, k)
    cos_table, sin_table = cos_ref[...], sin_ref[...]
    half = HEAD_SIZE // 2
    a, b = dq[:, :half], dq[:, half:]
    turned = jnp.concatenate([a * cos_table + b * sin_table, b * cos_table - a * sin_table], axis=-1)
    dq_ref[...] = turned.astype(low).reshape(dq_ref.shape)
    dk, dv = mm_tn(ds, q), mm_tn(soft.astype(low), do)
    first = core == 0
    keep, send = (t.reshape(keep_ref.shape) for t in (jnp.where(first, dk, dv), jnp.where(first, dv, dk)))
    for block in range(keep_ref.shape[0]):
        at = core_ref[1 + block]
        keep_ref[at] = keep[block]
        send_ref[at] = send[block].astype(low)


def attention_call(kernel, core, lengths, q, mine, other, query_pos, key_pos, extra, outs, name):
    ny, count, span, size = q.shape
    nz = mine.shape[0]
    rows = pl.BlockSpec((ny, 1, span, size), lambda i, *_: (0, i, 0, 0))
    keys = pl.BlockSpec((nz, ny, 1, span, size), lambda i, *_: (0, 0, i, 0, 0))

    def whole(value):
        return pl.BlockSpec(value.shape, lambda i, *_: (0,) * value.ndim)

    kinds = {"rows": (rows, q.shape), "keys": (keys, mine.shape)}
    return pl.pallas_call(
        kernel,
        grid_spec=pltpu.PrefetchScalarGridSpec(
            num_scalar_prefetch=2,
            grid=(count,),
            in_specs=[rows, keys, keys, whole(query_pos), whole(key_pos)]
            + [rows if value.shape == q.shape else whole(value) for value in extra],
            out_specs=[kinds[kind][0] for kind, _ in outs],
        ),
        out_shape=[jax.ShapeDtypeStruct(kinds[kind][1], dtype) for kind, dtype in outs],
        compiler_params=pltpu.CompilerParams(vmem_limit_bytes=48 * 2**20),
        cost_estimate=pl.CostEstimate(flops=1, bytes_accessed=1, transcendentals=0),
        name=name,
    )(core, lengths, q, mine, other, query_pos, key_pos, *extra)


def feed_back_kernel(dyb_ref, weight_ref, gate_ref, up_ref, out_ref):
    dm = mm(dyb_ref[...], weight_ref[...])
    gate, upward = gate_ref[...], up_ref[...]
    sig = jax.nn.sigmoid(gate)
    part = gate.shape[1]
    out_ref[:, :part] = (dm * upward * sig * (1.0 + gate * (1.0 - sig))).astype(out_ref.dtype)
    out_ref[:, part:] = (dm * gate * sig).astype(out_ref.dtype)


def feed_back(dyb, weight, both, lines=256):
    count, part = both.shape[0], both.shape[1] // 2

    def rows(width, column=0):
        return pl.BlockSpec((lines, width), lambda i: (i, column))

    return pl.pallas_call(
        feed_back_kernel,
        grid=(count // lines,),
        in_specs=[rows(dyb.shape[1]), pl.BlockSpec(weight.shape, lambda i: (0, 0)), rows(part), rows(part, 1)],
        out_specs=rows(2 * part),
        out_shape=jax.ShapeDtypeStruct((count, 2 * part), jnp.bfloat16),
        compiler_params=pltpu.CompilerParams(vmem_limit_bytes=48 * 2**20),
        cost_estimate=pl.CostEstimate(flops=1, bytes_accessed=1, transcendentals=0),
        name="feed_back",
    )(dyb, weight, both, both)


def attention_part(step, grad_ref):
    parts = []
    for head in range(8):
        member = jnp.where(step == 1, 2 * (head % 4) + head // 4, head)
        parts.append(grad_ref[member, :, pl.ds(pl.multiple_of(step * HEAD_SIZE, HEAD_SIZE), HEAD_SIZE)])
    return jnp.concatenate(parts, axis=1)


def feed_part(step, gate_up_ref, down_ref):
    size = down_ref.shape[2]
    at = pl.ds(pl.multiple_of(jnp.minimum(step // 2, 1) * size, size), size)
    parts = []
    for number in range(4):
        member = 4 * (step % 2) + number
        parts.append(jnp.where(step < 4, gate_up_ref[member, :, at], down_ref[member]))
    return jnp.concatenate(parts, axis=1)


def close_reciprocal(value):
    guess = pltpu.reciprocal(value, approx=True)
    return guess * (2.0 - value * guess)


def norm_of(lines_ref):
    gains = lines_ref[0:2]
    return jnp.sqrt(jnp.sum(gains * gains, keepdims=True) + lines_ref[2:3, 0:1])


def update_gains_kernel(lines_ref, weight_ref, mean_ref, square_ref, new_ref, new_mean_ref, new_square_ref, norm_ref):
    norm = norm_of(lines_ref)
    norm_ref[...] = norm
    new_ref[...], new_mean_ref[...], new_square_ref[...] = adamw(
        weight_ref[...], lines_ref[0:2] * (clip_norm / norm), mean_ref[...], square_ref[...], gain_rate, 0.0
    )


def update_gains(lines, weight, mean, square):
    f32 = jnp.float32
    return pl.pallas_call(
        update_gains_kernel,
        in_specs=[VMEM] * 4,
        out_specs=[VMEM] * 4,
        out_shape=[jax.ShapeDtypeStruct(weight.shape, f32)] * 3 + [jax.ShapeDtypeStruct((1, 1), f32)],
        name="update_gains",
    )(lines, weight, mean, square)


def update_kernel(part, lines_ref, weight_ref, mean_ref, square_ref, *refs):
    grads, (new_ref, new_mean_ref, new_square_ref, copy_ref, factor_ref) = refs[:-5], refs[-5:]

    @pl.when(pl.program_id(0) == 0)
    def _():
        factor_ref[...] = clip_norm / norm_of(lines_ref)

    gradient = part(pl.program_id(0), *grads).astype(jnp.float32) * factor_ref[...]
    new, mean, square = adamw(
        weight_ref[...], gradient, mean_ref[...], square_ref[...], matrix_rate, weight_decay, close_reciprocal
    )
    new_ref[...] = new
    new_mean_ref[...] = mean
    new_square_ref[...] = square
    copy_ref[...] = new.astype(copy_ref.dtype)


def update(part, lines, weight, mean, square, grads):
    size = 2048 if part is attention_part else 4096
    rows, width = weight.shape
    block = pl.BlockSpec((rows, size), lambda i: (0, i))
    f32 = jnp.float32
    return pl.pallas_call(
        functools.partial(update_kernel, part),
        grid=(width // size,),
        in_specs=[pl.BlockSpec(lines.shape, lambda i: (0, 0)), block, block, block]
        + [pl.BlockSpec(grad.shape, lambda i: (0, 0, 0)) for grad in grads],
        out_specs=[block] * 4,
        out_shape=[jax.ShapeDtypeStruct(weight.shape, dtype) for dtype in (f32, f32, f32, jnp.bfloat16)],
        scratch_shapes=[pltpu.VMEM((1, 1), f32)],
        compiler_params=pltpu.CompilerParams(vmem_limit_bytes=48 * 2**20),
        name="update",
    )(lines, weight, mean, square, *grads)


def is_square():
    return lax.axis_size("y") == 2 and lax.axis_size("x") == 2


def swap(blocks):
    return lax.all_to_all(blocks, TEAM, split_axis=0, concat_axis=0, tiled=True)


def over_planes(blocks):
    return lax.all_gather(blocks.reshape(-1, blocks.shape[-1]), "z", axis=0, tiled=True)


def scatter_planes(term):
    return lax.psum_scatter(term, "z", scatter_dimension=0, tiled=True)


def together(*values):
    return lax.optimization_barrier(values)


def scatter_team(rows, number, after=()):
    if not is_square():
        return swap(rows.reshape(8, -1, rows.shape[-1]))
    return turn(rows, number, after)[0]


def team_gather(local, number, after=()):
    if not is_square():
        return lax.all_gather(local, TEAM, axis=0, tiled=True)
    return plane_gather(local, number, after).reshape(-1, local.shape[1])


def team_sum(lefts, rights, number, after=()):
    if is_square():
        return plane_sum(lefts, rights, number, after)
    partial = mm_nt(jnp.concatenate(lefts, axis=1), jnp.concatenate(rights, axis=1))
    return lax.psum_scatter(partial.astype(jnp.bfloat16), TEAM, scatter_dimension=0, tiled=True).astype(jnp.float32)


def local(
    tokens,
    lengths,
    norm_gains,
    attention_weight,
    feed_weight,
    cotangent,
    attention_mean,
    attention_square,
    feed_mean,
    feed_square,
    gain_mean,
    gain_square,
):
    low = jnp.bfloat16
    sequences, span, width = tokens.shape
    ny, nx, nz = lax.axis_size("y"), lax.axis_size("x"), lax.axis_size("z")
    team = ny * nx * 2
    core = lax.axis_index("c")
    rows = attention_weight.shape[0]
    q_width, kv_width = QUERY_HEADS * HEAD_SIZE, KEY_VALUE_HEADS * HEAD_SIZE
    count = sequences * span
    all_sequences = nx * 2 * sequences
    reach = ny * span
    near = is_square()
    ff_part = FF // team

    def columns(start, size):
        return pl.ds(pl.multiple_of(start, size), size)

    def take_attention(sources, member, c):
        source = sources[0]
        starts = (
            member * HEAD_SIZE,
            q_width + c * kv_width + (member - c) // 2 * HEAD_SIZE,
            q_width + 2 * kv_width + member * HEAD_SIZE,
        )
        return jnp.concatenate([source[:, columns(s, HEAD_SIZE)].astype(low) for s in starts], axis=1)

    def take_feed(*parts):
        return lambda sources, member, c: jnp.concatenate(
            [sources[0][:, columns(part * FF + member * ff_part, ff_part)].astype(low) for part in parts], axis=1
        )

    def spread(source, take, size, number, after=()):
        if is_square():
            blocks = plane_swap([source], [(rows, size)], [take], number, after)[0]
        else:
            blocks = swap(jnp.stack([take([source], member, member % 2) for member in range(8)]))
        return blocks, over_planes(blocks)

    team_base = lax.axis_index("z") * reach
    team_pos = team_base + jnp.arange(reach, dtype=jnp.int32)
    own_pos = team_base + lax.axis_index("y") * span + jnp.arange(span, dtype=jnp.int32)
    if near:
        key_pos = jnp.concatenate([team_pos - back * reach for back in range(nz)])
    else:
        key_pos = jnp.arange(nz * reach, dtype=jnp.int32)
    query_at, key_at = team_pos[:, None], key_pos[None, :]
    cos_table, sin_table = angle_tables(team_pos)
    cos_rows, sin_rows = (t.reshape(ny, 1, span, -1) for t in (cos_table, sin_table))
    valid = (own_pos[None, :] < lengths[:, None]).astype(jnp.float32).reshape(count, 1)
    lengths_all = lax.all_gather(lengths, ("x", "c"), axis=0, tiled=True)
    planes = jnp.arange(nz, dtype=jnp.int32)
    if near:
        planes = (lax.axis_index("z") - planes) % nz
    core_at = jnp.concatenate([jnp.reshape(core, (1,)), planes]).astype(jnp.int32)

    def heads(value):
        return value.reshape(ny, all_sequences, span, HEAD_SIZE)

    x_in = tokens.reshape(count, width).astype(jnp.float32)
    normed_one, inverse_one = rms_forward(x_in, norm_gains[0])
    outer_grad = cotangent.reshape(count, width).astype(jnp.float32) * valid
    if is_square():
        attention_mine, gate_up_blocks, h1 = begin(
            attention_weight,
            feed_weight,
            normed_one.astype(low),
            (take_attention, take_feed(0, 1)),
            (3 * HEAD_SIZE, 2 * ff_part),
            nz,
            1,
        )
        h1 = h1.reshape(-1, width)
    else:
        attention_mine = spread(attention_weight, take_attention, 3 * HEAD_SIZE, 1)[1]
        gate_up_blocks, gate_up_weight = spread(feed_weight, take_feed(0, 1), 2 * ff_part, 2)
        h1 = team_gather(normed_one.astype(low), 3)
    query_weight = attention_mine[:, :HEAD_SIZE]
    kv_weight = attention_mine[:, HEAD_SIZE : 2 * HEAD_SIZE]
    out_weight = attention_mine[:, 2 * HEAD_SIZE :]
    kv_raw = heads(mm(h1, kv_weight))
    kv = jnp.where(core == 0, rotate(kv_raw, cos_rows, sin_rows), kv_raw).astype(low)
    q = rotate(heads(mm(h1, query_weight)), cos_rows, sin_rows).astype(low)
    if is_square():
        kv, other = climb(kv, nz, 2)
        gate_up_blocks, kv = together(gate_up_blocks, kv)
        gate_up_weight = over_planes(gate_up_blocks)
    else:
        kv = lax.all_gather(kv, "z", axis=0, tiled=False)
        other = lax.ppermute(kv, "c", [(0, 1), (1, 0)])
    attend = (core_at, lengths_all, q, kv, other, query_at, key_at)
    (o,) = attention_call(attention_kernel, *attend, (), [("rows", low)], "attention")
    o = o.reshape(-1, HEAD_SIZE)
    r = x_in + team_sum([o], [out_weight], 4)

    normed_two, inverse_two = rms_forward(r, norm_gains[1])
    h2 = team_gather(normed_two.astype(low), 16)
    dyb = team_gather(outer_grad.astype(low), 15, [h2])
    down_blocks, down_weight = spread(feed_weight, take_feed(2), ff_part, 12, [dyb])
    gate_up_weight, down_blocks = together(gate_up_weight, down_blocks)
    both = mm(h2, gate_up_weight)
    gate, upward = both[:, :ff_part], both[:, ff_part:]
    sig = jax.nn.sigmoid(gate)
    m = (gate * sig * upward).astype(low)
    down_term = mm_tn(dyb, m).astype(low)
    down_rows = scatter_planes(down_term)
    down_weight, down_term = together(down_weight, down_term)
    d_both = feed_back(dyb, down_weight, both)
    gate_up_term = mm_tn(h2, d_both).astype(low)
    gate_up_rows = scatter_planes(gate_up_term)
    dh2 = team_sum([d_both], [gate_up_weight], 7, [gate_up_term, down_term])
    mid_grad, gain_two = rms_back(dh2, r, inverse_two, norm_gains[1])
    dr = outer_grad + mid_grad
    drb = team_gather(dr.astype(low), 13, [down_rows])

    do = heads(mm(drb, out_weight).astype(low))
    dq, keep, theirs = attention_call(
        attention_back_kernel,
        *attend,
        (do, cos_table, sin_table),
        [("rows", low), ("keys", jnp.float32), ("keys", low)],
        "attention_back",
    )
    dq = dq.reshape(-1, HEAD_SIZE)
    dkv = keep + lax.ppermute(theirs, "c", [(0, 1), (1, 0)]).astype(jnp.float32)
    low_terms = dkv.astype(low)
    feed_sum = team_sum([m], [down_weight], 5, [low_terms])
    down_grad = scatter_team(down_rows, 6, [low_terms])
    dkv = lax.psum_scatter(low_terms, "z", scatter_dimension=0, tiled=True)[0]
    gate_up_grad = scatter_team(gate_up_rows, 8, [feed_sum, down_grad])
    dkv, gate_up_grad = together(dkv, gate_up_grad)
    dkv = dkv.astype(jnp.float32)
    dkv = jnp.where(core == 0, rotate(dkv, cos_rows, -sin_rows), dkv).astype(low).reshape(-1, HEAD_SIZE)
    layer_output = (r + feed_sum).astype(low)
    attention_term = jnp.concatenate([mm_tn(h1, dq), mm_tn(h1, dkv), mm_tn(drb, o)], axis=1).astype(low)
    attention_rows = scatter_planes(attention_term)
    dh1 = team_sum([dq, dkv], [query_weight, kv_weight], 9, [attention_term])
    in_grad, gain_one = rms_back(dh1, x_in, inverse_one, norm_gains[0])
    input_gradient = dr + in_grad
    local_squares = sum(jnp.sum(jnp.square(part.astype(jnp.float32))) for part in (gate_up_rows, down_rows))
    squares_line = jnp.full((6, width), local_squares)
    lines = jnp.concatenate([jnp.stack([gain_one, gain_two]), squares_line], axis=0)
    if is_square():
        attention_grad, lines = turn(attention_rows, 10, (), lines, nz)
    else:
        attention_grad = scatter_team(attention_rows, 10)
        lines = lines.at[2:].add(jnp.sum(jnp.square(attention_rows.astype(jnp.float32))))
        lines = lax.psum(lines, ALL)
    feed_new = update(feed_part, lines, feed_weight, feed_mean, feed_square, [gate_up_grad, down_grad])
    attention_new = update(attention_part, lines, attention_weight, attention_mean, attention_square, [attention_grad])
    *gains_new, gradient_norm = update_gains(lines, norm_gains, gain_mean, gain_square)
    return (
        layer_output.reshape(sequences, span, width),
        input_gradient.reshape(sequences, span, width),
        gradient_norm.reshape(()),
        *attention_new,
        *feed_new,
        *gains_new,
    )


def solution(mesh):
    ctx, fsdp = mesh.shape["ctx"], mesh.shape["fsdp"]
    inner = QUERY_HEADS // fsdp
    fine = Mesh(mesh.devices.reshape(ctx // inner, inner, fsdp // 2, 2), ALL)
    act = P(("x", "c"), ("z", "y"), None)
    matrix = P(ALL, None)
    return jax.shard_map(
        local,
        mesh=fine,
        in_specs=(act, P(("x", "c")), P(), matrix, matrix, act, matrix, matrix, matrix, matrix, P(), P()),
        out_specs=(act, act, P(), matrix, matrix, matrix, matrix, matrix, matrix, matrix, matrix, P(), P(), P()),
        check_vma=False,
    )
```

```python
import functools

import jax
import jax.numpy as jnp
from jax import lax
from jax.experimental import pallas as pl
from jax.experimental.pallas import tpu as pltpu
from jax.sharding import Mesh, PartitionSpec as P

QUERY_HEADS = 8
KEY_VALUE_HEADS = 4
HEAD_SIZE = 256
FF = 8192
STEP = 10

norm_eps = 1e-06
rope_base = 1000042.0
masked_value = -1e30
clip_norm = 1.0
beta_one = 0.9
beta_two = 0.95
adam_eps = 1e-08
matrix_rate = 0.03
gain_rate = 0.4
weight_decay = 0.1

TEAM = ("y", "x", "c")
ALL = ("z", "y", "x", "c")


MESH = pl.DeviceIdType.MESH
VMEM = pl.BlockSpec(memory_space=pltpu.VMEM)
HBM = pl.BlockSpec(memory_space=pl.ANY)


def place():
    y, x, c = lax.axis_index("y"), lax.axis_index("x"), lax.axis_index("c")
    return y, x, c, lambda yy, xx, cc: (yy * 2 + xx) * 2 + cc


def greet(others):
    barrier = pltpu.get_barrier_semaphore()
    for other in others:
        pl.semaphore_signal(barrier, inc=1, device_id=other, device_id_type=MESH)
    pl.semaphore_wait(barrier, len(others))


def gather_kernel(src, *refs):
    out, send, recv, own = refs[-4:]
    y, x, c, index = place()
    to_x, to_y, to_s = {"x": 1 - x}, {"y": 1 - y}, {"c": 1 - c}
    me, at_x, at_y, at_d = index(y, x, c), index(y, 1 - x, c), index(1 - y, x, c), index(1 - y, 1 - x, c)
    half = src.shape[0] // 2
    rows = (pl.ds(0, half), pl.ds(half, half))
    local = pltpu.make_async_copy(src, out.at[me], own)
    local.start()
    greet((to_x, to_y, to_s))

    def hop(slot, block, part, where, first=False):
        piece = out.at[block, rows[part]]
        return pltpu.make_async_remote_copy(
            src_ref=src.at[rows[part]] if first else piece,
            dst_ref=piece,
            send_sem=send.at[slot],
            recv_sem=recv.at[slot],
            device_id=where,
            device_id_type=MESH,
        )

    x0, x1 = hop(0, me, 0, to_x, True), hop(1, me, 1, to_x, True)
    y1, y0 = hop(2, me, 1, to_y, True), hop(3, me, 0, to_y, True)
    s0, s1 = hop(4, me, 0, to_s, True), hop(5, me, 1, to_s, True)
    for copy in (x0, y1, x1, y0, s0, s1):
        copy.start()
    x0.wait_recv()
    d0 = hop(6, at_x, 0, to_y)
    d0.start()
    y1.wait_recv()
    d1 = hop(7, at_y, 1, to_x)
    d1.start()
    sx0, sy1 = hop(8, at_x, 0, to_s), hop(9, at_y, 1, to_s)
    sx0.start()
    sy1.start()
    x1.wait_recv()
    sx1 = hop(10, at_x, 1, to_s)
    sx1.start()
    y0.wait_recv()
    sy0 = hop(11, at_y, 0, to_s)
    sy0.start()
    d0.wait_recv()
    sd0 = hop(12, at_d, 0, to_s)
    sd0.start()
    d1.wait_recv()
    sd1 = hop(13, at_d, 1, to_s)
    sd1.start()
    for copy in (s0, s1, sx0, sy1, sx1, sy0, sd0, sd1):
        copy.wait_recv()
    for copy in (x0, x1, y0, y1, s0, s1, d0, d1, sx0, sy1, sx1, sy0, sd0, sd1):
        copy.wait_send()
    local.wait()


def plane_gather(value, number, after=()):
    return pl.pallas_call(
        gather_kernel,
        out_shape=jax.ShapeDtypeStruct((8, *value.shape), value.dtype),
        in_specs=[VMEM] + [HBM] * len(after),
        out_specs=HBM,
        scratch_shapes=[
            pltpu.SemaphoreType.DMA((14,)),
            pltpu.SemaphoreType.DMA((14,)),
            pltpu.SemaphoreType.DMA,
        ],
        compiler_params=pltpu.CompilerParams(collective_id=number, has_side_effects=True),
        cost_estimate=pl.CostEstimate(flops=1, bytes_accessed=1, transcendentals=0),
        name="plane_gather",
    )(value, *after)


def sum_kernel(lefts, terms, tile, *refs):
    a_refs, w_refs = refs[:lefts], refs[lefts : lefts + len(terms)]
    out, s_send, s_recv, d_send, d_recv, x_send, x_recv, y_send, y_recv, x_acc, y_acc, send, recv = refs[-13:]
    y, x, c, index = place()
    to_x, to_y, to_s = {"x": 1 - x}, {"y": 1 - y}, {"c": 1 - c}
    rows, width = out.shape
    half = rows // 2
    parts = (pl.ds(0, half), pl.ds(half, half))
    f32, low = jnp.float32, jnp.bfloat16

    def product(block, put):
        lines = pl.ds(pl.multiple_of(block * rows, rows), rows)

        @pl.loop(0, width // tile)
        def _(step):
            cols = pl.ds(pl.multiple_of(step * tile, tile), tile)
            total = None
            for (left, start), w_ref in zip(terms, w_refs):
                term = mm_nt(a_refs[left][lines, start : start + w_ref.shape[1]], w_ref[cols, :])
                total = term if total is None else total + term
            put(cols, total)

    def hop(slot, src, dst, where):
        copy = pltpu.make_async_remote_copy(
            src_ref=src, dst_ref=dst, send_sem=send.at[slot], recv_sem=recv.at[slot],
            device_id=where, device_id_type=MESH,
        )
        return copy

    def to_sibling(slot, yy, xx):
        def put(cols, total):
            s_send[slot, :, cols] = total.astype(low)

        product(index(yy, xx, 1 - c), put)
        copy = hop(slot, s_send.at[slot], s_recv.at[slot], to_s)
        copy.start()
        return copy

    def with_sibling(slot, yy, xx, keep):
        def put(cols, total):
            keep[:, cols] = (total + s_recv[slot, :, cols].astype(f32)).astype(keep.dtype)

        product(index(yy, xx, c), put)

    greet((to_x, to_y, to_s))
    s0 = to_sibling(0, 1 - y, 1 - x)
    s1 = to_sibling(1, y, 1 - x)
    s0.wait_recv()
    with_sibling(0, 1 - y, 1 - x, d_send)
    d0 = hop(4, d_send.at[parts[0]], d_recv.at[parts[0]], to_x)
    d1 = hop(5, d_send.at[parts[1]], d_recv.at[parts[1]], to_y)
    d0.start()
    d1.start()
    s1.wait_recv()
    with_sibling(1, y, 1 - x, x_acc)
    x_send[parts[0]] = x_acc[parts[0]].astype(low)
    x0 = hop(6, x_send.at[parts[0]], x_recv.at[parts[0]], to_x)
    x0.start()
    s2 = to_sibling(2, 1 - y, x)
    s2.wait_recv()
    with_sibling(2, 1 - y, x, y_acc)
    y_send[parts[1]] = y_acc[parts[1]].astype(low)
    y1 = hop(7, y_send.at[parts[1]], y_recv.at[parts[1]], to_y)
    y1.start()
    s3 = to_sibling(3, y, x)
    d1.wait_recv()
    x_send[parts[1]] = (x_acc[parts[1]] + d_recv[parts[1]].astype(f32)).astype(low)
    x1 = hop(8, x_send.at[parts[1]], x_recv.at[parts[1]], to_x)
    x1.start()
    d0.wait_recv()
    y_send[parts[0]] = (y_acc[parts[0]] + d_recv[parts[0]].astype(f32)).astype(low)
    y0 = hop(9, y_send.at[parts[0]], y_recv.at[parts[0]], to_y)
    y0.start()
    s3.wait_recv()
    with_sibling(3, y, x, out)
    x0.wait_recv()
    y1.wait_recv()
    x1.wait_recv()
    y0.wait_recv()
    out[...] += x_recv[...].astype(f32) + y_recv[...].astype(f32)
    for copy in (s0, s1, s2, s3, d0, d1, x0, x1, y0, y1):
        copy.wait_send()


def plane_sum(lefts, rights, number, after=(), tile=512):
    ends = [(left, start) for left, a in enumerate(lefts) for start in range(0, a.shape[1], rights[0].shape[1])]
    terms = tuple(ends[: len(rights)])
    rows, width = lefts[0].shape[0] // 8, rights[0].shape[0]
    block = (rows, width)
    low, f32 = jnp.bfloat16, jnp.float32
    return pl.pallas_call(
        functools.partial(sum_kernel, len(lefts), terms, min(tile, width)),
        out_shape=jax.ShapeDtypeStruct(block, f32),
        in_specs=[VMEM] * (len(lefts) + len(rights)) + [HBM] * len(after),
        out_specs=VMEM,
        scratch_shapes=[
            pltpu.VMEM((4, *block), low),
            pltpu.VMEM((4, *block), low),
            *[pltpu.VMEM(block, low)] * 6,
            pltpu.VMEM(block, f32),
            pltpu.VMEM(block, f32),
            pltpu.SemaphoreType.DMA((10,)),
            pltpu.SemaphoreType.DMA((10,)),
        ],
        compiler_params=pltpu.CompilerParams(
            collective_id=number, has_side_effects=True, vmem_limit_bytes=48 * 2**20
        ),
        cost_estimate=pl.CostEstimate(flops=1, bytes_accessed=1, transcendentals=0),
        name="plane_sum",
    )(*lefts, *rights, *after)


def swap_kernel(pieces, takes, *refs):
    count = len(pieces)
    sources, (send, recv, own) = refs[: -2 * count - 3], refs[-3:]
    outs, holds = refs[-2 * count - 3 : -count - 3], refs[-count - 3 : -3]
    y, x, c, index = place()
    me = index(y, x, c)
    flips = [(fy, fx, fc) for fy, fx in ((1, 1), (0, 1), (1, 0), (0, 0)) for fc in (0, 1)]
    flips = [flip for flip in flips if flip != (0, 0, 0)]

    def there(flip):
        return tuple(1 - at if f else at for at, f in zip((y, x, c), flip))

    greet([dict(zip(("y", "x", "c"), there(flip))) for flip in flips])
    copies = []
    for piece in range(count):
        for number, flip in enumerate(flips):
            yy, xx, cc = there(flip)
            member = index(yy, xx, cc)
            holds[piece][number] = takes[piece](sources, member, cc)
            copy = pltpu.make_async_remote_copy(
                src_ref=holds[piece].at[number],
                dst_ref=outs[piece].at[me],
                send_sem=send.at[piece * 7 + number],
                recv_sem=recv.at[piece * 7 + number],
                device_id={"y": yy, "x": xx, "c": cc},
                device_id_type=MESH,
            )
            copy.start()
            copies.append(copy)
        holds[piece][7] = takes[piece](sources, me, c)
        keep = pltpu.make_async_copy(holds[piece].at[7], outs[piece].at[me], own.at[piece])
        keep.start()
        copies.append(keep)
    for copy in copies:
        copy.wait()


def plane_swap(sources, shapes, takes, number, after=()):
    low = jnp.bfloat16
    count = len(shapes)
    return pl.pallas_call(
        functools.partial(swap_kernel, shapes, takes),
        out_shape=[jax.ShapeDtypeStruct((8, *shape), low) for shape in shapes],
        in_specs=[VMEM] * len(sources) + [HBM] * len(after),
        out_specs=[HBM] * count,
        scratch_shapes=[
            *[pltpu.VMEM((8, *shape), low) for shape in shapes],
            pltpu.SemaphoreType.DMA((7 * count,)),
            pltpu.SemaphoreType.DMA((7 * count,)),
            pltpu.SemaphoreType.DMA((count,)),
        ],
        compiler_params=pltpu.CompilerParams(
            collective_id=number, has_side_effects=True, vmem_limit_bytes=48 * 2**20
        ),
        cost_estimate=pl.CostEstimate(flops=1, bytes_accessed=1, transcendentals=0),
        name="plane_swap",
    )(*sources, *after)


def team_of(y, x, c):
    flips = [(fy, fx, fc) for fy, fx in ((1, 1), (0, 1), (1, 0), (0, 0)) for fc in (0, 1)]
    return [
        tuple(1 - at if f else at for at, f in zip((y, x, c), flip)) for flip in flips if flip != (0, 0, 0)
    ]


def turn_kernel(planes, src, *refs):
    y, x, c, index = place()
    me = index(y, x, c)
    others = team_of(y, x, c)
    ids = [dict(zip(("y", "x", "c"), other)) for other in others]
    if planes:
        lines, out, total, near, far, held, send, recv, own, send_lines, recv_lines = refs[:1] + refs[-10:]
        z = lax.axis_index("z")
        column = [{"z": lax.rem(z + step, planes)} for step in range(1, planes)]
        fetch = pltpu.make_async_copy(src, held, own)
        fetch.start()
        fetch.wait()
        near[me] = lines[...]
        squares = jnp.zeros((8, held.shape[1]), jnp.float32)
        for start in range(0, held.shape[0], 64):
            part = held[start : start + 64].astype(jnp.float32)
            squares += jnp.sum(jnp.square(part).reshape(8, 8, -1), axis=0)
        near[me, 2:3] += jnp.sum(squares, keepdims=True)
    else:
        out, send, recv, own = refs[-4:]
        column = []
    greet(ids + column)
    count = src.shape[0] // 8

    def rows(member):
        return src.at[pl.ds(pl.multiple_of(member * count, count), count)]

    def spread(buffer, at, where, base):
        copies = [
            pltpu.make_async_remote_copy(
                src_ref=buffer.at[at],
                dst_ref=buffer.at[at],
                send_sem=send_lines.at[base + number],
                recv_sem=recv_lines.at[base + number],
                device_id=other,
                device_id_type=MESH,
            )
            for number, other in enumerate(where)
        ]
        for copy in copies:
            copy.start()
        return copies

    small = spread(near, me, ids, 0) if planes else []
    copies = [
        pltpu.make_async_remote_copy(
            src_ref=rows(index(*other)),
            dst_ref=out.at[me],
            send_sem=send.at[number],
            recv_sem=recv.at[number],
            device_id=where,
            device_id_type=MESH,
        )
        for number, (other, where) in enumerate(zip(others, ids))
    ]
    copies.append(pltpu.make_async_copy(rows(me), out.at[me], own))
    for copy in copies:
        copy.start()
    if planes:
        for copy in small:
            copy.wait()
        far[z] = jnp.sum(near[...], axis=0)
        for copy in spread(far, z, column, 7):
            copy.wait()
        total[...] = jnp.sum(far[...], axis=0)
    for copy in copies:
        copy.wait()


def turn(rows, number, after=(), lines=None, planes=0):
    block = (rows.shape[0] // 8, rows.shape[1])
    dma = pltpu.SemaphoreType.DMA
    out_shape, out_specs = [jax.ShapeDtypeStruct((8, *block), rows.dtype)], [HBM]
    in_specs, scratch = [HBM], [dma((7,)), dma((7,)), dma]
    operands = [rows]
    if planes:
        operands.append(lines)
        in_specs.append(VMEM)
        out_shape.append(jax.ShapeDtypeStruct(lines.shape, lines.dtype))
        out_specs.append(VMEM)
        buffers = [pltpu.VMEM((size, *lines.shape), lines.dtype) for size in (8, planes)]
        scratch = buffers + [pltpu.VMEM(rows.shape, rows.dtype)] + scratch + [dma((6 + planes,)), dma((6 + planes,))]
    return pl.pallas_call(
        functools.partial(turn_kernel, planes),
        out_shape=out_shape,
        in_specs=in_specs + [HBM] * len(after),
        out_specs=out_specs,
        scratch_shapes=scratch,
        compiler_params=pltpu.CompilerParams(
            collective_id=number, has_side_effects=True, vmem_limit_bytes=16 * 2**20
        ),
        cost_estimate=pl.CostEstimate(flops=1, bytes_accessed=1, transcendentals=0),
        name="turn",
    )(*operands, *after)


def hops(planes, send, recv, block, up):
    z = lax.axis_index("z")

    def step(number):
        gone, came = (z - number + 1, z - number) if up else (z + number - 1, z + number)
        goes = ((gone >= 0) & (z + 1 < planes)) if up else ((gone < planes) & (z >= 1))
        comes = (came >= 0) if up else (came < planes)

        def copy(b):
            return pltpu.make_async_remote_copy(
                src_ref=block(b),
                dst_ref=block(b),
                send_sem=send.at[number - 1],
                recv_sem=recv.at[number - 1],
                device_id={"z": z + 1 if up else z - 1},
                device_id_type=MESH,
            )

        return (
            lambda: pl.when(goes)(lambda: copy(gone).start()),
            lambda: pl.when(comes)(lambda: copy(came).wait_recv()),
            lambda: pl.when(goes)(lambda: copy(gone).wait_send()),
        )

    return [step(number) for number in range(1, planes)]


def ring(planes):
    z = lax.axis_index("z")
    return [{"z": lax.rem(z + 1, planes)}, {"z": lax.rem(z + planes - 1, planes)}]


def begin_kernel(
    planes, take_attention, take_gate_up, attention, feed, rows, all_attention, gate_up, all_rows,
    attention_hold, gate_up_hold, feed_hold, a_send, a_recv, g_send, g_recv, r_send, r_recv, u_send, u_recv, d_send, d_recv, own,
):
    y, x, c, index = place()
    z = lax.axis_index("z")
    me, at_x, at_y, at_d = index(y, x, c), index(y, 1 - x, c), index(1 - y, x, c), index(1 - y, 1 - x, c)
    others = team_of(y, x, c)
    ids = [dict(zip(("y", "x", "c"), other)) for other in others]
    to_x, to_y, to_s = {"x": 1 - x}, {"y": 1 - y}, {"c": 1 - c}
    count = attention.shape[0]

    def spread(source, take, hold, place_of, send, recv, local):
        copies = []
        for number, (other, where) in enumerate(zip(others, ids)):
            hold[number] = take([source], index(*other), other[2])
            copy = pltpu.make_async_remote_copy(
                src_ref=hold.at[number], dst_ref=place_of(me), send_sem=send.at[number], recv_sem=recv.at[number],
                device_id=where, device_id_type=MESH,
            )
            copy.start()
            copies.append(copy)
        hold[7] = take([source], me, c)
        keep = pltpu.make_async_copy(hold.at[7], place_of(me), local)
        keep.start()
        return copies, keep

    half = rows.shape[0] // 2
    parts = (pl.ds(0, half), pl.ds(half, half))

    def hop(slot, block, part, where, first=False):
        piece = all_rows.at[block, parts[part]]
        copy = pltpu.make_async_remote_copy(
            src_ref=rows.at[parts[part]] if first else piece, dst_ref=piece,
            send_sem=r_send.at[slot], recv_sem=r_recv.at[slot], device_id=where, device_id_type=MESH,
        )
        copy.start()
        return copy

    def attention_rows(start, size):
        return all_attention.at[pl.ds(pl.multiple_of(start, count), size)]

    fetch = pltpu.make_async_copy(feed.at[:, pl.ds(0, feed_hold.shape[1])], feed_hold, own.at[3])
    fetch.start()
    greet(ids + ring(planes))
    a_copies, a_keep = spread(
        attention, take_attention, attention_hold, lambda m: attention_rows((z * 8 + m) * count, count), a_send, a_recv, own.at[1]
    )
    for copy in a_copies:
        copy.wait_recv()
    a_keep.wait()

    def plane_block(b):
        return attention_rows(b * 8 * count, 8 * count)

    up = hops(planes, u_send, u_recv, plane_block, True)
    down = hops(planes, d_send, d_recv, plane_block, False)

    def pass_on(number):
        if number > 0:
            up[number - 1][1]()
            down[number - 1][1]()
        if number < planes - 1:
            up[number][0]()
            down[number][0]()

    pass_on(0)
    x0, y1 = hop(0, me, 0, to_x, True), hop(2, me, 1, to_y, True)
    x1, y0 = hop(1, me, 1, to_x, True), hop(3, me, 0, to_y, True)
    s0, s1 = hop(4, me, 0, to_s, True), hop(5, me, 1, to_s, True)
    mine = pltpu.make_async_copy(rows, all_rows.at[me], own.at[0])
    mine.start()
    fetch.wait()
    x0.wait_recv()
    d0 = hop(6, at_x, 0, to_y)
    y1.wait_recv()
    d1 = hop(7, at_y, 1, to_x)
    sx0, sy1 = hop(8, at_x, 0, to_s), hop(9, at_y, 1, to_s)
    g_copies, g_keep = spread(feed_hold, take_gate_up, gate_up_hold, lambda m: gate_up.at[m], g_send, g_recv, own.at[2])
    x1.wait_recv()
    sx1 = hop(10, at_x, 1, to_s)
    y0.wait_recv()
    sy0 = hop(11, at_y, 0, to_s)
    pass_on(1)
    d0.wait_recv()
    sd0 = hop(12, at_d, 0, to_s)
    d1.wait_recv()
    sd1 = hop(13, at_d, 1, to_s)
    for number in range(2, planes):
        pass_on(number)
    for copy in (s0, s1, sx0, sy1, sx1, sy0, sd0, sd1, *g_copies):
        copy.wait_recv()
    for copy in (x0, x1, y0, y1, s0, s1, d0, d1, sx0, sy1, sx1, sy0, sd0, sd1, *a_copies, *g_copies):
        copy.wait_send()
    for step in up + down:
        step[2]()
    g_keep.wait()
    mine.wait()


def begin(attention, feed, rows, takes, widths, planes, number):
    low, dma = jnp.bfloat16, pltpu.SemaphoreType.DMA
    count = attention.shape[0]
    return pl.pallas_call(
        functools.partial(begin_kernel, planes, *takes),
        out_shape=[
            jax.ShapeDtypeStruct((planes * 8 * count, widths[0]), low),
            jax.ShapeDtypeStruct((8, count, widths[1]), low),
            jax.ShapeDtypeStruct((8, *rows.shape), low),
        ],
        in_specs=[VMEM, HBM, VMEM],
        out_specs=[HBM] * 3,
        scratch_shapes=[pltpu.VMEM((8, count, width), low) for width in widths]
        + [pltpu.VMEM((count, 8 * widths[1]), feed.dtype)]
        + [dma((size,)) for size in (7, 7, 7, 7, 14, 14, *[planes - 1] * 4, 4)],
        compiler_params=pltpu.CompilerParams(
            collective_id=number, has_side_effects=True, vmem_limit_bytes=32 * 2**20
        ),
        cost_estimate=pl.CostEstimate(flops=1, bytes_accessed=1, transcendentals=0),
        name="begin",
    )(attention, feed, rows)


def climb_kernel(planes, block, mine, other, zeros, u_send, u_recv, s_send, s_recv, own, fill):
    z, c = lax.axis_index("z"), lax.axis_index("c")
    to_s = {"c": 1 - c}
    greet([to_s] + ring(planes))

    def across(n):
        return pltpu.make_async_remote_copy(
            src_ref=block if n == 0 else mine.at[n], dst_ref=other.at[n], send_sem=s_send.at[n], recv_sem=s_recv.at[n],
            device_id=to_s, device_id_type=MESH,
        )

    def along(n):
        return pltpu.make_async_remote_copy(
            src_ref=block if n == 1 else mine.at[n - 1], dst_ref=mine.at[n], send_sem=u_send.at[n - 1], recv_sem=u_recv.at[n - 1],
            device_id={"z": z + 1}, device_id_type=MESH,
        )

    keep = pltpu.make_async_copy(block, mine.at[0], own)
    more = z + 1 < planes
    pl.when(more)(lambda: along(1).start())
    across(0).start()
    keep.start()
    zeros[...] = jnp.zeros_like(zeros)
    for n in range(1, planes):

        @pl.when(z < n)
        def _():
            for number, buffer in enumerate((mine, other)):
                pltpu.make_async_copy(zeros, buffer.at[n], fill.at[2 * (n - 1) + number]).start()

    for n in range(1, planes):

        @pl.when(z >= n)
        def _():
            along(n).wait_recv()
            if n + 1 < planes:
                pl.when(more)(lambda: along(n + 1).start())
            across(n).start()

    across(0).wait()
    keep.wait()
    for n in range(1, planes):

        @pl.when(z >= n)
        def _():
            across(n).wait()

        @pl.when(z < n)
        def _():
            for number, buffer in enumerate((mine, other)):
                pltpu.make_async_copy(zeros, buffer.at[n], fill.at[2 * (n - 1) + number]).wait()

        pl.when((z >= n - 1) & more)(lambda: along(n).wait_send())


def climb(block, planes, number):
    dma = pltpu.SemaphoreType.DMA
    return pl.pallas_call(
        functools.partial(climb_kernel, planes),
        out_shape=[jax.ShapeDtypeStruct((planes, *block.shape), block.dtype)] * 2,
        in_specs=[VMEM],
        out_specs=[HBM] * 2,
        scratch_shapes=[pltpu.VMEM(block.shape, block.dtype)] + [dma((planes - 1,))] * 2 + [dma((planes,))] * 2 + [dma, dma((2 * (planes - 1),))],
        compiler_params=pltpu.CompilerParams(
            collective_id=number, has_side_effects=True, vmem_limit_bytes=16 * 2**20
        ),
        cost_estimate=pl.CostEstimate(flops=1, bytes_accessed=1, transcendentals=0),
        name="climb",
    )(block)


def dot(left, right, contract):
    return lax.dot_general(left, right, (contract, ((), ())), preferred_element_type=jnp.float32)


def mm(left, right):
    return dot(left, right, ((1,), (0,)))


def mm_nt(left, right):
    return dot(left, right, ((1,), (1,)))


def mm_tn(left, right):
    return dot(left, right, ((0,), (0,)))


def bmm(pattern, left, right):
    return jnp.einsum(pattern, left, right, preferred_element_type=jnp.float32)


def angle_tables(positions):
    half_dim = HEAD_SIZE // 2
    frequency = rope_base ** (-(jnp.arange(half_dim).astype(jnp.float32) * 2.0) / HEAD_SIZE)
    phases = positions.astype(jnp.float32)[:, None] * frequency[None, :]
    return (jnp.cos(phases), jnp.sin(phases))


def rotate(value, cos_table, sin_table):
    half = value.shape[-1] // 2
    a, b = value[..., :half], value[..., half:]
    return jnp.concatenate([a * cos_table - b * sin_table, b * cos_table + a * sin_table], axis=-1)


def rms_forward(value, gain_row):
    inverse = lax.rsqrt(jnp.mean(value * value, axis=-1, keepdims=True) + norm_eps)
    return (value * inverse * gain_row, inverse)


def rms_back(grad_out, value, inverse, gain_row):
    scaled = grad_out * gain_row
    grad_in = inverse * (
        scaled - value * inverse * inverse * jnp.mean(scaled * value, axis=-1, keepdims=True)
    )
    return (grad_in, jnp.sum(grad_out * value * inverse, axis=0))


def adamw(weight, gradient, moment_one, moment_two, step_rate, decay_rate, invert=jnp.reciprocal):
    mean_new = beta_one * moment_one + (1.0 - beta_one) * gradient
    square_new = beta_two * moment_two + (1.0 - beta_two) * gradient * gradient
    below = jnp.sqrt(square_new * (1.0 / (1.0 - beta_two**STEP))) + adam_eps
    direction = mean_new * (1.0 / (1.0 - beta_one**STEP)) * invert(below)
    return (weight - step_rate * (direction + decay_rate * weight), mean_new, square_new)


def attention_parts(core, length, q_ref, mine_ref, other_ref, query_ref, key_ref):
    mine, other = mine_ref[...].reshape(-1, HEAD_SIZE), other_ref[...].reshape(-1, HEAD_SIZE)
    first = core == 0
    k, v = jnp.where(first, mine, other), jnp.where(first, other, mine)
    q = q_ref[...].reshape(-1, HEAD_SIZE)
    at, key_at = query_ref[...], key_ref[...]
    allowed = (key_at <= at) & (key_at < length) & (key_at >= 0)
    scores = jnp.where(allowed, mm_nt(q, k) * HEAD_SIZE ** (-0.5), masked_value)
    exponent = jnp.exp(scores - jnp.max(scores, axis=-1, keepdims=True))
    return q, k, v, exponent / jnp.sum(exponent, axis=-1, keepdims=True)


def attention_kernel(core_ref, length_ref, q_ref, mine_ref, other_ref, query_ref, key_ref, out_ref):
    length = length_ref[pl.program_id(0)]
    _, _, v, soft = attention_parts(core_ref[0], length, q_ref, mine_ref, other_ref, query_ref, key_ref)
    out_ref[...] = mm(soft.astype(jnp.bfloat16), v).astype(jnp.bfloat16).reshape(out_ref.shape)


def attention_back_kernel(
    core_ref, length_ref, q_ref, mine_ref, other_ref, query_ref, key_ref, do_ref, cos_ref, sin_ref,
    dq_ref, keep_ref, send_ref,
):
    low = jnp.bfloat16
    core = core_ref[0]
    length = length_ref[pl.program_id(0)]
    q, k, v, soft = attention_parts(core, length, q_ref, mine_ref, other_ref, query_ref, key_ref)
    do = do_ref[...].reshape(-1, HEAD_SIZE)
    dp = mm_nt(do, v)
    delta = jnp.sum(soft * dp, axis=-1, keepdims=True)
    ds = (soft * (dp - delta) * HEAD_SIZE ** (-0.5)).astype(low)
    dq = mm(ds, k)
    cos_table, sin_table = cos_ref[...], sin_ref[...]
    half = HEAD_SIZE // 2
    a, b = dq[:, :half], dq[:, half:]
    turned = jnp.concatenate([a * cos_table + b * sin_table, b * cos_table - a * sin_table], axis=-1)
    dq_ref[...] = turned.astype(low).reshape(dq_ref.shape)
    dk, dv = mm_tn(ds, q), mm_tn(soft.astype(low), do)
    first = core == 0
    keep, send = (t.reshape(keep_ref.shape) for t in (jnp.where(first, dk, dv), jnp.where(first, dv, dk)))
    for block in range(keep_ref.shape[0]):
        at = core_ref[1 + block]
        keep_ref[at] = keep[block]
        send_ref[at] = send[block].astype(low)


def attention_call(kernel, core, lengths, q, mine, other, query_pos, key_pos, extra, outs, name):
    ny, count, span, size = q.shape
    nz = mine.shape[0]
    rows = pl.BlockSpec((ny, 1, span, size), lambda i, *_: (0, i, 0, 0))
    keys = pl.BlockSpec((nz, ny, 1, span, size), lambda i, *_: (0, 0, i, 0, 0))

    def whole(value):
        return pl.BlockSpec(value.shape, lambda i, *_: (0,) * value.ndim)

    kinds = {"rows": (rows, q.shape), "keys": (keys, mine.shape)}
    return pl.pallas_call(
        kernel,
        grid_spec=pltpu.PrefetchScalarGridSpec(
            num_scalar_prefetch=2,
            grid=(count,),
            in_specs=[rows, keys, keys, whole(query_pos), whole(key_pos)]
            + [rows if value.shape == q.shape else whole(value) for value in extra],
            out_specs=[kinds[kind][0] for kind, _ in outs],
        ),
        out_shape=[jax.ShapeDtypeStruct(kinds[kind][1], dtype) for kind, dtype in outs],
        compiler_params=pltpu.CompilerParams(vmem_limit_bytes=48 * 2**20),
        cost_estimate=pl.CostEstimate(flops=1, bytes_accessed=1, transcendentals=0),
        name=name,
    )(core, lengths, q, mine, other, query_pos, key_pos, *extra)


def feed_back_kernel(dyb_ref, weight_ref, gate_ref, up_ref, out_ref):
    dm = mm(dyb_ref[...], weight_ref[...])
    gate, upward = gate_ref[...], up_ref[...]
    sig = jax.nn.sigmoid(gate)
    part = gate.shape[1]
    out_ref[:, :part] = (dm * upward * sig * (1.0 + gate * (1.0 - sig))).astype(out_ref.dtype)
    out_ref[:, part:] = (dm * gate * sig).astype(out_ref.dtype)


def feed_back(dyb, weight, both, lines=256):
    count, part = both.shape[0], both.shape[1] // 2

    def rows(width, column=0):
        return pl.BlockSpec((lines, width), lambda i: (i, column))

    return pl.pallas_call(
        feed_back_kernel,
        grid=(count // lines,),
        in_specs=[rows(dyb.shape[1]), pl.BlockSpec(weight.shape, lambda i: (0, 0)), rows(part), rows(part, 1)],
        out_specs=rows(2 * part),
        out_shape=jax.ShapeDtypeStruct((count, 2 * part), jnp.bfloat16),
        compiler_params=pltpu.CompilerParams(vmem_limit_bytes=48 * 2**20),
        cost_estimate=pl.CostEstimate(flops=1, bytes_accessed=1, transcendentals=0),
        name="feed_back",
    )(dyb, weight, both, both)


def attention_part(step, grad_ref):
    parts = []
    for head in range(8):
        member = jnp.where(step == 1, 2 * (head % 4) + head // 4, head)
        parts.append(grad_ref[member, :, pl.ds(pl.multiple_of(step * HEAD_SIZE, HEAD_SIZE), HEAD_SIZE)])
    return jnp.concatenate(parts, axis=1)


def feed_part(step, gate_up_ref, down_ref):
    size = down_ref.shape[2]
    at = pl.ds(pl.multiple_of(jnp.minimum(step // 2, 1) * size, size), size)
    parts = []
    for number in range(4):
        member = 4 * (step % 2) + number
        parts.append(jnp.where(step < 4, gate_up_ref[member, :, at], down_ref[member]))
    return jnp.concatenate(parts, axis=1)


def close_reciprocal(value):
    guess = pltpu.reciprocal(value, approx=True)
    return guess * (2.0 - value * guess)


def norm_of(lines_ref):
    gains = lines_ref[0:2]
    return jnp.sqrt(jnp.sum(gains * gains, keepdims=True) + lines_ref[2:3, 0:1])


def update_gains_kernel(lines_ref, weight_ref, mean_ref, square_ref, new_ref, new_mean_ref, new_square_ref, norm_ref):
    norm = norm_of(lines_ref)
    norm_ref[...] = norm
    new_ref[...], new_mean_ref[...], new_square_ref[...] = adamw(
        weight_ref[...], lines_ref[0:2] * (clip_norm / norm), mean_ref[...], square_ref[...], gain_rate, 0.0
    )


def update_gains(lines, weight, mean, square):
    f32 = jnp.float32
    return pl.pallas_call(
        update_gains_kernel,
        in_specs=[VMEM] * 4,
        out_specs=[VMEM] * 4,
        out_shape=[jax.ShapeDtypeStruct(weight.shape, f32)] * 3 + [jax.ShapeDtypeStruct((1, 1), f32)],
        name="update_gains",
    )(lines, weight, mean, square)


def update_kernel(part, lines_ref, weight_ref, mean_ref, square_ref, *refs):
    grads, (new_ref, new_mean_ref, new_square_ref, copy_ref, factor_ref) = refs[:-5], refs[-5:]

    @pl.when(pl.program_id(0) == 0)
    def _():
        factor_ref[...] = clip_norm / norm_of(lines_ref)

    gradient = part(pl.program_id(0), *grads).astype(jnp.float32) * factor_ref[...]
    new, mean, square = adamw(
        weight_ref[...], gradient, mean_ref[...], square_ref[...], matrix_rate, weight_decay, close_reciprocal
    )
    new_ref[...] = new
    new_mean_ref[...] = mean
    new_square_ref[...] = square
    copy_ref[...] = new.astype(copy_ref.dtype)


def update(part, lines, weight, mean, square, grads):
    size = 2048 if part is attention_part else 4096
    rows, width = weight.shape
    block = pl.BlockSpec((rows, size), lambda i: (0, i))
    f32 = jnp.float32
    return pl.pallas_call(
        functools.partial(update_kernel, part),
        grid=(width // size,),
        in_specs=[pl.BlockSpec(lines.shape, lambda i: (0, 0)), block, block, block]
        + [pl.BlockSpec(grad.shape, lambda i: (0, 0, 0)) for grad in grads],
        out_specs=[block] * 4,
        out_shape=[jax.ShapeDtypeStruct(weight.shape, dtype) for dtype in (f32, f32, f32, jnp.bfloat16)],
        scratch_shapes=[pltpu.VMEM((1, 1), f32)],
        compiler_params=pltpu.CompilerParams(vmem_limit_bytes=48 * 2**20),
        name="update",
    )(lines, weight, mean, square, *grads)


def is_square():
    return lax.axis_size("y") == 2 and lax.axis_size("x") == 2


def swap(blocks):
    return lax.all_to_all(blocks, TEAM, split_axis=0, concat_axis=0, tiled=True)


def over_planes(blocks):
    return lax.all_gather(blocks.reshape(-1, blocks.shape[-1]), "z", axis=0, tiled=True)


def scatter_planes(term):
    return lax.psum_scatter(term, "z", scatter_dimension=0, tiled=True)


def together(*values):
    return lax.optimization_barrier(values)


def scatter_team(rows, number, after=()):
    if not is_square():
        return swap(rows.reshape(8, -1, rows.shape[-1]))
    return turn(rows, number, after)[0]


def team_gather(local, number, after=()):
    if not is_square():
        return lax.all_gather(local, TEAM, axis=0, tiled=True)
    return plane_gather(local, number, after).reshape(-1, local.shape[1])


def team_sum(lefts, rights, number, after=()):
    if is_square():
        return plane_sum(lefts, rights, number, after)
    partial = mm_nt(jnp.concatenate(lefts, axis=1), jnp.concatenate(rights, axis=1))
    return lax.psum_scatter(partial.astype(jnp.bfloat16), TEAM, scatter_dimension=0, tiled=True).astype(jnp.float32)


def local(
    tokens,
    lengths,
    norm_gains,
    attention_weight,
    feed_weight,
    cotangent,
    attention_mean,
    attention_square,
    feed_mean,
    feed_square,
    gain_mean,
    gain_square,
):
    low = jnp.bfloat16
    sequences, span, width = tokens.shape
    ny, nx, nz = lax.axis_size("y"), lax.axis_size("x"), lax.axis_size("z")
    team = ny * nx * 2
    core = lax.axis_index("c")
    rows = attention_weight.shape[0]
    q_width, kv_width = QUERY_HEADS * HEAD_SIZE, KEY_VALUE_HEADS * HEAD_SIZE
    count = sequences * span
    all_sequences = nx * 2 * sequences
    reach = ny * span
    near = is_square()
    ff_part = FF // team

    def columns(start, size):
        return pl.ds(pl.multiple_of(start, size), size)

    def take_attention(sources, member, c):
        source = sources[0]
        starts = (
            member * HEAD_SIZE,
            q_width + c * kv_width + (member - c) // 2 * HEAD_SIZE,
            q_width + 2 * kv_width + member * HEAD_SIZE,
        )
        return jnp.concatenate([source[:, columns(s, HEAD_SIZE)].astype(low) for s in starts], axis=1)

    def take_feed(*parts):
        return lambda sources, member, c: jnp.concatenate(
            [sources[0][:, columns(part * FF + member * ff_part, ff_part)].astype(low) for part in parts], axis=1
        )

    def spread(source, take, size, number, after=()):
        if is_square():
            blocks = plane_swap([source], [(rows, size)], [take], number, after)[0]
        else:
            blocks = swap(jnp.stack([take([source], member, member % 2) for member in range(8)]))
        return blocks, over_planes(blocks)

    team_base = lax.axis_index("z") * reach
    team_pos = team_base + jnp.arange(reach, dtype=jnp.int32)
    own_pos = team_base + lax.axis_index("y") * span + jnp.arange(span, dtype=jnp.int32)
    if near:
        key_pos = jnp.concatenate([team_pos - back * reach for back in range(nz)])
    else:
        key_pos = jnp.arange(nz * reach, dtype=jnp.int32)
    query_at, key_at = team_pos[:, None], key_pos[None, :]
    cos_table, sin_table = angle_tables(team_pos)
    cos_rows, sin_rows = (t.reshape(ny, 1, span, -1) for t in (cos_table, sin_table))
    valid = (own_pos[None, :] < lengths[:, None]).astype(jnp.float32).reshape(count, 1)
    lengths_all = lax.all_gather(lengths, ("x", "c"), axis=0, tiled=True)
    planes = jnp.arange(nz, dtype=jnp.int32)
    if near:
        planes = (lax.axis_index("z") - planes) % nz
    core_at = jnp.concatenate([jnp.reshape(core, (1,)), planes]).astype(jnp.int32)

    def heads(value):
        return value.reshape(ny, all_sequences, span, HEAD_SIZE)

    x_in = tokens.reshape(count, width).astype(jnp.float32)
    normed_one, inverse_one = rms_forward(x_in, norm_gains[0])
    outer_grad = cotangent.reshape(count, width).astype(jnp.float32) * valid
    if is_square():
        attention_mine, gate_up_blocks, h1 = begin(
            attention_weight,
            feed_weight,
            normed_one.astype(low),
            (take_attention, take_feed(0, 1)),
            (3 * HEAD_SIZE, 2 * ff_part),
            nz,
            1,
        )
        h1 = h1.reshape(-1, width)
    else:
        attention_mine = spread(attention_weight, take_attention, 3 * HEAD_SIZE, 1)[1]
        gate_up_blocks, gate_up_weight = spread(feed_weight, take_feed(0, 1), 2 * ff_part, 2)
        h1 = team_gather(normed_one.astype(low), 3)
    query_weight = attention_mine[:, :HEAD_SIZE]
    kv_weight = attention_mine[:, HEAD_SIZE : 2 * HEAD_SIZE]
    out_weight = attention_mine[:, 2 * HEAD_SIZE :]
    kv_raw = heads(mm(h1, kv_weight))
    kv = jnp.where(core == 0, rotate(kv_raw, cos_rows, sin_rows), kv_raw).astype(low)
    q = rotate(heads(mm(h1, query_weight)), cos_rows, sin_rows).astype(low)
    if is_square():
        kv, other = climb(kv, nz, 2)
        gate_up_blocks, kv = together(gate_up_blocks, kv)
        gate_up_weight = over_planes(gate_up_blocks)
    else:
        kv = lax.all_gather(kv, "z", axis=0, tiled=False)
        other = lax.ppermute(kv, "c", [(0, 1), (1, 0)])
    attend = (core_at, lengths_all, q, kv, other, query_at, key_at)
    (o,) = attention_call(attention_kernel, *attend, (), [("rows", low)], "attention")
    o = o.reshape(-1, HEAD_SIZE)
    r = x_in + team_sum([o], [out_weight], 4)

    normed_two, inverse_two = rms_forward(r, norm_gains[1])
    h2 = team_gather(normed_two.astype(low), 16)
    dyb = team_gather(outer_grad.astype(low), 15, [h2])
    down_blocks, down_weight = spread(feed_weight, take_feed(2), ff_part, 12, [dyb])
    gate_up_weight, down_blocks = together(gate_up_weight, down_blocks)
    both = mm(h2, gate_up_weight)
    gate, upward = both[:, :ff_part], both[:, ff_part:]
    sig = jax.nn.sigmoid(gate)
    m = (gate * sig * upward).astype(low)
    down_term = mm_tn(dyb, m).astype(low)
    down_rows = scatter_planes(down_term)
    down_weight, down_term = together(down_weight, down_term)
    d_both = feed_back(dyb, down_weight, both)
    gate_up_term = mm_tn(h2, d_both).astype(low)
    gate_up_rows = scatter_planes(gate_up_term)
    dh2 = team_sum([d_both], [gate_up_weight], 7, [gate_up_term, down_term])
    mid_grad, gain_two = rms_back(dh2, r, inverse_two, norm_gains[1])
    dr = outer_grad + mid_grad
    drb = team_gather(dr.astype(low), 13, [down_rows])

    do = heads(mm(drb, out_weight).astype(low))
    dq, keep, theirs = attention_call(
        attention_back_kernel,
        *attend,
        (do, cos_table, sin_table),
        [("rows", low), ("keys", jnp.float32), ("keys", low)],
        "attention_back",
    )
    dq = dq.reshape(-1, HEAD_SIZE)
    dkv = keep + lax.ppermute(theirs, "c", [(0, 1), (1, 0)]).astype(jnp.float32)
    low_terms = dkv.astype(low)
    feed_sum = team_sum([m], [down_weight], 5, [low_terms])
    down_grad = scatter_team(down_rows, 6, [low_terms])
    dkv = lax.psum_scatter(low_terms, "z", scatter_dimension=0, tiled=True)[0]
    gate_up_grad = scatter_team(gate_up_rows, 8, [feed_sum, down_grad])
    dkv, gate_up_grad = together(dkv, gate_up_grad)
    dkv = dkv.astype(jnp.float32)
    dkv = jnp.where(core == 0, rotate(dkv, cos_rows, -sin_rows), dkv).astype(low).reshape(-1, HEAD_SIZE)
    layer_output = (r + feed_sum).astype(low)
    attention_term = jnp.concatenate([mm_tn(h1, dq), mm_tn(h1, dkv), mm_tn(drb, o)], axis=1).astype(low)
    attention_rows = scatter_planes(attention_term)
    dh1 = team_sum([dq, dkv], [query_weight, kv_weight], 9, [attention_term])
    in_grad, gain_one = rms_back(dh1, x_in, inverse_one, norm_gains[0])
    input_gradient = dr + in_grad
    local_squares = sum(jnp.sum(jnp.square(part.astype(jnp.float32))) for part in (gate_up_rows, down_rows))
    squares_line = jnp.full((6, width), local_squares)
    lines = jnp.concatenate([jnp.stack([gain_one, gain_two]), squares_line], axis=0)
    if is_square():
        attention_grad, lines = turn(attention_rows, 10, (), lines, nz)
    else:
        attention_grad = scatter_team(attention_rows, 10)
        lines = lines.at[2:].add(jnp.sum(jnp.square(attention_rows.astype(jnp.float32))))
        lines = lax.psum(lines, ALL)
    feed_new = update(feed_part, lines, feed_weight, feed_mean, feed_square, [gate_up_grad, down_grad])
    attention_new = update(attention_part, lines, attention_weight, attention_mean, attention_square, [attention_grad])
    *gains_new, gradient_norm = update_gains(lines, norm_gains, gain_mean, gain_square)
    return (
        layer_output.reshape(sequences, span, width),
        input_gradient.reshape(sequences, span, width),
        gradient_norm.reshape(()),
        *attention_new,
        *feed_new,
        *gains_new,
    )


def solution(mesh):
    ctx, fsdp = mesh.shape["ctx"], mesh.shape["fsdp"]
    inner = QUERY_HEADS // fsdp
    fine = Mesh(mesh.devices.reshape(ctx // inner, inner, fsdp // 2, 2), ALL)
    act = P(("x", "c"), ("z", "y"), None)
    matrix = P(ALL, None)
    return jax.shard_map(
        local,
        mesh=fine,
        in_specs=(act, P(("x", "c")), P(), matrix, matrix, act, matrix, matrix, matrix, matrix, P(), P()),
        out_specs=(act, act, P(), matrix, matrix, matrix, matrix, matrix, matrix, matrix, matrix, P(), P(), P()),
        check_vma=False,
    )
```

```python
import functools

import jax
import jax.numpy as jnp
from jax import lax
from jax.experimental import pallas as pl
from jax.experimental.pallas import tpu as pltpu
from jax.sharding import Mesh, PartitionSpec as P

QUERY_HEADS = 8
KEY_VALUE_HEADS = 4
HEAD_SIZE = 256
FF = 8192
STEP = 10

norm_eps = 1e-06
rope_base = 1000042.0
masked_value = -1e30
clip_norm = 1.0
beta_one = 0.9
beta_two = 0.95
adam_eps = 1e-08
matrix_rate = 0.03
gain_rate = 0.4
weight_decay = 0.1

TEAM = ("y", "x", "c")
ALL = ("z", "y", "x", "c")


MESH = pl.DeviceIdType.MESH
VMEM = pl.BlockSpec(memory_space=pltpu.VMEM)
HBM = pl.BlockSpec(memory_space=pl.ANY)


def place():
    y, x, c = lax.axis_index("y"), lax.axis_index("x"), lax.axis_index("c")
    return y, x, c, lambda yy, xx, cc: (yy * 2 + xx) * 2 + cc


def greet(others):
    barrier = pltpu.get_barrier_semaphore()
    for other in others:
        pl.semaphore_signal(barrier, inc=1, device_id=other, device_id_type=MESH)
    pl.semaphore_wait(barrier, len(others))


def gather_kernel(src, *refs):
    out, send, recv, own = refs[-4:]
    y, x, c, index = place()
    to_x, to_y, to_s = {"x": 1 - x}, {"y": 1 - y}, {"c": 1 - c}
    me, at_x, at_y, at_d = index(y, x, c), index(y, 1 - x, c), index(1 - y, x, c), index(1 - y, 1 - x, c)
    half = src.shape[0] // 2
    rows = (pl.ds(0, half), pl.ds(half, half))
    local = pltpu.make_async_copy(src, out.at[me], own)
    local.start()
    greet((to_x, to_y, to_s))

    def hop(slot, block, part, where, first=False):
        piece = out.at[block, rows[part]]
        return pltpu.make_async_remote_copy(
            src_ref=src.at[rows[part]] if first else piece,
            dst_ref=piece,
            send_sem=send.at[slot],
            recv_sem=recv.at[slot],
            device_id=where,
            device_id_type=MESH,
        )

    x0, x1 = hop(0, me, 0, to_x, True), hop(1, me, 1, to_x, True)
    y1, y0 = hop(2, me, 1, to_y, True), hop(3, me, 0, to_y, True)
    s0, s1 = hop(4, me, 0, to_s, True), hop(5, me, 1, to_s, True)
    for copy in (x0, y1, x1, y0, s0, s1):
        copy.start()
    x0.wait_recv()
    d0 = hop(6, at_x, 0, to_y)
    d0.start()
    y1.wait_recv()
    d1 = hop(7, at_y, 1, to_x)
    d1.start()
    sx0, sy1 = hop(8, at_x, 0, to_s), hop(9, at_y, 1, to_s)
    sx0.start()
    sy1.start()
    x1.wait_recv()
    sx1 = hop(10, at_x, 1, to_s)
    sx1.start()
    y0.wait_recv()
    sy0 = hop(11, at_y, 0, to_s)
    sy0.start()
    d0.wait_recv()
    sd0 = hop(12, at_d, 0, to_s)
    sd0.start()
    d1.wait_recv()
    sd1 = hop(13, at_d, 1, to_s)
    sd1.start()
    for copy in (s0, s1, sx0, sy1, sx1, sy0, sd0, sd1):
        copy.wait_recv()
    for copy in (x0, x1, y0, y1, s0, s1, d0, d1, sx0, sy1, sx1, sy0, sd0, sd1):
        copy.wait_send()
    local.wait()


def plane_gather(value, number, after=()):
    return pl.pallas_call(
        gather_kernel,
        out_shape=jax.ShapeDtypeStruct((8, *value.shape), value.dtype),
        in_specs=[VMEM] + [HBM] * len(after),
        out_specs=HBM,
        scratch_shapes=[
            pltpu.SemaphoreType.DMA((14,)),
            pltpu.SemaphoreType.DMA((14,)),
            pltpu.SemaphoreType.DMA,
        ],
        compiler_params=pltpu.CompilerParams(collective_id=number, has_side_effects=True),
        cost_estimate=pl.CostEstimate(flops=1, bytes_accessed=1, transcendentals=0),
        name="plane_gather",
    )(value, *after)


def sum_kernel(lefts, terms, tile, *refs):
    a_refs, w_refs = refs[:lefts], refs[lefts : lefts + len(terms)]
    out, s_send, s_recv, d_send, d_recv, x_send, x_recv, y_send, y_recv, x_acc, y_acc, send, recv = refs[-13:]
    y, x, c, index = place()
    to_x, to_y, to_s = {"x": 1 - x}, {"y": 1 - y}, {"c": 1 - c}
    rows, width = out.shape
    half = rows // 2
    parts = (pl.ds(0, half), pl.ds(half, half))
    f32, low = jnp.float32, jnp.bfloat16

    def product(block, put):
        lines = pl.ds(pl.multiple_of(block * rows, rows), rows)

        @pl.loop(0, width // tile)
        def _(step):
            cols = pl.ds(pl.multiple_of(step * tile, tile), tile)
            total = None
            for (left, start), w_ref in zip(terms, w_refs):
                term = mm_nt(a_refs[left][lines, start : start + w_ref.shape[1]], w_ref[cols, :])
                total = term if total is None else total + term
            put(cols, total)

    def hop(slot, src, dst, where):
        copy = pltpu.make_async_remote_copy(
            src_ref=src, dst_ref=dst, send_sem=send.at[slot], recv_sem=recv.at[slot],
            device_id=where, device_id_type=MESH,
        )
        return copy

    def to_sibling(slot, yy, xx):
        def put(cols, total):
            s_send[slot, :, cols] = total.astype(low)

        product(index(yy, xx, 1 - c), put)
        copy = hop(slot, s_send.at[slot], s_recv.at[slot], to_s)
        copy.start()
        return copy

    def with_sibling(slot, yy, xx, keep):
        def put(cols, total):
            keep[:, cols] = (total + s_recv[slot, :, cols].astype(f32)).astype(keep.dtype)

        product(index(yy, xx, c), put)

    greet((to_x, to_y, to_s))
    s0 = to_sibling(0, 1 - y, 1 - x)
    s1 = to_sibling(1, y, 1 - x)
    s0.wait_recv()
    with_sibling(0, 1 - y, 1 - x, d_send)
    d0 = hop(4, d_send.at[parts[0]], d_recv.at[parts[0]], to_x)
    d1 = hop(5, d_send.at[parts[1]], d_recv.at[parts[1]], to_y)
    d0.start()
    d1.start()
    s1.wait_recv()
    with_sibling(1, y, 1 - x, x_acc)
    x_send[parts[0]] = x_acc[parts[0]].astype(low)
    x0 = hop(6, x_send.at[parts[0]], x_recv.at[parts[0]], to_x)
    x0.start()
    s2 = to_sibling(2, 1 - y, x)
    s2.wait_recv()
    with_sibling(2, 1 - y, x, y_acc)
    y_send[parts[1]] = y_acc[parts[1]].astype(low)
    y1 = hop(7, y_send.at[parts[1]], y_recv.at[parts[1]], to_y)
    y1.start()
    s3 = to_sibling(3, y, x)
    d1.wait_recv()
    x_send[parts[1]] = (x_acc[parts[1]] + d_recv[parts[1]].astype(f32)).astype(low)
    x1 = hop(8, x_send.at[parts[1]], x_recv.at[parts[1]], to_x)
    x1.start()
    d0.wait_recv()
    y_send[parts[0]] = (y_acc[parts[0]] + d_recv[parts[0]].astype(f32)).astype(low)
    y0 = hop(9, y_send.at[parts[0]], y_recv.at[parts[0]], to_y)
    y0.start()
    s3.wait_recv()
    with_sibling(3, y, x, out)
    x0.wait_recv()
    y1.wait_recv()
    x1.wait_recv()
    y0.wait_recv()
    out[...] += x_recv[...].astype(f32) + y_recv[...].astype(f32)
    for copy in (s0, s1, s2, s3, d0, d1, x0, x1, y0, y1):
        copy.wait_send()


def plane_sum(lefts, rights, number, after=(), tile=512):
    ends = [(left, start) for left, a in enumerate(lefts) for start in range(0, a.shape[1], rights[0].shape[1])]
    terms = tuple(ends[: len(rights)])
    rows, width = lefts[0].shape[0] // 8, rights[0].shape[0]
    block = (rows, width)
    low, f32 = jnp.bfloat16, jnp.float32
    return pl.pallas_call(
        functools.partial(sum_kernel, len(lefts), terms, min(tile, width)),
        out_shape=jax.ShapeDtypeStruct(block, f32),
        in_specs=[VMEM] * (len(lefts) + len(rights)) + [HBM] * len(after),
        out_specs=VMEM,
        scratch_shapes=[
            pltpu.VMEM((4, *block), low),
            pltpu.VMEM((4, *block), low),
            *[pltpu.VMEM(block, low)] * 6,
            pltpu.VMEM(block, f32),
            pltpu.VMEM(block, f32),
            pltpu.SemaphoreType.DMA((10,)),
            pltpu.SemaphoreType.DMA((10,)),
        ],
        compiler_params=pltpu.CompilerParams(
            collective_id=number, has_side_effects=True, vmem_limit_bytes=48 * 2**20
        ),
        cost_estimate=pl.CostEstimate(flops=1, bytes_accessed=1, transcendentals=0),
        name="plane_sum",
    )(*lefts, *rights, *after)


def swap_kernel(pieces, takes, *refs):
    count = len(pieces)
    sources, (send, recv, own) = refs[: -2 * count - 3], refs[-3:]
    outs, holds = refs[-2 * count - 3 : -count - 3], refs[-count - 3 : -3]
    y, x, c, index = place()
    me = index(y, x, c)
    flips = [(fy, fx, fc) for fy, fx in ((1, 1), (0, 1), (1, 0), (0, 0)) for fc in (0, 1)]
    flips = [flip for flip in flips if flip != (0, 0, 0)]

    def there(flip):
        return tuple(1 - at if f else at for at, f in zip((y, x, c), flip))

    greet([dict(zip(("y", "x", "c"), there(flip))) for flip in flips])
    copies = []
    for piece in range(count):
        for number, flip in enumerate(flips):
            yy, xx, cc = there(flip)
            member = index(yy, xx, cc)
            holds[piece][number] = takes[piece](sources, member, cc)
            copy = pltpu.make_async_remote_copy(
                src_ref=holds[piece].at[number],
                dst_ref=outs[piece].at[me],
                send_sem=send.at[piece * 7 + number],
                recv_sem=recv.at[piece * 7 + number],
                device_id={"y": yy, "x": xx, "c": cc},
                device_id_type=MESH,
            )
            copy.start()
            copies.append(copy)
        holds[piece][7] = takes[piece](sources, me, c)
        keep = pltpu.make_async_copy(holds[piece].at[7], outs[piece].at[me], own.at[piece])
        keep.start()
        copies.append(keep)
    for copy in copies:
        copy.wait()


def plane_swap(sources, shapes, takes, number, after=()):
    low = jnp.bfloat16
    count = len(shapes)
    return pl.pallas_call(
        functools.partial(swap_kernel, shapes, takes),
        out_shape=[jax.ShapeDtypeStruct((8, *shape), low) for shape in shapes],
        in_specs=[VMEM] * len(sources) + [HBM] * len(after),
        out_specs=[HBM] * count,
        scratch_shapes=[
            *[pltpu.VMEM((8, *shape), low) for shape in shapes],
            pltpu.SemaphoreType.DMA((7 * count,)),
            pltpu.SemaphoreType.DMA((7 * count,)),
            pltpu.SemaphoreType.DMA((count,)),
        ],
        compiler_params=pltpu.CompilerParams(
            collective_id=number, has_side_effects=True, vmem_limit_bytes=48 * 2**20
        ),
        cost_estimate=pl.CostEstimate(flops=1, bytes_accessed=1, transcendentals=0),
        name="plane_swap",
    )(*sources, *after)


def team_of(y, x, c):
    flips = [(fy, fx, fc) for fy, fx in ((1, 1), (0, 1), (1, 0), (0, 0)) for fc in (0, 1)]
    return [
        tuple(1 - at if f else at for at, f in zip((y, x, c), flip)) for flip in flips if flip != (0, 0, 0)
    ]


def turn_kernel(planes, src, *refs):
    y, x, c, index = place()
    me = index(y, x, c)
    others = team_of(y, x, c)
    ids = [dict(zip(("y", "x", "c"), other)) for other in others]
    if planes:
        out, total, near, far, held, send, recv, own, send_lines, recv_lines = refs[-10:]
        z = lax.axis_index("z")
        column = [{"z": lax.rem(z + step, planes)} for step in range(1, planes)]
        fetch = pltpu.make_async_copy(src, held, own)
        fetch.start()
        fetch.wait()
        squares = jnp.zeros((8, held.shape[1]), jnp.float32)
        for start in range(0, held.shape[0], 64):
            part = held[start : start + 64].astype(jnp.float32)
            squares += jnp.sum(jnp.square(part).reshape(8, 8, -1), axis=0)
        near[me] = jnp.broadcast_to(jnp.sum(squares, keepdims=True), near.shape[1:])
    else:
        out, send, recv, own = refs[-4:]
        column = []
    greet(ids + column)
    count = src.shape[0] // 8

    def rows(member):
        return src.at[pl.ds(pl.multiple_of(member * count, count), count)]

    def spread(buffer, at, where, base):
        copies = [
            pltpu.make_async_remote_copy(
                src_ref=buffer.at[at],
                dst_ref=buffer.at[at],
                send_sem=send_lines.at[base + number],
                recv_sem=recv_lines.at[base + number],
                device_id=other,
                device_id_type=MESH,
            )
            for number, other in enumerate(where)
        ]
        for copy in copies:
            copy.start()
        return copies

    small = spread(near, me, ids, 0) if planes else []
    copies = [
        pltpu.make_async_remote_copy(
            src_ref=rows(index(*other)),
            dst_ref=out.at[me],
            send_sem=send.at[number],
            recv_sem=recv.at[number],
            device_id=where,
            device_id_type=MESH,
        )
        for number, (other, where) in enumerate(zip(others, ids))
    ]
    copies.append(pltpu.make_async_copy(rows(me), out.at[me], own))
    for copy in copies:
        copy.start()
    if planes:
        for copy in small:
            copy.wait()
        far[z] = jnp.sum(near[...], axis=0)
        for copy in spread(far, z, column, 7):
            copy.wait()
        total[...] = jnp.sum(far[...], axis=0)
    for copy in copies:
        copy.wait()


def total_kernel(planes, src, *refs):
    out, near, far, send, recv = refs[-5:]
    y, x, c, index = place()
    z = lax.axis_index("z")
    ids = [dict(zip(("y", "x", "c"), other)) for other in team_of(y, x, c)]
    column = [{"z": lax.rem(z + step, planes)} for step in range(1, planes)]
    me = index(y, x, c)
    near[me] = src[...]
    greet(ids + column)

    def spread(buffer, at, where, base):
        copies = [
            pltpu.make_async_remote_copy(
                src_ref=buffer.at[at],
                dst_ref=buffer.at[at],
                send_sem=send.at[base + number],
                recv_sem=recv.at[base + number],
                device_id=other,
                device_id_type=MESH,
            )
            for number, other in enumerate(where)
        ]
        for copy in copies:
            copy.start()
        for copy in copies:
            copy.wait()

    spread(near, me, ids, 0)
    far[z] = jnp.sum(near[...], axis=0)
    spread(far, z, column, 7)
    out[...] = jnp.sum(far[...], axis=0)


def total_sum(value, planes, number, after=()):
    return pl.pallas_call(
        functools.partial(total_kernel, planes),
        out_shape=jax.ShapeDtypeStruct(value.shape, value.dtype),
        in_specs=[VMEM] + [HBM] * len(after),
        out_specs=VMEM,
        scratch_shapes=[pltpu.VMEM((size, *value.shape), value.dtype) for size in (8, planes)]
        + [pltpu.SemaphoreType.DMA((6 + planes,))] * 2,
        compiler_params=pltpu.CompilerParams(
            collective_id=number, has_side_effects=True, vmem_limit_bytes=16 * 2**20
        ),
        cost_estimate=pl.CostEstimate(flops=1, bytes_accessed=1, transcendentals=0),
        name="total_sum",
    )(value, *after)


def turn(rows, number, after=(), planes=0):
    block = (rows.shape[0] // 8, rows.shape[1])
    dma = pltpu.SemaphoreType.DMA
    out_shape, out_specs = [jax.ShapeDtypeStruct((8, *block), rows.dtype)], [HBM]
    scratch = [dma((7,)), dma((7,)), dma]
    if planes:
        tile = jax.ShapeDtypeStruct((8, 128), jnp.float32)
        out_shape.append(tile)
        out_specs.append(VMEM)
        buffers = [pltpu.VMEM((size, *tile.shape), tile.dtype) for size in (8, planes)]
        scratch = buffers + [pltpu.VMEM(rows.shape, rows.dtype)] + scratch + [dma((6 + planes,)), dma((6 + planes,))]
    return pl.pallas_call(
        functools.partial(turn_kernel, planes),
        out_shape=out_shape,
        in_specs=[HBM] * (1 + len(after)),
        out_specs=out_specs,
        scratch_shapes=scratch,
        compiler_params=pltpu.CompilerParams(
            collective_id=number, has_side_effects=True, vmem_limit_bytes=16 * 2**20
        ),
        cost_estimate=pl.CostEstimate(flops=1, bytes_accessed=1, transcendentals=0),
        name="turn",
    )(rows, *after)


def hops(planes, send, recv, block, up):
    z = lax.axis_index("z")

    def step(number):
        gone, came = (z - number + 1, z - number) if up else (z + number - 1, z + number)
        goes = ((gone >= 0) & (z + 1 < planes)) if up else ((gone < planes) & (z >= 1))
        comes = (came >= 0) if up else (came < planes)

        def copy(b):
            return pltpu.make_async_remote_copy(
                src_ref=block(b),
                dst_ref=block(b),
                send_sem=send.at[number - 1],
                recv_sem=recv.at[number - 1],
                device_id={"z": z + 1 if up else z - 1},
                device_id_type=MESH,
            )

        return (
            lambda: pl.when(goes)(lambda: copy(gone).start()),
            lambda: pl.when(comes)(lambda: copy(came).wait_recv()),
            lambda: pl.when(goes)(lambda: copy(gone).wait_send()),
        )

    return [step(number) for number in range(1, planes)]


def ring(planes):
    z = lax.axis_index("z")
    return [{"z": lax.rem(z + 1, planes)}, {"z": lax.rem(z + planes - 1, planes)}]


def spread_to(others, ids, source, take, hold, place_of, send, recv, own):
    y, x, c, index = place()
    me = index(y, x, c)
    copies = []
    for number, (other, where) in enumerate(zip(others, ids)):
        hold[number] = take([source], index(*other), other[2])
        copy = pltpu.make_async_remote_copy(
            src_ref=hold.at[number], dst_ref=place_of(me), send_sem=send.at[number], recv_sem=recv.at[number],
            device_id=where, device_id_type=MESH,
        )
        copy.start()
        copies.append(copy)
    hold[7] = take([source], me, c)
    keep = pltpu.make_async_copy(hold.at[7], place_of(me), own)
    keep.start()
    return copies, keep


def begin_kernel(
    planes, take, attention, tokens, gain, all_attention, all_rows,
    held, hold, rows, a_send, a_recv, r_send, r_recv, u_send, u_recv, d_send, d_recv, own,
):
    y, x, c, index = place()
    z = lax.axis_index("z")
    me, at_x, at_y, at_d = index(y, x, c), index(y, 1 - x, c), index(1 - y, x, c), index(1 - y, 1 - x, c)
    others = team_of(y, x, c)
    ids = [dict(zip(("y", "x", "c"), other)) for other in others]
    to_x, to_y, to_s = {"x": 1 - x}, {"y": 1 - y}, {"c": 1 - c}
    count = held.shape[0]
    half = rows.shape[0] // 2
    parts = (pl.ds(0, half), pl.ds(half, half))
    fetch = pltpu.make_async_copy(attention, held, own.at[0])
    fetch.start()
    greet(ids + ring(planes))
    fetch.wait()

    def attention_rows(start, size):
        return all_attention.at[pl.ds(pl.multiple_of(start, count), size)]

    a_copies, a_keep = spread_to(
        others, ids, held, take, hold, lambda m: attention_rows((z * 8 + m) * count, count), a_send, a_recv, own.at[1]
    )
    for start in range(0, rows.shape[0], 32):
        lines = pl.ds(start, 32)
        rows[lines] = rms_forward(tokens[lines].astype(jnp.float32), gain[...])[0].astype(rows.dtype)

    def hop(slot, block, part, where, first=False):
        piece = all_rows.at[block, parts[part]]
        copy = pltpu.make_async_remote_copy(
            src_ref=rows.at[parts[part]] if first else piece, dst_ref=piece,
            send_sem=r_send.at[slot], recv_sem=r_recv.at[slot], device_id=where, device_id_type=MESH,
        )
        copy.start()
        return copy

    for copy in a_copies:
        copy.wait_recv()
    a_keep.wait()

    def plane_block(b):
        return attention_rows(b * 8 * count, 8 * count)

    up = hops(planes, u_send, u_recv, plane_block, True)
    down = hops(planes, d_send, d_recv, plane_block, False)

    def pass_on(number):
        if number > 0:
            up[number - 1][1]()
            down[number - 1][1]()
        if number < planes - 1:
            up[number][0]()
            down[number][0]()

    pass_on(0)
    x0, y1 = hop(0, me, 0, to_x, True), hop(2, me, 1, to_y, True)
    x1, y0 = hop(1, me, 1, to_x, True), hop(3, me, 0, to_y, True)
    s0, s1 = hop(4, me, 0, to_s, True), hop(5, me, 1, to_s, True)
    mine = pltpu.make_async_copy(rows, all_rows.at[me], own.at[2])
    mine.start()
    x0.wait_recv()
    d0 = hop(6, at_x, 0, to_y)
    y1.wait_recv()
    d1 = hop(7, at_y, 1, to_x)
    sx0, sy1 = hop(8, at_x, 0, to_s), hop(9, at_y, 1, to_s)
    pass_on(1)
    x1.wait_recv()
    sx1 = hop(10, at_x, 1, to_s)
    y0.wait_recv()
    sy0 = hop(11, at_y, 0, to_s)
    d0.wait_recv()
    sd0 = hop(12, at_d, 0, to_s)
    d1.wait_recv()
    sd1 = hop(13, at_d, 1, to_s)
    for number in range(2, planes):
        pass_on(number)
    for copy in (s0, s1, sx0, sy1, sx1, sy0, sd0, sd1):
        copy.wait_recv()
    for copy in (x0, x1, y0, y1, s0, s1, d0, d1, sx0, sy1, sx1, sy0, sd0, sd1, *a_copies):
        copy.wait_send()
    for step in up + down:
        step[2]()
    mine.wait()


def begin(attention, tokens, gain, take, columns, planes, number):
    low, dma = jnp.bfloat16, pltpu.SemaphoreType.DMA
    count = attention.shape[0]
    return pl.pallas_call(
        functools.partial(begin_kernel, planes, take),
        out_shape=[
            jax.ShapeDtypeStruct((planes * 8 * count, columns), low),
            jax.ShapeDtypeStruct((8, *tokens.shape), low),
        ],
        in_specs=[HBM, VMEM, VMEM],
        out_specs=[HBM] * 2,
        scratch_shapes=[
            pltpu.VMEM(attention.shape, attention.dtype),
            pltpu.VMEM((8, count, columns), low),
            pltpu.VMEM(tokens.shape, low),
            *[dma((size,)) for size in (7, 7, 14, 14, *[planes - 1] * 4, 3)],
        ],
        compiler_params=pltpu.CompilerParams(
            collective_id=number, has_side_effects=True, vmem_limit_bytes=32 * 2**20
        ),
        cost_estimate=pl.CostEstimate(flops=1, bytes_accessed=1, transcendentals=0),
        name="begin",
    )(attention, tokens, gain)


def climb_kernel(
    planes, take, block, feed, mine, other, columns, zeros, held, hold, u_send, u_recv, s_send, s_recv, f_send, f_recv, own, fill
):
    y, x, c, index = place()
    z = lax.axis_index("z")
    to_s = {"c": 1 - c}
    others = team_of(y, x, c)
    ids = [dict(zip(("y", "x", "c"), where)) for where in others]
    fetch = pltpu.make_async_copy(feed.at[:, pl.ds(0, held.shape[1])], held, own.at[1])
    fetch.start()
    greet(ids + ring(planes))

    def across(n):
        return pltpu.make_async_remote_copy(
            src_ref=block if n == 0 else mine.at[n], dst_ref=other.at[n], send_sem=s_send.at[n], recv_sem=s_recv.at[n],
            device_id=to_s, device_id_type=MESH,
        )

    def along(n):
        return pltpu.make_async_remote_copy(
            src_ref=block if n == 1 else mine.at[n - 1], dst_ref=mine.at[n], send_sem=u_send.at[n - 1], recv_sem=u_recv.at[n - 1],
            device_id={"z": z + 1}, device_id_type=MESH,
        )

    keep = pltpu.make_async_copy(block, mine.at[0], own.at[0])
    more = z + 1 < planes
    pl.when(more)(lambda: along(1).start())
    across(0).start()
    keep.start()
    zeros[...] = jnp.zeros_like(zeros)
    for n in range(1, planes):

        @pl.when(z < n)
        def _():
            for number, buffer in enumerate((mine, other)):
                pltpu.make_async_copy(zeros, buffer.at[n], fill.at[2 * (n - 1) + number]).start()

    fetch.wait()
    f_copies, f_keep = spread_to(others, ids, held, take, hold, lambda m: columns.at[m], f_send, f_recv, own.at[2])
    for n in range(1, planes):

        @pl.when(z >= n)
        def _():
            along(n).wait_recv()
            if n + 1 < planes:
                pl.when(more)(lambda: along(n + 1).start())
            across(n).start()

    across(0).wait()
    keep.wait()
    for copy in f_copies:
        copy.wait()
    f_keep.wait()
    for n in range(1, planes):

        @pl.when(z >= n)
        def _():
            across(n).wait()

        @pl.when(z < n)
        def _():
            for number, buffer in enumerate((mine, other)):
                pltpu.make_async_copy(zeros, buffer.at[n], fill.at[2 * (n - 1) + number]).wait()

        pl.when((z >= n - 1) & more)(lambda: along(n).wait_send())


def climb(block, feed, take, columns, planes, number):
    dma = pltpu.SemaphoreType.DMA
    count = feed.shape[0]
    blocks = jax.ShapeDtypeStruct((planes, *block.shape), block.dtype)
    return pl.pallas_call(
        functools.partial(climb_kernel, planes, take),
        out_shape=[blocks, blocks, jax.ShapeDtypeStruct((8, count, columns), block.dtype)],
        in_specs=[VMEM, HBM],
        out_specs=[HBM] * 3,
        scratch_shapes=[
            pltpu.VMEM(block.shape, block.dtype),
            pltpu.VMEM((count, 8 * columns), feed.dtype),
            pltpu.VMEM((8, count, columns), block.dtype),
            *[dma((size,)) for size in (planes - 1, planes - 1, planes, planes, 7, 7, 3, 2 * (planes - 1))],
        ],
        compiler_params=pltpu.CompilerParams(
            collective_id=number, has_side_effects=True, vmem_limit_bytes=32 * 2**20
        ),
        cost_estimate=pl.CostEstimate(flops=1, bytes_accessed=1, transcendentals=0),
        name="climb",
    )(block, feed)


def descend_kernel(planes, terms, out, sends, recvs, send, recv):
    z = lax.axis_index("z")
    f32 = jnp.float32
    greet(ring(planes))

    def hop(step):
        return pltpu.make_async_remote_copy(
            src_ref=sends.at[step - 1], dst_ref=recvs.at[step - 1], send_sem=send.at[step - 1], recv_sem=recv.at[step - 1],
            device_id={"z": z - 1}, device_id_type=MESH,
        )

    def came(step):
        return (z + 1 < planes) & (z + 1 + step - planes >= 0)

    for step in range(1, planes):
        block = z + step - planes
        if step > 1:
            pl.when(came(step - 1))(lambda: hop(step - 1).wait_recv())

        @pl.when((block >= 0) & (z + 1 == planes))
        def _():
            sends[step - 1] = terms[block]

        if step > 1:

            @pl.when((block >= 0) & (z + 1 < planes))
            def _():
                sends[step - 1] = (terms[block].astype(f32) + recvs[step - 2].astype(f32)).astype(terms.dtype)

        pl.when(block >= 0)(lambda: hop(step).start())
    last = planes - 1
    out[...] = terms[z].astype(f32)

    @pl.when(came(last))
    def _():
        hop(last).wait_recv()
        out[...] += recvs[last - 1].astype(f32)

    for step in range(1, planes):
        pl.when(z + step - planes >= 0)(lambda: hop(step).wait_send())


def descend(terms, planes, number, after=()):
    block = terms.shape[1:]
    dma = pltpu.SemaphoreType.DMA
    return pl.pallas_call(
        lambda terms, *refs: descend_kernel(planes, terms, *refs[len(after) :]),
        out_shape=jax.ShapeDtypeStruct(block, jnp.float32),
        in_specs=[VMEM] + [HBM] * len(after),
        out_specs=VMEM,
        scratch_shapes=[pltpu.VMEM((planes - 1, *block), terms.dtype)] * 2 + [dma((planes - 1,))] * 2,
        compiler_params=pltpu.CompilerParams(
            collective_id=number, has_side_effects=True, vmem_limit_bytes=32 * 2**20
        ),
        cost_estimate=pl.CostEstimate(flops=1, bytes_accessed=1, transcendentals=0),
        name="descend",
    )(terms, *after)


def dot(left, right, contract):
    return lax.dot_general(left, right, (contract, ((), ())), preferred_element_type=jnp.float32)


def mm(left, right):
    return dot(left, right, ((1,), (0,)))


def mm_nt(left, right):
    return dot(left, right, ((1,), (1,)))


def mm_tn(left, right):
    return dot(left, right, ((0,), (0,)))


def bmm(pattern, left, right):
    return jnp.einsum(pattern, left, right, preferred_element_type=jnp.float32)


def angle_tables(positions):
    half_dim = HEAD_SIZE // 2
    frequency = rope_base ** (-(jnp.arange(half_dim).astype(jnp.float32) * 2.0) / HEAD_SIZE)
    phases = positions.astype(jnp.float32)[:, None] * frequency[None, :]
    return (jnp.cos(phases), jnp.sin(phases))


def rotate(value, cos_table, sin_table):
    half = value.shape[-1] // 2
    a, b = value[..., :half], value[..., half:]
    return jnp.concatenate([a * cos_table - b * sin_table, b * cos_table + a * sin_table], axis=-1)


def rms_forward(value, gain_row):
    inverse = lax.rsqrt(jnp.mean(value * value, axis=-1, keepdims=True) + norm_eps)
    return (value * inverse * gain_row, inverse)


def rms_back(grad_out, value, inverse, gain_row):
    scaled = grad_out * gain_row
    grad_in = inverse * (
        scaled - value * inverse * inverse * jnp.mean(scaled * value, axis=-1, keepdims=True)
    )
    return (grad_in, jnp.sum(grad_out * value * inverse, axis=0))


def adamw(weight, gradient, moment_one, moment_two, step_rate, decay_rate, invert=jnp.reciprocal):
    mean_new = beta_one * moment_one + (1.0 - beta_one) * gradient
    square_new = beta_two * moment_two + (1.0 - beta_two) * gradient * gradient
    below = jnp.sqrt(square_new * (1.0 / (1.0 - beta_two**STEP))) + adam_eps
    direction = mean_new * (1.0 / (1.0 - beta_one**STEP)) * invert(below)
    return (weight - step_rate * (direction + decay_rate * weight), mean_new, square_new)


def attention_parts(core, length, q_ref, mine_ref, other_ref, query_ref, key_ref):
    mine, other = mine_ref[...].reshape(-1, HEAD_SIZE), other_ref[...].reshape(-1, HEAD_SIZE)
    first = core == 0
    k, v = jnp.where(first, mine, other), jnp.where(first, other, mine)
    q = q_ref[...].reshape(-1, HEAD_SIZE)
    at, key_at = query_ref[...], key_ref[...]
    allowed = (key_at <= at) & (key_at < length) & (key_at >= 0)
    scores = jnp.where(allowed, mm_nt(q, k) * HEAD_SIZE ** (-0.5), masked_value)
    exponent = jnp.exp(scores - jnp.max(scores, axis=-1, keepdims=True))
    return q, k, v, exponent / jnp.sum(exponent, axis=-1, keepdims=True)


def attention_kernel(core_ref, length_ref, q_ref, mine_ref, other_ref, query_ref, key_ref, out_ref):
    length = length_ref[pl.program_id(0)]
    _, _, v, soft = attention_parts(core_ref[0], length, q_ref, mine_ref, other_ref, query_ref, key_ref)
    out_ref[...] = mm(soft.astype(jnp.bfloat16), v).astype(jnp.bfloat16).reshape(out_ref.shape)


def attention_back_kernel(
    core_ref, length_ref, q_ref, mine_ref, other_ref, query_ref, key_ref, do_ref, cos_ref, sin_ref,
    dq_ref, keep_ref, send_ref,
):
    low = jnp.bfloat16
    core = core_ref[0]
    length = length_ref[pl.program_id(0)]
    q, k, v, soft = attention_parts(core, length, q_ref, mine_ref, other_ref, query_ref, key_ref)
    do = do_ref[...].reshape(-1, HEAD_SIZE)
    dp = mm_nt(do, v)
    delta = jnp.sum(soft * dp, axis=-1, keepdims=True)
    ds = (soft * (dp - delta) * HEAD_SIZE ** (-0.5)).astype(low)
    dq = mm(ds, k)
    cos_table, sin_table = cos_ref[...], sin_ref[...]
    half = HEAD_SIZE // 2
    a, b = dq[:, :half], dq[:, half:]
    turned = jnp.concatenate([a * cos_table + b * sin_table, b * cos_table - a * sin_table], axis=-1)
    dq_ref[...] = turned.astype(low).reshape(dq_ref.shape)
    dk, dv = mm_tn(ds, q), mm_tn(soft.astype(low), do)
    first = core == 0
    keep, send = (t.reshape(keep_ref.shape) for t in (jnp.where(first, dk, dv), jnp.where(first, dv, dk)))
    for block in range(keep_ref.shape[0]):
        at = core_ref[1 + block]
        keep_ref[at] = keep[block]
        send_ref[at] = send[block].astype(low)


def attention_call(kernel, core, lengths, q, mine, other, query_pos, key_pos, extra, outs, name):
    ny, count, span, size = q.shape
    nz = mine.shape[0]
    rows = pl.BlockSpec((ny, 1, span, size), lambda i, *_: (0, i, 0, 0))
    keys = pl.BlockSpec((nz, ny, 1, span, size), lambda i, *_: (0, 0, i, 0, 0))

    def whole(value):
        return pl.BlockSpec(value.shape, lambda i, *_: (0,) * value.ndim)

    kinds = {"rows": (rows, q.shape), "keys": (keys, mine.shape)}
    return pl.pallas_call(
        kernel,
        grid_spec=pltpu.PrefetchScalarGridSpec(
            num_scalar_prefetch=2,
            grid=(count,),
            in_specs=[rows, keys, keys, whole(query_pos), whole(key_pos)]
            + [rows if value.shape == q.shape else whole(value) for value in extra],
            out_specs=[kinds[kind][0] for kind, _ in outs],
        ),
        out_shape=[jax.ShapeDtypeStruct(kinds[kind][1], dtype) for kind, dtype in outs],
        compiler_params=pltpu.CompilerParams(vmem_limit_bytes=48 * 2**20),
        cost_estimate=pl.CostEstimate(flops=1, bytes_accessed=1, transcendentals=0),
        name=name,
    )(core, lengths, q, mine, other, query_pos, key_pos, *extra)


def feed_back_kernel(dyb_ref, weight_ref, gate_ref, up_ref, out_ref):
    dm = mm(dyb_ref[...], weight_ref[...])
    gate, upward = gate_ref[...], up_ref[...]
    sig = jax.nn.sigmoid(gate)
    part = gate.shape[1]
    out_ref[:, :part] = (dm * upward * sig * (1.0 + gate * (1.0 - sig))).astype(out_ref.dtype)
    out_ref[:, part:] = (dm * gate * sig).astype(out_ref.dtype)


def feed_back(dyb, weight, both, lines=256):
    count, part = both.shape[0], both.shape[1] // 2

    def rows(width, column=0):
        return pl.BlockSpec((lines, width), lambda i: (i, column))

    return pl.pallas_call(
        feed_back_kernel,
        grid=(count // lines,),
        in_specs=[rows(dyb.shape[1]), pl.BlockSpec(weight.shape, lambda i: (0, 0)), rows(part), rows(part, 1)],
        out_specs=rows(2 * part),
        out_shape=jax.ShapeDtypeStruct((count, 2 * part), jnp.bfloat16),
        compiler_params=pltpu.CompilerParams(vmem_limit_bytes=48 * 2**20),
        cost_estimate=pl.CostEstimate(flops=1, bytes_accessed=1, transcendentals=0),
        name="feed_back",
    )(dyb, weight, both, both)


def attention_part(step, grad_ref):
    parts = []
    for head in range(8):
        member = jnp.where(step == 1, 2 * (head % 4) + head // 4, head)
        parts.append(grad_ref[member, :, pl.ds(pl.multiple_of(step * HEAD_SIZE, HEAD_SIZE), HEAD_SIZE)])
    return jnp.concatenate(parts, axis=1)


def feed_part(step, gate_up_ref, down_ref):
    size = down_ref.shape[2]
    at = pl.ds(pl.multiple_of(jnp.minimum(step // 2, 1) * size, size), size)
    parts = []
    for number in range(4):
        member = 4 * (step % 2) + number
        parts.append(jnp.where(step < 4, gate_up_ref[member, :, at], down_ref[member]))
    return jnp.concatenate(parts, axis=1)


def close_reciprocal(value):
    guess = pltpu.reciprocal(value, approx=True)
    return guess * (2.0 - value * guess)


def norm_of(lines_ref, tile_ref):
    gains = lines_ref[0:2]
    return jnp.sqrt(jnp.sum(gains * gains, keepdims=True) + lines_ref[2:3, 0:1] + tile_ref[0:1, 0:1])


def update_gains_kernel(
    lines_ref, tile_ref, weight_ref, mean_ref, square_ref, new_ref, new_mean_ref, new_square_ref, norm_ref
):
    norm = norm_of(lines_ref, tile_ref)
    norm_ref[...] = norm
    new_ref[...], new_mean_ref[...], new_square_ref[...] = adamw(
        weight_ref[...], lines_ref[0:2] * (clip_norm / norm), mean_ref[...], square_ref[...], gain_rate, 0.0
    )


def update_gains(sums, weight, mean, square):
    f32 = jnp.float32
    return pl.pallas_call(
        update_gains_kernel,
        in_specs=[VMEM] * 5,
        out_specs=[VMEM] * 4,
        out_shape=[jax.ShapeDtypeStruct(weight.shape, f32)] * 3 + [jax.ShapeDtypeStruct((1, 1), f32)],
        name="update_gains",
    )(*sums, weight, mean, square)


def update_kernel(part, lines_ref, tile_ref, weight_ref, mean_ref, square_ref, *refs):
    grads, (new_ref, new_mean_ref, new_square_ref, copy_ref, factor_ref) = refs[:-5], refs[-5:]

    @pl.when(pl.program_id(0) == 0)
    def _():
        factor_ref[...] = clip_norm / norm_of(lines_ref, tile_ref)

    gradient = part(pl.program_id(0), *grads).astype(jnp.float32) * factor_ref[...]
    at = pl.ds(pl.multiple_of(pl.program_id(0) * new_ref.shape[1], new_ref.shape[1]), new_ref.shape[1])
    new, mean, square = adamw(
        weight_ref[:, at], gradient, mean_ref[...], square_ref[:, at], matrix_rate, weight_decay, close_reciprocal
    )
    new_ref[...] = new
    new_mean_ref[...] = mean
    new_square_ref[...] = square
    copy_ref[...] = new.astype(copy_ref.dtype)


def update(part, sums, weight, mean, square, grads):
    size = 2048 if part is attention_part else 4096
    rows, width = weight.shape
    block = pl.BlockSpec((rows, size), lambda i: (0, i))
    f32 = jnp.float32
    return pl.pallas_call(
        functools.partial(update_kernel, part),
        grid=(width // size,),
        in_specs=[VMEM, VMEM, VMEM, block, VMEM] + [VMEM] * len(grads),
        out_specs=[block] * 4,
        out_shape=[jax.ShapeDtypeStruct(weight.shape, dtype) for dtype in (f32, f32, f32, jnp.bfloat16)],
        scratch_shapes=[pltpu.VMEM((1, 1), f32)],
        compiler_params=pltpu.CompilerParams(vmem_limit_bytes=24 * 2**20),
        name="update",
    )(*sums, weight, mean, square, *grads)


def is_square():
    return lax.axis_size("y") == 2 and lax.axis_size("x") == 2


def swap(blocks):
    return lax.all_to_all(blocks, TEAM, split_axis=0, concat_axis=0, tiled=True)


def over_planes(blocks):
    return lax.all_gather(blocks.reshape(-1, blocks.shape[-1]), "z", axis=0, tiled=True)


def scatter_planes(term):
    return lax.psum_scatter(term, "z", scatter_dimension=0, tiled=True)


def together(*values):
    return lax.optimization_barrier(values)


def scatter_team(rows, number, after=()):
    if not is_square():
        return swap(rows.reshape(8, -1, rows.shape[-1]))
    return turn(rows, number, after)[0]


def team_gather(local, number, after=()):
    if not is_square():
        return lax.all_gather(local, TEAM, axis=0, tiled=True)
    return plane_gather(local, number, after).reshape(-1, local.shape[1])


def team_sum(lefts, rights, number, after=()):
    if is_square():
        return plane_sum(lefts, rights, number, after)
    partial = mm_nt(jnp.concatenate(lefts, axis=1), jnp.concatenate(rights, axis=1))
    return lax.psum_scatter(partial.astype(jnp.bfloat16), TEAM, scatter_dimension=0, tiled=True).astype(jnp.float32)


def local(
    tokens,
    lengths,
    norm_gains,
    attention_weight,
    feed_weight,
    cotangent,
    attention_mean,
    attention_square,
    feed_mean,
    feed_square,
    gain_mean,
    gain_square,
):
    low = jnp.bfloat16
    sequences, span, width = tokens.shape
    ny, nx, nz = lax.axis_size("y"), lax.axis_size("x"), lax.axis_size("z")
    team = ny * nx * 2
    core = lax.axis_index("c")
    rows = attention_weight.shape[0]
    q_width, kv_width = QUERY_HEADS * HEAD_SIZE, KEY_VALUE_HEADS * HEAD_SIZE
    count = sequences * span
    all_sequences = nx * 2 * sequences
    reach = ny * span
    near = is_square()
    ff_part = FF // team

    def columns(start, size):
        return pl.ds(pl.multiple_of(start, size), size)

    def take_attention(sources, member, c):
        source = sources[0]
        starts = (
            member * HEAD_SIZE,
            q_width + c * kv_width + (member - c) // 2 * HEAD_SIZE,
            q_width + 2 * kv_width + member * HEAD_SIZE,
        )
        return jnp.concatenate([source[:, columns(s, HEAD_SIZE)].astype(low) for s in starts], axis=1)

    def take_feed(*parts):
        return lambda sources, member, c: jnp.concatenate(
            [sources[0][:, columns(part * FF + member * ff_part, ff_part)].astype(low) for part in parts], axis=1
        )

    def spread(source, take, size, number, after=()):
        if is_square():
            blocks = plane_swap([source], [(rows, size)], [take], number, after)[0]
        else:
            blocks = swap(jnp.stack([take([source], member, member % 2) for member in range(8)]))
        return blocks, over_planes(blocks)

    team_base = lax.axis_index("z") * reach
    team_pos = team_base + jnp.arange(reach, dtype=jnp.int32)
    own_pos = team_base + lax.axis_index("y") * span + jnp.arange(span, dtype=jnp.int32)
    if near:
        key_pos = jnp.concatenate([team_pos - back * reach for back in range(nz)])
    else:
        key_pos = jnp.arange(nz * reach, dtype=jnp.int32)
    query_at, key_at = team_pos[:, None], key_pos[None, :]
    cos_table, sin_table = angle_tables(team_pos)
    cos_rows, sin_rows = (t.reshape(ny, 1, span, -1) for t in (cos_table, sin_table))
    valid = (own_pos[None, :] < lengths[:, None]).astype(jnp.float32).reshape(count, 1)
    lengths_all = lax.all_gather(lengths, ("x", "c"), axis=0, tiled=True)
    planes = jnp.arange(nz, dtype=jnp.int32)
    if near:
        planes = (lax.axis_index("z") - planes) % nz
    core_at = jnp.concatenate([jnp.reshape(core, (1,)), planes]).astype(jnp.int32)

    def heads(value):
        return value.reshape(ny, all_sequences, span, HEAD_SIZE)

    x_in = tokens.reshape(count, width).astype(jnp.float32)
    normed_one, inverse_one = rms_forward(x_in, norm_gains[0])
    outer_grad = cotangent.reshape(count, width).astype(jnp.float32) * valid
    if is_square():
        attention_mine, h1 = begin(
            attention_weight,
            tokens.reshape(count, width),
            norm_gains[:1],
            take_attention,
            3 * HEAD_SIZE,
            nz,
            1,
        )
        h1 = h1.reshape(-1, width)
    else:
        attention_mine = spread(attention_weight, take_attention, 3 * HEAD_SIZE, 1)[1]
        gate_up_blocks, gate_up_weight = spread(feed_weight, take_feed(0, 1), 2 * ff_part, 2)
        h1 = team_gather(normed_one.astype(low), 3)
    query_weight = attention_mine[:, :HEAD_SIZE]
    kv_weight = attention_mine[:, HEAD_SIZE : 2 * HEAD_SIZE]
    out_weight = attention_mine[:, 2 * HEAD_SIZE :]
    kv_raw = heads(mm(h1, kv_weight))
    kv = jnp.where(core == 0, rotate(kv_raw, cos_rows, sin_rows), kv_raw).astype(low)
    q = rotate(heads(mm(h1, query_weight)), cos_rows, sin_rows).astype(low)
    if is_square():
        kv, other, gate_up_blocks = climb(
            kv.reshape(-1, HEAD_SIZE), feed_weight, take_feed(0, 1), 2 * ff_part, nz, 2
        )
        kv, other = (t.reshape(nz, ny, all_sequences, span, HEAD_SIZE) for t in (kv, other))
        gate_up_weight = over_planes(gate_up_blocks)
    else:
        kv = lax.all_gather(kv, "z", axis=0, tiled=False)
        other = lax.ppermute(kv, "c", [(0, 1), (1, 0)])
    attend = (core_at, lengths_all, q, kv, other, query_at, key_at)
    (o,) = attention_call(attention_kernel, *attend, (), [("rows", low)], "attention")
    o = o.reshape(-1, HEAD_SIZE)
    r = x_in + team_sum([o], [out_weight], 4)

    normed_two, inverse_two = rms_forward(r, norm_gains[1])
    h2 = team_gather(normed_two.astype(low), 16)
    dyb = team_gather(outer_grad.astype(low), 15, [h2])
    down_blocks, down_weight = spread(feed_weight, take_feed(2), ff_part, 12, [dyb])
    gate_up_weight, down_blocks = together(gate_up_weight, down_blocks)
    both = mm(h2, gate_up_weight)
    gate, upward = both[:, :ff_part], both[:, ff_part:]
    sig = jax.nn.sigmoid(gate)
    m = (gate * sig * upward).astype(low)
    down_term = mm_tn(dyb, m).astype(low)
    down_rows = scatter_planes(down_term)
    down_weight, down_term = together(down_weight, down_term)
    d_both = feed_back(dyb, down_weight, both)
    gate_up_term = mm_tn(h2, d_both).astype(low)
    gate_up_rows = scatter_planes(gate_up_term)
    dh2 = team_sum([d_both], [gate_up_weight], 7, [gate_up_term, down_term])
    mid_grad, gain_two = rms_back(dh2, r, inverse_two, norm_gains[1])
    dr = outer_grad + mid_grad
    drb = team_gather(dr.astype(low), 13, [down_rows])

    do = heads(mm(drb, out_weight).astype(low))
    dq, keep, theirs = attention_call(
        attention_back_kernel,
        *attend,
        (do, cos_table, sin_table),
        [("rows", low), ("keys", jnp.float32), ("keys", low)],
        "attention_back",
    )
    dq = dq.reshape(-1, HEAD_SIZE)
    dkv = keep + lax.ppermute(theirs, "c", [(0, 1), (1, 0)]).astype(jnp.float32)
    low_terms = dkv.astype(low)
    feed_sum = team_sum([m], [down_weight], 5, [low_terms])
    down_grad = scatter_team(down_rows, 6, [low_terms])
    if is_square():
        dkv = descend(
            low_terms.reshape(nz, -1, HEAD_SIZE), nz, 3, [gate_up_rows, feed_sum, down_grad]
        ).reshape(ny, all_sequences, span, HEAD_SIZE)
    else:
        dkv = lax.psum_scatter(low_terms, "z", scatter_dimension=0, tiled=True)[0].astype(jnp.float32)
    dkv = jnp.where(core == 0, rotate(dkv, cos_rows, -sin_rows), dkv).astype(low).reshape(-1, HEAD_SIZE)
    layer_output = (r + feed_sum).astype(low)
    attention_term = jnp.concatenate([mm_tn(h1, dq), mm_tn(h1, dkv), mm_tn(drb, o)], axis=1).astype(low)
    attention_rows = scatter_planes(attention_term)
    dh1 = team_sum([dq, dkv], [query_weight, kv_weight], 9, [attention_term])
    gate_up_grad = scatter_team(gate_up_rows, 8, [dh1])
    in_grad, gain_one = rms_back(dh1, x_in, inverse_one, norm_gains[0])
    input_gradient = dr + in_grad
    local_squares = sum(jnp.sum(jnp.square(part.astype(jnp.float32))) for part in (gate_up_rows, down_rows))
    lines = jnp.concatenate([jnp.stack([gain_one, gain_two]), jnp.full((6, width), local_squares)], axis=0)
    if is_square():
        lines = total_sum(lines, nz, 18, [gate_up_grad])
        attention_grad, tile = turn(attention_rows, 10, (), nz)
    else:
        lines = lax.psum(lines, ALL)
        attention_grad = scatter_team(attention_rows, 10)
        tile = lax.psum(jnp.full((8, 128), jnp.sum(jnp.square(attention_rows.astype(jnp.float32)))), ALL)
    sums = (lines, tile)
    feed_new = update(feed_part, sums, feed_weight, feed_mean, feed_square, [gate_up_grad, down_grad])
    attention_new = update(attention_part, sums, attention_weight, attention_mean, attention_square, [attention_grad])
    *gains_new, gradient_norm = update_gains(sums, norm_gains, gain_mean, gain_square)
    return (
        layer_output.reshape(sequences, span, width),
        input_gradient.reshape(sequences, span, width),
        gradient_norm.reshape(()),
        *attention_new,
        *feed_new,
        *gains_new,
    )


def solution(mesh):
    ctx, fsdp = mesh.shape["ctx"], mesh.shape["fsdp"]
    inner = QUERY_HEADS // fsdp
    fine = Mesh(mesh.devices.reshape(ctx // inner, inner, fsdp // 2, 2), ALL)
    act = P(("x", "c"), ("z", "y"), None)
    matrix = P(ALL, None)
    return jax.shard_map(
        local,
        mesh=fine,
        in_specs=(act, P(("x", "c")), P(), matrix, matrix, act, matrix, matrix, matrix, matrix, P(), P()),
        out_specs=(act, act, P(), matrix, matrix, matrix, matrix, matrix, matrix, matrix, matrix, P(), P(), P()),
        check_vma=False,
    )
```

```python
import functools

import jax
import jax.numpy as jnp
from jax import lax
from jax.experimental import pallas as pl
from jax.experimental.pallas import tpu as pltpu
from jax.sharding import Mesh, PartitionSpec as P

QUERY_HEADS = 8
KEY_VALUE_HEADS = 4
HEAD_SIZE = 256
FF = 8192
STEP = 10

norm_eps = 1e-06
rope_base = 1000042.0
masked_value = -1e30
clip_norm = 1.0
beta_one = 0.9
beta_two = 0.95
adam_eps = 1e-08
matrix_rate = 0.03
gain_rate = 0.4
weight_decay = 0.1

TEAM = ("y", "x", "c")
ALL = ("z", "y", "x", "c")


MESH = pl.DeviceIdType.MESH
VMEM = pl.BlockSpec(memory_space=pltpu.VMEM)
HBM = pl.BlockSpec(memory_space=pl.ANY)


def place():
    y, x, c = lax.axis_index("y"), lax.axis_index("x"), lax.axis_index("c")
    return y, x, c, lambda yy, xx, cc: (yy * 2 + xx) * 2 + cc


def greet(others):
    barrier = pltpu.get_barrier_semaphore()
    for other in others:
        pl.semaphore_signal(barrier, inc=1, device_id=other, device_id_type=MESH)
    pl.semaphore_wait(barrier, len(others))


def gather_kernel(src, *refs):
    out, send, recv, own = refs[-4:]
    y, x, c, index = place()
    to_x, to_y, to_s = {"x": 1 - x}, {"y": 1 - y}, {"c": 1 - c}
    me, at_x, at_y, at_d = index(y, x, c), index(y, 1 - x, c), index(1 - y, x, c), index(1 - y, 1 - x, c)
    half = src.shape[0] // 2
    rows = (pl.ds(0, half), pl.ds(half, half))
    local = pltpu.make_async_copy(src, out.at[me], own)
    local.start()
    greet((to_x, to_y, to_s))

    def hop(slot, block, part, where, first=False):
        piece = out.at[block, rows[part]]
        return pltpu.make_async_remote_copy(
            src_ref=src.at[rows[part]] if first else piece,
            dst_ref=piece,
            send_sem=send.at[slot],
            recv_sem=recv.at[slot],
            device_id=where,
            device_id_type=MESH,
        )

    x0, x1 = hop(0, me, 0, to_x, True), hop(1, me, 1, to_x, True)
    y1, y0 = hop(2, me, 1, to_y, True), hop(3, me, 0, to_y, True)
    s0, s1 = hop(4, me, 0, to_s, True), hop(5, me, 1, to_s, True)
    for copy in (x0, y1, x1, y0, s0, s1):
        copy.start()
    x0.wait_recv()
    d0 = hop(6, at_x, 0, to_y)
    d0.start()
    y1.wait_recv()
    d1 = hop(7, at_y, 1, to_x)
    d1.start()
    sx0, sy1 = hop(8, at_x, 0, to_s), hop(9, at_y, 1, to_s)
    sx0.start()
    sy1.start()
    x1.wait_recv()
    sx1 = hop(10, at_x, 1, to_s)
    sx1.start()
    y0.wait_recv()
    sy0 = hop(11, at_y, 0, to_s)
    sy0.start()
    d0.wait_recv()
    sd0 = hop(12, at_d, 0, to_s)
    sd0.start()
    d1.wait_recv()
    sd1 = hop(13, at_d, 1, to_s)
    sd1.start()
    for copy in (s0, s1, sx0, sy1, sx1, sy0, sd0, sd1):
        copy.wait_recv()
    for copy in (x0, x1, y0, y1, s0, s1, d0, d1, sx0, sy1, sx1, sy0, sd0, sd1):
        copy.wait_send()
    local.wait()


def plane_gather(value, number, after=()):
    return pl.pallas_call(
        gather_kernel,
        out_shape=jax.ShapeDtypeStruct((8, *value.shape), value.dtype),
        in_specs=[HBM] * (1 + len(after)),
        out_specs=HBM,
        scratch_shapes=[
            pltpu.SemaphoreType.DMA((14,)),
            pltpu.SemaphoreType.DMA((14,)),
            pltpu.SemaphoreType.DMA,
        ],
        compiler_params=pltpu.CompilerParams(collective_id=number, has_side_effects=True),
        cost_estimate=pl.CostEstimate(flops=1, bytes_accessed=1, transcendentals=0),
        name="plane_gather",
    )(value, *after)


def sum_kernel(lefts, terms, tile, *refs):
    a_refs, w_refs = refs[:lefts], refs[lefts : lefts + len(terms)]
    out, s_send, s_recv, d_send, d_recv, x_send, x_recv, y_send, y_recv, x_acc, y_acc, send, recv = refs[-13:]
    y, x, c, index = place()
    to_x, to_y, to_s = {"x": 1 - x}, {"y": 1 - y}, {"c": 1 - c}
    rows, width = out.shape
    half = rows // 2
    parts = (pl.ds(0, half), pl.ds(half, half))
    f32, low = jnp.float32, jnp.bfloat16

    def product(block, put):
        lines = pl.ds(pl.multiple_of(block * rows, rows), rows)

        @pl.loop(0, width // tile)
        def _(step):
            cols = pl.ds(pl.multiple_of(step * tile, tile), tile)
            total = None
            for (left, start), w_ref in zip(terms, w_refs):
                term = mm_nt(a_refs[left][lines, start : start + w_ref.shape[1]], w_ref[cols, :])
                total = term if total is None else total + term
            put(cols, total)

    def hop(slot, src, dst, where):
        copy = pltpu.make_async_remote_copy(
            src_ref=src, dst_ref=dst, send_sem=send.at[slot], recv_sem=recv.at[slot],
            device_id=where, device_id_type=MESH,
        )
        return copy

    def to_sibling(slot, yy, xx):
        def put(cols, total):
            s_send[slot, :, cols] = total.astype(low)

        product(index(yy, xx, 1 - c), put)
        copy = hop(slot, s_send.at[slot], s_recv.at[slot], to_s)
        copy.start()
        return copy

    def with_sibling(slot, yy, xx, keep):
        def put(cols, total):
            keep[:, cols] = (total + s_recv[slot, :, cols].astype(f32)).astype(keep.dtype)

        product(index(yy, xx, c), put)

    greet((to_x, to_y, to_s))
    s0 = to_sibling(0, 1 - y, 1 - x)
    s1 = to_sibling(1, y, 1 - x)
    s0.wait_recv()
    with_sibling(0, 1 - y, 1 - x, d_send)
    d0 = hop(4, d_send.at[parts[0]], d_recv.at[parts[0]], to_x)
    d1 = hop(5, d_send.at[parts[1]], d_recv.at[parts[1]], to_y)
    d0.start()
    d1.start()
    s1.wait_recv()
    with_sibling(1, y, 1 - x, x_acc)
    x_send[parts[0]] = x_acc[parts[0]].astype(low)
    x0 = hop(6, x_send.at[parts[0]], x_recv.at[parts[0]], to_x)
    x0.start()
    s2 = to_sibling(2, 1 - y, x)
    s2.wait_recv()
    with_sibling(2, 1 - y, x, y_acc)
    y_send[parts[1]] = y_acc[parts[1]].astype(low)
    y1 = hop(7, y_send.at[parts[1]], y_recv.at[parts[1]], to_y)
    y1.start()
    s3 = to_sibling(3, y, x)
    d1.wait_recv()
    x_send[parts[1]] = (x_acc[parts[1]] + d_recv[parts[1]].astype(f32)).astype(low)
    x1 = hop(8, x_send.at[parts[1]], x_recv.at[parts[1]], to_x)
    x1.start()
    d0.wait_recv()
    y_send[parts[0]] = (y_acc[parts[0]] + d_recv[parts[0]].astype(f32)).astype(low)
    y0 = hop(9, y_send.at[parts[0]], y_recv.at[parts[0]], to_y)
    y0.start()
    s3.wait_recv()
    with_sibling(3, y, x, out)
    x0.wait_recv()
    y1.wait_recv()
    x1.wait_recv()
    y0.wait_recv()
    out[...] += x_recv[...].astype(f32) + y_recv[...].astype(f32)
    for copy in (s0, s1, s2, s3, d0, d1, x0, x1, y0, y1):
        copy.wait_send()


def plane_sum(lefts, rights, number, after=(), tile=512):
    ends = [(left, start) for left, a in enumerate(lefts) for start in range(0, a.shape[1], rights[0].shape[1])]
    terms = tuple(ends[: len(rights)])
    rows, width = lefts[0].shape[0] // 8, rights[0].shape[0]
    block = (rows, width)
    low, f32 = jnp.bfloat16, jnp.float32
    return pl.pallas_call(
        functools.partial(sum_kernel, len(lefts), terms, min(tile, width)),
        out_shape=jax.ShapeDtypeStruct(block, f32),
        in_specs=[VMEM] * (len(lefts) + len(rights)) + [HBM] * len(after),
        out_specs=VMEM,
        scratch_shapes=[
            pltpu.VMEM((4, *block), low),
            pltpu.VMEM((4, *block), low),
            *[pltpu.VMEM(block, low)] * 6,
            pltpu.VMEM(block, f32),
            pltpu.VMEM(block, f32),
            pltpu.SemaphoreType.DMA((10,)),
            pltpu.SemaphoreType.DMA((10,)),
        ],
        compiler_params=pltpu.CompilerParams(
            collective_id=number, has_side_effects=True, vmem_limit_bytes=48 * 2**20
        ),
        cost_estimate=pl.CostEstimate(flops=1, bytes_accessed=1, transcendentals=0),
        name="plane_sum",
    )(*lefts, *rights, *after)


def swap_kernel(pieces, takes, *refs):
    count = len(pieces)
    sources, (send, recv, own) = refs[: -2 * count - 3], refs[-3:]
    outs, holds = refs[-2 * count - 3 : -count - 3], refs[-count - 3 : -3]
    y, x, c, index = place()
    me = index(y, x, c)
    flips = [(fy, fx, fc) for fy, fx in ((1, 1), (0, 1), (1, 0), (0, 0)) for fc in (0, 1)]
    flips = [flip for flip in flips if flip != (0, 0, 0)]

    def there(flip):
        return tuple(1 - at if f else at for at, f in zip((y, x, c), flip))

    greet([dict(zip(("y", "x", "c"), there(flip))) for flip in flips])
    copies = []
    for piece in range(count):
        for number, flip in enumerate(flips):
            yy, xx, cc = there(flip)
            member = index(yy, xx, cc)
            holds[piece][number] = takes[piece](sources, member, cc)
            copy = pltpu.make_async_remote_copy(
                src_ref=holds[piece].at[number],
                dst_ref=outs[piece].at[me],
                send_sem=send.at[piece * 7 + number],
                recv_sem=recv.at[piece * 7 + number],
                device_id={"y": yy, "x": xx, "c": cc},
                device_id_type=MESH,
            )
            copy.start()
            copies.append(copy)
        holds[piece][7] = takes[piece](sources, me, c)
        keep = pltpu.make_async_copy(holds[piece].at[7], outs[piece].at[me], own.at[piece])
        keep.start()
        copies.append(keep)
    for copy in copies:
        copy.wait()


def plane_swap(sources, shapes, takes, number, after=()):
    low = jnp.bfloat16
    count = len(shapes)
    return pl.pallas_call(
        functools.partial(swap_kernel, shapes, takes),
        out_shape=[jax.ShapeDtypeStruct((8, *shape), low) for shape in shapes],
        in_specs=[VMEM] * len(sources) + [HBM] * len(after),
        out_specs=[HBM] * count,
        scratch_shapes=[
            *[pltpu.VMEM((8, *shape), low) for shape in shapes],
            pltpu.SemaphoreType.DMA((7 * count,)),
            pltpu.SemaphoreType.DMA((7 * count,)),
            pltpu.SemaphoreType.DMA((count,)),
        ],
        compiler_params=pltpu.CompilerParams(
            collective_id=number, has_side_effects=True, vmem_limit_bytes=48 * 2**20
        ),
        cost_estimate=pl.CostEstimate(flops=1, bytes_accessed=1, transcendentals=0),
        name="plane_swap",
    )(*sources, *after)


def team_of(y, x, c):
    flips = [(fy, fx, fc) for fy, fx in ((1, 1), (0, 1), (1, 0), (0, 0)) for fc in (0, 1)]
    return [
        tuple(1 - at if f else at for at, f in zip((y, x, c), flip)) for flip in flips if flip != (0, 0, 0)
    ]


def turn_kernel(planes, src, *refs):
    y, x, c, index = place()
    me = index(y, x, c)
    others = team_of(y, x, c)
    ids = [dict(zip(("y", "x", "c"), other)) for other in others]
    if planes:
        out, total, near, far, held, send, recv, own, send_lines, recv_lines = refs[-10:]
        z = lax.axis_index("z")
        column = [{"z": lax.rem(z + step, planes)} for step in range(1, planes)]
        fetch = pltpu.make_async_copy(src, held, own)
        fetch.start()
        fetch.wait()
        squares = jnp.zeros((8, held.shape[1]), jnp.float32)
        for start in range(0, held.shape[0], 64):
            part = held[start : start + 64].astype(jnp.float32)
            squares += jnp.sum(jnp.square(part).reshape(8, 8, -1), axis=0)
        near[me] = jnp.broadcast_to(jnp.sum(squares, keepdims=True), near.shape[1:])
    else:
        out, send, recv, own = refs[-4:]
        column = []
    greet(ids + column)
    count = src.shape[0] // 8

    def rows(member):
        return src.at[pl.ds(pl.multiple_of(member * count, count), count)]

    def spread(buffer, at, where, base):
        copies = [
            pltpu.make_async_remote_copy(
                src_ref=buffer.at[at],
                dst_ref=buffer.at[at],
                send_sem=send_lines.at[base + number],
                recv_sem=recv_lines.at[base + number],
                device_id=other,
                device_id_type=MESH,
            )
            for number, other in enumerate(where)
        ]
        for copy in copies:
            copy.start()
        return copies

    small = spread(near, me, ids, 0) if planes else []
    copies = [
        pltpu.make_async_remote_copy(
            src_ref=rows(index(*other)),
            dst_ref=out.at[me],
            send_sem=send.at[number],
            recv_sem=recv.at[number],
            device_id=where,
            device_id_type=MESH,
        )
        for number, (other, where) in enumerate(zip(others, ids))
    ]
    copies.append(pltpu.make_async_copy(rows(me), out.at[me], own))
    for copy in copies:
        copy.start()
    if planes:
        for copy in small:
            copy.wait()
        far[z] = jnp.sum(near[...], axis=0)
        for copy in spread(far, z, column, 7):
            copy.wait()
        total[...] = jnp.sum(far[...], axis=0)
    for copy in copies:
        copy.wait()


def total_kernel(planes, src, *refs):
    out, near, far, send, recv = refs[-5:]
    y, x, c, index = place()
    z = lax.axis_index("z")
    ids = [dict(zip(("y", "x", "c"), other)) for other in team_of(y, x, c)]
    column = [{"z": lax.rem(z + step, planes)} for step in range(1, planes)]
    me = index(y, x, c)
    near[me] = src[...]
    greet(ids + column)

    def spread(buffer, at, where, base):
        copies = [
            pltpu.make_async_remote_copy(
                src_ref=buffer.at[at],
                dst_ref=buffer.at[at],
                send_sem=send.at[base + number],
                recv_sem=recv.at[base + number],
                device_id=other,
                device_id_type=MESH,
            )
            for number, other in enumerate(where)
        ]
        for copy in copies:
            copy.start()
        for copy in copies:
            copy.wait()

    spread(near, me, ids, 0)
    far[z] = jnp.sum(near[...], axis=0)
    spread(far, z, column, 7)
    out[...] = jnp.sum(far[...], axis=0)


def total_sum(value, planes, number, after=()):
    return pl.pallas_call(
        functools.partial(total_kernel, planes),
        out_shape=jax.ShapeDtypeStruct(value.shape, value.dtype),
        in_specs=[VMEM] + [HBM] * len(after),
        out_specs=VMEM,
        scratch_shapes=[pltpu.VMEM((size, *value.shape), value.dtype) for size in (8, planes)]
        + [pltpu.SemaphoreType.DMA((6 + planes,))] * 2,
        compiler_params=pltpu.CompilerParams(
            collective_id=number, has_side_effects=True, vmem_limit_bytes=16 * 2**20
        ),
        cost_estimate=pl.CostEstimate(flops=1, bytes_accessed=1, transcendentals=0),
        name="total_sum",
    )(value, *after)


def turn(rows, number, after=(), planes=0):
    block = (rows.shape[0] // 8, rows.shape[1])
    dma = pltpu.SemaphoreType.DMA
    out_shape, out_specs = [jax.ShapeDtypeStruct((8, *block), rows.dtype)], [HBM]
    scratch = [dma((7,)), dma((7,)), dma]
    if planes:
        tile = jax.ShapeDtypeStruct((8, 128), jnp.float32)
        out_shape.append(tile)
        out_specs.append(VMEM)
        buffers = [pltpu.VMEM((size, *tile.shape), tile.dtype) for size in (8, planes)]
        scratch = buffers + [pltpu.VMEM(rows.shape, rows.dtype)] + scratch + [dma((6 + planes,)), dma((6 + planes,))]
    return pl.pallas_call(
        functools.partial(turn_kernel, planes),
        out_shape=out_shape,
        in_specs=[HBM] * (1 + len(after)),
        out_specs=out_specs,
        scratch_shapes=scratch,
        compiler_params=pltpu.CompilerParams(
            collective_id=number, has_side_effects=True, vmem_limit_bytes=16 * 2**20
        ),
        cost_estimate=pl.CostEstimate(flops=1, bytes_accessed=1, transcendentals=0),
        name="turn",
    )(rows, *after)


def hops(planes, send, recv, block, up):
    z = lax.axis_index("z")

    def step(number):
        gone, came = (z - number + 1, z - number) if up else (z + number - 1, z + number)
        goes = ((gone >= 0) & (z + 1 < planes)) if up else ((gone < planes) & (z >= 1))
        comes = (came >= 0) if up else (came < planes)

        def copy(b):
            return pltpu.make_async_remote_copy(
                src_ref=block(b),
                dst_ref=block(b),
                send_sem=send.at[number - 1],
                recv_sem=recv.at[number - 1],
                device_id={"z": z + 1 if up else z - 1},
                device_id_type=MESH,
            )

        return (
            lambda: pl.when(goes)(lambda: copy(gone).start()),
            lambda: pl.when(comes)(lambda: copy(came).wait_recv()),
            lambda: pl.when(goes)(lambda: copy(gone).wait_send()),
        )

    return [step(number) for number in range(1, planes)]


def ring(planes):
    z = lax.axis_index("z")
    return [{"z": lax.rem(z + 1, planes)}, {"z": lax.rem(z + planes - 1, planes)}]


def spread_to(others, ids, source, take, hold, place_of, send, recv, own):
    y, x, c, index = place()
    me = index(y, x, c)
    copies = []
    for number, (other, where) in enumerate(zip(others, ids)):
        hold[number] = take([source], index(*other), other[2])
        copy = pltpu.make_async_remote_copy(
            src_ref=hold.at[number], dst_ref=place_of(me), send_sem=send.at[number], recv_sem=recv.at[number],
            device_id=where, device_id_type=MESH,
        )
        copy.start()
        copies.append(copy)
    hold[7] = take([source], me, c)
    keep = pltpu.make_async_copy(hold.at[7], place_of(me), own)
    keep.start()
    return copies, keep


def begin_kernel(
    planes, take, attention, tokens, gain, all_attention, all_rows,
    held, hold, rows, a_send, a_recv, r_send, r_recv, u_send, u_recv, d_send, d_recv, own,
):
    y, x, c, index = place()
    z = lax.axis_index("z")
    me, at_x, at_y, at_d = index(y, x, c), index(y, 1 - x, c), index(1 - y, x, c), index(1 - y, 1 - x, c)
    others = team_of(y, x, c)
    ids = [dict(zip(("y", "x", "c"), other)) for other in others]
    to_x, to_y, to_s = {"x": 1 - x}, {"y": 1 - y}, {"c": 1 - c}
    count = held.shape[0]
    half = rows.shape[0] // 2
    parts = (pl.ds(0, half), pl.ds(half, half))
    fetch = pltpu.make_async_copy(attention, held, own.at[0])
    fetch.start()
    greet(ids + ring(planes))
    fetch.wait()

    def attention_rows(start, size):
        return all_attention.at[pl.ds(pl.multiple_of(start, count), size)]

    a_copies, a_keep = spread_to(
        others, ids, held, take, hold, lambda m: attention_rows((z * 8 + m) * count, count), a_send, a_recv, own.at[1]
    )
    for start in range(0, rows.shape[0], 32):
        lines = pl.ds(start, 32)
        rows[lines] = rms_forward(tokens[lines].astype(jnp.float32), gain[...])[0].astype(rows.dtype)

    def hop(slot, block, part, where, first=False):
        piece = all_rows.at[block, parts[part]]
        copy = pltpu.make_async_remote_copy(
            src_ref=rows.at[parts[part]] if first else piece, dst_ref=piece,
            send_sem=r_send.at[slot], recv_sem=r_recv.at[slot], device_id=where, device_id_type=MESH,
        )
        copy.start()
        return copy

    for copy in a_copies:
        copy.wait_recv()
    a_keep.wait()

    def plane_block(b):
        return attention_rows(b * 8 * count, 8 * count)

    up = hops(planes, u_send, u_recv, plane_block, True)
    down = hops(planes, d_send, d_recv, plane_block, False)

    def pass_on(number):
        if number > 0:
            up[number - 1][1]()
            down[number - 1][1]()
        if number < planes - 1:
            up[number][0]()
            down[number][0]()

    pass_on(0)
    x0, y1 = hop(0, me, 0, to_x, True), hop(2, me, 1, to_y, True)
    x1, y0 = hop(1, me, 1, to_x, True), hop(3, me, 0, to_y, True)
    s0, s1 = hop(4, me, 0, to_s, True), hop(5, me, 1, to_s, True)
    mine = pltpu.make_async_copy(rows, all_rows.at[me], own.at[2])
    mine.start()
    x0.wait_recv()
    d0 = hop(6, at_x, 0, to_y)
    y1.wait_recv()
    d1 = hop(7, at_y, 1, to_x)
    sx0, sy1 = hop(8, at_x, 0, to_s), hop(9, at_y, 1, to_s)
    pass_on(1)
    x1.wait_recv()
    sx1 = hop(10, at_x, 1, to_s)
    y0.wait_recv()
    sy0 = hop(11, at_y, 0, to_s)
    d0.wait_recv()
    sd0 = hop(12, at_d, 0, to_s)
    d1.wait_recv()
    sd1 = hop(13, at_d, 1, to_s)
    for number in range(2, planes):
        pass_on(number)
    for copy in (s0, s1, sx0, sy1, sx1, sy0, sd0, sd1):
        copy.wait_recv()
    for copy in (x0, x1, y0, y1, s0, s1, d0, d1, sx0, sy1, sx1, sy0, sd0, sd1, *a_copies):
        copy.wait_send()
    for step in up + down:
        step[2]()
    mine.wait()


def begin(attention, tokens, gain, take, columns, planes, number):
    low, dma = jnp.bfloat16, pltpu.SemaphoreType.DMA
    count = attention.shape[0]
    return pl.pallas_call(
        functools.partial(begin_kernel, planes, take),
        out_shape=[
            jax.ShapeDtypeStruct((planes * 8 * count, columns), low),
            jax.ShapeDtypeStruct((8, *tokens.shape), low),
        ],
        in_specs=[HBM, VMEM, VMEM],
        out_specs=[HBM] * 2,
        scratch_shapes=[
            pltpu.VMEM(attention.shape, attention.dtype),
            pltpu.VMEM((8, count, columns), low),
            pltpu.VMEM(tokens.shape, low),
            *[dma((size,)) for size in (7, 7, 14, 14, *[planes - 1] * 4, 3)],
        ],
        compiler_params=pltpu.CompilerParams(
            collective_id=number, has_side_effects=True, vmem_limit_bytes=56 * 2**20
        ),
        cost_estimate=pl.CostEstimate(flops=1, bytes_accessed=1, transcendentals=0),
        name="begin",
    )(attention, tokens, gain)


def climb_kernel(
    planes, take, block, feed, mine, other, columns, zeros, stay, held, hold, u_send, u_recv, s_send, s_recv, f_send, f_recv, own, fill
):
    y, x, c, index = place()
    z = lax.axis_index("z")
    to_s = {"c": 1 - c}
    others = team_of(y, x, c)
    ids = [dict(zip(("y", "x", "c"), where)) for where in others]
    fetch = pltpu.make_async_copy(feed.at[:, pl.ds(0, held.shape[1])], held, own.at[1])
    fetch.start()
    greet(ids + ring(planes))

    def across(n):
        return pltpu.make_async_remote_copy(
            src_ref=block if n == 0 else mine.at[n], dst_ref=other.at[n], send_sem=s_send.at[n], recv_sem=s_recv.at[n],
            device_id=to_s, device_id_type=MESH,
        )

    def along(n):
        return pltpu.make_async_remote_copy(
            src_ref=block if n == 1 else mine.at[n - 1], dst_ref=mine.at[n], send_sem=u_send.at[n - 1], recv_sem=u_recv.at[n - 1],
            device_id={"z": z + 1}, device_id_type=MESH,
        )

    pull = pltpu.make_async_copy(block, stay, own.at[3])
    keep = pltpu.make_async_copy(stay, mine.at[0], own.at[0])
    more = z + 1 < planes
    pl.when(more)(lambda: along(1).start())
    across(0).start()
    pull.start()
    zeros[...] = jnp.zeros_like(zeros)
    pull.wait()
    keep.start()
    for n in range(1, planes):

        @pl.when(z < n)
        def _():
            for number, buffer in enumerate((mine, other)):
                pltpu.make_async_copy(zeros, buffer.at[n], fill.at[2 * (n - 1) + number]).start()

    fetch.wait()
    f_copies, f_keep = spread_to(others, ids, held, take, hold, lambda m: columns.at[m], f_send, f_recv, own.at[2])
    for n in range(1, planes):

        @pl.when(z >= n)
        def _():
            along(n).wait_recv()
            if n + 1 < planes:
                pl.when(more)(lambda: along(n + 1).start())
            across(n).start()

    across(0).wait()
    keep.wait()
    for copy in f_copies:
        copy.wait()
    f_keep.wait()
    for n in range(1, planes):

        @pl.when(z >= n)
        def _():
            across(n).wait()

        @pl.when(z < n)
        def _():
            for number, buffer in enumerate((mine, other)):
                pltpu.make_async_copy(zeros, buffer.at[n], fill.at[2 * (n - 1) + number]).wait()

        pl.when((z >= n - 1) & more)(lambda: along(n).wait_send())


def climb(block, feed, take, columns, planes, number):
    dma = pltpu.SemaphoreType.DMA
    count = feed.shape[0]
    blocks = jax.ShapeDtypeStruct((planes, *block.shape), block.dtype)
    return pl.pallas_call(
        functools.partial(climb_kernel, planes, take),
        out_shape=[blocks, blocks, jax.ShapeDtypeStruct((8, count, columns), block.dtype)],
        in_specs=[HBM, HBM],
        out_specs=[HBM] * 3,
        scratch_shapes=[
            pltpu.VMEM(block.shape, block.dtype),
            pltpu.VMEM(block.shape, block.dtype),
            pltpu.VMEM((count, 8 * columns), feed.dtype),
            pltpu.VMEM((8, count, columns), block.dtype),
            *[dma((size,)) for size in (planes - 1, planes - 1, planes, planes, 7, 7, 4, 2 * (planes - 1))],
        ],
        compiler_params=pltpu.CompilerParams(
            collective_id=number, has_side_effects=True, vmem_limit_bytes=56 * 2**20
        ),
        cost_estimate=pl.CostEstimate(flops=1, bytes_accessed=1, transcendentals=0),
        name="climb",
    )(block, feed)


def dot(left, right, contract):
    return lax.dot_general(left, right, (contract, ((), ())), preferred_element_type=jnp.float32)


def mm(left, right):
    return dot(left, right, ((1,), (0,)))


def mm_nt(left, right):
    return dot(left, right, ((1,), (1,)))


def mm_tn(left, right):
    return dot(left, right, ((0,), (0,)))


def bmm(pattern, left, right):
    return jnp.einsum(pattern, left, right, preferred_element_type=jnp.float32)


def angle_tables(positions):
    half_dim = HEAD_SIZE // 2
    frequency = rope_base ** (-(jnp.arange(half_dim).astype(jnp.float32) * 2.0) / HEAD_SIZE)
    phases = positions.astype(jnp.float32)[:, None] * frequency[None, :]
    return (jnp.cos(phases), jnp.sin(phases))


def rotate(value, cos_table, sin_table):
    half = value.shape[-1] // 2
    a, b = value[..., :half], value[..., half:]
    return jnp.concatenate([a * cos_table - b * sin_table, b * cos_table + a * sin_table], axis=-1)


def rms_forward(value, gain_row):
    inverse = lax.rsqrt(jnp.mean(value * value, axis=-1, keepdims=True) + norm_eps)
    return (value * inverse * gain_row, inverse)


def rms_back(grad_out, value, inverse, gain_row):
    scaled = grad_out * gain_row
    grad_in = inverse * (
        scaled - value * inverse * inverse * jnp.mean(scaled * value, axis=-1, keepdims=True)
    )
    return (grad_in, jnp.sum(grad_out * value * inverse, axis=0))


def adamw(weight, gradient, moment_one, moment_two, step_rate, decay_rate, invert=jnp.reciprocal):
    mean_new = beta_one * moment_one + (1.0 - beta_one) * gradient
    square_new = beta_two * moment_two + (1.0 - beta_two) * gradient * gradient
    below = jnp.sqrt(square_new * (1.0 / (1.0 - beta_two**STEP))) + adam_eps
    direction = mean_new * (1.0 / (1.0 - beta_one**STEP)) * invert(below)
    return (weight - step_rate * (direction + decay_rate * weight), mean_new, square_new)


def attention_parts(core, length, q_ref, mine_ref, other_ref, query_ref, key_ref):
    mine, other = mine_ref[...].reshape(-1, HEAD_SIZE), other_ref[...].reshape(-1, HEAD_SIZE)
    first = core == 0
    k, v = jnp.where(first, mine, other), jnp.where(first, other, mine)
    q = q_ref[...].reshape(-1, HEAD_SIZE)
    at, key_at = query_ref[...], key_ref[...]
    allowed = (key_at <= at) & (key_at < length) & (key_at >= 0)
    scores = jnp.where(allowed, mm_nt(q, k) * HEAD_SIZE ** (-0.5), masked_value)
    exponent = jnp.exp(scores - jnp.max(scores, axis=-1, keepdims=True))
    return q, k, v, exponent / jnp.sum(exponent, axis=-1, keepdims=True)


def attention_kernel(core_ref, length_ref, q_ref, mine_ref, other_ref, query_ref, key_ref, out_ref):
    length = length_ref[pl.program_id(0)]
    _, _, v, soft = attention_parts(core_ref[0], length, q_ref, mine_ref, other_ref, query_ref, key_ref)
    out_ref[...] = mm(soft.astype(jnp.bfloat16), v).astype(jnp.bfloat16).reshape(out_ref.shape)


def attention_back_kernel(
    core_ref, length_ref, q_ref, mine_ref, other_ref, query_ref, key_ref, do_ref, cos_ref, sin_ref,
    dq_ref, keep_ref, send_ref,
):
    low = jnp.bfloat16
    core = core_ref[0]
    length = length_ref[pl.program_id(0)]
    q, k, v, soft = attention_parts(core, length, q_ref, mine_ref, other_ref, query_ref, key_ref)
    do = do_ref[...].reshape(-1, HEAD_SIZE)
    dp = mm_nt(do, v)
    delta = jnp.sum(soft * dp, axis=-1, keepdims=True)
    ds = (soft * (dp - delta) * HEAD_SIZE ** (-0.5)).astype(low)
    dq = mm(ds, k)
    cos_table, sin_table = cos_ref[...], sin_ref[...]
    half = HEAD_SIZE // 2
    a, b = dq[:, :half], dq[:, half:]
    turned = jnp.concatenate([a * cos_table + b * sin_table, b * cos_table - a * sin_table], axis=-1)
    dq_ref[...] = turned.astype(low).reshape(dq_ref.shape)
    dk, dv = mm_tn(ds, q), mm_tn(soft.astype(low), do)
    first = core == 0
    keep, send = (t.reshape(keep_ref.shape) for t in (jnp.where(first, dk, dv), jnp.where(first, dv, dk)))
    for block in range(keep_ref.shape[0]):
        at = core_ref[1 + block]
        keep_ref[at] = keep[block]
        send_ref[at] = send[block].astype(low)


def attention_call(kernel, core, lengths, q, mine, other, query_pos, key_pos, extra, outs, name):
    ny, count, span, size = q.shape
    nz = mine.shape[0]
    rows = pl.BlockSpec((ny, 1, span, size), lambda i, *_: (0, i, 0, 0))
    keys = pl.BlockSpec((nz, ny, 1, span, size), lambda i, *_: (0, 0, i, 0, 0))

    def whole(value):
        return pl.BlockSpec(value.shape, lambda i, *_: (0,) * value.ndim)

    kinds = {"rows": (rows, q.shape), "keys": (keys, mine.shape)}
    return pl.pallas_call(
        kernel,
        grid_spec=pltpu.PrefetchScalarGridSpec(
            num_scalar_prefetch=2,
            grid=(count,),
            in_specs=[rows, keys, keys, whole(query_pos), whole(key_pos)]
            + [rows if value.shape == q.shape else whole(value) for value in extra],
            out_specs=[kinds[kind][0] for kind, _ in outs],
        ),
        out_shape=[jax.ShapeDtypeStruct(kinds[kind][1], dtype) for kind, dtype in outs],
        compiler_params=pltpu.CompilerParams(vmem_limit_bytes=48 * 2**20),
        cost_estimate=pl.CostEstimate(flops=1, bytes_accessed=1, transcendentals=0),
        name=name,
    )(core, lengths, q, mine, other, query_pos, key_pos, *extra)


def feed_back_kernel(dyb_ref, weight_ref, gate_ref, up_ref, out_ref):
    dm = mm(dyb_ref[...], weight_ref[...])
    gate, upward = gate_ref[...], up_ref[...]
    sig = jax.nn.sigmoid(gate)
    part = gate.shape[1]
    out_ref[:, :part] = (dm * upward * sig * (1.0 + gate * (1.0 - sig))).astype(out_ref.dtype)
    out_ref[:, part:] = (dm * gate * sig).astype(out_ref.dtype)


def feed_back(dyb, weight, both, lines=256):
    count, part = both.shape[0], both.shape[1] // 2

    def rows(width, column=0):
        return pl.BlockSpec((lines, width), lambda i: (i, column))

    return pl.pallas_call(
        feed_back_kernel,
        grid=(count // lines,),
        in_specs=[rows(dyb.shape[1]), pl.BlockSpec(weight.shape, lambda i: (0, 0)), rows(part), rows(part, 1)],
        out_specs=rows(2 * part),
        out_shape=jax.ShapeDtypeStruct((count, 2 * part), jnp.bfloat16),
        compiler_params=pltpu.CompilerParams(vmem_limit_bytes=48 * 2**20),
        cost_estimate=pl.CostEstimate(flops=1, bytes_accessed=1, transcendentals=0),
        name="feed_back",
    )(dyb, weight, both, both)


def attention_part(step, grad_ref):
    parts = []
    for head in range(8):
        member = jnp.where(step == 1, 2 * (head % 4) + head // 4, head)
        parts.append(grad_ref[member, :, pl.ds(pl.multiple_of(step * HEAD_SIZE, HEAD_SIZE), HEAD_SIZE)])
    return jnp.concatenate(parts, axis=1)


def feed_part(step, gate_up_ref, down_ref):
    size = down_ref.shape[2]
    at = pl.ds(pl.multiple_of(jnp.minimum(step // 2, 1) * size, size), size)
    parts = []
    for number in range(4):
        member = 4 * (step % 2) + number
        parts.append(jnp.where(step < 4, gate_up_ref[member, :, at], down_ref[member]))
    return jnp.concatenate(parts, axis=1)


def close_reciprocal(value):
    guess = pltpu.reciprocal(value, approx=True)
    return guess * (2.0 - value * guess)


def norm_of(lines_ref, tile_ref):
    gains = lines_ref[0:2]
    return jnp.sqrt(jnp.sum(gains * gains, keepdims=True) + lines_ref[2:3, 0:1] + tile_ref[0:1, 0:1])


def update_kernel(feed_steps, *refs):
    lines_ref, tile_ref, gate_up_ref, down_ref, attention_ref = refs[:5]
    gains, feed, attention = refs[5:8], refs[8:11], refs[11:14]
    new_gains, norm_ref, new_feed, new_attention, factor_ref = refs[14:17], refs[17], refs[18:22], refs[22:26], refs[26]
    step = pl.program_id(0)

    @pl.when(step == 0)
    def _():
        norm = norm_of(lines_ref, tile_ref)
        norm_ref[...] = norm
        factor_ref[...] = clip_norm / norm
        weight, mean, square = (ref[...] for ref in gains)
        gradient = lines_ref[0:2] * factor_ref[...]
        for ref, value in zip(new_gains, adamw(weight, gradient, mean, square, gain_rate, 0.0)):
            ref[...] = value

    def matrix(olds, news, gradient):
        weight, mean, square = (ref[...] for ref in olds)
        gradient = gradient.astype(jnp.float32) * factor_ref[...]
        values = adamw(weight, gradient, mean, square, matrix_rate, weight_decay, close_reciprocal)
        for ref, value in zip(news, (*values, values[0])):
            ref[...] = value.astype(ref.dtype)

    @pl.when(step < feed_steps)
    def _():
        matrix(feed, new_feed, feed_part(step, gate_up_ref, down_ref))

    @pl.when(step >= feed_steps)
    def _():
        matrix(attention, new_attention, attention_part(step - feed_steps, attention_ref))


def update(sums, grads, gains, feed, attention):
    f32, low = jnp.float32, jnp.bfloat16
    rows = feed[0].shape[0]
    wide, narrow = 4096, 2048
    feed_steps, attention_steps = feed[0].shape[1] // wide, attention[0].shape[1] // narrow
    feed_block = pl.BlockSpec((rows, wide), lambda i: (0, jnp.minimum(i, feed_steps - 1)))
    attention_block = pl.BlockSpec((rows, narrow), lambda i: (0, jnp.maximum(i - feed_steps, 0)))

    def whole(value):
        return pl.BlockSpec(value.shape, lambda i: (0,) * value.ndim)

    norm = jax.ShapeDtypeStruct((1, 1), f32)
    matrices = [jax.ShapeDtypeStruct(part[0].shape, dtype) for part in (feed, attention) for dtype in (f32, f32, f32, low)]
    return pl.pallas_call(
        functools.partial(update_kernel, feed_steps),
        grid=(feed_steps + attention_steps,),
        in_specs=[whole(value) for value in (*sums, *grads, *gains)] + [feed_block] * 3 + [attention_block] * 3,
        out_specs=[whole(value) for value in (*gains, norm)] + [feed_block] * 4 + [attention_block] * 4,
        out_shape=[jax.ShapeDtypeStruct(gains[0].shape, f32)] * 3 + [norm] + matrices,
        scratch_shapes=[pltpu.VMEM((1, 1), f32)],
        compiler_params=pltpu.CompilerParams(vmem_limit_bytes=56 * 2**20),
        name="update",
    )(*sums, *grads, *gains, *feed, *attention)


def is_square():
    return lax.axis_size("y") == 2 and lax.axis_size("x") == 2


def swap(blocks):
    return lax.all_to_all(blocks, TEAM, split_axis=0, concat_axis=0, tiled=True)


def over_planes(blocks):
    return lax.all_gather(blocks.reshape(-1, blocks.shape[-1]), "z", axis=0, tiled=True)


def scatter_planes(term):
    return lax.psum_scatter(term, "z", scatter_dimension=0, tiled=True)


def together(*values):
    return lax.optimization_barrier(values)


def scatter_team(rows, number, after=()):
    if not is_square():
        return swap(rows.reshape(8, -1, rows.shape[-1]))
    return turn(rows, number, after)[0]


def team_gather(local, number, after=()):
    if not is_square():
        return lax.all_gather(local, TEAM, axis=0, tiled=True)
    return plane_gather(local, number, after).reshape(-1, local.shape[1])


def team_sum(lefts, rights, number, after=()):
    if is_square():
        return plane_sum(lefts, rights, number, after)
    partial = mm_nt(jnp.concatenate(lefts, axis=1), jnp.concatenate(rights, axis=1))
    return lax.psum_scatter(partial.astype(jnp.bfloat16), TEAM, scatter_dimension=0, tiled=True).astype(jnp.float32)


def local(
    tokens,
    lengths,
    norm_gains,
    attention_weight,
    feed_weight,
    cotangent,
    attention_mean,
    attention_square,
    feed_mean,
    feed_square,
    gain_mean,
    gain_square,
):
    low = jnp.bfloat16
    sequences, span, width = tokens.shape
    ny, nx, nz = lax.axis_size("y"), lax.axis_size("x"), lax.axis_size("z")
    team = ny * nx * 2
    core = lax.axis_index("c")
    rows = attention_weight.shape[0]
    q_width, kv_width = QUERY_HEADS * HEAD_SIZE, KEY_VALUE_HEADS * HEAD_SIZE
    count = sequences * span
    all_sequences = nx * 2 * sequences
    reach = ny * span
    near = is_square()
    ff_part = FF // team

    def columns(start, size):
        return pl.ds(pl.multiple_of(start, size), size)

    def take_attention(sources, member, c):
        source = sources[0]
        starts = (
            member * HEAD_SIZE,
            q_width + c * kv_width + (member - c) // 2 * HEAD_SIZE,
            q_width + 2 * kv_width + member * HEAD_SIZE,
        )
        return jnp.concatenate([source[:, columns(s, HEAD_SIZE)].astype(low) for s in starts], axis=1)

    def take_feed(*parts):
        return lambda sources, member, c: jnp.concatenate(
            [sources[0][:, columns(part * FF + member * ff_part, ff_part)].astype(low) for part in parts], axis=1
        )

    def spread(source, take, size, number, after=()):
        if is_square():
            blocks = plane_swap([source], [(rows, size)], [take], number, after)[0]
        else:
            blocks = swap(jnp.stack([take([source], member, member % 2) for member in range(8)]))
        return blocks, over_planes(blocks)

    team_base = lax.axis_index("z") * reach
    team_pos = team_base + jnp.arange(reach, dtype=jnp.int32)
    own_pos = team_base + lax.axis_index("y") * span + jnp.arange(span, dtype=jnp.int32)
    if near:
        key_pos = jnp.concatenate([team_pos - back * reach for back in range(nz)])
    else:
        key_pos = jnp.arange(nz * reach, dtype=jnp.int32)
    query_at, key_at = team_pos[:, None], key_pos[None, :]
    cos_table, sin_table = angle_tables(team_pos)
    cos_rows, sin_rows = (t.reshape(ny, 1, span, -1) for t in (cos_table, sin_table))
    valid = (own_pos[None, :] < lengths[:, None]).astype(jnp.float32).reshape(count, 1)
    lengths_all = lax.all_gather(lengths, ("x", "c"), axis=0, tiled=True)
    planes = jnp.arange(nz, dtype=jnp.int32)
    if near:
        planes = (lax.axis_index("z") - planes) % nz
    core_at = jnp.concatenate([jnp.reshape(core, (1,)), planes]).astype(jnp.int32)

    def heads(value):
        return value.reshape(ny, all_sequences, span, HEAD_SIZE)

    x_in = tokens.reshape(count, width).astype(jnp.float32)
    normed_one, inverse_one = rms_forward(x_in, norm_gains[0])
    outer_grad = cotangent.reshape(count, width).astype(jnp.float32) * valid
    if is_square():
        attention_mine, h1 = begin(
            attention_weight,
            tokens.reshape(count, width),
            norm_gains[:1],
            take_attention,
            3 * HEAD_SIZE,
            nz,
            1,
        )
        h1 = h1.reshape(-1, width)
    else:
        attention_mine = spread(attention_weight, take_attention, 3 * HEAD_SIZE, 1)[1]
        gate_up_blocks, gate_up_weight = spread(feed_weight, take_feed(0, 1), 2 * ff_part, 2)
        h1 = team_gather(normed_one.astype(low), 3)
    query_weight = attention_mine[:, :HEAD_SIZE]
    kv_weight = attention_mine[:, HEAD_SIZE : 2 * HEAD_SIZE]
    out_weight = attention_mine[:, 2 * HEAD_SIZE :]
    kv_raw = heads(mm(h1, kv_weight))
    kv = jnp.where(core == 0, rotate(kv_raw, cos_rows, sin_rows), kv_raw).astype(low)
    q = rotate(heads(mm(h1, query_weight)), cos_rows, sin_rows).astype(low)
    if is_square():
        kv, other, gate_up_blocks = climb(
            kv.reshape(-1, HEAD_SIZE), feed_weight, take_feed(0, 1), 2 * ff_part, nz, 2
        )
        kv, other = (t.reshape(nz, ny, all_sequences, span, HEAD_SIZE) for t in (kv, other))
        gate_up_weight = over_planes(gate_up_blocks)
    else:
        kv = lax.all_gather(kv, "z", axis=0, tiled=False)
        other = lax.ppermute(kv, "c", [(0, 1), (1, 0)])
    attend = (core_at, lengths_all, q, kv, other, query_at, key_at)
    (o,) = attention_call(attention_kernel, *attend, (), [("rows", low)], "attention")
    o = o.reshape(-1, HEAD_SIZE)
    r = x_in + team_sum([o], [out_weight], 4)

    normed_two, inverse_two = rms_forward(r, norm_gains[1])
    h2 = team_gather(normed_two.astype(low), 16)
    dyb = team_gather(outer_grad.astype(low), 15, [h2])
    down_blocks, down_weight = spread(feed_weight, take_feed(2), ff_part, 12, [dyb])
    gate_up_weight, down_blocks = together(gate_up_weight, down_blocks)
    both = mm(h2, gate_up_weight)
    gate, upward = both[:, :ff_part], both[:, ff_part:]
    sig = jax.nn.sigmoid(gate)
    m = (gate * sig * upward).astype(low)
    down_term = mm_tn(dyb, m).astype(low)
    down_rows = scatter_planes(down_term)
    down_weight, down_term = together(down_weight, down_term)
    d_both = feed_back(dyb, down_weight, both)
    gate_up_term = mm_tn(h2, d_both).astype(low)
    gate_up_rows = scatter_planes(gate_up_term)
    dh2 = team_sum([d_both], [gate_up_weight], 7, [gate_up_term, down_term])
    mid_grad, gain_two = rms_back(dh2, r, inverse_two, norm_gains[1])
    dr = outer_grad + mid_grad
    drb = team_gather(dr.astype(low), 13, [down_rows])

    do = heads(mm(drb, out_weight).astype(low))
    dq, keep, theirs = attention_call(
        attention_back_kernel,
        *attend,
        (do, cos_table, sin_table),
        [("rows", low), ("keys", jnp.float32), ("keys", low)],
        "attention_back",
    )
    dq = dq.reshape(-1, HEAD_SIZE)
    dkv = keep + lax.ppermute(theirs, "c", [(0, 1), (1, 0)]).astype(jnp.float32)
    low_terms = dkv.astype(low)
    feed_sum = team_sum([m], [down_weight], 5, [low_terms])
    down_grad = scatter_team(down_rows, 6, [low_terms])
    dkv = lax.psum_scatter(low_terms, "z", scatter_dimension=0, tiled=True)[0]
    gate_up_grad = scatter_team(gate_up_rows, 8, [feed_sum, down_grad])
    dkv, gate_up_grad = together(dkv, gate_up_grad)
    dkv = dkv.astype(jnp.float32)
    dkv = jnp.where(core == 0, rotate(dkv, cos_rows, -sin_rows), dkv).astype(low).reshape(-1, HEAD_SIZE)
    layer_output = (r + feed_sum).astype(low)
    attention_term = jnp.concatenate([mm_tn(h1, dq), mm_tn(h1, dkv), mm_tn(drb, o)], axis=1).astype(low)
    attention_rows = scatter_planes(attention_term)
    dh1 = team_sum([dq, dkv], [query_weight, kv_weight], 9, [attention_term])
    in_grad, gain_one = rms_back(dh1, x_in, inverse_one, norm_gains[0])
    input_gradient = dr + in_grad
    local_squares = sum(jnp.sum(jnp.square(part.astype(jnp.float32))) for part in (gate_up_rows, down_rows))
    lines = jnp.concatenate([jnp.stack([gain_one, gain_two]), jnp.full((6, width), local_squares)], axis=0)
    if is_square():
        lines = total_sum(lines, nz, 18)
        attention_grad, tile = turn(attention_rows, 10, (), nz)
    else:
        lines = lax.psum(lines, ALL)
        attention_grad = scatter_team(attention_rows, 10)
        tile = lax.psum(jnp.full((8, 128), jnp.sum(jnp.square(attention_rows.astype(jnp.float32)))), ALL)
    news = update(
        (lines, tile),
        (gate_up_grad, down_grad, attention_grad),
        (norm_gains, gain_mean, gain_square),
        (feed_weight, feed_mean, feed_square),
        (attention_weight, attention_mean, attention_square),
    )
    gains_new, gradient_norm, feed_new, attention_new = news[:3], news[3], news[4:8], news[8:]
    return (
        layer_output.reshape(sequences, span, width),
        input_gradient.reshape(sequences, span, width),
        gradient_norm.reshape(()),
        *attention_new,
        *feed_new,
        *gains_new,
    )


def solution(mesh):
    ctx, fsdp = mesh.shape["ctx"], mesh.shape["fsdp"]
    inner = QUERY_HEADS // fsdp
    fine = Mesh(mesh.devices.reshape(ctx // inner, inner, fsdp // 2, 2), ALL)
    act = P(("x", "c"), ("z", "y"), None)
    matrix = P(ALL, None)
    return jax.shard_map(
        local,
        mesh=fine,
        in_specs=(act, P(("x", "c")), P(), matrix, matrix, act, matrix, matrix, matrix, matrix, P(), P()),
        out_specs=(act, act, P(), matrix, matrix, matrix, matrix, matrix, matrix, matrix, matrix, P(), P(), P()),
        check_vma=False,
    )
```

```python
import functools

import jax
import jax.numpy as jnp
from jax import lax
from jax.experimental import pallas as pl
from jax.experimental.pallas import tpu as pltpu
from jax.sharding import Mesh, PartitionSpec as P

QUERY_HEADS = 8
KEY_VALUE_HEADS = 4
HEAD_SIZE = 256
FF = 8192
STEP = 10

norm_eps = 1e-06
rope_base = 1000042.0
masked_value = -1e30
clip_norm = 1.0
beta_one = 0.9
beta_two = 0.95
adam_eps = 1e-08
matrix_rate = 0.03
gain_rate = 0.4
weight_decay = 0.1

TEAM = ("y", "x", "c")
ALL = ("z", "y", "x", "c")


MESH = pl.DeviceIdType.MESH
VMEM = pl.BlockSpec(memory_space=pltpu.VMEM)
HBM = pl.BlockSpec(memory_space=pl.ANY)


def place():
    y, x, c = lax.axis_index("y"), lax.axis_index("x"), lax.axis_index("c")
    return y, x, c, lambda yy, xx, cc: (yy * 2 + xx) * 2 + cc


def greet(others):
    barrier = pltpu.get_barrier_semaphore()
    for other in others:
        pl.semaphore_signal(barrier, inc=1, device_id=other, device_id_type=MESH)
    pl.semaphore_wait(barrier, len(others))


def gather_kernel(src, *refs):
    out, send, recv, own = refs[-4:]
    y, x, c, index = place()
    to_x, to_y, to_s = {"x": 1 - x}, {"y": 1 - y}, {"c": 1 - c}
    me, at_x, at_y, at_d = index(y, x, c), index(y, 1 - x, c), index(1 - y, x, c), index(1 - y, 1 - x, c)
    half = src.shape[0] // 2
    rows = (pl.ds(0, half), pl.ds(half, half))
    local = pltpu.make_async_copy(src, out.at[me], own)
    local.start()
    greet((to_x, to_y, to_s))

    def hop(slot, block, part, where, first=False):
        piece = out.at[block, rows[part]]
        return pltpu.make_async_remote_copy(
            src_ref=src.at[rows[part]] if first else piece,
            dst_ref=piece,
            send_sem=send.at[slot],
            recv_sem=recv.at[slot],
            device_id=where,
            device_id_type=MESH,
        )

    x0, x1 = hop(0, me, 0, to_x, True), hop(1, me, 1, to_x, True)
    y1, y0 = hop(2, me, 1, to_y, True), hop(3, me, 0, to_y, True)
    s0, s1 = hop(4, me, 0, to_s, True), hop(5, me, 1, to_s, True)
    for copy in (x0, y1, x1, y0, s0, s1):
        copy.start()
    x0.wait_recv()
    d0 = hop(6, at_x, 0, to_y)
    d0.start()
    y1.wait_recv()
    d1 = hop(7, at_y, 1, to_x)
    d1.start()
    sx0, sy1 = hop(8, at_x, 0, to_s), hop(9, at_y, 1, to_s)
    sx0.start()
    sy1.start()
    x1.wait_recv()
    sx1 = hop(10, at_x, 1, to_s)
    sx1.start()
    y0.wait_recv()
    sy0 = hop(11, at_y, 0, to_s)
    sy0.start()
    d0.wait_recv()
    sd0 = hop(12, at_d, 0, to_s)
    sd0.start()
    d1.wait_recv()
    sd1 = hop(13, at_d, 1, to_s)
    sd1.start()
    for copy in (s0, s1, sx0, sy1, sx1, sy0, sd0, sd1):
        copy.wait_recv()
    for copy in (x0, x1, y0, y1, s0, s1, d0, d1, sx0, sy1, sx1, sy0, sd0, sd1):
        copy.wait_send()
    local.wait()


def plane_gather(value, number, after=()):
    return pl.pallas_call(
        gather_kernel,
        out_shape=jax.ShapeDtypeStruct((8, *value.shape), value.dtype),
        in_specs=[HBM] * (1 + len(after)),
        out_specs=HBM,
        scratch_shapes=[
            pltpu.SemaphoreType.DMA((14,)),
            pltpu.SemaphoreType.DMA((14,)),
            pltpu.SemaphoreType.DMA,
        ],
        compiler_params=pltpu.CompilerParams(collective_id=number, has_side_effects=True),
        cost_estimate=pl.CostEstimate(flops=1, bytes_accessed=1, transcendentals=0),
        name="plane_gather",
    )(value, *after)


def sum_kernel(lefts, terms, tile, *refs):
    a_refs, w_refs = refs[:lefts], refs[lefts : lefts + len(terms)]
    out, s_send, s_recv, d_send, d_recv, x_send, x_recv, y_send, y_recv, x_acc, y_acc, send, recv = refs[-13:]
    y, x, c, index = place()
    to_x, to_y, to_s = {"x": 1 - x}, {"y": 1 - y}, {"c": 1 - c}
    rows, width = out.shape
    half = rows // 2
    parts = (pl.ds(0, half), pl.ds(half, half))
    f32, low = jnp.float32, jnp.bfloat16

    def product(block, put):
        lines = pl.ds(pl.multiple_of(block * rows, rows), rows)

        @pl.loop(0, width // tile)
        def _(step):
            cols = pl.ds(pl.multiple_of(step * tile, tile), tile)
            total = None
            for (left, start), w_ref in zip(terms, w_refs):
                term = mm_nt(a_refs[left][lines, start : start + w_ref.shape[1]], w_ref[cols, :])
                total = term if total is None else total + term
            put(cols, total)

    def hop(slot, src, dst, where):
        copy = pltpu.make_async_remote_copy(
            src_ref=src, dst_ref=dst, send_sem=send.at[slot], recv_sem=recv.at[slot],
            device_id=where, device_id_type=MESH,
        )
        return copy

    def to_sibling(slot, yy, xx):
        def put(cols, total):
            s_send[slot, :, cols] = total.astype(low)

        product(index(yy, xx, 1 - c), put)
        copy = hop(slot, s_send.at[slot], s_recv.at[slot], to_s)
        copy.start()
        return copy

    def with_sibling(slot, yy, xx, keep):
        def put(cols, total):
            keep[:, cols] = (total + s_recv[slot, :, cols].astype(f32)).astype(keep.dtype)

        product(index(yy, xx, c), put)

    greet((to_x, to_y, to_s))
    s0 = to_sibling(0, 1 - y, 1 - x)
    s1 = to_sibling(1, y, 1 - x)
    s0.wait_recv()
    with_sibling(0, 1 - y, 1 - x, d_send)
    d0 = hop(4, d_send.at[parts[0]], d_recv.at[parts[0]], to_x)
    d1 = hop(5, d_send.at[parts[1]], d_recv.at[parts[1]], to_y)
    d0.start()
    d1.start()
    s1.wait_recv()
    with_sibling(1, y, 1 - x, x_acc)
    x_send[parts[0]] = x_acc[parts[0]].astype(low)
    x0 = hop(6, x_send.at[parts[0]], x_recv.at[parts[0]], to_x)
    x0.start()
    s2 = to_sibling(2, 1 - y, x)
    s2.wait_recv()
    with_sibling(2, 1 - y, x, y_acc)
    y_send[parts[1]] = y_acc[parts[1]].astype(low)
    y1 = hop(7, y_send.at[parts[1]], y_recv.at[parts[1]], to_y)
    y1.start()
    s3 = to_sibling(3, y, x)
    d1.wait_recv()
    x_send[parts[1]] = (x_acc[parts[1]] + d_recv[parts[1]].astype(f32)).astype(low)
    x1 = hop(8, x_send.at[parts[1]], x_recv.at[parts[1]], to_x)
    x1.start()
    d0.wait_recv()
    y_send[parts[0]] = (y_acc[parts[0]] + d_recv[parts[0]].astype(f32)).astype(low)
    y0 = hop(9, y_send.at[parts[0]], y_recv.at[parts[0]], to_y)
    y0.start()
    s3.wait_recv()
    with_sibling(3, y, x, out)
    x0.wait_recv()
    y1.wait_recv()
    x1.wait_recv()
    y0.wait_recv()
    out[...] += x_recv[...].astype(f32) + y_recv[...].astype(f32)
    for copy in (s0, s1, s2, s3, d0, d1, x0, x1, y0, y1):
        copy.wait_send()


def plane_sum(lefts, rights, number, after=(), tile=512):
    ends = [(left, start) for left, a in enumerate(lefts) for start in range(0, a.shape[1], rights[0].shape[1])]
    terms = tuple(ends[: len(rights)])
    rows, width = lefts[0].shape[0] // 8, rights[0].shape[0]
    block = (rows, width)
    low, f32 = jnp.bfloat16, jnp.float32
    return pl.pallas_call(
        functools.partial(sum_kernel, len(lefts), terms, min(tile, width)),
        out_shape=jax.ShapeDtypeStruct(block, f32),
        in_specs=[VMEM] * (len(lefts) + len(rights)) + [HBM] * len(after),
        out_specs=VMEM,
        scratch_shapes=[
            pltpu.VMEM((4, *block), low),
            pltpu.VMEM((4, *block), low),
            *[pltpu.VMEM(block, low)] * 6,
            pltpu.VMEM(block, f32),
            pltpu.VMEM(block, f32),
            pltpu.SemaphoreType.DMA((10,)),
            pltpu.SemaphoreType.DMA((10,)),
        ],
        compiler_params=pltpu.CompilerParams(
            collective_id=number, has_side_effects=True, vmem_limit_bytes=48 * 2**20
        ),
        cost_estimate=pl.CostEstimate(flops=1, bytes_accessed=1, transcendentals=0),
        name="plane_sum",
    )(*lefts, *rights, *after)


def swap_kernel(pieces, takes, *refs):
    count = len(pieces)
    sources, (send, recv, own) = refs[: -2 * count - 3], refs[-3:]
    outs, holds = refs[-2 * count - 3 : -count - 3], refs[-count - 3 : -3]
    y, x, c, index = place()
    me = index(y, x, c)
    flips = [(fy, fx, fc) for fy, fx in ((1, 1), (0, 1), (1, 0), (0, 0)) for fc in (0, 1)]
    flips = [flip for flip in flips if flip != (0, 0, 0)]

    def there(flip):
        return tuple(1 - at if f else at for at, f in zip((y, x, c), flip))

    greet([dict(zip(("y", "x", "c"), there(flip))) for flip in flips])
    copies = []
    for piece in range(count):
        for number, flip in enumerate(flips):
            yy, xx, cc = there(flip)
            member = index(yy, xx, cc)
            holds[piece][number] = takes[piece](sources, member, cc)
            copy = pltpu.make_async_remote_copy(
                src_ref=holds[piece].at[number],
                dst_ref=outs[piece].at[me],
                send_sem=send.at[piece * 7 + number],
                recv_sem=recv.at[piece * 7 + number],
                device_id={"y": yy, "x": xx, "c": cc},
                device_id_type=MESH,
            )
            copy.start()
            copies.append(copy)
        holds[piece][7] = takes[piece](sources, me, c)
        keep = pltpu.make_async_copy(holds[piece].at[7], outs[piece].at[me], own.at[piece])
        keep.start()
        copies.append(keep)
    for copy in copies:
        copy.wait()


def plane_swap(sources, shapes, takes, number, after=()):
    low = jnp.bfloat16
    count = len(shapes)
    return pl.pallas_call(
        functools.partial(swap_kernel, shapes, takes),
        out_shape=[jax.ShapeDtypeStruct((8, *shape), low) for shape in shapes],
        in_specs=[VMEM] * len(sources) + [HBM] * len(after),
        out_specs=[HBM] * count,
        scratch_shapes=[
            *[pltpu.VMEM((8, *shape), low) for shape in shapes],
            pltpu.SemaphoreType.DMA((7 * count,)),
            pltpu.SemaphoreType.DMA((7 * count,)),
            pltpu.SemaphoreType.DMA((count,)),
        ],
        compiler_params=pltpu.CompilerParams(
            collective_id=number, has_side_effects=True, vmem_limit_bytes=48 * 2**20
        ),
        cost_estimate=pl.CostEstimate(flops=1, bytes_accessed=1, transcendentals=0),
        name="plane_swap",
    )(*sources, *after)


def team_of(y, x, c):
    flips = [(fy, fx, fc) for fy, fx in ((1, 1), (0, 1), (1, 0), (0, 0)) for fc in (0, 1)]
    return [
        tuple(1 - at if f else at for at, f in zip((y, x, c), flip)) for flip in flips if flip != (0, 0, 0)
    ]


def turn_kernel(planes, src, *refs):
    y, x, c, index = place()
    me = index(y, x, c)
    others = team_of(y, x, c)
    ids = [dict(zip(("y", "x", "c"), other)) for other in others]
    if planes:
        out, total, near, far, held, send, recv, own, send_lines, recv_lines = refs[-10:]
        z = lax.axis_index("z")
        column = [{"z": lax.rem(z + step, planes)} for step in range(1, planes)]
        fetch = pltpu.make_async_copy(src, held, own)
        fetch.start()
        fetch.wait()
        squares = jnp.zeros((8, held.shape[1]), jnp.float32)
        for start in range(0, held.shape[0], 64):
            part = held[start : start + 64].astype(jnp.float32)
            squares += jnp.sum(jnp.square(part).reshape(8, 8, -1), axis=0)
        near[me] = jnp.broadcast_to(jnp.sum(squares, keepdims=True), near.shape[1:])
    else:
        out, send, recv, own = refs[-4:]
        column = []
    greet(ids + column)
    count = src.shape[0] // 8

    def rows(member):
        return src.at[pl.ds(pl.multiple_of(member * count, count), count)]

    def spread(buffer, at, where, base):
        copies = [
            pltpu.make_async_remote_copy(
                src_ref=buffer.at[at],
                dst_ref=buffer.at[at],
                send_sem=send_lines.at[base + number],
                recv_sem=recv_lines.at[base + number],
                device_id=other,
                device_id_type=MESH,
            )
            for number, other in enumerate(where)
        ]
        for copy in copies:
            copy.start()
        return copies

    small = spread(near, me, ids, 0) if planes else []
    copies = [
        pltpu.make_async_remote_copy(
            src_ref=rows(index(*other)),
            dst_ref=out.at[me],
            send_sem=send.at[number],
            recv_sem=recv.at[number],
            device_id=where,
            device_id_type=MESH,
        )
        for number, (other, where) in enumerate(zip(others, ids))
    ]
    copies.append(pltpu.make_async_copy(rows(me), out.at[me], own))
    for copy in copies:
        copy.start()
    if planes:
        for copy in small:
            copy.wait()
        far[z] = jnp.sum(near[...], axis=0)
        for copy in spread(far, z, column, 7):
            copy.wait()
        total[...] = jnp.sum(far[...], axis=0)
    for copy in copies:
        copy.wait()


def total_kernel(planes, src, *refs):
    out, near, far, send, recv = refs[-5:]
    y, x, c, index = place()
    z = lax.axis_index("z")
    ids = [dict(zip(("y", "x", "c"), other)) for other in team_of(y, x, c)]
    column = [{"z": lax.rem(z + step, planes)} for step in range(1, planes)]
    me = index(y, x, c)
    near[me] = src[...]
    greet(ids + column)

    def spread(buffer, at, where, base):
        copies = [
            pltpu.make_async_remote_copy(
                src_ref=buffer.at[at],
                dst_ref=buffer.at[at],
                send_sem=send.at[base + number],
                recv_sem=recv.at[base + number],
                device_id=other,
                device_id_type=MESH,
            )
            for number, other in enumerate(where)
        ]
        for copy in copies:
            copy.start()
        for copy in copies:
            copy.wait()

    spread(near, me, ids, 0)
    far[z] = jnp.sum(near[...], axis=0)
    spread(far, z, column, 7)
    out[...] = jnp.sum(far[...], axis=0)


def total_sum(value, planes, number, after=()):
    return pl.pallas_call(
        functools.partial(total_kernel, planes),
        out_shape=jax.ShapeDtypeStruct(value.shape, value.dtype),
        in_specs=[VMEM] + [HBM] * len(after),
        out_specs=VMEM,
        scratch_shapes=[pltpu.VMEM((size, *value.shape), value.dtype) for size in (8, planes)]
        + [pltpu.SemaphoreType.DMA((6 + planes,))] * 2,
        compiler_params=pltpu.CompilerParams(
            collective_id=number, has_side_effects=True, vmem_limit_bytes=16 * 2**20
        ),
        cost_estimate=pl.CostEstimate(flops=1, bytes_accessed=1, transcendentals=0),
        name="total_sum",
    )(value, *after)


def turn(rows, number, after=(), planes=0):
    block = (rows.shape[0] // 8, rows.shape[1])
    dma = pltpu.SemaphoreType.DMA
    out_shape, out_specs = [jax.ShapeDtypeStruct((8, *block), rows.dtype)], [HBM]
    scratch = [dma((7,)), dma((7,)), dma]
    if planes:
        tile = jax.ShapeDtypeStruct((8, 128), jnp.float32)
        out_shape.append(tile)
        out_specs.append(VMEM)
        buffers = [pltpu.VMEM((size, *tile.shape), tile.dtype) for size in (8, planes)]
        scratch = buffers + [pltpu.VMEM(rows.shape, rows.dtype)] + scratch + [dma((6 + planes,)), dma((6 + planes,))]
    return pl.pallas_call(
        functools.partial(turn_kernel, planes),
        out_shape=out_shape,
        in_specs=[HBM] * (1 + len(after)),
        out_specs=out_specs,
        scratch_shapes=scratch,
        compiler_params=pltpu.CompilerParams(
            collective_id=number, has_side_effects=True, vmem_limit_bytes=16 * 2**20
        ),
        cost_estimate=pl.CostEstimate(flops=1, bytes_accessed=1, transcendentals=0),
        name="turn",
    )(rows, *after)


def hops(planes, send, recv, block, up):
    z = lax.axis_index("z")

    def step(number):
        gone, came = (z - number + 1, z - number) if up else (z + number - 1, z + number)
        goes = ((gone >= 0) & (z + 1 < planes)) if up else ((gone < planes) & (z >= 1))
        comes = (came >= 0) if up else (came < planes)

        def copy(b):
            return pltpu.make_async_remote_copy(
                src_ref=block(b),
                dst_ref=block(b),
                send_sem=send.at[number - 1],
                recv_sem=recv.at[number - 1],
                device_id={"z": z + 1 if up else z - 1},
                device_id_type=MESH,
            )

        return (
            lambda: pl.when(goes)(lambda: copy(gone).start()),
            lambda: pl.when(comes)(lambda: copy(came).wait_recv()),
            lambda: pl.when(goes)(lambda: copy(gone).wait_send()),
        )

    return [step(number) for number in range(1, planes)]


def ring(planes):
    z = lax.axis_index("z")
    return [{"z": lax.rem(z + 1, planes)}, {"z": lax.rem(z + planes - 1, planes)}]


def spread_to(others, ids, source, take, hold, place_of, send, recv, own):
    y, x, c, index = place()
    me = index(y, x, c)
    copies = []
    for number, (other, where) in enumerate(zip(others, ids)):
        hold[number] = take([source], index(*other), other[2])
        copy = pltpu.make_async_remote_copy(
            src_ref=hold.at[number], dst_ref=place_of(me), send_sem=send.at[number], recv_sem=recv.at[number],
            device_id=where, device_id_type=MESH,
        )
        copy.start()
        copies.append(copy)
    hold[7] = take([source], me, c)
    keep = pltpu.make_async_copy(hold.at[7], place_of(me), own)
    keep.start()
    return copies, keep


def begin_kernel(
    planes, take, attention, tokens, gain, all_attention, all_rows,
    held, hold, rows, a_send, a_recv, r_send, r_recv, u_send, u_recv, d_send, d_recv, own,
):
    y, x, c, index = place()
    z = lax.axis_index("z")
    me, at_x, at_y, at_d = index(y, x, c), index(y, 1 - x, c), index(1 - y, x, c), index(1 - y, 1 - x, c)
    others = team_of(y, x, c)
    ids = [dict(zip(("y", "x", "c"), other)) for other in others]
    to_x, to_y, to_s = {"x": 1 - x}, {"y": 1 - y}, {"c": 1 - c}
    count = held.shape[0]
    half = rows.shape[0] // 2
    parts = (pl.ds(0, half), pl.ds(half, half))
    fetch = pltpu.make_async_copy(attention, held, own.at[0])
    fetch.start()
    greet(ids + ring(planes))
    fetch.wait()

    def attention_rows(start, size):
        return all_attention.at[pl.ds(pl.multiple_of(start, count), size)]

    a_copies, a_keep = spread_to(
        others, ids, held, take, hold, lambda m: attention_rows((z * 8 + m) * count, count), a_send, a_recv, own.at[1]
    )

    def hop(slot, block, part, where, first=False):
        piece = all_rows.at[block, parts[part]]
        copy = pltpu.make_async_remote_copy(
            src_ref=rows.at[parts[part]] if first else piece, dst_ref=piece,
            send_sem=r_send.at[slot], recv_sem=r_recv.at[slot], device_id=where, device_id_type=MESH,
        )
        copy.start()
        return copy

    for copy in a_copies:
        copy.wait_recv()
    a_keep.wait()

    def plane_block(b):
        return attention_rows(b * 8 * count, 8 * count)

    up = hops(planes, u_send, u_recv, plane_block, True)
    down = hops(planes, d_send, d_recv, plane_block, False)

    def pass_on(number):
        if number > 0:
            up[number - 1][1]()
            down[number - 1][1]()
        if number < planes - 1:
            up[number][0]()
            down[number][0]()

    pass_on(0)

    @pl.loop(0, rows.shape[0] // 16)
    def _(group):
        lines = pl.ds(pl.multiple_of(group * 16, 16), 16)
        rows[lines] = rms_forward(tokens[lines].astype(jnp.float32), gain[...])[0].astype(rows.dtype)

    x0, y1 = hop(0, me, 0, to_x, True), hop(2, me, 1, to_y, True)
    x1, y0 = hop(1, me, 1, to_x, True), hop(3, me, 0, to_y, True)
    s0, s1 = hop(4, me, 0, to_s, True), hop(5, me, 1, to_s, True)
    mine = pltpu.make_async_copy(rows, all_rows.at[me], own.at[2])
    mine.start()
    x0.wait_recv()
    d0 = hop(6, at_x, 0, to_y)
    y1.wait_recv()
    d1 = hop(7, at_y, 1, to_x)
    sx0, sy1 = hop(8, at_x, 0, to_s), hop(9, at_y, 1, to_s)
    pass_on(1)
    x1.wait_recv()
    sx1 = hop(10, at_x, 1, to_s)
    y0.wait_recv()
    sy0 = hop(11, at_y, 0, to_s)
    d0.wait_recv()
    sd0 = hop(12, at_d, 0, to_s)
    d1.wait_recv()
    sd1 = hop(13, at_d, 1, to_s)
    for number in range(2, planes):
        pass_on(number)
    for copy in (s0, s1, sx0, sy1, sx1, sy0, sd0, sd1):
        copy.wait_recv()
    for copy in (x0, x1, y0, y1, s0, s1, d0, d1, sx0, sy1, sx1, sy0, sd0, sd1, *a_copies):
        copy.wait_send()
    for step in up + down:
        step[2]()
    mine.wait()


def begin(attention, tokens, gain, take, columns, planes, number):
    low, dma = jnp.bfloat16, pltpu.SemaphoreType.DMA
    count = attention.shape[0]
    return pl.pallas_call(
        functools.partial(begin_kernel, planes, take),
        out_shape=[
            jax.ShapeDtypeStruct((planes * 8 * count, columns), low),
            jax.ShapeDtypeStruct((8, *tokens.shape), low),
        ],
        in_specs=[HBM, VMEM, VMEM],
        out_specs=[HBM] * 2,
        scratch_shapes=[
            pltpu.VMEM(attention.shape, attention.dtype),
            pltpu.VMEM((8, count, columns), low),
            pltpu.VMEM(tokens.shape, low),
            *[dma((size,)) for size in (7, 7, 14, 14, *[planes - 1] * 4, 3)],
        ],
        compiler_params=pltpu.CompilerParams(
            collective_id=number, has_side_effects=True, vmem_limit_bytes=32 * 2**20
        ),
        cost_estimate=pl.CostEstimate(flops=1, bytes_accessed=1, transcendentals=0),
        name="begin",
    )(attention, tokens, gain)


def climb_kernel(
    planes, take, block, feed, mine, other, columns, zeros, stay, held, hold, u_send, u_recv, s_send, s_recv, f_send, f_recv, own, fill
):
    y, x, c, index = place()
    z = lax.axis_index("z")
    to_s = {"c": 1 - c}
    others = team_of(y, x, c)
    ids = [dict(zip(("y", "x", "c"), where)) for where in others]
    fetch = pltpu.make_async_copy(feed.at[:, pl.ds(0, held.shape[1])], held, own.at[1])
    fetch.start()
    greet(ids + ring(planes))

    def across(n):
        return pltpu.make_async_remote_copy(
            src_ref=block if n == 0 else mine.at[n], dst_ref=other.at[n], send_sem=s_send.at[n], recv_sem=s_recv.at[n],
            device_id=to_s, device_id_type=MESH,
        )

    def along(n):
        return pltpu.make_async_remote_copy(
            src_ref=block if n == 1 else mine.at[n - 1], dst_ref=mine.at[n], send_sem=u_send.at[n - 1], recv_sem=u_recv.at[n - 1],
            device_id={"z": z + 1}, device_id_type=MESH,
        )

    pull = pltpu.make_async_copy(block, stay, own.at[3])
    keep = pltpu.make_async_copy(stay, mine.at[0], own.at[0])
    more = z + 1 < planes
    pl.when(more)(lambda: along(1).start())
    across(0).start()
    pull.start()
    zeros[...] = jnp.zeros_like(zeros)
    pull.wait()
    keep.start()
    for n in range(1, planes):

        @pl.when(z < n)
        def _():
            for number, buffer in enumerate((mine, other)):
                pltpu.make_async_copy(zeros, buffer.at[n], fill.at[2 * (n - 1) + number]).start()

    fetch.wait()
    f_copies, f_keep = spread_to(others, ids, held, take, hold, lambda m: columns.at[m], f_send, f_recv, own.at[2])
    for n in range(1, planes):

        @pl.when(z >= n)
        def _():
            along(n).wait_recv()
            if n + 1 < planes:
                pl.when(more)(lambda: along(n + 1).start())
            across(n).start()

    across(0).wait()
    keep.wait()
    for copy in f_copies:
        copy.wait()
    f_keep.wait()
    for n in range(1, planes):

        @pl.when(z >= n)
        def _():
            across(n).wait()

        @pl.when(z < n)
        def _():
            for number, buffer in enumerate((mine, other)):
                pltpu.make_async_copy(zeros, buffer.at[n], fill.at[2 * (n - 1) + number]).wait()

        pl.when((z >= n - 1) & more)(lambda: along(n).wait_send())


def climb(block, feed, take, columns, planes, number):
    dma = pltpu.SemaphoreType.DMA
    count = feed.shape[0]
    blocks = jax.ShapeDtypeStruct((planes, *block.shape), block.dtype)
    return pl.pallas_call(
        functools.partial(climb_kernel, planes, take),
        out_shape=[blocks, blocks, jax.ShapeDtypeStruct((8, count, columns), block.dtype)],
        in_specs=[HBM, HBM],
        out_specs=[HBM] * 3,
        scratch_shapes=[
            pltpu.VMEM(block.shape, block.dtype),
            pltpu.VMEM(block.shape, block.dtype),
            pltpu.VMEM((count, 8 * columns), feed.dtype),
            pltpu.VMEM((8, count, columns), block.dtype),
            *[dma((size,)) for size in (planes - 1, planes - 1, planes, planes, 7, 7, 4, 2 * (planes - 1))],
        ],
        compiler_params=pltpu.CompilerParams(
            collective_id=number, has_side_effects=True, vmem_limit_bytes=56 * 2**20
        ),
        cost_estimate=pl.CostEstimate(flops=1, bytes_accessed=1, transcendentals=0),
        name="climb",
    )(block, feed)


def dot(left, right, contract):
    return lax.dot_general(left, right, (contract, ((), ())), preferred_element_type=jnp.float32)


def mm(left, right):
    return dot(left, right, ((1,), (0,)))


def mm_nt(left, right):
    return dot(left, right, ((1,), (1,)))


def mm_tn(left, right):
    return dot(left, right, ((0,), (0,)))


def bmm(pattern, left, right):
    return jnp.einsum(pattern, left, right, preferred_element_type=jnp.float32)


def angle_tables(positions):
    half_dim = HEAD_SIZE // 2
    frequency = rope_base ** (-(jnp.arange(half_dim).astype(jnp.float32) * 2.0) / HEAD_SIZE)
    phases = positions.astype(jnp.float32)[:, None] * frequency[None, :]
    return (jnp.cos(phases), jnp.sin(phases))


def rotate(value, cos_table, sin_table):
    half = value.shape[-1] // 2
    a, b = value[..., :half], value[..., half:]
    return jnp.concatenate([a * cos_table - b * sin_table, b * cos_table + a * sin_table], axis=-1)


def rms_forward(value, gain_row):
    inverse = lax.rsqrt(jnp.mean(value * value, axis=-1, keepdims=True) + norm_eps)
    return (value * inverse * gain_row, inverse)


def rms_back(grad_out, value, inverse, gain_row):
    scaled = grad_out * gain_row
    grad_in = inverse * (
        scaled - value * inverse * inverse * jnp.mean(scaled * value, axis=-1, keepdims=True)
    )
    return (grad_in, jnp.sum(grad_out * value * inverse, axis=0))


def adamw(weight, gradient, moment_one, moment_two, step_rate, decay_rate, invert=jnp.reciprocal):
    mean_new = beta_one * moment_one + (1.0 - beta_one) * gradient
    square_new = beta_two * moment_two + (1.0 - beta_two) * gradient * gradient
    below = jnp.sqrt(square_new * (1.0 / (1.0 - beta_two**STEP))) + adam_eps
    direction = mean_new * (1.0 / (1.0 - beta_one**STEP)) * invert(below)
    return (weight - step_rate * (direction + decay_rate * weight), mean_new, square_new)


def attention_parts(core, length, q_ref, mine_ref, other_ref, query_ref, key_ref):
    mine, other = mine_ref[...].reshape(-1, HEAD_SIZE), other_ref[...].reshape(-1, HEAD_SIZE)
    first = core == 0
    k, v = jnp.where(first, mine, other), jnp.where(first, other, mine)
    q = q_ref[...].reshape(-1, HEAD_SIZE)
    at, key_at = query_ref[...], key_ref[...]
    allowed = (key_at <= at) & (key_at < length) & (key_at >= 0)
    scores = jnp.where(allowed, mm_nt(q, k) * HEAD_SIZE ** (-0.5), masked_value)
    exponent = jnp.exp(scores - jnp.max(scores, axis=-1, keepdims=True))
    return q, k, v, exponent / jnp.sum(exponent, axis=-1, keepdims=True)


def attention_kernel(core_ref, length_ref, q_ref, mine_ref, other_ref, query_ref, key_ref, out_ref):
    length = length_ref[pl.program_id(0)]
    _, _, v, soft = attention_parts(core_ref[0], length, q_ref, mine_ref, other_ref, query_ref, key_ref)
    out_ref[...] = mm(soft.astype(jnp.bfloat16), v).astype(jnp.bfloat16).reshape(out_ref.shape)


def attention_back_kernel(
    core_ref, length_ref, q_ref, mine_ref, other_ref, query_ref, key_ref, do_ref, cos_ref, sin_ref,
    dq_ref, keep_ref, send_ref,
):
    low = jnp.bfloat16
    core = core_ref[0]
    length = length_ref[pl.program_id(0)]
    q, k, v, soft = attention_parts(core, length, q_ref, mine_ref, other_ref, query_ref, key_ref)
    do = do_ref[...].reshape(-1, HEAD_SIZE)
    dp = mm_nt(do, v)
    delta = jnp.sum(soft * dp, axis=-1, keepdims=True)
    ds = (soft * (dp - delta) * HEAD_SIZE ** (-0.5)).astype(low)
    dq = mm(ds, k)
    cos_table, sin_table = cos_ref[...], sin_ref[...]
    half = HEAD_SIZE // 2
    a, b = dq[:, :half], dq[:, half:]
    turned = jnp.concatenate([a * cos_table + b * sin_table, b * cos_table - a * sin_table], axis=-1)
    dq_ref[...] = turned.astype(low).reshape(dq_ref.shape)
    dk, dv = mm_tn(ds, q), mm_tn(soft.astype(low), do)
    first = core == 0
    keep, send = (t.reshape(keep_ref.shape) for t in (jnp.where(first, dk, dv), jnp.where(first, dv, dk)))
    for block in range(keep_ref.shape[0]):
        at = core_ref[1 + block]
        keep_ref[at] = keep[block]
        send_ref[at] = send[block].astype(low)


def attention_call(kernel, core, lengths, q, mine, other, query_pos, key_pos, extra, outs, name):
    ny, count, span, size = q.shape
    nz = mine.shape[0]
    rows = pl.BlockSpec((ny, 1, span, size), lambda i, *_: (0, i, 0, 0))
    keys = pl.BlockSpec((nz, ny, 1, span, size), lambda i, *_: (0, 0, i, 0, 0))

    def whole(value):
        return pl.BlockSpec(value.shape, lambda i, *_: (0,) * value.ndim)

    kinds = {"rows": (rows, q.shape), "keys": (keys, mine.shape)}
    return pl.pallas_call(
        kernel,
        grid_spec=pltpu.PrefetchScalarGridSpec(
            num_scalar_prefetch=2,
            grid=(count,),
            in_specs=[rows, keys, keys, whole(query_pos), whole(key_pos)]
            + [rows if value.shape == q.shape else whole(value) for value in extra],
            out_specs=[kinds[kind][0] for kind, _ in outs],
        ),
        out_shape=[jax.ShapeDtypeStruct(kinds[kind][1], dtype) for kind, dtype in outs],
        compiler_params=pltpu.CompilerParams(vmem_limit_bytes=48 * 2**20),
        cost_estimate=pl.CostEstimate(flops=1, bytes_accessed=1, transcendentals=0),
        name=name,
    )(core, lengths, q, mine, other, query_pos, key_pos, *extra)


def feed_back_kernel(dyb_ref, weight_ref, gate_ref, up_ref, out_ref):
    dm = mm(dyb_ref[...], weight_ref[...])
    gate, upward = gate_ref[...], up_ref[...]
    sig = jax.nn.sigmoid(gate)
    part = gate.shape[1]
    out_ref[:, :part] = (dm * upward * sig * (1.0 + gate * (1.0 - sig))).astype(out_ref.dtype)
    out_ref[:, part:] = (dm * gate * sig).astype(out_ref.dtype)


def feed_back(dyb, weight, both, lines=256):
    count, part = both.shape[0], both.shape[1] // 2

    def rows(width, column=0):
        return pl.BlockSpec((lines, width), lambda i: (i, column))

    return pl.pallas_call(
        feed_back_kernel,
        grid=(count // lines,),
        in_specs=[rows(dyb.shape[1]), pl.BlockSpec(weight.shape, lambda i: (0, 0)), rows(part), rows(part, 1)],
        out_specs=rows(2 * part),
        out_shape=jax.ShapeDtypeStruct((count, 2 * part), jnp.bfloat16),
        compiler_params=pltpu.CompilerParams(vmem_limit_bytes=48 * 2**20),
        cost_estimate=pl.CostEstimate(flops=1, bytes_accessed=1, transcendentals=0),
        name="feed_back",
    )(dyb, weight, both, both)


def close_reciprocal(value):
    guess = pltpu.reciprocal(value, approx=True)
    return guess * (2.0 - value * guess)


def norm_of(lines_ref, tile_ref):
    gains = lines_ref[:-8]
    return jnp.sqrt(jnp.sum(gains * gains, keepdims=True) + lines_ref[-8:-7, 0:1] + tile_ref[0:1, 0:1])


def update_kernel(feed_steps, *refs):
    lines_ref, tile_ref, gain_ref, gate_up_ref, down_ref, attention_ref = refs[:6]
    gains, feed, attention = refs[6:9], refs[9:12], refs[12:15]
    new_gains, norm_ref, new_feed, new_attention, factor_ref = refs[15:18], refs[18], refs[19:23], refs[23:27], refs[27]
    step = pl.program_id(0)

    @pl.when(step == 0)
    def _():
        norm = norm_of(lines_ref, tile_ref)
        norm_ref[...] = norm
        factor_ref[...] = clip_norm / norm
        weight, mean, square = (ref[...] for ref in gains)
        gradient = gain_ref[...] * factor_ref[...]
        for ref, value in zip(new_gains, adamw(weight, gradient, mean, square, gain_rate, 0.0)):
            ref[...] = value

    def matrix(olds, news, size, grad_ref, member_of, start):
        factor = factor_ref[...]
        piece = min(size, 512)

        @pl.loop(0, olds[0].shape[0] // 16)
        def _(group):
            lines = pl.ds(pl.multiple_of(group * 16, 16), 16)
            for number in range(olds[0].shape[1] // size):
                for offset in range(0, size, piece):
                    at = pl.ds(number * size + offset, piece)
                    from_ = pl.ds(pl.multiple_of(start + offset, 256), piece)
                    gradient = grad_ref[member_of(number), lines, from_].astype(jnp.float32) * factor
                    weight, mean, square = (ref[lines, at] for ref in olds)
                    values = adamw(weight, gradient, mean, square, matrix_rate, weight_decay, close_reciprocal)
                    for ref, value in zip(news, (*values, values[0])):
                        ref[lines, at] = value.astype(ref.dtype)

    size = down_ref.shape[2]
    half = feed_steps // 3

    @pl.when(step < 2 * half)
    def _():
        matrix(feed, new_feed, size, gate_up_ref, lambda n: 4 * (step % half) + n, step // half * size)

    @pl.when((step >= 2 * half) & (step < feed_steps))
    def _():
        matrix(feed, new_feed, size, down_ref, lambda n: 4 * (step % half) + n, 0)

    kind = step - feed_steps
    for number, order in ((0, lambda n: n), (1, lambda n: 2 * (n % 4) + n // 4), (2, lambda n: n)):

        @pl.when(kind == number)
        def _():
            matrix(attention, new_attention, HEAD_SIZE, attention_ref, order, number * HEAD_SIZE)


def update(sums, grads, gains, feed, attention):
    f32, low = jnp.float32, jnp.bfloat16
    rows = feed[0].shape[0]
    wide, narrow = 4096, 2048
    feed_steps, attention_steps = feed[0].shape[1] // wide, attention[0].shape[1] // narrow
    feed_block = pl.BlockSpec((rows, wide), lambda i: (0, jnp.minimum(i, feed_steps - 1)))
    attention_block = pl.BlockSpec((rows, narrow), lambda i: (0, jnp.maximum(i - feed_steps, 0)))

    def whole(value):
        return pl.BlockSpec(value.shape, lambda i: (0,) * value.ndim)

    norm = jax.ShapeDtypeStruct((1, 1), f32)
    matrices = [jax.ShapeDtypeStruct(part[0].shape, dtype) for part in (feed, attention) for dtype in (f32, f32, f32, low)]
    return pl.pallas_call(
        functools.partial(update_kernel, feed_steps),
        grid=(feed_steps + attention_steps,),
        in_specs=[whole(value) for value in (*sums, *grads, *gains)] + [feed_block] * 3 + [attention_block] * 3,
        out_specs=[whole(value) for value in (*gains, norm)] + [feed_block] * 4 + [attention_block] * 4,
        out_shape=[jax.ShapeDtypeStruct(gains[0].shape, f32)] * 3 + [norm] + matrices,
        scratch_shapes=[pltpu.VMEM((1, 1), f32)],
        compiler_params=pltpu.CompilerParams(vmem_limit_bytes=56 * 2**20),
        name="update",
    )(*sums, *grads, *gains, *feed, *attention)


def is_square():
    return lax.axis_size("y") == 2 and lax.axis_size("x") == 2


def swap(blocks):
    return lax.all_to_all(blocks, TEAM, split_axis=0, concat_axis=0, tiled=True)


def over_planes(blocks):
    return lax.all_gather(blocks.reshape(-1, blocks.shape[-1]), "z", axis=0, tiled=True)


def scatter_planes(term):
    return lax.psum_scatter(term, "z", scatter_dimension=0, tiled=True)


def together(*values):
    return lax.optimization_barrier(values)


def scatter_team(rows, number, after=()):
    if not is_square():
        return swap(rows.reshape(8, -1, rows.shape[-1]))
    return turn(rows, number, after)[0]


def team_gather(local, number, after=()):
    if not is_square():
        return lax.all_gather(local, TEAM, axis=0, tiled=True)
    return plane_gather(local, number, after).reshape(-1, local.shape[1])


def team_sum(lefts, rights, number, after=()):
    if is_square():
        return plane_sum(lefts, rights, number, after)
    partial = mm_nt(jnp.concatenate(lefts, axis=1), jnp.concatenate(rights, axis=1))
    return lax.psum_scatter(partial.astype(jnp.bfloat16), TEAM, scatter_dimension=0, tiled=True).astype(jnp.float32)


def local(
    tokens,
    lengths,
    norm_gains,
    attention_weight,
    feed_weight,
    cotangent,
    attention_mean,
    attention_square,
    feed_mean,
    feed_square,
    gain_mean,
    gain_square,
):
    low = jnp.bfloat16
    sequences, span, width = tokens.shape
    ny, nx, nz = lax.axis_size("y"), lax.axis_size("x"), lax.axis_size("z")
    team = ny * nx * 2
    core = lax.axis_index("c")
    rows = attention_weight.shape[0]
    q_width, kv_width = QUERY_HEADS * HEAD_SIZE, KEY_VALUE_HEADS * HEAD_SIZE
    count = sequences * span
    all_sequences = nx * 2 * sequences
    reach = ny * span
    near = is_square()
    ff_part = FF // team

    def columns(start, size):
        return pl.ds(pl.multiple_of(start, size), size)

    def take_attention(sources, member, c):
        source = sources[0]
        starts = (
            member * HEAD_SIZE,
            q_width + c * kv_width + (member - c) // 2 * HEAD_SIZE,
            q_width + 2 * kv_width + member * HEAD_SIZE,
        )
        return jnp.concatenate([source[:, columns(s, HEAD_SIZE)].astype(low) for s in starts], axis=1)

    def take_feed(*parts):
        return lambda sources, member, c: jnp.concatenate(
            [sources[0][:, columns(part * FF + member * ff_part, ff_part)].astype(low) for part in parts], axis=1
        )

    def spread(source, take, size, number, after=()):
        if is_square():
            blocks = plane_swap([source], [(rows, size)], [take], number, after)[0]
        else:
            blocks = swap(jnp.stack([take([source], member, member % 2) for member in range(8)]))
        return blocks, over_planes(blocks)

    team_base = lax.axis_index("z") * reach
    team_pos = team_base + jnp.arange(reach, dtype=jnp.int32)
    own_pos = team_base + lax.axis_index("y") * span + jnp.arange(span, dtype=jnp.int32)
    if near:
        key_pos = jnp.concatenate([team_pos - back * reach for back in range(nz)])
    else:
        key_pos = jnp.arange(nz * reach, dtype=jnp.int32)
    query_at, key_at = team_pos[:, None], key_pos[None, :]
    cos_table, sin_table = angle_tables(team_pos)
    cos_rows, sin_rows = (t.reshape(ny, 1, span, -1) for t in (cos_table, sin_table))
    valid = (own_pos[None, :] < lengths[:, None]).astype(jnp.float32).reshape(count, 1)
    lengths_all = lax.all_gather(lengths, ("x", "c"), axis=0, tiled=True)
    planes = jnp.arange(nz, dtype=jnp.int32)
    if near:
        planes = (lax.axis_index("z") - planes) % nz
    core_at = jnp.concatenate([jnp.reshape(core, (1,)), planes]).astype(jnp.int32)

    def heads(value):
        return value.reshape(ny, all_sequences, span, HEAD_SIZE)

    x_in = tokens.reshape(count, width).astype(jnp.float32)
    normed_one, inverse_one = rms_forward(x_in, norm_gains[0])
    outer_grad = cotangent.reshape(count, width).astype(jnp.float32) * valid
    if is_square():
        attention_mine, h1 = begin(
            attention_weight,
            tokens.reshape(count, width),
            norm_gains[:1],
            take_attention,
            3 * HEAD_SIZE,
            nz,
            1,
        )
        h1 = h1.reshape(-1, width)
    else:
        attention_mine = spread(attention_weight, take_attention, 3 * HEAD_SIZE, 1)[1]
        gate_up_blocks, gate_up_weight = spread(feed_weight, take_feed(0, 1), 2 * ff_part, 2)
        h1 = team_gather(normed_one.astype(low), 3)
    query_weight = attention_mine[:, :HEAD_SIZE]
    kv_weight = attention_mine[:, HEAD_SIZE : 2 * HEAD_SIZE]
    out_weight = attention_mine[:, 2 * HEAD_SIZE :]
    kv_raw = heads(mm(h1, kv_weight))
    kv = jnp.where(core == 0, rotate(kv_raw, cos_rows, sin_rows), kv_raw).astype(low)
    q = rotate(heads(mm(h1, query_weight)), cos_rows, sin_rows).astype(low)
    if is_square():
        kv, other, gate_up_blocks = climb(
            kv.reshape(-1, HEAD_SIZE), feed_weight, take_feed(0, 1), 2 * ff_part, nz, 2
        )
        kv, other = (t.reshape(nz, ny, all_sequences, span, HEAD_SIZE) for t in (kv, other))
        gate_up_weight = over_planes(gate_up_blocks)
    else:
        kv = lax.all_gather(kv, "z", axis=0, tiled=False)
        other = lax.ppermute(kv, "c", [(0, 1), (1, 0)])
    attend = (core_at, lengths_all, q, kv, other, query_at, key_at)
    (o,) = attention_call(attention_kernel, *attend, (), [("rows", low)], "attention")
    o = o.reshape(-1, HEAD_SIZE)
    r = x_in + team_sum([o], [out_weight], 4)

    normed_two, inverse_two = rms_forward(r, norm_gains[1])
    h2 = team_gather(normed_two.astype(low), 16)
    dyb = team_gather(outer_grad.astype(low), 15, [h2])
    down_blocks, down_weight = spread(feed_weight, take_feed(2), ff_part, 12, [dyb])
    gate_up_weight, down_blocks = together(gate_up_weight, down_blocks)
    both = mm(h2, gate_up_weight)
    gate, upward = both[:, :ff_part], both[:, ff_part:]
    sig = jax.nn.sigmoid(gate)
    m = (gate * sig * upward).astype(low)
    down_term = mm_tn(dyb, m).astype(low)
    down_rows = scatter_planes(down_term)
    down_weight, down_term = together(down_weight, down_term)
    d_both = feed_back(dyb, down_weight, both)
    gate_up_term = mm_tn(h2, d_both).astype(low)
    gate_up_rows = scatter_planes(gate_up_term)
    dh2 = team_sum([d_both], [gate_up_weight], 7, [gate_up_term, down_term])
    mid_grad, gain_two = rms_back(dh2, r, inverse_two, norm_gains[1])
    dr = outer_grad + mid_grad
    drb = team_gather(dr.astype(low), 13, [down_rows])

    do = heads(mm(drb, out_weight).astype(low))
    dq, keep, theirs = attention_call(
        attention_back_kernel,
        *attend,
        (do, cos_table, sin_table),
        [("rows", low), ("keys", jnp.float32), ("keys", low)],
        "attention_back",
    )
    dq = dq.reshape(-1, HEAD_SIZE)
    dkv = keep + lax.ppermute(theirs, "c", [(0, 1), (1, 0)]).astype(jnp.float32)
    low_terms = dkv.astype(low)
    feed_sum = team_sum([m], [down_weight], 5, [low_terms])
    down_grad = scatter_team(down_rows, 6, [low_terms])
    dkv = lax.psum_scatter(low_terms, "z", scatter_dimension=0, tiled=True)[0]
    gate_up_grad = scatter_team(gate_up_rows, 8, [feed_sum, down_grad])
    dkv, gate_up_grad = together(dkv, gate_up_grad)
    dkv = dkv.astype(jnp.float32)
    dkv = jnp.where(core == 0, rotate(dkv, cos_rows, -sin_rows), dkv).astype(low).reshape(-1, HEAD_SIZE)
    layer_output = (r + feed_sum).astype(low)
    attention_term = jnp.concatenate([mm_tn(h1, dq), mm_tn(h1, dkv), mm_tn(drb, o)], axis=1).astype(low)
    attention_rows = scatter_planes(attention_term)
    dh1 = team_sum([dq, dkv], [query_weight, kv_weight], 9, [attention_term])
    in_grad, gain_one = rms_back(dh1, x_in, inverse_one, norm_gains[0])
    input_gradient = dr + in_grad
    local_squares = sum(jnp.sum(jnp.square(part.astype(jnp.float32))) for part in (gate_up_rows, down_rows))
    gain_local = jnp.stack([gain_one, gain_two]).reshape(-1, 128)
    lines = jnp.concatenate([gain_local, jnp.full((8, 128), local_squares)], axis=0)
    if is_square():
        lines = total_sum(lines, nz, 18)
        attention_grad, tile = turn(attention_rows, 10, (), nz)
    else:
        lines = lax.psum(lines, ALL)
        attention_grad = scatter_team(attention_rows, 10)
        tile = lax.psum(jnp.full((8, 128), jnp.sum(jnp.square(attention_rows.astype(jnp.float32)))), ALL)
    gain_grad = lines[:-8].reshape(2, width)
    news = update(
        (lines, tile, gain_grad),
        (gate_up_grad, down_grad, attention_grad),
        (norm_gains, gain_mean, gain_square),
        (feed_weight, feed_mean, feed_square),
        (attention_weight, attention_mean, attention_square),
    )
    gains_new, gradient_norm, feed_new, attention_new = news[:3], news[3], news[4:8], news[8:]
    return (
        layer_output.reshape(sequences, span, width),
        input_gradient.reshape(sequences, span, width),
        gradient_norm.reshape(()),
        *attention_new,
        *feed_new,
        *gains_new,
    )


def solution(mesh):
    ctx, fsdp = mesh.shape["ctx"], mesh.shape["fsdp"]
    inner = QUERY_HEADS // fsdp
    fine = Mesh(mesh.devices.reshape(ctx // inner, inner, fsdp // 2, 2), ALL)
    act = P(("x", "c"), ("z", "y"), None)
    matrix = P(ALL, None)
    return jax.shard_map(
        local,
        mesh=fine,
        in_specs=(act, P(("x", "c")), P(), matrix, matrix, act, matrix, matrix, matrix, matrix, P(), P()),
        out_specs=(act, act, P(), matrix, matrix, matrix, matrix, matrix, matrix, matrix, matrix, P(), P(), P()),
        check_vma=False,
    )
```

```python
import functools

import jax
import jax.numpy as jnp
from jax import lax
from jax.experimental import pallas as pl
from jax.experimental.pallas import tpu as pltpu
from jax.sharding import Mesh, PartitionSpec as P

QUERY_HEADS = 8
KEY_VALUE_HEADS = 4
HEAD_SIZE = 256
FF = 8192
STEP = 10

norm_eps = 1e-06
rope_base = 1000042.0
masked_value = -1e30
clip_norm = 1.0
beta_one = 0.9
beta_two = 0.95
adam_eps = 1e-08
matrix_rate = 0.03
gain_rate = 0.4
weight_decay = 0.1

TEAM = ("y", "x", "c")
ALL = ("z", "y", "x", "c")


MESH = pl.DeviceIdType.MESH
VMEM = pl.BlockSpec(memory_space=pltpu.VMEM)
HBM = pl.BlockSpec(memory_space=pl.ANY)


def place():
    y, x, c = lax.axis_index("y"), lax.axis_index("x"), lax.axis_index("c")
    return y, x, c, lambda yy, xx, cc: (yy * 2 + xx) * 2 + cc


def greet(others):
    barrier = pltpu.get_barrier_semaphore()
    for other in others:
        pl.semaphore_signal(barrier, inc=1, device_id=other, device_id_type=MESH)
    pl.semaphore_wait(barrier, len(others))


def gather_kernel(src, *refs):
    out, send, recv, own = refs[-4:]
    y, x, c, index = place()
    to_x, to_y, to_s = {"x": 1 - x}, {"y": 1 - y}, {"c": 1 - c}
    me, at_x, at_y, at_d = index(y, x, c), index(y, 1 - x, c), index(1 - y, x, c), index(1 - y, 1 - x, c)
    half = src.shape[0] // 2
    rows = (pl.ds(0, half), pl.ds(half, half))
    local = pltpu.make_async_copy(src, out.at[me], own)
    local.start()
    greet((to_x, to_y, to_s))

    def hop(slot, block, part, where, first=False):
        piece = out.at[block, rows[part]]
        return pltpu.make_async_remote_copy(
            src_ref=src.at[rows[part]] if first else piece,
            dst_ref=piece,
            send_sem=send.at[slot],
            recv_sem=recv.at[slot],
            device_id=where,
            device_id_type=MESH,
        )

    x0, x1 = hop(0, me, 0, to_x, True), hop(1, me, 1, to_x, True)
    y1, y0 = hop(2, me, 1, to_y, True), hop(3, me, 0, to_y, True)
    s0, s1 = hop(4, me, 0, to_s, True), hop(5, me, 1, to_s, True)
    for copy in (x0, y1, x1, y0, s0, s1):
        copy.start()
    x0.wait_recv()
    d0 = hop(6, at_x, 0, to_y)
    d0.start()
    y1.wait_recv()
    d1 = hop(7, at_y, 1, to_x)
    d1.start()
    sx0, sy1 = hop(8, at_x, 0, to_s), hop(9, at_y, 1, to_s)
    sx0.start()
    sy1.start()
    x1.wait_recv()
    sx1 = hop(10, at_x, 1, to_s)
    sx1.start()
    y0.wait_recv()
    sy0 = hop(11, at_y, 0, to_s)
    sy0.start()
    d0.wait_recv()
    sd0 = hop(12, at_d, 0, to_s)
    sd0.start()
    d1.wait_recv()
    sd1 = hop(13, at_d, 1, to_s)
    sd1.start()
    for copy in (s0, s1, sx0, sy1, sx1, sy0, sd0, sd1):
        copy.wait_recv()
    for copy in (x0, x1, y0, y1, s0, s1, d0, d1, sx0, sy1, sx1, sy0, sd0, sd1):
        copy.wait_send()
    local.wait()


def plane_gather(value, number, after=()):
    return pl.pallas_call(
        gather_kernel,
        out_shape=jax.ShapeDtypeStruct((8, *value.shape), value.dtype),
        in_specs=[HBM] * (1 + len(after)),
        out_specs=HBM,
        scratch_shapes=[
            pltpu.SemaphoreType.DMA((14,)),
            pltpu.SemaphoreType.DMA((14,)),
            pltpu.SemaphoreType.DMA,
        ],
        compiler_params=pltpu.CompilerParams(collective_id=number, has_side_effects=True),
        cost_estimate=pl.CostEstimate(flops=1, bytes_accessed=1, transcendentals=0),
        name="plane_gather",
    )(value, *after)


def sum_kernel(lefts, terms, tile, *refs):
    a_refs, w_refs = refs[:lefts], refs[lefts : lefts + len(terms)]
    out, s_send, s_recv, d_send, d_recv, x_send, x_recv, y_send, y_recv, x_acc, y_acc, send, recv = refs[-13:]
    y, x, c, index = place()
    to_x, to_y, to_s = {"x": 1 - x}, {"y": 1 - y}, {"c": 1 - c}
    rows, width = out.shape
    half = rows // 2
    parts = (pl.ds(0, half), pl.ds(half, half))
    f32, low = jnp.float32, jnp.bfloat16

    def product(block, put):
        lines = pl.ds(pl.multiple_of(block * rows, rows), rows)

        @pl.loop(0, width // tile)
        def _(step):
            cols = pl.ds(pl.multiple_of(step * tile, tile), tile)
            total = None
            for (left, start), w_ref in zip(terms, w_refs):
                term = mm_nt(a_refs[left][lines, start : start + w_ref.shape[1]], w_ref[cols, :])
                total = term if total is None else total + term
            put(cols, total)

    def hop(slot, src, dst, where):
        copy = pltpu.make_async_remote_copy(
            src_ref=src, dst_ref=dst, send_sem=send.at[slot], recv_sem=recv.at[slot],
            device_id=where, device_id_type=MESH,
        )
        return copy

    def to_sibling(slot, yy, xx):
        def put(cols, total):
            s_send[slot, :, cols] = total.astype(low)

        product(index(yy, xx, 1 - c), put)
        copy = hop(slot, s_send.at[slot], s_recv.at[slot], to_s)
        copy.start()
        return copy

    def with_sibling(slot, yy, xx, keep):
        def put(cols, total):
            keep[:, cols] = (total + s_recv[slot, :, cols].astype(f32)).astype(keep.dtype)

        product(index(yy, xx, c), put)

    greet((to_x, to_y, to_s))
    s0 = to_sibling(0, 1 - y, 1 - x)
    s1 = to_sibling(1, y, 1 - x)
    s0.wait_recv()
    with_sibling(0, 1 - y, 1 - x, d_send)
    d0 = hop(4, d_send.at[parts[0]], d_recv.at[parts[0]], to_x)
    d1 = hop(5, d_send.at[parts[1]], d_recv.at[parts[1]], to_y)
    d0.start()
    d1.start()
    s1.wait_recv()
    with_sibling(1, y, 1 - x, x_acc)
    x_send[parts[0]] = x_acc[parts[0]].astype(low)
    x0 = hop(6, x_send.at[parts[0]], x_recv.at[parts[0]], to_x)
    x0.start()
    s2 = to_sibling(2, 1 - y, x)
    s2.wait_recv()
    with_sibling(2, 1 - y, x, y_acc)
    y_send[parts[1]] = y_acc[parts[1]].astype(low)
    y1 = hop(7, y_send.at[parts[1]], y_recv.at[parts[1]], to_y)
    y1.start()
    s3 = to_sibling(3, y, x)
    d1.wait_recv()
    x_send[parts[1]] = (x_acc[parts[1]] + d_recv[parts[1]].astype(f32)).astype(low)
    x1 = hop(8, x_send.at[parts[1]], x_recv.at[parts[1]], to_x)
    x1.start()
    d0.wait_recv()
    y_send[parts[0]] = (y_acc[parts[0]] + d_recv[parts[0]].astype(f32)).astype(low)
    y0 = hop(9, y_send.at[parts[0]], y_recv.at[parts[0]], to_y)
    y0.start()
    s3.wait_recv()
    with_sibling(3, y, x, out)
    x0.wait_recv()
    y1.wait_recv()
    x1.wait_recv()
    y0.wait_recv()
    out[...] += x_recv[...].astype(f32) + y_recv[...].astype(f32)
    for copy in (s0, s1, s2, s3, d0, d1, x0, x1, y0, y1):
        copy.wait_send()


def plane_sum(lefts, rights, number, after=(), tile=512):
    ends = [(left, start) for left, a in enumerate(lefts) for start in range(0, a.shape[1], rights[0].shape[1])]
    terms = tuple(ends[: len(rights)])
    rows, width = lefts[0].shape[0] // 8, rights[0].shape[0]
    block = (rows, width)
    low, f32 = jnp.bfloat16, jnp.float32
    return pl.pallas_call(
        functools.partial(sum_kernel, len(lefts), terms, min(tile, width)),
        out_shape=jax.ShapeDtypeStruct(block, f32),
        in_specs=[VMEM] * (len(lefts) + len(rights)) + [HBM] * len(after),
        out_specs=VMEM,
        scratch_shapes=[
            pltpu.VMEM((4, *block), low),
            pltpu.VMEM((4, *block), low),
            *[pltpu.VMEM(block, low)] * 6,
            pltpu.VMEM(block, f32),
            pltpu.VMEM(block, f32),
            pltpu.SemaphoreType.DMA((10,)),
            pltpu.SemaphoreType.DMA((10,)),
        ],
        compiler_params=pltpu.CompilerParams(
            collective_id=number, has_side_effects=True, vmem_limit_bytes=48 * 2**20
        ),
        cost_estimate=pl.CostEstimate(flops=1, bytes_accessed=1, transcendentals=0),
        name="plane_sum",
    )(*lefts, *rights, *after)


def swap_kernel(pieces, takes, *refs):
    count = len(pieces)
    sources, (send, recv, own) = refs[: -2 * count - 3], refs[-3:]
    outs, holds = refs[-2 * count - 3 : -count - 3], refs[-count - 3 : -3]
    y, x, c, index = place()
    me = index(y, x, c)
    flips = [(fy, fx, fc) for fy, fx in ((1, 1), (0, 1), (1, 0), (0, 0)) for fc in (0, 1)]
    flips = [flip for flip in flips if flip != (0, 0, 0)]

    def there(flip):
        return tuple(1 - at if f else at for at, f in zip((y, x, c), flip))

    greet([dict(zip(("y", "x", "c"), there(flip))) for flip in flips])
    copies = []
    for piece in range(count):
        for number, flip in enumerate(flips):
            yy, xx, cc = there(flip)
            member = index(yy, xx, cc)
            holds[piece][number] = takes[piece](sources, member, cc)
            copy = pltpu.make_async_remote_copy(
                src_ref=holds[piece].at[number],
                dst_ref=outs[piece].at[me],
                send_sem=send.at[piece * 7 + number],
                recv_sem=recv.at[piece * 7 + number],
                device_id={"y": yy, "x": xx, "c": cc},
                device_id_type=MESH,
            )
            copy.start()
            copies.append(copy)
        holds[piece][7] = takes[piece](sources, me, c)
        keep = pltpu.make_async_copy(holds[piece].at[7], outs[piece].at[me], own.at[piece])
        keep.start()
        copies.append(keep)
    for copy in copies:
        copy.wait()


def plane_swap(sources, shapes, takes, number, after=()):
    low = jnp.bfloat16
    count = len(shapes)
    return pl.pallas_call(
        functools.partial(swap_kernel, shapes, takes),
        out_shape=[jax.ShapeDtypeStruct((8, *shape), low) for shape in shapes],
        in_specs=[VMEM] * len(sources) + [HBM] * len(after),
        out_specs=[HBM] * count,
        scratch_shapes=[
            *[pltpu.VMEM((8, *shape), low) for shape in shapes],
            pltpu.SemaphoreType.DMA((7 * count,)),
            pltpu.SemaphoreType.DMA((7 * count,)),
            pltpu.SemaphoreType.DMA((count,)),
        ],
        compiler_params=pltpu.CompilerParams(
            collective_id=number, has_side_effects=True, vmem_limit_bytes=48 * 2**20
        ),
        cost_estimate=pl.CostEstimate(flops=1, bytes_accessed=1, transcendentals=0),
        name="plane_swap",
    )(*sources, *after)


def team_of(y, x, c):
    flips = [(fy, fx, fc) for fy, fx in ((1, 1), (0, 1), (1, 0), (0, 0)) for fc in (0, 1)]
    return [
        tuple(1 - at if f else at for at, f in zip((y, x, c), flip)) for flip in flips if flip != (0, 0, 0)
    ]


def turn_kernel(planes, src, *refs):
    y, x, c, index = place()
    me = index(y, x, c)
    others = team_of(y, x, c)
    ids = [dict(zip(("y", "x", "c"), other)) for other in others]
    if planes:
        out, total, near, far, held, send, recv, own, send_lines, recv_lines = refs[-10:]
        z = lax.axis_index("z")
        column = [{"z": lax.rem(z + step, planes)} for step in range(1, planes)]
        fetch = pltpu.make_async_copy(src, held, own)
        fetch.start()
        fetch.wait()
        squares = jnp.zeros((8, held.shape[1]), jnp.float32)
        for start in range(0, held.shape[0], 64):
            part = held[start : start + 64].astype(jnp.float32)
            squares += jnp.sum(jnp.square(part).reshape(8, 8, -1), axis=0)
        near[me] = jnp.broadcast_to(jnp.sum(squares, keepdims=True), near.shape[1:])
    else:
        out, send, recv, own = refs[-4:]
        column = []
    greet(ids + column)
    count = src.shape[0] // 8

    def rows(member):
        return src.at[pl.ds(pl.multiple_of(member * count, count), count)]

    def spread(buffer, at, where, base):
        copies = [
            pltpu.make_async_remote_copy(
                src_ref=buffer.at[at],
                dst_ref=buffer.at[at],
                send_sem=send_lines.at[base + number],
                recv_sem=recv_lines.at[base + number],
                device_id=other,
                device_id_type=MESH,
            )
            for number, other in enumerate(where)
        ]
        for copy in copies:
            copy.start()
        return copies

    small = spread(near, me, ids, 0) if planes else []
    copies = [
        pltpu.make_async_remote_copy(
            src_ref=rows(index(*other)),
            dst_ref=out.at[me],
            send_sem=send.at[number],
            recv_sem=recv.at[number],
            device_id=where,
            device_id_type=MESH,
        )
        for number, (other, where) in enumerate(zip(others, ids))
    ]
    copies.append(pltpu.make_async_copy(rows(me), out.at[me], own))
    for copy in copies:
        copy.start()
    if planes:
        for copy in small:
            copy.wait()
        far[z] = jnp.sum(near[...], axis=0)
        for copy in spread(far, z, column, 7):
            copy.wait()
        total[...] = jnp.sum(far[...], axis=0)
    for copy in copies:
        copy.wait()


def total_kernel(planes, src, *refs):
    out, near, far, send, recv = refs[-5:]
    y, x, c, index = place()
    z = lax.axis_index("z")
    ids = [dict(zip(("y", "x", "c"), other)) for other in team_of(y, x, c)]
    column = [{"z": lax.rem(z + step, planes)} for step in range(1, planes)]
    me = index(y, x, c)
    near[me] = src[...]
    greet(ids + column)

    def spread(buffer, at, where, base):
        copies = [
            pltpu.make_async_remote_copy(
                src_ref=buffer.at[at],
                dst_ref=buffer.at[at],
                send_sem=send.at[base + number],
                recv_sem=recv.at[base + number],
                device_id=other,
                device_id_type=MESH,
            )
            for number, other in enumerate(where)
        ]
        for copy in copies:
            copy.start()
        for copy in copies:
            copy.wait()

    spread(near, me, ids, 0)
    far[z] = jnp.sum(near[...], axis=0)
    spread(far, z, column, 7)
    out[...] = jnp.sum(far[...], axis=0)


def total_sum(value, planes, number, after=()):
    return pl.pallas_call(
        functools.partial(total_kernel, planes),
        out_shape=jax.ShapeDtypeStruct(value.shape, value.dtype),
        in_specs=[VMEM] + [HBM] * len(after),
        out_specs=VMEM,
        scratch_shapes=[pltpu.VMEM((size, *value.shape), value.dtype) for size in (8, planes)]
        + [pltpu.SemaphoreType.DMA((6 + planes,))] * 2,
        compiler_params=pltpu.CompilerParams(
            collective_id=number, has_side_effects=True, vmem_limit_bytes=16 * 2**20
        ),
        cost_estimate=pl.CostEstimate(flops=1, bytes_accessed=1, transcendentals=0),
        name="total_sum",
    )(value, *after)


def turn(rows, number, after=(), planes=0):
    block = (rows.shape[0] // 8, rows.shape[1])
    dma = pltpu.SemaphoreType.DMA
    out_shape, out_specs = [jax.ShapeDtypeStruct((8, *block), rows.dtype)], [HBM]
    scratch = [dma((7,)), dma((7,)), dma]
    if planes:
        tile = jax.ShapeDtypeStruct((8, 128), jnp.float32)
        out_shape.append(tile)
        out_specs.append(VMEM)
        buffers = [pltpu.VMEM((size, *tile.shape), tile.dtype) for size in (8, planes)]
        scratch = buffers + [pltpu.VMEM(rows.shape, rows.dtype)] + scratch + [dma((6 + planes,)), dma((6 + planes,))]
    return pl.pallas_call(
        functools.partial(turn_kernel, planes),
        out_shape=out_shape,
        in_specs=[HBM] * (1 + len(after)),
        out_specs=out_specs,
        scratch_shapes=scratch,
        compiler_params=pltpu.CompilerParams(
            collective_id=number, has_side_effects=True, vmem_limit_bytes=16 * 2**20
        ),
        cost_estimate=pl.CostEstimate(flops=1, bytes_accessed=1, transcendentals=0),
        name="turn",
    )(rows, *after)


def hops(planes, send, recv, block, up):
    z = lax.axis_index("z")

    def step(number):
        gone, came = (z - number + 1, z - number) if up else (z + number - 1, z + number)
        goes = ((gone >= 0) & (z + 1 < planes)) if up else ((gone < planes) & (z >= 1))
        comes = (came >= 0) if up else (came < planes)

        def copy(b):
            return pltpu.make_async_remote_copy(
                src_ref=block(b),
                dst_ref=block(b),
                send_sem=send.at[number - 1],
                recv_sem=recv.at[number - 1],
                device_id={"z": z + 1 if up else z - 1},
                device_id_type=MESH,
            )

        return (
            lambda: pl.when(goes)(lambda: copy(gone).start()),
            lambda: pl.when(comes)(lambda: copy(came).wait_recv()),
            lambda: pl.when(goes)(lambda: copy(gone).wait_send()),
        )

    return [step(number) for number in range(1, planes)]


def ring(planes):
    z = lax.axis_index("z")
    return [{"z": lax.rem(z + 1, planes)}, {"z": lax.rem(z + planes - 1, planes)}]


def spread_to(others, ids, source, take, hold, place_of, send, recv, own):
    y, x, c, index = place()
    me = index(y, x, c)
    copies = []
    for number, (other, where) in enumerate(zip(others, ids)):
        hold[number] = take([source], index(*other), other[2])
        copy = pltpu.make_async_remote_copy(
            src_ref=hold.at[number], dst_ref=place_of(me), send_sem=send.at[number], recv_sem=recv.at[number],
            device_id=where, device_id_type=MESH,
        )
        copy.start()
        copies.append(copy)
    hold[7] = take([source], me, c)
    keep = pltpu.make_async_copy(hold.at[7], place_of(me), own)
    keep.start()
    return copies, keep


def begin_kernel(
    planes, take, attention, tokens, gain, all_attention, all_rows,
    held, hold, rows, a_send, a_recv, r_send, r_recv, u_send, u_recv, d_send, d_recv, own,
):
    y, x, c, index = place()
    z = lax.axis_index("z")
    me, at_x, at_y, at_d = index(y, x, c), index(y, 1 - x, c), index(1 - y, x, c), index(1 - y, 1 - x, c)
    others = team_of(y, x, c)
    ids = [dict(zip(("y", "x", "c"), other)) for other in others]
    to_x, to_y, to_s = {"x": 1 - x}, {"y": 1 - y}, {"c": 1 - c}
    count = held.shape[0]
    half = rows.shape[0] // 2
    parts = (pl.ds(0, half), pl.ds(half, half))
    fetch = pltpu.make_async_copy(attention, held, own.at[0])
    fetch.start()
    greet(ids + ring(planes))
    fetch.wait()

    def attention_rows(start, size):
        return all_attention.at[pl.ds(pl.multiple_of(start, count), size)]

    a_copies, a_keep = spread_to(
        others, ids, held, take, hold, lambda m: attention_rows((z * 8 + m) * count, count), a_send, a_recv, own.at[1]
    )

    def hop(slot, block, part, where, first=False):
        piece = all_rows.at[block, parts[part]]
        copy = pltpu.make_async_remote_copy(
            src_ref=rows.at[parts[part]] if first else piece, dst_ref=piece,
            send_sem=r_send.at[slot], recv_sem=r_recv.at[slot], device_id=where, device_id_type=MESH,
        )
        copy.start()
        return copy

    for copy in a_copies:
        copy.wait_recv()
    a_keep.wait()

    def plane_block(b):
        return attention_rows(b * 8 * count, 8 * count)

    up = hops(planes, u_send, u_recv, plane_block, True)
    down = hops(planes, d_send, d_recv, plane_block, False)

    def pass_on(number):
        if number > 0:
            up[number - 1][1]()
            down[number - 1][1]()
        if number < planes - 1:
            up[number][0]()
            down[number][0]()

    pass_on(0)

    @pl.loop(0, rows.shape[0] // 16)
    def _(group):
        lines = pl.ds(pl.multiple_of(group * 16, 16), 16)
        rows[lines] = rms_forward(tokens[lines].astype(jnp.float32), gain[...])[0].astype(rows.dtype)

    x0, y1 = hop(0, me, 0, to_x, True), hop(2, me, 1, to_y, True)
    x1, y0 = hop(1, me, 1, to_x, True), hop(3, me, 0, to_y, True)
    s0, s1 = hop(4, me, 0, to_s, True), hop(5, me, 1, to_s, True)
    mine = pltpu.make_async_copy(rows, all_rows.at[me], own.at[2])
    mine.start()
    x0.wait_recv()
    d0 = hop(6, at_x, 0, to_y)
    y1.wait_recv()
    d1 = hop(7, at_y, 1, to_x)
    sx0, sy1 = hop(8, at_x, 0, to_s), hop(9, at_y, 1, to_s)
    pass_on(1)
    x1.wait_recv()
    sx1 = hop(10, at_x, 1, to_s)
    y0.wait_recv()
    sy0 = hop(11, at_y, 0, to_s)
    d0.wait_recv()
    sd0 = hop(12, at_d, 0, to_s)
    d1.wait_recv()
    sd1 = hop(13, at_d, 1, to_s)
    for number in range(2, planes):
        pass_on(number)
    for copy in (s0, s1, sx0, sy1, sx1, sy0, sd0, sd1):
        copy.wait_recv()
    for copy in (x0, x1, y0, y1, s0, s1, d0, d1, sx0, sy1, sx1, sy0, sd0, sd1, *a_copies):
        copy.wait_send()
    for step in up + down:
        step[2]()
    mine.wait()


def begin(attention, tokens, gain, take, columns, planes, number):
    low, dma = jnp.bfloat16, pltpu.SemaphoreType.DMA
    count = attention.shape[0]
    return pl.pallas_call(
        functools.partial(begin_kernel, planes, take),
        out_shape=[
            jax.ShapeDtypeStruct((planes * 8 * count, columns), low),
            jax.ShapeDtypeStruct((8, *tokens.shape), low),
        ],
        in_specs=[HBM, VMEM, VMEM],
        out_specs=[HBM] * 2,
        scratch_shapes=[
            pltpu.VMEM(attention.shape, attention.dtype),
            pltpu.VMEM((8, count, columns), low),
            pltpu.VMEM(tokens.shape, low),
            *[dma((size,)) for size in (7, 7, 14, 14, *[planes - 1] * 4, 3)],
        ],
        compiler_params=pltpu.CompilerParams(
            collective_id=number, has_side_effects=True, vmem_limit_bytes=32 * 2**20
        ),
        cost_estimate=pl.CostEstimate(flops=1, bytes_accessed=1, transcendentals=0),
        name="begin",
    )(attention, tokens, gain)


def climb_kernel(
    planes, take, block, feed, mine, other, columns, zeros, stay, held, hold, u_send, u_recv, s_send, s_recv, f_send, f_recv, own, fill
):
    y, x, c, index = place()
    z = lax.axis_index("z")
    to_s = {"c": 1 - c}
    others = team_of(y, x, c)
    ids = [dict(zip(("y", "x", "c"), where)) for where in others]
    fetch = pltpu.make_async_copy(feed.at[:, pl.ds(0, held.shape[1])], held, own.at[1])
    fetch.start()
    greet(ids + ring(planes))

    def across(n):
        return pltpu.make_async_remote_copy(
            src_ref=block if n == 0 else mine.at[n], dst_ref=other.at[n], send_sem=s_send.at[n], recv_sem=s_recv.at[n],
            device_id=to_s, device_id_type=MESH,
        )

    def along(n):
        return pltpu.make_async_remote_copy(
            src_ref=block if n == 1 else mine.at[n - 1], dst_ref=mine.at[n], send_sem=u_send.at[n - 1], recv_sem=u_recv.at[n - 1],
            device_id={"z": z + 1}, device_id_type=MESH,
        )

    pull = pltpu.make_async_copy(block, stay, own.at[3])
    keep = pltpu.make_async_copy(stay, mine.at[0], own.at[0])
    more = z + 1 < planes
    pl.when(more)(lambda: along(1).start())
    across(0).start()
    pull.start()
    zeros[...] = jnp.zeros_like(zeros)
    pull.wait()
    keep.start()
    for n in range(1, planes):

        @pl.when(z < n)
        def _():
            for number, buffer in enumerate((mine, other)):
                pltpu.make_async_copy(zeros, buffer.at[n], fill.at[2 * (n - 1) + number]).start()

    fetch.wait()
    f_copies, f_keep = spread_to(others, ids, held, take, hold, lambda m: columns.at[m], f_send, f_recv, own.at[2])
    for n in range(1, planes):

        @pl.when(z >= n)
        def _():
            along(n).wait_recv()
            if n + 1 < planes:
                pl.when(more)(lambda: along(n + 1).start())
            across(n).start()

    across(0).wait()
    keep.wait()
    for copy in f_copies:
        copy.wait()
    f_keep.wait()
    for n in range(1, planes):

        @pl.when(z >= n)
        def _():
            across(n).wait()

        @pl.when(z < n)
        def _():
            for number, buffer in enumerate((mine, other)):
                pltpu.make_async_copy(zeros, buffer.at[n], fill.at[2 * (n - 1) + number]).wait()

        pl.when((z >= n - 1) & more)(lambda: along(n).wait_send())


def climb(block, feed, take, columns, planes, number):
    dma = pltpu.SemaphoreType.DMA
    count = feed.shape[0]
    blocks = jax.ShapeDtypeStruct((planes, *block.shape), block.dtype)
    return pl.pallas_call(
        functools.partial(climb_kernel, planes, take),
        out_shape=[blocks, blocks, jax.ShapeDtypeStruct((8, count, columns), block.dtype)],
        in_specs=[HBM, HBM],
        out_specs=[HBM] * 3,
        scratch_shapes=[
            pltpu.VMEM(block.shape, block.dtype),
            pltpu.VMEM(block.shape, block.dtype),
            pltpu.VMEM((count, 8 * columns), feed.dtype),
            pltpu.VMEM((8, count, columns), block.dtype),
            *[dma((size,)) for size in (planes - 1, planes - 1, planes, planes, 7, 7, 4, 2 * (planes - 1))],
        ],
        compiler_params=pltpu.CompilerParams(
            collective_id=number, has_side_effects=True, vmem_limit_bytes=56 * 2**20
        ),
        cost_estimate=pl.CostEstimate(flops=1, bytes_accessed=1, transcendentals=0),
        name="climb",
    )(block, feed)


def fall_kernel(planes, terms, rows, out, blocks, sends, recvs, send, recv, t_send, t_recv, own):
    y, x, c, index = place()
    z = lax.axis_index("z")
    me = index(y, x, c)
    others = team_of(y, x, c)
    ids = [dict(zip(("y", "x", "c"), other)) for other in others]
    f32 = jnp.float32
    count = rows.shape[0] // 8
    greet(ids + ring(planes))

    def rows_of(member):
        return rows.at[pl.ds(pl.multiple_of(member * count, count), count)]

    def hop(step):
        return pltpu.make_async_remote_copy(
            src_ref=sends.at[step - 1], dst_ref=recvs.at[step - 1], send_sem=send.at[step - 1], recv_sem=recv.at[step - 1],
            device_id={"z": z - 1}, device_id_type=MESH,
        )

    def came(step):
        return (z + 1 < planes) & (z + 1 + step - planes >= 0)

    copies = [
        pltpu.make_async_remote_copy(
            src_ref=rows_of(index(*other)), dst_ref=blocks.at[me], send_sem=t_send.at[number], recv_sem=t_recv.at[number],
            device_id=where, device_id_type=MESH,
        )
        for number, (other, where) in enumerate(zip(others, ids))
    ]
    copies.append(pltpu.make_async_copy(rows_of(me), blocks.at[me], own))
    for step in range(1, planes):
        block = z + step - planes
        if step > 1:
            pl.when(came(step - 1))(lambda: hop(step - 1).wait_recv())

        @pl.when((block >= 0) & (z + 1 == planes))
        def _():
            sends[step - 1] = terms[block]

        if step > 1:

            @pl.when((block >= 0) & (z + 1 < planes))
            def _():
                sends[step - 1] = (terms[block].astype(f32) + recvs[step - 2].astype(f32)).astype(terms.dtype)

        pl.when(block >= 0)(lambda: hop(step).start())
        if step == 1:
            for copy in copies:
                copy.start()
    last = planes - 1
    out[...] = terms[z].astype(f32)

    @pl.when(came(last))
    def _():
        hop(last).wait_recv()
        out[...] += recvs[last - 1].astype(f32)

    for step in range(1, planes):
        pl.when(z + step - planes >= 0)(lambda: hop(step).wait_send())
    for copy in copies:
        copy.wait()


def fall(terms, rows, planes, number, after=()):
    block = terms.shape[1:]
    dma = pltpu.SemaphoreType.DMA
    return pl.pallas_call(
        lambda terms, rows, *refs: fall_kernel(planes, terms, rows, *refs[len(after) :]),
        out_shape=[
            jax.ShapeDtypeStruct(block, jnp.float32),
            jax.ShapeDtypeStruct((8, rows.shape[0] // 8, rows.shape[1]), rows.dtype),
        ],
        in_specs=[VMEM, HBM] + [HBM] * len(after),
        out_specs=[VMEM, HBM],
        scratch_shapes=[pltpu.VMEM((planes - 1, *block), terms.dtype)] * 2
        + [dma((planes - 1,))] * 2
        + [dma((7,)), dma((7,)), dma],
        compiler_params=pltpu.CompilerParams(
            collective_id=number, has_side_effects=True, vmem_limit_bytes=40 * 2**20
        ),
        cost_estimate=pl.CostEstimate(flops=1, bytes_accessed=1, transcendentals=0),
        name="fall",
    )(terms, rows, *after)


def dot(left, right, contract):
    return lax.dot_general(left, right, (contract, ((), ())), preferred_element_type=jnp.float32)


def mm(left, right):
    return dot(left, right, ((1,), (0,)))


def mm_nt(left, right):
    return dot(left, right, ((1,), (1,)))


def mm_tn(left, right):
    return dot(left, right, ((0,), (0,)))


def bmm(pattern, left, right):
    return jnp.einsum(pattern, left, right, preferred_element_type=jnp.float32)


def angle_tables(positions):
    half_dim = HEAD_SIZE // 2
    frequency = rope_base ** (-(jnp.arange(half_dim).astype(jnp.float32) * 2.0) / HEAD_SIZE)
    phases = positions.astype(jnp.float32)[:, None] * frequency[None, :]
    return (jnp.cos(phases), jnp.sin(phases))


def rotate(value, cos_table, sin_table):
    half = value.shape[-1] // 2
    a, b = value[..., :half], value[..., half:]
    return jnp.concatenate([a * cos_table - b * sin_table, b * cos_table + a * sin_table], axis=-1)


def rms_forward(value, gain_row):
    inverse = lax.rsqrt(jnp.mean(value * value, axis=-1, keepdims=True) + norm_eps)
    return (value * inverse * gain_row, inverse)


def rms_back(grad_out, value, inverse, gain_row):
    scaled = grad_out * gain_row
    grad_in = inverse * (
        scaled - value * inverse * inverse * jnp.mean(scaled * value, axis=-1, keepdims=True)
    )
    return (grad_in, jnp.sum(grad_out * value * inverse, axis=0))


def adamw(weight, gradient, moment_one, moment_two, step_rate, decay_rate, invert=jnp.reciprocal):
    mean_new = beta_one * moment_one + (1.0 - beta_one) * gradient
    square_new = beta_two * moment_two + (1.0 - beta_two) * gradient * gradient
    below = jnp.sqrt(square_new * (1.0 / (1.0 - beta_two**STEP))) + adam_eps
    direction = mean_new * (1.0 / (1.0 - beta_one**STEP)) * invert(below)
    return (weight - step_rate * (direction + decay_rate * weight), mean_new, square_new)


def attention_parts(core, length, q_ref, mine_ref, other_ref, query_ref, key_ref):
    mine, other = mine_ref[...].reshape(-1, HEAD_SIZE), other_ref[...].reshape(-1, HEAD_SIZE)
    first = core == 0
    k, v = jnp.where(first, mine, other), jnp.where(first, other, mine)
    q = q_ref[...].reshape(-1, HEAD_SIZE)
    at, key_at = query_ref[...], key_ref[...]
    allowed = (key_at <= at) & (key_at < length) & (key_at >= 0)
    scores = jnp.where(allowed, mm_nt(q, k) * HEAD_SIZE ** (-0.5), masked_value)
    exponent = jnp.exp(scores - jnp.max(scores, axis=-1, keepdims=True))
    return q, k, v, exponent / jnp.sum(exponent, axis=-1, keepdims=True)


def attention_kernel(core_ref, length_ref, q_ref, mine_ref, other_ref, query_ref, key_ref, out_ref):
    length = length_ref[pl.program_id(0)]
    _, _, v, soft = attention_parts(core_ref[0], length, q_ref, mine_ref, other_ref, query_ref, key_ref)
    out_ref[...] = mm(soft.astype(jnp.bfloat16), v).astype(jnp.bfloat16).reshape(out_ref.shape)


def attention_back_kernel(
    core_ref, length_ref, q_ref, mine_ref, other_ref, query_ref, key_ref, do_ref, cos_ref, sin_ref,
    dq_ref, keep_ref, send_ref,
):
    low = jnp.bfloat16
    core = core_ref[0]
    length = length_ref[pl.program_id(0)]
    q, k, v, soft = attention_parts(core, length, q_ref, mine_ref, other_ref, query_ref, key_ref)
    do = do_ref[...].reshape(-1, HEAD_SIZE)
    dp = mm_nt(do, v)
    delta = jnp.sum(soft * dp, axis=-1, keepdims=True)
    ds = (soft * (dp - delta) * HEAD_SIZE ** (-0.5)).astype(low)
    dq = mm(ds, k)
    cos_table, sin_table = cos_ref[...], sin_ref[...]
    half = HEAD_SIZE // 2
    a, b = dq[:, :half], dq[:, half:]
    turned = jnp.concatenate([a * cos_table + b * sin_table, b * cos_table - a * sin_table], axis=-1)
    dq_ref[...] = turned.astype(low).reshape(dq_ref.shape)
    dk, dv = mm_tn(ds, q), mm_tn(soft.astype(low), do)
    first = core == 0
    keep, send = (t.reshape(keep_ref.shape) for t in (jnp.where(first, dk, dv), jnp.where(first, dv, dk)))
    for block in range(keep_ref.shape[0]):
        at = core_ref[1 + block]
        keep_ref[at] = keep[block]
        send_ref[at] = send[block].astype(low)


def attention_call(kernel, core, lengths, q, mine, other, query_pos, key_pos, extra, outs, name):
    ny, count, span, size = q.shape
    nz = mine.shape[0]
    rows = pl.BlockSpec((ny, 1, span, size), lambda i, *_: (0, i, 0, 0))
    keys = pl.BlockSpec((nz, ny, 1, span, size), lambda i, *_: (0, 0, i, 0, 0))

    def whole(value):
        return pl.BlockSpec(value.shape, lambda i, *_: (0,) * value.ndim)

    kinds = {"rows": (rows, q.shape), "keys": (keys, mine.shape)}
    return pl.pallas_call(
        kernel,
        grid_spec=pltpu.PrefetchScalarGridSpec(
            num_scalar_prefetch=2,
            grid=(count,),
            in_specs=[rows, keys, keys, whole(query_pos), whole(key_pos)]
            + [rows if value.shape == q.shape else whole(value) for value in extra],
            out_specs=[kinds[kind][0] for kind, _ in outs],
        ),
        out_shape=[jax.ShapeDtypeStruct(kinds[kind][1], dtype) for kind, dtype in outs],
        compiler_params=pltpu.CompilerParams(vmem_limit_bytes=48 * 2**20),
        cost_estimate=pl.CostEstimate(flops=1, bytes_accessed=1, transcendentals=0),
        name=name,
    )(core, lengths, q, mine, other, query_pos, key_pos, *extra)


def feed_back_kernel(dyb_ref, weight_ref, gate_ref, up_ref, out_ref):
    dm = mm(dyb_ref[...], weight_ref[...])
    gate, upward = gate_ref[...], up_ref[...]
    sig = jax.nn.sigmoid(gate)
    part = gate.shape[1]
    out_ref[:, :part] = (dm * upward * sig * (1.0 + gate * (1.0 - sig))).astype(out_ref.dtype)
    out_ref[:, part:] = (dm * gate * sig).astype(out_ref.dtype)


def feed_back(dyb, weight, both, lines=256):
    count, part = both.shape[0], both.shape[1] // 2

    def rows(width, column=0):
        return pl.BlockSpec((lines, width), lambda i: (i, column))

    return pl.pallas_call(
        feed_back_kernel,
        grid=(count // lines,),
        in_specs=[rows(dyb.shape[1]), pl.BlockSpec(weight.shape, lambda i: (0, 0)), rows(part), rows(part, 1)],
        out_specs=rows(2 * part),
        out_shape=jax.ShapeDtypeStruct((count, 2 * part), jnp.bfloat16),
        compiler_params=pltpu.CompilerParams(vmem_limit_bytes=48 * 2**20),
        cost_estimate=pl.CostEstimate(flops=1, bytes_accessed=1, transcendentals=0),
        name="feed_back",
    )(dyb, weight, both, both)


def close_reciprocal(value):
    guess = pltpu.reciprocal(value, approx=True)
    return guess * (2.0 - value * guess)


def norm_of(lines_ref, tile_ref):
    gains = lines_ref[:-8]
    return jnp.sqrt(jnp.sum(gains * gains, keepdims=True) + lines_ref[-8:-7, 0:1] + tile_ref[0:1, 0:1])


def update_kernel(*refs):
    lines_ref, tile_ref, gain_ref, gate_up_ref, down_ref, attention_ref = refs[:6]
    gains, feed, attention = refs[6:9], refs[9:12], refs[12:15]
    new_gains, norm_ref, new_feed, new_attention, factor_ref = refs[15:18], refs[18], refs[19:23], refs[23:27], refs[27]
    rows = feed[0].shape[0]
    lines = pl.ds(pl.multiple_of(pl.program_id(0) * rows, rows), rows)

    @pl.when(pl.program_id(0) == 0)
    def _():
        norm = norm_of(lines_ref, tile_ref)
        norm_ref[...] = norm
        factor_ref[...] = clip_norm / norm
        weight, mean, square = (ref[...] for ref in gains)
        gradient = gain_ref[...] * factor_ref[...]
        for ref, value in zip(new_gains, adamw(weight, gradient, mean, square, gain_rate, 0.0)):
            ref[...] = value

    factor = factor_ref[...]

    def piece(olds, news, grad_ref, member, start, column, size):
        at = pl.ds(pl.multiple_of(column, size), size)
        gradient = grad_ref[member, lines, pl.ds(start, size)].astype(jnp.float32) * factor
        weight, mean, square = (ref[:, at] for ref in olds)
        values = adamw(weight, gradient, mean, square, matrix_rate, weight_decay, close_reciprocal)
        for ref, value in zip(news, (*values, values[0])):
            ref[:, at] = value.astype(ref.dtype)

    part = down_ref.shape[2]
    size = min(part, 512)

    @pl.loop(0, 8)
    def _(member):
        for offset in range(0, part, size):
            for number, (grad_ref, start) in enumerate(((gate_up_ref, 0), (gate_up_ref, part), (down_ref, 0))):
                column = (number * 8 + member) * part + offset
                piece(feed, new_feed, grad_ref, member, start + offset, column, size)
        core = lax.rem(member, 2)
        kv_column = (8 + 4 * core + lax.div(member, 2)) * HEAD_SIZE
        for number, column in enumerate((member * HEAD_SIZE, kv_column, (16 + member) * HEAD_SIZE)):
            piece(attention, new_attention, attention_ref, member, number * HEAD_SIZE, column, HEAD_SIZE)


def update(sums, grads, gains, feed, attention):
    f32, low = jnp.float32, jnp.bfloat16
    rows = min(feed[0].shape[0], 16)

    def some(value):
        return pl.BlockSpec((rows, value.shape[1]), lambda i: (i, 0))

    def whole(value):
        return pl.BlockSpec(value.shape, lambda i: (0,) * value.ndim)

    norm = jax.ShapeDtypeStruct((1, 1), f32)
    matrices = [jax.ShapeDtypeStruct(part[0].shape, dtype) for part in (feed, attention) for dtype in (f32, f32, f32, low)]
    return pl.pallas_call(
        update_kernel,
        grid=(feed[0].shape[0] // rows,),
        in_specs=[whole(value) for value in (*sums, *grads, *gains)] + [some(value) for value in (*feed, *attention)],
        out_specs=[whole(value) for value in (*gains, norm)] + [some(value) for value in matrices],
        out_shape=[jax.ShapeDtypeStruct(gains[0].shape, f32)] * 3 + [norm] + matrices,
        scratch_shapes=[pltpu.VMEM((1, 1), f32)],
        compiler_params=pltpu.CompilerParams(vmem_limit_bytes=56 * 2**20),
        name="update",
    )(*sums, *grads, *gains, *feed, *attention)


def is_square():
    return lax.axis_size("y") == 2 and lax.axis_size("x") == 2


def swap(blocks):
    return lax.all_to_all(blocks, TEAM, split_axis=0, concat_axis=0, tiled=True)


def over_planes(blocks):
    return lax.all_gather(blocks.reshape(-1, blocks.shape[-1]), "z", axis=0, tiled=True)


def scatter_planes(term):
    return lax.psum_scatter(term, "z", scatter_dimension=0, tiled=True)


def together(*values):
    return lax.optimization_barrier(values)


def scatter_team(rows, number, after=()):
    if not is_square():
        return swap(rows.reshape(8, -1, rows.shape[-1]))
    return turn(rows, number, after)[0]


def team_gather(local, number, after=()):
    if not is_square():
        return lax.all_gather(local, TEAM, axis=0, tiled=True)
    return plane_gather(local, number, after).reshape(-1, local.shape[1])


def team_sum(lefts, rights, number, after=()):
    if is_square():
        return plane_sum(lefts, rights, number, after)
    partial = mm_nt(jnp.concatenate(lefts, axis=1), jnp.concatenate(rights, axis=1))
    return lax.psum_scatter(partial.astype(jnp.bfloat16), TEAM, scatter_dimension=0, tiled=True).astype(jnp.float32)


def local(
    tokens,
    lengths,
    norm_gains,
    attention_weight,
    feed_weight,
    cotangent,
    attention_mean,
    attention_square,
    feed_mean,
    feed_square,
    gain_mean,
    gain_square,
):
    low = jnp.bfloat16
    sequences, span, width = tokens.shape
    ny, nx, nz = lax.axis_size("y"), lax.axis_size("x"), lax.axis_size("z")
    team = ny * nx * 2
    core = lax.axis_index("c")
    rows = attention_weight.shape[0]
    q_width, kv_width = QUERY_HEADS * HEAD_SIZE, KEY_VALUE_HEADS * HEAD_SIZE
    count = sequences * span
    all_sequences = nx * 2 * sequences
    reach = ny * span
    near = is_square()
    ff_part = FF // team

    def columns(start, size):
        return pl.ds(pl.multiple_of(start, size), size)

    def take_attention(sources, member, c):
        source = sources[0]
        starts = (
            member * HEAD_SIZE,
            q_width + c * kv_width + (member - c) // 2 * HEAD_SIZE,
            q_width + 2 * kv_width + member * HEAD_SIZE,
        )
        return jnp.concatenate([source[:, columns(s, HEAD_SIZE)].astype(low) for s in starts], axis=1)

    def take_feed(*parts):
        return lambda sources, member, c: jnp.concatenate(
            [sources[0][:, columns(part * FF + member * ff_part, ff_part)].astype(low) for part in parts], axis=1
        )

    def spread(source, take, size, number, after=()):
        if is_square():
            blocks = plane_swap([source], [(rows, size)], [take], number, after)[0]
        else:
            blocks = swap(jnp.stack([take([source], member, member % 2) for member in range(8)]))
        return blocks, over_planes(blocks)

    team_base = lax.axis_index("z") * reach
    team_pos = team_base + jnp.arange(reach, dtype=jnp.int32)
    own_pos = team_base + lax.axis_index("y") * span + jnp.arange(span, dtype=jnp.int32)
    if near:
        key_pos = jnp.concatenate([team_pos - back * reach for back in range(nz)])
    else:
        key_pos = jnp.arange(nz * reach, dtype=jnp.int32)
    query_at, key_at = team_pos[:, None], key_pos[None, :]
    cos_table, sin_table = angle_tables(team_pos)
    cos_rows, sin_rows = (t.reshape(ny, 1, span, -1) for t in (cos_table, sin_table))
    valid = (own_pos[None, :] < lengths[:, None]).astype(jnp.float32).reshape(count, 1)
    lengths_all = lax.all_gather(lengths, ("x", "c"), axis=0, tiled=True)
    planes = jnp.arange(nz, dtype=jnp.int32)
    if near:
        planes = (lax.axis_index("z") - planes) % nz
    core_at = jnp.concatenate([jnp.reshape(core, (1,)), planes]).astype(jnp.int32)

    def heads(value):
        return value.reshape(ny, all_sequences, span, HEAD_SIZE)

    x_in = tokens.reshape(count, width).astype(jnp.float32)
    normed_one, inverse_one = rms_forward(x_in, norm_gains[0])
    outer_grad = cotangent.reshape(count, width).astype(jnp.float32) * valid
    if is_square():
        attention_mine, h1 = begin(
            attention_weight,
            tokens.reshape(count, width),
            norm_gains[:1],
            take_attention,
            3 * HEAD_SIZE,
            nz,
            1,
        )
        h1 = h1.reshape(-1, width)
    else:
        attention_mine = spread(attention_weight, take_attention, 3 * HEAD_SIZE, 1)[1]
        gate_up_blocks, gate_up_weight = spread(feed_weight, take_feed(0, 1), 2 * ff_part, 2)
        h1 = team_gather(normed_one.astype(low), 3)
    query_weight = attention_mine[:, :HEAD_SIZE]
    kv_weight = attention_mine[:, HEAD_SIZE : 2 * HEAD_SIZE]
    out_weight = attention_mine[:, 2 * HEAD_SIZE :]
    kv_raw = heads(mm(h1, kv_weight))
    kv = jnp.where(core == 0, rotate(kv_raw, cos_rows, sin_rows), kv_raw).astype(low)
    q = rotate(heads(mm(h1, query_weight)), cos_rows, sin_rows).astype(low)
    if is_square():
        kv, other, gate_up_blocks = climb(
            kv.reshape(-1, HEAD_SIZE), feed_weight, take_feed(0, 1), 2 * ff_part, nz, 2
        )
        kv, other = (t.reshape(nz, ny, all_sequences, span, HEAD_SIZE) for t in (kv, other))
        gate_up_weight = over_planes(gate_up_blocks)
    else:
        kv = lax.all_gather(kv, "z", axis=0, tiled=False)
        other = lax.ppermute(kv, "c", [(0, 1), (1, 0)])
    attend = (core_at, lengths_all, q, kv, other, query_at, key_at)
    (o,) = attention_call(attention_kernel, *attend, (), [("rows", low)], "attention")
    o = o.reshape(-1, HEAD_SIZE)
    r = x_in + team_sum([o], [out_weight], 4)

    normed_two, inverse_two = rms_forward(r, norm_gains[1])
    h2 = team_gather(normed_two.astype(low), 16)
    dyb = team_gather(outer_grad.astype(low), 15, [h2])
    down_blocks, down_weight = spread(feed_weight, take_feed(2), ff_part, 12, [dyb])
    gate_up_weight, down_blocks = together(gate_up_weight, down_blocks)
    both = mm(h2, gate_up_weight)
    gate, upward = both[:, :ff_part], both[:, ff_part:]
    sig = jax.nn.sigmoid(gate)
    m = (gate * sig * upward).astype(low)
    down_term = mm_tn(dyb, m).astype(low)
    down_rows = scatter_planes(down_term)
    down_weight, down_term = together(down_weight, down_term)
    d_both = feed_back(dyb, down_weight, both)
    gate_up_term = mm_tn(h2, d_both).astype(low)
    gate_up_rows = scatter_planes(gate_up_term)
    dh2 = team_sum([d_both], [gate_up_weight], 7, [gate_up_term, down_term])
    mid_grad, gain_two = rms_back(dh2, r, inverse_two, norm_gains[1])
    dr = outer_grad + mid_grad
    drb = team_gather(dr.astype(low), 13, [down_rows])

    do = heads(mm(drb, out_weight).astype(low))
    dq, keep, theirs = attention_call(
        attention_back_kernel,
        *attend,
        (do, cos_table, sin_table),
        [("rows", low), ("keys", jnp.float32), ("keys", low)],
        "attention_back",
    )
    dq = dq.reshape(-1, HEAD_SIZE)
    dkv = keep + lax.ppermute(theirs, "c", [(0, 1), (1, 0)]).astype(jnp.float32)
    low_terms = dkv.astype(low)
    feed_sum = team_sum([m], [down_weight], 5, [low_terms])
    down_grad = scatter_team(down_rows, 6, [low_terms])
    layer_output = (r + feed_sum).astype(low)
    local_squares = sum(jnp.sum(jnp.square(part.astype(jnp.float32))) for part in (gate_up_rows, down_rows))
    if is_square():
        dkv, gate_up_grad = fall(low_terms.reshape(nz, -1, HEAD_SIZE), gate_up_rows, nz, 8, [layer_output, down_grad])
        dkv = dkv.reshape(ny, all_sequences, span, HEAD_SIZE)
    else:
        dkv = lax.psum_scatter(low_terms, "z", scatter_dimension=0, tiled=True)[0].astype(jnp.float32)
        gate_up_grad = scatter_team(gate_up_rows, 8)
    dkv = jnp.where(core == 0, rotate(dkv, cos_rows, -sin_rows), dkv).astype(low).reshape(-1, HEAD_SIZE)
    attention_term = jnp.concatenate([mm_tn(h1, dq), mm_tn(h1, dkv), mm_tn(drb, o)], axis=1).astype(low)
    attention_rows = scatter_planes(attention_term)
    dh1 = team_sum([dq, dkv], [query_weight, kv_weight], 9, [attention_term])
    in_grad, gain_one = rms_back(dh1, x_in, inverse_one, norm_gains[0])
    input_gradient = dr + in_grad
    gain_local = jnp.stack([gain_one, gain_two]).reshape(-1, 128)
    lines = jnp.concatenate([gain_local, jnp.full((8, 128), local_squares)], axis=0)
    if is_square():
        lines = total_sum(lines, nz, 18)
        attention_grad, tile = turn(attention_rows, 10, (), nz)
    else:
        lines = lax.psum(lines, ALL)
        attention_grad = scatter_team(attention_rows, 10)
        tile = lax.psum(jnp.full((8, 128), jnp.sum(jnp.square(attention_rows.astype(jnp.float32)))), ALL)
    gain_grad = lines[:-8].reshape(2, width)
    news = update(
        (lines, tile, gain_grad),
        (gate_up_grad, down_grad, attention_grad),
        (norm_gains, gain_mean, gain_square),
        (feed_weight, feed_mean, feed_square),
        (attention_weight, attention_mean, attention_square),
    )
    gains_new, gradient_norm, feed_new, attention_new = news[:3], news[3], news[4:8], news[8:]
    return (
        layer_output.reshape(sequences, span, width),
        input_gradient.reshape(sequences, span, width),
        gradient_norm.reshape(()),
        *attention_new,
        *feed_new,
        *gains_new,
    )


def solution(mesh):
    ctx, fsdp = mesh.shape["ctx"], mesh.shape["fsdp"]
    inner = QUERY_HEADS // fsdp
    fine = Mesh(mesh.devices.reshape(ctx // inner, inner, fsdp // 2, 2), ALL)
    act = P(("x", "c"), ("z", "y"), None)
    matrix = P(ALL, None)
    return jax.shard_map(
        local,
        mesh=fine,
        in_specs=(act, P(("x", "c")), P(), matrix, matrix, act, matrix, matrix, matrix, matrix, P(), P()),
        out_specs=(act, act, P(), matrix, matrix, matrix, matrix, matrix, matrix, matrix, matrix, P(), P(), P()),
        check_vma=False,
    )
```

```python
import functools

import jax
import jax.numpy as jnp
from jax import lax
from jax.experimental import pallas as pl
from jax.experimental.pallas import tpu as pltpu
from jax.sharding import Mesh, PartitionSpec as P

QUERY_HEADS = 8
KEY_VALUE_HEADS = 4
HEAD_SIZE = 256
FF = 8192
STEP = 10

norm_eps = 1e-06
rope_base = 1000042.0
masked_value = -1e30
clip_norm = 1.0
beta_one = 0.9
beta_two = 0.95
adam_eps = 1e-08
matrix_rate = 0.03
gain_rate = 0.4
weight_decay = 0.1

TEAM = ("y", "x", "c")
ALL = ("z", "y", "x", "c")


MESH = pl.DeviceIdType.MESH
VMEM = pl.BlockSpec(memory_space=pltpu.VMEM)
HBM = pl.BlockSpec(memory_space=pl.ANY)


def place():
    y, x, c = lax.axis_index("y"), lax.axis_index("x"), lax.axis_index("c")
    return y, x, c, lambda yy, xx, cc: (yy * 2 + xx) * 2 + cc


def greet(others):
    barrier = pltpu.get_barrier_semaphore()
    for other in others:
        pl.semaphore_signal(barrier, inc=1, device_id=other, device_id_type=MESH)
    pl.semaphore_wait(barrier, len(others))


def gather_kernel(src, *refs):
    out, send, recv, own = refs[-4:]
    y, x, c, index = place()
    to_x, to_y, to_s = {"x": 1 - x}, {"y": 1 - y}, {"c": 1 - c}
    me, at_x, at_y, at_d = index(y, x, c), index(y, 1 - x, c), index(1 - y, x, c), index(1 - y, 1 - x, c)
    half = src.shape[0] // 2
    rows = (pl.ds(0, half), pl.ds(half, half))
    local = pltpu.make_async_copy(src, out.at[me], own)
    local.start()
    greet((to_x, to_y, to_s))

    def hop(slot, block, part, where, first=False):
        piece = out.at[block, rows[part]]
        return pltpu.make_async_remote_copy(
            src_ref=src.at[rows[part]] if first else piece,
            dst_ref=piece,
            send_sem=send.at[slot],
            recv_sem=recv.at[slot],
            device_id=where,
            device_id_type=MESH,
        )

    x0, x1 = hop(0, me, 0, to_x, True), hop(1, me, 1, to_x, True)
    y1, y0 = hop(2, me, 1, to_y, True), hop(3, me, 0, to_y, True)
    s0, s1 = hop(4, me, 0, to_s, True), hop(5, me, 1, to_s, True)
    for copy in (x0, y1, x1, y0, s0, s1):
        copy.start()
    x0.wait_recv()
    d0 = hop(6, at_x, 0, to_y)
    d0.start()
    y1.wait_recv()
    d1 = hop(7, at_y, 1, to_x)
    d1.start()
    sx0, sy1 = hop(8, at_x, 0, to_s), hop(9, at_y, 1, to_s)
    sx0.start()
    sy1.start()
    x1.wait_recv()
    sx1 = hop(10, at_x, 1, to_s)
    sx1.start()
    y0.wait_recv()
    sy0 = hop(11, at_y, 0, to_s)
    sy0.start()
    d0.wait_recv()
    sd0 = hop(12, at_d, 0, to_s)
    sd0.start()
    d1.wait_recv()
    sd1 = hop(13, at_d, 1, to_s)
    sd1.start()
    for copy in (s0, s1, sx0, sy1, sx1, sy0, sd0, sd1):
        copy.wait_recv()
    for copy in (x0, x1, y0, y1, s0, s1, d0, d1, sx0, sy1, sx1, sy0, sd0, sd1):
        copy.wait_send()
    local.wait()


def plane_gather(value, number, after=()):
    return pl.pallas_call(
        gather_kernel,
        out_shape=jax.ShapeDtypeStruct((8, *value.shape), value.dtype),
        in_specs=[HBM] * (1 + len(after)),
        out_specs=HBM,
        scratch_shapes=[
            pltpu.SemaphoreType.DMA((14,)),
            pltpu.SemaphoreType.DMA((14,)),
            pltpu.SemaphoreType.DMA,
        ],
        compiler_params=pltpu.CompilerParams(collective_id=number, has_side_effects=True),
        cost_estimate=pl.CostEstimate(flops=1, bytes_accessed=1, transcendentals=0),
        name="plane_gather",
    )(value, *after)


def sum_kernel(lefts, terms, tile, *refs):
    a_refs, w_refs = refs[:lefts], refs[lefts : lefts + len(terms)]
    out, s_send, s_recv, d_send, d_recv, x_send, x_recv, y_send, y_recv, x_acc, y_acc, send, recv = refs[-13:]
    y, x, c, index = place()
    to_x, to_y, to_s = {"x": 1 - x}, {"y": 1 - y}, {"c": 1 - c}
    rows, width = out.shape
    half = rows // 2
    parts = (pl.ds(0, half), pl.ds(half, half))
    f32, low = jnp.float32, jnp.bfloat16

    def product(block, put):
        lines = pl.ds(pl.multiple_of(block * rows, rows), rows)

        @pl.loop(0, width // tile)
        def _(step):
            cols = pl.ds(pl.multiple_of(step * tile, tile), tile)
            total = None
            for (left, start), w_ref in zip(terms, w_refs):
                term = mm_nt(a_refs[left][lines, start : start + w_ref.shape[1]], w_ref[cols, :])
                total = term if total is None else total + term
            put(cols, total)

    def hop(slot, src, dst, where):
        copy = pltpu.make_async_remote_copy(
            src_ref=src, dst_ref=dst, send_sem=send.at[slot], recv_sem=recv.at[slot],
            device_id=where, device_id_type=MESH,
        )
        return copy

    def to_sibling(slot, yy, xx):
        def put(cols, total):
            s_send[slot, :, cols] = total.astype(low)

        product(index(yy, xx, 1 - c), put)
        copy = hop(slot, s_send.at[slot], s_recv.at[slot], to_s)
        copy.start()
        return copy

    def with_sibling(slot, yy, xx, keep):
        def put(cols, total):
            keep[:, cols] = (total + s_recv[slot, :, cols].astype(f32)).astype(keep.dtype)

        product(index(yy, xx, c), put)

    greet((to_x, to_y, to_s))
    s0 = to_sibling(0, 1 - y, 1 - x)
    s1 = to_sibling(1, y, 1 - x)
    s0.wait_recv()
    with_sibling(0, 1 - y, 1 - x, d_send)
    d0 = hop(4, d_send.at[parts[0]], d_recv.at[parts[0]], to_x)
    d1 = hop(5, d_send.at[parts[1]], d_recv.at[parts[1]], to_y)
    d0.start()
    d1.start()
    s1.wait_recv()
    with_sibling(1, y, 1 - x, x_acc)
    x_send[parts[0]] = x_acc[parts[0]].astype(low)
    x0 = hop(6, x_send.at[parts[0]], x_recv.at[parts[0]], to_x)
    x0.start()
    s2 = to_sibling(2, 1 - y, x)
    s2.wait_recv()
    with_sibling(2, 1 - y, x, y_acc)
    y_send[parts[1]] = y_acc[parts[1]].astype(low)
    y1 = hop(7, y_send.at[parts[1]], y_recv.at[parts[1]], to_y)
    y1.start()
    s3 = to_sibling(3, y, x)
    d1.wait_recv()
    x_send[parts[1]] = (x_acc[parts[1]] + d_recv[parts[1]].astype(f32)).astype(low)
    x1 = hop(8, x_send.at[parts[1]], x_recv.at[parts[1]], to_x)
    x1.start()
    d0.wait_recv()
    y_send[parts[0]] = (y_acc[parts[0]] + d_recv[parts[0]].astype(f32)).astype(low)
    y0 = hop(9, y_send.at[parts[0]], y_recv.at[parts[0]], to_y)
    y0.start()
    s3.wait_recv()
    with_sibling(3, y, x, out)
    x0.wait_recv()
    y1.wait_recv()
    x1.wait_recv()
    y0.wait_recv()
    out[...] += x_recv[...].astype(f32) + y_recv[...].astype(f32)
    for copy in (s0, s1, s2, s3, d0, d1, x0, x1, y0, y1):
        copy.wait_send()


def plane_sum(lefts, rights, number, after=(), tile=512):
    ends = [(left, start) for left, a in enumerate(lefts) for start in range(0, a.shape[1], rights[0].shape[1])]
    terms = tuple(ends[: len(rights)])
    rows, width = lefts[0].shape[0] // 8, rights[0].shape[0]
    block = (rows, width)
    low, f32 = jnp.bfloat16, jnp.float32
    return pl.pallas_call(
        functools.partial(sum_kernel, len(lefts), terms, min(tile, width)),
        out_shape=jax.ShapeDtypeStruct(block, f32),
        in_specs=[VMEM] * (len(lefts) + len(rights)) + [HBM] * len(after),
        out_specs=VMEM,
        scratch_shapes=[
            pltpu.VMEM((4, *block), low),
            pltpu.VMEM((4, *block), low),
            *[pltpu.VMEM(block, low)] * 6,
            pltpu.VMEM(block, f32),
            pltpu.VMEM(block, f32),
            pltpu.SemaphoreType.DMA((10,)),
            pltpu.SemaphoreType.DMA((10,)),
        ],
        compiler_params=pltpu.CompilerParams(
            collective_id=number, has_side_effects=True, vmem_limit_bytes=48 * 2**20
        ),
        cost_estimate=pl.CostEstimate(flops=1, bytes_accessed=1, transcendentals=0),
        name="plane_sum",
    )(*lefts, *rights, *after)


def swap_kernel(pieces, takes, *refs):
    count = len(pieces)
    sources, (send, recv, own) = refs[: -2 * count - 3], refs[-3:]
    outs, holds = refs[-2 * count - 3 : -count - 3], refs[-count - 3 : -3]
    y, x, c, index = place()
    me = index(y, x, c)
    flips = [(fy, fx, fc) for fy, fx in ((1, 1), (0, 1), (1, 0), (0, 0)) for fc in (0, 1)]
    flips = [flip for flip in flips if flip != (0, 0, 0)]

    def there(flip):
        return tuple(1 - at if f else at for at, f in zip((y, x, c), flip))

    greet([dict(zip(("y", "x", "c"), there(flip))) for flip in flips])
    copies = []
    for piece in range(count):
        for number, flip in enumerate(flips):
            yy, xx, cc = there(flip)
            member = index(yy, xx, cc)
            holds[piece][number] = takes[piece](sources, member, cc)
            copy = pltpu.make_async_remote_copy(
                src_ref=holds[piece].at[number],
                dst_ref=outs[piece].at[me],
                send_sem=send.at[piece * 7 + number],
                recv_sem=recv.at[piece * 7 + number],
                device_id={"y": yy, "x": xx, "c": cc},
                device_id_type=MESH,
            )
            copy.start()
            copies.append(copy)
        holds[piece][7] = takes[piece](sources, me, c)
        keep = pltpu.make_async_copy(holds[piece].at[7], outs[piece].at[me], own.at[piece])
        keep.start()
        copies.append(keep)
    for copy in copies:
        copy.wait()


def plane_swap(sources, shapes, takes, number, after=()):
    low = jnp.bfloat16
    count = len(shapes)
    return pl.pallas_call(
        functools.partial(swap_kernel, shapes, takes),
        out_shape=[jax.ShapeDtypeStruct((8, *shape), low) for shape in shapes],
        in_specs=[VMEM] * len(sources) + [HBM] * len(after),
        out_specs=[HBM] * count,
        scratch_shapes=[
            *[pltpu.VMEM((8, *shape), low) for shape in shapes],
            pltpu.SemaphoreType.DMA((7 * count,)),
            pltpu.SemaphoreType.DMA((7 * count,)),
            pltpu.SemaphoreType.DMA((count,)),
        ],
        compiler_params=pltpu.CompilerParams(
            collective_id=number, has_side_effects=True, vmem_limit_bytes=48 * 2**20
        ),
        cost_estimate=pl.CostEstimate(flops=1, bytes_accessed=1, transcendentals=0),
        name="plane_swap",
    )(*sources, *after)


def team_of(y, x, c):
    flips = [(fy, fx, fc) for fy, fx in ((1, 1), (0, 1), (1, 0), (0, 0)) for fc in (0, 1)]
    return [
        tuple(1 - at if f else at for at, f in zip((y, x, c), flip)) for flip in flips if flip != (0, 0, 0)
    ]


def turn_kernel(planes, src, *refs):
    y, x, c, index = place()
    me = index(y, x, c)
    others = team_of(y, x, c)
    ids = [dict(zip(("y", "x", "c"), other)) for other in others]
    if planes:
        out, total, near, far, held, send, recv, own, send_lines, recv_lines = refs[-10:]
        z = lax.axis_index("z")
        column = [{"z": lax.rem(z + step, planes)} for step in range(1, planes)]
        fetch = pltpu.make_async_copy(src, held, own)
        fetch.start()
        fetch.wait()
        squares = jnp.zeros((8, held.shape[1]), jnp.float32)
        for start in range(0, held.shape[0], 64):
            part = held[start : start + 64].astype(jnp.float32)
            squares += jnp.sum(jnp.square(part).reshape(8, 8, -1), axis=0)
        near[me] = jnp.broadcast_to(jnp.sum(squares, keepdims=True), near.shape[1:])
    else:
        out, send, recv, own = refs[-4:]
        column = []
    greet(ids + column)
    count = src.shape[0] // 8

    def rows(member):
        return src.at[pl.ds(pl.multiple_of(member * count, count), count)]

    def spread(buffer, at, where, base):
        copies = [
            pltpu.make_async_remote_copy(
                src_ref=buffer.at[at],
                dst_ref=buffer.at[at],
                send_sem=send_lines.at[base + number],
                recv_sem=recv_lines.at[base + number],
                device_id=other,
                device_id_type=MESH,
            )
            for number, other in enumerate(where)
        ]
        for copy in copies:
            copy.start()
        return copies

    small = spread(near, me, ids, 0) if planes else []
    copies = [
        pltpu.make_async_remote_copy(
            src_ref=rows(index(*other)),
            dst_ref=out.at[me],
            send_sem=send.at[number],
            recv_sem=recv.at[number],
            device_id=where,
            device_id_type=MESH,
        )
        for number, (other, where) in enumerate(zip(others, ids))
    ]
    copies.append(pltpu.make_async_copy(rows(me), out.at[me], own))
    for copy in copies:
        copy.start()
    if planes:
        for copy in small:
            copy.wait()
        far[z] = jnp.sum(near[...], axis=0)
        for copy in spread(far, z, column, 7):
            copy.wait()
        total[...] = jnp.sum(far[...], axis=0)
    for copy in copies:
        copy.wait()


def total_kernel(planes, src, *refs):
    out, near, far, send, recv = refs[-5:]
    y, x, c, index = place()
    z = lax.axis_index("z")
    ids = [dict(zip(("y", "x", "c"), other)) for other in team_of(y, x, c)]
    column = [{"z": lax.rem(z + step, planes)} for step in range(1, planes)]
    me = index(y, x, c)
    near[me] = src[...]
    greet(ids + column)

    def spread(buffer, at, where, base):
        copies = [
            pltpu.make_async_remote_copy(
                src_ref=buffer.at[at],
                dst_ref=buffer.at[at],
                send_sem=send.at[base + number],
                recv_sem=recv.at[base + number],
                device_id=other,
                device_id_type=MESH,
            )
            for number, other in enumerate(where)
        ]
        for copy in copies:
            copy.start()
        for copy in copies:
            copy.wait()

    spread(near, me, ids, 0)
    far[z] = jnp.sum(near[...], axis=0)
    spread(far, z, column, 7)
    out[...] = jnp.sum(far[...], axis=0)


def total_sum(value, planes, number, after=()):
    return pl.pallas_call(
        functools.partial(total_kernel, planes),
        out_shape=jax.ShapeDtypeStruct(value.shape, value.dtype),
        in_specs=[VMEM] + [HBM] * len(after),
        out_specs=VMEM,
        scratch_shapes=[pltpu.VMEM((size, *value.shape), value.dtype) for size in (8, planes)]
        + [pltpu.SemaphoreType.DMA((6 + planes,))] * 2,
        compiler_params=pltpu.CompilerParams(
            collective_id=number, has_side_effects=True, vmem_limit_bytes=16 * 2**20
        ),
        cost_estimate=pl.CostEstimate(flops=1, bytes_accessed=1, transcendentals=0),
        name="total_sum",
    )(value, *after)


def turn(rows, number, after=(), planes=0):
    block = (rows.shape[0] // 8, rows.shape[1])
    dma = pltpu.SemaphoreType.DMA
    out_shape, out_specs = [jax.ShapeDtypeStruct((8, *block), rows.dtype)], [HBM]
    scratch = [dma((7,)), dma((7,)), dma]
    if planes:
        tile = jax.ShapeDtypeStruct((8, 128), jnp.float32)
        out_shape.append(tile)
        out_specs.append(VMEM)
        buffers = [pltpu.VMEM((size, *tile.shape), tile.dtype) for size in (8, planes)]
        scratch = buffers + [pltpu.VMEM(rows.shape, rows.dtype)] + scratch + [dma((6 + planes,)), dma((6 + planes,))]
    return pl.pallas_call(
        functools.partial(turn_kernel, planes),
        out_shape=out_shape,
        in_specs=[HBM] * (1 + len(after)),
        out_specs=out_specs,
        scratch_shapes=scratch,
        compiler_params=pltpu.CompilerParams(
            collective_id=number, has_side_effects=True, vmem_limit_bytes=56 * 2**20
        ),
        cost_estimate=pl.CostEstimate(flops=1, bytes_accessed=1, transcendentals=0),
        name="turn",
    )(rows, *after)


def hops(planes, send, recv, block, up):
    z = lax.axis_index("z")

    def step(number):
        gone, came = (z - number + 1, z - number) if up else (z + number - 1, z + number)
        goes = ((gone >= 0) & (z + 1 < planes)) if up else ((gone < planes) & (z >= 1))
        comes = (came >= 0) if up else (came < planes)

        def copy(b):
            return pltpu.make_async_remote_copy(
                src_ref=block(b),
                dst_ref=block(b),
                send_sem=send.at[number - 1],
                recv_sem=recv.at[number - 1],
                device_id={"z": z + 1 if up else z - 1},
                device_id_type=MESH,
            )

        return (
            lambda: pl.when(goes)(lambda: copy(gone).start()),
            lambda: pl.when(comes)(lambda: copy(came).wait_recv()),
            lambda: pl.when(goes)(lambda: copy(gone).wait_send()),
        )

    return [step(number) for number in range(1, planes)]


def ring(planes):
    z = lax.axis_index("z")
    return [{"z": lax.rem(z + 1, planes)}, {"z": lax.rem(z + planes - 1, planes)}]


def spread_to(others, ids, source, take, hold, place_of, send, recv, own):
    y, x, c, index = place()
    me = index(y, x, c)
    copies = []
    for number, (other, where) in enumerate(zip(others, ids)):
        hold[number] = take([source], index(*other), other[2])
        copy = pltpu.make_async_remote_copy(
            src_ref=hold.at[number], dst_ref=place_of(me), send_sem=send.at[number], recv_sem=recv.at[number],
            device_id=where, device_id_type=MESH,
        )
        copy.start()
        copies.append(copy)
    hold[7] = take([source], me, c)
    keep = pltpu.make_async_copy(hold.at[7], place_of(me), own)
    keep.start()
    return copies, keep


def begin_kernel(
    planes, take, take_feed, attention, feed, tokens, gain, all_attention, all_rows, columns,
    held, hold, feed_held, feed_hold, rows, a_send, a_recv, f_send, f_recv, r_send, r_recv, u_send, u_recv, d_send, d_recv, own,
):
    y, x, c, index = place()
    z = lax.axis_index("z")
    me, at_x, at_y, at_d = index(y, x, c), index(y, 1 - x, c), index(1 - y, x, c), index(1 - y, 1 - x, c)
    others = team_of(y, x, c)
    ids = [dict(zip(("y", "x", "c"), other)) for other in others]
    to_x, to_y, to_s = {"x": 1 - x}, {"y": 1 - y}, {"c": 1 - c}
    count = held.shape[0]
    half = rows.shape[0] // 2
    parts = (pl.ds(0, half), pl.ds(half, half))
    fetch = pltpu.make_async_copy(attention, held, own.at[0])
    fetch.start()
    fetch_feed = pltpu.make_async_copy(feed.at[:, pl.ds(0, feed_held.shape[1])], feed_held, own.at[3])
    fetch_feed.start()
    greet(ids + ring(planes))
    fetch.wait()

    def attention_rows(start, size):
        return all_attention.at[pl.ds(pl.multiple_of(start, count), size)]

    a_copies, a_keep = spread_to(
        others, ids, held, take, hold, lambda m: attention_rows((z * 8 + m) * count, count), a_send, a_recv, own.at[1]
    )

    def hop(slot, block, part, where, first=False):
        piece = all_rows.at[block, parts[part]]
        copy = pltpu.make_async_remote_copy(
            src_ref=rows.at[parts[part]] if first else piece, dst_ref=piece,
            send_sem=r_send.at[slot], recv_sem=r_recv.at[slot], device_id=where, device_id_type=MESH,
        )
        copy.start()
        return copy

    for copy in a_copies:
        copy.wait_recv()
    a_keep.wait()

    def plane_block(b):
        return attention_rows(b * 8 * count, 8 * count)

    up = hops(planes, u_send, u_recv, plane_block, True)
    down = hops(planes, d_send, d_recv, plane_block, False)

    def pass_on(number):
        if number > 0:
            up[number - 1][1]()
            down[number - 1][1]()
        if number < planes - 1:
            up[number][0]()
            down[number][0]()

    pass_on(0)

    @pl.loop(0, rows.shape[0] // 16)
    def _(group):
        lines = pl.ds(pl.multiple_of(group * 16, 16), 16)
        rows[lines] = rms_forward(tokens[lines].astype(jnp.float32), gain[...])[0].astype(rows.dtype)

    x0, y1 = hop(0, me, 0, to_x, True), hop(2, me, 1, to_y, True)
    x1, y0 = hop(1, me, 1, to_x, True), hop(3, me, 0, to_y, True)
    s0, s1 = hop(4, me, 0, to_s, True), hop(5, me, 1, to_s, True)
    mine = pltpu.make_async_copy(rows, all_rows.at[me], own.at[2])
    mine.start()
    x0.wait_recv()
    d0 = hop(6, at_x, 0, to_y)
    y1.wait_recv()
    d1 = hop(7, at_y, 1, to_x)
    sx0, sy1 = hop(8, at_x, 0, to_s), hop(9, at_y, 1, to_s)
    fetch_feed.wait()
    f_copies, f_keep = spread_to(
        others, ids, feed_held, take_feed, feed_hold, lambda m: columns.at[m], f_send, f_recv, own.at[4]
    )
    pass_on(1)
    x1.wait_recv()
    sx1 = hop(10, at_x, 1, to_s)
    y0.wait_recv()
    sy0 = hop(11, at_y, 0, to_s)
    d0.wait_recv()
    sd0 = hop(12, at_d, 0, to_s)
    d1.wait_recv()
    sd1 = hop(13, at_d, 1, to_s)
    for number in range(2, planes):
        pass_on(number)
    for copy in (s0, s1, sx0, sy1, sx1, sy0, sd0, sd1, *f_copies):
        copy.wait_recv()
    for copy in (x0, x1, y0, y1, s0, s1, d0, d1, sx0, sy1, sx1, sy0, sd0, sd1, *a_copies, *f_copies):
        copy.wait_send()
    for step in up + down:
        step[2]()
    mine.wait()
    f_keep.wait()


def begin(attention, feed, tokens, gain, takes, widths, planes, number):
    low, dma = jnp.bfloat16, pltpu.SemaphoreType.DMA
    count = attention.shape[0]
    return pl.pallas_call(
        functools.partial(begin_kernel, planes, *takes),
        out_shape=[
            jax.ShapeDtypeStruct((planes * 8 * count, widths[0]), low),
            jax.ShapeDtypeStruct((8, *tokens.shape), low),
            jax.ShapeDtypeStruct((8, count, widths[1]), low),
        ],
        in_specs=[HBM, HBM, VMEM, VMEM],
        out_specs=[HBM] * 3,
        scratch_shapes=[
            pltpu.VMEM(attention.shape, attention.dtype),
            pltpu.VMEM((8, count, widths[0]), low),
            pltpu.VMEM((count, 8 * widths[1]), feed.dtype),
            pltpu.VMEM((8, count, widths[1]), low),
            pltpu.VMEM(tokens.shape, low),
            *[dma((size,)) for size in (7, 7, 7, 7, 14, 14, *[planes - 1] * 4, 5)],
        ],
        compiler_params=pltpu.CompilerParams(
            collective_id=number, has_side_effects=True, vmem_limit_bytes=32 * 2**20
        ),
        cost_estimate=pl.CostEstimate(flops=1, bytes_accessed=1, transcendentals=0),
        name="begin",
    )(attention, feed, tokens, gain)


def turned(value, cos_table, sin_table):
    half = value.shape[1] // 2
    first, second = value[:, :half], value[:, half:]
    return jnp.concatenate([first * cos_table - second * sin_table, second * cos_table + first * sin_table], axis=1)


def climb_kernel(
    planes, rows, weight, cos, sin, mine, other, zeros, stay, u_send, u_recv, s_send, s_recv, own, fill
):
    z, c = lax.axis_index("z"), lax.axis_index("c")
    to_s = {"c": 1 - c}
    barrier = pltpu.get_barrier_semaphore()
    for where in [to_s] + ring(planes):
        pl.semaphore_signal(barrier, inc=1, device_id=where, device_id_type=MESH)
    count, (sides, span) = rows.shape[0], cos.shape[:2]
    size = 512
    for start in range(0, count, size):
        value = mm(rows[start : start + size], weight[...])
        for line in range(0, size, span):
            side = (start + line) // (count // sides)
            part = value[line : line + span]
            part = jnp.where(c == 0, turned(part, cos[side], sin[side]), part)
            stay[start + line : start + line + span] = part.astype(stay.dtype)
    zeros[...] = jnp.zeros_like(zeros)
    pl.semaphore_wait(barrier, 3)

    def across(n):
        return pltpu.make_async_remote_copy(
            src_ref=stay if n == 0 else mine.at[n], dst_ref=other.at[n], send_sem=s_send.at[n], recv_sem=s_recv.at[n],
            device_id=to_s, device_id_type=MESH,
        )

    def along(n):
        return pltpu.make_async_remote_copy(
            src_ref=stay if n == 1 else mine.at[n - 1], dst_ref=mine.at[n], send_sem=u_send.at[n - 1], recv_sem=u_recv.at[n - 1],
            device_id={"z": z + 1}, device_id_type=MESH,
        )

    def fills(n):
        return [
            pltpu.make_async_copy(zeros, buffer.at[n], fill.at[2 * (n - 1) + number])
            for number, buffer in enumerate((mine, other))
        ]

    keep = pltpu.make_async_copy(stay, mine.at[0], own)
    more = z + 1 < planes
    pl.when(more)(lambda: along(1).start())
    across(0).start()
    keep.start()
    for n in range(1, planes):

        @pl.when(z < n)
        def _():
            for copy in fills(n):
                copy.start()

    for n in range(1, planes):

        @pl.when(z >= n)
        def _():
            along(n).wait_recv()
            if n + 1 < planes:
                pl.when(more)(lambda: along(n + 1).start())
            across(n).start()

    across(0).wait()
    keep.wait()
    for n in range(1, planes):

        @pl.when(z >= n)
        def _():
            across(n).wait()

        @pl.when(z < n)
        def _():
            for copy in fills(n):
                copy.wait()

        pl.when((z >= n - 1) & more)(lambda: along(n).wait_send())


def climb(rows, weight, cos, sin, planes, number):
    dma = pltpu.SemaphoreType.DMA
    block = (rows.shape[0], weight.shape[1])
    blocks = jax.ShapeDtypeStruct((planes, *block), rows.dtype)
    return pl.pallas_call(
        functools.partial(climb_kernel, planes),
        out_shape=[blocks, blocks],
        in_specs=[VMEM] * 4,
        out_specs=[HBM] * 2,
        scratch_shapes=[
            pltpu.VMEM(block, rows.dtype),
            pltpu.VMEM(block, rows.dtype),
            *[dma((size,)) for size in (planes - 1, planes - 1, planes, planes)],
            dma,
            dma((2 * (planes - 1),)),
        ],
        compiler_params=pltpu.CompilerParams(
            collective_id=number, has_side_effects=True, vmem_limit_bytes=32 * 2**20
        ),
        cost_estimate=pl.CostEstimate(flops=1, bytes_accessed=1, transcendentals=0),
        name="climb",
    )(rows, weight, cos, sin)


def fall_kernel(
    planes, terms, rows, left, query_term, out_term, cos, sin, value, term, blocks,
    sends, recvs, total, send, recv, t_send, t_recv, own,
):
    y, x, c, index = place()
    z = lax.axis_index("z")
    me = index(y, x, c)
    others = team_of(y, x, c)
    ids = [dict(zip(("y", "x", "c"), other)) for other in others]
    f32 = jnp.float32
    count = rows.shape[0] // 8
    greet(ids + ring(planes))

    def rows_of(member):
        return rows.at[pl.ds(pl.multiple_of(member * count, count), count)]

    def hop(step):
        return pltpu.make_async_remote_copy(
            src_ref=sends.at[step - 1], dst_ref=recvs.at[step - 1], send_sem=send.at[step - 1], recv_sem=recv.at[step - 1],
            device_id={"z": z - 1}, device_id_type=MESH,
        )

    def came(step):
        return (z + 1 < planes) & (z + 1 + step - planes >= 0)

    copies = [
        pltpu.make_async_remote_copy(
            src_ref=rows_of(index(*other)), dst_ref=blocks.at[me], send_sem=t_send.at[number], recv_sem=t_recv.at[number],
            device_id=where, device_id_type=MESH,
        )
        for number, (other, where) in enumerate(zip(others, ids))
    ]
    copies.append(pltpu.make_async_copy(rows_of(me), blocks.at[me], own))
    size = terms.shape[2]
    for step in range(1, planes):
        block = z + step - planes
        if step > 1:
            pl.when(came(step - 1))(lambda: hop(step - 1).wait_recv())

        @pl.when((block >= 0) & (z + 1 == planes))
        def _():
            sends[step - 1] = terms[block]

        if step > 1:

            @pl.when((block >= 0) & (z + 1 < planes))
            def _():
                sends[step - 1] = (terms[block].astype(f32) + recvs[step - 2].astype(f32)).astype(terms.dtype)

        pl.when(block >= 0)(lambda: hop(step).start())
        if step == 1:
            for copy in copies:
                copy.start()
            total[...] = terms[z].astype(f32)
            term[:, :size] = query_term[...]
            term[:, 2 * size :] = out_term[...]
    last = planes - 1

    @pl.when(came(last))
    def _():
        hop(last).wait_recv()
        total[...] += recvs[last - 1].astype(f32)

    sides, span = cos.shape[:2]
    for line in range(0, total.shape[0], span):
        side = line // (total.shape[0] // sides)
        part = total[line : line + span]
        part = jnp.where(c == 0, turned(part, cos[side], -sin[side]), part)
        value[line : line + span] = part.astype(value.dtype)
    for start in range(0, left.shape[1], 512):
        term[start : start + 512, size : 2 * size] = mm_tn(left[:, start : start + 512], value[...]).astype(term.dtype)
    for step in range(1, planes):
        pl.when(z + step - planes >= 0)(lambda: hop(step).wait_send())
    for copy in copies:
        copy.wait()


def fall(terms, rows, left, query_term, out_term, cos, sin, planes, number):
    block = terms.shape[1:]
    dma, low = pltpu.SemaphoreType.DMA, terms.dtype
    return pl.pallas_call(
        functools.partial(fall_kernel, planes),
        out_shape=[
            jax.ShapeDtypeStruct(block, low),
            jax.ShapeDtypeStruct((left.shape[1], 3 * block[1]), low),
            jax.ShapeDtypeStruct((8, rows.shape[0] // 8, rows.shape[1]), low),
        ],
        in_specs=[VMEM, HBM] + [VMEM] * 5,
        out_specs=[VMEM, VMEM, HBM],
        scratch_shapes=[pltpu.VMEM((planes - 1, *block), low)] * 2
        + [pltpu.VMEM(block, jnp.float32)]
        + [dma((planes - 1,))] * 2
        + [dma((7,)), dma((7,)), dma],
        compiler_params=pltpu.CompilerParams(
            collective_id=number, has_side_effects=True, vmem_limit_bytes=40 * 2**20
        ),
        cost_estimate=pl.CostEstimate(flops=1, bytes_accessed=1, transcendentals=0),
        name="fall",
    )(terms, rows, left, query_term, out_term, cos, sin)


def dot(left, right, contract):
    return lax.dot_general(left, right, (contract, ((), ())), preferred_element_type=jnp.float32)


def mm(left, right):
    return dot(left, right, ((1,), (0,)))


def mm_nt(left, right):
    return dot(left, right, ((1,), (1,)))


def mm_tn(left, right):
    return dot(left, right, ((0,), (0,)))


def bmm(pattern, left, right):
    return jnp.einsum(pattern, left, right, preferred_element_type=jnp.float32)


def angle_tables(positions):
    half_dim = HEAD_SIZE // 2
    frequency = rope_base ** (-(jnp.arange(half_dim).astype(jnp.float32) * 2.0) / HEAD_SIZE)
    phases = positions.astype(jnp.float32)[:, None] * frequency[None, :]
    return (jnp.cos(phases), jnp.sin(phases))


def rotate(value, cos_table, sin_table):
    half = value.shape[-1] // 2
    a, b = value[..., :half], value[..., half:]
    return jnp.concatenate([a * cos_table - b * sin_table, b * cos_table + a * sin_table], axis=-1)


def rms_forward(value, gain_row):
    inverse = lax.rsqrt(jnp.mean(value * value, axis=-1, keepdims=True) + norm_eps)
    return (value * inverse * gain_row, inverse)


def rms_back(grad_out, value, inverse, gain_row):
    scaled = grad_out * gain_row
    grad_in = inverse * (
        scaled - value * inverse * inverse * jnp.mean(scaled * value, axis=-1, keepdims=True)
    )
    return (grad_in, jnp.sum(grad_out * value * inverse, axis=0))


def adamw(weight, gradient, moment_one, moment_two, step_rate, decay_rate, invert=jnp.reciprocal):
    mean_new = beta_one * moment_one + (1.0 - beta_one) * gradient
    square_new = beta_two * moment_two + (1.0 - beta_two) * gradient * gradient
    below = jnp.sqrt(square_new * (1.0 / (1.0 - beta_two**STEP))) + adam_eps
    direction = mean_new * (1.0 / (1.0 - beta_one**STEP)) * invert(below)
    return (weight - step_rate * (direction + decay_rate * weight), mean_new, square_new)


def attention_parts(core, length, q_ref, mine_ref, other_ref, query_ref, key_ref):
    mine, other = mine_ref[...].reshape(-1, HEAD_SIZE), other_ref[...].reshape(-1, HEAD_SIZE)
    first = core == 0
    k, v = jnp.where(first, mine, other), jnp.where(first, other, mine)
    q = q_ref[...].reshape(-1, HEAD_SIZE)
    at, key_at = query_ref[...], key_ref[...]
    allowed = (key_at <= at) & (key_at < length) & (key_at >= 0)
    scores = jnp.where(allowed, mm_nt(q, k) * HEAD_SIZE ** (-0.5), masked_value)
    exponent = jnp.exp(scores - jnp.max(scores, axis=-1, keepdims=True))
    return q, k, v, exponent / jnp.sum(exponent, axis=-1, keepdims=True)


def attention_kernel(core_ref, length_ref, q_ref, mine_ref, other_ref, query_ref, key_ref, out_ref):
    length = length_ref[pl.program_id(0)]
    _, _, v, soft = attention_parts(core_ref[0], length, q_ref, mine_ref, other_ref, query_ref, key_ref)
    out_ref[...] = mm(soft.astype(jnp.bfloat16), v).astype(jnp.bfloat16).reshape(out_ref.shape)


def attention_back_kernel(
    core_ref, length_ref, q_ref, mine_ref, other_ref, query_ref, key_ref, do_ref, cos_ref, sin_ref,
    dq_ref, keep_ref, send_ref,
):
    low = jnp.bfloat16
    core = core_ref[0]
    length = length_ref[pl.program_id(0)]
    q, k, v, soft = attention_parts(core, length, q_ref, mine_ref, other_ref, query_ref, key_ref)
    do = do_ref[...].reshape(-1, HEAD_SIZE)
    dp = mm_nt(do, v)
    delta = jnp.sum(soft * dp, axis=-1, keepdims=True)
    ds = (soft * (dp - delta) * HEAD_SIZE ** (-0.5)).astype(low)
    dq = mm(ds, k)
    cos_table, sin_table = cos_ref[...], sin_ref[...]
    half = HEAD_SIZE // 2
    a, b = dq[:, :half], dq[:, half:]
    turned = jnp.concatenate([a * cos_table + b * sin_table, b * cos_table - a * sin_table], axis=-1)
    dq_ref[...] = turned.astype(low).reshape(dq_ref.shape)
    dk, dv = mm_tn(ds, q), mm_tn(soft.astype(low), do)
    first = core == 0
    keep, send = (t.reshape(keep_ref.shape) for t in (jnp.where(first, dk, dv), jnp.where(first, dv, dk)))
    for block in range(keep_ref.shape[0]):
        at = core_ref[1 + block]
        keep_ref[at] = keep[block]
        send_ref[at] = send[block].astype(low)


def attention_call(kernel, core, lengths, q, mine, other, query_pos, key_pos, extra, outs, name):
    ny, count, span, size = q.shape
    nz = mine.shape[0]
    rows = pl.BlockSpec((ny, 1, span, size), lambda i, *_: (0, i, 0, 0))
    keys = pl.BlockSpec((nz, ny, 1, span, size), lambda i, *_: (0, 0, i, 0, 0))

    def whole(value):
        return pl.BlockSpec(value.shape, lambda i, *_: (0,) * value.ndim)

    kinds = {"rows": (rows, q.shape), "keys": (keys, mine.shape)}
    return pl.pallas_call(
        kernel,
        grid_spec=pltpu.PrefetchScalarGridSpec(
            num_scalar_prefetch=2,
            grid=(count,),
            in_specs=[rows, keys, keys, whole(query_pos), whole(key_pos)]
            + [rows if value.shape == q.shape else whole(value) for value in extra],
            out_specs=[kinds[kind][0] for kind, _ in outs],
        ),
        out_shape=[jax.ShapeDtypeStruct(kinds[kind][1], dtype) for kind, dtype in outs],
        compiler_params=pltpu.CompilerParams(vmem_limit_bytes=48 * 2**20),
        cost_estimate=pl.CostEstimate(flops=1, bytes_accessed=1, transcendentals=0),
        name=name,
    )(core, lengths, q, mine, other, query_pos, key_pos, *extra)


def feed_back_kernel(dyb_ref, weight_ref, gate_ref, up_ref, out_ref):
    dm = mm(dyb_ref[...], weight_ref[...])
    gate, upward = gate_ref[...], up_ref[...]
    sig = jax.nn.sigmoid(gate)
    part = gate.shape[1]
    out_ref[:, :part] = (dm * upward * sig * (1.0 + gate * (1.0 - sig))).astype(out_ref.dtype)
    out_ref[:, part:] = (dm * gate * sig).astype(out_ref.dtype)


def feed_back(dyb, weight, both, lines=256):
    count, part = both.shape[0], both.shape[1] // 2

    def rows(width, column=0):
        return pl.BlockSpec((lines, width), lambda i: (i, column))

    return pl.pallas_call(
        feed_back_kernel,
        grid=(count // lines,),
        in_specs=[rows(dyb.shape[1]), pl.BlockSpec(weight.shape, lambda i: (0, 0)), rows(part), rows(part, 1)],
        out_specs=rows(2 * part),
        out_shape=jax.ShapeDtypeStruct((count, 2 * part), jnp.bfloat16),
        compiler_params=pltpu.CompilerParams(vmem_limit_bytes=48 * 2**20),
        cost_estimate=pl.CostEstimate(flops=1, bytes_accessed=1, transcendentals=0),
        name="feed_back",
    )(dyb, weight, both, both)


def close_reciprocal(value):
    guess = pltpu.reciprocal(value, approx=True)
    return guess * (2.0 - value * guess)


def norm_of(lines_ref, tile_ref):
    gains = lines_ref[:-8]
    return jnp.sqrt(jnp.sum(gains * gains, keepdims=True) + lines_ref[-8:-7, 0:1] + tile_ref[0:1, 0:1])


def update_kernel(*refs):
    lines_ref, tile_ref, gain_ref, gate_up_ref, down_ref, attention_ref = refs[:6]
    gains, feed, attention = refs[6:9], refs[9:12], refs[12:15]
    new_gains, norm_ref, new_feed, new_attention, factor_ref = refs[15:18], refs[18], refs[19:23], refs[23:27], refs[27]
    rows = feed[0].shape[0]
    lines = pl.ds(pl.multiple_of(pl.program_id(0) * rows, rows), rows)

    @pl.when(pl.program_id(0) == 0)
    def _():
        norm = norm_of(lines_ref, tile_ref)
        norm_ref[...] = norm
        factor_ref[...] = clip_norm / norm
        weight, mean, square = (ref[...] for ref in gains)
        gradient = gain_ref[...] * factor_ref[...]
        for ref, value in zip(new_gains, adamw(weight, gradient, mean, square, gain_rate, 0.0)):
            ref[...] = value

    factor = factor_ref[...]

    def piece(olds, news, grad_ref, member, start, column, size):
        at = pl.ds(pl.multiple_of(column, size), size)
        gradient = grad_ref[member, lines, pl.ds(start, size)].astype(jnp.float32) * factor
        weight, mean, square = (ref[:, at] for ref in olds)
        values = adamw(weight, gradient, mean, square, matrix_rate, weight_decay, close_reciprocal)
        for ref, value in zip(news, (*values, values[0])):
            ref[:, at] = value.astype(ref.dtype)

    part = down_ref.shape[2]
    size = min(part, 512)

    @pl.loop(0, 8)
    def _(member):
        for offset in range(0, part, size):
            for number, (grad_ref, start) in enumerate(((gate_up_ref, 0), (gate_up_ref, part), (down_ref, 0))):
                column = (number * 8 + member) * part + offset
                piece(feed, new_feed, grad_ref, member, start + offset, column, size)
        core = lax.rem(member, 2)
        kv_column = (8 + 4 * core + lax.div(member, 2)) * HEAD_SIZE
        for number, column in enumerate((member * HEAD_SIZE, kv_column, (16 + member) * HEAD_SIZE)):
            piece(attention, new_attention, attention_ref, member, number * HEAD_SIZE, column, HEAD_SIZE)


def update(sums, grads, gains, feed, attention):
    f32, low = jnp.float32, jnp.bfloat16
    rows = min(feed[0].shape[0], 16)

    def some(value):
        return pl.BlockSpec((rows, value.shape[1]), lambda i: (i, 0))

    def whole(value):
        return pl.BlockSpec(value.shape, lambda i: (0,) * value.ndim)

    norm = jax.ShapeDtypeStruct((1, 1), f32)
    matrices = [jax.ShapeDtypeStruct(part[0].shape, dtype) for part in (feed, attention) for dtype in (f32, f32, f32, low)]
    return pl.pallas_call(
        update_kernel,
        grid=(feed[0].shape[0] // rows,),
        in_specs=[whole(value) for value in (*sums, *grads, *gains)] + [some(value) for value in (*feed, *attention)],
        out_specs=[whole(value) for value in (*gains, norm)] + [some(value) for value in matrices],
        out_shape=[jax.ShapeDtypeStruct(gains[0].shape, f32)] * 3 + [norm] + matrices,
        scratch_shapes=[pltpu.VMEM((1, 1), f32)],
        compiler_params=pltpu.CompilerParams(vmem_limit_bytes=56 * 2**20),
        name="update",
    )(*sums, *grads, *gains, *feed, *attention)


def is_square():
    return lax.axis_size("y") == 2 and lax.axis_size("x") == 2


def swap(blocks):
    return lax.all_to_all(blocks, TEAM, split_axis=0, concat_axis=0, tiled=True)


def over_planes(blocks):
    return lax.all_gather(blocks.reshape(-1, blocks.shape[-1]), "z", axis=0, tiled=True)


def scatter_planes(term):
    return lax.psum_scatter(term, "z", scatter_dimension=0, tiled=True)


def together(*values):
    return lax.optimization_barrier(values)


def scatter_team(rows, number, after=()):
    if not is_square():
        return swap(rows.reshape(8, -1, rows.shape[-1]))
    return turn(rows, number, after)[0]


def team_gather(local, number, after=()):
    if not is_square():
        return lax.all_gather(local, TEAM, axis=0, tiled=True)
    return plane_gather(local, number, after).reshape(-1, local.shape[1])


def team_sum(lefts, rights, number, after=()):
    if is_square():
        return plane_sum(lefts, rights, number, after)
    partial = mm_nt(jnp.concatenate(lefts, axis=1), jnp.concatenate(rights, axis=1))
    return lax.psum_scatter(partial.astype(jnp.bfloat16), TEAM, scatter_dimension=0, tiled=True).astype(jnp.float32)


def local(
    tokens,
    lengths,
    norm_gains,
    attention_weight,
    feed_weight,
    cotangent,
    attention_mean,
    attention_square,
    feed_mean,
    feed_square,
    gain_mean,
    gain_square,
):
    low = jnp.bfloat16
    sequences, span, width = tokens.shape
    ny, nx, nz = lax.axis_size("y"), lax.axis_size("x"), lax.axis_size("z")
    team = ny * nx * 2
    core = lax.axis_index("c")
    rows = attention_weight.shape[0]
    q_width, kv_width = QUERY_HEADS * HEAD_SIZE, KEY_VALUE_HEADS * HEAD_SIZE
    count = sequences * span
    all_sequences = nx * 2 * sequences
    reach = ny * span
    near = is_square()
    ff_part = FF // team

    def columns(start, size):
        return pl.ds(pl.multiple_of(start, size), size)

    def take_attention(sources, member, c):
        source = sources[0]
        starts = (
            member * HEAD_SIZE,
            q_width + c * kv_width + (member - c) // 2 * HEAD_SIZE,
            q_width + 2 * kv_width + member * HEAD_SIZE,
        )
        return jnp.concatenate([source[:, columns(s, HEAD_SIZE)].astype(low) for s in starts], axis=1)

    def take_feed(*parts):
        return lambda sources, member, c: jnp.concatenate(
            [sources[0][:, columns(part * FF + member * ff_part, ff_part)].astype(low) for part in parts], axis=1
        )

    def spread(source, take, size, number, after=()):
        if is_square():
            blocks = plane_swap([source], [(rows, size)], [take], number, after)[0]
        else:
            blocks = swap(jnp.stack([take([source], member, member % 2) for member in range(8)]))
        return blocks, over_planes(blocks)

    team_base = lax.axis_index("z") * reach
    team_pos = team_base + jnp.arange(reach, dtype=jnp.int32)
    own_pos = team_base + lax.axis_index("y") * span + jnp.arange(span, dtype=jnp.int32)
    if near:
        key_pos = jnp.concatenate([team_pos - back * reach for back in range(nz)])
    else:
        key_pos = jnp.arange(nz * reach, dtype=jnp.int32)
    query_at, key_at = team_pos[:, None], key_pos[None, :]
    cos_table, sin_table = angle_tables(team_pos)
    cos_rows, sin_rows = (t.reshape(ny, 1, span, -1) for t in (cos_table, sin_table))
    valid = (own_pos[None, :] < lengths[:, None]).astype(jnp.float32).reshape(count, 1)
    lengths_all = lax.all_gather(lengths, ("x", "c"), axis=0, tiled=True)
    planes = jnp.arange(nz, dtype=jnp.int32)
    if near:
        planes = (lax.axis_index("z") - planes) % nz
    core_at = jnp.concatenate([jnp.reshape(core, (1,)), planes]).astype(jnp.int32)

    def heads(value):
        return value.reshape(ny, all_sequences, span, HEAD_SIZE)

    x_in = tokens.reshape(count, width).astype(jnp.float32)
    normed_one, inverse_one = rms_forward(x_in, norm_gains[0])
    outer_grad = cotangent.reshape(count, width).astype(jnp.float32) * valid
    if is_square():
        attention_mine, h1, gate_up_blocks = begin(
            attention_weight,
            feed_weight,
            tokens.reshape(count, width),
            norm_gains[:1],
            (take_attention, take_feed(0, 1)),
            (3 * HEAD_SIZE, 2 * ff_part),
            nz,
            1,
        )
        h1 = h1.reshape(-1, width)
    else:
        attention_mine = spread(attention_weight, take_attention, 3 * HEAD_SIZE, 1)[1]
        gate_up_blocks, gate_up_weight = spread(feed_weight, take_feed(0, 1), 2 * ff_part, 2)
        h1 = team_gather(normed_one.astype(low), 3)
    query_weight = attention_mine[:, :HEAD_SIZE]
    kv_weight = attention_mine[:, HEAD_SIZE : 2 * HEAD_SIZE]
    out_weight = attention_mine[:, 2 * HEAD_SIZE :]
    tables = [t.reshape(ny, span, -1) for t in (cos_table, sin_table)]
    if is_square():
        kv, other = climb(h1, kv_weight, *tables, nz, 2)
        kv, other = (t.reshape(nz, ny, all_sequences, span, HEAD_SIZE) for t in (kv, other))
        gate_up_blocks, kv = together(gate_up_blocks, kv)
        gate_up_weight = over_planes(gate_up_blocks)
    else:
        kv_raw = heads(mm(h1, kv_weight))
        kv = jnp.where(core == 0, rotate(kv_raw, cos_rows, sin_rows), kv_raw).astype(low)
        kv = lax.all_gather(kv, "z", axis=0, tiled=False)
        other = lax.ppermute(kv, "c", [(0, 1), (1, 0)])
    q = rotate(heads(mm(h1, query_weight)), cos_rows, sin_rows).astype(low)
    attend = (core_at, lengths_all, q, kv, other, query_at, key_at)
    (o,) = attention_call(attention_kernel, *attend, (), [("rows", low)], "attention")
    o = o.reshape(-1, HEAD_SIZE)
    r = x_in + team_sum([o], [out_weight], 4)

    normed_two, inverse_two = rms_forward(r, norm_gains[1])
    h2 = team_gather(normed_two.astype(low), 16)
    dyb = team_gather(outer_grad.astype(low), 15, [h2])
    down_blocks, down_weight = spread(feed_weight, take_feed(2), ff_part, 12, [dyb])
    gate_up_weight, down_blocks = together(gate_up_weight, down_blocks)
    both = mm(h2, gate_up_weight)
    gate, upward = both[:, :ff_part], both[:, ff_part:]
    sig = jax.nn.sigmoid(gate)
    m = (gate * sig * upward).astype(low)
    down_term = mm_tn(dyb, m).astype(low)
    down_rows = scatter_planes(down_term)
    down_weight, down_term = together(down_weight, down_term)
    d_both = feed_back(dyb, down_weight, both)
    gate_up_term = mm_tn(h2, d_both).astype(low)
    gate_up_rows = scatter_planes(gate_up_term)
    dh2 = team_sum([d_both], [gate_up_weight], 7, [gate_up_term, down_term])
    mid_grad, gain_two = rms_back(dh2, r, inverse_two, norm_gains[1])
    dr = outer_grad + mid_grad
    drb = team_gather(dr.astype(low), 13, [down_rows])

    do = heads(mm(drb, out_weight).astype(low))
    dq, keep, theirs = attention_call(
        attention_back_kernel,
        *attend,
        (do, cos_table, sin_table),
        [("rows", low), ("keys", jnp.float32), ("keys", low)],
        "attention_back",
    )
    dq = dq.reshape(-1, HEAD_SIZE)
    dkv = keep + lax.ppermute(theirs, "c", [(0, 1), (1, 0)]).astype(jnp.float32)
    low_terms = dkv.astype(low)
    feed_sum = team_sum([m], [down_weight], 5, [low_terms])
    down_grad = scatter_team(down_rows, 6, [low_terms])
    layer_output = (r + feed_sum).astype(low)
    local_squares = sum(jnp.sum(jnp.square(part.astype(jnp.float32))) for part in (gate_up_rows, down_rows))
    query_term, out_term = mm_tn(h1, dq).astype(low), mm_tn(drb, o).astype(low)
    low_terms, gate_up_rows, layer_output, down_grad, query_term, out_term = together(
        low_terms, gate_up_rows, layer_output, down_grad, query_term, out_term
    )
    if is_square():
        low_terms = low_terms.reshape(nz, -1, HEAD_SIZE)
        dkv, attention_term, gate_up_grad = fall(low_terms, gate_up_rows, h1, query_term, out_term, *tables, nz, 8)
    else:
        dkv = lax.psum_scatter(low_terms, "z", scatter_dimension=0, tiled=True)[0].astype(jnp.float32)
        dkv = jnp.where(core == 0, rotate(dkv, cos_rows, -sin_rows), dkv).astype(low).reshape(-1, HEAD_SIZE)
        attention_term = jnp.concatenate([query_term, mm_tn(h1, dkv).astype(low), out_term], axis=1)
        gate_up_grad = scatter_team(gate_up_rows, 8)
    attention_rows = scatter_planes(attention_term)
    dh1 = team_sum([dq, dkv], [query_weight, kv_weight], 9, [attention_term])
    in_grad, gain_one = rms_back(dh1, x_in, inverse_one, norm_gains[0])
    input_gradient = dr + in_grad
    gain_local = jnp.stack([gain_one, gain_two]).reshape(-1, 128)
    lines = jnp.concatenate([gain_local, jnp.full((8, 128), local_squares)], axis=0)
    if is_square():
        lines = total_sum(lines, nz, 18)
        attention_grad, tile = turn(attention_rows, 10, (), nz)
    else:
        lines = lax.psum(lines, ALL)
        attention_grad = scatter_team(attention_rows, 10)
        tile = lax.psum(jnp.full((8, 128), jnp.sum(jnp.square(attention_rows.astype(jnp.float32)))), ALL)
    gain_grad = lines[:-8].reshape(2, width)
    news = update(
        (lines, tile, gain_grad),
        (gate_up_grad, down_grad, attention_grad),
        (norm_gains, gain_mean, gain_square),
        (feed_weight, feed_mean, feed_square),
        (attention_weight, attention_mean, attention_square),
    )
    gains_new, gradient_norm, feed_new, attention_new = news[:3], news[3], news[4:8], news[8:]
    return (
        layer_output.reshape(sequences, span, width),
        input_gradient.reshape(sequences, span, width),
        gradient_norm.reshape(()),
        *attention_new,
        *feed_new,
        *gains_new,
    )


def solution(mesh):
    ctx, fsdp = mesh.shape["ctx"], mesh.shape["fsdp"]
    inner = QUERY_HEADS // fsdp
    fine = Mesh(mesh.devices.reshape(ctx // inner, inner, fsdp // 2, 2), ALL)
    act = P(("x", "c"), ("z", "y"), None)
    matrix = P(ALL, None)
    return jax.shard_map(
        local,
        mesh=fine,
        in_specs=(act, P(("x", "c")), P(), matrix, matrix, act, matrix, matrix, matrix, matrix, P(), P()),
        out_specs=(act, act, P(), matrix, matrix, matrix, matrix, matrix, matrix, matrix, matrix, P(), P(), P()),
        check_vma=False,
    )
```

```python
import functools

import jax
import jax.numpy as jnp
from jax import lax
from jax.experimental import pallas as pl
from jax.experimental.pallas import tpu as pltpu
from jax.sharding import Mesh, PartitionSpec as P

QUERY_HEADS = 8
KEY_VALUE_HEADS = 4
HEAD_SIZE = 256
FF = 8192
STEP = 10

norm_eps = 1e-06
rope_base = 1000042.0
masked_value = -1e30
clip_norm = 1.0
beta_one = 0.9
beta_two = 0.95
adam_eps = 1e-08
matrix_rate = 0.03
gain_rate = 0.4
weight_decay = 0.1

TEAM = ("y", "x", "c")
ALL = ("z", "y", "x", "c")


MESH = pl.DeviceIdType.MESH
VMEM = pl.BlockSpec(memory_space=pltpu.VMEM)
HBM = pl.BlockSpec(memory_space=pl.ANY)


def place():
    y, x, c = lax.axis_index("y"), lax.axis_index("x"), lax.axis_index("c")
    return y, x, c, lambda yy, xx, cc: (yy * 2 + xx) * 2 + cc


def greet(others):
    barrier = pltpu.get_barrier_semaphore()
    for other in others:
        pl.semaphore_signal(barrier, inc=1, device_id=other, device_id_type=MESH)
    pl.semaphore_wait(barrier, len(others))


def gather_kernel(src, *refs):
    out, send, recv, own = refs[-4:]
    y, x, c, index = place()
    to_x, to_y, to_s = {"x": 1 - x}, {"y": 1 - y}, {"c": 1 - c}
    me, at_x, at_y, at_d = index(y, x, c), index(y, 1 - x, c), index(1 - y, x, c), index(1 - y, 1 - x, c)
    half = src.shape[0] // 2
    rows = (pl.ds(0, half), pl.ds(half, half))
    local = pltpu.make_async_copy(src, out.at[me], own)
    local.start()
    greet((to_x, to_y, to_s))

    def hop(slot, block, part, where, first=False):
        piece = out.at[block, rows[part]]
        return pltpu.make_async_remote_copy(
            src_ref=src.at[rows[part]] if first else piece,
            dst_ref=piece,
            send_sem=send.at[slot],
            recv_sem=recv.at[slot],
            device_id=where,
            device_id_type=MESH,
        )

    x0, x1 = hop(0, me, 0, to_x, True), hop(1, me, 1, to_x, True)
    y1, y0 = hop(2, me, 1, to_y, True), hop(3, me, 0, to_y, True)
    s0, s1 = hop(4, me, 0, to_s, True), hop(5, me, 1, to_s, True)
    for copy in (x0, y1, x1, y0, s0, s1):
        copy.start()
    x0.wait_recv()
    d0 = hop(6, at_x, 0, to_y)
    d0.start()
    y1.wait_recv()
    d1 = hop(7, at_y, 1, to_x)
    d1.start()
    sx0, sy1 = hop(8, at_x, 0, to_s), hop(9, at_y, 1, to_s)
    sx0.start()
    sy1.start()
    x1.wait_recv()
    sx1 = hop(10, at_x, 1, to_s)
    sx1.start()
    y0.wait_recv()
    sy0 = hop(11, at_y, 0, to_s)
    sy0.start()
    d0.wait_recv()
    sd0 = hop(12, at_d, 0, to_s)
    sd0.start()
    d1.wait_recv()
    sd1 = hop(13, at_d, 1, to_s)
    sd1.start()
    for copy in (s0, s1, sx0, sy1, sx1, sy0, sd0, sd1):
        copy.wait_recv()
    for copy in (x0, x1, y0, y1, s0, s1, d0, d1, sx0, sy1, sx1, sy0, sd0, sd1):
        copy.wait_send()
    local.wait()


def plane_gather(value, number, after=()):
    return pl.pallas_call(
        gather_kernel,
        out_shape=jax.ShapeDtypeStruct((8, *value.shape), value.dtype),
        in_specs=[HBM] * (1 + len(after)),
        out_specs=HBM,
        scratch_shapes=[
            pltpu.SemaphoreType.DMA((14,)),
            pltpu.SemaphoreType.DMA((14,)),
            pltpu.SemaphoreType.DMA,
        ],
        compiler_params=pltpu.CompilerParams(collective_id=number, has_side_effects=True),
        cost_estimate=pl.CostEstimate(flops=1, bytes_accessed=1, transcendentals=0),
        name="plane_gather",
    )(value, *after)


def sum_kernel(lefts, terms, tile, *refs):
    a_refs, w_refs = refs[:lefts], refs[lefts : lefts + len(terms)]
    out, s_send, s_recv, d_send, d_recv, x_send, x_recv, y_send, y_recv, x_acc, y_acc, send, recv = refs[-13:]
    y, x, c, index = place()
    to_x, to_y, to_s = {"x": 1 - x}, {"y": 1 - y}, {"c": 1 - c}
    rows, width = out.shape
    half = rows // 2
    parts = (pl.ds(0, half), pl.ds(half, half))
    f32, low = jnp.float32, jnp.bfloat16

    def product(block, put):
        lines = pl.ds(pl.multiple_of(block * rows, rows), rows)

        @pl.loop(0, width // tile)
        def _(step):
            cols = pl.ds(pl.multiple_of(step * tile, tile), tile)
            total = None
            for (left, start), w_ref in zip(terms, w_refs):
                term = mm_nt(a_refs[left][lines, start : start + w_ref.shape[1]], w_ref[cols, :])
                total = term if total is None else total + term
            put(cols, total)

    def hop(slot, src, dst, where):
        copy = pltpu.make_async_remote_copy(
            src_ref=src, dst_ref=dst, send_sem=send.at[slot], recv_sem=recv.at[slot],
            device_id=where, device_id_type=MESH,
        )
        return copy

    def to_sibling(slot, yy, xx):
        def put(cols, total):
            s_send[slot, :, cols] = total.astype(low)

        product(index(yy, xx, 1 - c), put)
        copy = hop(slot, s_send.at[slot], s_recv.at[slot], to_s)
        copy.start()
        return copy

    def with_sibling(slot, yy, xx, keep):
        def put(cols, total):
            keep[:, cols] = (total + s_recv[slot, :, cols].astype(f32)).astype(keep.dtype)

        product(index(yy, xx, c), put)

    greet((to_x, to_y, to_s))
    s0 = to_sibling(0, 1 - y, 1 - x)
    s1 = to_sibling(1, y, 1 - x)
    s0.wait_recv()
    with_sibling(0, 1 - y, 1 - x, d_send)
    d0 = hop(4, d_send.at[parts[0]], d_recv.at[parts[0]], to_x)
    d1 = hop(5, d_send.at[parts[1]], d_recv.at[parts[1]], to_y)
    d0.start()
    d1.start()
    s1.wait_recv()
    with_sibling(1, y, 1 - x, x_acc)
    x_send[parts[0]] = x_acc[parts[0]].astype(low)
    x0 = hop(6, x_send.at[parts[0]], x_recv.at[parts[0]], to_x)
    x0.start()
    s2 = to_sibling(2, 1 - y, x)
    s2.wait_recv()
    with_sibling(2, 1 - y, x, y_acc)
    y_send[parts[1]] = y_acc[parts[1]].astype(low)
    y1 = hop(7, y_send.at[parts[1]], y_recv.at[parts[1]], to_y)
    y1.start()
    s3 = to_sibling(3, y, x)
    d1.wait_recv()
    x_send[parts[1]] = (x_acc[parts[1]] + d_recv[parts[1]].astype(f32)).astype(low)
    x1 = hop(8, x_send.at[parts[1]], x_recv.at[parts[1]], to_x)
    x1.start()
    d0.wait_recv()
    y_send[parts[0]] = (y_acc[parts[0]] + d_recv[parts[0]].astype(f32)).astype(low)
    y0 = hop(9, y_send.at[parts[0]], y_recv.at[parts[0]], to_y)
    y0.start()
    s3.wait_recv()
    with_sibling(3, y, x, out)
    x0.wait_recv()
    y1.wait_recv()
    x1.wait_recv()
    y0.wait_recv()
    out[...] += x_recv[...].astype(f32) + y_recv[...].astype(f32)
    for copy in (s0, s1, s2, s3, d0, d1, x0, x1, y0, y1):
        copy.wait_send()


def plane_sum(lefts, rights, number, after=(), tile=512):
    ends = [(left, start) for left, a in enumerate(lefts) for start in range(0, a.shape[1], rights[0].shape[1])]
    terms = tuple(ends[: len(rights)])
    rows, width = lefts[0].shape[0] // 8, rights[0].shape[0]
    block = (rows, width)
    low, f32 = jnp.bfloat16, jnp.float32
    return pl.pallas_call(
        functools.partial(sum_kernel, len(lefts), terms, min(tile, width)),
        out_shape=jax.ShapeDtypeStruct(block, f32),
        in_specs=[VMEM] * (len(lefts) + len(rights)) + [HBM] * len(after),
        out_specs=VMEM,
        scratch_shapes=[
            pltpu.VMEM((4, *block), low),
            pltpu.VMEM((4, *block), low),
            *[pltpu.VMEM(block, low)] * 6,
            pltpu.VMEM(block, f32),
            pltpu.VMEM(block, f32),
            pltpu.SemaphoreType.DMA((10,)),
            pltpu.SemaphoreType.DMA((10,)),
        ],
        compiler_params=pltpu.CompilerParams(
            collective_id=number, has_side_effects=True, vmem_limit_bytes=48 * 2**20
        ),
        cost_estimate=pl.CostEstimate(flops=1, bytes_accessed=1, transcendentals=0),
        name="plane_sum",
    )(*lefts, *rights, *after)


def swap_kernel(pieces, takes, *refs):
    count = len(pieces)
    sources, (send, recv, own) = refs[: -2 * count - 3], refs[-3:]
    outs, holds = refs[-2 * count - 3 : -count - 3], refs[-count - 3 : -3]
    y, x, c, index = place()
    me = index(y, x, c)
    flips = [(fy, fx, fc) for fy, fx in ((1, 1), (0, 1), (1, 0), (0, 0)) for fc in (0, 1)]
    flips = [flip for flip in flips if flip != (0, 0, 0)]

    def there(flip):
        return tuple(1 - at if f else at for at, f in zip((y, x, c), flip))

    greet([dict(zip(("y", "x", "c"), there(flip))) for flip in flips])
    copies = []
    for piece in range(count):
        for number, flip in enumerate(flips):
            yy, xx, cc = there(flip)
            member = index(yy, xx, cc)
            holds[piece][number] = takes[piece](sources, member, cc)
            copy = pltpu.make_async_remote_copy(
                src_ref=holds[piece].at[number],
                dst_ref=outs[piece].at[me],
                send_sem=send.at[piece * 7 + number],
                recv_sem=recv.at[piece * 7 + number],
                device_id={"y": yy, "x": xx, "c": cc},
                device_id_type=MESH,
            )
            copy.start()
            copies.append(copy)
        holds[piece][7] = takes[piece](sources, me, c)
        keep = pltpu.make_async_copy(holds[piece].at[7], outs[piece].at[me], own.at[piece])
        keep.start()
        copies.append(keep)
    for copy in copies:
        copy.wait()


def plane_swap(sources, shapes, takes, number, after=()):
    low = jnp.bfloat16
    count = len(shapes)
    return pl.pallas_call(
        functools.partial(swap_kernel, shapes, takes),
        out_shape=[jax.ShapeDtypeStruct((8, *shape), low) for shape in shapes],
        in_specs=[VMEM] * len(sources) + [HBM] * len(after),
        out_specs=[HBM] * count,
        scratch_shapes=[
            *[pltpu.VMEM((8, *shape), low) for shape in shapes],
            pltpu.SemaphoreType.DMA((7 * count,)),
            pltpu.SemaphoreType.DMA((7 * count,)),
            pltpu.SemaphoreType.DMA((count,)),
        ],
        compiler_params=pltpu.CompilerParams(
            collective_id=number, has_side_effects=True, vmem_limit_bytes=48 * 2**20
        ),
        cost_estimate=pl.CostEstimate(flops=1, bytes_accessed=1, transcendentals=0),
        name="plane_swap",
    )(*sources, *after)


def team_of(y, x, c):
    flips = [(fy, fx, fc) for fy, fx in ((1, 1), (0, 1), (1, 0), (0, 0)) for fc in (0, 1)]
    return [
        tuple(1 - at if f else at for at, f in zip((y, x, c), flip)) for flip in flips if flip != (0, 0, 0)
    ]


def turn_kernel(planes, src, *refs):
    y, x, c, index = place()
    me = index(y, x, c)
    others = team_of(y, x, c)
    ids = [dict(zip(("y", "x", "c"), other)) for other in others]
    if planes:
        out, total, near, far, held, send, recv, own, send_lines, recv_lines = refs[-10:]
        z = lax.axis_index("z")
        column = [{"z": lax.rem(z + step, planes)} for step in range(1, planes)]
        fetch = pltpu.make_async_copy(src, held, own)
        fetch.start()
        fetch.wait()
        squares = jnp.zeros((8, held.shape[1]), jnp.float32)
        for start in range(0, held.shape[0], 64):
            part = held[start : start + 64].astype(jnp.float32)
            squares += jnp.sum(jnp.square(part).reshape(8, 8, -1), axis=0)
        near[me] = jnp.broadcast_to(jnp.sum(squares, keepdims=True), near.shape[1:])
    else:
        out, send, recv, own = refs[-4:]
        column = []
    greet(ids + column)
    count = src.shape[0] // 8

    def rows(member):
        return src.at[pl.ds(pl.multiple_of(member * count, count), count)]

    def spread(buffer, at, where, base):
        copies = [
            pltpu.make_async_remote_copy(
                src_ref=buffer.at[at],
                dst_ref=buffer.at[at],
                send_sem=send_lines.at[base + number],
                recv_sem=recv_lines.at[base + number],
                device_id=other,
                device_id_type=MESH,
            )
            for number, other in enumerate(where)
        ]
        for copy in copies:
            copy.start()
        return copies

    small = spread(near, me, ids, 0) if planes else []
    copies = [
        pltpu.make_async_remote_copy(
            src_ref=rows(index(*other)),
            dst_ref=out.at[me],
            send_sem=send.at[number],
            recv_sem=recv.at[number],
            device_id=where,
            device_id_type=MESH,
        )
        for number, (other, where) in enumerate(zip(others, ids))
    ]
    copies.append(pltpu.make_async_copy(rows(me), out.at[me], own))
    for copy in copies:
        copy.start()
    if planes:
        for copy in small:
            copy.wait()
        far[z] = jnp.sum(near[...], axis=0)
        for copy in spread(far, z, column, 7):
            copy.wait()
        total[...] = jnp.sum(far[...], axis=0)
    for copy in copies:
        copy.wait()


def total_kernel(planes, src, *refs):
    out, near, far, send, recv = refs[-5:]
    y, x, c, index = place()
    z = lax.axis_index("z")
    ids = [dict(zip(("y", "x", "c"), other)) for other in team_of(y, x, c)]
    column = [{"z": lax.rem(z + step, planes)} for step in range(1, planes)]
    me = index(y, x, c)
    near[me] = src[...]
    greet(ids + column)

    def spread(buffer, at, where, base):
        copies = [
            pltpu.make_async_remote_copy(
                src_ref=buffer.at[at],
                dst_ref=buffer.at[at],
                send_sem=send.at[base + number],
                recv_sem=recv.at[base + number],
                device_id=other,
                device_id_type=MESH,
            )
            for number, other in enumerate(where)
        ]
        for copy in copies:
            copy.start()
        for copy in copies:
            copy.wait()

    spread(near, me, ids, 0)
    far[z] = jnp.sum(near[...], axis=0)
    spread(far, z, column, 7)
    out[...] = jnp.sum(far[...], axis=0)


def total_sum(value, planes, number, after=()):
    return pl.pallas_call(
        functools.partial(total_kernel, planes),
        out_shape=jax.ShapeDtypeStruct(value.shape, value.dtype),
        in_specs=[VMEM] + [HBM] * len(after),
        out_specs=VMEM,
        scratch_shapes=[pltpu.VMEM((size, *value.shape), value.dtype) for size in (8, planes)]
        + [pltpu.SemaphoreType.DMA((6 + planes,))] * 2,
        compiler_params=pltpu.CompilerParams(
            collective_id=number, has_side_effects=True, vmem_limit_bytes=16 * 2**20
        ),
        cost_estimate=pl.CostEstimate(flops=1, bytes_accessed=1, transcendentals=0),
        name="total_sum",
    )(value, *after)


def turn(rows, number, after=(), planes=0):
    block = (rows.shape[0] // 8, rows.shape[1])
    dma = pltpu.SemaphoreType.DMA
    out_shape, out_specs = [jax.ShapeDtypeStruct((8, *block), rows.dtype)], [HBM]
    scratch = [dma((7,)), dma((7,)), dma]
    if planes:
        tile = jax.ShapeDtypeStruct((8, 128), jnp.float32)
        out_shape.append(tile)
        out_specs.append(VMEM)
        buffers = [pltpu.VMEM((size, *tile.shape), tile.dtype) for size in (8, planes)]
        scratch = buffers + [pltpu.VMEM(rows.shape, rows.dtype)] + scratch + [dma((6 + planes,)), dma((6 + planes,))]
    return pl.pallas_call(
        functools.partial(turn_kernel, planes),
        out_shape=out_shape,
        in_specs=[HBM] * (1 + len(after)),
        out_specs=out_specs,
        scratch_shapes=scratch,
        compiler_params=pltpu.CompilerParams(
            collective_id=number, has_side_effects=True, vmem_limit_bytes=56 * 2**20
        ),
        cost_estimate=pl.CostEstimate(flops=1, bytes_accessed=1, transcendentals=0),
        name="turn",
    )(rows, *after)


def hops(planes, send, recv, block, up):
    z = lax.axis_index("z")

    def step(number):
        gone, came = (z - number + 1, z - number) if up else (z + number - 1, z + number)
        goes = ((gone >= 0) & (z + 1 < planes)) if up else ((gone < planes) & (z >= 1))
        comes = (came >= 0) if up else (came < planes)

        def copy(b):
            return pltpu.make_async_remote_copy(
                src_ref=block(b),
                dst_ref=block(b),
                send_sem=send.at[number - 1],
                recv_sem=recv.at[number - 1],
                device_id={"z": z + 1 if up else z - 1},
                device_id_type=MESH,
            )

        return (
            lambda: pl.when(goes)(lambda: copy(gone).start()),
            lambda: pl.when(comes)(lambda: copy(came).wait_recv()),
            lambda: pl.when(goes)(lambda: copy(gone).wait_send()),
        )

    return [step(number) for number in range(1, planes)]


def ring(planes):
    z = lax.axis_index("z")
    return [{"z": lax.rem(z + 1, planes)}, {"z": lax.rem(z + planes - 1, planes)}]


def spread_to(others, ids, source, take, hold, place_of, send, recv, own):
    y, x, c, index = place()
    me = index(y, x, c)
    copies = []
    for number, (other, where) in enumerate(zip(others, ids)):
        hold[number] = take([source], index(*other), other[2])
        copy = pltpu.make_async_remote_copy(
            src_ref=hold.at[number], dst_ref=place_of(me), send_sem=send.at[number], recv_sem=recv.at[number],
            device_id=where, device_id_type=MESH,
        )
        copy.start()
        copies.append(copy)
    hold[7] = take([source], me, c)
    keep = pltpu.make_async_copy(hold.at[7], place_of(me), own)
    keep.start()
    return copies, keep


def begin_kernel(
    planes, take, take_feed, attention, feed, tokens_from, gain, all_attention, all_rows, columns,
    tokens, held, hold, feed_held, feed_hold, rows, a_send, a_recv, f_send, f_recv, r_send, r_recv, u_send, u_recv, d_send, d_recv, own,
):
    y, x, c, index = place()
    z = lax.axis_index("z")
    me, at_x, at_y, at_d = index(y, x, c), index(y, 1 - x, c), index(1 - y, x, c), index(1 - y, 1 - x, c)
    others = team_of(y, x, c)
    ids = [dict(zip(("y", "x", "c"), other)) for other in others]
    to_x, to_y, to_s = {"x": 1 - x}, {"y": 1 - y}, {"c": 1 - c}
    count = held.shape[0]
    half = rows.shape[0] // 2
    parts = (pl.ds(0, half), pl.ds(half, half))
    fetch = pltpu.make_async_copy(attention, held, own.at[0])
    fetch.start()
    fetch_tokens = pltpu.make_async_copy(tokens_from, tokens, own.at[5])
    fetch_tokens.start()
    fetch_feed = pltpu.make_async_copy(feed.at[:, pl.ds(0, feed_held.shape[1])], feed_held, own.at[3])
    fetch_feed.start()
    greet(ids + ring(planes))
    fetch.wait()

    def attention_rows(start, size):
        return all_attention.at[pl.ds(pl.multiple_of(start, count), size)]

    a_copies, a_keep = spread_to(
        others, ids, held, take, hold, lambda m: attention_rows((z * 8 + m) * count, count), a_send, a_recv, own.at[1]
    )

    def hop(slot, block, part, where, first=False):
        piece = all_rows.at[block, parts[part]]
        copy = pltpu.make_async_remote_copy(
            src_ref=rows.at[parts[part]] if first else piece, dst_ref=piece,
            send_sem=r_send.at[slot], recv_sem=r_recv.at[slot], device_id=where, device_id_type=MESH,
        )
        copy.start()
        return copy

    for copy in a_copies:
        copy.wait_recv()
    a_keep.wait()

    def plane_block(b):
        return attention_rows(b * 8 * count, 8 * count)

    up = hops(planes, u_send, u_recv, plane_block, True)
    down = hops(planes, d_send, d_recv, plane_block, False)

    def pass_on(number):
        if number > 0:
            up[number - 1][1]()
            down[number - 1][1]()
        if number < planes - 1:
            up[number][0]()
            down[number][0]()

    pass_on(0)
    fetch_tokens.wait()

    @pl.loop(0, rows.shape[0] // 16)
    def _(group):
        lines = pl.ds(pl.multiple_of(group * 16, 16), 16)
        rows[lines] = rms_forward(tokens[lines].astype(jnp.float32), gain[...])[0].astype(rows.dtype)

    x0, y1 = hop(0, me, 0, to_x, True), hop(2, me, 1, to_y, True)
    x1, y0 = hop(1, me, 1, to_x, True), hop(3, me, 0, to_y, True)
    s0, s1 = hop(4, me, 0, to_s, True), hop(5, me, 1, to_s, True)
    mine = pltpu.make_async_copy(rows, all_rows.at[me], own.at[2])
    mine.start()
    x0.wait_recv()
    d0 = hop(6, at_x, 0, to_y)
    y1.wait_recv()
    d1 = hop(7, at_y, 1, to_x)
    sx0, sy1 = hop(8, at_x, 0, to_s), hop(9, at_y, 1, to_s)
    fetch_feed.wait()
    f_copies, f_keep = spread_to(
        others, ids, feed_held, take_feed, feed_hold, lambda m: columns.at[m], f_send, f_recv, own.at[4]
    )
    pass_on(1)
    x1.wait_recv()
    sx1 = hop(10, at_x, 1, to_s)
    y0.wait_recv()
    sy0 = hop(11, at_y, 0, to_s)
    d0.wait_recv()
    sd0 = hop(12, at_d, 0, to_s)
    d1.wait_recv()
    sd1 = hop(13, at_d, 1, to_s)
    for number in range(2, planes):
        pass_on(number)
    for copy in (s0, s1, sx0, sy1, sx1, sy0, sd0, sd1, *f_copies):
        copy.wait_recv()
    for copy in (x0, x1, y0, y1, s0, s1, d0, d1, sx0, sy1, sx1, sy0, sd0, sd1, *a_copies, *f_copies):
        copy.wait_send()
    for step in up + down:
        step[2]()
    mine.wait()
    f_keep.wait()


def begin(attention, feed, tokens, gain, takes, widths, planes, number):
    low, dma = jnp.bfloat16, pltpu.SemaphoreType.DMA
    count = attention.shape[0]
    return pl.pallas_call(
        functools.partial(begin_kernel, planes, *takes),
        out_shape=[
            jax.ShapeDtypeStruct((planes * 8 * count, widths[0]), low),
            jax.ShapeDtypeStruct((8, *tokens.shape), low),
            jax.ShapeDtypeStruct((8, count, widths[1]), low),
        ],
        in_specs=[HBM, HBM, HBM, VMEM],
        out_specs=[HBM] * 3,
        scratch_shapes=[
            pltpu.VMEM(tokens.shape, tokens.dtype),
            pltpu.VMEM(attention.shape, attention.dtype),
            pltpu.VMEM((8, count, widths[0]), low),
            pltpu.VMEM((count, 8 * widths[1]), feed.dtype),
            pltpu.VMEM((8, count, widths[1]), low),
            pltpu.VMEM(tokens.shape, low),
            *[dma((size,)) for size in (7, 7, 7, 7, 14, 14, *[planes - 1] * 4, 6)],
        ],
        compiler_params=pltpu.CompilerParams(
            collective_id=number, has_side_effects=True, vmem_limit_bytes=54 * 2**20
        ),
        cost_estimate=pl.CostEstimate(flops=1, bytes_accessed=1, transcendentals=0),
        name="begin",
    )(attention, feed, tokens, gain)


def turned(value, cos_table, sin_table):
    half = value.shape[1] // 2
    first, second = value[:, :half], value[:, half:]
    return jnp.concatenate([first * cos_table - second * sin_table, second * cos_table + first * sin_table], axis=1)


def climb_kernel(
    planes, rows, weights, cos, sin, mine, other, weight, held, zeros, stay, u_send, u_recv, s_send, s_recv, own, fill, move
):
    z, c = lax.axis_index("z"), lax.axis_index("c")
    to_s = {"c": 1 - c}
    barrier = pltpu.get_barrier_semaphore()
    for where in [to_s] + ring(planes):
        pl.semaphore_signal(barrier, inc=1, device_id=where, device_id_type=MESH)
    count, (sides, span) = rows.shape[0], cos.shape[:2]
    size = 512
    pull_weight = pltpu.make_async_copy(
        weights.at[:, pl.ds(weight.shape[1], weight.shape[1])], weight, move.at[count // size]
    )
    pull_weight.start()
    pulls = [
        pltpu.make_async_copy(rows.at[pl.ds(start, size)], held.at[pl.ds(start, size)], move.at[start // size])
        for start in range(0, count, size)
    ]
    for copy in pulls:
        copy.start()
    pull_weight.wait()
    for start in range(0, count, size):
        pulls[start // size].wait()
        value = mm(held[start : start + size], weight[...])
        for line in range(0, size, span):
            side = (start + line) // (count // sides)
            part = value[line : line + span]
            part = jnp.where(c == 0, turned(part, cos[side], sin[side]), part)
            stay[start + line : start + line + span] = part.astype(stay.dtype)
    zeros[...] = jnp.zeros_like(zeros)
    pl.semaphore_wait(barrier, 3)

    def across(n):
        return pltpu.make_async_remote_copy(
            src_ref=stay if n == 0 else mine.at[n], dst_ref=other.at[n], send_sem=s_send.at[n], recv_sem=s_recv.at[n],
            device_id=to_s, device_id_type=MESH,
        )

    def along(n):
        return pltpu.make_async_remote_copy(
            src_ref=stay if n == 1 else mine.at[n - 1], dst_ref=mine.at[n], send_sem=u_send.at[n - 1], recv_sem=u_recv.at[n - 1],
            device_id={"z": z + 1}, device_id_type=MESH,
        )

    def fills(n):
        return [
            pltpu.make_async_copy(zeros, buffer.at[n], fill.at[2 * (n - 1) + number])
            for number, buffer in enumerate((mine, other))
        ]

    keep = pltpu.make_async_copy(stay, mine.at[0], own)
    more = z + 1 < planes
    pl.when(more)(lambda: along(1).start())
    across(0).start()
    keep.start()
    for n in range(1, planes):

        @pl.when(z < n)
        def _():
            for copy in fills(n):
                copy.start()

    for n in range(1, planes):

        @pl.when(z >= n)
        def _():
            along(n).wait_recv()
            if n + 1 < planes:
                pl.when(more)(lambda: along(n + 1).start())
            across(n).start()

    across(0).wait()
    keep.wait()
    for n in range(1, planes):

        @pl.when(z >= n)
        def _():
            across(n).wait()

        @pl.when(z < n)
        def _():
            for copy in fills(n):
                copy.wait()

        pl.when((z >= n - 1) & more)(lambda: along(n).wait_send())


def climb(rows, weights, cos, sin, planes, number):
    dma = pltpu.SemaphoreType.DMA
    block = (rows.shape[0], weights.shape[1] // 3)
    blocks = jax.ShapeDtypeStruct((planes, *block), rows.dtype)
    return pl.pallas_call(
        functools.partial(climb_kernel, planes),
        out_shape=[blocks, blocks],
        in_specs=[HBM] * 2 + [VMEM] * 2,
        out_specs=[HBM] * 2,
        scratch_shapes=[
            pltpu.VMEM((weights.shape[0], block[1]), rows.dtype),
            pltpu.VMEM(rows.shape, rows.dtype),
            pltpu.VMEM(block, rows.dtype),
            pltpu.VMEM(block, rows.dtype),
            *[dma((size,)) for size in (planes - 1, planes - 1, planes, planes)],
            dma,
            dma((2 * (planes - 1),)),
            dma((rows.shape[0] // 512 + 1,)),
        ],
        compiler_params=pltpu.CompilerParams(
            collective_id=number, has_side_effects=True, vmem_limit_bytes=56 * 2**20
        ),
        cost_estimate=pl.CostEstimate(flops=1, bytes_accessed=1, transcendentals=0),
        name="climb",
    )(rows, weights, cos, sin)


def fall_kernel(
    planes, terms_from, rows, left_from, query_term, out_term, cos, sin, value, term, blocks,
    terms, left, sends, recvs, total, held, send, recv, t_send, t_recv, own, move, fetch,
):
    y, x, c, index = place()
    z = lax.axis_index("z")
    me = index(y, x, c)
    others = team_of(y, x, c)
    ids = [dict(zip(("y", "x", "c"), other)) for other in others]
    f32 = jnp.float32
    count = rows.shape[0] // 8
    size = terms.shape[2]
    given = ((query_term, 0), (out_term, 2))
    pulls = [pltpu.make_async_copy(ref, held.at[n], move.at[n]) for n, (ref, _) in enumerate(given)]
    get_terms = pltpu.make_async_copy(terms_from, terms, fetch.at[0])
    get_terms.start()
    get_left = pltpu.make_async_copy(left_from, left, fetch.at[1])
    get_left.start()
    for copy in pulls:
        copy.start()
    greet(ids + ring(planes))
    get_terms.wait()

    def rows_of(member):
        return rows.at[pl.ds(pl.multiple_of(member * count, count), count)]

    def hop(step):
        return pltpu.make_async_remote_copy(
            src_ref=sends.at[step - 1], dst_ref=recvs.at[step - 1], send_sem=send.at[step - 1], recv_sem=recv.at[step - 1],
            device_id={"z": z - 1}, device_id_type=MESH,
        )

    def came(step):
        return (z + 1 < planes) & (z + 1 + step - planes >= 0)

    copies = [
        pltpu.make_async_remote_copy(
            src_ref=rows_of(index(*other)), dst_ref=blocks.at[me], send_sem=t_send.at[number], recv_sem=t_recv.at[number],
            device_id=where, device_id_type=MESH,
        )
        for number, (other, where) in enumerate(zip(others, ids))
    ]
    copies.append(pltpu.make_async_copy(rows_of(me), blocks.at[me], own))
    pushes = []
    for step in range(1, planes):
        block = z + step - planes
        if step > 1:
            pl.when(came(step - 1))(lambda: hop(step - 1).wait_recv())

        @pl.when((block >= 0) & (z + 1 == planes))
        def _():
            sends[step - 1] = terms[block]

        if step > 1:

            @pl.when((block >= 0) & (z + 1 < planes))
            def _():
                sends[step - 1] = (terms[block].astype(f32) + recvs[step - 2].astype(f32)).astype(terms.dtype)

        pl.when(block >= 0)(lambda: hop(step).start())
        if step == 1:
            for copy in copies:
                copy.start()
            total[...] = terms[z].astype(f32)
            for n, (_, column) in enumerate(given):
                pulls[n].wait()
                pushes.append(
                    pltpu.make_async_copy(held.at[n], term.at[:, pl.ds(column * size, size)], move.at[2 + n])
                )
                pushes[-1].start()
    last = planes - 1

    @pl.when(came(last))
    def _():
        hop(last).wait_recv()
        total[...] += recvs[last - 1].astype(f32)

    sides, span = cos.shape[:2]
    for line in range(0, total.shape[0], span):
        side = line // (total.shape[0] // sides)
        part = total[line : line + span]
        part = jnp.where(c == 0, turned(part, cos[side], -sin[side]), part)
        value[line : line + span] = part.astype(value.dtype)
    get_left.wait()
    for start in range(0, left.shape[1], 512):
        lines = pl.ds(start, 512)
        held[2, lines] = mm_tn(left[:, start : start + 512], value[...]).astype(held.dtype)
        pushes.append(
            pltpu.make_async_copy(
                held.at[2, lines], term.at[lines, pl.ds(size, size)], move.at[4 + start // 512]
            )
        )
        pushes[-1].start()
    for step in range(1, planes):
        pl.when(z + step - planes >= 0)(lambda: hop(step).wait_send())
    for copy in copies + pushes:
        copy.wait()


def fall(terms, rows, left, query_term, out_term, cos, sin, planes, number):
    block = terms.shape[1:]
    dma, low = pltpu.SemaphoreType.DMA, terms.dtype
    return pl.pallas_call(
        functools.partial(fall_kernel, planes),
        out_shape=[
            jax.ShapeDtypeStruct(block, low),
            jax.ShapeDtypeStruct((left.shape[1], 3 * block[1]), low),
            jax.ShapeDtypeStruct((8, rows.shape[0] // 8, rows.shape[1]), low),
        ],
        in_specs=[HBM] * 5 + [VMEM] * 2,
        out_specs=[VMEM, HBM, HBM],
        scratch_shapes=[pltpu.VMEM(terms.shape, low), pltpu.VMEM(left.shape, low)]
        + [pltpu.VMEM((planes - 1, *block), low)] * 2
        + [pltpu.VMEM(block, jnp.float32), pltpu.VMEM((3, left.shape[1], block[1]), low)]
        + [dma((planes - 1,))] * 2
        + [dma((7,)), dma((7,)), dma, dma((4 + left.shape[1] // 512,)), dma((2,))],
        compiler_params=pltpu.CompilerParams(
            collective_id=number, has_side_effects=True, vmem_limit_bytes=56 * 2**20
        ),
        cost_estimate=pl.CostEstimate(flops=1, bytes_accessed=1, transcendentals=0),
        name="fall",
    )(terms, rows, left, query_term, out_term, cos, sin)


def dot(left, right, contract):
    return lax.dot_general(left, right, (contract, ((), ())), preferred_element_type=jnp.float32)


def mm(left, right):
    return dot(left, right, ((1,), (0,)))


def mm_nt(left, right):
    return dot(left, right, ((1,), (1,)))


def mm_tn(left, right):
    return dot(left, right, ((0,), (0,)))


def bmm(pattern, left, right):
    return jnp.einsum(pattern, left, right, preferred_element_type=jnp.float32)


def angle_tables(positions):
    half_dim = HEAD_SIZE // 2
    frequency = rope_base ** (-(jnp.arange(half_dim).astype(jnp.float32) * 2.0) / HEAD_SIZE)
    phases = positions.astype(jnp.float32)[:, None] * frequency[None, :]
    return (jnp.cos(phases), jnp.sin(phases))


def rotate(value, cos_table, sin_table):
    half = value.shape[-1] // 2
    a, b = value[..., :half], value[..., half:]
    return jnp.concatenate([a * cos_table - b * sin_table, b * cos_table + a * sin_table], axis=-1)


def rms_forward(value, gain_row):
    inverse = lax.rsqrt(jnp.mean(value * value, axis=-1, keepdims=True) + norm_eps)
    return (value * inverse * gain_row, inverse)


def rms_back(grad_out, value, inverse, gain_row):
    scaled = grad_out * gain_row
    grad_in = inverse * (
        scaled - value * inverse * inverse * jnp.mean(scaled * value, axis=-1, keepdims=True)
    )
    return (grad_in, jnp.sum(grad_out * value * inverse, axis=0))


def adamw(weight, gradient, moment_one, moment_two, step_rate, decay_rate, invert=jnp.reciprocal):
    mean_new = beta_one * moment_one + (1.0 - beta_one) * gradient
    square_new = beta_two * moment_two + (1.0 - beta_two) * gradient * gradient
    below = jnp.sqrt(square_new * (1.0 / (1.0 - beta_two**STEP))) + adam_eps
    direction = mean_new * (1.0 / (1.0 - beta_one**STEP)) * invert(below)
    return (weight - step_rate * (direction + decay_rate * weight), mean_new, square_new)


def attention_parts(core, length, q_ref, mine_ref, other_ref, query_ref, key_ref):
    mine, other = mine_ref[...].reshape(-1, HEAD_SIZE), other_ref[...].reshape(-1, HEAD_SIZE)
    first = core == 0
    k, v = jnp.where(first, mine, other), jnp.where(first, other, mine)
    q = q_ref[...].reshape(-1, HEAD_SIZE)
    at, key_at = query_ref[...], key_ref[...]
    allowed = (key_at <= at) & (key_at < length) & (key_at >= 0)
    scores = jnp.where(allowed, mm_nt(q, k) * HEAD_SIZE ** (-0.5), masked_value)
    exponent = jnp.exp(scores - jnp.max(scores, axis=-1, keepdims=True))
    return q, k, v, exponent / jnp.sum(exponent, axis=-1, keepdims=True)


def attention_kernel(core_ref, length_ref, q_ref, mine_ref, other_ref, query_ref, key_ref, out_ref):
    length = length_ref[pl.program_id(0)]
    _, _, v, soft = attention_parts(core_ref[0], length, q_ref, mine_ref, other_ref, query_ref, key_ref)
    out_ref[...] = mm(soft.astype(jnp.bfloat16), v).astype(jnp.bfloat16).reshape(out_ref.shape)


def attention_back_kernel(
    core_ref, length_ref, q_ref, mine_ref, other_ref, query_ref, key_ref, do_ref, cos_ref, sin_ref,
    dq_ref, keep_ref, send_ref,
):
    low = jnp.bfloat16
    core = core_ref[0]
    length = length_ref[pl.program_id(0)]
    q, k, v, soft = attention_parts(core, length, q_ref, mine_ref, other_ref, query_ref, key_ref)
    do = do_ref[...].reshape(-1, HEAD_SIZE)
    dp = mm_nt(do, v)
    delta = jnp.sum(soft * dp, axis=-1, keepdims=True)
    ds = (soft * (dp - delta) * HEAD_SIZE ** (-0.5)).astype(low)
    dq = mm(ds, k)
    cos_table, sin_table = cos_ref[...], sin_ref[...]
    half = HEAD_SIZE // 2
    a, b = dq[:, :half], dq[:, half:]
    turned = jnp.concatenate([a * cos_table + b * sin_table, b * cos_table - a * sin_table], axis=-1)
    dq_ref[...] = turned.astype(low).reshape(dq_ref.shape)
    dk, dv = mm_tn(ds, q), mm_tn(soft.astype(low), do)
    first = core == 0
    keep, send = (t.reshape(keep_ref.shape) for t in (jnp.where(first, dk, dv), jnp.where(first, dv, dk)))
    for block in range(keep_ref.shape[0]):
        at = core_ref[1 + block]
        keep_ref[at] = keep[block]
        send_ref[at] = send[block].astype(low)


def attention_call(kernel, core, lengths, q, mine, other, query_pos, key_pos, extra, outs, name):
    ny, count, span, size = q.shape
    nz = mine.shape[0]
    rows = pl.BlockSpec((ny, 1, span, size), lambda i, *_: (0, i, 0, 0))
    keys = pl.BlockSpec((nz, ny, 1, span, size), lambda i, *_: (0, 0, i, 0, 0))

    def whole(value):
        return pl.BlockSpec(value.shape, lambda i, *_: (0,) * value.ndim)

    kinds = {"rows": (rows, q.shape), "keys": (keys, mine.shape)}
    return pl.pallas_call(
        kernel,
        grid_spec=pltpu.PrefetchScalarGridSpec(
            num_scalar_prefetch=2,
            grid=(count,),
            in_specs=[rows, keys, keys, whole(query_pos), whole(key_pos)]
            + [rows if value.shape == q.shape else whole(value) for value in extra],
            out_specs=[kinds[kind][0] for kind, _ in outs],
        ),
        out_shape=[jax.ShapeDtypeStruct(kinds[kind][1], dtype) for kind, dtype in outs],
        compiler_params=pltpu.CompilerParams(vmem_limit_bytes=48 * 2**20),
        cost_estimate=pl.CostEstimate(flops=1, bytes_accessed=1, transcendentals=0),
        name=name,
    )(core, lengths, q, mine, other, query_pos, key_pos, *extra)


def feed_back_kernel(dyb_ref, weight_ref, gate_ref, up_ref, out_ref):
    dm = mm(dyb_ref[...], weight_ref[...])
    gate, upward = gate_ref[...], up_ref[...]
    sig = jax.nn.sigmoid(gate)
    part = gate.shape[1]
    out_ref[:, :part] = (dm * upward * sig * (1.0 + gate * (1.0 - sig))).astype(out_ref.dtype)
    out_ref[:, part:] = (dm * gate * sig).astype(out_ref.dtype)


def feed_back(dyb, weight, both, lines=256):
    count, part = both.shape[0], both.shape[1] // 2

    def rows(width, column=0):
        return pl.BlockSpec((lines, width), lambda i: (i, column))

    return pl.pallas_call(
        feed_back_kernel,
        grid=(count // lines,),
        in_specs=[rows(dyb.shape[1]), pl.BlockSpec(weight.shape, lambda i: (0, 0)), rows(part), rows(part, 1)],
        out_specs=rows(2 * part),
        out_shape=jax.ShapeDtypeStruct((count, 2 * part), jnp.bfloat16),
        compiler_params=pltpu.CompilerParams(vmem_limit_bytes=48 * 2**20),
        cost_estimate=pl.CostEstimate(flops=1, bytes_accessed=1, transcendentals=0),
        name="feed_back",
    )(dyb, weight, both, both)


def close_reciprocal(value):
    guess = pltpu.reciprocal(value, approx=True)
    return guess * (2.0 - value * guess)


def norm_of(lines_ref, tile_ref):
    gains = lines_ref[:-8]
    return jnp.sqrt(jnp.sum(gains * gains, keepdims=True) + lines_ref[-8:-7, 0:1] + tile_ref[0:1, 0:1])


def update_kernel(*refs):
    lines_ref, tile_ref, gain_ref, gate_up_ref, down_ref, attention_ref = refs[:6]
    gains, feed, attention = refs[6:9], refs[9:12], refs[12:15]
    new_gains, norm_ref, new_feed, new_attention, factor_ref = refs[15:18], refs[18], refs[19:23], refs[23:27], refs[27]
    rows = feed[0].shape[0]
    lines = pl.ds(pl.multiple_of(pl.program_id(0) * rows, rows), rows)

    @pl.when(pl.program_id(0) == 0)
    def _():
        norm = norm_of(lines_ref, tile_ref)
        norm_ref[...] = norm
        factor_ref[...] = clip_norm / norm
        weight, mean, square = (ref[...] for ref in gains)
        gradient = gain_ref[...] * factor_ref[...]
        for ref, value in zip(new_gains, adamw(weight, gradient, mean, square, gain_rate, 0.0)):
            ref[...] = value

    factor = factor_ref[...]

    def piece(olds, news, grad_ref, member, start, column, size):
        at = pl.ds(pl.multiple_of(column, size), size)
        gradient = grad_ref[member, lines, pl.ds(start, size)].astype(jnp.float32) * factor
        weight, mean, square = (ref[:, at] for ref in olds)
        values = adamw(weight, gradient, mean, square, matrix_rate, weight_decay, close_reciprocal)
        for ref, value in zip(news, (*values, values[0])):
            ref[:, at] = value.astype(ref.dtype)

    part = down_ref.shape[2]
    size = min(part, 512)

    @pl.loop(0, 8)
    def _(member):
        for offset in range(0, part, size):
            for number, (grad_ref, start) in enumerate(((gate_up_ref, 0), (gate_up_ref, part), (down_ref, 0))):
                column = (number * 8 + member) * part + offset
                piece(feed, new_feed, grad_ref, member, start + offset, column, size)
        core = lax.rem(member, 2)
        kv_column = (8 + 4 * core + lax.div(member, 2)) * HEAD_SIZE
        for number, column in enumerate((member * HEAD_SIZE, kv_column, (16 + member) * HEAD_SIZE)):
            piece(attention, new_attention, attention_ref, member, number * HEAD_SIZE, column, HEAD_SIZE)


def update(sums, grads, gains, feed, attention):
    f32, low = jnp.float32, jnp.bfloat16
    rows = min(feed[0].shape[0], 16)

    def some(value):
        return pl.BlockSpec((rows, value.shape[1]), lambda i: (i, 0))

    def whole(value):
        return pl.BlockSpec(value.shape, lambda i: (0,) * value.ndim)

    norm = jax.ShapeDtypeStruct((1, 1), f32)
    matrices = [jax.ShapeDtypeStruct(part[0].shape, dtype) for part in (feed, attention) for dtype in (f32, f32, f32, low)]
    return pl.pallas_call(
        update_kernel,
        grid=(feed[0].shape[0] // rows,),
        in_specs=[whole(value) for value in (*sums, *grads, *gains)] + [some(value) for value in (*feed, *attention)],
        out_specs=[whole(value) for value in (*gains, norm)] + [some(value) for value in matrices],
        out_shape=[jax.ShapeDtypeStruct(gains[0].shape, f32)] * 3 + [norm] + matrices,
        scratch_shapes=[pltpu.VMEM((1, 1), f32)],
        compiler_params=pltpu.CompilerParams(vmem_limit_bytes=56 * 2**20),
        name="update",
    )(*sums, *grads, *gains, *feed, *attention)


def is_square():
    return lax.axis_size("y") == 2 and lax.axis_size("x") == 2


def swap(blocks):
    return lax.all_to_all(blocks, TEAM, split_axis=0, concat_axis=0, tiled=True)


def over_planes(blocks):
    return lax.all_gather(blocks.reshape(-1, blocks.shape[-1]), "z", axis=0, tiled=True)


def scatter_planes(term):
    return lax.psum_scatter(term, "z", scatter_dimension=0, tiled=True)


def together(*values):
    return lax.optimization_barrier(values)


def scatter_team(rows, number, after=()):
    if not is_square():
        return swap(rows.reshape(8, -1, rows.shape[-1]))
    return turn(rows, number, after)[0]


def team_gather(local, number, after=()):
    if not is_square():
        return lax.all_gather(local, TEAM, axis=0, tiled=True)
    return plane_gather(local, number, after).reshape(-1, local.shape[1])


def team_sum(lefts, rights, number, after=()):
    if is_square():
        return plane_sum(lefts, rights, number, after)
    partial = mm_nt(jnp.concatenate(lefts, axis=1), jnp.concatenate(rights, axis=1))
    return lax.psum_scatter(partial.astype(jnp.bfloat16), TEAM, scatter_dimension=0, tiled=True).astype(jnp.float32)


def local(
    tokens,
    lengths,
    norm_gains,
    attention_weight,
    feed_weight,
    cotangent,
    attention_mean,
    attention_square,
    feed_mean,
    feed_square,
    gain_mean,
    gain_square,
):
    low = jnp.bfloat16
    sequences, span, width = tokens.shape
    ny, nx, nz = lax.axis_size("y"), lax.axis_size("x"), lax.axis_size("z")
    team = ny * nx * 2
    core = lax.axis_index("c")
    rows = attention_weight.shape[0]
    q_width, kv_width = QUERY_HEADS * HEAD_SIZE, KEY_VALUE_HEADS * HEAD_SIZE
    count = sequences * span
    all_sequences = nx * 2 * sequences
    reach = ny * span
    near = is_square()
    ff_part = FF // team

    def columns(start, size):
        return pl.ds(pl.multiple_of(start, size), size)

    def take_attention(sources, member, c):
        source = sources[0]
        starts = (
            member * HEAD_SIZE,
            q_width + c * kv_width + (member - c) // 2 * HEAD_SIZE,
            q_width + 2 * kv_width + member * HEAD_SIZE,
        )
        return jnp.concatenate([source[:, columns(s, HEAD_SIZE)].astype(low) for s in starts], axis=1)

    def take_feed(*parts):
        return lambda sources, member, c: jnp.concatenate(
            [sources[0][:, columns(part * FF + member * ff_part, ff_part)].astype(low) for part in parts], axis=1
        )

    def spread(source, take, size, number, after=()):
        if is_square():
            blocks = plane_swap([source], [(rows, size)], [take], number, after)[0]
        else:
            blocks = swap(jnp.stack([take([source], member, member % 2) for member in range(8)]))
        return blocks, over_planes(blocks)

    team_base = lax.axis_index("z") * reach
    team_pos = team_base + jnp.arange(reach, dtype=jnp.int32)
    own_pos = team_base + lax.axis_index("y") * span + jnp.arange(span, dtype=jnp.int32)
    if near:
        key_pos = jnp.concatenate([team_pos - back * reach for back in range(nz)])
    else:
        key_pos = jnp.arange(nz * reach, dtype=jnp.int32)
    query_at, key_at = team_pos[:, None], key_pos[None, :]
    cos_table, sin_table = angle_tables(team_pos)
    cos_rows, sin_rows = (t.reshape(ny, 1, span, -1) for t in (cos_table, sin_table))
    valid = (own_pos[None, :] < lengths[:, None]).astype(jnp.float32).reshape(count, 1)
    lengths_all = lax.all_gather(lengths, ("x", "c"), axis=0, tiled=True)
    planes = jnp.arange(nz, dtype=jnp.int32)
    if near:
        planes = (lax.axis_index("z") - planes) % nz
    core_at = jnp.concatenate([jnp.reshape(core, (1,)), planes]).astype(jnp.int32)

    def heads(value):
        return value.reshape(ny, all_sequences, span, HEAD_SIZE)

    x_in = tokens.reshape(count, width).astype(jnp.float32)
    normed_one, inverse_one = rms_forward(x_in, norm_gains[0])
    outer_grad = cotangent.reshape(count, width).astype(jnp.float32) * valid
    if is_square():
        attention_mine, h1, gate_up_blocks = begin(
            attention_weight,
            feed_weight,
            tokens.reshape(count, width),
            norm_gains[:1],
            (take_attention, take_feed(0, 1)),
            (3 * HEAD_SIZE, 2 * ff_part),
            nz,
            1,
        )
        h1 = h1.reshape(-1, width)
    else:
        attention_mine = spread(attention_weight, take_attention, 3 * HEAD_SIZE, 1)[1]
        gate_up_blocks, gate_up_weight = spread(feed_weight, take_feed(0, 1), 2 * ff_part, 2)
        h1 = team_gather(normed_one.astype(low), 3)
    query_weight = attention_mine[:, :HEAD_SIZE]
    kv_weight = attention_mine[:, HEAD_SIZE : 2 * HEAD_SIZE]
    out_weight = attention_mine[:, 2 * HEAD_SIZE :]
    tables = [t.reshape(ny, span, -1) for t in (cos_table, sin_table)]
    if is_square():
        kv, other = climb(h1, attention_mine, *tables, nz, 2)
        kv, other = (t.reshape(nz, ny, all_sequences, span, HEAD_SIZE) for t in (kv, other))
        gate_up_blocks, kv = together(gate_up_blocks, kv)
        gate_up_weight = over_planes(gate_up_blocks)
    else:
        kv_raw = heads(mm(h1, kv_weight))
        kv = jnp.where(core == 0, rotate(kv_raw, cos_rows, sin_rows), kv_raw).astype(low)
        kv = lax.all_gather(kv, "z", axis=0, tiled=False)
        other = lax.ppermute(kv, "c", [(0, 1), (1, 0)])
    q = rotate(heads(mm(h1, query_weight)), cos_rows, sin_rows).astype(low)
    attend = (core_at, lengths_all, q, kv, other, query_at, key_at)
    (o,) = attention_call(attention_kernel, *attend, (), [("rows", low)], "attention")
    o = o.reshape(-1, HEAD_SIZE)
    r = x_in + team_sum([o], [out_weight], 4)

    normed_two, inverse_two = rms_forward(r, norm_gains[1])
    h2 = team_gather(normed_two.astype(low), 16)
    dyb = team_gather(outer_grad.astype(low), 15, [h2])
    down_blocks, down_weight = spread(feed_weight, take_feed(2), ff_part, 12, [dyb])
    gate_up_weight, down_blocks = together(gate_up_weight, down_blocks)
    both = mm(h2, gate_up_weight)
    gate, upward = both[:, :ff_part], both[:, ff_part:]
    sig = jax.nn.sigmoid(gate)
    m = (gate * sig * upward).astype(low)
    down_term = mm_tn(dyb, m).astype(low)
    down_rows = scatter_planes(down_term)
    down_weight, down_term = together(down_weight, down_term)
    d_both = feed_back(dyb, down_weight, both)
    gate_up_term = mm_tn(h2, d_both).astype(low)
    gate_up_rows = scatter_planes(gate_up_term)
    dh2 = team_sum([d_both], [gate_up_weight], 7, [gate_up_term, down_term])
    mid_grad, gain_two = rms_back(dh2, r, inverse_two, norm_gains[1])
    dr = outer_grad + mid_grad
    drb = team_gather(dr.astype(low), 13, [down_rows])

    do = heads(mm(drb, out_weight).astype(low))
    dq, keep, theirs = attention_call(
        attention_back_kernel,
        *attend,
        (do, cos_table, sin_table),
        [("rows", low), ("keys", jnp.float32), ("keys", low)],
        "attention_back",
    )
    dq = dq.reshape(-1, HEAD_SIZE)
    dkv = keep + lax.ppermute(theirs, "c", [(0, 1), (1, 0)]).astype(jnp.float32)
    low_terms = dkv.astype(low)
    feed_sum = team_sum([m], [down_weight], 5, [low_terms])
    down_grad = scatter_team(down_rows, 6, [low_terms])
    layer_output = (r + feed_sum).astype(low)
    local_squares = sum(jnp.sum(jnp.square(part.astype(jnp.float32))) for part in (gate_up_rows, down_rows))
    query_term, out_term = mm_tn(h1, dq).astype(low), mm_tn(drb, o).astype(low)
    low_terms, gate_up_rows, layer_output, down_grad, query_term, out_term = together(
        low_terms, gate_up_rows, layer_output, down_grad, query_term, out_term
    )
    if is_square():
        low_terms = low_terms.reshape(nz, -1, HEAD_SIZE)
        dkv, attention_term, gate_up_grad = fall(low_terms, gate_up_rows, h1, query_term, out_term, *tables, nz, 8)
    else:
        dkv = lax.psum_scatter(low_terms, "z", scatter_dimension=0, tiled=True)[0].astype(jnp.float32)
        dkv = jnp.where(core == 0, rotate(dkv, cos_rows, -sin_rows), dkv).astype(low).reshape(-1, HEAD_SIZE)
        attention_term = jnp.concatenate([query_term, mm_tn(h1, dkv).astype(low), out_term], axis=1)
        gate_up_grad = scatter_team(gate_up_rows, 8)
    attention_rows = scatter_planes(attention_term)
    dh1 = team_sum([dq, dkv], [query_weight, kv_weight], 9, [attention_term])
    in_grad, gain_one = rms_back(dh1, x_in, inverse_one, norm_gains[0])
    input_gradient = dr + in_grad
    gain_local = jnp.stack([gain_one, gain_two]).reshape(-1, 128)
    lines = jnp.concatenate([gain_local, jnp.full((8, 128), local_squares)], axis=0)
    if is_square():
        lines = total_sum(lines, nz, 18)
        attention_grad, tile = turn(attention_rows, 10, (), nz)
    else:
        lines = lax.psum(lines, ALL)
        attention_grad = scatter_team(attention_rows, 10)
        tile = lax.psum(jnp.full((8, 128), jnp.sum(jnp.square(attention_rows.astype(jnp.float32)))), ALL)
    gain_grad = lines[:-8].reshape(2, width)
    news = update(
        (lines, tile, gain_grad),
        (gate_up_grad, down_grad, attention_grad),
        (norm_gains, gain_mean, gain_square),
        (feed_weight, feed_mean, feed_square),
        (attention_weight, attention_mean, attention_square),
    )
    gains_new, gradient_norm, feed_new, attention_new = news[:3], news[3], news[4:8], news[8:]
    return (
        layer_output.reshape(sequences, span, width),
        input_gradient.reshape(sequences, span, width),
        gradient_norm.reshape(()),
        *attention_new,
        *feed_new,
        *gains_new,
    )


def solution(mesh):
    ctx, fsdp = mesh.shape["ctx"], mesh.shape["fsdp"]
    inner = QUERY_HEADS // fsdp
    fine = Mesh(mesh.devices.reshape(ctx // inner, inner, fsdp // 2, 2), ALL)
    act = P(("x", "c"), ("z", "y"), None)
    matrix = P(ALL, None)
    return jax.shard_map(
        local,
        mesh=fine,
        in_specs=(act, P(("x", "c")), P(), matrix, matrix, act, matrix, matrix, matrix, matrix, P(), P()),
        out_specs=(act, act, P(), matrix, matrix, matrix, matrix, matrix, matrix, matrix, matrix, P(), P(), P()),
        check_vma=False,
    )
```

```python
import functools

import jax
import jax.numpy as jnp
from jax import lax
from jax.experimental import pallas as pl
from jax.experimental.pallas import tpu as pltpu
from jax.sharding import Mesh, PartitionSpec as P

QUERY_HEADS = 8
KEY_VALUE_HEADS = 4
HEAD_SIZE = 256
FF = 8192
STEP = 10

norm_eps = 1e-06
rope_base = 1000042.0
masked_value = -1e30
clip_norm = 1.0
beta_one = 0.9
beta_two = 0.95
adam_eps = 1e-08
matrix_rate = 0.03
gain_rate = 0.4
weight_decay = 0.1

TEAM = ("y", "x", "c")
ALL = ("z", "y", "x", "c")


MESH = pl.DeviceIdType.MESH
VMEM = pl.BlockSpec(memory_space=pltpu.VMEM)
HBM = pl.BlockSpec(memory_space=pl.ANY)


def place():
    y, x, c = lax.axis_index("y"), lax.axis_index("x"), lax.axis_index("c")
    return y, x, c, lambda yy, xx, cc: (yy * 2 + xx) * 2 + cc


def greet(others):
    barrier = pltpu.get_barrier_semaphore()
    for other in others:
        pl.semaphore_signal(barrier, inc=1, device_id=other, device_id_type=MESH)
    pl.semaphore_wait(barrier, len(others))


def gather_kernel(src, *refs):
    out, send, recv, own = refs[-4:]
    y, x, c, index = place()
    to_x, to_y, to_s = {"x": 1 - x}, {"y": 1 - y}, {"c": 1 - c}
    me, at_x, at_y, at_d = index(y, x, c), index(y, 1 - x, c), index(1 - y, x, c), index(1 - y, 1 - x, c)
    half = src.shape[0] // 2
    rows = (pl.ds(0, half), pl.ds(half, half))
    local = pltpu.make_async_copy(src, out.at[me], own)
    local.start()
    greet((to_x, to_y, to_s))

    def hop(slot, block, part, where, first=False):
        piece = out.at[block, rows[part]]
        return pltpu.make_async_remote_copy(
            src_ref=src.at[rows[part]] if first else piece,
            dst_ref=piece,
            send_sem=send.at[slot],
            recv_sem=recv.at[slot],
            device_id=where,
            device_id_type=MESH,
        )

    x0, x1 = hop(0, me, 0, to_x, True), hop(1, me, 1, to_x, True)
    y1, y0 = hop(2, me, 1, to_y, True), hop(3, me, 0, to_y, True)
    s0, s1 = hop(4, me, 0, to_s, True), hop(5, me, 1, to_s, True)
    for copy in (x0, y1, x1, y0, s0, s1):
        copy.start()
    x0.wait_recv()
    d0 = hop(6, at_x, 0, to_y)
    d0.start()
    y1.wait_recv()
    d1 = hop(7, at_y, 1, to_x)
    d1.start()
    sx0, sy1 = hop(8, at_x, 0, to_s), hop(9, at_y, 1, to_s)
    sx0.start()
    sy1.start()
    x1.wait_recv()
    sx1 = hop(10, at_x, 1, to_s)
    sx1.start()
    y0.wait_recv()
    sy0 = hop(11, at_y, 0, to_s)
    sy0.start()
    d0.wait_recv()
    sd0 = hop(12, at_d, 0, to_s)
    sd0.start()
    d1.wait_recv()
    sd1 = hop(13, at_d, 1, to_s)
    sd1.start()
    for copy in (s0, s1, sx0, sy1, sx1, sy0, sd0, sd1):
        copy.wait_recv()
    for copy in (x0, x1, y0, y1, s0, s1, d0, d1, sx0, sy1, sx1, sy0, sd0, sd1):
        copy.wait_send()
    local.wait()


def plane_gather(value, number, after=()):
    return pl.pallas_call(
        gather_kernel,
        out_shape=jax.ShapeDtypeStruct((8, *value.shape), value.dtype),
        in_specs=[HBM] * (1 + len(after)),
        out_specs=HBM,
        scratch_shapes=[
            pltpu.SemaphoreType.DMA((14,)),
            pltpu.SemaphoreType.DMA((14,)),
            pltpu.SemaphoreType.DMA,
        ],
        compiler_params=pltpu.CompilerParams(collective_id=number, has_side_effects=True),
        cost_estimate=pl.CostEstimate(flops=1, bytes_accessed=1, transcendentals=0),
        name="plane_gather",
    )(value, *after)


def sum_kernel(lefts, terms, tile, *refs):
    a_refs, w_refs = refs[:lefts], refs[lefts : lefts + len(terms)]
    out, s_send, s_recv, d_send, d_recv, x_send, x_recv, y_send, y_recv, x_acc, y_acc, send, recv = refs[-13:]
    y, x, c, index = place()
    to_x, to_y, to_s = {"x": 1 - x}, {"y": 1 - y}, {"c": 1 - c}
    rows, width = out.shape
    half = rows // 2
    parts = (pl.ds(0, half), pl.ds(half, half))
    f32, low = jnp.float32, jnp.bfloat16

    def product(block, put):
        lines = pl.ds(pl.multiple_of(block * rows, rows), rows)

        @pl.loop(0, width // tile)
        def _(step):
            cols = pl.ds(pl.multiple_of(step * tile, tile), tile)
            total = None
            for (left, start), w_ref in zip(terms, w_refs):
                term = mm_nt(a_refs[left][lines, start : start + w_ref.shape[1]], w_ref[cols, :])
                total = term if total is None else total + term
            put(cols, total)

    def hop(slot, src, dst, where):
        copy = pltpu.make_async_remote_copy(
            src_ref=src, dst_ref=dst, send_sem=send.at[slot], recv_sem=recv.at[slot],
            device_id=where, device_id_type=MESH,
        )
        return copy

    def to_sibling(slot, yy, xx):
        def put(cols, total):
            s_send[slot, :, cols] = total.astype(low)

        product(index(yy, xx, 1 - c), put)
        copy = hop(slot, s_send.at[slot], s_recv.at[slot], to_s)
        copy.start()
        return copy

    def with_sibling(slot, yy, xx, keep):
        def put(cols, total):
            keep[:, cols] = (total + s_recv[slot, :, cols].astype(f32)).astype(keep.dtype)

        product(index(yy, xx, c), put)

    greet((to_x, to_y, to_s))
    s0 = to_sibling(0, 1 - y, 1 - x)
    s1 = to_sibling(1, y, 1 - x)
    s0.wait_recv()
    with_sibling(0, 1 - y, 1 - x, d_send)
    d0 = hop(4, d_send.at[parts[0]], d_recv.at[parts[0]], to_x)
    d1 = hop(5, d_send.at[parts[1]], d_recv.at[parts[1]], to_y)
    d0.start()
    d1.start()
    s1.wait_recv()
    with_sibling(1, y, 1 - x, x_acc)
    x_send[parts[0]] = x_acc[parts[0]].astype(low)
    x0 = hop(6, x_send.at[parts[0]], x_recv.at[parts[0]], to_x)
    x0.start()
    s2 = to_sibling(2, 1 - y, x)
    s2.wait_recv()
    with_sibling(2, 1 - y, x, y_acc)
    y_send[parts[1]] = y_acc[parts[1]].astype(low)
    y1 = hop(7, y_send.at[parts[1]], y_recv.at[parts[1]], to_y)
    y1.start()
    s3 = to_sibling(3, y, x)
    d1.wait_recv()
    x_send[parts[1]] = (x_acc[parts[1]] + d_recv[parts[1]].astype(f32)).astype(low)
    x1 = hop(8, x_send.at[parts[1]], x_recv.at[parts[1]], to_x)
    x1.start()
    d0.wait_recv()
    y_send[parts[0]] = (y_acc[parts[0]] + d_recv[parts[0]].astype(f32)).astype(low)
    y0 = hop(9, y_send.at[parts[0]], y_recv.at[parts[0]], to_y)
    y0.start()
    s3.wait_recv()
    with_sibling(3, y, x, out)
    x0.wait_recv()
    y1.wait_recv()
    x1.wait_recv()
    y0.wait_recv()
    out[...] += x_recv[...].astype(f32) + y_recv[...].astype(f32)
    for copy in (s0, s1, s2, s3, d0, d1, x0, x1, y0, y1):
        copy.wait_send()


def plane_sum(lefts, rights, number, after=(), tile=512):
    ends = [(left, start) for left, a in enumerate(lefts) for start in range(0, a.shape[1], rights[0].shape[1])]
    terms = tuple(ends[: len(rights)])
    rows, width = lefts[0].shape[0] // 8, rights[0].shape[0]
    block = (rows, width)
    low, f32 = jnp.bfloat16, jnp.float32
    return pl.pallas_call(
        functools.partial(sum_kernel, len(lefts), terms, min(tile, width)),
        out_shape=jax.ShapeDtypeStruct(block, f32),
        in_specs=[VMEM] * (len(lefts) + len(rights)) + [HBM] * len(after),
        out_specs=VMEM,
        scratch_shapes=[
            pltpu.VMEM((4, *block), low),
            pltpu.VMEM((4, *block), low),
            *[pltpu.VMEM(block, low)] * 6,
            pltpu.VMEM(block, f32),
            pltpu.VMEM(block, f32),
            pltpu.SemaphoreType.DMA((10,)),
            pltpu.SemaphoreType.DMA((10,)),
        ],
        compiler_params=pltpu.CompilerParams(
            collective_id=number, has_side_effects=True, vmem_limit_bytes=48 * 2**20
        ),
        cost_estimate=pl.CostEstimate(flops=1, bytes_accessed=1, transcendentals=0),
        name="plane_sum",
    )(*lefts, *rights, *after)


def swap_kernel(pieces, takes, *refs):
    count = len(pieces)
    sources, (send, recv, own) = refs[: -2 * count - 3], refs[-3:]
    outs, holds = refs[-2 * count - 3 : -count - 3], refs[-count - 3 : -3]
    y, x, c, index = place()
    me = index(y, x, c)
    flips = [(fy, fx, fc) for fy, fx in ((1, 1), (0, 1), (1, 0), (0, 0)) for fc in (0, 1)]
    flips = [flip for flip in flips if flip != (0, 0, 0)]

    def there(flip):
        return tuple(1 - at if f else at for at, f in zip((y, x, c), flip))

    greet([dict(zip(("y", "x", "c"), there(flip))) for flip in flips])
    copies = []
    for piece in range(count):
        for number, flip in enumerate(flips):
            yy, xx, cc = there(flip)
            member = index(yy, xx, cc)
            holds[piece][number] = takes[piece](sources, member, cc)
            copy = pltpu.make_async_remote_copy(
                src_ref=holds[piece].at[number],
                dst_ref=outs[piece].at[me],
                send_sem=send.at[piece * 7 + number],
                recv_sem=recv.at[piece * 7 + number],
                device_id={"y": yy, "x": xx, "c": cc},
                device_id_type=MESH,
            )
            copy.start()
            copies.append(copy)
        holds[piece][7] = takes[piece](sources, me, c)
        keep = pltpu.make_async_copy(holds[piece].at[7], outs[piece].at[me], own.at[piece])
        keep.start()
        copies.append(keep)
    for copy in copies:
        copy.wait()


def plane_swap(sources, shapes, takes, number, after=()):
    low = jnp.bfloat16
    count = len(shapes)
    return pl.pallas_call(
        functools.partial(swap_kernel, shapes, takes),
        out_shape=[jax.ShapeDtypeStruct((8, *shape), low) for shape in shapes],
        in_specs=[VMEM] * len(sources) + [HBM] * len(after),
        out_specs=[HBM] * count,
        scratch_shapes=[
            *[pltpu.VMEM((8, *shape), low) for shape in shapes],
            pltpu.SemaphoreType.DMA((7 * count,)),
            pltpu.SemaphoreType.DMA((7 * count,)),
            pltpu.SemaphoreType.DMA((count,)),
        ],
        compiler_params=pltpu.CompilerParams(
            collective_id=number, has_side_effects=True, vmem_limit_bytes=48 * 2**20
        ),
        cost_estimate=pl.CostEstimate(flops=1, bytes_accessed=1, transcendentals=0),
        name="plane_swap",
    )(*sources, *after)


def team_of(y, x, c):
    flips = [(fy, fx, fc) for fy, fx in ((1, 1), (0, 1), (1, 0), (0, 0)) for fc in (0, 1)]
    return [
        tuple(1 - at if f else at for at, f in zip((y, x, c), flip)) for flip in flips if flip != (0, 0, 0)
    ]


def turn_kernel(planes, src, *refs):
    y, x, c, index = place()
    me = index(y, x, c)
    others = team_of(y, x, c)
    ids = [dict(zip(("y", "x", "c"), other)) for other in others]
    if planes:
        out, total, near, far, held, send, recv, own, send_lines, recv_lines = refs[-10:]
        z = lax.axis_index("z")
        column = [{"z": lax.rem(z + step, planes)} for step in range(1, planes)]
        fetch = pltpu.make_async_copy(src, held, own)
        fetch.start()
        fetch.wait()
        squares = jnp.zeros((8, held.shape[1]), jnp.float32)
        for start in range(0, held.shape[0], 64):
            part = held[start : start + 64].astype(jnp.float32)
            squares += jnp.sum(jnp.square(part).reshape(8, 8, -1), axis=0)
        near[me] = jnp.broadcast_to(jnp.sum(squares, keepdims=True), near.shape[1:])
    else:
        out, send, recv, own = refs[-4:]
        column = []
    greet(ids + column)
    count = src.shape[0] // 8

    def rows(member):
        return src.at[pl.ds(pl.multiple_of(member * count, count), count)]

    def spread(buffer, at, where, base):
        copies = [
            pltpu.make_async_remote_copy(
                src_ref=buffer.at[at],
                dst_ref=buffer.at[at],
                send_sem=send_lines.at[base + number],
                recv_sem=recv_lines.at[base + number],
                device_id=other,
                device_id_type=MESH,
            )
            for number, other in enumerate(where)
        ]
        for copy in copies:
            copy.start()
        return copies

    small = spread(near, me, ids, 0) if planes else []
    copies = [
        pltpu.make_async_remote_copy(
            src_ref=rows(index(*other)),
            dst_ref=out.at[me],
            send_sem=send.at[number],
            recv_sem=recv.at[number],
            device_id=where,
            device_id_type=MESH,
        )
        for number, (other, where) in enumerate(zip(others, ids))
    ]
    copies.append(pltpu.make_async_copy(rows(me), out.at[me], own))
    for copy in copies:
        copy.start()
    if planes:
        for copy in small:
            copy.wait()
        far[z] = jnp.sum(near[...], axis=0)
        for copy in spread(far, z, column, 7):
            copy.wait()
        total[...] = jnp.sum(far[...], axis=0)
    for copy in copies:
        copy.wait()


def total_kernel(planes, src, *refs):
    out, near, far, send, recv = refs[-5:]
    y, x, c, index = place()
    z = lax.axis_index("z")
    ids = [dict(zip(("y", "x", "c"), other)) for other in team_of(y, x, c)]
    column = [{"z": lax.rem(z + step, planes)} for step in range(1, planes)]
    me = index(y, x, c)
    near[me] = src[...]
    greet(ids + column)

    def spread(buffer, at, where, base):
        copies = [
            pltpu.make_async_remote_copy(
                src_ref=buffer.at[at],
                dst_ref=buffer.at[at],
                send_sem=send.at[base + number],
                recv_sem=recv.at[base + number],
                device_id=other,
                device_id_type=MESH,
            )
            for number, other in enumerate(where)
        ]
        for copy in copies:
            copy.start()
        for copy in copies:
            copy.wait()

    spread(near, me, ids, 0)
    far[z] = jnp.sum(near[...], axis=0)
    spread(far, z, column, 7)
    out[...] = jnp.sum(far[...], axis=0)


def total_sum(value, planes, number, after=()):
    return pl.pallas_call(
        functools.partial(total_kernel, planes),
        out_shape=jax.ShapeDtypeStruct(value.shape, value.dtype),
        in_specs=[VMEM] + [HBM] * len(after),
        out_specs=VMEM,
        scratch_shapes=[pltpu.VMEM((size, *value.shape), value.dtype) for size in (8, planes)]
        + [pltpu.SemaphoreType.DMA((6 + planes,))] * 2,
        compiler_params=pltpu.CompilerParams(
            collective_id=number, has_side_effects=True, vmem_limit_bytes=16 * 2**20
        ),
        cost_estimate=pl.CostEstimate(flops=1, bytes_accessed=1, transcendentals=0),
        name="total_sum",
    )(value, *after)


def turn(rows, number, after=(), planes=0):
    block = (rows.shape[0] // 8, rows.shape[1])
    dma = pltpu.SemaphoreType.DMA
    out_shape, out_specs = [jax.ShapeDtypeStruct((8, *block), rows.dtype)], [HBM]
    scratch = [dma((7,)), dma((7,)), dma]
    if planes:
        tile = jax.ShapeDtypeStruct((8, 128), jnp.float32)
        out_shape.append(tile)
        out_specs.append(VMEM)
        buffers = [pltpu.VMEM((size, *tile.shape), tile.dtype) for size in (8, planes)]
        scratch = buffers + [pltpu.VMEM(rows.shape, rows.dtype)] + scratch + [dma((6 + planes,)), dma((6 + planes,))]
    return pl.pallas_call(
        functools.partial(turn_kernel, planes),
        out_shape=out_shape,
        in_specs=[HBM] * (1 + len(after)),
        out_specs=out_specs,
        scratch_shapes=scratch,
        compiler_params=pltpu.CompilerParams(
            collective_id=number, has_side_effects=True, vmem_limit_bytes=56 * 2**20
        ),
        cost_estimate=pl.CostEstimate(flops=1, bytes_accessed=1, transcendentals=0),
        name="turn",
    )(rows, *after)


def hops(planes, send, recv, block, up):
    z = lax.axis_index("z")

    def step(number):
        gone, came = (z - number + 1, z - number) if up else (z + number - 1, z + number)
        goes = ((gone >= 0) & (z + 1 < planes)) if up else ((gone < planes) & (z >= 1))
        comes = (came >= 0) if up else (came < planes)

        def copy(b):
            return pltpu.make_async_remote_copy(
                src_ref=block(b),
                dst_ref=block(b),
                send_sem=send.at[number - 1],
                recv_sem=recv.at[number - 1],
                device_id={"z": z + 1 if up else z - 1},
                device_id_type=MESH,
            )

        return (
            lambda: pl.when(goes)(lambda: copy(gone).start()),
            lambda: pl.when(comes)(lambda: copy(came).wait_recv()),
            lambda: pl.when(goes)(lambda: copy(gone).wait_send()),
        )

    return [step(number) for number in range(1, planes)]


def ring(planes):
    z = lax.axis_index("z")
    return [{"z": lax.rem(z + 1, planes)}, {"z": lax.rem(z + planes - 1, planes)}]


def spread_to(others, ids, source, take, hold, place_of, send, recv, own):
    y, x, c, index = place()
    me = index(y, x, c)
    copies = []
    for number, (other, where) in enumerate(zip(others, ids)):
        hold[number] = take([source], index(*other), other[2])
        copy = pltpu.make_async_remote_copy(
            src_ref=hold.at[number], dst_ref=place_of(me), send_sem=send.at[number], recv_sem=recv.at[number],
            device_id=where, device_id_type=MESH,
        )
        copy.start()
        copies.append(copy)
    hold[7] = take([source], me, c)
    keep = pltpu.make_async_copy(hold.at[7], place_of(me), own)
    keep.start()
    return copies, keep


def begin_kernel(
    planes, take, take_feed, attention, feed, tokens_from, gain, all_attention, all_rows, columns,
    tokens, held, hold, feed_held, feed_hold, rows, a_send, a_recv, f_send, f_recv, r_send, r_recv, u_send, u_recv, d_send, d_recv, own,
):
    y, x, c, index = place()
    z = lax.axis_index("z")
    me, at_x, at_y, at_d = index(y, x, c), index(y, 1 - x, c), index(1 - y, x, c), index(1 - y, 1 - x, c)
    others = team_of(y, x, c)
    ids = [dict(zip(("y", "x", "c"), other)) for other in others]
    to_x, to_y, to_s = {"x": 1 - x}, {"y": 1 - y}, {"c": 1 - c}
    count = held.shape[0]
    half = rows.shape[0] // 2
    parts = (pl.ds(0, half), pl.ds(half, half))
    fetch = pltpu.make_async_copy(attention, held, own.at[0])
    fetch.start()
    fetch_tokens = pltpu.make_async_copy(tokens_from, tokens, own.at[5])
    fetch_tokens.start()
    fetch_feed = pltpu.make_async_copy(feed.at[:, pl.ds(0, feed_held.shape[1])], feed_held, own.at[3])
    fetch_feed.start()
    greet(ids + ring(planes))
    fetch.wait()

    def attention_rows(start, size):
        return all_attention.at[pl.ds(pl.multiple_of(start, count), size)]

    a_copies, a_keep = spread_to(
        others, ids, held, take, hold, lambda m: attention_rows((z * 8 + m) * count, count), a_send, a_recv, own.at[1]
    )

    def hop(slot, block, part, where, first=False):
        piece = all_rows.at[block, parts[part]]
        copy = pltpu.make_async_remote_copy(
            src_ref=rows.at[parts[part]] if first else piece, dst_ref=piece,
            send_sem=r_send.at[slot], recv_sem=r_recv.at[slot], device_id=where, device_id_type=MESH,
        )
        copy.start()
        return copy

    for copy in a_copies:
        copy.wait_recv()
    a_keep.wait()

    def plane_block(b):
        return attention_rows(b * 8 * count, 8 * count)

    up = hops(planes, u_send, u_recv, plane_block, True)
    down = hops(planes, d_send, d_recv, plane_block, False)

    def pass_on(number):
        if number > 0:
            up[number - 1][1]()
            down[number - 1][1]()
        if number < planes - 1:
            up[number][0]()
            down[number][0]()

    pass_on(0)
    fetch_tokens.wait()

    @pl.loop(0, rows.shape[0] // 16)
    def _(group):
        lines = pl.ds(pl.multiple_of(group * 16, 16), 16)
        rows[lines] = rms_forward(tokens[lines].astype(jnp.float32), gain[...])[0].astype(rows.dtype)

    x0, y1 = hop(0, me, 0, to_x, True), hop(2, me, 1, to_y, True)
    x1, y0 = hop(1, me, 1, to_x, True), hop(3, me, 0, to_y, True)
    s0, s1 = hop(4, me, 0, to_s, True), hop(5, me, 1, to_s, True)
    mine = pltpu.make_async_copy(rows, all_rows.at[me], own.at[2])
    mine.start()
    x0.wait_recv()
    d0 = hop(6, at_x, 0, to_y)
    y1.wait_recv()
    d1 = hop(7, at_y, 1, to_x)
    sx0, sy1 = hop(8, at_x, 0, to_s), hop(9, at_y, 1, to_s)
    fetch_feed.wait()
    f_copies, f_keep = spread_to(
        others, ids, feed_held, take_feed, feed_hold, lambda m: columns.at[m], f_send, f_recv, own.at[4]
    )
    pass_on(1)
    x1.wait_recv()
    sx1 = hop(10, at_x, 1, to_s)
    y0.wait_recv()
    sy0 = hop(11, at_y, 0, to_s)
    pass_on(2)
    d0.wait_recv()
    sd0 = hop(12, at_d, 0, to_s)
    d1.wait_recv()
    sd1 = hop(13, at_d, 1, to_s)
    for number in range(3, planes):
        pass_on(number)
    for copy in (s0, s1, sx0, sy1, sx1, sy0, sd0, sd1, *f_copies):
        copy.wait_recv()
    for copy in (x0, x1, y0, y1, s0, s1, d0, d1, sx0, sy1, sx1, sy0, sd0, sd1, *a_copies, *f_copies):
        copy.wait_send()
    for step in up + down:
        step[2]()
    mine.wait()
    f_keep.wait()


def begin(attention, feed, tokens, gain, takes, widths, planes, number):
    low, dma = jnp.bfloat16, pltpu.SemaphoreType.DMA
    count = attention.shape[0]
    return pl.pallas_call(
        functools.partial(begin_kernel, planes, *takes),
        out_shape=[
            jax.ShapeDtypeStruct((planes * 8 * count, widths[0]), low),
            jax.ShapeDtypeStruct((8, *tokens.shape), low),
            jax.ShapeDtypeStruct((8, count, widths[1]), low),
        ],
        in_specs=[HBM, HBM, HBM, VMEM],
        out_specs=[HBM] * 3,
        scratch_shapes=[
            pltpu.VMEM(tokens.shape, tokens.dtype),
            pltpu.VMEM(attention.shape, attention.dtype),
            pltpu.VMEM((8, count, widths[0]), low),
            pltpu.VMEM((count, 8 * widths[1]), feed.dtype),
            pltpu.VMEM((8, count, widths[1]), low),
            pltpu.VMEM(tokens.shape, low),
            *[dma((size,)) for size in (7, 7, 7, 7, 14, 14, *[planes - 1] * 4, 6)],
        ],
        compiler_params=pltpu.CompilerParams(
            collective_id=number, has_side_effects=True, vmem_limit_bytes=54 * 2**20
        ),
        cost_estimate=pl.CostEstimate(flops=1, bytes_accessed=1, transcendentals=0),
        name="begin",
    )(attention, feed, tokens, gain)


def turned(value, cos_table, sin_table):
    half = value.shape[1] // 2
    first, second = value[:, :half], value[:, half:]
    return jnp.concatenate([first * cos_table - second * sin_table, second * cos_table + first * sin_table], axis=1)


def climb_kernel(
    planes, rows, weights, cos, sin, mine, other, weight, held, zeros, stay, u_send, u_recv, s_send, s_recv, own, fill, move
):
    z, c = lax.axis_index("z"), lax.axis_index("c")
    to_s = {"c": 1 - c}
    barrier = pltpu.get_barrier_semaphore()
    for where in [to_s] + ring(planes):
        pl.semaphore_signal(barrier, inc=1, device_id=where, device_id_type=MESH)
    count, (sides, span) = rows.shape[0], cos.shape[:2]
    size = 512
    pull_weight = pltpu.make_async_copy(
        weights.at[:, pl.ds(weight.shape[1], weight.shape[1])], weight, move.at[count // size]
    )
    pull_weight.start()
    pulls = [
        pltpu.make_async_copy(rows.at[pl.ds(start, size)], held.at[pl.ds(start, size)], move.at[start // size])
        for start in range(0, count, size)
    ]
    for copy in pulls:
        copy.start()
    pull_weight.wait()
    for start in range(0, count, size):
        pulls[start // size].wait()
        value = mm(held[start : start + size], weight[...])
        for line in range(0, size, span):
            side = (start + line) // (count // sides)
            part = value[line : line + span]
            part = jnp.where(c == 0, turned(part, cos[side], sin[side]), part)
            stay[start + line : start + line + span] = part.astype(stay.dtype)
    zeros[...] = jnp.zeros_like(zeros)
    pl.semaphore_wait(barrier, 3)

    def across(n):
        return pltpu.make_async_remote_copy(
            src_ref=stay if n == 0 else mine.at[n], dst_ref=other.at[n], send_sem=s_send.at[n], recv_sem=s_recv.at[n],
            device_id=to_s, device_id_type=MESH,
        )

    def along(n):
        return pltpu.make_async_remote_copy(
            src_ref=stay if n == 1 else mine.at[n - 1], dst_ref=mine.at[n], send_sem=u_send.at[n - 1], recv_sem=u_recv.at[n - 1],
            device_id={"z": z + 1}, device_id_type=MESH,
        )

    def fills(n):
        return [
            pltpu.make_async_copy(zeros, buffer.at[n], fill.at[2 * (n - 1) + number])
            for number, buffer in enumerate((mine, other))
        ]

    keep = pltpu.make_async_copy(stay, mine.at[0], own)
    more = z + 1 < planes
    pl.when(more)(lambda: along(1).start())
    across(0).start()
    keep.start()
    for n in range(1, planes):

        @pl.when(z < n)
        def _():
            for copy in fills(n):
                copy.start()

    for n in range(1, planes):

        @pl.when(z >= n)
        def _():
            along(n).wait_recv()
            if n + 1 < planes:
                pl.when(more)(lambda: along(n + 1).start())
            across(n).start()

    across(0).wait()
    keep.wait()
    for n in range(1, planes):

        @pl.when(z >= n)
        def _():
            across(n).wait()

        @pl.when(z < n)
        def _():
            for copy in fills(n):
                copy.wait()

        pl.when((z >= n - 1) & more)(lambda: along(n).wait_send())


def climb(rows, weights, cos, sin, planes, number):
    dma = pltpu.SemaphoreType.DMA
    block = (rows.shape[0], weights.shape[1] // 3)
    blocks = jax.ShapeDtypeStruct((planes, *block), rows.dtype)
    return pl.pallas_call(
        functools.partial(climb_kernel, planes),
        out_shape=[blocks, blocks],
        in_specs=[HBM] * 2 + [VMEM] * 2,
        out_specs=[HBM] * 2,
        scratch_shapes=[
            pltpu.VMEM((weights.shape[0], block[1]), rows.dtype),
            pltpu.VMEM(rows.shape, rows.dtype),
            pltpu.VMEM(block, rows.dtype),
            pltpu.VMEM(block, rows.dtype),
            *[dma((size,)) for size in (planes - 1, planes - 1, planes, planes)],
            dma,
            dma((2 * (planes - 1),)),
            dma((rows.shape[0] // 512 + 1,)),
        ],
        compiler_params=pltpu.CompilerParams(
            collective_id=number, has_side_effects=True, vmem_limit_bytes=56 * 2**20
        ),
        cost_estimate=pl.CostEstimate(flops=1, bytes_accessed=1, transcendentals=0),
        name="climb",
    )(rows, weights, cos, sin)


def fall_kernel(
    planes, terms_from, rows, left_from, query_term, out_term, cos, sin, value, term, blocks,
    terms, left, sends, recvs, total, held, send, recv, t_send, t_recv, own, move, fetch,
):
    y, x, c, index = place()
    z = lax.axis_index("z")
    me = index(y, x, c)
    others = team_of(y, x, c)
    ids = [dict(zip(("y", "x", "c"), other)) for other in others]
    f32 = jnp.float32
    count = rows.shape[0] // 8
    size = terms.shape[2]
    given = ((query_term, 0), (out_term, 2))
    pulls = [pltpu.make_async_copy(ref, held.at[n], move.at[n]) for n, (ref, _) in enumerate(given)]
    get_terms = pltpu.make_async_copy(terms_from, terms, fetch.at[0])
    get_terms.start()
    get_left = pltpu.make_async_copy(left_from, left, fetch.at[1])
    get_left.start()
    for copy in pulls:
        copy.start()
    greet(ids + ring(planes))
    get_terms.wait()

    def rows_of(member):
        return rows.at[pl.ds(pl.multiple_of(member * count, count), count)]

    def hop(step):
        return pltpu.make_async_remote_copy(
            src_ref=sends.at[step - 1], dst_ref=recvs.at[step - 1], send_sem=send.at[step - 1], recv_sem=recv.at[step - 1],
            device_id={"z": z - 1}, device_id_type=MESH,
        )

    def came(step):
        return (z + 1 < planes) & (z + 1 + step - planes >= 0)

    copies = [
        pltpu.make_async_remote_copy(
            src_ref=rows_of(index(*other)), dst_ref=blocks.at[me], send_sem=t_send.at[number], recv_sem=t_recv.at[number],
            device_id=where, device_id_type=MESH,
        )
        for number, (other, where) in enumerate(zip(others, ids))
    ]
    copies.append(pltpu.make_async_copy(rows_of(me), blocks.at[me], own))
    pushes = []
    for step in range(1, planes):
        block = z + step - planes
        if step > 1:
            pl.when(came(step - 1))(lambda: hop(step - 1).wait_recv())

        @pl.when((block >= 0) & (z + 1 == planes))
        def _():
            sends[step - 1] = terms[block]

        if step > 1:

            @pl.when((block >= 0) & (z + 1 < planes))
            def _():
                sends[step - 1] = (terms[block].astype(f32) + recvs[step - 2].astype(f32)).astype(terms.dtype)

        pl.when(block >= 0)(lambda: hop(step).start())
        if step == 1:
            for copy in copies:
                copy.start()
            total[...] = terms[z].astype(f32)
            for n, (_, column) in enumerate(given):
                pulls[n].wait()
                pushes.append(
                    pltpu.make_async_copy(held.at[n], term.at[:, pl.ds(column * size, size)], move.at[2 + n])
                )
                pushes[-1].start()
    last = planes - 1

    @pl.when(came(last))
    def _():
        hop(last).wait_recv()
        total[...] += recvs[last - 1].astype(f32)

    sides, span = cos.shape[:2]
    for line in range(0, total.shape[0], span):
        side = line // (total.shape[0] // sides)
        part = total[line : line + span]
        part = jnp.where(c == 0, turned(part, cos[side], -sin[side]), part)
        value[line : line + span] = part.astype(value.dtype)
    get_left.wait()
    upright = value[...].astype(f32).T.astype(value.dtype)
    for start in range(0, left.shape[1], 512):
        lines = pl.ds(start, 512)
        held[2, lines] = mm(upright, left[:, start : start + 512]).T.astype(held.dtype)
        pushes.append(
            pltpu.make_async_copy(
                held.at[2, lines], term.at[lines, pl.ds(size, size)], move.at[4 + start // 512]
            )
        )
        pushes[-1].start()
    for step in range(1, planes):
        pl.when(z + step - planes >= 0)(lambda: hop(step).wait_send())
    for copy in copies + pushes:
        copy.wait()


def fall(terms, rows, left, query_term, out_term, cos, sin, planes, number):
    block = terms.shape[1:]
    dma, low = pltpu.SemaphoreType.DMA, terms.dtype
    return pl.pallas_call(
        functools.partial(fall_kernel, planes),
        out_shape=[
            jax.ShapeDtypeStruct(block, low),
            jax.ShapeDtypeStruct((left.shape[1], 3 * block[1]), low),
            jax.ShapeDtypeStruct((8, rows.shape[0] // 8, rows.shape[1]), low),
        ],
        in_specs=[HBM] * 5 + [VMEM] * 2,
        out_specs=[VMEM, HBM, HBM],
        scratch_shapes=[pltpu.VMEM(terms.shape, low), pltpu.VMEM(left.shape, low)]
        + [pltpu.VMEM((planes - 1, *block), low)] * 2
        + [pltpu.VMEM(block, jnp.float32), pltpu.VMEM((3, left.shape[1], block[1]), low)]
        + [dma((planes - 1,))] * 2
        + [dma((7,)), dma((7,)), dma, dma((4 + left.shape[1] // 512,)), dma((2,))],
        compiler_params=pltpu.CompilerParams(
            collective_id=number, has_side_effects=True, vmem_limit_bytes=56 * 2**20
        ),
        cost_estimate=pl.CostEstimate(flops=1, bytes_accessed=1, transcendentals=0),
        name="fall",
    )(terms, rows, left, query_term, out_term, cos, sin)


def dot(left, right, contract):
    return lax.dot_general(left, right, (contract, ((), ())), preferred_element_type=jnp.float32)


def mm(left, right):
    return dot(left, right, ((1,), (0,)))


def mm_nt(left, right):
    return dot(left, right, ((1,), (1,)))


def mm_tn(left, right):
    return dot(left, right, ((0,), (0,)))


def bmm(pattern, left, right):
    return jnp.einsum(pattern, left, right, preferred_element_type=jnp.float32)


def angle_tables(positions):
    half_dim = HEAD_SIZE // 2
    frequency = rope_base ** (-(jnp.arange(half_dim).astype(jnp.float32) * 2.0) / HEAD_SIZE)
    phases = positions.astype(jnp.float32)[:, None] * frequency[None, :]
    return (jnp.cos(phases), jnp.sin(phases))


def rotate(value, cos_table, sin_table):
    half = value.shape[-1] // 2
    a, b = value[..., :half], value[..., half:]
    return jnp.concatenate([a * cos_table - b * sin_table, b * cos_table + a * sin_table], axis=-1)


def rms_forward(value, gain_row):
    inverse = lax.rsqrt(jnp.mean(value * value, axis=-1, keepdims=True) + norm_eps)
    return (value * inverse * gain_row, inverse)


def rms_back(grad_out, value, inverse, gain_row):
    scaled = grad_out * gain_row
    grad_in = inverse * (
        scaled - value * inverse * inverse * jnp.mean(scaled * value, axis=-1, keepdims=True)
    )
    return (grad_in, jnp.sum(grad_out * value * inverse, axis=0))


def adamw(weight, gradient, moment_one, moment_two, step_rate, decay_rate, invert=jnp.reciprocal):
    mean_new = beta_one * moment_one + (1.0 - beta_one) * gradient
    square_new = beta_two * moment_two + (1.0 - beta_two) * gradient * gradient
    below = jnp.sqrt(square_new * (1.0 / (1.0 - beta_two**STEP))) + adam_eps
    direction = mean_new * (1.0 / (1.0 - beta_one**STEP)) * invert(below)
    return (weight - step_rate * (direction + decay_rate * weight), mean_new, square_new)


def attention_parts(core, length, q_ref, mine_ref, other_ref, query_ref, key_ref):
    mine, other = mine_ref[...].reshape(-1, HEAD_SIZE), other_ref[...].reshape(-1, HEAD_SIZE)
    first = core == 0
    k, v = jnp.where(first, mine, other), jnp.where(first, other, mine)
    q = q_ref[...].reshape(-1, HEAD_SIZE)
    at, key_at = query_ref[...], key_ref[...]
    allowed = (key_at <= at) & (key_at < length) & (key_at >= 0)
    scores = jnp.where(allowed, mm_nt(q, k) * HEAD_SIZE ** (-0.5), masked_value)
    exponent = jnp.exp(scores - jnp.max(scores, axis=-1, keepdims=True))
    return q, k, v, exponent / jnp.sum(exponent, axis=-1, keepdims=True)


def attention_kernel(core_ref, length_ref, q_ref, mine_ref, other_ref, query_ref, key_ref, out_ref):
    length = length_ref[pl.program_id(0)]
    _, _, v, soft = attention_parts(core_ref[0], length, q_ref, mine_ref, other_ref, query_ref, key_ref)
    out_ref[...] = mm(soft.astype(jnp.bfloat16), v).astype(jnp.bfloat16).reshape(out_ref.shape)


def attention_back_kernel(
    core_ref, length_ref, q_ref, mine_ref, other_ref, query_ref, key_ref, do_ref, cos_ref, sin_ref,
    dq_ref, keep_ref, send_ref,
):
    low = jnp.bfloat16
    core = core_ref[0]
    length = length_ref[pl.program_id(0)]
    q, k, v, soft = attention_parts(core, length, q_ref, mine_ref, other_ref, query_ref, key_ref)
    do = do_ref[...].reshape(-1, HEAD_SIZE)
    dp = mm_nt(do, v)
    delta = jnp.sum(soft * dp, axis=-1, keepdims=True)
    ds = (soft * (dp - delta) * HEAD_SIZE ** (-0.5)).astype(low)
    dq = mm(ds, k)
    cos_table, sin_table = cos_ref[...], sin_ref[...]
    half = HEAD_SIZE // 2
    a, b = dq[:, :half], dq[:, half:]
    turned = jnp.concatenate([a * cos_table + b * sin_table, b * cos_table - a * sin_table], axis=-1)
    dq_ref[...] = turned.astype(low).reshape(dq_ref.shape)
    dk, dv = mm_tn(ds, q), mm_tn(soft.astype(low), do)
    first = core == 0
    keep, send = (t.reshape(keep_ref.shape) for t in (jnp.where(first, dk, dv), jnp.where(first, dv, dk)))
    for block in range(keep_ref.shape[0]):
        at = core_ref[1 + block]
        keep_ref[at] = keep[block]
        send_ref[at] = send[block].astype(low)


def attention_call(kernel, core, lengths, q, mine, other, query_pos, key_pos, extra, outs, name):
    ny, count, span, size = q.shape
    nz = mine.shape[0]
    rows = pl.BlockSpec((ny, 1, span, size), lambda i, *_: (0, i, 0, 0))
    keys = pl.BlockSpec((nz, ny, 1, span, size), lambda i, *_: (0, 0, i, 0, 0))

    def whole(value):
        return pl.BlockSpec(value.shape, lambda i, *_: (0,) * value.ndim)

    kinds = {"rows": (rows, q.shape), "keys": (keys, mine.shape)}
    return pl.pallas_call(
        kernel,
        grid_spec=pltpu.PrefetchScalarGridSpec(
            num_scalar_prefetch=2,
            grid=(count,),
            in_specs=[rows, keys, keys, whole(query_pos), whole(key_pos)]
            + [rows if value.shape == q.shape else whole(value) for value in extra],
            out_specs=[kinds[kind][0] for kind, _ in outs],
        ),
        out_shape=[jax.ShapeDtypeStruct(kinds[kind][1], dtype) for kind, dtype in outs],
        compiler_params=pltpu.CompilerParams(vmem_limit_bytes=48 * 2**20),
        cost_estimate=pl.CostEstimate(flops=1, bytes_accessed=1, transcendentals=0),
        name=name,
    )(core, lengths, q, mine, other, query_pos, key_pos, *extra)


def feed_back_kernel(dyb_ref, weight_ref, gate_ref, up_ref, out_ref):
    dm = mm(dyb_ref[...], weight_ref[...])
    gate, upward = gate_ref[...], up_ref[...]
    sig = jax.nn.sigmoid(gate)
    part = gate.shape[1]
    out_ref[:, :part] = (dm * upward * sig * (1.0 + gate * (1.0 - sig))).astype(out_ref.dtype)
    out_ref[:, part:] = (dm * gate * sig).astype(out_ref.dtype)


def feed_back(dyb, weight, both, lines=256):
    count, part = both.shape[0], both.shape[1] // 2

    def rows(width, column=0):
        return pl.BlockSpec((lines, width), lambda i: (i, column))

    return pl.pallas_call(
        feed_back_kernel,
        grid=(count // lines,),
        in_specs=[rows(dyb.shape[1]), pl.BlockSpec(weight.shape, lambda i: (0, 0)), rows(part), rows(part, 1)],
        out_specs=rows(2 * part),
        out_shape=jax.ShapeDtypeStruct((count, 2 * part), jnp.bfloat16),
        compiler_params=pltpu.CompilerParams(vmem_limit_bytes=48 * 2**20),
        cost_estimate=pl.CostEstimate(flops=1, bytes_accessed=1, transcendentals=0),
        name="feed_back",
    )(dyb, weight, both, both)


def close_reciprocal(value):
    guess = pltpu.reciprocal(value, approx=True)
    return guess * (2.0 - value * guess)


def norm_of(lines_ref, tile_ref):
    gains = lines_ref[:-8]
    return jnp.sqrt(jnp.sum(gains * gains, keepdims=True) + lines_ref[-8:-7, 0:1] + tile_ref[0:1, 0:1])


def update_kernel(*refs):
    lines_ref, tile_ref, gain_ref, gate_up_ref, down_ref, attention_ref = refs[:6]
    gains, feed, attention = refs[6:9], refs[9:12], refs[12:15]
    new_gains, norm_ref, new_feed, new_attention, factor_ref = refs[15:18], refs[18], refs[19:23], refs[23:27], refs[27]
    rows = feed[0].shape[0]
    lines = pl.ds(pl.multiple_of(pl.program_id(0) * rows, rows), rows)

    @pl.when(pl.program_id(0) == 0)
    def _():
        norm = norm_of(lines_ref, tile_ref)
        norm_ref[...] = norm
        factor_ref[...] = clip_norm / norm
        weight, mean, square = (ref[...] for ref in gains)
        gradient = gain_ref[...] * factor_ref[...]
        for ref, value in zip(new_gains, adamw(weight, gradient, mean, square, gain_rate, 0.0)):
            ref[...] = value

    factor = factor_ref[...]

    def piece(olds, news, grad_ref, member, start, column, size):
        at = pl.ds(pl.multiple_of(column, size), size)
        gradient = grad_ref[member, lines, pl.ds(start, size)].astype(jnp.float32) * factor
        weight, mean, square = (ref[:, at] for ref in olds)
        values = adamw(weight, gradient, mean, square, matrix_rate, weight_decay, close_reciprocal)
        for ref, value in zip(news, (*values, values[0])):
            ref[:, at] = value.astype(ref.dtype)

    part = down_ref.shape[2]
    size = min(part, 512)

    @pl.loop(0, 8)
    def _(member):
        for offset in range(0, part, size):
            for number, (grad_ref, start) in enumerate(((gate_up_ref, 0), (gate_up_ref, part), (down_ref, 0))):
                column = (number * 8 + member) * part + offset
                piece(feed, new_feed, grad_ref, member, start + offset, column, size)
        core = lax.rem(member, 2)
        kv_column = (8 + 4 * core + lax.div(member, 2)) * HEAD_SIZE
        for number, column in enumerate((member * HEAD_SIZE, kv_column, (16 + member) * HEAD_SIZE)):
            piece(attention, new_attention, attention_ref, member, number * HEAD_SIZE, column, HEAD_SIZE)


def update(sums, grads, gains, feed, attention):
    f32, low = jnp.float32, jnp.bfloat16
    rows = min(feed[0].shape[0], 16)

    def some(value):
        return pl.BlockSpec((rows, value.shape[1]), lambda i: (i, 0))

    def whole(value):
        return pl.BlockSpec(value.shape, lambda i: (0,) * value.ndim)

    norm = jax.ShapeDtypeStruct((1, 1), f32)
    matrices = [jax.ShapeDtypeStruct(part[0].shape, dtype) for part in (feed, attention) for dtype in (f32, f32, f32, low)]
    return pl.pallas_call(
        update_kernel,
        grid=(feed[0].shape[0] // rows,),
        in_specs=[whole(value) for value in (*sums, *grads, *gains)] + [some(value) for value in (*feed, *attention)],
        out_specs=[whole(value) for value in (*gains, norm)] + [some(value) for value in matrices],
        out_shape=[jax.ShapeDtypeStruct(gains[0].shape, f32)] * 3 + [norm] + matrices,
        scratch_shapes=[pltpu.VMEM((1, 1), f32)],
        compiler_params=pltpu.CompilerParams(vmem_limit_bytes=56 * 2**20),
        name="update",
    )(*sums, *grads, *gains, *feed, *attention)


def is_square():
    return lax.axis_size("y") == 2 and lax.axis_size("x") == 2


def swap(blocks):
    return lax.all_to_all(blocks, TEAM, split_axis=0, concat_axis=0, tiled=True)


def over_planes(blocks):
    return lax.all_gather(blocks.reshape(-1, blocks.shape[-1]), "z", axis=0, tiled=True)


def scatter_planes(term):
    return lax.psum_scatter(term, "z", scatter_dimension=0, tiled=True)


def together(*values):
    return lax.optimization_barrier(values)


def scatter_team(rows, number, after=()):
    if not is_square():
        return swap(rows.reshape(8, -1, rows.shape[-1]))
    return turn(rows, number, after)[0]


def team_gather(local, number, after=()):
    if not is_square():
        return lax.all_gather(local, TEAM, axis=0, tiled=True)
    return plane_gather(local, number, after).reshape(-1, local.shape[1])


def team_sum(lefts, rights, number, after=()):
    if is_square():
        return plane_sum(lefts, rights, number, after)
    partial = mm_nt(jnp.concatenate(lefts, axis=1), jnp.concatenate(rights, axis=1))
    return lax.psum_scatter(partial.astype(jnp.bfloat16), TEAM, scatter_dimension=0, tiled=True).astype(jnp.float32)


def local(
    tokens,
    lengths,
    norm_gains,
    attention_weight,
    feed_weight,
    cotangent,
    attention_mean,
    attention_square,
    feed_mean,
    feed_square,
    gain_mean,
    gain_square,
):
    low = jnp.bfloat16
    sequences, span, width = tokens.shape
    ny, nx, nz = lax.axis_size("y"), lax.axis_size("x"), lax.axis_size("z")
    team = ny * nx * 2
    core = lax.axis_index("c")
    rows = attention_weight.shape[0]
    q_width, kv_width = QUERY_HEADS * HEAD_SIZE, KEY_VALUE_HEADS * HEAD_SIZE
    count = sequences * span
    all_sequences = nx * 2 * sequences
    reach = ny * span
    near = is_square()
    ff_part = FF // team

    def columns(start, size):
        return pl.ds(pl.multiple_of(start, size), size)

    def take_attention(sources, member, c):
        source = sources[0]
        starts = (
            member * HEAD_SIZE,
            q_width + c * kv_width + (member - c) // 2 * HEAD_SIZE,
            q_width + 2 * kv_width + member * HEAD_SIZE,
        )
        return jnp.concatenate([source[:, columns(s, HEAD_SIZE)].astype(low) for s in starts], axis=1)

    def take_feed(*parts):
        return lambda sources, member, c: jnp.concatenate(
            [sources[0][:, columns(part * FF + member * ff_part, ff_part)].astype(low) for part in parts], axis=1
        )

    def spread(source, take, size, number, after=()):
        if is_square():
            blocks = plane_swap([source], [(rows, size)], [take], number, after)[0]
        else:
            blocks = swap(jnp.stack([take([source], member, member % 2) for member in range(8)]))
        return blocks, over_planes(blocks)

    team_base = lax.axis_index("z") * reach
    team_pos = team_base + jnp.arange(reach, dtype=jnp.int32)
    own_pos = team_base + lax.axis_index("y") * span + jnp.arange(span, dtype=jnp.int32)
    if near:
        key_pos = jnp.concatenate([team_pos - back * reach for back in range(nz)])
    else:
        key_pos = jnp.arange(nz * reach, dtype=jnp.int32)
    query_at, key_at = team_pos[:, None], key_pos[None, :]
    cos_table, sin_table = angle_tables(team_pos)
    cos_rows, sin_rows = (t.reshape(ny, 1, span, -1) for t in (cos_table, sin_table))
    valid = (own_pos[None, :] < lengths[:, None]).astype(jnp.float32).reshape(count, 1)
    lengths_all = lax.all_gather(lengths, ("x", "c"), axis=0, tiled=True)
    planes = jnp.arange(nz, dtype=jnp.int32)
    if near:
        planes = (lax.axis_index("z") - planes) % nz
    core_at = jnp.concatenate([jnp.reshape(core, (1,)), planes]).astype(jnp.int32)

    def heads(value):
        return value.reshape(ny, all_sequences, span, HEAD_SIZE)

    x_in = tokens.reshape(count, width).astype(jnp.float32)
    normed_one, inverse_one = rms_forward(x_in, norm_gains[0])
    outer_grad = cotangent.reshape(count, width).astype(jnp.float32) * valid
    if is_square():
        attention_mine, h1, gate_up_blocks = begin(
            attention_weight,
            feed_weight,
            tokens.reshape(count, width),
            norm_gains[:1],
            (take_attention, take_feed(0, 1)),
            (3 * HEAD_SIZE, 2 * ff_part),
            nz,
            1,
        )
        h1 = h1.reshape(-1, width)
    else:
        attention_mine = spread(attention_weight, take_attention, 3 * HEAD_SIZE, 1)[1]
        gate_up_blocks, gate_up_weight = spread(feed_weight, take_feed(0, 1), 2 * ff_part, 2)
        h1 = team_gather(normed_one.astype(low), 3)
    query_weight = attention_mine[:, :HEAD_SIZE]
    kv_weight = attention_mine[:, HEAD_SIZE : 2 * HEAD_SIZE]
    out_weight = attention_mine[:, 2 * HEAD_SIZE :]
    tables = [t.reshape(ny, span, -1) for t in (cos_table, sin_table)]
    if is_square():
        kv, other = climb(h1, attention_mine, *tables, nz, 2)
        kv, other = (t.reshape(nz, ny, all_sequences, span, HEAD_SIZE) for t in (kv, other))
        gate_up_blocks, kv = together(gate_up_blocks, kv)
        gate_up_weight = over_planes(gate_up_blocks)
    else:
        kv_raw = heads(mm(h1, kv_weight))
        kv = jnp.where(core == 0, rotate(kv_raw, cos_rows, sin_rows), kv_raw).astype(low)
        kv = lax.all_gather(kv, "z", axis=0, tiled=False)
        other = lax.ppermute(kv, "c", [(0, 1), (1, 0)])
    q = rotate(heads(mm(h1, query_weight)), cos_rows, sin_rows).astype(low)
    attend = (core_at, lengths_all, q, kv, other, query_at, key_at)
    (o,) = attention_call(attention_kernel, *attend, (), [("rows", low)], "attention")
    o = o.reshape(-1, HEAD_SIZE)
    r = x_in + team_sum([o], [out_weight], 4)

    normed_two, inverse_two = rms_forward(r, norm_gains[1])
    h2 = team_gather(normed_two.astype(low), 16)
    dyb = team_gather(outer_grad.astype(low), 15, [h2])
    down_blocks, down_weight = spread(feed_weight, take_feed(2), ff_part, 12, [dyb])
    gate_up_weight, down_blocks = together(gate_up_weight, down_blocks)
    both = mm(h2, gate_up_weight)
    gate, upward = both[:, :ff_part], both[:, ff_part:]
    sig = jax.nn.sigmoid(gate)
    m = (gate * sig * upward).astype(low)
    down_term = mm_tn(dyb, m).astype(low)
    down_rows = scatter_planes(down_term)
    down_weight, down_term = together(down_weight, down_term)
    d_both = feed_back(dyb, down_weight, both)
    gate_up_term = mm_tn(h2, d_both).astype(low)
    gate_up_rows = scatter_planes(gate_up_term)
    dh2 = team_sum([d_both], [gate_up_weight], 7, [gate_up_term, down_term])
    mid_grad, gain_two = rms_back(dh2, r, inverse_two, norm_gains[1])
    dr = outer_grad + mid_grad
    drb = team_gather(dr.astype(low), 13, [down_rows])

    do = heads(mm(drb, out_weight).astype(low))
    dq, keep, theirs = attention_call(
        attention_back_kernel,
        *attend,
        (do, cos_table, sin_table),
        [("rows", low), ("keys", jnp.float32), ("keys", low)],
        "attention_back",
    )
    dq = dq.reshape(-1, HEAD_SIZE)
    dkv = keep + lax.ppermute(theirs, "c", [(0, 1), (1, 0)]).astype(jnp.float32)
    low_terms = dkv.astype(low)
    feed_sum = team_sum([m], [down_weight], 5, [low_terms])
    down_grad = scatter_team(down_rows, 6, [low_terms])
    layer_output = (r + feed_sum).astype(low)
    local_squares = sum(jnp.sum(jnp.square(part.astype(jnp.float32))) for part in (gate_up_rows, down_rows))
    query_term, out_term = mm_tn(h1, dq).astype(low), mm_tn(drb, o).astype(low)
    low_terms, gate_up_rows, layer_output, down_grad, query_term, out_term = together(
        low_terms, gate_up_rows, layer_output, down_grad, query_term, out_term
    )
    if is_square():
        low_terms = low_terms.reshape(nz, -1, HEAD_SIZE)
        dkv, attention_term, gate_up_grad = fall(low_terms, gate_up_rows, h1, query_term, out_term, *tables, nz, 8)
    else:
        dkv = lax.psum_scatter(low_terms, "z", scatter_dimension=0, tiled=True)[0].astype(jnp.float32)
        dkv = jnp.where(core == 0, rotate(dkv, cos_rows, -sin_rows), dkv).astype(low).reshape(-1, HEAD_SIZE)
        attention_term = jnp.concatenate([query_term, mm_tn(h1, dkv).astype(low), out_term], axis=1)
        gate_up_grad = scatter_team(gate_up_rows, 8)
    attention_rows = scatter_planes(attention_term)
    dh1 = team_sum([dq, dkv], [query_weight, kv_weight], 9, [attention_term])
    in_grad, gain_one = rms_back(dh1, x_in, inverse_one, norm_gains[0])
    input_gradient = dr + in_grad
    gain_local = jnp.stack([gain_one, gain_two]).reshape(-1, 128)
    lines = jnp.concatenate([gain_local, jnp.full((8, 128), local_squares)], axis=0)
    if is_square():
        lines = total_sum(lines, nz, 18)
        attention_grad, tile = turn(attention_rows, 10, (), nz)
    else:
        lines = lax.psum(lines, ALL)
        attention_grad = scatter_team(attention_rows, 10)
        tile = lax.psum(jnp.full((8, 128), jnp.sum(jnp.square(attention_rows.astype(jnp.float32)))), ALL)
    gain_grad = lines[:-8].reshape(2, width)
    news = update(
        (lines, tile, gain_grad),
        (gate_up_grad, down_grad, attention_grad),
        (norm_gains, gain_mean, gain_square),
        (feed_weight, feed_mean, feed_square),
        (attention_weight, attention_mean, attention_square),
    )
    gains_new, gradient_norm, feed_new, attention_new = news[:3], news[3], news[4:8], news[8:]
    return (
        layer_output.reshape(sequences, span, width),
        input_gradient.reshape(sequences, span, width),
        gradient_norm.reshape(()),
        *attention_new,
        *feed_new,
        *gains_new,
    )


def solution(mesh):
    ctx, fsdp = mesh.shape["ctx"], mesh.shape["fsdp"]
    inner = QUERY_HEADS // fsdp
    fine = Mesh(mesh.devices.reshape(ctx // inner, inner, fsdp // 2, 2), ALL)
    act = P(("x", "c"), ("z", "y"), None)
    matrix = P(ALL, None)
    return jax.shard_map(
        local,
        mesh=fine,
        in_specs=(act, P(("x", "c")), P(), matrix, matrix, act, matrix, matrix, matrix, matrix, P(), P()),
        out_specs=(act, act, P(), matrix, matrix, matrix, matrix, matrix, matrix, matrix, matrix, P(), P(), P()),
        check_vma=False,
    )
```

```python
import functools

import jax
import jax.numpy as jnp
from jax import lax
from jax.experimental import pallas as pl
from jax.experimental.pallas import tpu as pltpu
from jax.sharding import Mesh, PartitionSpec as P

QUERY_HEADS = 8
KEY_VALUE_HEADS = 4
HEAD_SIZE = 256
FF = 8192
STEP = 10

norm_eps = 1e-06
rope_base = 1000042.0
masked_value = -1e30
clip_norm = 1.0
beta_one = 0.9
beta_two = 0.95
adam_eps = 1e-08
matrix_rate = 0.03
gain_rate = 0.4
weight_decay = 0.1

TEAM = ("y", "x", "c")
ALL = ("z", "y", "x", "c")


MESH = pl.DeviceIdType.MESH
VMEM = pl.BlockSpec(memory_space=pltpu.VMEM)
HBM = pl.BlockSpec(memory_space=pl.ANY)


def place():
    y, x, c = lax.axis_index("y"), lax.axis_index("x"), lax.axis_index("c")
    return y, x, c, lambda yy, xx, cc: (yy * 2 + xx) * 2 + cc


def hail(others):
    barrier = pltpu.get_barrier_semaphore()
    for other in others:
        pl.semaphore_signal(barrier, inc=1, device_id=other, device_id_type=MESH)
    return lambda: pl.semaphore_wait(barrier, len(others))


def greet(others):
    hail(others)()


def gather_kernel(src, *refs):
    out, send, recv, own = refs[-4:]
    y, x, c, index = place()
    to_x, to_y, to_s = {"x": 1 - x}, {"y": 1 - y}, {"c": 1 - c}
    me, at_x, at_y, at_d = index(y, x, c), index(y, 1 - x, c), index(1 - y, x, c), index(1 - y, 1 - x, c)
    half = src.shape[0] // 2
    rows = (pl.ds(0, half), pl.ds(half, half))
    local = pltpu.make_async_copy(src, out.at[me], own)
    local.start()
    greet((to_x, to_y, to_s))

    def hop(slot, block, part, where, first=False):
        piece = out.at[block, rows[part]]
        return pltpu.make_async_remote_copy(
            src_ref=src.at[rows[part]] if first else piece,
            dst_ref=piece,
            send_sem=send.at[slot],
            recv_sem=recv.at[slot],
            device_id=where,
            device_id_type=MESH,
        )

    x0, x1 = hop(0, me, 0, to_x, True), hop(1, me, 1, to_x, True)
    y1, y0 = hop(2, me, 1, to_y, True), hop(3, me, 0, to_y, True)
    s0, s1 = hop(4, me, 0, to_s, True), hop(5, me, 1, to_s, True)
    for copy in (x0, y1, x1, y0, s0, s1):
        copy.start()
    x0.wait_recv()
    d0 = hop(6, at_x, 0, to_y)
    d0.start()
    y1.wait_recv()
    d1 = hop(7, at_y, 1, to_x)
    d1.start()
    sx0, sy1 = hop(8, at_x, 0, to_s), hop(9, at_y, 1, to_s)
    sx0.start()
    sy1.start()
    x1.wait_recv()
    sx1 = hop(10, at_x, 1, to_s)
    sx1.start()
    y0.wait_recv()
    sy0 = hop(11, at_y, 0, to_s)
    sy0.start()
    d0.wait_recv()
    sd0 = hop(12, at_d, 0, to_s)
    sd0.start()
    d1.wait_recv()
    sd1 = hop(13, at_d, 1, to_s)
    sd1.start()
    for copy in (s0, s1, sx0, sy1, sx1, sy0, sd0, sd1):
        copy.wait_recv()
    for copy in (x0, x1, y0, y1, s0, s1, d0, d1, sx0, sy1, sx1, sy0, sd0, sd1):
        copy.wait_send()
    local.wait()


def plane_gather(value, number, after=()):
    return pl.pallas_call(
        gather_kernel,
        out_shape=jax.ShapeDtypeStruct((8, *value.shape), value.dtype),
        in_specs=[HBM] * (1 + len(after)),
        out_specs=HBM,
        scratch_shapes=[
            pltpu.SemaphoreType.DMA((14,)),
            pltpu.SemaphoreType.DMA((14,)),
            pltpu.SemaphoreType.DMA,
        ],
        compiler_params=pltpu.CompilerParams(collective_id=number, has_side_effects=True),
        cost_estimate=pl.CostEstimate(flops=1, bytes_accessed=1, transcendentals=0),
        name="plane_gather",
    )(value, *after)


def sum_kernel(lefts, terms, tile, *refs):
    a_refs, w_refs = refs[:lefts], refs[lefts : lefts + len(terms)]
    out, s_send, s_recv, d_send, d_recv, x_send, x_recv, y_send, y_recv, x_acc, y_acc, send, recv = refs[-13:]
    y, x, c, index = place()
    to_x, to_y, to_s = {"x": 1 - x}, {"y": 1 - y}, {"c": 1 - c}
    rows, width = out.shape
    half = rows // 2
    parts = (pl.ds(0, half), pl.ds(half, half))
    f32, low = jnp.float32, jnp.bfloat16

    def product(block, put):
        lines = pl.ds(pl.multiple_of(block * rows, rows), rows)

        @pl.loop(0, width // tile)
        def _(step):
            cols = pl.ds(pl.multiple_of(step * tile, tile), tile)
            total = None
            for (left, start), w_ref in zip(terms, w_refs):
                term = mm_nt(a_refs[left][lines, start : start + w_ref.shape[1]], w_ref[cols, :])
                total = term if total is None else total + term
            put(cols, total)

    def hop(slot, src, dst, where):
        copy = pltpu.make_async_remote_copy(
            src_ref=src, dst_ref=dst, send_sem=send.at[slot], recv_sem=recv.at[slot],
            device_id=where, device_id_type=MESH,
        )
        return copy

    def to_sibling(slot, yy, xx):
        def put(cols, total):
            s_send[slot, :, cols] = total.astype(low)

        product(index(yy, xx, 1 - c), put)
        copy = hop(slot, s_send.at[slot], s_recv.at[slot], to_s)
        copy.start()
        return copy

    def with_sibling(slot, yy, xx, keep):
        def put(cols, total):
            keep[:, cols] = (total + s_recv[slot, :, cols].astype(f32)).astype(keep.dtype)

        product(index(yy, xx, c), put)

    greet((to_x, to_y, to_s))
    s0 = to_sibling(0, 1 - y, 1 - x)
    s1 = to_sibling(1, y, 1 - x)
    s0.wait_recv()
    with_sibling(0, 1 - y, 1 - x, d_send)
    d0 = hop(4, d_send.at[parts[0]], d_recv.at[parts[0]], to_x)
    d1 = hop(5, d_send.at[parts[1]], d_recv.at[parts[1]], to_y)
    d0.start()
    d1.start()
    s1.wait_recv()
    with_sibling(1, y, 1 - x, x_acc)
    x_send[parts[0]] = x_acc[parts[0]].astype(low)
    x0 = hop(6, x_send.at[parts[0]], x_recv.at[parts[0]], to_x)
    x0.start()
    s2 = to_sibling(2, 1 - y, x)
    s2.wait_recv()
    with_sibling(2, 1 - y, x, y_acc)
    y_send[parts[1]] = y_acc[parts[1]].astype(low)
    y1 = hop(7, y_send.at[parts[1]], y_recv.at[parts[1]], to_y)
    y1.start()
    s3 = to_sibling(3, y, x)
    d1.wait_recv()
    x_send[parts[1]] = (x_acc[parts[1]] + d_recv[parts[1]].astype(f32)).astype(low)
    x1 = hop(8, x_send.at[parts[1]], x_recv.at[parts[1]], to_x)
    x1.start()
    d0.wait_recv()
    y_send[parts[0]] = (y_acc[parts[0]] + d_recv[parts[0]].astype(f32)).astype(low)
    y0 = hop(9, y_send.at[parts[0]], y_recv.at[parts[0]], to_y)
    y0.start()
    s3.wait_recv()
    with_sibling(3, y, x, out)
    x0.wait_recv()
    y1.wait_recv()
    x1.wait_recv()
    y0.wait_recv()
    out[...] += x_recv[...].astype(f32) + y_recv[...].astype(f32)
    for copy in (s0, s1, s2, s3, d0, d1, x0, x1, y0, y1):
        copy.wait_send()


def plane_sum(lefts, rights, number, after=(), tile=512):
    ends = [(left, start) for left, a in enumerate(lefts) for start in range(0, a.shape[1], rights[0].shape[1])]
    terms = tuple(ends[: len(rights)])
    rows, width = lefts[0].shape[0] // 8, rights[0].shape[0]
    block = (rows, width)
    low, f32 = jnp.bfloat16, jnp.float32
    return pl.pallas_call(
        functools.partial(sum_kernel, len(lefts), terms, min(tile, width)),
        out_shape=jax.ShapeDtypeStruct(block, f32),
        in_specs=[VMEM] * (len(lefts) + len(rights)) + [HBM] * len(after),
        out_specs=VMEM,
        scratch_shapes=[
            pltpu.VMEM((4, *block), low),
            pltpu.VMEM((4, *block), low),
            *[pltpu.VMEM(block, low)] * 6,
            pltpu.VMEM(block, f32),
            pltpu.VMEM(block, f32),
            pltpu.SemaphoreType.DMA((10,)),
            pltpu.SemaphoreType.DMA((10,)),
        ],
        compiler_params=pltpu.CompilerParams(
            collective_id=number, has_side_effects=True, vmem_limit_bytes=48 * 2**20
        ),
        cost_estimate=pl.CostEstimate(flops=1, bytes_accessed=1, transcendentals=0),
        name="plane_sum",
    )(*lefts, *rights, *after)


def swap_kernel(pieces, takes, *refs):
    count = len(pieces)
    sources, (send, recv, own) = refs[: -2 * count - 3], refs[-3:]
    outs, holds = refs[-2 * count - 3 : -count - 3], refs[-count - 3 : -3]
    y, x, c, index = place()
    me = index(y, x, c)
    flips = [(fy, fx, fc) for fy, fx in ((1, 1), (0, 1), (1, 0), (0, 0)) for fc in (0, 1)]
    flips = [flip for flip in flips if flip != (0, 0, 0)]

    def there(flip):
        return tuple(1 - at if f else at for at, f in zip((y, x, c), flip))

    greet([dict(zip(("y", "x", "c"), there(flip))) for flip in flips])
    copies = []
    for piece in range(count):
        for number, flip in enumerate(flips):
            yy, xx, cc = there(flip)
            member = index(yy, xx, cc)
            holds[piece][number] = takes[piece](sources, member, cc)
            copy = pltpu.make_async_remote_copy(
                src_ref=holds[piece].at[number],
                dst_ref=outs[piece].at[me],
                send_sem=send.at[piece * 7 + number],
                recv_sem=recv.at[piece * 7 + number],
                device_id={"y": yy, "x": xx, "c": cc},
                device_id_type=MESH,
            )
            copy.start()
            copies.append(copy)
        holds[piece][7] = takes[piece](sources, me, c)
        keep = pltpu.make_async_copy(holds[piece].at[7], outs[piece].at[me], own.at[piece])
        keep.start()
        copies.append(keep)
    for copy in copies:
        copy.wait()


def plane_swap(sources, shapes, takes, number, after=()):
    low = jnp.bfloat16
    count = len(shapes)
    return pl.pallas_call(
        functools.partial(swap_kernel, shapes, takes),
        out_shape=[jax.ShapeDtypeStruct((8, *shape), low) for shape in shapes],
        in_specs=[VMEM] * len(sources) + [HBM] * len(after),
        out_specs=[HBM] * count,
        scratch_shapes=[
            *[pltpu.VMEM((8, *shape), low) for shape in shapes],
            pltpu.SemaphoreType.DMA((7 * count,)),
            pltpu.SemaphoreType.DMA((7 * count,)),
            pltpu.SemaphoreType.DMA((count,)),
        ],
        compiler_params=pltpu.CompilerParams(
            collective_id=number, has_side_effects=True, vmem_limit_bytes=48 * 2**20
        ),
        cost_estimate=pl.CostEstimate(flops=1, bytes_accessed=1, transcendentals=0),
        name="plane_swap",
    )(*sources, *after)


def team_of(y, x, c):
    flips = [(fy, fx, fc) for fy, fx in ((1, 1), (0, 1), (1, 0), (0, 0)) for fc in (0, 1)]
    return [
        tuple(1 - at if f else at for at, f in zip((y, x, c), flip)) for flip in flips if flip != (0, 0, 0)
    ]


def turn_kernel(planes, src, *refs):
    y, x, c, index = place()
    me = index(y, x, c)
    others = team_of(y, x, c)
    ids = [dict(zip(("y", "x", "c"), other)) for other in others]
    if planes:
        out, total, near, far, held, send, recv, own, send_lines, recv_lines = refs[-10:]
        z = lax.axis_index("z")
        column = [{"z": lax.rem(z + step, planes)} for step in range(1, planes)]
        fetch = pltpu.make_async_copy(src, held, own.at[1])
        fetch.start()
    else:
        out, send, recv, own = refs[-4:]
        column = []
    greet(ids + column)
    count = src.shape[0] // 8

    def rows(member):
        return src.at[pl.ds(pl.multiple_of(member * count, count), count)]

    def spread(buffer, at, where, base):
        copies = [
            pltpu.make_async_remote_copy(
                src_ref=buffer.at[at],
                dst_ref=buffer.at[at],
                send_sem=send_lines.at[base + number],
                recv_sem=recv_lines.at[base + number],
                device_id=other,
                device_id_type=MESH,
            )
            for number, other in enumerate(where)
        ]
        for copy in copies:
            copy.start()
        return copies

    copies = [
        pltpu.make_async_remote_copy(
            src_ref=rows(index(*other)),
            dst_ref=out.at[me],
            send_sem=send.at[number],
            recv_sem=recv.at[number],
            device_id=where,
            device_id_type=MESH,
        )
        for number, (other, where) in enumerate(zip(others, ids))
    ]
    copies.append(pltpu.make_async_copy(rows(me), out.at[me], own.at[0]))
    for copy in copies:
        copy.start()
    if planes:
        fetch.wait()
        squares = jnp.zeros((8, held.shape[1]), jnp.float32)
        for start in range(0, held.shape[0], 64):
            part = held[start : start + 64].astype(jnp.float32)
            squares += jnp.sum(jnp.square(part).reshape(8, 8, -1), axis=0)
        near[me] = jnp.broadcast_to(jnp.sum(squares, keepdims=True), near.shape[1:])
        for copy in spread(near, me, ids, 0):
            copy.wait()
        far[z] = jnp.sum(near[...], axis=0)
        for copy in spread(far, z, column, 7):
            copy.wait()
        total[...] = jnp.sum(far[...], axis=0)
    for copy in copies:
        copy.wait()


def total_kernel(planes, src, *refs):
    out, near, far, send, recv = refs[-5:]
    y, x, c, index = place()
    z = lax.axis_index("z")
    ids = [dict(zip(("y", "x", "c"), other)) for other in team_of(y, x, c)]
    column = [{"z": lax.rem(z + step, planes)} for step in range(1, planes)]
    me = index(y, x, c)
    near[me] = src[...]
    greet(ids + column)

    def spread(buffer, at, where, base):
        copies = [
            pltpu.make_async_remote_copy(
                src_ref=buffer.at[at],
                dst_ref=buffer.at[at],
                send_sem=send.at[base + number],
                recv_sem=recv.at[base + number],
                device_id=other,
                device_id_type=MESH,
            )
            for number, other in enumerate(where)
        ]
        for copy in copies:
            copy.start()
        for copy in copies:
            copy.wait()

    spread(near, me, ids, 0)
    far[z] = jnp.sum(near[...], axis=0)
    spread(far, z, column, 7)
    out[...] = jnp.sum(far[...], axis=0)


def total_sum(value, planes, number, after=()):
    return pl.pallas_call(
        functools.partial(total_kernel, planes),
        out_shape=jax.ShapeDtypeStruct(value.shape, value.dtype),
        in_specs=[VMEM] + [HBM] * len(after),
        out_specs=VMEM,
        scratch_shapes=[pltpu.VMEM((size, *value.shape), value.dtype) for size in (8, planes)]
        + [pltpu.SemaphoreType.DMA((6 + planes,))] * 2,
        compiler_params=pltpu.CompilerParams(
            collective_id=number, has_side_effects=True, vmem_limit_bytes=16 * 2**20
        ),
        cost_estimate=pl.CostEstimate(flops=1, bytes_accessed=1, transcendentals=0),
        name="total_sum",
    )(value, *after)


def turn(rows, number, after=(), planes=0):
    block = (rows.shape[0] // 8, rows.shape[1])
    dma = pltpu.SemaphoreType.DMA
    out_shape, out_specs = [jax.ShapeDtypeStruct((8, *block), rows.dtype)], [HBM]
    scratch = [dma((7,)), dma((7,)), dma((2,))]
    if planes:
        tile = jax.ShapeDtypeStruct((8, 128), jnp.float32)
        out_shape.append(tile)
        out_specs.append(VMEM)
        buffers = [pltpu.VMEM((size, *tile.shape), tile.dtype) for size in (8, planes)]
        scratch = buffers + [pltpu.VMEM(rows.shape, rows.dtype)] + scratch + [dma((6 + planes,)), dma((6 + planes,))]
    return pl.pallas_call(
        functools.partial(turn_kernel, planes),
        out_shape=out_shape,
        in_specs=[HBM] * (1 + len(after)),
        out_specs=out_specs,
        scratch_shapes=scratch,
        compiler_params=pltpu.CompilerParams(
            collective_id=number, has_side_effects=True, vmem_limit_bytes=56 * 2**20
        ),
        cost_estimate=pl.CostEstimate(flops=1, bytes_accessed=1, transcendentals=0),
        name="turn",
    )(rows, *after)


def hops(planes, send, recv, block, up):
    z = lax.axis_index("z")

    def step(number):
        gone, came = (z - number + 1, z - number) if up else (z + number - 1, z + number)
        goes = ((gone >= 0) & (z + 1 < planes)) if up else ((gone < planes) & (z >= 1))
        comes = (came >= 0) if up else (came < planes)

        def copy(b):
            return pltpu.make_async_remote_copy(
                src_ref=block(b),
                dst_ref=block(b),
                send_sem=send.at[number - 1],
                recv_sem=recv.at[number - 1],
                device_id={"z": z + 1 if up else z - 1},
                device_id_type=MESH,
            )

        return (
            lambda: pl.when(goes)(lambda: copy(gone).start()),
            lambda: pl.when(comes)(lambda: copy(came).wait_recv()),
            lambda: pl.when(goes)(lambda: copy(gone).wait_send()),
        )

    return [step(number) for number in range(1, planes)]


def ring(planes):
    z = lax.axis_index("z")
    return [{"z": lax.rem(z + 1, planes)}, {"z": lax.rem(z + planes - 1, planes)}]


def spread_to(others, ids, source, take, hold, place_of, send, recv, own, ready=None):
    y, x, c, index = place()
    me = index(y, x, c)
    copies = []
    if ready is not None:
        for number, other in enumerate(others):
            hold[number] = take([source], index(*other), other[2])
        ready()
    for number, (other, where) in enumerate(zip(others, ids)):
        if ready is None:
            hold[number] = take([source], index(*other), other[2])
        copy = pltpu.make_async_remote_copy(
            src_ref=hold.at[number], dst_ref=place_of(me), send_sem=send.at[number], recv_sem=recv.at[number],
            device_id=where, device_id_type=MESH,
        )
        copy.start()
        copies.append(copy)
    hold[7] = take([source], me, c)
    keep = pltpu.make_async_copy(hold.at[7], place_of(me), own)
    keep.start()
    return copies, keep


def begin_kernel(
    planes, take, take_feed, attention, feed, tokens_from, gain, all_attention, all_rows, columns,
    tokens, held, hold, feed_held, feed_hold, rows, a_send, a_recv, f_send, f_recv, r_send, r_recv, u_send, u_recv, d_send, d_recv, own,
):
    y, x, c, index = place()
    z = lax.axis_index("z")
    me, at_x, at_y, at_d = index(y, x, c), index(y, 1 - x, c), index(1 - y, x, c), index(1 - y, 1 - x, c)
    others = team_of(y, x, c)
    ids = [dict(zip(("y", "x", "c"), other)) for other in others]
    to_x, to_y, to_s = {"x": 1 - x}, {"y": 1 - y}, {"c": 1 - c}
    count = held.shape[0]
    half = rows.shape[0] // 2
    parts = (pl.ds(0, half), pl.ds(half, half))
    fetch = pltpu.make_async_copy(attention, held, own.at[0])
    fetch.start()
    fetch_tokens = pltpu.make_async_copy(tokens_from, tokens, own.at[5])
    fetch_tokens.start()
    fetch_feed = pltpu.make_async_copy(feed.at[:, pl.ds(0, feed_held.shape[1])], feed_held, own.at[3])
    fetch_feed.start()
    ready = hail(ids + ring(planes))
    fetch.wait()

    def attention_rows(start, size):
        return all_attention.at[pl.ds(pl.multiple_of(start, count), size)]

    a_copies, a_keep = spread_to(
        others, ids, held, take, hold, lambda m: attention_rows((z * 8 + m) * count, count), a_send, a_recv, own.at[1], ready
    )

    def hop(slot, block, part, where, first=False):
        piece = all_rows.at[block, parts[part]]
        copy = pltpu.make_async_remote_copy(
            src_ref=rows.at[parts[part]] if first else piece, dst_ref=piece,
            send_sem=r_send.at[slot], recv_sem=r_recv.at[slot], device_id=where, device_id_type=MESH,
        )
        copy.start()
        return copy

    for copy in a_copies:
        copy.wait_recv()
    a_keep.wait()

    def plane_block(b):
        return attention_rows(b * 8 * count, 8 * count)

    up = hops(planes, u_send, u_recv, plane_block, True)
    down = hops(planes, d_send, d_recv, plane_block, False)

    def pass_on(number):
        if number > 0:
            up[number - 1][1]()
            down[number - 1][1]()
        if number < planes - 1:
            up[number][0]()
            down[number][0]()

    pass_on(0)
    fetch_tokens.wait()

    @pl.loop(0, rows.shape[0] // 16)
    def _(group):
        lines = pl.ds(pl.multiple_of(group * 16, 16), 16)
        rows[lines] = rms_forward(tokens[lines].astype(jnp.float32), gain[...])[0].astype(rows.dtype)

    x0, y1 = hop(0, me, 0, to_x, True), hop(2, me, 1, to_y, True)
    x1, y0 = hop(1, me, 1, to_x, True), hop(3, me, 0, to_y, True)
    s0, s1 = hop(4, me, 0, to_s, True), hop(5, me, 1, to_s, True)
    mine = pltpu.make_async_copy(rows, all_rows.at[me], own.at[2])
    mine.start()
    x0.wait_recv()
    d0 = hop(6, at_x, 0, to_y)
    y1.wait_recv()
    d1 = hop(7, at_y, 1, to_x)
    sx0, sy1 = hop(8, at_x, 0, to_s), hop(9, at_y, 1, to_s)
    fetch_feed.wait()
    f_copies, f_keep = spread_to(
        others, ids, feed_held, take_feed, feed_hold, lambda m: columns.at[m], f_send, f_recv, own.at[4]
    )
    pass_on(1)
    x1.wait_recv()
    sx1 = hop(10, at_x, 1, to_s)
    y0.wait_recv()
    sy0 = hop(11, at_y, 0, to_s)
    pass_on(2)
    d0.wait_recv()
    sd0 = hop(12, at_d, 0, to_s)
    d1.wait_recv()
    sd1 = hop(13, at_d, 1, to_s)
    for number in range(3, planes):
        pass_on(number)
    for copy in (s0, s1, sx0, sy1, sx1, sy0, sd0, sd1, *f_copies):
        copy.wait_recv()
    for copy in (x0, x1, y0, y1, s0, s1, d0, d1, sx0, sy1, sx1, sy0, sd0, sd1, *a_copies, *f_copies):
        copy.wait_send()
    for step in up + down:
        step[2]()
    mine.wait()
    f_keep.wait()


def begin(attention, feed, tokens, gain, takes, widths, planes, number):
    low, dma = jnp.bfloat16, pltpu.SemaphoreType.DMA
    count = attention.shape[0]
    return pl.pallas_call(
        functools.partial(begin_kernel, planes, *takes),
        out_shape=[
            jax.ShapeDtypeStruct((planes * 8 * count, widths[0]), low),
            jax.ShapeDtypeStruct((8, *tokens.shape), low),
            jax.ShapeDtypeStruct((8, count, widths[1]), low),
        ],
        in_specs=[HBM, HBM, HBM, VMEM],
        out_specs=[HBM] * 3,
        scratch_shapes=[
            pltpu.VMEM(tokens.shape, tokens.dtype),
            pltpu.VMEM(attention.shape, attention.dtype),
            pltpu.VMEM((8, count, widths[0]), low),
            pltpu.VMEM((count, 8 * widths[1]), feed.dtype),
            pltpu.VMEM((8, count, widths[1]), low),
            pltpu.VMEM(tokens.shape, low),
            *[dma((size,)) for size in (7, 7, 7, 7, 14, 14, *[planes - 1] * 4, 6)],
        ],
        compiler_params=pltpu.CompilerParams(
            collective_id=number, has_side_effects=True, vmem_limit_bytes=54 * 2**20
        ),
        cost_estimate=pl.CostEstimate(flops=1, bytes_accessed=1, transcendentals=0),
        name="begin",
    )(attention, feed, tokens, gain)


def turned(value, cos_table, sin_table):
    half = value.shape[1] // 2
    first, second = value[:, :half], value[:, half:]
    return jnp.concatenate([first * cos_table - second * sin_table, second * cos_table + first * sin_table], axis=1)


def climb_kernel(
    planes, rows, weights, cos, sin, mine, other, weight, held, zeros, stay, u_send, u_recv, s_send, s_recv, own, fill, move
):
    z, c = lax.axis_index("z"), lax.axis_index("c")
    to_s = {"c": 1 - c}
    barrier = pltpu.get_barrier_semaphore()
    for where in [to_s] + ring(planes):
        pl.semaphore_signal(barrier, inc=1, device_id=where, device_id_type=MESH)
    count, (sides, span) = rows.shape[0], cos.shape[:2]
    size = 512
    pull_weight = pltpu.make_async_copy(
        weights.at[:, pl.ds(weight.shape[1], weight.shape[1])], weight, move.at[count // size]
    )
    pull_weight.start()
    pulls = [
        pltpu.make_async_copy(rows.at[pl.ds(start, size)], held.at[pl.ds(start, size)], move.at[start // size])
        for start in range(0, count, size)
    ]
    for copy in pulls:
        copy.start()
    pull_weight.wait()
    for start in range(0, count, size):
        pulls[start // size].wait()
        value = mm(held[start : start + size], weight[...])
        for line in range(0, size, span):
            side = (start + line) // (count // sides)
            part = value[line : line + span]
            part = jnp.where(c == 0, turned(part, cos[side], sin[side]), part)
            stay[start + line : start + line + span] = part.astype(stay.dtype)
    zeros[...] = jnp.zeros_like(zeros)
    pl.semaphore_wait(barrier, 3)

    def across(n):
        return pltpu.make_async_remote_copy(
            src_ref=stay if n == 0 else mine.at[n], dst_ref=other.at[n], send_sem=s_send.at[n], recv_sem=s_recv.at[n],
            device_id=to_s, device_id_type=MESH,
        )

    def along(n):
        return pltpu.make_async_remote_copy(
            src_ref=stay if n == 1 else mine.at[n - 1], dst_ref=mine.at[n], send_sem=u_send.at[n - 1], recv_sem=u_recv.at[n - 1],
            device_id={"z": z + 1}, device_id_type=MESH,
        )

    def fills(n):
        return [
            pltpu.make_async_copy(zeros, buffer.at[n], fill.at[2 * (n - 1) + number])
            for number, buffer in enumerate((mine, other))
        ]

    keep = pltpu.make_async_copy(stay, mine.at[0], own)
    more = z + 1 < planes
    pl.when(more)(lambda: along(1).start())
    across(0).start()
    keep.start()
    for n in range(1, planes):

        @pl.when(z < n)
        def _():
            for copy in fills(n):
                copy.start()

    for n in range(1, planes):

        @pl.when(z >= n)
        def _():
            along(n).wait_recv()
            if n + 1 < planes:
                pl.when(more)(lambda: along(n + 1).start())
            across(n).start()

    across(0).wait()
    keep.wait()
    for n in range(1, planes):

        @pl.when(z >= n)
        def _():
            across(n).wait()

        @pl.when(z < n)
        def _():
            for copy in fills(n):
                copy.wait()

        pl.when((z >= n - 1) & more)(lambda: along(n).wait_send())


def climb(rows, weights, cos, sin, planes, number):
    dma = pltpu.SemaphoreType.DMA
    block = (rows.shape[0], weights.shape[1] // 3)
    blocks = jax.ShapeDtypeStruct((planes, *block), rows.dtype)
    return pl.pallas_call(
        functools.partial(climb_kernel, planes),
        out_shape=[blocks, blocks],
        in_specs=[HBM] * 2 + [VMEM] * 2,
        out_specs=[HBM] * 2,
        scratch_shapes=[
            pltpu.VMEM((weights.shape[0], block[1]), rows.dtype),
            pltpu.VMEM(rows.shape, rows.dtype),
            pltpu.VMEM(block, rows.dtype),
            pltpu.VMEM(block, rows.dtype),
            *[dma((size,)) for size in (planes - 1, planes - 1, planes, planes)],
            dma,
            dma((2 * (planes - 1),)),
            dma((rows.shape[0] // 512 + 1,)),
        ],
        compiler_params=pltpu.CompilerParams(
            collective_id=number, has_side_effects=True, vmem_limit_bytes=56 * 2**20
        ),
        cost_estimate=pl.CostEstimate(flops=1, bytes_accessed=1, transcendentals=0),
        name="climb",
    )(rows, weights, cos, sin)


def fall_kernel(
    planes, terms_from, rows, left_from, query_term, out_term, cos, sin, value, term, blocks,
    terms, left, sends, recvs, total, first, held, send, recv, t_send, t_recv, own, move, fetch,
):
    y, x, c, index = place()
    z = lax.axis_index("z")
    me = index(y, x, c)
    others = team_of(y, x, c)
    ids = [dict(zip(("y", "x", "c"), other)) for other in others]
    f32 = jnp.float32
    count = rows.shape[0] // 8
    size = terms.shape[2]
    given = ((query_term, 0), (out_term, 2))
    pulls = [pltpu.make_async_copy(ref, held.at[n], move.at[n]) for n, (ref, _) in enumerate(given)]
    get_terms = pltpu.make_async_copy(terms_from, terms, fetch.at[0])
    get_terms.start()
    get_left = pltpu.make_async_copy(left_from, left, fetch.at[1])
    get_left.start()
    for copy in pulls:
        copy.start()
    greet(ids + ring(planes))
    get_terms.wait()

    def rows_of(member):
        return rows.at[pl.ds(pl.multiple_of(member * count, count), count)]

    half = terms.shape[1] // 2
    parts = [pl.ds(n * half, half) for n in range(2)]

    def hop(step, n):
        slot = 2 * (step - 1) + n
        return pltpu.make_async_remote_copy(
            src_ref=sends.at[step - 1, parts[n]], dst_ref=recvs.at[step - 1, parts[n]],
            send_sem=send.at[slot], recv_sem=recv.at[slot], device_id={"z": z - 1}, device_id_type=MESH,
        )

    def came(step):
        return (z + 1 < planes) & (z + 1 + step - planes >= 0)

    copies = [
        pltpu.make_async_remote_copy(
            src_ref=rows_of(index(*other)), dst_ref=blocks.at[me], send_sem=t_send.at[number], recv_sem=t_recv.at[number],
            device_id=where, device_id_type=MESH,
        )
        for number, (other, where) in enumerate(zip(others, ids))
    ]
    copies.append(pltpu.make_async_copy(rows_of(me), blocks.at[me], own))
    pushes = []
    for step in range(1, planes):
        block = z + step - planes
        for n in range(2):
            lines = parts[n]
            if step > 1:
                pl.when(came(step - 1))(lambda: hop(step - 1, n).wait_recv())

            @pl.when((block >= 0) & (z + 1 == planes))
            def _():
                sends[step - 1, lines] = terms[block, lines]

            if step > 1:

                @pl.when((block >= 0) & (z + 1 < planes))
                def _():
                    added = terms[block, lines].astype(f32) + recvs[step - 2, lines].astype(f32)
                    sends[step - 1, lines] = added.astype(terms.dtype)

            pl.when(block >= 0)(lambda: hop(step, n).start())
        if step == 1:
            for copy in copies:
                copy.start()
            total[...] = terms[z].astype(f32)
            for n, (_, column) in enumerate(given):
                pulls[n].wait()
                pushes.append(
                    pltpu.make_async_copy(held.at[n], term.at[:, pl.ds(column * size, size)], move.at[2 + n])
                )
                pushes[-1].start()
    last = planes - 1
    sides, span = cos.shape[:2]
    get_left.wait()
    for n in range(2):
        lines = parts[n]

        @pl.when(came(last))
        def _():
            hop(last, n).wait_recv()
            total[lines] += recvs[last - 1, lines].astype(f32)

        for line in range(n * half, (n + 1) * half, span):
            side = line // (total.shape[0] // sides)
            part = total[line : line + span]
            part = jnp.where(c == 0, turned(part, cos[side], -sin[side]), part)
            value[line : line + span] = part.astype(value.dtype)
        upright = value[lines].astype(f32).T.astype(value.dtype)
        for start in range(0, left.shape[1], 512):
            columns = pl.ds(start, 512)
            made = mm(upright, left[lines, columns])
            if n == 0:
                first[:, columns] = made
                continue
            held[2, columns] = (first[:, columns] + made).T.astype(held.dtype)
            pushes.append(
                pltpu.make_async_copy(
                    held.at[2, columns], term.at[columns, pl.ds(size, size)], move.at[4 + start // 512]
                )
            )
            pushes[-1].start()
    for step in range(1, planes):
        for n in range(2):
            pl.when(z + step - planes >= 0)(lambda: hop(step, n).wait_send())
    for copy in copies + pushes:
        copy.wait()


def fall(terms, rows, left, query_term, out_term, cos, sin, planes, number):
    block = terms.shape[1:]
    dma, low = pltpu.SemaphoreType.DMA, terms.dtype
    return pl.pallas_call(
        functools.partial(fall_kernel, planes),
        out_shape=[
            jax.ShapeDtypeStruct(block, low),
            jax.ShapeDtypeStruct((left.shape[1], 3 * block[1]), low),
            jax.ShapeDtypeStruct((8, rows.shape[0] // 8, rows.shape[1]), low),
        ],
        in_specs=[HBM] * 5 + [VMEM] * 2,
        out_specs=[VMEM, HBM, HBM],
        scratch_shapes=[pltpu.VMEM(terms.shape, low), pltpu.VMEM(left.shape, low)]
        + [pltpu.VMEM((planes - 1, *block), low)] * 2
        + [pltpu.VMEM(block, jnp.float32), pltpu.VMEM((block[1], left.shape[1]), jnp.float32)]
        + [pltpu.VMEM((3, left.shape[1], block[1]), low)]
        + [dma((2 * (planes - 1),))] * 2
        + [dma((7,)), dma((7,)), dma, dma((4 + left.shape[1] // 512,)), dma((2,))],
        compiler_params=pltpu.CompilerParams(
            collective_id=number, has_side_effects=True, vmem_limit_bytes=56 * 2**20
        ),
        cost_estimate=pl.CostEstimate(flops=1, bytes_accessed=1, transcendentals=0),
        name="fall",
    )(terms, rows, left, query_term, out_term, cos, sin)


def dot(left, right, contract):
    return lax.dot_general(left, right, (contract, ((), ())), preferred_element_type=jnp.float32)


def mm(left, right):
    return dot(left, right, ((1,), (0,)))


def mm_nt(left, right):
    return dot(left, right, ((1,), (1,)))


def mm_tn(left, right):
    return dot(left, right, ((0,), (0,)))


def bmm(pattern, left, right):
    return jnp.einsum(pattern, left, right, preferred_element_type=jnp.float32)


def angle_tables(positions):
    half_dim = HEAD_SIZE // 2
    frequency = rope_base ** (-(jnp.arange(half_dim).astype(jnp.float32) * 2.0) / HEAD_SIZE)
    phases = positions.astype(jnp.float32)[:, None] * frequency[None, :]
    return (jnp.cos(phases), jnp.sin(phases))


def rotate(value, cos_table, sin_table):
    half = value.shape[-1] // 2
    a, b = value[..., :half], value[..., half:]
    return jnp.concatenate([a * cos_table - b * sin_table, b * cos_table + a * sin_table], axis=-1)


def rms_forward(value, gain_row):
    inverse = lax.rsqrt(jnp.mean(value * value, axis=-1, keepdims=True) + norm_eps)
    return (value * inverse * gain_row, inverse)


def rms_back(grad_out, value, inverse, gain_row):
    scaled = grad_out * gain_row
    grad_in = inverse * (
        scaled - value * inverse * inverse * jnp.mean(scaled * value, axis=-1, keepdims=True)
    )
    return (grad_in, jnp.sum(grad_out * value * inverse, axis=0))


def adamw(weight, gradient, moment_one, moment_two, step_rate, decay_rate, invert=jnp.reciprocal):
    mean_new = beta_one * moment_one + (1.0 - beta_one) * gradient
    square_new = beta_two * moment_two + (1.0 - beta_two) * gradient * gradient
    below = jnp.sqrt(square_new * (1.0 / (1.0 - beta_two**STEP))) + adam_eps
    direction = mean_new * (1.0 / (1.0 - beta_one**STEP)) * invert(below)
    return (weight - step_rate * (direction + decay_rate * weight), mean_new, square_new)


def attention_parts(core, length, q_ref, mine_ref, other_ref, query_ref, key_ref):
    mine, other = mine_ref[...].reshape(-1, HEAD_SIZE), other_ref[...].reshape(-1, HEAD_SIZE)
    first = core == 0
    k, v = jnp.where(first, mine, other), jnp.where(first, other, mine)
    q = q_ref[...].reshape(-1, HEAD_SIZE)
    at, key_at = query_ref[...], key_ref[...]
    allowed = (key_at <= at) & (key_at < length) & (key_at >= 0)
    scores = jnp.where(allowed, mm_nt(q, k) * HEAD_SIZE ** (-0.5), masked_value)
    exponent = jnp.exp(scores - jnp.max(scores, axis=-1, keepdims=True))
    return q, k, v, exponent / jnp.sum(exponent, axis=-1, keepdims=True)


def attention_kernel(core_ref, length_ref, q_ref, mine_ref, other_ref, query_ref, key_ref, out_ref):
    length = length_ref[pl.program_id(0)]
    _, _, v, soft = attention_parts(core_ref[0], length, q_ref, mine_ref, other_ref, query_ref, key_ref)
    out_ref[...] = mm(soft.astype(jnp.bfloat16), v).astype(jnp.bfloat16).reshape(out_ref.shape)


def attention_back_kernel(
    core_ref, length_ref, q_ref, mine_ref, other_ref, query_ref, key_ref, do_ref, cos_ref, sin_ref,
    dq_ref, keep_ref, send_ref,
):
    low = jnp.bfloat16
    core = core_ref[0]
    length = length_ref[pl.program_id(0)]
    q, k, v, soft = attention_parts(core, length, q_ref, mine_ref, other_ref, query_ref, key_ref)
    do = do_ref[...].reshape(-1, HEAD_SIZE)
    dp = mm_nt(do, v)
    delta = jnp.sum(soft * dp, axis=-1, keepdims=True)
    ds = (soft * (dp - delta) * HEAD_SIZE ** (-0.5)).astype(low)
    dq = mm(ds, k)
    cos_table, sin_table = cos_ref[...], sin_ref[...]
    half = HEAD_SIZE // 2
    a, b = dq[:, :half], dq[:, half:]
    turned = jnp.concatenate([a * cos_table + b * sin_table, b * cos_table - a * sin_table], axis=-1)
    dq_ref[...] = turned.astype(low).reshape(dq_ref.shape)
    dk, dv = mm_tn(ds, q), mm_tn(soft.astype(low), do)
    first = core == 0
    keep, send = (t.reshape(keep_ref.shape) for t in (jnp.where(first, dk, dv), jnp.where(first, dv, dk)))
    for block in range(keep_ref.shape[0]):
        at = core_ref[1 + block]
        keep_ref[at] = keep[block]
        send_ref[at] = send[block].astype(low)


def attention_call(kernel, core, lengths, q, mine, other, query_pos, key_pos, extra, outs, name):
    ny, count, span, size = q.shape
    nz = mine.shape[0]
    rows = pl.BlockSpec((ny, 1, span, size), lambda i, *_: (0, i, 0, 0))
    keys = pl.BlockSpec((nz, ny, 1, span, size), lambda i, *_: (0, 0, i, 0, 0))

    def whole(value):
        return pl.BlockSpec(value.shape, lambda i, *_: (0,) * value.ndim)

    kinds = {"rows": (rows, q.shape), "keys": (keys, mine.shape)}
    return pl.pallas_call(
        kernel,
        grid_spec=pltpu.PrefetchScalarGridSpec(
            num_scalar_prefetch=2,
            grid=(count,),
            in_specs=[rows, keys, keys, whole(query_pos), whole(key_pos)]
            + [rows if value.shape == q.shape else whole(value) for value in extra],
            out_specs=[kinds[kind][0] for kind, _ in outs],
        ),
        out_shape=[jax.ShapeDtypeStruct(kinds[kind][1], dtype) for kind, dtype in outs],
        compiler_params=pltpu.CompilerParams(vmem_limit_bytes=48 * 2**20),
        cost_estimate=pl.CostEstimate(flops=1, bytes_accessed=1, transcendentals=0),
        name=name,
    )(core, lengths, q, mine, other, query_pos, key_pos, *extra)


def feed_back_kernel(dyb_ref, weight_ref, gate_ref, up_ref, out_ref):
    dm = mm(dyb_ref[...], weight_ref[...])
    gate, upward = gate_ref[...], up_ref[...]
    sig = jax.nn.sigmoid(gate)
    part = gate.shape[1]
    out_ref[:, :part] = (dm * upward * sig * (1.0 + gate * (1.0 - sig))).astype(out_ref.dtype)
    out_ref[:, part:] = (dm * gate * sig).astype(out_ref.dtype)


def feed_back(dyb, weight, both, lines=256):
    count, part = both.shape[0], both.shape[1] // 2

    def rows(width, column=0):
        return pl.BlockSpec((lines, width), lambda i: (i, column))

    return pl.pallas_call(
        feed_back_kernel,
        grid=(count // lines,),
        in_specs=[rows(dyb.shape[1]), pl.BlockSpec(weight.shape, lambda i: (0, 0)), rows(part), rows(part, 1)],
        out_specs=rows(2 * part),
        out_shape=jax.ShapeDtypeStruct((count, 2 * part), jnp.bfloat16),
        compiler_params=pltpu.CompilerParams(vmem_limit_bytes=48 * 2**20),
        cost_estimate=pl.CostEstimate(flops=1, bytes_accessed=1, transcendentals=0),
        name="feed_back",
    )(dyb, weight, both, both)


def close_reciprocal(value):
    guess = pltpu.reciprocal(value, approx=True)
    return guess * (2.0 - value * guess)


def norm_of(lines_ref, tile_ref):
    gains = lines_ref[:-8]
    return jnp.sqrt(jnp.sum(gains * gains, keepdims=True) + lines_ref[-8:-7, 0:1] + tile_ref[0:1, 0:1])


def update_kernel(*refs):
    lines_ref, tile_ref, gain_ref, gate_up_ref, down_ref, attention_ref = refs[:6]
    gains, feed, attention = refs[6:9], refs[9:12], refs[12:15]
    new_gains, norm_ref, new_feed, new_attention, factor_ref = refs[15:18], refs[18], refs[19:23], refs[23:27], refs[27]
    rows = feed[0].shape[0]
    lines = pl.ds(pl.multiple_of(pl.program_id(0) * rows, rows), rows)

    @pl.when(pl.program_id(0) == 0)
    def _():
        norm = norm_of(lines_ref, tile_ref)
        norm_ref[...] = norm
        factor_ref[...] = clip_norm / norm
        weight, mean, square = (ref[...] for ref in gains)
        gradient = gain_ref[...] * factor_ref[...]
        for ref, value in zip(new_gains, adamw(weight, gradient, mean, square, gain_rate, 0.0)):
            ref[...] = value

    factor = factor_ref[...]

    def piece(olds, news, grad_ref, member, start, column, size):
        at = pl.ds(pl.multiple_of(column, size), size)
        gradient = grad_ref[member, lines, pl.ds(start, size)].astype(jnp.float32) * factor
        weight, mean, square = (ref[:, at] for ref in olds)
        values = adamw(weight, gradient, mean, square, matrix_rate, weight_decay, close_reciprocal)
        for ref, value in zip(news, (*values, values[0])):
            ref[:, at] = value.astype(ref.dtype)

    part = down_ref.shape[2]
    size = min(part, 512)

    @pl.loop(0, 8)
    def _(member):
        for offset in range(0, part, size):
            for number, (grad_ref, start) in enumerate(((gate_up_ref, 0), (gate_up_ref, part), (down_ref, 0))):
                column = (number * 8 + member) * part + offset
                piece(feed, new_feed, grad_ref, member, start + offset, column, size)
        core = lax.rem(member, 2)
        kv_column = (8 + 4 * core + lax.div(member, 2)) * HEAD_SIZE
        for number, column in enumerate((member * HEAD_SIZE, kv_column, (16 + member) * HEAD_SIZE)):
            piece(attention, new_attention, attention_ref, member, number * HEAD_SIZE, column, HEAD_SIZE)


def update(sums, grads, gains, feed, attention):
    f32, low = jnp.float32, jnp.bfloat16
    rows = min(feed[0].shape[0], 16)

    def some(value):
        return pl.BlockSpec((rows, value.shape[1]), lambda i: (i, 0))

    def whole(value):
        return pl.BlockSpec(value.shape, lambda i: (0,) * value.ndim)

    norm = jax.ShapeDtypeStruct((1, 1), f32)
    matrices = [jax.ShapeDtypeStruct(part[0].shape, dtype) for part in (feed, attention) for dtype in (f32, f32, f32, low)]
    return pl.pallas_call(
        update_kernel,
        grid=(feed[0].shape[0] // rows,),
        in_specs=[whole(value) for value in (*sums, *grads, *gains)] + [some(value) for value in (*feed, *attention)],
        out_specs=[whole(value) for value in (*gains, norm)] + [some(value) for value in matrices],
        out_shape=[jax.ShapeDtypeStruct(gains[0].shape, f32)] * 3 + [norm] + matrices,
        scratch_shapes=[pltpu.VMEM((1, 1), f32)],
        compiler_params=pltpu.CompilerParams(vmem_limit_bytes=56 * 2**20),
        name="update",
    )(*sums, *grads, *gains, *feed, *attention)


def is_square():
    return lax.axis_size("y") == 2 and lax.axis_size("x") == 2


def swap(blocks):
    return lax.all_to_all(blocks, TEAM, split_axis=0, concat_axis=0, tiled=True)


def over_planes(blocks):
    return lax.all_gather(blocks.reshape(-1, blocks.shape[-1]), "z", axis=0, tiled=True)


def scatter_planes(term):
    return lax.psum_scatter(term, "z", scatter_dimension=0, tiled=True)


def together(*values):
    return lax.optimization_barrier(values)


def scatter_team(rows, number, after=()):
    if not is_square():
        return swap(rows.reshape(8, -1, rows.shape[-1]))
    return turn(rows, number, after)[0]


def team_gather(local, number, after=()):
    if not is_square():
        return lax.all_gather(local, TEAM, axis=0, tiled=True)
    return plane_gather(local, number, after).reshape(-1, local.shape[1])


def team_sum(lefts, rights, number, after=()):
    if is_square():
        return plane_sum(lefts, rights, number, after)
    partial = mm_nt(jnp.concatenate(lefts, axis=1), jnp.concatenate(rights, axis=1))
    return lax.psum_scatter(partial.astype(jnp.bfloat16), TEAM, scatter_dimension=0, tiled=True).astype(jnp.float32)


def local(
    tokens,
    lengths,
    norm_gains,
    attention_weight,
    feed_weight,
    cotangent,
    attention_mean,
    attention_square,
    feed_mean,
    feed_square,
    gain_mean,
    gain_square,
):
    low = jnp.bfloat16
    sequences, span, width = tokens.shape
    ny, nx, nz = lax.axis_size("y"), lax.axis_size("x"), lax.axis_size("z")
    team = ny * nx * 2
    core = lax.axis_index("c")
    rows = attention_weight.shape[0]
    q_width, kv_width = QUERY_HEADS * HEAD_SIZE, KEY_VALUE_HEADS * HEAD_SIZE
    count = sequences * span
    all_sequences = nx * 2 * sequences
    reach = ny * span
    near = is_square()
    ff_part = FF // team

    def columns(start, size):
        return pl.ds(pl.multiple_of(start, size), size)

    def take_attention(sources, member, c):
        source = sources[0]
        starts = (
            member * HEAD_SIZE,
            q_width + c * kv_width + (member - c) // 2 * HEAD_SIZE,
            q_width + 2 * kv_width + member * HEAD_SIZE,
        )
        return jnp.concatenate([source[:, columns(s, HEAD_SIZE)].astype(low) for s in starts], axis=1)

    def take_feed(*parts):
        return lambda sources, member, c: jnp.concatenate(
            [sources[0][:, columns(part * FF + member * ff_part, ff_part)].astype(low) for part in parts], axis=1
        )

    def spread(source, take, size, number, after=()):
        if is_square():
            blocks = plane_swap([source], [(rows, size)], [take], number, after)[0]
        else:
            blocks = swap(jnp.stack([take([source], member, member % 2) for member in range(8)]))
        return blocks, over_planes(blocks)

    team_base = lax.axis_index("z") * reach
    team_pos = team_base + jnp.arange(reach, dtype=jnp.int32)
    own_pos = team_base + lax.axis_index("y") * span + jnp.arange(span, dtype=jnp.int32)
    if near:
        key_pos = jnp.concatenate([team_pos - back * reach for back in range(nz)])
    else:
        key_pos = jnp.arange(nz * reach, dtype=jnp.int32)
    query_at, key_at = team_pos[:, None], key_pos[None, :]
    cos_table, sin_table = angle_tables(team_pos)
    cos_rows, sin_rows = (t.reshape(ny, 1, span, -1) for t in (cos_table, sin_table))
    valid = (own_pos[None, :] < lengths[:, None]).astype(jnp.float32).reshape(count, 1)
    lengths_all = lax.all_gather(lengths, ("x", "c"), axis=0, tiled=True)
    planes = jnp.arange(nz, dtype=jnp.int32)
    if near:
        planes = (lax.axis_index("z") - planes) % nz
    core_at = jnp.concatenate([jnp.reshape(core, (1,)), planes]).astype(jnp.int32)

    def heads(value):
        return value.reshape(ny, all_sequences, span, HEAD_SIZE)

    x_in = tokens.reshape(count, width).astype(jnp.float32)
    normed_one, inverse_one = rms_forward(x_in, norm_gains[0])
    outer_grad = cotangent.reshape(count, width).astype(jnp.float32) * valid
    if is_square():
        attention_mine, h1, gate_up_blocks = begin(
            attention_weight,
            feed_weight,
            tokens.reshape(count, width),
            norm_gains[:1],
            (take_attention, take_feed(0, 1)),
            (3 * HEAD_SIZE, 2 * ff_part),
            nz,
            1,
        )
        h1 = h1.reshape(-1, width)
    else:
        attention_mine = spread(attention_weight, take_attention, 3 * HEAD_SIZE, 1)[1]
        gate_up_blocks, gate_up_weight = spread(feed_weight, take_feed(0, 1), 2 * ff_part, 2)
        h1 = team_gather(normed_one.astype(low), 3)
    query_weight = attention_mine[:, :HEAD_SIZE]
    kv_weight = attention_mine[:, HEAD_SIZE : 2 * HEAD_SIZE]
    out_weight = attention_mine[:, 2 * HEAD_SIZE :]
    tables = [t.reshape(ny, span, -1) for t in (cos_table, sin_table)]
    if is_square():
        kv, other = climb(h1, attention_mine, *tables, nz, 2)
        kv, other = (t.reshape(nz, ny, all_sequences, span, HEAD_SIZE) for t in (kv, other))
        gate_up_blocks, kv = together(gate_up_blocks, kv)
        gate_up_weight = over_planes(gate_up_blocks)
    else:
        kv_raw = heads(mm(h1, kv_weight))
        kv = jnp.where(core == 0, rotate(kv_raw, cos_rows, sin_rows), kv_raw).astype(low)
        kv = lax.all_gather(kv, "z", axis=0, tiled=False)
        other = lax.ppermute(kv, "c", [(0, 1), (1, 0)])
    q = rotate(heads(mm(h1, query_weight)), cos_rows, sin_rows).astype(low)
    attend = (core_at, lengths_all, q, kv, other, query_at, key_at)
    (o,) = attention_call(attention_kernel, *attend, (), [("rows", low)], "attention")
    o = o.reshape(-1, HEAD_SIZE)
    r = x_in + team_sum([o], [out_weight], 4)

    normed_two, inverse_two = rms_forward(r, norm_gains[1])
    h2 = team_gather(normed_two.astype(low), 16)
    dyb = team_gather(outer_grad.astype(low), 15, [h2])
    down_blocks, down_weight = spread(feed_weight, take_feed(2), ff_part, 12, [dyb])
    gate_up_weight, down_blocks = together(gate_up_weight, down_blocks)
    both = mm(h2, gate_up_weight)
    gate, upward = both[:, :ff_part], both[:, ff_part:]
    sig = jax.nn.sigmoid(gate)
    m = (gate * sig * upward).astype(low)
    down_term = mm_tn(dyb, m).astype(low)
    down_rows = scatter_planes(down_term)
    down_weight, down_term = together(down_weight, down_term)
    d_both = feed_back(dyb, down_weight, both)
    gate_up_term = mm_tn(h2, d_both).astype(low)
    gate_up_rows = scatter_planes(gate_up_term)
    dh2 = team_sum([d_both], [gate_up_weight], 7, [gate_up_term, down_term])
    mid_grad, gain_two = rms_back(dh2, r, inverse_two, norm_gains[1])
    dr = outer_grad + mid_grad
    drb = team_gather(dr.astype(low), 13, [down_rows])

    do = heads(mm(drb, out_weight).astype(low))
    dq, keep, theirs = attention_call(
        attention_back_kernel,
        *attend,
        (do, cos_table, sin_table),
        [("rows", low), ("keys", jnp.float32), ("keys", low)],
        "attention_back",
    )
    dq = dq.reshape(-1, HEAD_SIZE)
    dkv = keep + lax.ppermute(theirs, "c", [(0, 1), (1, 0)]).astype(jnp.float32)
    low_terms = dkv.astype(low)
    feed_sum = team_sum([m], [down_weight], 5, [low_terms])
    down_grad = scatter_team(down_rows, 6, [low_terms])
    layer_output = (r + feed_sum).astype(low)
    local_squares = sum(jnp.sum(jnp.square(part.astype(jnp.float32))) for part in (gate_up_rows, down_rows))
    query_term, out_term = mm_tn(h1, dq).astype(low), mm_tn(drb, o).astype(low)
    low_terms, gate_up_rows, layer_output, down_grad, query_term, out_term = together(
        low_terms, gate_up_rows, layer_output, down_grad, query_term, out_term
    )
    if is_square():
        low_terms = low_terms.reshape(nz, -1, HEAD_SIZE)
        dkv, attention_term, gate_up_grad = fall(low_terms, gate_up_rows, h1, query_term, out_term, *tables, nz, 8)
    else:
        dkv = lax.psum_scatter(low_terms, "z", scatter_dimension=0, tiled=True)[0].astype(jnp.float32)
        dkv = jnp.where(core == 0, rotate(dkv, cos_rows, -sin_rows), dkv).astype(low).reshape(-1, HEAD_SIZE)
        attention_term = jnp.concatenate([query_term, mm_tn(h1, dkv).astype(low), out_term], axis=1)
        gate_up_grad = scatter_team(gate_up_rows, 8)
    attention_rows = scatter_planes(attention_term)
    dh1 = team_sum([dq, dkv], [query_weight, kv_weight], 9, [attention_term])
    in_grad, gain_one = rms_back(dh1, x_in, inverse_one, norm_gains[0])
    input_gradient = dr + in_grad
    gain_local = jnp.stack([gain_one, gain_two]).reshape(-1, 128)
    lines = jnp.concatenate([gain_local, jnp.full((8, 128), local_squares)], axis=0)
    if is_square():
        lines = total_sum(lines, nz, 18)
        attention_grad, tile = turn(attention_rows, 10, (), nz)
    else:
        lines = lax.psum(lines, ALL)
        attention_grad = scatter_team(attention_rows, 10)
        tile = lax.psum(jnp.full((8, 128), jnp.sum(jnp.square(attention_rows.astype(jnp.float32)))), ALL)
    gain_grad = lines[:-8].reshape(2, width)
    news = update(
        (lines, tile, gain_grad),
        (gate_up_grad, down_grad, attention_grad),
        (norm_gains, gain_mean, gain_square),
        (feed_weight, feed_mean, feed_square),
        (attention_weight, attention_mean, attention_square),
    )
    gains_new, gradient_norm, feed_new, attention_new = news[:3], news[3], news[4:8], news[8:]
    return (
        layer_output.reshape(sequences, span, width),
        input_gradient.reshape(sequences, span, width),
        gradient_norm.reshape(()),
        *attention_new,
        *feed_new,
        *gains_new,
    )


def solution(mesh):
    ctx, fsdp = mesh.shape["ctx"], mesh.shape["fsdp"]
    inner = QUERY_HEADS // fsdp
    fine = Mesh(mesh.devices.reshape(ctx // inner, inner, fsdp // 2, 2), ALL)
    act = P(("x", "c"), ("z", "y"), None)
    matrix = P(ALL, None)
    return jax.shard_map(
        local,
        mesh=fine,
        in_specs=(act, P(("x", "c")), P(), matrix, matrix, act, matrix, matrix, matrix, matrix, P(), P()),
        out_specs=(act, act, P(), matrix, matrix, matrix, matrix, matrix, matrix, matrix, matrix, P(), P(), P()),
        check_vma=False,
    )
```

```python
import functools

import jax
import jax.numpy as jnp
from jax import lax
from jax.experimental import pallas as pl
from jax.experimental.pallas import tpu as pltpu
from jax.sharding import Mesh, PartitionSpec as P

QUERY_HEADS = 8
KEY_VALUE_HEADS = 4
HEAD_SIZE = 256
FF = 8192
STEP = 10

norm_eps = 1e-06
rope_base = 1000042.0
masked_value = -1e30
clip_norm = 1.0
beta_one = 0.9
beta_two = 0.95
adam_eps = 1e-08
matrix_rate = 0.03
gain_rate = 0.4
weight_decay = 0.1

TEAM = ("y", "x", "c")
ALL = ("z", "y", "x", "c")


MESH = pl.DeviceIdType.MESH
VMEM = pl.BlockSpec(memory_space=pltpu.VMEM)
HBM = pl.BlockSpec(memory_space=pl.ANY)


def place():
    y, x, c = lax.axis_index("y"), lax.axis_index("x"), lax.axis_index("c")
    return y, x, c, lambda yy, xx, cc: (yy * 2 + xx) * 2 + cc


def hail(others):
    barrier = pltpu.get_barrier_semaphore()
    for other in others:
        pl.semaphore_signal(barrier, inc=1, device_id=other, device_id_type=MESH)
    return lambda: pl.semaphore_wait(barrier, len(others))


def greet(others):
    hail(others)()


def gather_kernel(src, *refs):
    out, send, recv, own = refs[-4:]
    y, x, c, index = place()
    to_x, to_y, to_s = {"x": 1 - x}, {"y": 1 - y}, {"c": 1 - c}
    me, at_x, at_y, at_d = index(y, x, c), index(y, 1 - x, c), index(1 - y, x, c), index(1 - y, 1 - x, c)
    half = src.shape[0] // 2
    rows = (pl.ds(0, half), pl.ds(half, half))
    local = pltpu.make_async_copy(src, out.at[me], own)
    local.start()
    greet((to_x, to_y, to_s))

    def hop(slot, block, part, where, first=False):
        piece = out.at[block, rows[part]]
        return pltpu.make_async_remote_copy(
            src_ref=src.at[rows[part]] if first else piece,
            dst_ref=piece,
            send_sem=send.at[slot],
            recv_sem=recv.at[slot],
            device_id=where,
            device_id_type=MESH,
        )

    x0, x1 = hop(0, me, 0, to_x, True), hop(1, me, 1, to_x, True)
    y1, y0 = hop(2, me, 1, to_y, True), hop(3, me, 0, to_y, True)
    s0, s1 = hop(4, me, 0, to_s, True), hop(5, me, 1, to_s, True)
    for copy in (x0, y1, x1, y0, s0, s1):
        copy.start()
    x0.wait_recv()
    d0 = hop(6, at_x, 0, to_y)
    d0.start()
    y1.wait_recv()
    d1 = hop(7, at_y, 1, to_x)
    d1.start()
    sx0, sy1 = hop(8, at_x, 0, to_s), hop(9, at_y, 1, to_s)
    sx0.start()
    sy1.start()
    x1.wait_recv()
    sx1 = hop(10, at_x, 1, to_s)
    sx1.start()
    y0.wait_recv()
    sy0 = hop(11, at_y, 0, to_s)
    sy0.start()
    d0.wait_recv()
    sd0 = hop(12, at_d, 0, to_s)
    sd0.start()
    d1.wait_recv()
    sd1 = hop(13, at_d, 1, to_s)
    sd1.start()
    for copy in (s0, s1, sx0, sy1, sx1, sy0, sd0, sd1):
        copy.wait_recv()
    for copy in (x0, x1, y0, y1, s0, s1, d0, d1, sx0, sy1, sx1, sy0, sd0, sd1):
        copy.wait_send()
    local.wait()


def plane_gather(value, number, after=()):
    return pl.pallas_call(
        gather_kernel,
        out_shape=jax.ShapeDtypeStruct((8, *value.shape), value.dtype),
        in_specs=[HBM] * (1 + len(after)),
        out_specs=HBM,
        scratch_shapes=[
            pltpu.SemaphoreType.DMA((14,)),
            pltpu.SemaphoreType.DMA((14,)),
            pltpu.SemaphoreType.DMA,
        ],
        compiler_params=pltpu.CompilerParams(collective_id=number, has_side_effects=True),
        cost_estimate=pl.CostEstimate(flops=1, bytes_accessed=1, transcendentals=0),
        name="plane_gather",
    )(value, *after)


def sum_kernel(lefts, terms, tile, *refs):
    a_refs, w_refs = refs[:lefts], refs[lefts : lefts + len(terms)]
    out, s_send, s_recv, d_send, d_recv, x_send, x_recv, y_send, y_recv, x_acc, y_acc, send, recv = refs[-13:]
    y, x, c, index = place()
    to_x, to_y, to_s = {"x": 1 - x}, {"y": 1 - y}, {"c": 1 - c}
    rows, width = out.shape
    half = rows // 2
    parts = (pl.ds(0, half), pl.ds(half, half))
    f32, low = jnp.float32, jnp.bfloat16

    def product(block, put):
        lines = pl.ds(pl.multiple_of(block * rows, rows), rows)

        @pl.loop(0, width // tile)
        def _(step):
            cols = pl.ds(pl.multiple_of(step * tile, tile), tile)
            total = None
            for (left, start), w_ref in zip(terms, w_refs):
                term = mm_nt(a_refs[left][lines, start : start + w_ref.shape[1]], w_ref[cols, :])
                total = term if total is None else total + term
            put(cols, total)

    def hop(slot, src, dst, where):
        copy = pltpu.make_async_remote_copy(
            src_ref=src, dst_ref=dst, send_sem=send.at[slot], recv_sem=recv.at[slot],
            device_id=where, device_id_type=MESH,
        )
        return copy

    def to_sibling(slot, yy, xx):
        def put(cols, total):
            s_send[slot, :, cols] = total.astype(low)

        product(index(yy, xx, 1 - c), put)
        copy = hop(slot, s_send.at[slot], s_recv.at[slot], to_s)
        copy.start()
        return copy

    def with_sibling(slot, yy, xx, keep):
        def put(cols, total):
            keep[:, cols] = (total + s_recv[slot, :, cols].astype(f32)).astype(keep.dtype)

        product(index(yy, xx, c), put)

    greet((to_x, to_y, to_s))
    s0 = to_sibling(0, 1 - y, 1 - x)
    s1 = to_sibling(1, y, 1 - x)
    s0.wait_recv()
    with_sibling(0, 1 - y, 1 - x, d_send)
    d0 = hop(4, d_send.at[parts[0]], d_recv.at[parts[0]], to_x)
    d1 = hop(5, d_send.at[parts[1]], d_recv.at[parts[1]], to_y)
    d0.start()
    d1.start()
    s1.wait_recv()
    with_sibling(1, y, 1 - x, x_acc)
    x_send[parts[0]] = x_acc[parts[0]].astype(low)
    x0 = hop(6, x_send.at[parts[0]], x_recv.at[parts[0]], to_x)
    x0.start()
    s2 = to_sibling(2, 1 - y, x)
    s2.wait_recv()
    with_sibling(2, 1 - y, x, y_acc)
    y_send[parts[1]] = y_acc[parts[1]].astype(low)
    y1 = hop(7, y_send.at[parts[1]], y_recv.at[parts[1]], to_y)
    y1.start()
    s3 = to_sibling(3, y, x)
    d1.wait_recv()
    x_send[parts[1]] = (x_acc[parts[1]] + d_recv[parts[1]].astype(f32)).astype(low)
    x1 = hop(8, x_send.at[parts[1]], x_recv.at[parts[1]], to_x)
    x1.start()
    d0.wait_recv()
    y_send[parts[0]] = (y_acc[parts[0]] + d_recv[parts[0]].astype(f32)).astype(low)
    y0 = hop(9, y_send.at[parts[0]], y_recv.at[parts[0]], to_y)
    y0.start()
    s3.wait_recv()
    with_sibling(3, y, x, out)
    x0.wait_recv()
    y1.wait_recv()
    x1.wait_recv()
    y0.wait_recv()
    out[...] += x_recv[...].astype(f32) + y_recv[...].astype(f32)
    for copy in (s0, s1, s2, s3, d0, d1, x0, x1, y0, y1):
        copy.wait_send()


def plane_sum(lefts, rights, number, after=(), tile=512):
    ends = [(left, start) for left, a in enumerate(lefts) for start in range(0, a.shape[1], rights[0].shape[1])]
    terms = tuple(ends[: len(rights)])
    rows, width = lefts[0].shape[0] // 8, rights[0].shape[0]
    block = (rows, width)
    low, f32 = jnp.bfloat16, jnp.float32
    return pl.pallas_call(
        functools.partial(sum_kernel, len(lefts), terms, min(tile, width)),
        out_shape=jax.ShapeDtypeStruct(block, f32),
        in_specs=[VMEM] * (len(lefts) + len(rights)) + [HBM] * len(after),
        out_specs=VMEM,
        scratch_shapes=[
            pltpu.VMEM((4, *block), low),
            pltpu.VMEM((4, *block), low),
            *[pltpu.VMEM(block, low)] * 6,
            pltpu.VMEM(block, f32),
            pltpu.VMEM(block, f32),
            pltpu.SemaphoreType.DMA((10,)),
            pltpu.SemaphoreType.DMA((10,)),
        ],
        compiler_params=pltpu.CompilerParams(
            collective_id=number, has_side_effects=True, vmem_limit_bytes=48 * 2**20
        ),
        cost_estimate=pl.CostEstimate(flops=1, bytes_accessed=1, transcendentals=0),
        name="plane_sum",
    )(*lefts, *rights, *after)


def swap_kernel(pieces, takes, *refs):
    count = len(pieces)
    sources, (send, recv, own) = refs[: -2 * count - 3], refs[-3:]
    outs, holds = refs[-2 * count - 3 : -count - 3], refs[-count - 3 : -3]
    y, x, c, index = place()
    me = index(y, x, c)
    flips = [(fy, fx, fc) for fy, fx in ((1, 1), (0, 1), (1, 0), (0, 0)) for fc in (0, 1)]
    flips = [flip for flip in flips if flip != (0, 0, 0)]

    def there(flip):
        return tuple(1 - at if f else at for at, f in zip((y, x, c), flip))

    greet([dict(zip(("y", "x", "c"), there(flip))) for flip in flips])
    copies = []
    for piece in range(count):
        for number, flip in enumerate(flips):
            yy, xx, cc = there(flip)
            member = index(yy, xx, cc)
            holds[piece][number] = takes[piece](sources, member, cc)
            copy = pltpu.make_async_remote_copy(
                src_ref=holds[piece].at[number],
                dst_ref=outs[piece].at[me],
                send_sem=send.at[piece * 7 + number],
                recv_sem=recv.at[piece * 7 + number],
                device_id={"y": yy, "x": xx, "c": cc},
                device_id_type=MESH,
            )
            copy.start()
            copies.append(copy)
        holds[piece][7] = takes[piece](sources, me, c)
        keep = pltpu.make_async_copy(holds[piece].at[7], outs[piece].at[me], own.at[piece])
        keep.start()
        copies.append(keep)
    for copy in copies:
        copy.wait()


def plane_swap(sources, shapes, takes, number, after=()):
    low = jnp.bfloat16
    count = len(shapes)
    return pl.pallas_call(
        functools.partial(swap_kernel, shapes, takes),
        out_shape=[jax.ShapeDtypeStruct((8, *shape), low) for shape in shapes],
        in_specs=[VMEM] * len(sources) + [HBM] * len(after),
        out_specs=[HBM] * count,
        scratch_shapes=[
            *[pltpu.VMEM((8, *shape), low) for shape in shapes],
            pltpu.SemaphoreType.DMA((7 * count,)),
            pltpu.SemaphoreType.DMA((7 * count,)),
            pltpu.SemaphoreType.DMA((count,)),
        ],
        compiler_params=pltpu.CompilerParams(
            collective_id=number, has_side_effects=True, vmem_limit_bytes=48 * 2**20
        ),
        cost_estimate=pl.CostEstimate(flops=1, bytes_accessed=1, transcendentals=0),
        name="plane_swap",
    )(*sources, *after)


def team_of(y, x, c):
    flips = [(fy, fx, fc) for fy, fx in ((1, 1), (0, 1), (1, 0), (0, 0)) for fc in (0, 1)]
    return [
        tuple(1 - at if f else at for at, f in zip((y, x, c), flip)) for flip in flips if flip != (0, 0, 0)
    ]


def turn_kernel(planes, src, *refs):
    y, x, c, index = place()
    me = index(y, x, c)
    others = team_of(y, x, c)
    ids = [dict(zip(("y", "x", "c"), other)) for other in others]
    if planes:
        out, total, near, far, held, send, recv, own, send_lines, recv_lines = refs[-10:]
        z = lax.axis_index("z")
        column = [{"z": lax.rem(z + step, planes)} for step in range(1, planes)]
        fetch = pltpu.make_async_copy(src, held, own.at[1])
        fetch.start()
    else:
        out, send, recv, own = refs[-4:]
        column = []
    ready = hail(ids + column)
    if planes:
        fetch.wait()
        squares = jnp.zeros((8, held.shape[1]), jnp.float32)
        for start in range(0, held.shape[0], 64):
            part = held[start : start + 64].astype(jnp.float32)
            squares += jnp.sum(jnp.square(part).reshape(8, 8, -1), axis=0)
        near[me] = jnp.broadcast_to(jnp.sum(squares, keepdims=True), near.shape[1:])
    ready()
    count = src.shape[0] // 8

    def rows(member):
        return src.at[pl.ds(pl.multiple_of(member * count, count), count)]

    def spread(buffer, at, where, base):
        copies = [
            pltpu.make_async_remote_copy(
                src_ref=buffer.at[at],
                dst_ref=buffer.at[at],
                send_sem=send_lines.at[base + number],
                recv_sem=recv_lines.at[base + number],
                device_id=other,
                device_id_type=MESH,
            )
            for number, other in enumerate(where)
        ]
        for copy in copies:
            copy.start()
        return copies

    copies = [
        pltpu.make_async_remote_copy(
            src_ref=rows(index(*other)),
            dst_ref=out.at[me],
            send_sem=send.at[number],
            recv_sem=recv.at[number],
            device_id=where,
            device_id_type=MESH,
        )
        for number, (other, where) in enumerate(zip(others, ids))
    ]
    copies.append(pltpu.make_async_copy(rows(me), out.at[me], own.at[0]))
    small = spread(near, me, ids, 0) if planes else []
    for copy in copies:
        copy.start()
    if planes:
        for copy in small:
            copy.wait()
        far[z] = jnp.sum(near[...], axis=0)
        for copy in spread(far, z, column, 7):
            copy.wait()
        total[...] = jnp.sum(far[...], axis=0)
    for copy in copies:
        copy.wait()


def total_kernel(planes, src, *refs):
    out, near, far, send, recv = refs[-5:]
    y, x, c, index = place()
    z = lax.axis_index("z")
    ids = [dict(zip(("y", "x", "c"), other)) for other in team_of(y, x, c)]
    column = [{"z": lax.rem(z + step, planes)} for step in range(1, planes)]
    me = index(y, x, c)
    near[me] = src[...]
    greet(ids + column)

    def spread(buffer, at, where, base):
        copies = [
            pltpu.make_async_remote_copy(
                src_ref=buffer.at[at],
                dst_ref=buffer.at[at],
                send_sem=send.at[base + number],
                recv_sem=recv.at[base + number],
                device_id=other,
                device_id_type=MESH,
            )
            for number, other in enumerate(where)
        ]
        for copy in copies:
            copy.start()
        for copy in copies:
            copy.wait()

    spread(near, me, ids, 0)
    far[z] = jnp.sum(near[...], axis=0)
    spread(far, z, column, 7)
    out[...] = jnp.sum(far[...], axis=0)


def total_sum(value, planes, number, after=()):
    return pl.pallas_call(
        functools.partial(total_kernel, planes),
        out_shape=jax.ShapeDtypeStruct(value.shape, value.dtype),
        in_specs=[VMEM] + [HBM] * len(after),
        out_specs=VMEM,
        scratch_shapes=[pltpu.VMEM((size, *value.shape), value.dtype) for size in (8, planes)]
        + [pltpu.SemaphoreType.DMA((6 + planes,))] * 2,
        compiler_params=pltpu.CompilerParams(
            collective_id=number, has_side_effects=True, vmem_limit_bytes=16 * 2**20
        ),
        cost_estimate=pl.CostEstimate(flops=1, bytes_accessed=1, transcendentals=0),
        name="total_sum",
    )(value, *after)


def turn(rows, number, after=(), planes=0):
    block = (rows.shape[0] // 8, rows.shape[1])
    dma = pltpu.SemaphoreType.DMA
    out_shape, out_specs = [jax.ShapeDtypeStruct((8, *block), rows.dtype)], [HBM]
    scratch = [dma((7,)), dma((7,)), dma((2,))]
    if planes:
        tile = jax.ShapeDtypeStruct((8, 128), jnp.float32)
        out_shape.append(tile)
        out_specs.append(VMEM)
        buffers = [pltpu.VMEM((size, *tile.shape), tile.dtype) for size in (8, planes)]
        scratch = buffers + [pltpu.VMEM(rows.shape, rows.dtype)] + scratch + [dma((6 + planes,)), dma((6 + planes,))]
    return pl.pallas_call(
        functools.partial(turn_kernel, planes),
        out_shape=out_shape,
        in_specs=[HBM] * (1 + len(after)),
        out_specs=out_specs,
        scratch_shapes=scratch,
        compiler_params=pltpu.CompilerParams(
            collective_id=number, has_side_effects=True, vmem_limit_bytes=56 * 2**20
        ),
        cost_estimate=pl.CostEstimate(flops=1, bytes_accessed=1, transcendentals=0),
        name="turn",
    )(rows, *after)


def hops(planes, send, recv, block, up):
    z = lax.axis_index("z")

    def step(number):
        gone, came = (z - number + 1, z - number) if up else (z + number - 1, z + number)
        goes = ((gone >= 0) & (z + 1 < planes)) if up else ((gone < planes) & (z >= 1))
        comes = (came >= 0) if up else (came < planes)

        def copy(b):
            return pltpu.make_async_remote_copy(
                src_ref=block(b),
                dst_ref=block(b),
                send_sem=send.at[number - 1],
                recv_sem=recv.at[number - 1],
                device_id={"z": z + 1 if up else z - 1},
                device_id_type=MESH,
            )

        return (
            lambda: pl.when(goes)(lambda: copy(gone).start()),
            lambda: pl.when(comes)(lambda: copy(came).wait_recv()),
            lambda: pl.when(goes)(lambda: copy(gone).wait_send()),
        )

    return [step(number) for number in range(1, planes)]


def ring(planes):
    z = lax.axis_index("z")
    return [{"z": lax.rem(z + 1, planes)}, {"z": lax.rem(z + planes - 1, planes)}]


def spread_to(others, ids, source, take, hold, place_of, send, recv, own, ready=None):
    y, x, c, index = place()
    me = index(y, x, c)
    copies = []
    if ready is not None:
        for number, other in enumerate(others):
            hold[number] = take([source], index(*other), other[2])
        ready()
    for number, (other, where) in enumerate(zip(others, ids)):
        if ready is None:
            hold[number] = take([source], index(*other), other[2])
        copy = pltpu.make_async_remote_copy(
            src_ref=hold.at[number], dst_ref=place_of(me), send_sem=send.at[number], recv_sem=recv.at[number],
            device_id=where, device_id_type=MESH,
        )
        copy.start()
        copies.append(copy)
    hold[7] = take([source], me, c)
    keep = pltpu.make_async_copy(hold.at[7], place_of(me), own)
    keep.start()
    return copies, keep


def begin_kernel(
    planes, take, take_feed, attention, feed, tokens_from, gain, all_attention, all_rows, columns,
    tokens, held, hold, feed_held, feed_hold, rows, a_send, a_recv, f_send, f_recv, r_send, r_recv, u_send, u_recv, d_send, d_recv, own,
):
    y, x, c, index = place()
    z = lax.axis_index("z")
    me, at_x, at_y, at_d = index(y, x, c), index(y, 1 - x, c), index(1 - y, x, c), index(1 - y, 1 - x, c)
    others = team_of(y, x, c)
    ids = [dict(zip(("y", "x", "c"), other)) for other in others]
    to_x, to_y, to_s = {"x": 1 - x}, {"y": 1 - y}, {"c": 1 - c}
    count = held.shape[0]
    half = rows.shape[0] // 2
    parts = (pl.ds(0, half), pl.ds(half, half))
    fetch = pltpu.make_async_copy(attention, held, own.at[0])
    fetch.start()
    fetch_tokens = pltpu.make_async_copy(tokens_from, tokens, own.at[5])
    fetch_tokens.start()
    fetch_feed = pltpu.make_async_copy(feed.at[:, pl.ds(0, feed_held.shape[1])], feed_held, own.at[3])
    fetch_feed.start()
    ready = hail(ids + ring(planes))
    fetch.wait()

    def attention_rows(start, size):
        return all_attention.at[pl.ds(pl.multiple_of(start, count), size)]

    a_copies, a_keep = spread_to(
        others, ids, held, take, hold, lambda m: attention_rows((z * 8 + m) * count, count), a_send, a_recv, own.at[1], ready
    )

    def hop(slot, block, part, where, first=False):
        piece = all_rows.at[block, parts[part]]
        copy = pltpu.make_async_remote_copy(
            src_ref=rows.at[parts[part]] if first else piece, dst_ref=piece,
            send_sem=r_send.at[slot], recv_sem=r_recv.at[slot], device_id=where, device_id_type=MESH,
        )
        copy.start()
        return copy

    for copy in a_copies:
        copy.wait_recv()
    a_keep.wait()

    def plane_block(b):
        return attention_rows(b * 8 * count, 8 * count)

    up = hops(planes, u_send, u_recv, plane_block, True)
    down = hops(planes, d_send, d_recv, plane_block, False)

    def pass_on(number):
        if number > 0:
            up[number - 1][1]()
            down[number - 1][1]()
        if number < planes - 1:
            up[number][0]()
            down[number][0]()

    pass_on(0)
    fetch_tokens.wait()

    @pl.loop(0, rows.shape[0] // 16)
    def _(group):
        lines = pl.ds(pl.multiple_of(group * 16, 16), 16)
        rows[lines] = rms_forward(tokens[lines].astype(jnp.float32), gain[...])[0].astype(rows.dtype)

    x0, y1 = hop(0, me, 0, to_x, True), hop(2, me, 1, to_y, True)
    x1, y0 = hop(1, me, 1, to_x, True), hop(3, me, 0, to_y, True)
    s0, s1 = hop(4, me, 0, to_s, True), hop(5, me, 1, to_s, True)
    mine = pltpu.make_async_copy(rows, all_rows.at[me], own.at[2])
    mine.start()
    x0.wait_recv()
    d0 = hop(6, at_x, 0, to_y)
    y1.wait_recv()
    d1 = hop(7, at_y, 1, to_x)
    sx0, sy1 = hop(8, at_x, 0, to_s), hop(9, at_y, 1, to_s)
    fetch_feed.wait()
    f_copies, f_keep = spread_to(
        others, ids, feed_held, take_feed, feed_hold, lambda m: columns.at[m], f_send, f_recv, own.at[4]
    )
    pass_on(1)
    x1.wait_recv()
    sx1 = hop(10, at_x, 1, to_s)
    y0.wait_recv()
    sy0 = hop(11, at_y, 0, to_s)
    pass_on(2)
    d0.wait_recv()
    sd0 = hop(12, at_d, 0, to_s)
    d1.wait_recv()
    sd1 = hop(13, at_d, 1, to_s)
    for number in range(3, planes):
        pass_on(number)
    for copy in (s0, s1, sx0, sy1, sx1, sy0, sd0, sd1, *f_copies):
        copy.wait_recv()
    for copy in (x0, x1, y0, y1, s0, s1, d0, d1, sx0, sy1, sx1, sy0, sd0, sd1, *a_copies, *f_copies):
        copy.wait_send()
    for step in up + down:
        step[2]()
    mine.wait()
    f_keep.wait()


def begin(attention, feed, tokens, gain, takes, widths, planes, number):
    low, dma = jnp.bfloat16, pltpu.SemaphoreType.DMA
    count = attention.shape[0]
    return pl.pallas_call(
        functools.partial(begin_kernel, planes, *takes),
        out_shape=[
            jax.ShapeDtypeStruct((planes * 8 * count, widths[0]), low),
            jax.ShapeDtypeStruct((8, *tokens.shape), low),
            jax.ShapeDtypeStruct((8, count, widths[1]), low),
        ],
        in_specs=[HBM, HBM, HBM, VMEM],
        out_specs=[HBM] * 3,
        scratch_shapes=[
            pltpu.VMEM(tokens.shape, tokens.dtype),
            pltpu.VMEM(attention.shape, attention.dtype),
            pltpu.VMEM((8, count, widths[0]), low),
            pltpu.VMEM((count, 8 * widths[1]), feed.dtype),
            pltpu.VMEM((8, count, widths[1]), low),
            pltpu.VMEM(tokens.shape, low),
            *[dma((size,)) for size in (7, 7, 7, 7, 14, 14, *[planes - 1] * 4, 6)],
        ],
        compiler_params=pltpu.CompilerParams(
            collective_id=number, has_side_effects=True, vmem_limit_bytes=54 * 2**20
        ),
        cost_estimate=pl.CostEstimate(flops=1, bytes_accessed=1, transcendentals=0),
        name="begin",
    )(attention, feed, tokens, gain)


def turned(value, cos_table, sin_table):
    half = value.shape[1] // 2
    first, second = value[:, :half], value[:, half:]
    return jnp.concatenate([first * cos_table - second * sin_table, second * cos_table + first * sin_table], axis=1)


def climb_kernel(
    planes, rows, weights, cos, sin, mine, other, weight, held, zeros, stay, u_send, u_recv, s_send, s_recv, own, fill, move
):
    z, c = lax.axis_index("z"), lax.axis_index("c")
    to_s = {"c": 1 - c}
    barrier = pltpu.get_barrier_semaphore()
    for where in [to_s] + ring(planes):
        pl.semaphore_signal(barrier, inc=1, device_id=where, device_id_type=MESH)
    count, (sides, span) = rows.shape[0], cos.shape[:2]
    size = 512
    pull_weight = pltpu.make_async_copy(
        weights.at[:, pl.ds(weight.shape[1], weight.shape[1])], weight, move.at[count // size]
    )
    pull_weight.start()
    pulls = [
        pltpu.make_async_copy(rows.at[pl.ds(start, size)], held.at[pl.ds(start, size)], move.at[start // size])
        for start in range(0, count, size)
    ]
    for copy in pulls:
        copy.start()
    pull_weight.wait()
    for start in range(0, count, size):
        pulls[start // size].wait()
        value = mm(held[start : start + size], weight[...])
        for line in range(0, size, span):
            side = (start + line) // (count // sides)
            part = value[line : line + span]
            part = jnp.where(c == 0, turned(part, cos[side], sin[side]), part)
            stay[start + line : start + line + span] = part.astype(stay.dtype)
    zeros[...] = jnp.zeros_like(zeros)
    pl.semaphore_wait(barrier, 3)

    def across(n):
        return pltpu.make_async_remote_copy(
            src_ref=stay if n == 0 else mine.at[n], dst_ref=other.at[n], send_sem=s_send.at[n], recv_sem=s_recv.at[n],
            device_id=to_s, device_id_type=MESH,
        )

    def along(n):
        return pltpu.make_async_remote_copy(
            src_ref=stay if n == 1 else mine.at[n - 1], dst_ref=mine.at[n], send_sem=u_send.at[n - 1], recv_sem=u_recv.at[n - 1],
            device_id={"z": z + 1}, device_id_type=MESH,
        )

    def fills(n):
        return [
            pltpu.make_async_copy(zeros, buffer.at[n], fill.at[2 * (n - 1) + number])
            for number, buffer in enumerate((mine, other))
        ]

    keep = pltpu.make_async_copy(stay, mine.at[0], own)
    more = z + 1 < planes
    pl.when(more)(lambda: along(1).start())
    across(0).start()
    keep.start()
    for n in range(1, planes):

        @pl.when(z < n)
        def _():
            for copy in fills(n):
                copy.start()

    for n in range(1, planes):

        @pl.when(z >= n)
        def _():
            along(n).wait_recv()
            if n + 1 < planes:
                pl.when(more)(lambda: along(n + 1).start())
            across(n).start()

    across(0).wait()
    keep.wait()
    for n in range(1, planes):

        @pl.when(z >= n)
        def _():
            across(n).wait()

        @pl.when(z < n)
        def _():
            for copy in fills(n):
                copy.wait()

        pl.when((z >= n - 1) & more)(lambda: along(n).wait_send())


def climb(rows, weights, cos, sin, planes, number):
    dma = pltpu.SemaphoreType.DMA
    block = (rows.shape[0], weights.shape[1] // 3)
    blocks = jax.ShapeDtypeStruct((planes, *block), rows.dtype)
    return pl.pallas_call(
        functools.partial(climb_kernel, planes),
        out_shape=[blocks, blocks],
        in_specs=[HBM] * 2 + [VMEM] * 2,
        out_specs=[HBM] * 2,
        scratch_shapes=[
            pltpu.VMEM((weights.shape[0], block[1]), rows.dtype),
            pltpu.VMEM(rows.shape, rows.dtype),
            pltpu.VMEM(block, rows.dtype),
            pltpu.VMEM(block, rows.dtype),
            *[dma((size,)) for size in (planes - 1, planes - 1, planes, planes)],
            dma,
            dma((2 * (planes - 1),)),
            dma((rows.shape[0] // 512 + 1,)),
        ],
        compiler_params=pltpu.CompilerParams(
            collective_id=number, has_side_effects=True, vmem_limit_bytes=56 * 2**20
        ),
        cost_estimate=pl.CostEstimate(flops=1, bytes_accessed=1, transcendentals=0),
        name="climb",
    )(rows, weights, cos, sin)


def fall_kernel(
    planes, terms_from, rows, left_from, query_term, out_term, cos, sin, value, term, blocks,
    terms, left, sends, recvs, total, first, held, send, recv, t_send, t_recv, own, move, fetch,
):
    y, x, c, index = place()
    z = lax.axis_index("z")
    me = index(y, x, c)
    others = team_of(y, x, c)
    ids = [dict(zip(("y", "x", "c"), other)) for other in others]
    f32 = jnp.float32
    count = rows.shape[0] // 8
    size = terms.shape[2]
    given = ((query_term, 0), (out_term, 2))
    pulls = [pltpu.make_async_copy(ref, held.at[n], move.at[n]) for n, (ref, _) in enumerate(given)]
    get_terms = pltpu.make_async_copy(terms_from, terms, fetch.at[0])
    get_terms.start()
    get_left = pltpu.make_async_copy(left_from, left, fetch.at[1])
    get_left.start()
    for copy in pulls:
        copy.start()
    greet(ids + ring(planes))
    get_terms.wait()

    def rows_of(member):
        return rows.at[pl.ds(pl.multiple_of(member * count, count), count)]

    half = terms.shape[1] // 2
    parts = [pl.ds(n * half, half) for n in range(2)]

    def hop(step, n):
        slot = 2 * (step - 1) + n
        return pltpu.make_async_remote_copy(
            src_ref=sends.at[step - 1, parts[n]], dst_ref=recvs.at[step - 1, parts[n]],
            send_sem=send.at[slot], recv_sem=recv.at[slot], device_id={"z": z - 1}, device_id_type=MESH,
        )

    def came(step):
        return (z + 1 < planes) & (z + 1 + step - planes >= 0)

    copies = [
        pltpu.make_async_remote_copy(
            src_ref=rows_of(index(*other)), dst_ref=blocks.at[me], send_sem=t_send.at[number], recv_sem=t_recv.at[number],
            device_id=where, device_id_type=MESH,
        )
        for number, (other, where) in enumerate(zip(others, ids))
    ]
    copies.append(pltpu.make_async_copy(rows_of(me), blocks.at[me], own))
    pushes = []
    for step in range(1, planes):
        block = z + step - planes
        for n in range(2):
            lines = parts[n]
            if step > 1:
                pl.when(came(step - 1))(lambda: hop(step - 1, n).wait_recv())

            @pl.when((block >= 0) & (z + 1 == planes))
            def _():
                sends[step - 1, lines] = terms[block, lines]

            if step > 1:

                @pl.when((block >= 0) & (z + 1 < planes))
                def _():
                    added = terms[block, lines].astype(f32) + recvs[step - 2, lines].astype(f32)
                    sends[step - 1, lines] = added.astype(terms.dtype)

            pl.when(block >= 0)(lambda: hop(step, n).start())
        if step == 1:
            for copy in copies:
                copy.start()
            total[...] = terms[z].astype(f32)
            for n, (_, column) in enumerate(given):
                pulls[n].wait()
                pushes.append(
                    pltpu.make_async_copy(held.at[n], term.at[:, pl.ds(column * size, size)], move.at[2 + n])
                )
                pushes[-1].start()
    last = planes - 1
    sides, span = cos.shape[:2]
    get_left.wait()
    for n in range(2):
        lines = parts[n]

        @pl.when(came(last))
        def _():
            hop(last, n).wait_recv()
            total[lines] += recvs[last - 1, lines].astype(f32)

        for line in range(n * half, (n + 1) * half, span):
            side = line // (total.shape[0] // sides)
            part = total[line : line + span]
            part = jnp.where(c == 0, turned(part, cos[side], -sin[side]), part)
            value[line : line + span] = part.astype(value.dtype)
        upright = value[lines].astype(f32).T.astype(value.dtype)
        for start in range(0, left.shape[1], 512):
            columns = pl.ds(start, 512)
            made = mm(upright, left[lines, columns])
            if n == 0:
                first[:, columns] = made
                continue
            held[2, columns] = (first[:, columns] + made).T.astype(held.dtype)
            pushes.append(
                pltpu.make_async_copy(
                    held.at[2, columns], term.at[columns, pl.ds(size, size)], move.at[4 + start // 512]
                )
            )
            pushes[-1].start()
    for step in range(1, planes):
        for n in range(2):
            pl.when(z + step - planes >= 0)(lambda: hop(step, n).wait_send())
    for copy in copies + pushes:
        copy.wait()


def fall(terms, rows, left, query_term, out_term, cos, sin, planes, number):
    block = terms.shape[1:]
    dma, low = pltpu.SemaphoreType.DMA, terms.dtype
    return pl.pallas_call(
        functools.partial(fall_kernel, planes),
        out_shape=[
            jax.ShapeDtypeStruct(block, low),
            jax.ShapeDtypeStruct((left.shape[1], 3 * block[1]), low),
            jax.ShapeDtypeStruct((8, rows.shape[0] // 8, rows.shape[1]), low),
        ],
        in_specs=[HBM] * 5 + [VMEM] * 2,
        out_specs=[VMEM, HBM, HBM],
        scratch_shapes=[pltpu.VMEM(terms.shape, low), pltpu.VMEM(left.shape, low)]
        + [pltpu.VMEM((planes - 1, *block), low)] * 2
        + [pltpu.VMEM(block, jnp.float32), pltpu.VMEM((block[1], left.shape[1]), jnp.float32)]
        + [pltpu.VMEM((3, left.shape[1], block[1]), low)]
        + [dma((2 * (planes - 1),))] * 2
        + [dma((7,)), dma((7,)), dma, dma((4 + left.shape[1] // 512,)), dma((2,))],
        compiler_params=pltpu.CompilerParams(
            collective_id=number, has_side_effects=True, vmem_limit_bytes=56 * 2**20
        ),
        cost_estimate=pl.CostEstimate(flops=1, bytes_accessed=1, transcendentals=0),
        name="fall",
    )(terms, rows, left, query_term, out_term, cos, sin)


def dot(left, right, contract):
    return lax.dot_general(left, right, (contract, ((), ())), preferred_element_type=jnp.float32)


def mm(left, right):
    return dot(left, right, ((1,), (0,)))


def mm_nt(left, right):
    return dot(left, right, ((1,), (1,)))


def mm_tn(left, right):
    return dot(left, right, ((0,), (0,)))


def bmm(pattern, left, right):
    return jnp.einsum(pattern, left, right, preferred_element_type=jnp.float32)


def angle_tables(positions):
    half_dim = HEAD_SIZE // 2
    frequency = rope_base ** (-(jnp.arange(half_dim).astype(jnp.float32) * 2.0) / HEAD_SIZE)
    phases = positions.astype(jnp.float32)[:, None] * frequency[None, :]
    return (jnp.cos(phases), jnp.sin(phases))


def rotate(value, cos_table, sin_table):
    half = value.shape[-1] // 2
    a, b = value[..., :half], value[..., half:]
    return jnp.concatenate([a * cos_table - b * sin_table, b * cos_table + a * sin_table], axis=-1)


def rms_forward(value, gain_row):
    inverse = lax.rsqrt(jnp.mean(value * value, axis=-1, keepdims=True) + norm_eps)
    return (value * inverse * gain_row, inverse)


def rms_back(grad_out, value, inverse, gain_row):
    scaled = grad_out * gain_row
    grad_in = inverse * (
        scaled - value * inverse * inverse * jnp.mean(scaled * value, axis=-1, keepdims=True)
    )
    return (grad_in, jnp.sum(grad_out * value * inverse, axis=0))


def adamw(weight, gradient, moment_one, moment_two, step_rate, decay_rate, invert=jnp.reciprocal):
    mean_new = beta_one * moment_one + (1.0 - beta_one) * gradient
    square_new = beta_two * moment_two + (1.0 - beta_two) * gradient * gradient
    below = jnp.sqrt(square_new * (1.0 / (1.0 - beta_two**STEP))) + adam_eps
    direction = mean_new * (1.0 / (1.0 - beta_one**STEP)) * invert(below)
    return (weight - step_rate * (direction + decay_rate * weight), mean_new, square_new)


def attention_parts(core, length, q_ref, mine_ref, other_ref, query_ref, key_ref):
    mine, other = mine_ref[...].reshape(-1, HEAD_SIZE), other_ref[...].reshape(-1, HEAD_SIZE)
    first = core == 0
    k, v = jnp.where(first, mine, other), jnp.where(first, other, mine)
    q = q_ref[...].reshape(-1, HEAD_SIZE)
    at, key_at = query_ref[...], key_ref[...]
    allowed = (key_at <= at) & (key_at < length) & (key_at >= 0)
    scores = jnp.where(allowed, mm_nt(q, k) * HEAD_SIZE ** (-0.5), masked_value)
    exponent = jnp.exp(scores - jnp.max(scores, axis=-1, keepdims=True))
    return q, k, v, exponent / jnp.sum(exponent, axis=-1, keepdims=True)


def attention_kernel(core_ref, length_ref, q_ref, mine_ref, other_ref, query_ref, key_ref, out_ref):
    length = length_ref[pl.program_id(0)]
    _, _, v, soft = attention_parts(core_ref[0], length, q_ref, mine_ref, other_ref, query_ref, key_ref)
    out_ref[...] = mm(soft.astype(jnp.bfloat16), v).astype(jnp.bfloat16).reshape(out_ref.shape)


def attention_back_kernel(
    core_ref, length_ref, q_ref, mine_ref, other_ref, query_ref, key_ref, do_ref, cos_ref, sin_ref,
    dq_ref, keep_ref, send_ref,
):
    low = jnp.bfloat16
    core = core_ref[0]
    length = length_ref[pl.program_id(0)]
    q, k, v, soft = attention_parts(core, length, q_ref, mine_ref, other_ref, query_ref, key_ref)
    do = do_ref[...].reshape(-1, HEAD_SIZE)
    dp = mm_nt(do, v)
    delta = jnp.sum(soft * dp, axis=-1, keepdims=True)
    ds = (soft * (dp - delta) * HEAD_SIZE ** (-0.5)).astype(low)
    dq = mm(ds, k)
    cos_table, sin_table = cos_ref[...], sin_ref[...]
    half = HEAD_SIZE // 2
    a, b = dq[:, :half], dq[:, half:]
    turned = jnp.concatenate([a * cos_table + b * sin_table, b * cos_table - a * sin_table], axis=-1)
    dq_ref[...] = turned.astype(low).reshape(dq_ref.shape)
    dk, dv = mm_tn(ds, q), mm_tn(soft.astype(low), do)
    first = core == 0
    keep, send = (t.reshape(keep_ref.shape) for t in (jnp.where(first, dk, dv), jnp.where(first, dv, dk)))
    for block in range(keep_ref.shape[0]):
        at = core_ref[1 + block]
        keep_ref[at] = keep[block]
        send_ref[at] = send[block].astype(low)


def attention_call(kernel, core, lengths, q, mine, other, query_pos, key_pos, extra, outs, name):
    ny, count, span, size = q.shape
    nz = mine.shape[0]
    rows = pl.BlockSpec((ny, 1, span, size), lambda i, *_: (0, i, 0, 0))
    keys = pl.BlockSpec((nz, ny, 1, span, size), lambda i, *_: (0, 0, i, 0, 0))

    def whole(value):
        return pl.BlockSpec(value.shape, lambda i, *_: (0,) * value.ndim)

    kinds = {"rows": (rows, q.shape), "keys": (keys, mine.shape)}
    return pl.pallas_call(
        kernel,
        grid_spec=pltpu.PrefetchScalarGridSpec(
            num_scalar_prefetch=2,
            grid=(count,),
            in_specs=[rows, keys, keys, whole(query_pos), whole(key_pos)]
            + [rows if value.shape == q.shape else whole(value) for value in extra],
            out_specs=[kinds[kind][0] for kind, _ in outs],
        ),
        out_shape=[jax.ShapeDtypeStruct(kinds[kind][1], dtype) for kind, dtype in outs],
        compiler_params=pltpu.CompilerParams(vmem_limit_bytes=48 * 2**20),
        cost_estimate=pl.CostEstimate(flops=1, bytes_accessed=1, transcendentals=0),
        name=name,
    )(core, lengths, q, mine, other, query_pos, key_pos, *extra)


def feed_back_kernel(dyb_ref, weight_ref, gate_ref, up_ref, out_ref):
    dm = mm(dyb_ref[...], weight_ref[...])
    gate, upward = gate_ref[...], up_ref[...]
    sig = jax.nn.sigmoid(gate)
    part = gate.shape[1]
    out_ref[:, :part] = (dm * upward * sig * (1.0 + gate * (1.0 - sig))).astype(out_ref.dtype)
    out_ref[:, part:] = (dm * gate * sig).astype(out_ref.dtype)


def feed_back(dyb, weight, both, lines=256):
    count, part = both.shape[0], both.shape[1] // 2

    def rows(width, column=0):
        return pl.BlockSpec((lines, width), lambda i: (i, column))

    return pl.pallas_call(
        feed_back_kernel,
        grid=(count // lines,),
        in_specs=[rows(dyb.shape[1]), pl.BlockSpec(weight.shape, lambda i: (0, 0)), rows(part), rows(part, 1)],
        out_specs=rows(2 * part),
        out_shape=jax.ShapeDtypeStruct((count, 2 * part), jnp.bfloat16),
        compiler_params=pltpu.CompilerParams(vmem_limit_bytes=48 * 2**20),
        cost_estimate=pl.CostEstimate(flops=1, bytes_accessed=1, transcendentals=0),
        name="feed_back",
    )(dyb, weight, both, both)


def close_reciprocal(value):
    guess = pltpu.reciprocal(value, approx=True)
    return guess * (2.0 - value * guess)


def norm_of(lines_ref, tile_ref):
    gains = lines_ref[:-8]
    return jnp.sqrt(jnp.sum(gains * gains, keepdims=True) + lines_ref[-8:-7, 0:1] + tile_ref[0:1, 0:1])


def update_kernel(*refs):
    lines_ref, tile_ref, gain_ref, gate_up_ref, down_ref, attention_ref = refs[:6]
    gains, feed, attention = refs[6:9], refs[9:12], refs[12:15]
    new_gains, norm_ref, new_feed, new_attention, factor_ref = refs[15:18], refs[18], refs[19:23], refs[23:27], refs[27]
    rows = feed[0].shape[0]
    lines = pl.ds(pl.multiple_of(pl.program_id(0) * rows, rows), rows)

    @pl.when((pl.program_id(0) == 0) & (pl.program_id(1) == 0))
    def _():
        norm = norm_of(lines_ref, tile_ref)
        norm_ref[...] = norm
        factor_ref[...] = clip_norm / norm
        weight, mean, square = (ref[...] for ref in gains)
        gradient = gain_ref[...] * factor_ref[...]
        for ref, value in zip(new_gains, adamw(weight, gradient, mean, square, gain_rate, 0.0)):
            ref[...] = value

    factor = factor_ref[...]

    def piece(olds, news, grad_ref, member, start, column, size):
        at = pl.ds(pl.multiple_of(column, size), size)
        gradient = grad_ref[member, lines, pl.ds(start, size)].astype(jnp.float32) * factor
        weight, mean, square = (ref[:, at] for ref in olds)
        values = adamw(weight, gradient, mean, square, matrix_rate, weight_decay, close_reciprocal)
        for ref, value in zip(news, (*values, values[0])):
            ref[:, at] = value.astype(ref.dtype)

    part = down_ref.shape[2]
    size = min(part, 512)

    def run(grad_ref, start, first, count, column):
        @pl.loop(0, count)
        def _(number):
            for offset in range(0, part, size):
                piece(feed, new_feed, grad_ref, first + number, start + offset, column + number * part + offset, size)

    @pl.when(pl.program_id(1) == 0)
    def _():
        run(gate_up_ref, 0, 0, 8, 0)
        run(gate_up_ref, part, 0, 4, 8 * part)

        @pl.loop(0, 8)
        def _(member):
            core = lax.rem(member, 2)
            kv_column = (8 + 4 * core + lax.div(member, 2)) * HEAD_SIZE
            for number, column in enumerate((member * HEAD_SIZE, kv_column, (16 + member) * HEAD_SIZE)):
                piece(attention, new_attention, attention_ref, member, number * HEAD_SIZE, column, HEAD_SIZE)

    @pl.when(pl.program_id(1) == 1)
    def _():
        run(gate_up_ref, part, 4, 4, 0)
        run(down_ref, 0, 0, 8, 4 * part)


def update(sums, grads, gains, feed, attention):
    f32, low = jnp.float32, jnp.bfloat16
    rows = min(feed[0].shape[0], 16)

    def some(value):
        if value.shape[1] == feed[0].shape[1]:
            return pl.BlockSpec((rows, value.shape[1] // 2), lambda i, j: (i, j))
        return pl.BlockSpec((rows, value.shape[1]), lambda i, j: (i, 0))

    def whole(value):
        return pl.BlockSpec(value.shape, lambda i, j: (0,) * value.ndim)

    norm = jax.ShapeDtypeStruct((1, 1), f32)
    matrices = [jax.ShapeDtypeStruct(part[0].shape, dtype) for part in (feed, attention) for dtype in (f32, f32, f32, low)]
    return pl.pallas_call(
        update_kernel,
        grid=(feed[0].shape[0] // rows, 2),
        in_specs=[whole(value) for value in (*sums, *grads, *gains)] + [some(value) for value in (*feed, *attention)],
        out_specs=[whole(value) for value in (*gains, norm)] + [some(value) for value in matrices],
        out_shape=[jax.ShapeDtypeStruct(gains[0].shape, f32)] * 3 + [norm] + matrices,
        scratch_shapes=[pltpu.VMEM((1, 1), f32)],
        compiler_params=pltpu.CompilerParams(vmem_limit_bytes=56 * 2**20),
        name="update",
    )(*sums, *grads, *gains, *feed, *attention)


def is_square():
    return lax.axis_size("y") == 2 and lax.axis_size("x") == 2


def swap(blocks):
    return lax.all_to_all(blocks, TEAM, split_axis=0, concat_axis=0, tiled=True)


def over_planes(blocks):
    return lax.all_gather(blocks.reshape(-1, blocks.shape[-1]), "z", axis=0, tiled=True)


def scatter_planes(term):
    return lax.psum_scatter(term, "z", scatter_dimension=0, tiled=True)


def together(*values):
    return lax.optimization_barrier(values)


def scatter_team(rows, number, after=()):
    if not is_square():
        return swap(rows.reshape(8, -1, rows.shape[-1]))
    return turn(rows, number, after)[0]


def team_gather(local, number, after=()):
    if not is_square():
        return lax.all_gather(local, TEAM, axis=0, tiled=True)
    return plane_gather(local, number, after).reshape(-1, local.shape[1])


def team_sum(lefts, rights, number, after=()):
    if is_square():
        return plane_sum(lefts, rights, number, after)
    partial = mm_nt(jnp.concatenate(lefts, axis=1), jnp.concatenate(rights, axis=1))
    return lax.psum_scatter(partial.astype(jnp.bfloat16), TEAM, scatter_dimension=0, tiled=True).astype(jnp.float32)


def local(
    tokens,
    lengths,
    norm_gains,
    attention_weight,
    feed_weight,
    cotangent,
    attention_mean,
    attention_square,
    feed_mean,
    feed_square,
    gain_mean,
    gain_square,
):
    low = jnp.bfloat16
    sequences, span, width = tokens.shape
    ny, nx, nz = lax.axis_size("y"), lax.axis_size("x"), lax.axis_size("z")
    team = ny * nx * 2
    core = lax.axis_index("c")
    rows = attention_weight.shape[0]
    q_width, kv_width = QUERY_HEADS * HEAD_SIZE, KEY_VALUE_HEADS * HEAD_SIZE
    count = sequences * span
    all_sequences = nx * 2 * sequences
    reach = ny * span
    near = is_square()
    ff_part = FF // team

    def columns(start, size):
        return pl.ds(pl.multiple_of(start, size), size)

    def take_attention(sources, member, c):
        source = sources[0]
        starts = (
            member * HEAD_SIZE,
            q_width + c * kv_width + (member - c) // 2 * HEAD_SIZE,
            q_width + 2 * kv_width + member * HEAD_SIZE,
        )
        return jnp.concatenate([source[:, columns(s, HEAD_SIZE)].astype(low) for s in starts], axis=1)

    def take_feed(*parts):
        return lambda sources, member, c: jnp.concatenate(
            [sources[0][:, columns(part * FF + member * ff_part, ff_part)].astype(low) for part in parts], axis=1
        )

    def spread(source, take, size, number, after=()):
        if is_square():
            blocks = plane_swap([source], [(rows, size)], [take], number, after)[0]
        else:
            blocks = swap(jnp.stack([take([source], member, member % 2) for member in range(8)]))
        return blocks, over_planes(blocks)

    team_base = lax.axis_index("z") * reach
    team_pos = team_base + jnp.arange(reach, dtype=jnp.int32)
    own_pos = team_base + lax.axis_index("y") * span + jnp.arange(span, dtype=jnp.int32)
    if near:
        key_pos = jnp.concatenate([team_pos - back * reach for back in range(nz)])
    else:
        key_pos = jnp.arange(nz * reach, dtype=jnp.int32)
    query_at, key_at = team_pos[:, None], key_pos[None, :]
    cos_table, sin_table = angle_tables(team_pos)
    cos_rows, sin_rows = (t.reshape(ny, 1, span, -1) for t in (cos_table, sin_table))
    valid = (own_pos[None, :] < lengths[:, None]).astype(jnp.float32).reshape(count, 1)
    lengths_all = lax.all_gather(lengths, ("x", "c"), axis=0, tiled=True)
    planes = jnp.arange(nz, dtype=jnp.int32)
    if near:
        planes = (lax.axis_index("z") - planes) % nz
    core_at = jnp.concatenate([jnp.reshape(core, (1,)), planes]).astype(jnp.int32)

    def heads(value):
        return value.reshape(ny, all_sequences, span, HEAD_SIZE)

    x_in = tokens.reshape(count, width).astype(jnp.float32)
    normed_one, inverse_one = rms_forward(x_in, norm_gains[0])
    outer_grad = cotangent.reshape(count, width).astype(jnp.float32) * valid
    if is_square():
        attention_mine, h1, gate_up_blocks = begin(
            attention_weight,
            feed_weight,
            tokens.reshape(count, width),
            norm_gains[:1],
            (take_attention, take_feed(0, 1)),
            (3 * HEAD_SIZE, 2 * ff_part),
            nz,
            1,
        )
        h1 = h1.reshape(-1, width)
    else:
        attention_mine = spread(attention_weight, take_attention, 3 * HEAD_SIZE, 1)[1]
        gate_up_blocks, gate_up_weight = spread(feed_weight, take_feed(0, 1), 2 * ff_part, 2)
        h1 = team_gather(normed_one.astype(low), 3)
    query_weight = attention_mine[:, :HEAD_SIZE]
    kv_weight = attention_mine[:, HEAD_SIZE : 2 * HEAD_SIZE]
    out_weight = attention_mine[:, 2 * HEAD_SIZE :]
    tables = [t.reshape(ny, span, -1) for t in (cos_table, sin_table)]
    if is_square():
        kv, other = climb(h1, attention_mine, *tables, nz, 2)
        kv, other = (t.reshape(nz, ny, all_sequences, span, HEAD_SIZE) for t in (kv, other))
        gate_up_blocks, kv = together(gate_up_blocks, kv)
        gate_up_weight = over_planes(gate_up_blocks)
    else:
        kv_raw = heads(mm(h1, kv_weight))
        kv = jnp.where(core == 0, rotate(kv_raw, cos_rows, sin_rows), kv_raw).astype(low)
        kv = lax.all_gather(kv, "z", axis=0, tiled=False)
        other = lax.ppermute(kv, "c", [(0, 1), (1, 0)])
    q = rotate(heads(mm(h1, query_weight)), cos_rows, sin_rows).astype(low)
    attend = (core_at, lengths_all, q, kv, other, query_at, key_at)
    (o,) = attention_call(attention_kernel, *attend, (), [("rows", low)], "attention")
    o = o.reshape(-1, HEAD_SIZE)
    r = x_in + team_sum([o], [out_weight], 4)

    normed_two, inverse_two = rms_forward(r, norm_gains[1])
    h2 = team_gather(normed_two.astype(low), 16)
    dyb = team_gather(outer_grad.astype(low), 15, [h2])
    down_blocks, down_weight = spread(feed_weight, take_feed(2), ff_part, 12, [dyb])
    gate_up_weight, down_blocks = together(gate_up_weight, down_blocks)
    both = mm(h2, gate_up_weight)
    gate, upward = both[:, :ff_part], both[:, ff_part:]
    sig = jax.nn.sigmoid(gate)
    m = (gate * sig * upward).astype(low)
    down_term = mm_tn(dyb, m).astype(low)
    down_rows = scatter_planes(down_term)
    down_weight, down_term = together(down_weight, down_term)
    d_both = feed_back(dyb, down_weight, both)
    gate_up_term = mm_tn(h2, d_both).astype(low)
    gate_up_rows = scatter_planes(gate_up_term)
    dh2 = team_sum([d_both], [gate_up_weight], 7, [gate_up_term, down_term])
    mid_grad, gain_two = rms_back(dh2, r, inverse_two, norm_gains[1])
    dr = outer_grad + mid_grad
    drb = team_gather(dr.astype(low), 13, [down_rows])

    do = heads(mm(drb, out_weight).astype(low))
    dq, keep, theirs = attention_call(
        attention_back_kernel,
        *attend,
        (do, cos_table, sin_table),
        [("rows", low), ("keys", jnp.float32), ("keys", low)],
        "attention_back",
    )
    dq = dq.reshape(-1, HEAD_SIZE)
    dkv = keep + lax.ppermute(theirs, "c", [(0, 1), (1, 0)]).astype(jnp.float32)
    low_terms = dkv.astype(low)
    feed_sum = team_sum([m], [down_weight], 5, [low_terms])
    down_grad = scatter_team(down_rows, 6, [low_terms])
    layer_output = (r + feed_sum).astype(low)
    local_squares = sum(jnp.sum(jnp.square(part.astype(jnp.float32))) for part in (gate_up_rows, down_rows))
    query_term, out_term = mm_tn(h1, dq).astype(low), mm_tn(drb, o).astype(low)
    low_terms, gate_up_rows, layer_output, down_grad, query_term, out_term = together(
        low_terms, gate_up_rows, layer_output, down_grad, query_term, out_term
    )
    if is_square():
        low_terms = low_terms.reshape(nz, -1, HEAD_SIZE)
        dkv, attention_term, gate_up_grad = fall(low_terms, gate_up_rows, h1, query_term, out_term, *tables, nz, 8)
    else:
        dkv = lax.psum_scatter(low_terms, "z", scatter_dimension=0, tiled=True)[0].astype(jnp.float32)
        dkv = jnp.where(core == 0, rotate(dkv, cos_rows, -sin_rows), dkv).astype(low).reshape(-1, HEAD_SIZE)
        attention_term = jnp.concatenate([query_term, mm_tn(h1, dkv).astype(low), out_term], axis=1)
        gate_up_grad = scatter_team(gate_up_rows, 8)
    attention_rows = scatter_planes(attention_term)
    dh1 = team_sum([dq, dkv], [query_weight, kv_weight], 9, [attention_term])
    in_grad, gain_one = rms_back(dh1, x_in, inverse_one, norm_gains[0])
    input_gradient = dr + in_grad
    gain_local = jnp.stack([gain_one, gain_two]).reshape(-1, 128)
    lines = jnp.concatenate([gain_local, jnp.full((8, 128), local_squares)], axis=0)
    if is_square():
        lines = total_sum(lines, nz, 18)
        attention_grad, tile = turn(attention_rows, 10, (), nz)
    else:
        lines = lax.psum(lines, ALL)
        attention_grad = scatter_team(attention_rows, 10)
        tile = lax.psum(jnp.full((8, 128), jnp.sum(jnp.square(attention_rows.astype(jnp.float32)))), ALL)
    gain_grad = lines[:-8].reshape(2, width)
    news = update(
        (lines, tile, gain_grad),
        (gate_up_grad, down_grad, attention_grad),
        (norm_gains, gain_mean, gain_square),
        (feed_weight, feed_mean, feed_square),
        (attention_weight, attention_mean, attention_square),
    )
    gains_new, gradient_norm, feed_new, attention_new = news[:3], news[3], news[4:8], news[8:]
    return (
        layer_output.reshape(sequences, span, width),
        input_gradient.reshape(sequences, span, width),
        gradient_norm.reshape(()),
        *attention_new,
        *feed_new,
        *gains_new,
    )


def solution(mesh):
    ctx, fsdp = mesh.shape["ctx"], mesh.shape["fsdp"]
    inner = QUERY_HEADS // fsdp
    fine = Mesh(mesh.devices.reshape(ctx // inner, inner, fsdp // 2, 2), ALL)
    act = P(("x", "c"), ("z", "y"), None)
    matrix = P(ALL, None)
    return jax.shard_map(
        local,
        mesh=fine,
        in_specs=(act, P(("x", "c")), P(), matrix, matrix, act, matrix, matrix, matrix, matrix, P(), P()),
        out_specs=(act, act, P(), matrix, matrix, matrix, matrix, matrix, matrix, matrix, matrix, P(), P(), P()),
        check_vma=False,
    )
```

```python
import functools

import jax
import jax.numpy as jnp
from jax import lax
from jax.experimental import pallas as pl
from jax.experimental.pallas import tpu as pltpu
from jax.sharding import Mesh, PartitionSpec as P

QUERY_HEADS = 8
KEY_VALUE_HEADS = 4
HEAD_SIZE = 256
FF = 8192
STEP = 10

norm_eps = 1e-06
rope_base = 1000042.0
masked_value = -1e30
clip_norm = 1.0
beta_one = 0.9
beta_two = 0.95
adam_eps = 1e-08
matrix_rate = 0.03
gain_rate = 0.4
weight_decay = 0.1

TEAM = ("y", "x", "c")
ALL = ("z", "y", "x", "c")


MESH = pl.DeviceIdType.MESH
VMEM = pl.BlockSpec(memory_space=pltpu.VMEM)
HBM = pl.BlockSpec(memory_space=pl.ANY)


def place():
    y, x, c = lax.axis_index("y"), lax.axis_index("x"), lax.axis_index("c")
    return y, x, c, lambda yy, xx, cc: (yy * 2 + xx) * 2 + cc


def hail(others):
    barrier = pltpu.get_barrier_semaphore()
    for other in others:
        pl.semaphore_signal(barrier, inc=1, device_id=other, device_id_type=MESH)
    return lambda: pl.semaphore_wait(barrier, len(others))


def greet(others):
    hail(others)()


def gather_kernel(src, *refs):
    out, send, recv, own = refs[-4:]
    y, x, c, index = place()
    to_x, to_y, to_s = {"x": 1 - x}, {"y": 1 - y}, {"c": 1 - c}
    me, at_x, at_y, at_d = index(y, x, c), index(y, 1 - x, c), index(1 - y, x, c), index(1 - y, 1 - x, c)
    half = src.shape[0] // 2
    rows = (pl.ds(0, half), pl.ds(half, half))
    local = pltpu.make_async_copy(src, out.at[me], own)
    local.start()
    greet((to_x, to_y, to_s))

    def hop(slot, block, part, where, first=False):
        piece = out.at[block, rows[part]]
        return pltpu.make_async_remote_copy(
            src_ref=src.at[rows[part]] if first else piece,
            dst_ref=piece,
            send_sem=send.at[slot],
            recv_sem=recv.at[slot],
            device_id=where,
            device_id_type=MESH,
        )

    x0, x1 = hop(0, me, 0, to_x, True), hop(1, me, 1, to_x, True)
    y1, y0 = hop(2, me, 1, to_y, True), hop(3, me, 0, to_y, True)
    s0, s1 = hop(4, me, 0, to_s, True), hop(5, me, 1, to_s, True)
    for copy in (x0, y1, x1, y0, s0, s1):
        copy.start()
    x0.wait_recv()
    d0 = hop(6, at_x, 0, to_y)
    d0.start()
    y1.wait_recv()
    d1 = hop(7, at_y, 1, to_x)
    d1.start()
    sx0, sy1 = hop(8, at_x, 0, to_s), hop(9, at_y, 1, to_s)
    sx0.start()
    sy1.start()
    x1.wait_recv()
    sx1 = hop(10, at_x, 1, to_s)
    sx1.start()
    y0.wait_recv()
    sy0 = hop(11, at_y, 0, to_s)
    sy0.start()
    d0.wait_recv()
    sd0 = hop(12, at_d, 0, to_s)
    sd0.start()
    d1.wait_recv()
    sd1 = hop(13, at_d, 1, to_s)
    sd1.start()
    for copy in (s0, s1, sx0, sy1, sx1, sy0, sd0, sd1):
        copy.wait_recv()
    for copy in (x0, x1, y0, y1, s0, s1, d0, d1, sx0, sy1, sx1, sy0, sd0, sd1):
        copy.wait_send()
    local.wait()


def plane_gather(value, number, after=()):
    return pl.pallas_call(
        gather_kernel,
        out_shape=jax.ShapeDtypeStruct((8, *value.shape), value.dtype),
        in_specs=[HBM] * (1 + len(after)),
        out_specs=HBM,
        scratch_shapes=[
            pltpu.SemaphoreType.DMA((14,)),
            pltpu.SemaphoreType.DMA((14,)),
            pltpu.SemaphoreType.DMA,
        ],
        compiler_params=pltpu.CompilerParams(collective_id=number, has_side_effects=True),
        cost_estimate=pl.CostEstimate(flops=1, bytes_accessed=1, transcendentals=0),
        name="plane_gather",
    )(value, *after)


def sum_kernel(lefts, terms, tile, *refs):
    a_refs, w_refs = refs[:lefts], refs[lefts : lefts + len(terms)]
    out, s_send, s_recv, d_send, d_recv, x_send, x_recv, y_send, y_recv, x_acc, y_acc, send, recv = refs[-13:]
    y, x, c, index = place()
    to_x, to_y, to_s = {"x": 1 - x}, {"y": 1 - y}, {"c": 1 - c}
    rows, width = out.shape
    half = rows // 2
    parts = (pl.ds(0, half), pl.ds(half, half))
    f32, low = jnp.float32, jnp.bfloat16

    def product(block, put):
        lines = pl.ds(pl.multiple_of(block * rows, rows), rows)

        @pl.loop(0, width // tile)
        def _(step):
            cols = pl.ds(pl.multiple_of(step * tile, tile), tile)
            total = None
            for (left, start), w_ref in zip(terms, w_refs):
                term = mm_nt(a_refs[left][lines, start : start + w_ref.shape[1]], w_ref[cols, :])
                total = term if total is None else total + term
            put(cols, total)

    def hop(slot, src, dst, where):
        copy = pltpu.make_async_remote_copy(
            src_ref=src, dst_ref=dst, send_sem=send.at[slot], recv_sem=recv.at[slot],
            device_id=where, device_id_type=MESH,
        )
        return copy

    def to_sibling(slot, yy, xx):
        def put(cols, total):
            s_send[slot, :, cols] = total.astype(low)

        product(index(yy, xx, 1 - c), put)
        copy = hop(slot, s_send.at[slot], s_recv.at[slot], to_s)
        copy.start()
        return copy

    def with_sibling(slot, yy, xx, keep):
        def put(cols, total):
            keep[:, cols] = (total + s_recv[slot, :, cols].astype(f32)).astype(keep.dtype)

        product(index(yy, xx, c), put)

    greet((to_x, to_y, to_s))
    s0 = to_sibling(0, 1 - y, 1 - x)
    s1 = to_sibling(1, y, 1 - x)
    s0.wait_recv()
    with_sibling(0, 1 - y, 1 - x, d_send)
    d0 = hop(4, d_send.at[parts[0]], d_recv.at[parts[0]], to_x)
    d1 = hop(5, d_send.at[parts[1]], d_recv.at[parts[1]], to_y)
    d0.start()
    d1.start()
    s1.wait_recv()
    with_sibling(1, y, 1 - x, x_acc)
    x_send[parts[0]] = x_acc[parts[0]].astype(low)
    x0 = hop(6, x_send.at[parts[0]], x_recv.at[parts[0]], to_x)
    x0.start()
    s2 = to_sibling(2, 1 - y, x)
    s2.wait_recv()
    with_sibling(2, 1 - y, x, y_acc)
    y_send[parts[1]] = y_acc[parts[1]].astype(low)
    y1 = hop(7, y_send.at[parts[1]], y_recv.at[parts[1]], to_y)
    y1.start()
    s3 = to_sibling(3, y, x)
    d1.wait_recv()
    x_send[parts[1]] = (x_acc[parts[1]] + d_recv[parts[1]].astype(f32)).astype(low)
    x1 = hop(8, x_send.at[parts[1]], x_recv.at[parts[1]], to_x)
    x1.start()
    d0.wait_recv()
    y_send[parts[0]] = (y_acc[parts[0]] + d_recv[parts[0]].astype(f32)).astype(low)
    y0 = hop(9, y_send.at[parts[0]], y_recv.at[parts[0]], to_y)
    y0.start()
    s3.wait_recv()
    with_sibling(3, y, x, out)
    x0.wait_recv()
    y1.wait_recv()
    x1.wait_recv()
    y0.wait_recv()
    out[...] += x_recv[...].astype(f32) + y_recv[...].astype(f32)
    for copy in (s0, s1, s2, s3, d0, d1, x0, x1, y0, y1):
        copy.wait_send()


def plane_sum(lefts, rights, number, after=(), tile=512):
    ends = [(left, start) for left, a in enumerate(lefts) for start in range(0, a.shape[1], rights[0].shape[1])]
    terms = tuple(ends[: len(rights)])
    rows, width = lefts[0].shape[0] // 8, rights[0].shape[0]
    block = (rows, width)
    low, f32 = jnp.bfloat16, jnp.float32
    return pl.pallas_call(
        functools.partial(sum_kernel, len(lefts), terms, min(tile, width)),
        out_shape=jax.ShapeDtypeStruct(block, f32),
        in_specs=[VMEM] * (len(lefts) + len(rights)) + [HBM] * len(after),
        out_specs=VMEM,
        scratch_shapes=[
            pltpu.VMEM((4, *block), low),
            pltpu.VMEM((4, *block), low),
            *[pltpu.VMEM(block, low)] * 6,
            pltpu.VMEM(block, f32),
            pltpu.VMEM(block, f32),
            pltpu.SemaphoreType.DMA((10,)),
            pltpu.SemaphoreType.DMA((10,)),
        ],
        compiler_params=pltpu.CompilerParams(
            collective_id=number, has_side_effects=True, vmem_limit_bytes=48 * 2**20
        ),
        cost_estimate=pl.CostEstimate(flops=1, bytes_accessed=1, transcendentals=0),
        name="plane_sum",
    )(*lefts, *rights, *after)


def swap_kernel(pieces, takes, *refs):
    count = len(pieces)
    sources, (send, recv, own) = refs[: -2 * count - 3], refs[-3:]
    outs, holds = refs[-2 * count - 3 : -count - 3], refs[-count - 3 : -3]
    y, x, c, index = place()
    me = index(y, x, c)
    flips = [(fy, fx, fc) for fy, fx in ((1, 1), (0, 1), (1, 0), (0, 0)) for fc in (0, 1)]
    flips = [flip for flip in flips if flip != (0, 0, 0)]

    def there(flip):
        return tuple(1 - at if f else at for at, f in zip((y, x, c), flip))

    greet([dict(zip(("y", "x", "c"), there(flip))) for flip in flips])
    copies = []
    for piece in range(count):
        for number, flip in enumerate(flips):
            yy, xx, cc = there(flip)
            member = index(yy, xx, cc)
            holds[piece][number] = takes[piece](sources, member, cc)
            copy = pltpu.make_async_remote_copy(
                src_ref=holds[piece].at[number],
                dst_ref=outs[piece].at[me],
                send_sem=send.at[piece * 7 + number],
                recv_sem=recv.at[piece * 7 + number],
                device_id={"y": yy, "x": xx, "c": cc},
                device_id_type=MESH,
            )
            copy.start()
            copies.append(copy)
        holds[piece][7] = takes[piece](sources, me, c)
        keep = pltpu.make_async_copy(holds[piece].at[7], outs[piece].at[me], own.at[piece])
        keep.start()
        copies.append(keep)
    for copy in copies:
        copy.wait()


def plane_swap(sources, shapes, takes, number, after=()):
    low = jnp.bfloat16
    count = len(shapes)
    return pl.pallas_call(
        functools.partial(swap_kernel, shapes, takes),
        out_shape=[jax.ShapeDtypeStruct((8, *shape), low) for shape in shapes],
        in_specs=[VMEM] * len(sources) + [HBM] * len(after),
        out_specs=[HBM] * count,
        scratch_shapes=[
            *[pltpu.VMEM((8, *shape), low) for shape in shapes],
            pltpu.SemaphoreType.DMA((7 * count,)),
            pltpu.SemaphoreType.DMA((7 * count,)),
            pltpu.SemaphoreType.DMA((count,)),
        ],
        compiler_params=pltpu.CompilerParams(
            collective_id=number, has_side_effects=True, vmem_limit_bytes=48 * 2**20
        ),
        cost_estimate=pl.CostEstimate(flops=1, bytes_accessed=1, transcendentals=0),
        name="plane_swap",
    )(*sources, *after)


def team_of(y, x, c):
    flips = [(fy, fx, fc) for fy, fx in ((1, 1), (0, 1), (1, 0), (0, 0)) for fc in (0, 1)]
    return [
        tuple(1 - at if f else at for at, f in zip((y, x, c), flip)) for flip in flips if flip != (0, 0, 0)
    ]


def turn_kernel(planes, src, *refs):
    y, x, c, index = place()
    me = index(y, x, c)
    others = team_of(y, x, c)
    ids = [dict(zip(("y", "x", "c"), other)) for other in others]
    if planes:
        out, total, near, far, held, send, recv, own, send_lines, recv_lines = refs[-10:]
        z = lax.axis_index("z")
        column = [{"z": lax.rem(z + step, planes)} for step in range(1, planes)]
        fetch = pltpu.make_async_copy(src, held, own.at[1])
        fetch.start()
    else:
        out, send, recv, own = refs[-4:]
        column = []
    ready = hail(ids + column)
    if planes:
        fetch.wait()
        squares = jnp.zeros((8, held.shape[1]), jnp.float32)
        for start in range(0, held.shape[0], 64):
            part = held[start : start + 64].astype(jnp.float32)
            squares += jnp.sum(jnp.square(part).reshape(8, 8, -1), axis=0)
        near[me] = jnp.broadcast_to(jnp.sum(squares, keepdims=True), near.shape[1:])
    ready()
    count = src.shape[0] // 8

    def rows(member):
        return src.at[pl.ds(pl.multiple_of(member * count, count), count)]

    def spread(buffer, at, where, base):
        copies = [
            pltpu.make_async_remote_copy(
                src_ref=buffer.at[at],
                dst_ref=buffer.at[at],
                send_sem=send_lines.at[base + number],
                recv_sem=recv_lines.at[base + number],
                device_id=other,
                device_id_type=MESH,
            )
            for number, other in enumerate(where)
        ]
        for copy in copies:
            copy.start()
        return copies

    copies = [
        pltpu.make_async_remote_copy(
            src_ref=rows(index(*other)),
            dst_ref=out.at[me],
            send_sem=send.at[number],
            recv_sem=recv.at[number],
            device_id=where,
            device_id_type=MESH,
        )
        for number, (other, where) in enumerate(zip(others, ids))
    ]
    copies.append(pltpu.make_async_copy(rows(me), out.at[me], own.at[0]))
    small = spread(near, me, ids, 0) if planes else []
    for copy in copies:
        copy.start()
    if planes:
        for copy in small:
            copy.wait()
        far[z] = jnp.sum(near[...], axis=0)
        for copy in spread(far, z, column, 7):
            copy.wait()
        total[...] = jnp.sum(far[...], axis=0)
    for copy in copies:
        copy.wait()


def total_kernel(planes, src, *refs):
    out, near, far, send, recv = refs[-5:]
    y, x, c, index = place()
    z = lax.axis_index("z")
    ids = [dict(zip(("y", "x", "c"), other)) for other in team_of(y, x, c)]
    column = [{"z": lax.rem(z + step, planes)} for step in range(1, planes)]
    me = index(y, x, c)
    near[me] = src[...]
    greet(ids + column)

    def spread(buffer, at, where, base):
        copies = [
            pltpu.make_async_remote_copy(
                src_ref=buffer.at[at],
                dst_ref=buffer.at[at],
                send_sem=send.at[base + number],
                recv_sem=recv.at[base + number],
                device_id=other,
                device_id_type=MESH,
            )
            for number, other in enumerate(where)
        ]
        for copy in copies:
            copy.start()
        for copy in copies:
            copy.wait()

    spread(near, me, ids, 0)
    far[z] = jnp.sum(near[...], axis=0)
    spread(far, z, column, 7)
    out[...] = jnp.sum(far[...], axis=0)


def total_sum(value, planes, number, after=()):
    return pl.pallas_call(
        functools.partial(total_kernel, planes),
        out_shape=jax.ShapeDtypeStruct(value.shape, value.dtype),
        in_specs=[VMEM] + [HBM] * len(after),
        out_specs=VMEM,
        scratch_shapes=[pltpu.VMEM((size, *value.shape), value.dtype) for size in (8, planes)]
        + [pltpu.SemaphoreType.DMA((6 + planes,))] * 2,
        compiler_params=pltpu.CompilerParams(
            collective_id=number, has_side_effects=True, vmem_limit_bytes=16 * 2**20
        ),
        cost_estimate=pl.CostEstimate(flops=1, bytes_accessed=1, transcendentals=0),
        name="total_sum",
    )(value, *after)


def turn(rows, number, after=(), planes=0):
    block = (rows.shape[0] // 8, rows.shape[1])
    dma = pltpu.SemaphoreType.DMA
    out_shape, out_specs = [jax.ShapeDtypeStruct((8, *block), rows.dtype)], [HBM]
    scratch = [dma((7,)), dma((7,)), dma((2,))]
    if planes:
        tile = jax.ShapeDtypeStruct((8, 128), jnp.float32)
        out_shape.append(tile)
        out_specs.append(VMEM)
        buffers = [pltpu.VMEM((size, *tile.shape), tile.dtype) for size in (8, planes)]
        scratch = buffers + [pltpu.VMEM(rows.shape, rows.dtype)] + scratch + [dma((6 + planes,)), dma((6 + planes,))]
    return pl.pallas_call(
        functools.partial(turn_kernel, planes),
        out_shape=out_shape,
        in_specs=[HBM] * (1 + len(after)),
        out_specs=out_specs,
        scratch_shapes=scratch,
        compiler_params=pltpu.CompilerParams(
            collective_id=number, has_side_effects=True, vmem_limit_bytes=56 * 2**20
        ),
        cost_estimate=pl.CostEstimate(flops=1, bytes_accessed=1, transcendentals=0),
        name="turn",
    )(rows, *after)


def hops(planes, send, recv, block, up):
    z = lax.axis_index("z")

    def step(number):
        gone, came = (z - number + 1, z - number) if up else (z + number - 1, z + number)
        goes = ((gone >= 0) & (z + 1 < planes)) if up else ((gone < planes) & (z >= 1))
        comes = (came >= 0) if up else (came < planes)

        def copy(b):
            return pltpu.make_async_remote_copy(
                src_ref=block(b),
                dst_ref=block(b),
                send_sem=send.at[number - 1],
                recv_sem=recv.at[number - 1],
                device_id={"z": z + 1 if up else z - 1},
                device_id_type=MESH,
            )

        return (
            lambda: pl.when(goes)(lambda: copy(gone).start()),
            lambda: pl.when(comes)(lambda: copy(came).wait_recv()),
            lambda: pl.when(goes)(lambda: copy(gone).wait_send()),
        )

    return [step(number) for number in range(1, planes)]


def ring(planes):
    z = lax.axis_index("z")
    return [{"z": lax.rem(z + 1, planes)}, {"z": lax.rem(z + planes - 1, planes)}]


def spread_to(others, ids, source, take, hold, place_of, send, recv, own, ready=None):
    y, x, c, index = place()
    me = index(y, x, c)
    copies = []
    if ready is not None:
        for number, other in enumerate(others):
            hold[number] = take([source], index(*other), other[2])
        ready()
    for number, (other, where) in enumerate(zip(others, ids)):
        if ready is None:
            hold[number] = take([source], index(*other), other[2])
        copy = pltpu.make_async_remote_copy(
            src_ref=hold.at[number], dst_ref=place_of(me), send_sem=send.at[number], recv_sem=recv.at[number],
            device_id=where, device_id_type=MESH,
        )
        copy.start()
        copies.append(copy)
    hold[7] = take([source], me, c)
    keep = pltpu.make_async_copy(hold.at[7], place_of(me), own)
    keep.start()
    return copies, keep


def begin_kernel(
    planes, take, take_feed, attention, feed, tokens_from, gain, all_attention, all_rows, columns,
    tokens, held, hold, feed_held, feed_hold, rows, a_send, a_recv, f_send, f_recv, r_send, r_recv, u_send, u_recv, d_send, d_recv, own,
):
    y, x, c, index = place()
    z = lax.axis_index("z")
    me, at_x, at_y, at_d = index(y, x, c), index(y, 1 - x, c), index(1 - y, x, c), index(1 - y, 1 - x, c)
    others = team_of(y, x, c)
    ids = [dict(zip(("y", "x", "c"), other)) for other in others]
    to_x, to_y, to_s = {"x": 1 - x}, {"y": 1 - y}, {"c": 1 - c}
    count = held.shape[0]
    half = rows.shape[0] // 2
    parts = (pl.ds(0, half), pl.ds(half, half))
    fetch = pltpu.make_async_copy(attention, held, own.at[0])
    fetch.start()
    fetch_tokens = pltpu.make_async_copy(tokens_from, tokens, own.at[5])
    fetch_tokens.start()
    fetch_feed = pltpu.make_async_copy(feed.at[:, pl.ds(0, feed_held.shape[1])], feed_held, own.at[3])
    fetch_feed.start()
    ready = hail(ids + ring(planes))
    fetch.wait()

    def attention_rows(start, size):
        return all_attention.at[pl.ds(pl.multiple_of(start, count), size)]

    a_copies, a_keep = spread_to(
        others, ids, held, take, hold, lambda m: attention_rows((z * 8 + m) * count, count), a_send, a_recv, own.at[1], ready
    )

    def hop(slot, block, part, where, first=False):
        piece = all_rows.at[block, parts[part]]
        copy = pltpu.make_async_remote_copy(
            src_ref=rows.at[parts[part]] if first else piece, dst_ref=piece,
            send_sem=r_send.at[slot], recv_sem=r_recv.at[slot], device_id=where, device_id_type=MESH,
        )
        copy.start()
        return copy

    for copy in a_copies:
        copy.wait_recv()
    a_keep.wait()

    def plane_block(b):
        return attention_rows(b * 8 * count, 8 * count)

    up = hops(planes, u_send, u_recv, plane_block, True)
    down = hops(planes, d_send, d_recv, plane_block, False)

    def pass_on(number):
        if number > 0:
            up[number - 1][1]()
            down[number - 1][1]()
        if number < planes - 1:
            up[number][0]()
            down[number][0]()

    pass_on(0)
    fetch_tokens.wait()

    @pl.loop(0, rows.shape[0] // 16)
    def _(group):
        lines = pl.ds(pl.multiple_of(group * 16, 16), 16)
        rows[lines] = rms_forward(tokens[lines].astype(jnp.float32), gain[...])[0].astype(rows.dtype)

    x0, y1 = hop(0, me, 0, to_x, True), hop(2, me, 1, to_y, True)
    x1, y0 = hop(1, me, 1, to_x, True), hop(3, me, 0, to_y, True)
    s0, s1 = hop(4, me, 0, to_s, True), hop(5, me, 1, to_s, True)
    mine = pltpu.make_async_copy(rows, all_rows.at[me], own.at[2])
    mine.start()
    x0.wait_recv()
    d0 = hop(6, at_x, 0, to_y)
    y1.wait_recv()
    d1 = hop(7, at_y, 1, to_x)
    sx0, sy1 = hop(8, at_x, 0, to_s), hop(9, at_y, 1, to_s)
    fetch_feed.wait()
    f_copies, f_keep = spread_to(
        others, ids, feed_held, take_feed, feed_hold, lambda m: columns.at[m], f_send, f_recv, own.at[4]
    )
    pass_on(1)
    x1.wait_recv()
    sx1 = hop(10, at_x, 1, to_s)
    y0.wait_recv()
    sy0 = hop(11, at_y, 0, to_s)
    pass_on(2)
    d0.wait_recv()
    sd0 = hop(12, at_d, 0, to_s)
    d1.wait_recv()
    sd1 = hop(13, at_d, 1, to_s)
    for number in range(3, planes):
        pass_on(number)
    for copy in (s0, s1, sx0, sy1, sx1, sy0, sd0, sd1, *f_copies):
        copy.wait_recv()
    for copy in (x0, x1, y0, y1, s0, s1, d0, d1, sx0, sy1, sx1, sy0, sd0, sd1, *a_copies, *f_copies):
        copy.wait_send()
    for step in up + down:
        step[2]()
    mine.wait()
    f_keep.wait()


def begin(attention, feed, tokens, gain, takes, widths, planes, number):
    low, dma = jnp.bfloat16, pltpu.SemaphoreType.DMA
    count = attention.shape[0]
    return pl.pallas_call(
        functools.partial(begin_kernel, planes, *takes),
        out_shape=[
            jax.ShapeDtypeStruct((planes * 8 * count, widths[0]), low),
            jax.ShapeDtypeStruct((8, *tokens.shape), low),
            jax.ShapeDtypeStruct((8, count, widths[1]), low),
        ],
        in_specs=[HBM, HBM, HBM, VMEM],
        out_specs=[HBM] * 3,
        scratch_shapes=[
            pltpu.VMEM(tokens.shape, tokens.dtype),
            pltpu.VMEM(attention.shape, attention.dtype),
            pltpu.VMEM((8, count, widths[0]), low),
            pltpu.VMEM((count, 8 * widths[1]), feed.dtype),
            pltpu.VMEM((8, count, widths[1]), low),
            pltpu.VMEM(tokens.shape, low),
            *[dma((size,)) for size in (7, 7, 7, 7, 14, 14, *[planes - 1] * 4, 6)],
        ],
        compiler_params=pltpu.CompilerParams(
            collective_id=number, has_side_effects=True, vmem_limit_bytes=54 * 2**20
        ),
        cost_estimate=pl.CostEstimate(flops=1, bytes_accessed=1, transcendentals=0),
        name="begin",
    )(attention, feed, tokens, gain)


def turned(value, cos_table, sin_table):
    half = value.shape[1] // 2
    first, second = value[:, :half], value[:, half:]
    return jnp.concatenate([first * cos_table - second * sin_table, second * cos_table + first * sin_table], axis=1)


def climb_kernel(
    planes, rows, weights, cos, sin, mine, other, weight, held, zeros, stay, u_send, u_recv, s_send, s_recv, own, fill, move
):
    z, c = lax.axis_index("z"), lax.axis_index("c")
    to_s = {"c": 1 - c}
    barrier = pltpu.get_barrier_semaphore()
    for where in [to_s] + ring(planes):
        pl.semaphore_signal(barrier, inc=1, device_id=where, device_id_type=MESH)
    count, (sides, span) = rows.shape[0], cos.shape[:2]
    size = 512
    pull_weight = pltpu.make_async_copy(
        weights.at[:, pl.ds(weight.shape[1], weight.shape[1])], weight, move.at[count // size]
    )
    pull_weight.start()
    pulls = [
        pltpu.make_async_copy(rows.at[pl.ds(start, size)], held.at[pl.ds(start, size)], move.at[start // size])
        for start in range(0, count, size)
    ]
    for copy in pulls:
        copy.start()
    pull_weight.wait()
    for start in range(0, count, size):
        pulls[start // size].wait()
        value = mm(held[start : start + size], weight[...])
        for line in range(0, size, span):
            side = (start + line) // (count // sides)
            part = value[line : line + span]
            part = jnp.where(c == 0, turned(part, cos[side], sin[side]), part)
            stay[start + line : start + line + span] = part.astype(stay.dtype)
    zeros[...] = jnp.zeros_like(zeros)
    pl.semaphore_wait(barrier, 3)

    def across(n):
        return pltpu.make_async_remote_copy(
            src_ref=stay if n == 0 else mine.at[n], dst_ref=other.at[n], send_sem=s_send.at[n], recv_sem=s_recv.at[n],
            device_id=to_s, device_id_type=MESH,
        )

    def along(n):
        return pltpu.make_async_remote_copy(
            src_ref=stay if n == 1 else mine.at[n - 1], dst_ref=mine.at[n], send_sem=u_send.at[n - 1], recv_sem=u_recv.at[n - 1],
            device_id={"z": z + 1}, device_id_type=MESH,
        )

    def fills(n):
        return [
            pltpu.make_async_copy(zeros, buffer.at[n], fill.at[2 * (n - 1) + number])
            for number, buffer in enumerate((mine, other))
        ]

    keep = pltpu.make_async_copy(stay, mine.at[0], own)
    more = z + 1 < planes
    pl.when(more)(lambda: along(1).start())
    across(0).start()
    keep.start()
    for n in range(1, planes):

        @pl.when(z < n)
        def _():
            for copy in fills(n):
                copy.start()

    for n in range(1, planes):

        @pl.when(z >= n)
        def _():
            along(n).wait_recv()
            if n + 1 < planes:
                pl.when(more)(lambda: along(n + 1).start())
            across(n).start()

    across(0).wait()
    keep.wait()
    for n in range(1, planes):

        @pl.when(z >= n)
        def _():
            across(n).wait()

        @pl.when(z < n)
        def _():
            for copy in fills(n):
                copy.wait()

        pl.when((z >= n - 1) & more)(lambda: along(n).wait_send())


def climb(rows, weights, cos, sin, planes, number):
    dma = pltpu.SemaphoreType.DMA
    block = (rows.shape[0], weights.shape[1] // 3)
    blocks = jax.ShapeDtypeStruct((planes, *block), rows.dtype)
    return pl.pallas_call(
        functools.partial(climb_kernel, planes),
        out_shape=[blocks, blocks],
        in_specs=[HBM] * 2 + [VMEM] * 2,
        out_specs=[HBM] * 2,
        scratch_shapes=[
            pltpu.VMEM((weights.shape[0], block[1]), rows.dtype),
            pltpu.VMEM(rows.shape, rows.dtype),
            pltpu.VMEM(block, rows.dtype),
            pltpu.VMEM(block, rows.dtype),
            *[dma((size,)) for size in (planes - 1, planes - 1, planes, planes)],
            dma,
            dma((2 * (planes - 1),)),
            dma((rows.shape[0] // 512 + 1,)),
        ],
        compiler_params=pltpu.CompilerParams(
            collective_id=number, has_side_effects=True, vmem_limit_bytes=56 * 2**20
        ),
        cost_estimate=pl.CostEstimate(flops=1, bytes_accessed=1, transcendentals=0),
        name="climb",
    )(rows, weights, cos, sin)


def fall_kernel(
    planes, terms_from, rows, left_from, query_term, out_term, cos, sin, value, term, blocks,
    terms, left, sends, recvs, total, first, held, send, recv, t_send, t_recv, own, move, fetch,
):
    y, x, c, index = place()
    z = lax.axis_index("z")
    me = index(y, x, c)
    others = team_of(y, x, c)
    ids = [dict(zip(("y", "x", "c"), other)) for other in others]
    f32 = jnp.float32
    count = rows.shape[0] // 8
    size = terms.shape[2]
    given = ((query_term, 0), (out_term, 2))
    pulls = [pltpu.make_async_copy(ref, held.at[n], move.at[n]) for n, (ref, _) in enumerate(given)]
    get_terms = pltpu.make_async_copy(terms_from, terms, fetch.at[0])
    get_terms.start()
    get_left = pltpu.make_async_copy(left_from, left, fetch.at[1])
    get_left.start()
    for copy in pulls:
        copy.start()
    greet(ids + ring(planes))
    get_terms.wait()

    def rows_of(member):
        return rows.at[pl.ds(pl.multiple_of(member * count, count), count)]

    half = terms.shape[1] // 2
    parts = [pl.ds(n * half, half) for n in range(2)]

    def hop(step, n):
        slot = 2 * (step - 1) + n
        return pltpu.make_async_remote_copy(
            src_ref=sends.at[step - 1, parts[n]], dst_ref=recvs.at[step - 1, parts[n]],
            send_sem=send.at[slot], recv_sem=recv.at[slot], device_id={"z": z - 1}, device_id_type=MESH,
        )

    def came(step):
        return (z + 1 < planes) & (z + 1 + step - planes >= 0)

    copies = [
        pltpu.make_async_remote_copy(
            src_ref=rows_of(index(*other)), dst_ref=blocks.at[me], send_sem=t_send.at[number], recv_sem=t_recv.at[number],
            device_id=where, device_id_type=MESH,
        )
        for number, (other, where) in enumerate(zip(others, ids))
    ]
    copies.append(pltpu.make_async_copy(rows_of(me), blocks.at[me], own))
    pushes = []
    for step in range(1, planes):
        block = z + step - planes
        for n in range(2):
            lines = parts[n]
            if step > 1:
                pl.when(came(step - 1))(lambda: hop(step - 1, n).wait_recv())

            @pl.when((block >= 0) & (z + 1 == planes))
            def _():
                sends[step - 1, lines] = terms[block, lines]

            if step > 1:

                @pl.when((block >= 0) & (z + 1 < planes))
                def _():
                    added = terms[block, lines].astype(f32) + recvs[step - 2, lines].astype(f32)
                    sends[step - 1, lines] = added.astype(terms.dtype)

            pl.when(block >= 0)(lambda: hop(step, n).start())
        if step == 1:
            for copy in copies:
                copy.start()
            total[...] = terms[z].astype(f32)
            for n, (_, column) in enumerate(given):
                pulls[n].wait()
                pushes.append(
                    pltpu.make_async_copy(held.at[n], term.at[:, pl.ds(column * size, size)], move.at[2 + n])
                )
                pushes[-1].start()
    last = planes - 1
    sides, span = cos.shape[:2]
    get_left.wait()
    for n in range(2):
        lines = parts[n]

        @pl.when(came(last))
        def _():
            hop(last, n).wait_recv()
            total[lines] += recvs[last - 1, lines].astype(f32)

        for line in range(n * half, (n + 1) * half, span):
            side = line // (total.shape[0] // sides)
            part = total[line : line + span]
            part = jnp.where(c == 0, turned(part, cos[side], -sin[side]), part)
            value[line : line + span] = part.astype(value.dtype)
        upright = value[lines].astype(f32).T.astype(value.dtype)
        for start in range(0, left.shape[1], 512):
            columns = pl.ds(start, 512)
            made = mm(upright, left[lines, columns])
            if n == 0:
                first[:, columns] = made
                continue
            held[2, columns] = (first[:, columns] + made).T.astype(held.dtype)
            pushes.append(
                pltpu.make_async_copy(
                    held.at[2, columns], term.at[columns, pl.ds(size, size)], move.at[4 + start // 512]
                )
            )
            pushes[-1].start()
    for step in range(1, planes):
        for n in range(2):
            pl.when(z + step - planes >= 0)(lambda: hop(step, n).wait_send())
    for copy in copies + pushes:
        copy.wait()


def fall(terms, rows, left, query_term, out_term, cos, sin, planes, number):
    block = terms.shape[1:]
    dma, low = pltpu.SemaphoreType.DMA, terms.dtype
    return pl.pallas_call(
        functools.partial(fall_kernel, planes),
        out_shape=[
            jax.ShapeDtypeStruct(block, low),
            jax.ShapeDtypeStruct((left.shape[1], 3 * block[1]), low),
            jax.ShapeDtypeStruct((8, rows.shape[0] // 8, rows.shape[1]), low),
        ],
        in_specs=[HBM] * 5 + [VMEM] * 2,
        out_specs=[VMEM, HBM, HBM],
        scratch_shapes=[pltpu.VMEM(terms.shape, low), pltpu.VMEM(left.shape, low)]
        + [pltpu.VMEM((planes - 1, *block), low)] * 2
        + [pltpu.VMEM(block, jnp.float32), pltpu.VMEM((block[1], left.shape[1]), jnp.float32)]
        + [pltpu.VMEM((3, left.shape[1], block[1]), low)]
        + [dma((2 * (planes - 1),))] * 2
        + [dma((7,)), dma((7,)), dma, dma((4 + left.shape[1] // 512,)), dma((2,))],
        compiler_params=pltpu.CompilerParams(
            collective_id=number, has_side_effects=True, vmem_limit_bytes=56 * 2**20
        ),
        cost_estimate=pl.CostEstimate(flops=1, bytes_accessed=1, transcendentals=0),
        name="fall",
    )(terms, rows, left, query_term, out_term, cos, sin)


def dot(left, right, contract):
    return lax.dot_general(left, right, (contract, ((), ())), preferred_element_type=jnp.float32)


def mm(left, right):
    return dot(left, right, ((1,), (0,)))


def mm_nt(left, right):
    return dot(left, right, ((1,), (1,)))


def mm_tn(left, right):
    return dot(left, right, ((0,), (0,)))


def bmm(pattern, left, right):
    return jnp.einsum(pattern, left, right, preferred_element_type=jnp.float32)


def angle_tables(positions):
    half_dim = HEAD_SIZE // 2
    frequency = rope_base ** (-(jnp.arange(half_dim).astype(jnp.float32) * 2.0) / HEAD_SIZE)
    phases = positions.astype(jnp.float32)[:, None] * frequency[None, :]
    return (jnp.cos(phases), jnp.sin(phases))


def rotate(value, cos_table, sin_table):
    half = value.shape[-1] // 2
    a, b = value[..., :half], value[..., half:]
    return jnp.concatenate([a * cos_table - b * sin_table, b * cos_table + a * sin_table], axis=-1)


def rms_forward(value, gain_row):
    inverse = lax.rsqrt(jnp.mean(value * value, axis=-1, keepdims=True) + norm_eps)
    return (value * inverse * gain_row, inverse)


def rms_back(grad_out, value, inverse, gain_row):
    scaled = grad_out * gain_row
    grad_in = inverse * (
        scaled - value * inverse * inverse * jnp.mean(scaled * value, axis=-1, keepdims=True)
    )
    return (grad_in, jnp.sum(grad_out * value * inverse, axis=0))


def adamw(weight, gradient, moment_one, moment_two, step_rate, decay_rate, invert=jnp.reciprocal):
    mean_new = beta_one * moment_one + (1.0 - beta_one) * gradient
    square_new = beta_two * moment_two + (1.0 - beta_two) * gradient * gradient
    below = jnp.sqrt(square_new * (1.0 / (1.0 - beta_two**STEP))) + adam_eps
    direction = mean_new * (1.0 / (1.0 - beta_one**STEP)) * invert(below)
    return (weight - step_rate * (direction + decay_rate * weight), mean_new, square_new)


def attention_parts(core, length, q_ref, mine_ref, other_ref, query_ref, key_ref):
    mine, other = mine_ref[...].reshape(-1, HEAD_SIZE), other_ref[...].reshape(-1, HEAD_SIZE)
    first = core == 0
    k, v = jnp.where(first, mine, other), jnp.where(first, other, mine)
    q = q_ref[...].reshape(-1, HEAD_SIZE)
    at, key_at = query_ref[...], key_ref[...]
    allowed = (key_at <= at) & (key_at < length) & (key_at >= 0)
    scores = jnp.where(allowed, mm_nt(q, k) * HEAD_SIZE ** (-0.5), masked_value)
    exponent = jnp.exp(scores - jnp.max(scores, axis=-1, keepdims=True))
    return q, k, v, exponent / jnp.sum(exponent, axis=-1, keepdims=True)


def attention_kernel(core_ref, length_ref, q_ref, mine_ref, other_ref, query_ref, key_ref, out_ref):
    length = length_ref[pl.program_id(0)]
    _, _, v, soft = attention_parts(core_ref[0], length, q_ref, mine_ref, other_ref, query_ref, key_ref)
    out_ref[...] = mm(soft.astype(jnp.bfloat16), v).astype(jnp.bfloat16).reshape(out_ref.shape)


def attention_back_kernel(
    core_ref, length_ref, q_ref, mine_ref, other_ref, query_ref, key_ref, do_ref, cos_ref, sin_ref,
    dq_ref, keep_ref, send_ref,
):
    low = jnp.bfloat16
    core = core_ref[0]
    length = length_ref[pl.program_id(0)]
    q, k, v, soft = attention_parts(core, length, q_ref, mine_ref, other_ref, query_ref, key_ref)
    do = do_ref[...].reshape(-1, HEAD_SIZE)
    dp = mm_nt(do, v)
    delta = jnp.sum(soft * dp, axis=-1, keepdims=True)
    ds = (soft * (dp - delta) * HEAD_SIZE ** (-0.5)).astype(low)
    dq = mm(ds, k)
    cos_table, sin_table = cos_ref[...], sin_ref[...]
    half = HEAD_SIZE // 2
    a, b = dq[:, :half], dq[:, half:]
    turned = jnp.concatenate([a * cos_table + b * sin_table, b * cos_table - a * sin_table], axis=-1)
    dq_ref[...] = turned.astype(low).reshape(dq_ref.shape)
    dk, dv = mm_tn(ds, q), mm_tn(soft.astype(low), do)
    first = core == 0
    keep, send = (t.reshape(keep_ref.shape) for t in (jnp.where(first, dk, dv), jnp.where(first, dv, dk)))
    for block in range(keep_ref.shape[0]):
        at = core_ref[1 + block]
        keep_ref[at] = keep[block]
        send_ref[at] = send[block].astype(low)


def attention_call(kernel, core, lengths, q, mine, other, query_pos, key_pos, extra, outs, name):
    ny, count, span, size = q.shape
    nz = mine.shape[0]
    rows = pl.BlockSpec((ny, 1, span, size), lambda i, *_: (0, i, 0, 0))
    keys = pl.BlockSpec((nz, ny, 1, span, size), lambda i, *_: (0, 0, i, 0, 0))

    def whole(value):
        return pl.BlockSpec(value.shape, lambda i, *_: (0,) * value.ndim)

    kinds = {"rows": (rows, q.shape), "keys": (keys, mine.shape)}
    return pl.pallas_call(
        kernel,
        grid_spec=pltpu.PrefetchScalarGridSpec(
            num_scalar_prefetch=2,
            grid=(count,),
            in_specs=[rows, keys, keys, whole(query_pos), whole(key_pos)]
            + [rows if value.shape == q.shape else whole(value) for value in extra],
            out_specs=[kinds[kind][0] for kind, _ in outs],
        ),
        out_shape=[jax.ShapeDtypeStruct(kinds[kind][1], dtype) for kind, dtype in outs],
        compiler_params=pltpu.CompilerParams(vmem_limit_bytes=48 * 2**20),
        cost_estimate=pl.CostEstimate(flops=1, bytes_accessed=1, transcendentals=0),
        name=name,
    )(core, lengths, q, mine, other, query_pos, key_pos, *extra)


def feed_back_kernel(dyb_ref, weight_ref, gate_ref, up_ref, out_ref):
    dm = mm(dyb_ref[...], weight_ref[...])
    gate, upward = gate_ref[...], up_ref[...]
    sig = jax.nn.sigmoid(gate)
    part = gate.shape[1]
    out_ref[:, :part] = (dm * upward * sig * (1.0 + gate * (1.0 - sig))).astype(out_ref.dtype)
    out_ref[:, part:] = (dm * gate * sig).astype(out_ref.dtype)


def feed_back(dyb, weight, both, lines=256):
    count, part = both.shape[0], both.shape[1] // 2

    def rows(width, column=0):
        return pl.BlockSpec((lines, width), lambda i: (i, column))

    return pl.pallas_call(
        feed_back_kernel,
        grid=(count // lines,),
        in_specs=[rows(dyb.shape[1]), pl.BlockSpec(weight.shape, lambda i: (0, 0)), rows(part), rows(part, 1)],
        out_specs=rows(2 * part),
        out_shape=jax.ShapeDtypeStruct((count, 2 * part), jnp.bfloat16),
        compiler_params=pltpu.CompilerParams(vmem_limit_bytes=48 * 2**20),
        cost_estimate=pl.CostEstimate(flops=1, bytes_accessed=1, transcendentals=0),
        name="feed_back",
    )(dyb, weight, both, both)


def close_reciprocal(value):
    guess = pltpu.reciprocal(value, approx=True)
    return guess * (2.0 - value * guess)


def norm_of(lines_ref, tile_ref):
    gains = lines_ref[:-8]
    return jnp.sqrt(jnp.sum(gains * gains, keepdims=True) + lines_ref[-8:-7, 0:1] + tile_ref[0:1, 0:1])


def update_kernel(*refs):
    lines_ref, tile_ref, gain_ref, gate_up_ref, down_ref, attention_ref = refs[:6]
    gains, feed, attention = refs[6:9], refs[9:12], refs[12:15]
    new_gains, norm_ref, new_feed, new_attention, factor_ref = refs[15:18], refs[18], refs[19:23], refs[23:27], refs[27]
    rows = feed[0].shape[0]
    lines = pl.ds(pl.multiple_of(pl.program_id(0) * rows, rows), rows)

    @pl.when(pl.program_id(0) == 0)
    def _():
        norm = norm_of(lines_ref, tile_ref)
        norm_ref[...] = norm
        factor_ref[...] = clip_norm / norm
        weight, mean, square = (ref[...] for ref in gains)
        gradient = gain_ref[...] * factor_ref[...]
        for ref, value in zip(new_gains, adamw(weight, gradient, mean, square, gain_rate, 0.0)):
            ref[...] = value

    factor = factor_ref[...]

    def piece(olds, news, grad_ref, member, start, column, size):
        at = pl.ds(pl.multiple_of(column, size), size)
        gradient = grad_ref[member, lines, pl.ds(start, size)].astype(jnp.float32) * factor
        weight, mean, square = (ref[:, at] for ref in olds)
        values = adamw(weight, gradient, mean, square, matrix_rate, weight_decay, close_reciprocal)
        for ref, value in zip(news, (*values, values[0])):
            ref[:, at] = value.astype(ref.dtype)

    part = down_ref.shape[2]
    size = min(part, 512)

    @pl.loop(0, 8)
    def _(member):
        for offset in range(0, part, size):
            for number, (grad_ref, start) in enumerate(((gate_up_ref, 0), (gate_up_ref, part), (down_ref, 0))):
                column = (number * 8 + member) * part + offset
                piece(feed, new_feed, grad_ref, member, start + offset, column, size)
        core = lax.rem(member, 2)
        kv_column = (8 + 4 * core + lax.div(member, 2)) * HEAD_SIZE
        for number, column in enumerate((member * HEAD_SIZE, kv_column, (16 + member) * HEAD_SIZE)):
            piece(attention, new_attention, attention_ref, member, number * HEAD_SIZE, column, HEAD_SIZE)


def update(sums, grads, gains, feed, attention):
    f32, low = jnp.float32, jnp.bfloat16
    rows = min(feed[0].shape[0], 16)

    def some(value):
        return pl.BlockSpec((rows, value.shape[1]), lambda i: (i, 0))

    def whole(value):
        return pl.BlockSpec(value.shape, lambda i: (0,) * value.ndim)

    norm = jax.ShapeDtypeStruct((1, 1), f32)
    matrices = [jax.ShapeDtypeStruct(part[0].shape, dtype) for part in (feed, attention) for dtype in (f32, f32, f32, low)]
    return pl.pallas_call(
        update_kernel,
        grid=(feed[0].shape[0] // rows,),
        in_specs=[whole(value) for value in (*sums, *grads, *gains)] + [some(value) for value in (*feed, *attention)],
        out_specs=[whole(value) for value in (*gains, norm)] + [some(value) for value in matrices],
        out_shape=[jax.ShapeDtypeStruct(gains[0].shape, f32)] * 3 + [norm] + matrices,
        scratch_shapes=[pltpu.VMEM((1, 1), f32)],
        compiler_params=pltpu.CompilerParams(vmem_limit_bytes=56 * 2**20),
        name="update",
    )(*sums, *grads, *gains, *feed, *attention)


def is_square():
    return lax.axis_size("y") == 2 and lax.axis_size("x") == 2


def swap(blocks):
    return lax.all_to_all(blocks, TEAM, split_axis=0, concat_axis=0, tiled=True)


def over_planes(blocks):
    return lax.all_gather(blocks.reshape(-1, blocks.shape[-1]), "z", axis=0, tiled=True)


def scatter_planes(term):
    return lax.psum_scatter(term, "z", scatter_dimension=0, tiled=True)


def together(*values):
    return lax.optimization_barrier(values)


def scatter_team(rows, number, after=()):
    if not is_square():
        return swap(rows.reshape(8, -1, rows.shape[-1]))
    return turn(rows, number, after)[0]


def team_gather(local, number, after=()):
    if not is_square():
        return lax.all_gather(local, TEAM, axis=0, tiled=True)
    return plane_gather(local, number, after).reshape(-1, local.shape[1])


def team_sum(lefts, rights, number, after=()):
    if is_square():
        return plane_sum(lefts, rights, number, after)
    partial = mm_nt(jnp.concatenate(lefts, axis=1), jnp.concatenate(rights, axis=1))
    return lax.psum_scatter(partial.astype(jnp.bfloat16), TEAM, scatter_dimension=0, tiled=True).astype(jnp.float32)


def local(
    tokens,
    lengths,
    norm_gains,
    attention_weight,
    feed_weight,
    cotangent,
    attention_mean,
    attention_square,
    feed_mean,
    feed_square,
    gain_mean,
    gain_square,
):
    low = jnp.bfloat16
    sequences, span, width = tokens.shape
    ny, nx, nz = lax.axis_size("y"), lax.axis_size("x"), lax.axis_size("z")
    team = ny * nx * 2
    core = lax.axis_index("c")
    rows = attention_weight.shape[0]
    q_width, kv_width = QUERY_HEADS * HEAD_SIZE, KEY_VALUE_HEADS * HEAD_SIZE
    count = sequences * span
    all_sequences = nx * 2 * sequences
    reach = ny * span
    near = is_square()
    ff_part = FF // team

    def columns(start, size):
        return pl.ds(pl.multiple_of(start, size), size)

    def take_attention(sources, member, c):
        source = sources[0]
        starts = (
            member * HEAD_SIZE,
            q_width + c * kv_width + (member - c) // 2 * HEAD_SIZE,
            q_width + 2 * kv_width + member * HEAD_SIZE,
        )
        return jnp.concatenate([source[:, columns(s, HEAD_SIZE)].astype(low) for s in starts], axis=1)

    def take_feed(*parts):
        return lambda sources, member, c: jnp.concatenate(
            [sources[0][:, columns(part * FF + member * ff_part, ff_part)].astype(low) for part in parts], axis=1
        )

    def spread(source, take, size, number, after=()):
        if is_square():
            blocks = plane_swap([source], [(rows, size)], [take], number, after)[0]
        else:
            blocks = swap(jnp.stack([take([source], member, member % 2) for member in range(8)]))
        return blocks, over_planes(blocks)

    team_base = lax.axis_index("z") * reach
    team_pos = team_base + jnp.arange(reach, dtype=jnp.int32)
    own_pos = team_base + lax.axis_index("y") * span + jnp.arange(span, dtype=jnp.int32)
    if near:
        key_pos = jnp.concatenate([team_pos - back * reach for back in range(nz)])
    else:
        key_pos = jnp.arange(nz * reach, dtype=jnp.int32)
    query_at, key_at = team_pos[:, None], key_pos[None, :]
    cos_table, sin_table = angle_tables(team_pos)
    cos_rows, sin_rows = (t.reshape(ny, 1, span, -1) for t in (cos_table, sin_table))
    valid = (own_pos[None, :] < lengths[:, None]).astype(jnp.float32).reshape(count, 1)
    lengths_all = lax.all_gather(lengths, ("x", "c"), axis=0, tiled=True)
    planes = jnp.arange(nz, dtype=jnp.int32)
    if near:
        planes = (lax.axis_index("z") - planes) % nz
    core_at = jnp.concatenate([jnp.reshape(core, (1,)), planes]).astype(jnp.int32)

    def heads(value):
        return value.reshape(ny, all_sequences, span, HEAD_SIZE)

    x_in = tokens.reshape(count, width).astype(jnp.float32)
    normed_one, inverse_one = rms_forward(x_in, norm_gains[0])
    outer_grad = cotangent.reshape(count, width).astype(jnp.float32) * valid
    if is_square():
        attention_mine, h1, gate_up_blocks = begin(
            attention_weight,
            feed_weight,
            tokens.reshape(count, width),
            norm_gains[:1],
            (take_attention, take_feed(0, 1)),
            (3 * HEAD_SIZE, 2 * ff_part),
            nz,
            1,
        )
        h1 = h1.reshape(-1, width)
    else:
        attention_mine = spread(attention_weight, take_attention, 3 * HEAD_SIZE, 1)[1]
        gate_up_blocks, gate_up_weight = spread(feed_weight, take_feed(0, 1), 2 * ff_part, 2)
        h1 = team_gather(normed_one.astype(low), 3)
    query_weight = attention_mine[:, :HEAD_SIZE]
    kv_weight = attention_mine[:, HEAD_SIZE : 2 * HEAD_SIZE]
    out_weight = attention_mine[:, 2 * HEAD_SIZE :]
    tables = [t.reshape(ny, span, -1) for t in (cos_table, sin_table)]
    if is_square():
        kv, other = climb(h1, attention_mine, *tables, nz, 2)
        kv, other = (t.reshape(nz, ny, all_sequences, span, HEAD_SIZE) for t in (kv, other))
        gate_up_blocks, kv = together(gate_up_blocks, kv)
        gate_up_weight = over_planes(gate_up_blocks)
    else:
        kv_raw = heads(mm(h1, kv_weight))
        kv = jnp.where(core == 0, rotate(kv_raw, cos_rows, sin_rows), kv_raw).astype(low)
        kv = lax.all_gather(kv, "z", axis=0, tiled=False)
        other = lax.ppermute(kv, "c", [(0, 1), (1, 0)])
    q = rotate(heads(mm(h1, query_weight)), cos_rows, sin_rows).astype(low)
    attend = (core_at, lengths_all, q, kv, other, query_at, key_at)
    (o,) = attention_call(attention_kernel, *attend, (), [("rows", low)], "attention")
    o = o.reshape(-1, HEAD_SIZE)
    r = x_in + team_sum([o], [out_weight], 4)

    normed_two, inverse_two = rms_forward(r, norm_gains[1])
    h2 = team_gather(normed_two.astype(low), 16)
    dyb = team_gather(outer_grad.astype(low), 15, [h2])
    down_blocks, down_weight = spread(feed_weight, take_feed(2), ff_part, 12, [dyb])
    gate_up_weight, down_blocks = together(gate_up_weight, down_blocks)
    both = mm(h2, gate_up_weight)
    gate, upward = both[:, :ff_part], both[:, ff_part:]
    sig = jax.nn.sigmoid(gate)
    m = (gate * sig * upward).astype(low)
    down_term = mm_tn(dyb, m).astype(low)
    down_rows = scatter_planes(down_term)
    down_weight, down_term = together(down_weight, down_term)
    d_both = feed_back(dyb, down_weight, both)
    gate_up_term = mm_tn(h2, d_both).astype(low)
    gate_up_rows = scatter_planes(gate_up_term)
    dh2 = team_sum([d_both], [gate_up_weight], 7, [gate_up_term, down_term])
    mid_grad, gain_two = rms_back(dh2, r, inverse_two, norm_gains[1])
    dr = outer_grad + mid_grad
    drb = team_gather(dr.astype(low), 13, [down_rows])

    do = heads(mm(drb, out_weight).astype(low))
    dq, keep, theirs = attention_call(
        attention_back_kernel,
        *attend,
        (do, cos_table, sin_table),
        [("rows", low), ("keys", jnp.float32), ("keys", low)],
        "attention_back",
    )
    dq = dq.reshape(-1, HEAD_SIZE)
    dkv = keep + lax.ppermute(theirs, "c", [(0, 1), (1, 0)]).astype(jnp.float32)
    low_terms = dkv.astype(low)
    feed_sum = team_sum([m], [down_weight], 5, [low_terms])
    down_grad = scatter_team(down_rows, 6, [low_terms])
    layer_output = (r + feed_sum).astype(low)
    local_squares = sum(jnp.sum(jnp.square(part.astype(jnp.float32))) for part in (gate_up_rows, down_rows))
    query_term, out_term = mm_tn(h1, dq).astype(low), mm_tn(drb, o).astype(low)
    low_terms, gate_up_rows, layer_output, down_grad, query_term, out_term = together(
        low_terms, gate_up_rows, layer_output, down_grad, query_term, out_term
    )
    if is_square():
        low_terms = low_terms.reshape(nz, -1, HEAD_SIZE)
        dkv, attention_term, gate_up_grad = fall(low_terms, gate_up_rows, h1, query_term, out_term, *tables, nz, 8)
    else:
        dkv = lax.psum_scatter(low_terms, "z", scatter_dimension=0, tiled=True)[0].astype(jnp.float32)
        dkv = jnp.where(core == 0, rotate(dkv, cos_rows, -sin_rows), dkv).astype(low).reshape(-1, HEAD_SIZE)
        attention_term = jnp.concatenate([query_term, mm_tn(h1, dkv).astype(low), out_term], axis=1)
        gate_up_grad = scatter_team(gate_up_rows, 8)
    attention_rows = scatter_planes(attention_term)
    dh1 = team_sum([dq, dkv], [query_weight, kv_weight], 9, [attention_term])
    in_grad, gain_one = rms_back(dh1, x_in, inverse_one, norm_gains[0])
    input_gradient = dr + in_grad
    gain_local = jnp.stack([gain_one, gain_two]).reshape(-1, 128)
    lines = jnp.concatenate([gain_local, jnp.full((8, 128), local_squares)], axis=0)
    if is_square():
        lines = total_sum(lines, nz, 18)
        attention_grad, tile = turn(attention_rows, 10, (), nz)
    else:
        lines = lax.psum(lines, ALL)
        attention_grad = scatter_team(attention_rows, 10)
        tile = lax.psum(jnp.full((8, 128), jnp.sum(jnp.square(attention_rows.astype(jnp.float32)))), ALL)
    gain_grad = lines[:-8].reshape(2, width)
    news = update(
        (lines, tile, gain_grad),
        (gate_up_grad, down_grad, attention_grad),
        (norm_gains, gain_mean, gain_square),
        (feed_weight, feed_mean, feed_square),
        (attention_weight, attention_mean, attention_square),
    )
    gains_new, gradient_norm, feed_new, attention_new = news[:3], news[3], news[4:8], news[8:]
    return (
        layer_output.reshape(sequences, span, width),
        input_gradient.reshape(sequences, span, width),
        gradient_norm.reshape(()),
        *attention_new,
        *feed_new,
        *gains_new,
    )


def solution(mesh):
    ctx, fsdp = mesh.shape["ctx"], mesh.shape["fsdp"]
    inner = QUERY_HEADS // fsdp
    fine = Mesh(mesh.devices.reshape(ctx // inner, inner, fsdp // 2, 2), ALL)
    act = P(("x", "c"), ("z", "y"), None)
    matrix = P(ALL, None)
    return jax.shard_map(
        local,
        mesh=fine,
        in_specs=(act, P(("x", "c")), P(), matrix, matrix, act, matrix, matrix, matrix, matrix, P(), P()),
        out_specs=(act, act, P(), matrix, matrix, matrix, matrix, matrix, matrix, matrix, matrix, P(), P(), P()),
        check_vma=False,
    )
```

```python
import functools

import jax
import jax.numpy as jnp
from jax import lax
from jax.experimental import pallas as pl
from jax.experimental.pallas import tpu as pltpu
from jax.sharding import Mesh, PartitionSpec as P

QUERY_HEADS = 8
KEY_VALUE_HEADS = 4
HEAD_SIZE = 256
FF = 8192
STEP = 10

norm_eps = 1e-06
rope_base = 1000042.0
masked_value = -1e30
clip_norm = 1.0
beta_one = 0.9
beta_two = 0.95
adam_eps = 1e-08
matrix_rate = 0.03
gain_rate = 0.4
weight_decay = 0.1

TEAM = ("y", "x", "c")
ALL = ("z", "y", "x", "c")


MESH = pl.DeviceIdType.MESH
VMEM = pl.BlockSpec(memory_space=pltpu.VMEM)
HBM = pl.BlockSpec(memory_space=pl.ANY)


def place():
    y, x, c = lax.axis_index("y"), lax.axis_index("x"), lax.axis_index("c")
    return y, x, c, lambda yy, xx, cc: (yy * 2 + xx) * 2 + cc


def hail(others):
    barrier = pltpu.get_barrier_semaphore()
    for other in others:
        pl.semaphore_signal(barrier, inc=1, device_id=other, device_id_type=MESH)
    return lambda: pl.semaphore_wait(barrier, len(others))


def greet(others):
    hail(others)()


def gather_kernel(src, *refs):
    out, send, recv, own = refs[-4:]
    y, x, c, index = place()
    to_x, to_y, to_s = {"x": 1 - x}, {"y": 1 - y}, {"c": 1 - c}
    me, at_x, at_y, at_d = index(y, x, c), index(y, 1 - x, c), index(1 - y, x, c), index(1 - y, 1 - x, c)
    half = src.shape[0] // 2
    rows = (pl.ds(0, half), pl.ds(half, half))
    local = pltpu.make_async_copy(src, out.at[me], own)
    local.start()
    greet((to_x, to_y, to_s))

    def hop(slot, block, part, where, first=False):
        piece = out.at[block, rows[part]]
        return pltpu.make_async_remote_copy(
            src_ref=src.at[rows[part]] if first else piece,
            dst_ref=piece,
            send_sem=send.at[slot],
            recv_sem=recv.at[slot],
            device_id=where,
            device_id_type=MESH,
        )

    x0, x1 = hop(0, me, 0, to_x, True), hop(1, me, 1, to_x, True)
    y1, y0 = hop(2, me, 1, to_y, True), hop(3, me, 0, to_y, True)
    s0, s1 = hop(4, me, 0, to_s, True), hop(5, me, 1, to_s, True)
    for copy in (x0, y1, x1, y0, s0, s1):
        copy.start()
    x0.wait_recv()
    d0 = hop(6, at_x, 0, to_y)
    d0.start()
    y1.wait_recv()
    d1 = hop(7, at_y, 1, to_x)
    d1.start()
    sx0, sy1 = hop(8, at_x, 0, to_s), hop(9, at_y, 1, to_s)
    sx0.start()
    sy1.start()
    x1.wait_recv()
    sx1 = hop(10, at_x, 1, to_s)
    sx1.start()
    y0.wait_recv()
    sy0 = hop(11, at_y, 0, to_s)
    sy0.start()
    d0.wait_recv()
    sd0 = hop(12, at_d, 0, to_s)
    sd0.start()
    d1.wait_recv()
    sd1 = hop(13, at_d, 1, to_s)
    sd1.start()
    for copy in (s0, s1, sx0, sy1, sx1, sy0, sd0, sd1):
        copy.wait_recv()
    for copy in (x0, x1, y0, y1, s0, s1, d0, d1, sx0, sy1, sx1, sy0, sd0, sd1):
        copy.wait_send()
    local.wait()


def plane_gather(value, number, after=()):
    return pl.pallas_call(
        gather_kernel,
        out_shape=jax.ShapeDtypeStruct((8, *value.shape), value.dtype),
        in_specs=[HBM] * (1 + len(after)),
        out_specs=HBM,
        scratch_shapes=[
            pltpu.SemaphoreType.DMA((14,)),
            pltpu.SemaphoreType.DMA((14,)),
            pltpu.SemaphoreType.DMA,
        ],
        compiler_params=pltpu.CompilerParams(collective_id=number, has_side_effects=True),
        cost_estimate=pl.CostEstimate(flops=1, bytes_accessed=1, transcendentals=0),
        name="plane_gather",
    )(value, *after)


def sum_kernel(lefts, terms, tile, *refs):
    a_refs, w_refs = refs[:lefts], refs[lefts : lefts + len(terms)]
    out, s_send, s_recv, d_send, d_recv, x_send, x_recv, y_send, y_recv, x_acc, y_acc, send, recv = refs[-13:]
    y, x, c, index = place()
    to_x, to_y, to_s = {"x": 1 - x}, {"y": 1 - y}, {"c": 1 - c}
    rows, width = out.shape
    half = rows // 2
    parts = (pl.ds(0, half), pl.ds(half, half))
    f32, low = jnp.float32, jnp.bfloat16

    def product(block, put):
        lines = pl.ds(pl.multiple_of(block * rows, rows), rows)

        @pl.loop(0, width // tile)
        def _(step):
            cols = pl.ds(pl.multiple_of(step * tile, tile), tile)
            total = None
            for (left, start), w_ref in zip(terms, w_refs):
                term = mm_nt(a_refs[left][lines, start : start + w_ref.shape[1]], w_ref[cols, :])
                total = term if total is None else total + term
            put(cols, total)

    def hop(slot, src, dst, where):
        copy = pltpu.make_async_remote_copy(
            src_ref=src, dst_ref=dst, send_sem=send.at[slot], recv_sem=recv.at[slot],
            device_id=where, device_id_type=MESH,
        )
        return copy

    def to_sibling(slot, yy, xx):
        def put(cols, total):
            s_send[slot, :, cols] = total.astype(low)

        product(index(yy, xx, 1 - c), put)
        copy = hop(slot, s_send.at[slot], s_recv.at[slot], to_s)
        copy.start()
        return copy

    def with_sibling(slot, yy, xx, keep):
        def put(cols, total):
            keep[:, cols] = (total + s_recv[slot, :, cols].astype(f32)).astype(keep.dtype)

        product(index(yy, xx, c), put)

    greet((to_x, to_y, to_s))
    s0 = to_sibling(0, 1 - y, 1 - x)
    s1 = to_sibling(1, y, 1 - x)
    s0.wait_recv()
    with_sibling(0, 1 - y, 1 - x, d_send)
    d0 = hop(4, d_send.at[parts[0]], d_recv.at[parts[0]], to_x)
    d1 = hop(5, d_send.at[parts[1]], d_recv.at[parts[1]], to_y)
    d0.start()
    d1.start()
    s1.wait_recv()
    with_sibling(1, y, 1 - x, x_acc)
    x_send[parts[0]] = x_acc[parts[0]].astype(low)
    x0 = hop(6, x_send.at[parts[0]], x_recv.at[parts[0]], to_x)
    x0.start()
    s2 = to_sibling(2, 1 - y, x)
    s2.wait_recv()
    with_sibling(2, 1 - y, x, y_acc)
    y_send[parts[1]] = y_acc[parts[1]].astype(low)
    y1 = hop(7, y_send.at[parts[1]], y_recv.at[parts[1]], to_y)
    y1.start()
    s3 = to_sibling(3, y, x)
    d1.wait_recv()
    x_send[parts[1]] = (x_acc[parts[1]] + d_recv[parts[1]].astype(f32)).astype(low)
    x1 = hop(8, x_send.at[parts[1]], x_recv.at[parts[1]], to_x)
    x1.start()
    d0.wait_recv()
    y_send[parts[0]] = (y_acc[parts[0]] + d_recv[parts[0]].astype(f32)).astype(low)
    y0 = hop(9, y_send.at[parts[0]], y_recv.at[parts[0]], to_y)
    y0.start()
    s3.wait_recv()
    with_sibling(3, y, x, out)
    x0.wait_recv()
    y1.wait_recv()
    x1.wait_recv()
    y0.wait_recv()
    out[...] += x_recv[...].astype(f32) + y_recv[...].astype(f32)
    for copy in (s0, s1, s2, s3, d0, d1, x0, x1, y0, y1):
        copy.wait_send()


def plane_sum(lefts, rights, number, after=(), tile=512):
    ends = [(left, start) for left, a in enumerate(lefts) for start in range(0, a.shape[1], rights[0].shape[1])]
    terms = tuple(ends[: len(rights)])
    rows, width = lefts[0].shape[0] // 8, rights[0].shape[0]
    block = (rows, width)
    low, f32 = jnp.bfloat16, jnp.float32
    return pl.pallas_call(
        functools.partial(sum_kernel, len(lefts), terms, min(tile, width)),
        out_shape=jax.ShapeDtypeStruct(block, f32),
        in_specs=[VMEM] * (len(lefts) + len(rights)) + [HBM] * len(after),
        out_specs=VMEM,
        scratch_shapes=[
            pltpu.VMEM((4, *block), low),
            pltpu.VMEM((4, *block), low),
            *[pltpu.VMEM(block, low)] * 6,
            pltpu.VMEM(block, f32),
            pltpu.VMEM(block, f32),
            pltpu.SemaphoreType.DMA((10,)),
            pltpu.SemaphoreType.DMA((10,)),
        ],
        compiler_params=pltpu.CompilerParams(
            collective_id=number, has_side_effects=True, vmem_limit_bytes=48 * 2**20
        ),
        cost_estimate=pl.CostEstimate(flops=1, bytes_accessed=1, transcendentals=0),
        name="plane_sum",
    )(*lefts, *rights, *after)


def swap_kernel(pieces, takes, *refs):
    count = len(pieces)
    sources, (send, recv, own) = refs[: -2 * count - 3], refs[-3:]
    outs, holds = refs[-2 * count - 3 : -count - 3], refs[-count - 3 : -3]
    y, x, c, index = place()
    me = index(y, x, c)
    flips = [(fy, fx, fc) for fy, fx in ((1, 1), (0, 1), (1, 0), (0, 0)) for fc in (0, 1)]
    flips = [flip for flip in flips if flip != (0, 0, 0)]

    def there(flip):
        return tuple(1 - at if f else at for at, f in zip((y, x, c), flip))

    greet([dict(zip(("y", "x", "c"), there(flip))) for flip in flips])
    copies = []
    for piece in range(count):
        for number, flip in enumerate(flips):
            yy, xx, cc = there(flip)
            member = index(yy, xx, cc)
            holds[piece][number] = takes[piece](sources, member, cc)
            copy = pltpu.make_async_remote_copy(
                src_ref=holds[piece].at[number],
                dst_ref=outs[piece].at[me],
                send_sem=send.at[piece * 7 + number],
                recv_sem=recv.at[piece * 7 + number],
                device_id={"y": yy, "x": xx, "c": cc},
                device_id_type=MESH,
            )
            copy.start()
            copies.append(copy)
        holds[piece][7] = takes[piece](sources, me, c)
        keep = pltpu.make_async_copy(holds[piece].at[7], outs[piece].at[me], own.at[piece])
        keep.start()
        copies.append(keep)
    for copy in copies:
        copy.wait()


def plane_swap(sources, shapes, takes, number, after=()):
    low = jnp.bfloat16
    count = len(shapes)
    return pl.pallas_call(
        functools.partial(swap_kernel, shapes, takes),
        out_shape=[jax.ShapeDtypeStruct((8, *shape), low) for shape in shapes],
        in_specs=[VMEM] * len(sources) + [HBM] * len(after),
        out_specs=[HBM] * count,
        scratch_shapes=[
            *[pltpu.VMEM((8, *shape), low) for shape in shapes],
            pltpu.SemaphoreType.DMA((7 * count,)),
            pltpu.SemaphoreType.DMA((7 * count,)),
            pltpu.SemaphoreType.DMA((count,)),
        ],
        compiler_params=pltpu.CompilerParams(
            collective_id=number, has_side_effects=True, vmem_limit_bytes=48 * 2**20
        ),
        cost_estimate=pl.CostEstimate(flops=1, bytes_accessed=1, transcendentals=0),
        name="plane_swap",
    )(*sources, *after)


def team_of(y, x, c):
    flips = [(fy, fx, fc) for fy, fx in ((1, 1), (0, 1), (1, 0), (0, 0)) for fc in (0, 1)]
    return [
        tuple(1 - at if f else at for at, f in zip((y, x, c), flip)) for flip in flips if flip != (0, 0, 0)
    ]


def turn_kernel(planes, src, *refs):
    y, x, c, index = place()
    me = index(y, x, c)
    others = team_of(y, x, c)
    ids = [dict(zip(("y", "x", "c"), other)) for other in others]
    if planes:
        out, total, near, far, held, send, recv, own, send_lines, recv_lines = refs[-10:]
        z = lax.axis_index("z")
        column = [{"z": lax.rem(z + step, planes)} for step in range(1, planes)]
        fetch = pltpu.make_async_copy(src, held, own.at[1])
        fetch.start()
    else:
        out, send, recv, own = refs[-4:]
        column = []
    ready = hail(ids + column)
    if planes:
        fetch.wait()
        squares = jnp.zeros((8, held.shape[1]), jnp.float32)
        for start in range(0, held.shape[0], 64):
            part = held[start : start + 64].astype(jnp.float32)
            squares += jnp.sum(jnp.square(part).reshape(8, 8, -1), axis=0)
        near[me] = jnp.broadcast_to(jnp.sum(squares, keepdims=True), near.shape[1:])
    ready()
    count = src.shape[0] // 8

    def rows(member):
        return src.at[pl.ds(pl.multiple_of(member * count, count), count)]

    def spread(buffer, at, where, base):
        copies = [
            pltpu.make_async_remote_copy(
                src_ref=buffer.at[at],
                dst_ref=buffer.at[at],
                send_sem=send_lines.at[base + number],
                recv_sem=recv_lines.at[base + number],
                device_id=other,
                device_id_type=MESH,
            )
            for number, other in enumerate(where)
        ]
        for copy in copies:
            copy.start()
        return copies

    copies = [
        pltpu.make_async_remote_copy(
            src_ref=rows(index(*other)),
            dst_ref=out.at[me],
            send_sem=send.at[number],
            recv_sem=recv.at[number],
            device_id=where,
            device_id_type=MESH,
        )
        for number, (other, where) in enumerate(zip(others, ids))
    ]
    copies.append(pltpu.make_async_copy(rows(me), out.at[me], own.at[0]))
    small = spread(near, me, ids, 0) if planes else []
    for copy in copies:
        copy.start()
    if planes:
        for copy in small:
            copy.wait()
        far[z] = jnp.sum(near[...], axis=0)
        for copy in spread(far, z, column, 7):
            copy.wait()
        total[...] = jnp.sum(far[...], axis=0)
    for copy in copies:
        copy.wait()


def total_kernel(planes, src, *refs):
    out, near, far, send, recv = refs[-5:]
    y, x, c, index = place()
    z = lax.axis_index("z")
    ids = [dict(zip(("y", "x", "c"), other)) for other in team_of(y, x, c)]
    column = [{"z": lax.rem(z + step, planes)} for step in range(1, planes)]
    me = index(y, x, c)
    near[me] = src[...]
    greet(ids + column)

    def spread(buffer, at, where, base):
        copies = [
            pltpu.make_async_remote_copy(
                src_ref=buffer.at[at],
                dst_ref=buffer.at[at],
                send_sem=send.at[base + number],
                recv_sem=recv.at[base + number],
                device_id=other,
                device_id_type=MESH,
            )
            for number, other in enumerate(where)
        ]
        for copy in copies:
            copy.start()
        for copy in copies:
            copy.wait()

    spread(near, me, ids, 0)
    far[z] = jnp.sum(near[...], axis=0)
    spread(far, z, column, 7)
    out[...] = jnp.sum(far[...], axis=0)


def total_sum(value, planes, number, after=()):
    return pl.pallas_call(
        functools.partial(total_kernel, planes),
        out_shape=jax.ShapeDtypeStruct(value.shape, value.dtype),
        in_specs=[VMEM] + [HBM] * len(after),
        out_specs=VMEM,
        scratch_shapes=[pltpu.VMEM((size, *value.shape), value.dtype) for size in (8, planes)]
        + [pltpu.SemaphoreType.DMA((6 + planes,))] * 2,
        compiler_params=pltpu.CompilerParams(
            collective_id=number, has_side_effects=True, vmem_limit_bytes=16 * 2**20
        ),
        cost_estimate=pl.CostEstimate(flops=1, bytes_accessed=1, transcendentals=0),
        name="total_sum",
    )(value, *after)


def turn(rows, number, after=(), planes=0):
    block = (rows.shape[0] // 8, rows.shape[1])
    dma = pltpu.SemaphoreType.DMA
    out_shape, out_specs = [jax.ShapeDtypeStruct((8, *block), rows.dtype)], [HBM]
    scratch = [dma((7,)), dma((7,)), dma((2,))]
    if planes:
        tile = jax.ShapeDtypeStruct((8, 128), jnp.float32)
        out_shape.append(tile)
        out_specs.append(VMEM)
        buffers = [pltpu.VMEM((size, *tile.shape), tile.dtype) for size in (8, planes)]
        scratch = buffers + [pltpu.VMEM(rows.shape, rows.dtype)] + scratch + [dma((6 + planes,)), dma((6 + planes,))]
    return pl.pallas_call(
        functools.partial(turn_kernel, planes),
        out_shape=out_shape,
        in_specs=[HBM] * (1 + len(after)),
        out_specs=out_specs,
        scratch_shapes=scratch,
        compiler_params=pltpu.CompilerParams(
            collective_id=number, has_side_effects=True, vmem_limit_bytes=56 * 2**20
        ),
        cost_estimate=pl.CostEstimate(flops=1, bytes_accessed=1, transcendentals=0),
        name="turn",
    )(rows, *after)


def hops(planes, send, recv, block, up):
    z = lax.axis_index("z")

    def step(number):
        gone, came = (z - number + 1, z - number) if up else (z + number - 1, z + number)
        goes = ((gone >= 0) & (z + 1 < planes)) if up else ((gone < planes) & (z >= 1))
        comes = (came >= 0) if up else (came < planes)

        def copy(b):
            return pltpu.make_async_remote_copy(
                src_ref=block(b),
                dst_ref=block(b),
                send_sem=send.at[number - 1],
                recv_sem=recv.at[number - 1],
                device_id={"z": z + 1 if up else z - 1},
                device_id_type=MESH,
            )

        return (
            lambda: pl.when(goes)(lambda: copy(gone).start()),
            lambda: pl.when(comes)(lambda: copy(came).wait_recv()),
            lambda: pl.when(goes)(lambda: copy(gone).wait_send()),
        )

    return [step(number) for number in range(1, planes)]


def ring(planes):
    z = lax.axis_index("z")
    return [{"z": lax.rem(z + 1, planes)}, {"z": lax.rem(z + planes - 1, planes)}]


def spread_to(others, ids, source, take, hold, place_of, send, recv, own, ready=None):
    y, x, c, index = place()
    me = index(y, x, c)
    copies = []
    if ready is not None:
        for number, other in enumerate(others):
            hold[number] = take([source], index(*other), other[2])
        ready()
    for number, (other, where) in enumerate(zip(others, ids)):
        if ready is None:
            hold[number] = take([source], index(*other), other[2])
        copy = pltpu.make_async_remote_copy(
            src_ref=hold.at[number], dst_ref=place_of(me), send_sem=send.at[number], recv_sem=recv.at[number],
            device_id=where, device_id_type=MESH,
        )
        copy.start()
        copies.append(copy)
    hold[7] = take([source], me, c)
    keep = pltpu.make_async_copy(hold.at[7], place_of(me), own)
    keep.start()
    return copies, keep


def begin_kernel(
    planes, take, take_feed, attention, feed, tokens_from, gain, all_attention, all_rows, columns,
    tokens, held, hold, feed_held, feed_hold, rows, a_send, a_recv, f_send, f_recv, r_send, r_recv, u_send, u_recv, d_send, d_recv, own,
):
    y, x, c, index = place()
    z = lax.axis_index("z")
    me, at_x, at_y, at_d = index(y, x, c), index(y, 1 - x, c), index(1 - y, x, c), index(1 - y, 1 - x, c)
    others = team_of(y, x, c)
    ids = [dict(zip(("y", "x", "c"), other)) for other in others]
    to_x, to_y, to_s = {"x": 1 - x}, {"y": 1 - y}, {"c": 1 - c}
    count = held.shape[0]
    half = rows.shape[0] // 2
    parts = (pl.ds(0, half), pl.ds(half, half))
    fetch = pltpu.make_async_copy(attention, held, own.at[0])
    fetch.start()
    fetch_tokens = pltpu.make_async_copy(tokens_from, tokens, own.at[5])
    fetch_tokens.start()
    fetch_feed = pltpu.make_async_copy(feed.at[:, pl.ds(0, feed_held.shape[1])], feed_held, own.at[3])
    fetch_feed.start()
    ready = hail(ids + ring(planes))
    fetch.wait()

    def attention_rows(start, size):
        return all_attention.at[pl.ds(pl.multiple_of(start, count), size)]

    a_copies, a_keep = spread_to(
        others, ids, held, take, hold, lambda m: attention_rows((z * 8 + m) * count, count), a_send, a_recv, own.at[1], ready
    )

    def hop(slot, block, part, where, first=False):
        piece = all_rows.at[block, parts[part]]
        copy = pltpu.make_async_remote_copy(
            src_ref=rows.at[parts[part]] if first else piece, dst_ref=piece,
            send_sem=r_send.at[slot], recv_sem=r_recv.at[slot], device_id=where, device_id_type=MESH,
        )
        copy.start()
        return copy

    for copy in a_copies:
        copy.wait_recv()
    a_keep.wait()

    def plane_block(b):
        return attention_rows(b * 8 * count, 8 * count)

    up = hops(planes, u_send, u_recv, plane_block, True)
    down = hops(planes, d_send, d_recv, plane_block, False)

    def pass_on(number):
        if number > 0:
            up[number - 1][1]()
            down[number - 1][1]()
        if number < planes - 1:
            up[number][0]()
            down[number][0]()

    pass_on(0)
    fetch_tokens.wait()

    @pl.loop(0, rows.shape[0] // 16)
    def _(group):
        lines = pl.ds(pl.multiple_of(group * 16, 16), 16)
        rows[lines] = rms_forward(tokens[lines].astype(jnp.float32), gain[...])[0].astype(rows.dtype)

    x0, y1 = hop(0, me, 0, to_x, True), hop(2, me, 1, to_y, True)
    x1, y0 = hop(1, me, 1, to_x, True), hop(3, me, 0, to_y, True)
    s0, s1 = hop(4, me, 0, to_s, True), hop(5, me, 1, to_s, True)
    mine = pltpu.make_async_copy(rows, all_rows.at[me], own.at[2])
    mine.start()
    x0.wait_recv()
    d0 = hop(6, at_x, 0, to_y)
    y1.wait_recv()
    d1 = hop(7, at_y, 1, to_x)
    sx0, sy1 = hop(8, at_x, 0, to_s), hop(9, at_y, 1, to_s)
    fetch_feed.wait()
    f_copies, f_keep = spread_to(
        others, ids, feed_held, take_feed, feed_hold, lambda m: columns.at[m], f_send, f_recv, own.at[4]
    )
    pass_on(1)
    x1.wait_recv()
    sx1 = hop(10, at_x, 1, to_s)
    y0.wait_recv()
    sy0 = hop(11, at_y, 0, to_s)
    pass_on(2)
    d0.wait_recv()
    sd0 = hop(12, at_d, 0, to_s)
    d1.wait_recv()
    sd1 = hop(13, at_d, 1, to_s)
    for number in range(3, planes):
        pass_on(number)
    for copy in (s0, s1, sx0, sy1, sx1, sy0, sd0, sd1, *f_copies):
        copy.wait_recv()
    for copy in (x0, x1, y0, y1, s0, s1, d0, d1, sx0, sy1, sx1, sy0, sd0, sd1, *a_copies, *f_copies):
        copy.wait_send()
    for step in up + down:
        step[2]()
    mine.wait()
    f_keep.wait()


def begin(attention, feed, tokens, gain, takes, widths, planes, number):
    low, dma = jnp.bfloat16, pltpu.SemaphoreType.DMA
    count = attention.shape[0]
    return pl.pallas_call(
        functools.partial(begin_kernel, planes, *takes),
        out_shape=[
            jax.ShapeDtypeStruct((planes * 8 * count, widths[0]), low),
            jax.ShapeDtypeStruct((8, *tokens.shape), low),
            jax.ShapeDtypeStruct((8, count, widths[1]), low),
        ],
        in_specs=[HBM, HBM, HBM, VMEM],
        out_specs=[HBM] * 3,
        scratch_shapes=[
            pltpu.VMEM(tokens.shape, tokens.dtype),
            pltpu.VMEM(attention.shape, attention.dtype),
            pltpu.VMEM((8, count, widths[0]), low),
            pltpu.VMEM((count, 8 * widths[1]), feed.dtype),
            pltpu.VMEM((8, count, widths[1]), low),
            pltpu.VMEM(tokens.shape, low),
            *[dma((size,)) for size in (7, 7, 7, 7, 14, 14, *[planes - 1] * 4, 6)],
        ],
        compiler_params=pltpu.CompilerParams(
            collective_id=number, has_side_effects=True, vmem_limit_bytes=54 * 2**20
        ),
        cost_estimate=pl.CostEstimate(flops=1, bytes_accessed=1, transcendentals=0),
        name="begin",
    )(attention, feed, tokens, gain)


def turned(value, cos_table, sin_table):
    half = value.shape[1] // 2
    first, second = value[:, :half], value[:, half:]
    return jnp.concatenate([first * cos_table - second * sin_table, second * cos_table + first * sin_table], axis=1)


def climb_kernel(
    planes, rows, weights, cos, sin, mine, other, weight, held, zeros, stay, u_send, u_recv, s_send, s_recv, own, fill, move
):
    z, c = lax.axis_index("z"), lax.axis_index("c")
    to_s = {"c": 1 - c}
    barrier = pltpu.get_barrier_semaphore()
    for where in [to_s] + ring(planes):
        pl.semaphore_signal(barrier, inc=1, device_id=where, device_id_type=MESH)
    count, (sides, span) = rows.shape[0], cos.shape[:2]
    size = 512
    pull_weight = pltpu.make_async_copy(
        weights.at[:, pl.ds(weight.shape[1], weight.shape[1])], weight, move.at[count // size]
    )
    pull_weight.start()
    pulls = [
        pltpu.make_async_copy(rows.at[pl.ds(start, size)], held.at[pl.ds(start, size)], move.at[start // size])
        for start in range(0, count, size)
    ]
    for copy in pulls:
        copy.start()
    pull_weight.wait()
    for start in range(0, count, size):
        pulls[start // size].wait()
        value = mm(held[start : start + size], weight[...])
        for line in range(0, size, span):
            side = (start + line) // (count // sides)
            part = value[line : line + span]
            part = jnp.where(c == 0, turned(part, cos[side], sin[side]), part)
            stay[start + line : start + line + span] = part.astype(stay.dtype)
    zeros[...] = jnp.zeros_like(zeros)
    pl.semaphore_wait(barrier, 3)

    def across(n):
        return pltpu.make_async_remote_copy(
            src_ref=stay if n == 0 else mine.at[n], dst_ref=other.at[n], send_sem=s_send.at[n], recv_sem=s_recv.at[n],
            device_id=to_s, device_id_type=MESH,
        )

    def along(n):
        return pltpu.make_async_remote_copy(
            src_ref=stay if n == 1 else mine.at[n - 1], dst_ref=mine.at[n], send_sem=u_send.at[n - 1], recv_sem=u_recv.at[n - 1],
            device_id={"z": z + 1}, device_id_type=MESH,
        )

    def fills(n):
        return [
            pltpu.make_async_copy(zeros, buffer.at[n], fill.at[2 * (n - 1) + number])
            for number, buffer in enumerate((mine, other))
        ]

    keep = pltpu.make_async_copy(stay, mine.at[0], own)
    more = z + 1 < planes
    pl.when(more)(lambda: along(1).start())
    across(0).start()
    keep.start()
    for n in range(1, planes):

        @pl.when(z < n)
        def _():
            for copy in fills(n):
                copy.start()

    for n in range(1, planes):

        @pl.when(z >= n)
        def _():
            along(n).wait_recv()
            if n + 1 < planes:
                pl.when(more)(lambda: along(n + 1).start())
            across(n).start()

    across(0).wait()
    keep.wait()
    for n in range(1, planes):

        @pl.when(z >= n)
        def _():
            across(n).wait()

        @pl.when(z < n)
        def _():
            for copy in fills(n):
                copy.wait()

        pl.when((z >= n - 1) & more)(lambda: along(n).wait_send())


def climb(rows, weights, cos, sin, planes, number):
    dma = pltpu.SemaphoreType.DMA
    block = (rows.shape[0], weights.shape[1] // 3)
    blocks = jax.ShapeDtypeStruct((planes, *block), rows.dtype)
    return pl.pallas_call(
        functools.partial(climb_kernel, planes),
        out_shape=[blocks, blocks],
        in_specs=[HBM] * 2 + [VMEM] * 2,
        out_specs=[HBM] * 2,
        scratch_shapes=[
            pltpu.VMEM((weights.shape[0], block[1]), rows.dtype),
            pltpu.VMEM(rows.shape, rows.dtype),
            pltpu.VMEM(block, rows.dtype),
            pltpu.VMEM(block, rows.dtype),
            *[dma((size,)) for size in (planes - 1, planes - 1, planes, planes)],
            dma,
            dma((2 * (planes - 1),)),
            dma((rows.shape[0] // 512 + 1,)),
        ],
        compiler_params=pltpu.CompilerParams(
            collective_id=number, has_side_effects=True, vmem_limit_bytes=56 * 2**20
        ),
        cost_estimate=pl.CostEstimate(flops=1, bytes_accessed=1, transcendentals=0),
        name="climb",
    )(rows, weights, cos, sin)


def fall_kernel(
    planes, terms_from, rows, left_from, query_term, out_term, cos, sin, value, term, blocks,
    terms, left, sends, recvs, total, first, held, send, recv, t_send, t_recv, own, move, fetch,
):
    y, x, c, index = place()
    z = lax.axis_index("z")
    me = index(y, x, c)
    others = team_of(y, x, c)
    ids = [dict(zip(("y", "x", "c"), other)) for other in others]
    f32 = jnp.float32
    count = rows.shape[0] // 8
    size = terms.shape[2]
    given = ((query_term, 0), (out_term, 2))
    pulls = [pltpu.make_async_copy(ref, held.at[n], move.at[n]) for n, (ref, _) in enumerate(given)]
    get_terms = pltpu.make_async_copy(terms_from, terms, fetch.at[0])
    get_terms.start()
    get_left = pltpu.make_async_copy(left_from, left, fetch.at[1])
    get_left.start()
    for copy in pulls:
        copy.start()
    greet(ids + ring(planes))
    get_terms.wait()

    def rows_of(member):
        return rows.at[pl.ds(pl.multiple_of(member * count, count), count)]

    pieces = 3
    third = terms.shape[1] // pieces
    parts = [pl.ds(n * third, third) for n in range(pieces)]

    def hop(step, n):
        slot = pieces * (step - 1) + n
        return pltpu.make_async_remote_copy(
            src_ref=sends.at[step - 1, parts[n]], dst_ref=recvs.at[step - 1, parts[n]],
            send_sem=send.at[slot], recv_sem=recv.at[slot], device_id={"z": z - 1}, device_id_type=MESH,
        )

    def came(step):
        return (z + 1 < planes) & (z + 1 + step - planes >= 0)

    copies = [
        pltpu.make_async_remote_copy(
            src_ref=rows_of(index(*other)), dst_ref=blocks.at[me], send_sem=t_send.at[number], recv_sem=t_recv.at[number],
            device_id=where, device_id_type=MESH,
        )
        for number, (other, where) in enumerate(zip(others, ids))
    ]
    copies.append(pltpu.make_async_copy(rows_of(me), blocks.at[me], own))
    pushes = []
    for step in range(1, planes):
        block = z + step - planes
        for n in range(pieces):
            lines = parts[n]
            if step > 1:
                pl.when(came(step - 1))(lambda: hop(step - 1, n).wait_recv())

            @pl.when((block >= 0) & (z + 1 == planes))
            def _():
                sends[step - 1, lines] = terms[block, lines]

            if step > 1:

                @pl.when((block >= 0) & (z + 1 < planes))
                def _():
                    added = terms[block, lines].astype(f32) + recvs[step - 2, lines].astype(f32)
                    sends[step - 1, lines] = added.astype(terms.dtype)

            pl.when(block >= 0)(lambda: hop(step, n).start())
        if step == 1:
            for copy in copies:
                copy.start()
            total[...] = terms[z].astype(f32)
            for n, (_, column) in enumerate(given):
                pulls[n].wait()
                pushes.append(
                    pltpu.make_async_copy(held.at[n], term.at[:, pl.ds(column * size, size)], move.at[2 + n])
                )
                pushes[-1].start()
    last = planes - 1
    sides, span = cos.shape[:2]
    get_left.wait()
    for n in range(pieces):
        lines = parts[n]

        @pl.when(came(last))
        def _():
            hop(last, n).wait_recv()
            total[lines] += recvs[last - 1, lines].astype(f32)

        for line in range(n * third, (n + 1) * third, span):
            side = line // (total.shape[0] // sides)
            part = total[line : line + span]
            part = jnp.where(c == 0, turned(part, cos[side], -sin[side]), part)
            value[line : line + span] = part.astype(value.dtype)
        upright = value[lines].astype(f32).T.astype(value.dtype)
        for start in range(0, left.shape[1], 512):
            columns = pl.ds(start, 512)
            made = mm(upright, left[lines, columns])
            if n > 0:
                made += first[:, columns]
            if n < pieces - 1:
                first[:, columns] = made
                continue
            held[2, columns] = made.T.astype(held.dtype)
            pushes.append(
                pltpu.make_async_copy(
                    held.at[2, columns], term.at[columns, pl.ds(size, size)], move.at[4 + start // 512]
                )
            )
            pushes[-1].start()
    for step in range(1, planes):
        for n in range(pieces):
            pl.when(z + step - planes >= 0)(lambda: hop(step, n).wait_send())
    for copy in copies + pushes:
        copy.wait()


def fall(terms, rows, left, query_term, out_term, cos, sin, planes, number):
    block = terms.shape[1:]
    dma, low = pltpu.SemaphoreType.DMA, terms.dtype
    return pl.pallas_call(
        functools.partial(fall_kernel, planes),
        out_shape=[
            jax.ShapeDtypeStruct(block, low),
            jax.ShapeDtypeStruct((left.shape[1], 3 * block[1]), low),
            jax.ShapeDtypeStruct((8, rows.shape[0] // 8, rows.shape[1]), low),
        ],
        in_specs=[HBM] * 5 + [VMEM] * 2,
        out_specs=[VMEM, HBM, HBM],
        scratch_shapes=[pltpu.VMEM(terms.shape, low), pltpu.VMEM(left.shape, low)]
        + [pltpu.VMEM((planes - 1, *block), low)] * 2
        + [pltpu.VMEM(block, jnp.float32), pltpu.VMEM((block[1], left.shape[1]), jnp.float32)]
        + [pltpu.VMEM((3, left.shape[1], block[1]), low)]
        + [dma((3 * (planes - 1),))] * 2
        + [dma((7,)), dma((7,)), dma, dma((4 + left.shape[1] // 512,)), dma((2,))],
        compiler_params=pltpu.CompilerParams(
            collective_id=number, has_side_effects=True, vmem_limit_bytes=56 * 2**20
        ),
        cost_estimate=pl.CostEstimate(flops=1, bytes_accessed=1, transcendentals=0),
        name="fall",
    )(terms, rows, left, query_term, out_term, cos, sin)


def dot(left, right, contract):
    return lax.dot_general(left, right, (contract, ((), ())), preferred_element_type=jnp.float32)


def mm(left, right):
    return dot(left, right, ((1,), (0,)))


def mm_nt(left, right):
    return dot(left, right, ((1,), (1,)))


def mm_tn(left, right):
    return dot(left, right, ((0,), (0,)))


def bmm(pattern, left, right):
    return jnp.einsum(pattern, left, right, preferred_element_type=jnp.float32)


def angle_tables(positions):
    half_dim = HEAD_SIZE // 2
    frequency = rope_base ** (-(jnp.arange(half_dim).astype(jnp.float32) * 2.0) / HEAD_SIZE)
    phases = positions.astype(jnp.float32)[:, None] * frequency[None, :]
    return (jnp.cos(phases), jnp.sin(phases))


def rotate(value, cos_table, sin_table):
    half = value.shape[-1] // 2
    a, b = value[..., :half], value[..., half:]
    return jnp.concatenate([a * cos_table - b * sin_table, b * cos_table + a * sin_table], axis=-1)


def rms_forward(value, gain_row):
    inverse = lax.rsqrt(jnp.mean(value * value, axis=-1, keepdims=True) + norm_eps)
    return (value * inverse * gain_row, inverse)


def rms_back(grad_out, value, inverse, gain_row):
    scaled = grad_out * gain_row
    grad_in = inverse * (
        scaled - value * inverse * inverse * jnp.mean(scaled * value, axis=-1, keepdims=True)
    )
    return (grad_in, jnp.sum(grad_out * value * inverse, axis=0))


def adamw(weight, gradient, moment_one, moment_two, step_rate, decay_rate, invert=jnp.reciprocal):
    mean_new = beta_one * moment_one + (1.0 - beta_one) * gradient
    square_new = beta_two * moment_two + (1.0 - beta_two) * gradient * gradient
    below = jnp.sqrt(square_new * (1.0 / (1.0 - beta_two**STEP))) + adam_eps
    direction = mean_new * (1.0 / (1.0 - beta_one**STEP)) * invert(below)
    return (weight - step_rate * (direction + decay_rate * weight), mean_new, square_new)


def attention_parts(core, length, q_ref, mine_ref, other_ref, query_ref, key_ref):
    mine, other = mine_ref[...].reshape(-1, HEAD_SIZE), other_ref[...].reshape(-1, HEAD_SIZE)
    first = core == 0
    k, v = jnp.where(first, mine, other), jnp.where(first, other, mine)
    q = q_ref[...].reshape(-1, HEAD_SIZE)
    at, key_at = query_ref[...], key_ref[...]
    allowed = (key_at <= at) & (key_at < length) & (key_at >= 0)
    scores = jnp.where(allowed, mm_nt(q, k) * HEAD_SIZE ** (-0.5), masked_value)
    exponent = jnp.exp(scores - jnp.max(scores, axis=-1, keepdims=True))
    return q, k, v, exponent / jnp.sum(exponent, axis=-1, keepdims=True)


def attention_kernel(core_ref, length_ref, q_ref, mine_ref, other_ref, query_ref, key_ref, out_ref):
    length = length_ref[pl.program_id(0)]
    _, _, v, soft = attention_parts(core_ref[0], length, q_ref, mine_ref, other_ref, query_ref, key_ref)
    out_ref[...] = mm(soft.astype(jnp.bfloat16), v).astype(jnp.bfloat16).reshape(out_ref.shape)


def attention_back_kernel(
    core_ref, length_ref, q_ref, mine_ref, other_ref, query_ref, key_ref, do_ref, cos_ref, sin_ref,
    dq_ref, keep_ref, send_ref,
):
    low = jnp.bfloat16
    core = core_ref[0]
    length = length_ref[pl.program_id(0)]
    q, k, v, soft = attention_parts(core, length, q_ref, mine_ref, other_ref, query_ref, key_ref)
    do = do_ref[...].reshape(-1, HEAD_SIZE)
    dp = mm_nt(do, v)
    delta = jnp.sum(soft * dp, axis=-1, keepdims=True)
    ds = (soft * (dp - delta) * HEAD_SIZE ** (-0.5)).astype(low)
    dq = mm(ds, k)
    cos_table, sin_table = cos_ref[...], sin_ref[...]
    half = HEAD_SIZE // 2
    a, b = dq[:, :half], dq[:, half:]
    turned = jnp.concatenate([a * cos_table + b * sin_table, b * cos_table - a * sin_table], axis=-1)
    dq_ref[...] = turned.astype(low).reshape(dq_ref.shape)
    dk, dv = mm_tn(ds, q), mm_tn(soft.astype(low), do)
    first = core == 0
    keep, send = (t.reshape(keep_ref.shape) for t in (jnp.where(first, dk, dv), jnp.where(first, dv, dk)))
    for block in range(keep_ref.shape[0]):
        at = core_ref[1 + block]
        keep_ref[at] = keep[block]
        send_ref[at] = send[block].astype(low)


def attention_call(kernel, core, lengths, q, mine, other, query_pos, key_pos, extra, outs, name):
    ny, count, span, size = q.shape
    nz = mine.shape[0]
    rows = pl.BlockSpec((ny, 1, span, size), lambda i, *_: (0, i, 0, 0))
    keys = pl.BlockSpec((nz, ny, 1, span, size), lambda i, *_: (0, 0, i, 0, 0))

    def whole(value):
        return pl.BlockSpec(value.shape, lambda i, *_: (0,) * value.ndim)

    kinds = {"rows": (rows, q.shape), "keys": (keys, mine.shape)}
    return pl.pallas_call(
        kernel,
        grid_spec=pltpu.PrefetchScalarGridSpec(
            num_scalar_prefetch=2,
            grid=(count,),
            in_specs=[rows, keys, keys, whole(query_pos), whole(key_pos)]
            + [rows if value.shape == q.shape else whole(value) for value in extra],
            out_specs=[kinds[kind][0] for kind, _ in outs],
        ),
        out_shape=[jax.ShapeDtypeStruct(kinds[kind][1], dtype) for kind, dtype in outs],
        compiler_params=pltpu.CompilerParams(vmem_limit_bytes=48 * 2**20),
        cost_estimate=pl.CostEstimate(flops=1, bytes_accessed=1, transcendentals=0),
        name=name,
    )(core, lengths, q, mine, other, query_pos, key_pos, *extra)


def feed_back_kernel(dyb_ref, weight_ref, gate_ref, up_ref, out_ref):
    dm = mm(dyb_ref[...], weight_ref[...])
    gate, upward = gate_ref[...], up_ref[...]
    sig = jax.nn.sigmoid(gate)
    part = gate.shape[1]
    out_ref[:, :part] = (dm * upward * sig * (1.0 + gate * (1.0 - sig))).astype(out_ref.dtype)
    out_ref[:, part:] = (dm * gate * sig).astype(out_ref.dtype)


def feed_back(dyb, weight, both, lines=256):
    count, part = both.shape[0], both.shape[1] // 2

    def rows(width, column=0):
        return pl.BlockSpec((lines, width), lambda i: (i, column))

    return pl.pallas_call(
        feed_back_kernel,
        grid=(count // lines,),
        in_specs=[rows(dyb.shape[1]), pl.BlockSpec(weight.shape, lambda i: (0, 0)), rows(part), rows(part, 1)],
        out_specs=rows(2 * part),
        out_shape=jax.ShapeDtypeStruct((count, 2 * part), jnp.bfloat16),
        compiler_params=pltpu.CompilerParams(vmem_limit_bytes=48 * 2**20),
        cost_estimate=pl.CostEstimate(flops=1, bytes_accessed=1, transcendentals=0),
        name="feed_back",
    )(dyb, weight, both, both)


def close_reciprocal(value):
    guess = pltpu.reciprocal(value, approx=True)
    return guess * (2.0 - value * guess)


def norm_of(lines_ref, tile_ref):
    gains = lines_ref[:-8]
    return jnp.sqrt(jnp.sum(gains * gains, keepdims=True) + lines_ref[-8:-7, 0:1] + tile_ref[0:1, 0:1])


def update_kernel(*refs):
    lines_ref, tile_ref, gain_ref, gate_up_ref, down_ref, attention_ref = refs[:6]
    gains, feed, attention = refs[6:9], refs[9:12], refs[12:15]
    new_gains, norm_ref, new_feed, new_attention, factor_ref = refs[15:18], refs[18], refs[19:23], refs[23:27], refs[27]
    rows = feed[0].shape[0]
    lines = pl.ds(pl.multiple_of(pl.program_id(0) * rows, rows), rows)

    @pl.when(pl.program_id(0) == 0)
    def _():
        norm = norm_of(lines_ref, tile_ref)
        norm_ref[...] = norm
        factor_ref[...] = clip_norm / norm
        weight, mean, square = (ref[...] for ref in gains)
        gradient = gain_ref[...] * factor_ref[...]
        for ref, value in zip(new_gains, adamw(weight, gradient, mean, square, gain_rate, 0.0)):
            ref[...] = value

    factor = factor_ref[...]

    def piece(olds, news, grad_ref, member, start, column, size):
        at = pl.ds(pl.multiple_of(column, size), size)
        gradient = grad_ref[member, lines, pl.ds(start, size)].astype(jnp.float32) * factor
        weight, mean, square = (ref[:, at] for ref in olds)
        values = adamw(weight, gradient, mean, square, matrix_rate, weight_decay, close_reciprocal)
        for ref, value in zip(news, (*values, values[0])):
            ref[:, at] = value.astype(ref.dtype)

    part = down_ref.shape[2]
    size = min(part, 512)

    @pl.loop(0, 8)
    def _(member):
        for offset in range(0, part, size):
            for number, (grad_ref, start) in enumerate(((gate_up_ref, 0), (gate_up_ref, part), (down_ref, 0))):
                column = (number * 8 + member) * part + offset
                piece(feed, new_feed, grad_ref, member, start + offset, column, size)
        core = lax.rem(member, 2)
        kv_column = (8 + 4 * core + lax.div(member, 2)) * HEAD_SIZE
        for number, column in enumerate((member * HEAD_SIZE, kv_column, (16 + member) * HEAD_SIZE)):
            piece(attention, new_attention, attention_ref, member, number * HEAD_SIZE, column, HEAD_SIZE)


def update(sums, grads, gains, feed, attention):
    f32, low = jnp.float32, jnp.bfloat16
    rows = min(feed[0].shape[0], 16)

    def some(value):
        return pl.BlockSpec((rows, value.shape[1]), lambda i: (i, 0))

    def whole(value):
        return pl.BlockSpec(value.shape, lambda i: (0,) * value.ndim)

    norm = jax.ShapeDtypeStruct((1, 1), f32)
    matrices = [jax.ShapeDtypeStruct(part[0].shape, dtype) for part in (feed, attention) for dtype in (f32, f32, f32, low)]
    return pl.pallas_call(
        update_kernel,
        grid=(feed[0].shape[0] // rows,),
        in_specs=[whole(value) for value in (*sums, *grads, *gains)] + [some(value) for value in (*feed, *attention)],
        out_specs=[whole(value) for value in (*gains, norm)] + [some(value) for value in matrices],
        out_shape=[jax.ShapeDtypeStruct(gains[0].shape, f32)] * 3 + [norm] + matrices,
        scratch_shapes=[pltpu.VMEM((1, 1), f32)],
        compiler_params=pltpu.CompilerParams(vmem_limit_bytes=56 * 2**20),
        name="update",
    )(*sums, *grads, *gains, *feed, *attention)


def is_square():
    return lax.axis_size("y") == 2 and lax.axis_size("x") == 2


def swap(blocks):
    return lax.all_to_all(blocks, TEAM, split_axis=0, concat_axis=0, tiled=True)


def over_planes(blocks):
    return lax.all_gather(blocks.reshape(-1, blocks.shape[-1]), "z", axis=0, tiled=True)


def scatter_planes(term):
    return lax.psum_scatter(term, "z", scatter_dimension=0, tiled=True)


def together(*values):
    return lax.optimization_barrier(values)


def scatter_team(rows, number, after=()):
    if not is_square():
        return swap(rows.reshape(8, -1, rows.shape[-1]))
    return turn(rows, number, after)[0]


def team_gather(local, number, after=()):
    if not is_square():
        return lax.all_gather(local, TEAM, axis=0, tiled=True)
    return plane_gather(local, number, after).reshape(-1, local.shape[1])


def team_sum(lefts, rights, number, after=()):
    if is_square():
        return plane_sum(lefts, rights, number, after)
    partial = mm_nt(jnp.concatenate(lefts, axis=1), jnp.concatenate(rights, axis=1))
    return lax.psum_scatter(partial.astype(jnp.bfloat16), TEAM, scatter_dimension=0, tiled=True).astype(jnp.float32)


def local(
    tokens,
    lengths,
    norm_gains,
    attention_weight,
    feed_weight,
    cotangent,
    attention_mean,
    attention_square,
    feed_mean,
    feed_square,
    gain_mean,
    gain_square,
):
    low = jnp.bfloat16
    sequences, span, width = tokens.shape
    ny, nx, nz = lax.axis_size("y"), lax.axis_size("x"), lax.axis_size("z")
    team = ny * nx * 2
    core = lax.axis_index("c")
    rows = attention_weight.shape[0]
    q_width, kv_width = QUERY_HEADS * HEAD_SIZE, KEY_VALUE_HEADS * HEAD_SIZE
    count = sequences * span
    all_sequences = nx * 2 * sequences
    reach = ny * span
    near = is_square()
    ff_part = FF // team

    def columns(start, size):
        return pl.ds(pl.multiple_of(start, size), size)

    def take_attention(sources, member, c):
        source = sources[0]
        starts = (
            member * HEAD_SIZE,
            q_width + c * kv_width + (member - c) // 2 * HEAD_SIZE,
            q_width + 2 * kv_width + member * HEAD_SIZE,
        )
        return jnp.concatenate([source[:, columns(s, HEAD_SIZE)].astype(low) for s in starts], axis=1)

    def take_feed(*parts):
        return lambda sources, member, c: jnp.concatenate(
            [sources[0][:, columns(part * FF + member * ff_part, ff_part)].astype(low) for part in parts], axis=1
        )

    def spread(source, take, size, number, after=()):
        if is_square():
            blocks = plane_swap([source], [(rows, size)], [take], number, after)[0]
        else:
            blocks = swap(jnp.stack([take([source], member, member % 2) for member in range(8)]))
        return blocks, over_planes(blocks)

    team_base = lax.axis_index("z") * reach
    team_pos = team_base + jnp.arange(reach, dtype=jnp.int32)
    own_pos = team_base + lax.axis_index("y") * span + jnp.arange(span, dtype=jnp.int32)
    if near:
        key_pos = jnp.concatenate([team_pos - back * reach for back in range(nz)])
    else:
        key_pos = jnp.arange(nz * reach, dtype=jnp.int32)
    query_at, key_at = team_pos[:, None], key_pos[None, :]
    cos_table, sin_table = angle_tables(team_pos)
    cos_rows, sin_rows = (t.reshape(ny, 1, span, -1) for t in (cos_table, sin_table))
    valid = (own_pos[None, :] < lengths[:, None]).astype(jnp.float32).reshape(count, 1)
    lengths_all = lax.all_gather(lengths, ("x", "c"), axis=0, tiled=True)
    planes = jnp.arange(nz, dtype=jnp.int32)
    if near:
        planes = (lax.axis_index("z") - planes) % nz
    core_at = jnp.concatenate([jnp.reshape(core, (1,)), planes]).astype(jnp.int32)

    def heads(value):
        return value.reshape(ny, all_sequences, span, HEAD_SIZE)

    x_in = tokens.reshape(count, width).astype(jnp.float32)
    normed_one, inverse_one = rms_forward(x_in, norm_gains[0])
    outer_grad = cotangent.reshape(count, width).astype(jnp.float32) * valid
    if is_square():
        attention_mine, h1, gate_up_blocks = begin(
            attention_weight,
            feed_weight,
            tokens.reshape(count, width),
            norm_gains[:1],
            (take_attention, take_feed(0, 1)),
            (3 * HEAD_SIZE, 2 * ff_part),
            nz,
            1,
        )
        h1 = h1.reshape(-1, width)
    else:
        attention_mine = spread(attention_weight, take_attention, 3 * HEAD_SIZE, 1)[1]
        gate_up_blocks, gate_up_weight = spread(feed_weight, take_feed(0, 1), 2 * ff_part, 2)
        h1 = team_gather(normed_one.astype(low), 3)
    query_weight = attention_mine[:, :HEAD_SIZE]
    kv_weight = attention_mine[:, HEAD_SIZE : 2 * HEAD_SIZE]
    out_weight = attention_mine[:, 2 * HEAD_SIZE :]
    tables = [t.reshape(ny, span, -1) for t in (cos_table, sin_table)]
    if is_square():
        kv, other = climb(h1, attention_mine, *tables, nz, 2)
        kv, other = (t.reshape(nz, ny, all_sequences, span, HEAD_SIZE) for t in (kv, other))
        gate_up_blocks, kv = together(gate_up_blocks, kv)
        gate_up_weight = over_planes(gate_up_blocks)
    else:
        kv_raw = heads(mm(h1, kv_weight))
        kv = jnp.where(core == 0, rotate(kv_raw, cos_rows, sin_rows), kv_raw).astype(low)
        kv = lax.all_gather(kv, "z", axis=0, tiled=False)
        other = lax.ppermute(kv, "c", [(0, 1), (1, 0)])
    q = rotate(heads(mm(h1, query_weight)), cos_rows, sin_rows).astype(low)
    attend = (core_at, lengths_all, q, kv, other, query_at, key_at)
    (o,) = attention_call(attention_kernel, *attend, (), [("rows", low)], "attention")
    o = o.reshape(-1, HEAD_SIZE)
    r = x_in + team_sum([o], [out_weight], 4)

    normed_two, inverse_two = rms_forward(r, norm_gains[1])
    h2 = team_gather(normed_two.astype(low), 16)
    dyb = team_gather(outer_grad.astype(low), 15, [h2])
    down_blocks, down_weight = spread(feed_weight, take_feed(2), ff_part, 12, [dyb])
    gate_up_weight, down_blocks = together(gate_up_weight, down_blocks)
    both = mm(h2, gate_up_weight)
    gate, upward = both[:, :ff_part], both[:, ff_part:]
    sig = jax.nn.sigmoid(gate)
    m = (gate * sig * upward).astype(low)
    down_term = mm_tn(dyb, m).astype(low)
    down_rows = scatter_planes(down_term)
    down_weight, down_term = together(down_weight, down_term)
    d_both = feed_back(dyb, down_weight, both)
    gate_up_term = mm_tn(h2, d_both).astype(low)
    gate_up_rows = scatter_planes(gate_up_term)
    dh2 = team_sum([d_both], [gate_up_weight], 7, [gate_up_term, down_term])
    mid_grad, gain_two = rms_back(dh2, r, inverse_two, norm_gains[1])
    dr = outer_grad + mid_grad
    drb = team_gather(dr.astype(low), 13, [down_rows])

    do = heads(mm(drb, out_weight).astype(low))
    dq, keep, theirs = attention_call(
        attention_back_kernel,
        *attend,
        (do, cos_table, sin_table),
        [("rows", low), ("keys", jnp.float32), ("keys", low)],
        "attention_back",
    )
    dq = dq.reshape(-1, HEAD_SIZE)
    dkv = keep + lax.ppermute(theirs, "c", [(0, 1), (1, 0)]).astype(jnp.float32)
    low_terms = dkv.astype(low)
    feed_sum = team_sum([m], [down_weight], 5, [low_terms])
    down_grad = scatter_team(down_rows, 6, [low_terms])
    layer_output = (r + feed_sum).astype(low)
    local_squares = sum(jnp.sum(jnp.square(part.astype(jnp.float32))) for part in (gate_up_rows, down_rows))
    query_term, out_term = mm_tn(h1, dq).astype(low), mm_tn(drb, o).astype(low)
    low_terms, gate_up_rows, layer_output, down_grad, query_term, out_term = together(
        low_terms, gate_up_rows, layer_output, down_grad, query_term, out_term
    )
    if is_square():
        low_terms = low_terms.reshape(nz, -1, HEAD_SIZE)
        dkv, attention_term, gate_up_grad = fall(low_terms, gate_up_rows, h1, query_term, out_term, *tables, nz, 8)
    else:
        dkv = lax.psum_scatter(low_terms, "z", scatter_dimension=0, tiled=True)[0].astype(jnp.float32)
        dkv = jnp.where(core == 0, rotate(dkv, cos_rows, -sin_rows), dkv).astype(low).reshape(-1, HEAD_SIZE)
        attention_term = jnp.concatenate([query_term, mm_tn(h1, dkv).astype(low), out_term], axis=1)
        gate_up_grad = scatter_team(gate_up_rows, 8)
    attention_rows = scatter_planes(attention_term)
    dh1 = team_sum([dq, dkv], [query_weight, kv_weight], 9)
    in_grad, gain_one = rms_back(dh1, x_in, inverse_one, norm_gains[0])
    input_gradient = dr + in_grad
    gain_local = jnp.stack([gain_one, gain_two]).reshape(-1, 128)
    lines = jnp.concatenate([gain_local, jnp.full((8, 128), local_squares)], axis=0)
    if is_square():
        lines = total_sum(lines, nz, 18)
        attention_grad, tile = turn(attention_rows, 10, (), nz)
    else:
        lines = lax.psum(lines, ALL)
        attention_grad = scatter_team(attention_rows, 10)
        tile = lax.psum(jnp.full((8, 128), jnp.sum(jnp.square(attention_rows.astype(jnp.float32)))), ALL)
    gain_grad = lines[:-8].reshape(2, width)
    news = update(
        (lines, tile, gain_grad),
        (gate_up_grad, down_grad, attention_grad),
        (norm_gains, gain_mean, gain_square),
        (feed_weight, feed_mean, feed_square),
        (attention_weight, attention_mean, attention_square),
    )
    gains_new, gradient_norm, feed_new, attention_new = news[:3], news[3], news[4:8], news[8:]
    return (
        layer_output.reshape(sequences, span, width),
        input_gradient.reshape(sequences, span, width),
        gradient_norm.reshape(()),
        *attention_new,
        *feed_new,
        *gains_new,
    )


def solution(mesh):
    ctx, fsdp = mesh.shape["ctx"], mesh.shape["fsdp"]
    inner = QUERY_HEADS // fsdp
    fine = Mesh(mesh.devices.reshape(ctx // inner, inner, fsdp // 2, 2), ALL)
    act = P(("x", "c"), ("z", "y"), None)
    matrix = P(ALL, None)
    return jax.shard_map(
        local,
        mesh=fine,
        in_specs=(act, P(("x", "c")), P(), matrix, matrix, act, matrix, matrix, matrix, matrix, P(), P()),
        out_specs=(act, act, P(), matrix, matrix, matrix, matrix, matrix, matrix, matrix, matrix, P(), P(), P()),
        check_vma=False,
    )
```
